32 devices in a mesh: grp: 2 (over y), row: 16 (over z, x, core), chan: 1.
Axes of the slice: x: 2, y: 2, z: 4, core: 2. Of those that a mesh axis runs over, the one named last changes fastest.
Arguments:
- pair: bfloat16 [256, 128, 128], P(('grp', 'row'), 'chan'), parts along dimension 0, may hold values from -150 to 150
- cotangent: bfloat16 [256, 128, 128], P(('grp', 'row'), 'chan'), parts along dimension 0, may hold values from -6 to 6
- residue_mask: int32 [256], P('grp'), parts along dimension 0, may hold values from 0 to 1, as said below
- ln_in_gain: float32 [128], replicated, may hold values from 0.5 to 1.5
- ln_in_bias: float32 [128], replicated, may hold values from -3 to 3
- w_proj: bfloat16 [128, 512], replicated, may hold values from -0.5 to 0.5
- w_gate: bfloat16 [128, 128], replicated, may hold values from -0.5 to 0.5
- ln_out_gain: float32 [128], replicated, may hold values from 0.5 to 1.5
- ln_out_bias: float32 [128], replicated, may hold values from -3 to 3
- w_out: bfloat16 [128, 128], replicated, may hold values from -0.5 to 0.5
Outputs:
- grad_pair: bfloat16 [256, 128, 128], P(('grp', 'row'), 'chan'), parts along dimension 0
The draws below stay inside these ranges and needn't reach their ends.
There are 2 independent parts, one for each index of `grp`. The reference program is written for one: setup_inputs(seed, part) draws one part's arguments, and reference() takes and returns one part's arrays. A program takes and returns all parts, laid end to end along the dimension named above; an argument that names none is the same for every part. Nothing has to cross between parts.
Inputs may be any that keep to these rules, and one draw needn't show every extreme that they name: residue_mask is 1 on a leading run of residues and 0 on the rest; the count of ones is a multiple of 8, at least 64 and below 128.
All inputs are finite; a program needn't handle non-finite values.
Results may differ from the reference program's by a relative error of at most 0.0075.
Values may be sent and summed in bfloat16 or wider, within the bound.
No kernel may reach another device: no remote copies, remote signals or barrier semaphores. Data moves between devices by JAX's collectives and lax.ppermute only.
A program may use at most 64 MiB of HBM per device.

```python
import math
import jax
import jax.numpy as jnp
from jax import lax

C = 128
H = 128
ROWS_DEV = 8
N = 128


def draw_pair(key, part):
    key = jax.random.fold_in(key, 11)
    key_values, key_chan, key_cell = jax.random.split(key, 3)
    chan_scale = jnp.exp(jax.random.uniform(key_chan, (C,), jnp.float32, 0.0, math.log(10.0)))
    cell_scale = jnp.exp(jax.random.uniform(key_cell, (N, N, 1), jnp.float32, math.log(0.3), math.log(3.0)))
    values = jnp.clip(jax.random.normal(key_values, (N, N, C), jnp.float32), -5.0, 5.0)
    return (values * chan_scale * cell_scale).astype(jnp.bfloat16)


def draw_residue_mask(key, part):
    key = jax.random.fold_in(key, 5)
    block_count = N // ROWS_DEV
    padded = jax.random.randint(key, (), 1, block_count // 2 + 1)
    length = (block_count - padded) * ROWS_DEV
    return (jnp.arange(N, dtype=jnp.int32) < length).astype(jnp.int32)


def steps_of(own_key, extent, shards, least, high):
    def one(dim, blocks):
        draws = jax.random.uniform(jax.random.fold_in(jax.random.fold_in(own_key, 6), dim), (blocks,), jnp.float32, least / len(shards), high / len(shards))
        return jnp.repeat(jnp.exp(draws), extent[dim] // blocks).reshape((-1,) + (1,) * (len(extent) - dim - 1))

    factor_of = one(*shards[0])
    for cut in shards[1:]:
        factor_of = factor_of * one(*cut)
    return factor_of


def normal_values(stream_key, shape, deviation, most, cuts=(), kind=jnp.bfloat16):
    loudness = steps_of(stream_key, shape, cuts, -0.22, 0.18) if cuts else 1.0
    values = jax.random.normal(stream_key, shape, jnp.float32) * deviation * loudness
    return jnp.minimum(jnp.maximum(values, -most), most).astype(kind)


def setup_inputs(seed: int = 0, part: int = 0) -> dict:
    splits = jax.random.split(jax.random.key(seed), 11)
    own_keys = jax.random.split(jax.random.fold_in(splits[10], part), 11)
    pair = draw_pair(jax.random.fold_in(jax.random.fold_in(splits[10], part), 71), part)
    cotangent = normal_values(own_keys[1], (N, N, C), 1.0, 6.0, ((0, 16),))
    residue_mask = draw_residue_mask(jax.random.fold_in(jax.random.fold_in(splits[10], part), 71), part)
    ln_in_gain = jnp.clip(jax.random.uniform(splits[3], (C,), jnp.float32, 0.5, 1.5), 0.5, 1.5)
    ln_in_bias = normal_values(splits[4], (C,), 0.5, 3.0, (), jnp.float32)
    w_proj = normal_values(splits[5], (C, 4 * H), C ** -0.5, 0.5)
    w_gate = normal_values(splits[6], (C, C), C ** -0.5, 0.5)
    ln_out_gain = jnp.clip(jax.random.uniform(splits[7], (H,), jnp.float32, 0.5, 1.5), 0.5, 1.5)
    ln_out_bias = normal_values(splits[8], (H,), 0.5, 3.0, (), jnp.float32)
    w_out = normal_values(splits[9], (H, C), H ** -0.5, 0.5)
    return {"pair": pair, "cotangent": cotangent, "residue_mask": residue_mask, "ln_in_gain": ln_in_gain, "ln_in_bias": ln_in_bias, "w_proj": w_proj, "w_gate": w_gate, "ln_out_gain": ln_out_gain, "ln_out_bias": ln_out_bias, "w_out": w_out}


def normalize(values, reduce_axis):
    mean_value = lax.optimization_barrier(jnp.mean(values, axis=reduce_axis, keepdims=True))
    centered = values - mean_value
    variance = lax.optimization_barrier(jnp.mean(centered * centered, axis=reduce_axis, keepdims=True))
    inv_std = lax.rsqrt(variance + 1e-05)
    return (centered * inv_std, inv_std)

def norm_backward(upstream, normed, inv_std, reduce_axis):
    mean_grad = lax.optimization_barrier(jnp.mean(upstream, axis=reduce_axis, keepdims=True))
    mean_cross = lax.optimization_barrier(jnp.mean(upstream * normed, axis=reduce_axis, keepdims=True))
    return inv_std * (upstream - mean_grad - normed * mean_cross)

def input_norm(pair_block, ln_in_gain, ln_in_bias):
    normed, inv_std = normalize(pair_block.astype(jnp.float32), -1)
    normed_pair = (normed * ln_in_gain + ln_in_bias).astype(jnp.bfloat16)
    return (normed, inv_std, normed_pair)

def reference(pair, cotangent, residue_mask, ln_in_gain, ln_in_bias, w_proj, w_gate, ln_out_gain, ln_out_bias, w_out):
    full_len = pair.shape[0]
    pair_width = pair.shape[2]
    hidden = w_out.shape[0]
    block_count = full_len // ROWS_DEV
    mask_float = residue_mask.astype(jnp.float32)
    pair_blocks = pair.reshape(block_count, ROWS_DEV, full_len, pair_width)
    cot_blocks = cotangent.reshape(block_count, ROWS_DEV, full_len, pair_width)
    mask_blocks = mask_float.reshape(block_count, ROWS_DEV)

    def projections(pair_block, row_mask):
        normed, inv_std, normed_pair = input_norm(pair_block, ln_in_gain, ln_in_bias)
        projected = jnp.dot(normed_pair, w_proj, preferred_element_type=jnp.float32)
        projected = jnp.transpose(projected, (2, 0, 1))
        cell_mask = (row_mask[:, None] * mask_float[None, :])[None]
        return (normed, inv_std, normed_pair, projected, cell_mask)

    def forward_block(inputs):
        pair_block, row_mask = inputs
        _, _, _, projected, cell_mask = projections(pair_block, row_mask)
        left_panel = cell_mask * jax.nn.sigmoid(projected[:hidden]) * projected[hidden:2 * hidden]
        right_panel = cell_mask * jax.nn.sigmoid(projected[2 * hidden:3 * hidden]) * projected[3 * hidden:]
        return (left_panel.astype(jnp.bfloat16), right_panel.astype(jnp.bfloat16))
    left_blocks, right_blocks = lax.map(forward_block, (pair_blocks, mask_blocks))
    left_all = jnp.transpose(left_blocks, (1, 0, 2, 3)).reshape(hidden, full_len, full_len)
    right_all = jnp.transpose(right_blocks, (1, 0, 2, 3)).reshape(hidden, full_len, full_len)

    def tri_channel(inputs):
        left_one, right_one = inputs
        product = jnp.dot(left_one.astype(jnp.float32), right_one.astype(jnp.float32).T, preferred_element_type=jnp.float32)
        return product.astype(jnp.bfloat16)
    tri_all = lax.map(tri_channel, (left_all, right_all))
    tri_blocks = jnp.transpose(tri_all.reshape(hidden, block_count, ROWS_DEV, full_len), (1, 0, 2, 3))

    def middle_block(inputs):
        pair_block, tri_block, cot_block = inputs
        _, _, normed_pair = input_norm(pair_block, ln_in_gain, ln_in_bias)
        tri_hat, inv_tri = normalize(tri_block.astype(jnp.float32), 0)
        scaled = (tri_hat * ln_out_gain[:, None, None] + ln_out_bias[:, None, None]).astype(jnp.bfloat16)
        proj_out = jnp.einsum('hrm,hc->rmc', scaled.astype(jnp.float32), w_out.astype(jnp.float32))
        gate_value = jax.nn.sigmoid(jnp.dot(normed_pair, w_gate, preferred_element_type=jnp.float32))
        cot_float = cot_block.astype(jnp.float32)
        d_gate_pre = (cot_float * proj_out * gate_value * (1.0 - gate_value)).astype(jnp.bfloat16)
        d_scaled = (cot_float * gate_value).astype(jnp.bfloat16)
        d_hat = jnp.einsum('rmc,hc->hrm', d_scaled.astype(jnp.float32), w_out.astype(jnp.float32))
        d_hat = d_hat * ln_out_gain[:, None, None]
        d_tri = norm_backward(d_hat, tri_hat, inv_tri, 0).astype(jnp.bfloat16)
        return (d_tri, d_gate_pre)
    d_tri_blocks, d_gate_blocks = lax.map(middle_block, (pair_blocks, tri_blocks, cot_blocks))
    d_tri_all = jnp.transpose(d_tri_blocks, (1, 0, 2, 3)).reshape(hidden, full_len, full_len)

    def tri_backward(inputs):
        d_one, left_one, right_one = inputs
        d_float = d_one.astype(jnp.float32)
        d_left = jnp.dot(d_float, right_one.astype(jnp.float32), preferred_element_type=jnp.float32)
        d_right = jnp.dot(d_float.T, left_one.astype(jnp.float32), preferred_element_type=jnp.float32)
        return (d_left.astype(jnp.bfloat16), d_right.astype(jnp.bfloat16))
    d_left_all, d_right_all = lax.map(tri_backward, (d_tri_all, left_all, right_all))
    d_left_blocks = jnp.transpose(d_left_all.reshape(hidden, block_count, ROWS_DEV, full_len), (1, 0, 2, 3))
    d_right_blocks = jnp.transpose(d_right_all.reshape(hidden, block_count, ROWS_DEV, full_len), (1, 0, 2, 3))

    def final_block(inputs):
        pair_block, row_mask, d_left, d_right, d_gate_pre = inputs
        normed, inv_std, _, projected, cell_mask = projections(pair_block, row_mask)

        def gating(d_value, gate_proj, value_proj):
            sigmoid_val = jax.nn.sigmoid(gate_proj)
            masked_grad = d_value.astype(jnp.float32) * cell_mask
            return (masked_grad * value_proj * sigmoid_val * (1.0 - sigmoid_val), masked_grad * sigmoid_val)
        gate_left, value_left = gating(d_left, projected[:hidden], projected[hidden:2 * hidden])
        gate_right, value_right = gating(d_right, projected[2 * hidden:3 * hidden], projected[3 * hidden:])
        d_proj = jnp.concatenate([gate_left, value_left, gate_right, value_right], axis=0).astype(jnp.bfloat16)
        d_normed = jnp.einsum('hrm,ch->rmc', d_proj.astype(jnp.float32), w_proj.astype(jnp.float32))
        d_normed = d_normed + jnp.einsum('rmd,cd->rmc', d_gate_pre.astype(jnp.float32), w_gate.astype(jnp.float32))
        d_input = d_normed * ln_in_gain
        return norm_backward(d_input, normed, inv_std, -1).astype(jnp.bfloat16)
    grads = lax.map(final_block, (pair_blocks, mask_blocks, d_left_blocks, d_right_blocks, d_gate_blocks))
    return grads.reshape(full_len, full_len, pair_width)
```

```python
import jax
import jax.numpy as jnp
from jax import lax
from jax.sharding import PartitionSpec as P


def normalize(values, reduce_axis):
    mean_value = jnp.mean(values, axis=reduce_axis, keepdims=True)
    centered = values - mean_value
    variance = jnp.mean(centered * centered, axis=reduce_axis, keepdims=True)
    inv_std = lax.rsqrt(variance + 1e-05)
    return (centered * inv_std, inv_std)


def norm_backward(upstream, normed, inv_std, reduce_axis):
    mean_grad = jnp.mean(upstream, axis=reduce_axis, keepdims=True)
    mean_cross = jnp.mean(upstream * normed, axis=reduce_axis, keepdims=True)
    return inv_std * (upstream - mean_grad - normed * mean_cross)


def exchange(values, split_axis, concat_axis):
    count = lax.axis_size("row")
    me = lax.axis_index("row")
    size = values.shape[split_axis] // count
    received = [lax.dynamic_slice_in_dim(values, me * size, size, split_axis)]
    for step in range(1, count):
        target = lax.rem(me + step, count)
        piece = lax.dynamic_slice_in_dim(values, target * size, size, split_axis)
        received.append(lax.ppermute(piece, "row", [(d, (d + step) % count) for d in range(count)]))
    width = values.shape[concat_axis]
    shape = list(received[0].shape)
    shape[concat_axis] = width * count
    result = jnp.zeros(shape, values.dtype)
    for step in range(count):
        source = lax.rem(me - step + count, count)
        result = lax.dynamic_update_slice_in_dim(result, received[step], source * width, concat_axis)
    return result


def shards(
    pair,
    cotangent,
    residue_mask,
    ln_in_gain,
    ln_in_bias,
    w_proj,
    w_gate,
    ln_out_gain,
    ln_out_bias,
    w_out,
):
    local_rows = pair.shape[0]
    local_cols = pair.shape[1]
    hidden = w_out.shape[0]
    chan_index = lax.axis_index("chan")
    row_start = lax.axis_index("row") * local_rows
    col_start = chan_index * local_cols
    mask_float = residue_mask.astype(jnp.float32)
    row_mask = lax.dynamic_slice_in_dim(mask_float, row_start, local_rows)
    col_mask = lax.dynamic_slice_in_dim(mask_float, col_start, local_cols)
    cell_mask = (row_mask[:, None] * col_mask[None, :])[None]
    normed, inv_std = normalize(pair.astype(jnp.float32), -1)
    normed_pair = (normed * ln_in_gain + ln_in_bias).astype(jnp.bfloat16)
    projected = jnp.einsum("rmc,ch->hrm", normed_pair, w_proj, preferred_element_type=jnp.float32)
    left_panel = (
        cell_mask * jax.nn.sigmoid(projected[:hidden]) * projected[hidden : 2 * hidden]
    ).astype(jnp.bfloat16)
    right_panel = (
        cell_mask * jax.nn.sigmoid(projected[2 * hidden : 3 * hidden]) * projected[3 * hidden :]
    ).astype(jnp.bfloat16)
    panels = exchange(jnp.stack([left_panel, right_panel]), 1, 2)
    left_all = panels[0]
    right_all = panels[1]
    right_rows = lax.all_to_all(right_all, "chan", split_axis=1, concat_axis=2, tiled=True)
    partner = right_rows
    tri_part = jnp.einsum(
        "gik,gjk->gij",
        lax.all_gather(left_all, "chan", axis=2, tiled=True),
        partner,
        preferred_element_type=jnp.float32,
    ).astype(jnp.bfloat16)
    tri_cells = exchange(tri_part, 1, 0)
    tri_hat, inv_tri = normalize(tri_cells.astype(jnp.float32), 0)
    scaled = (tri_hat * ln_out_gain[:, None, None] + ln_out_bias[:, None, None]).astype(
        jnp.bfloat16
    )
    proj_out = jnp.einsum("hrm,hc->rmc", scaled, w_out, preferred_element_type=jnp.float32)
    gate_value = jax.nn.sigmoid(
        jnp.einsum("rmc,cd->rmd", normed_pair, w_gate, preferred_element_type=jnp.float32)
    )
    cot_float = cotangent.astype(jnp.float32)
    d_gate_pre = (cot_float * proj_out * gate_value * (1.0 - gate_value)).astype(jnp.bfloat16)
    d_scaled = (cot_float * gate_value).astype(jnp.bfloat16)
    d_hat = jnp.einsum("rmc,hc->hrm", d_scaled, w_out, preferred_element_type=jnp.float32)
    d_hat = d_hat * ln_out_gain[:, None, None]
    d_tri = norm_backward(d_hat, tri_hat, inv_tri, 0).astype(jnp.bfloat16)
    d_tri_all = exchange(d_tri, 0, 1)
    panel_piece = lax.all_gather(d_tri_all, "chan", axis=2, tiled=True)
    partner = right_all
    d_left = jnp.einsum("gij,gjk->gik", panel_piece, partner, preferred_element_type=jnp.float32)
    contribution = jnp.einsum(
        "gij,gik->gjk", panel_piece, left_all, preferred_element_type=jnp.float32
    )
    d_right = contribution
    d_left, d_right = (d_left, d_right)
    d_stack = jnp.stack([d_left, d_right]).astype(jnp.bfloat16)
    d_panels = exchange(d_stack, 2, 1)

    def gating(d_value, gate_proj, value_proj):
        sigmoid_val = jax.nn.sigmoid(gate_proj)
        masked_grad = d_value.astype(jnp.float32) * cell_mask
        return (
            masked_grad * value_proj * sigmoid_val * (1.0 - sigmoid_val),
            masked_grad * sigmoid_val,
        )

    gate_left, value_left = gating(d_panels[0], projected[:hidden], projected[hidden : 2 * hidden])
    gate_right, value_right = gating(
        d_panels[1], projected[2 * hidden : 3 * hidden], projected[3 * hidden :]
    )
    d_proj = jnp.concatenate([gate_left, value_left, gate_right, value_right], axis=0).astype(
        jnp.bfloat16
    )
    d_normed = jnp.einsum("hrm,ch->rmc", d_proj, w_proj, preferred_element_type=jnp.float32)
    d_normed = d_normed + jnp.einsum(
        "rmd,cd->rmc", d_gate_pre, w_gate, preferred_element_type=jnp.float32
    )
    d_input = d_normed * ln_in_gain
    return norm_backward(d_input, normed, inv_std, -1).astype(jnp.bfloat16)


def solution(mesh):
    return jax.shard_map(
        shards,
        mesh=mesh,
        in_specs=(
            P(("grp", "row"), "chan", None),
            P(("grp", "row"), "chan", None),
            P("grp"),
            P(),
            P(),
            P(),
            P(),
            P(),
            P(),
            P(),
        ),
        out_specs=P(("grp", "row"), "chan", None),
        check_vma=False,
    )
```

```python
import jax
import jax.numpy as jnp
from jax import lax
from jax.sharding import PartitionSpec as P


def normalize(values, reduce_axis):
    mean_value = jnp.mean(values, axis=reduce_axis, keepdims=True)
    centered = values - mean_value
    variance = jnp.mean(centered * centered, axis=reduce_axis, keepdims=True)
    inv_std = lax.rsqrt(variance + 1e-05)
    return (centered * inv_std, inv_std)


def norm_backward(upstream, normed, inv_std, reduce_axis):
    mean_grad = jnp.mean(upstream, axis=reduce_axis, keepdims=True)
    mean_cross = jnp.mean(upstream * normed, axis=reduce_axis, keepdims=True)
    return inv_std * (upstream - mean_grad - normed * mean_cross)


def shards(
    pair,
    cotangent,
    residue_mask,
    ln_in_gain,
    ln_in_bias,
    w_proj,
    w_gate,
    ln_out_gain,
    ln_out_bias,
    w_out,
):
    local_rows = pair.shape[0]
    local_cols = pair.shape[1]
    hidden = w_out.shape[0]
    chan_index = lax.axis_index("chan")
    row_start = lax.axis_index("row") * local_rows
    col_start = chan_index * local_cols
    mask_float = residue_mask.astype(jnp.float32)
    row_mask = lax.dynamic_slice_in_dim(mask_float, row_start, local_rows)
    col_mask = lax.dynamic_slice_in_dim(mask_float, col_start, local_cols)
    cell_mask = (row_mask[:, None] * col_mask[None, :])[None]
    normed, inv_std = normalize(pair.astype(jnp.float32), -1)
    normed_pair = (normed * ln_in_gain + ln_in_bias).astype(jnp.bfloat16)
    projected = jnp.einsum("rmc,ch->hrm", normed_pair, w_proj, preferred_element_type=jnp.float32)
    left_panel = (
        cell_mask * jax.nn.sigmoid(projected[:hidden]) * projected[hidden : 2 * hidden]
    ).astype(jnp.bfloat16)
    right_panel = (
        cell_mask * jax.nn.sigmoid(projected[2 * hidden : 3 * hidden]) * projected[3 * hidden :]
    ).astype(jnp.bfloat16)
    right_rows = lax.all_gather(jnp.transpose(right_panel, (1, 0, 2)), "row", axis=0, tiled=True)
    left_all = lax.all_to_all(left_panel, "row", split_axis=0, concat_axis=1, tiled=True)
    tri_cells = jnp.einsum(
        "hik,jhk->hij",
        lax.all_gather(left_panel, "chan", axis=2, tiled=True),
        lax.all_to_all(right_rows, "chan", split_axis=0, concat_axis=2, tiled=True),
        preferred_element_type=jnp.float32,
    ).astype(jnp.bfloat16)
    tri_hat, inv_tri = normalize(tri_cells.astype(jnp.float32), 0)
    scaled = (tri_hat * ln_out_gain[:, None, None] + ln_out_bias[:, None, None]).astype(
        jnp.bfloat16
    )
    proj_out = jnp.einsum("hrm,hc->rmc", scaled, w_out, preferred_element_type=jnp.float32)
    gate_value = jax.nn.sigmoid(
        jnp.einsum("rmc,cd->rmd", normed_pair, w_gate, preferred_element_type=jnp.float32)
    )
    cot_float = cotangent.astype(jnp.float32)
    d_gate_pre = (cot_float * proj_out * gate_value * (1.0 - gate_value)).astype(jnp.bfloat16)
    d_scaled = (cot_float * gate_value).astype(jnp.bfloat16)
    d_hat = jnp.einsum("rmc,hc->hrm", d_scaled, w_out, preferred_element_type=jnp.float32)
    d_hat = d_hat * ln_out_gain[:, None, None]
    d_tri = norm_backward(d_hat, tri_hat, inv_tri, 0).astype(jnp.bfloat16)
    d_tri_all = lax.all_to_all(d_tri, "row", split_axis=0, concat_axis=1, tiled=True)
    d_tri_wide = lax.all_gather(d_tri, "chan", axis=2, tiled=True)
    d_left = jnp.einsum(
        "hij,jhk->hik", d_tri_wide, right_rows, preferred_element_type=jnp.float32
    ).astype(jnp.bfloat16)
    panel_piece = lax.all_gather(d_tri_all, "chan", axis=2, tiled=True)
    d_right = jnp.einsum(
        "gij,gik->gjk", panel_piece, left_all, preferred_element_type=jnp.float32
    ).astype(jnp.bfloat16)
    d_right = lax.all_to_all(d_right, "row", split_axis=1, concat_axis=0, tiled=True)

    def gating(d_value, gate_proj, value_proj):
        sigmoid_val = jax.nn.sigmoid(gate_proj)
        masked_grad = d_value.astype(jnp.float32) * cell_mask
        return (
            masked_grad * value_proj * sigmoid_val * (1.0 - sigmoid_val),
            masked_grad * sigmoid_val,
        )

    gate_left, value_left = gating(d_left, projected[:hidden], projected[hidden : 2 * hidden])
    gate_right, value_right = gating(
        d_right, projected[2 * hidden : 3 * hidden], projected[3 * hidden :]
    )
    d_proj = jnp.concatenate([gate_left, value_left, gate_right, value_right], axis=0).astype(
        jnp.bfloat16
    )
    d_normed = jnp.einsum("hrm,ch->rmc", d_proj, w_proj, preferred_element_type=jnp.float32)
    d_normed = d_normed + jnp.einsum(
        "rmd,cd->rmc", d_gate_pre, w_gate, preferred_element_type=jnp.float32
    )
    d_input = d_normed * ln_in_gain
    return norm_backward(d_input, normed, inv_std, -1).astype(jnp.bfloat16)


def solution(mesh):
    return jax.shard_map(
        shards,
        mesh=mesh,
        in_specs=(
            P(("grp", "row"), "chan", None),
            P(("grp", "row"), "chan", None),
            P("grp"),
            P(),
            P(),
            P(),
            P(),
            P(),
            P(),
            P(),
        ),
        out_specs=P(("grp", "row"), "chan", None),
        check_vma=False,
    )
```

```python
import functools

import jax
import jax.numpy as jnp
from jax import lax
from jax.experimental import pallas as pl
from jax.experimental.pallas import tpu as pltpu
from jax.sharding import PartitionSpec as P

F32 = jnp.float32
BF16 = jnp.bfloat16
VMEM_LIMIT = 16 * 1024 * 1024


def dot(lhs, rhs, lhs_dim, rhs_dim):
    return lax.dot_general(
        lhs, rhs, (((lhs_dim,), (rhs_dim,)), ((), ())), preferred_element_type=F32
    )


def transposed(matrix):
    return jnp.transpose(matrix.astype(F32)).astype(BF16)


def sigmoid(values):
    return 1.0 / (1.0 + jnp.exp(-values))


def input_norm(pair_row):
    values = pair_row.astype(F32)
    centered = values - jnp.mean(values, axis=-1, keepdims=True)
    variance = jnp.mean(centered * centered, axis=-1, keepdims=True)
    inv_std = lax.rsqrt(variance + 1e-05)
    return centered * inv_std, inv_std


def call(kernel, name, outs, args, scratch=(), smem=(), flops=0):
    spaces = [pltpu.SMEM if n in smem else pltpu.VMEM for n in range(len(args))]
    moved = sum(a.size * a.dtype.itemsize for a in args) + sum(
        o.size * jnp.dtype(o.dtype).itemsize for o in outs
    )
    return pl.pallas_call(
        kernel,
        name=name,
        out_shape=outs,
        in_specs=[pl.BlockSpec(memory_space=space) for space in spaces],
        out_specs=[pl.BlockSpec(memory_space=pltpu.VMEM) for _ in outs],
        scratch_shapes=list(scratch),
        compiler_params=pltpu.CompilerParams(vmem_limit_bytes=VMEM_LIMIT),
        cost_estimate=pl.CostEstimate(flops=flops, bytes_accessed=moved, transcendentals=0),
    )(*args)


def cell_mask_row(mask_scalars, mask_vector, rows, row):
    own = mask_scalars[lax.axis_index("row") * rows + row].astype(F32)
    return mask_vector[...].astype(F32) * own


def project_kernel(pair, mask_scalars, mask_vector, gain, bias, w_proj, panels):
    rows = pair.shape[0]
    hidden = w_proj.shape[1] // 4
    count, _, width = panels.shape
    block = hidden // count
    w_flip = transposed(w_proj[...])
    for row in range(rows):
        normed, _ = input_norm(pair[row])
        zln = (normed * gain[...] + bias[...]).astype(BF16)
        proj = dot(w_flip, zln, 1, 1)
        mask = cell_mask_row(mask_scalars, mask_vector, rows, row)
        left = mask * sigmoid(proj[:hidden]) * proj[hidden : 2 * hidden]
        right = mask * sigmoid(proj[2 * hidden : 3 * hidden]) * proj[3 * hidden :]
        both = jnp.concatenate(
            [left.reshape(count, block, width), right.reshape(count, block, width)], axis=1
        )
        panels[:, row * 2 * block : (row + 1) * 2 * block, :] = both.astype(BF16)


def prepare_kernel(
    pair,
    cotangent,
    mask_scalars,
    mask_vector,
    gain,
    bias,
    w_proj,
    w_gate,
    out_gain,
    w_out,
    d_hat_centered,
    gate_slope,
    slopes,
):
    rows = pair.shape[0]
    hidden = w_out.shape[0]
    w_flip = transposed(w_proj[...])
    for row in range(rows):
        normed, _ = input_norm(pair[row])
        zln = (normed * gain[...] + bias[...]).astype(BF16)
        gate = sigmoid(dot(zln, w_gate[...], 1, 0))
        cot = cotangent[row].astype(F32)
        d_scaled = (cot * gate).astype(BF16)
        d_hat = dot(w_out[...], d_scaled, 1, 1) * out_gain[...]
        d_hat_centered[row] = d_hat - jnp.mean(d_hat, axis=0, keepdims=True)
        gate_slope[row] = cot * gate * (1.0 - gate)
        proj = dot(w_flip, zln, 1, 1)
        mask = cell_mask_row(mask_scalars, mask_vector, rows, row)
        for side in range(2):
            base = 2 * side * hidden
            sig = sigmoid(proj[base : base + hidden])
            masked = mask * sig
            slopes[row, base : base + hidden, :] = (
                masked * (1.0 - sig) * proj[base + hidden : base + 2 * hidden]
            )
            slopes[row, base + hidden : base + 2 * hidden, :] = masked


def tri_kernel(panels, products, matrices, wide, narrow):
    count, depth, width = panels.shape
    block = matrices.shape[0] // 2
    total = matrices.shape[1]
    wide[...] = panels[...].astype(F32).reshape(count * depth, width)
    for h in range(block):
        left = wide[pl.ds(h, total, stride=2 * block), :].astype(BF16)
        right = wide[pl.ds(block + h, total, stride=2 * block), :].astype(BF16)
        matrices[h] = left
        matrices[block + h] = right
        narrow[pl.ds(h, total, stride=block), :] = dot(left, right, 1, 1)
    products[...] = narrow[...].astype(BF16).reshape(products.shape)


def row_pair(ref, first, block):
    count, _, width = ref.shape
    both = ref[:, first * block : (first + 2) * block, :].astype(F32)
    return [
        both[:, n * block : (n + 1) * block, :].reshape(count * block, width) for n in range(2)
    ]


def hidden_norm(tri):
    centered = tri - jnp.mean(tri, axis=0, keepdims=True)
    variance = jnp.mean(centered * centered, axis=0, keepdims=True)
    inv_std = lax.rsqrt(variance + 1e-05)
    return centered * inv_std, inv_std


def middle_kernel(products, d_hat_centered, d_products):
    rows, hidden, width = d_hat_centered.shape
    count = products.shape[0]
    block = hidden // count
    for first in range(0, rows, 2):
        parts = []
        for n, tri in enumerate(row_pair(products, first, block)):
            tri_hat, inv_std = hidden_norm(tri)
            d_hat = d_hat_centered[first + n]
            cross = jnp.mean(d_hat * tri_hat, axis=0, keepdims=True)
            d_tri = inv_std * (d_hat - tri_hat * cross)
            parts.append(d_tri.reshape(count, block, width))
        d_products[:, first * block : (first + 2) * block, :] = jnp.concatenate(
            parts, axis=1
        ).astype(BF16)


def gate_back_kernel(products, gate_slope, out_gain, out_bias, w_out, w_gate, d_zln_gate):
    rows = gate_slope.shape[0]
    block = w_out.shape[0] // products.shape[0]
    for first in range(0, rows, 2):
        for n, tri in enumerate(row_pair(products, first, block)):
            tri_hat, _ = hidden_norm(tri)
            scaled = (tri_hat * out_gain[...] + out_bias[...]).astype(BF16)
            proj_out = dot(scaled, w_out[...], 0, 0)
            d_gate_pre = (proj_out * gate_slope[first + n]).astype(BF16)
            d_zln_gate[first + n] = dot(d_gate_pre, w_gate[...], 1, 1)


def products_kernel(d_products, matrices, d_panels, narrow, wide):
    count, depth, width = d_products.shape
    block = matrices.shape[0] // 2
    total = matrices.shape[1]
    narrow[...] = d_products[...].astype(F32).reshape(count * depth, width)
    for h in range(block):
        d_tri = narrow[pl.ds(h, total, stride=block), :].astype(BF16)
        wide[pl.ds(h, total, stride=2 * block), :] = dot(d_tri, matrices[block + h], 1, 0)
        wide[pl.ds(block + h, total, stride=2 * block), :] = dot(d_tri, matrices[h], 0, 0)
    d_panels[...] = wide[...].astype(BF16).reshape(d_panels.shape)


def finish_kernel(d_panels, slopes, d_zln_gate, pair, gain, w_proj, grad):
    rows = pair.shape[0]
    count, depth, width = d_panels.shape
    block = depth // rows // 2
    hidden = count * block
    w_flip = transposed(w_proj[...])
    for row in range(rows):
        both = d_panels[:, row * 2 * block : (row + 1) * 2 * block, :].astype(F32)
        parts = []
        for side in range(2):
            d_value = both[:, side * block : (side + 1) * block, :].reshape(hidden, width)
            base = 2 * side * hidden
            parts.append(d_value * slopes[row, base : base + hidden, :])
            parts.append(d_value * slopes[row, base + hidden : base + 2 * hidden, :])
        d_proj = jnp.concatenate(parts, axis=0).astype(BF16)
        d_zln = dot(d_proj, w_flip, 0, 0) + d_zln_gate[row]
        d_in = d_zln * gain[...]
        normed, inv_std = input_norm(pair[row])
        mean_grad = jnp.mean(d_in, axis=-1, keepdims=True)
        mean_cross = jnp.mean(d_in * normed, axis=-1, keepdims=True)
        grad[row] = (inv_std * (d_in - mean_grad - normed * mean_cross)).astype(BF16)


def swap(values):
    return lax.all_to_all(values, "row", split_axis=0, concat_axis=0, tiled=True)


def kernel_shards(
    pair,
    cotangent,
    residue_mask,
    ln_in_gain,
    ln_in_bias,
    w_proj,
    w_gate,
    ln_out_gain,
    ln_out_bias,
    w_out,
):
    rows, width, channels = pair.shape
    hidden = w_out.shape[0]
    count = lax.axis_size("row")
    block = hidden // count
    total = rows * count
    shape = jax.ShapeDtypeStruct
    mask_vector = residue_mask.reshape(1, width)
    gain, bias = ln_in_gain.reshape(1, channels), ln_in_bias.reshape(1, channels)
    out_gain, out_bias = ln_out_gain.reshape(hidden, 1), ln_out_bias.reshape(hidden, 1)
    cells = rows * width
    (panels,) = call(
        project_kernel,
        "project",
        [shape((count, rows * 2 * block, width), BF16)],
        [pair, residue_mask, mask_vector, gain, bias, w_proj],
        smem=(1,),
        flops=2 * cells * channels * 4 * hidden,
    )
    panels = swap(panels)
    d_hat_centered, gate_slope, slopes = call(
        prepare_kernel,
        "prepare",
        [
            shape((rows, hidden, width), F32),
            shape((rows, width, channels), F32),
            shape((rows, 4 * hidden, width), F32),
        ],
        [pair, cotangent, residue_mask, mask_vector, gain, bias, w_proj, w_gate, out_gain, w_out],
        smem=(2,),
        flops=2 * cells * channels * 6 * hidden,
    )
    wide = pltpu.VMEM((total * 2 * block, width), F32)
    narrow = pltpu.VMEM((total * block, width), F32)
    products, matrices = call(
        tri_kernel,
        "tri",
        [shape((count, rows * block, width), BF16), shape((2 * block, total, width), BF16)],
        [panels],
        scratch=[wide, narrow],
        flops=2 * block * total * width * total,
    )
    products = swap(products)
    (d_products,) = call(
        middle_kernel,
        "middle",
        [shape((count, rows * block, width), BF16)],
        [products, d_hat_centered],
        flops=20 * cells * hidden,
    )
    d_products = swap(d_products)
    (d_zln_gate,) = call(
        gate_back_kernel,
        "gate_back",
        [shape((rows, width, channels), F32)],
        [products, gate_slope, out_gain, out_bias, w_out, w_gate],
        flops=4 * cells * channels * hidden,
    )
    (d_panels,) = call(
        products_kernel,
        "products",
        [shape((count, rows * 2 * block, width), BF16)],
        [d_products, matrices],
        scratch=[narrow, wide],
        flops=4 * block * total * width * total,
    )
    d_panels = swap(d_panels)
    (grad,) = call(
        finish_kernel,
        "finish",
        [shape(pair.shape, BF16)],
        [d_panels, slopes, d_zln_gate, pair, gain, w_proj],
        flops=2 * cells * channels * 4 * hidden,
    )
    return grad


def normalize(values, reduce_axis):
    mean_value = jnp.mean(values, axis=reduce_axis, keepdims=True)
    centered = values - mean_value
    variance = jnp.mean(centered * centered, axis=reduce_axis, keepdims=True)
    inv_std = lax.rsqrt(variance + 1e-05)
    return (centered * inv_std, inv_std)


def norm_backward(upstream, normed, inv_std, reduce_axis):
    mean_grad = jnp.mean(upstream, axis=reduce_axis, keepdims=True)
    mean_cross = jnp.mean(upstream * normed, axis=reduce_axis, keepdims=True)
    return inv_std * (upstream - mean_grad - normed * mean_cross)


def shards(
    pair,
    cotangent,
    residue_mask,
    ln_in_gain,
    ln_in_bias,
    w_proj,
    w_gate,
    ln_out_gain,
    ln_out_bias,
    w_out,
):
    local_rows = pair.shape[0]
    local_cols = pair.shape[1]
    hidden = w_out.shape[0]
    chan_index = lax.axis_index("chan")
    row_start = lax.axis_index("row") * local_rows
    col_start = chan_index * local_cols
    mask_float = residue_mask.astype(jnp.float32)
    row_mask = lax.dynamic_slice_in_dim(mask_float, row_start, local_rows)
    col_mask = lax.dynamic_slice_in_dim(mask_float, col_start, local_cols)
    cell_mask = (row_mask[:, None] * col_mask[None, :])[None]
    normed, inv_std = normalize(pair.astype(jnp.float32), -1)
    normed_pair = (normed * ln_in_gain + ln_in_bias).astype(jnp.bfloat16)
    projected = jnp.einsum("rmc,ch->hrm", normed_pair, w_proj, preferred_element_type=jnp.float32)
    left_panel = (
        cell_mask * jax.nn.sigmoid(projected[:hidden]) * projected[hidden : 2 * hidden]
    ).astype(jnp.bfloat16)
    right_panel = (
        cell_mask * jax.nn.sigmoid(projected[2 * hidden : 3 * hidden]) * projected[3 * hidden :]
    ).astype(jnp.bfloat16)
    panels = lax.all_to_all(
        jnp.stack([left_panel, right_panel]), "row", split_axis=1, concat_axis=2, tiled=True
    )
    left_all = panels[0]
    right_all = panels[1]
    right_rows = lax.all_to_all(right_all, "chan", split_axis=1, concat_axis=2, tiled=True)
    partner = right_rows
    tri_part = jnp.einsum(
        "gik,gjk->gij",
        lax.all_gather(left_all, "chan", axis=2, tiled=True),
        partner,
        preferred_element_type=jnp.float32,
    ).astype(jnp.bfloat16)
    tri_cells = lax.all_to_all(tri_part, "row", split_axis=1, concat_axis=0, tiled=True)
    tri_hat, inv_tri = normalize(tri_cells.astype(jnp.float32), 0)
    scaled = (tri_hat * ln_out_gain[:, None, None] + ln_out_bias[:, None, None]).astype(
        jnp.bfloat16
    )
    proj_out = jnp.einsum("hrm,hc->rmc", scaled, w_out, preferred_element_type=jnp.float32)
    gate_value = jax.nn.sigmoid(
        jnp.einsum("rmc,cd->rmd", normed_pair, w_gate, preferred_element_type=jnp.float32)
    )
    cot_float = cotangent.astype(jnp.float32)
    d_gate_pre = (cot_float * proj_out * gate_value * (1.0 - gate_value)).astype(jnp.bfloat16)
    d_scaled = (cot_float * gate_value).astype(jnp.bfloat16)
    d_hat = jnp.einsum("rmc,hc->hrm", d_scaled, w_out, preferred_element_type=jnp.float32)
    d_hat = d_hat * ln_out_gain[:, None, None]
    d_tri = norm_backward(d_hat, tri_hat, inv_tri, 0).astype(jnp.bfloat16)
    d_tri_all = lax.all_to_all(d_tri, "row", split_axis=0, concat_axis=1, tiled=True)
    panel_piece = lax.all_gather(d_tri_all, "chan", axis=2, tiled=True)
    partner = right_all
    d_left = jnp.einsum("gij,gjk->gik", panel_piece, partner, preferred_element_type=jnp.float32)
    contribution = jnp.einsum(
        "gij,gik->gjk", panel_piece, left_all, preferred_element_type=jnp.float32
    )
    d_right = contribution
    d_left, d_right = (d_left, d_right)
    d_stack = jnp.stack([d_left, d_right]).astype(jnp.bfloat16)
    d_panels = lax.all_to_all(d_stack, "row", split_axis=2, concat_axis=1, tiled=True)

    def gating(d_value, gate_proj, value_proj):
        sigmoid_val = jax.nn.sigmoid(gate_proj)
        masked_grad = d_value.astype(jnp.float32) * cell_mask
        return (
            masked_grad * value_proj * sigmoid_val * (1.0 - sigmoid_val),
            masked_grad * sigmoid_val,
        )

    gate_left, value_left = gating(d_panels[0], projected[:hidden], projected[hidden : 2 * hidden])
    gate_right, value_right = gating(
        d_panels[1], projected[2 * hidden : 3 * hidden], projected[3 * hidden :]
    )
    d_proj = jnp.concatenate([gate_left, value_left, gate_right, value_right], axis=0).astype(
        jnp.bfloat16
    )
    d_normed = jnp.einsum("hrm,ch->rmc", d_proj, w_proj, preferred_element_type=jnp.float32)
    d_normed = d_normed + jnp.einsum(
        "rmd,cd->rmc", d_gate_pre, w_gate, preferred_element_type=jnp.float32
    )
    d_input = d_normed * ln_in_gain
    return norm_backward(d_input, normed, inv_std, -1).astype(jnp.bfloat16)


def solution(mesh):
    fits = mesh.shape["chan"] == 1 and mesh.shape["row"] <= 16
    return jax.shard_map(
        kernel_shards if fits else shards,
        mesh=mesh,
        in_specs=(
            P(("grp", "row"), "chan", None),
            P(("grp", "row"), "chan", None),
            P("grp"),
            P(),
            P(),
            P(),
            P(),
            P(),
            P(),
            P(),
        ),
        out_specs=P(("grp", "row"), "chan", None),
        check_vma=False,
    )
```

```python
import functools

import jax
import jax.numpy as jnp
from jax import lax
from jax.experimental import pallas as pl
from jax.experimental.pallas import tpu as pltpu
from jax.sharding import PartitionSpec as P

F32 = jnp.float32
BF16 = jnp.bfloat16
VMEM_LIMIT = 16 * 1024 * 1024


def dot(lhs, rhs, lhs_dim, rhs_dim):
    return lax.dot_general(
        lhs, rhs, (((lhs_dim,), (rhs_dim,)), ((), ())), preferred_element_type=F32
    )


def transposed(matrix):
    return jnp.transpose(matrix.astype(F32)).astype(BF16)


def sigmoid(values):
    return 1.0 / (1.0 + jnp.exp(-values))


def column(row):
    size = row.shape[1]
    return jnp.transpose(jnp.broadcast_to(row, (size, size)))


def norm_rows(values):
    centered = values - jnp.mean(values, axis=0, keepdims=True)
    variance = jnp.mean(centered * centered, axis=0, keepdims=True)
    inv_std = lax.rsqrt(variance + 1e-05)
    return centered * inv_std, inv_std


def call(kernel, name, outs, args, fetched=(), scratch=(), flops=0, limit=VMEM_LIMIT):
    moved = sum(a.size * a.dtype.itemsize for a in args) + sum(
        o.size * jnp.dtype(o.dtype).itemsize for o in outs
    )
    n_args, n_outs, n_fetched = len(args), len(outs), len(fetched)

    def body(*refs):
        ins = list(refs[:n_args])
        rest = refs[n_args + n_outs :]
        copies = []
        for n, place in enumerate(fetched):
            copies.append(pltpu.make_async_copy(ins[place], rest[n], rest[n_fetched].at[n]))
            ins[place] = rest[n]
        for copy in copies:
            copy.start()
        for copy in copies:
            copy.wait()
        kernel(*ins, *refs[n_args : n_args + n_outs], *rest[n_fetched + (n_fetched > 0) :])

    buffers = [pltpu.VMEM(args[place].shape, args[place].dtype) for place in fetched]
    if fetched:
        buffers.append(pltpu.SemaphoreType.DMA((n_fetched,)))
    return pl.pallas_call(
        body,
        name=name,
        out_shape=outs,
        in_specs=[
            pl.BlockSpec(memory_space=pltpu.HBM if n in fetched else pltpu.VMEM)
            for n in range(n_args)
        ],
        out_specs=[pl.BlockSpec(memory_space=pltpu.VMEM) for _ in outs],
        scratch_shapes=buffers + list(scratch),
        compiler_params=pltpu.CompilerParams(vmem_limit_bytes=limit),
        cost_estimate=pl.CostEstimate(flops=flops, bytes_accessed=moved, transcendentals=0),
    )(*args)


def cell_masks(mask, rows):
    columns = mask[...].astype(F32)
    shape = (rows, columns.shape[1])
    first = lax.axis_index("row") * rows
    own = lax.broadcasted_iota(jnp.int32, shape, 1) == (
        lax.broadcasted_iota(jnp.int32, shape, 0) + first
    )
    row_mask = jnp.sum(jnp.where(own, columns, 0.0), axis=1, keepdims=True)
    cells = row_mask * columns
    return [cells[row : row + 1] for row in range(rows)]


def project_kernel(pair, mask, gain, bias, w_proj, panels):
    rows = pair.shape[0]
    hidden = w_proj.shape[1] // 4
    count, _, width = panels.shape
    block = hidden // count
    w_flip = transposed(w_proj[...])
    gain_col, bias_col = column(gain[...]), column(bias[...])
    masks = cell_masks(mask, rows)
    for row in range(rows):
        normed, _ = norm_rows(jnp.transpose(pair[row].astype(F32)))
        zln = (normed * gain_col + bias_col).astype(BF16)
        proj = dot(w_flip, zln, 1, 0)
        left = masks[row] * sigmoid(proj[:hidden]) * proj[hidden : 2 * hidden]
        right = masks[row] * sigmoid(proj[2 * hidden : 3 * hidden]) * proj[3 * hidden :]
        both = jnp.concatenate(
            [left.reshape(count, block, width), right.reshape(count, block, width)], axis=1
        )
        panels[:, row * 2 * block : (row + 1) * 2 * block, :] = both.astype(BF16)


def prepare_kernel(
    pair, cotangent, gain, bias, w_gate, out_gain, w_out, d_hat_centered, gate_slope
):
    gate_flip = transposed(w_gate[...])
    gain_col, bias_col = column(gain[...]), column(bias[...])
    out_gain_col = column(out_gain[...])
    for row in range(pair.shape[0]):
        normed, _ = norm_rows(jnp.transpose(pair[row].astype(F32)))
        zln = (normed * gain_col + bias_col).astype(BF16)
        gate = sigmoid(dot(gate_flip, zln, 1, 0))
        cot = jnp.transpose(cotangent[row].astype(F32))
        d_scaled = (cot * gate).astype(BF16)
        d_hat = dot(w_out[...], d_scaled, 1, 0) * out_gain_col
        d_hat_centered[row] = d_hat - jnp.mean(d_hat, axis=0, keepdims=True)
        gate_slope[row] = cot * gate * (1.0 - gate)


def tri_kernel(panels, products, matrices, wide, narrow):
    count, depth, width = panels.shape
    block = matrices.shape[0] // 2
    total = matrices.shape[1]
    wide[...] = panels[...].astype(F32).reshape(count * depth, width)
    for h in range(block):
        left = wide[pl.ds(h, total, stride=2 * block), :].astype(BF16)
        right = wide[pl.ds(block + h, total, stride=2 * block), :].astype(BF16)
        matrices[h] = left
        matrices[block + h] = right
        narrow[pl.ds(h, total, stride=block), :] = dot(left, right, 1, 1)
    products[...] = narrow[...].astype(BF16).reshape(products.shape)


def row_pair(ref, first, block):
    count, _, width = ref.shape
    both = ref[:, first * block : (first + 2) * block, :].astype(F32)
    return [
        both[:, n * block : (n + 1) * block, :].reshape(count * block, width) for n in range(2)
    ]


def middle_kernel(products, d_hat_centered, d_products):
    rows, hidden, width = d_hat_centered.shape
    count = products.shape[0]
    block = hidden // count
    for first in range(0, rows, 2):
        parts = []
        for n, tri in enumerate(row_pair(products, first, block)):
            tri_hat, inv_std = norm_rows(tri)
            d_hat = d_hat_centered[first + n]
            cross = jnp.mean(d_hat * tri_hat, axis=0, keepdims=True)
            d_tri = inv_std * (d_hat - tri_hat * cross)
            parts.append(d_tri.reshape(count, block, width))
        d_products[:, first * block : (first + 2) * block, :] = jnp.concatenate(
            parts, axis=1
        ).astype(BF16)


def products_kernel(d_products, matrices, d_panels, narrow, wide):
    count, depth, width = d_products.shape
    block = matrices.shape[0] // 2
    total = matrices.shape[1]
    narrow[...] = d_products[...].astype(F32).reshape(count * depth, width)
    for h in range(block):
        d_tri = narrow[pl.ds(h, total, stride=block), :].astype(BF16)
        wide[pl.ds(h, total, stride=2 * block), :] = dot(d_tri, matrices[block + h], 1, 0)
        wide[pl.ds(block + h, total, stride=2 * block), :] = dot(d_tri, matrices[h], 0, 0)
    d_panels[...] = wide[...].astype(BF16).reshape(d_panels.shape)


def slopes_kernel(
    products,
    gate_slope,
    pair,
    mask,
    gain,
    bias,
    w_proj,
    w_gate,
    out_gain,
    out_bias,
    w_out,
    slopes,
    d_zln_gate,
    normed_in,
    inv_in,
):
    rows = pair.shape[0]
    hidden = w_out.shape[0]
    block = hidden // products.shape[0]
    w_flip = transposed(w_proj[...])
    out_flip = transposed(w_out[...])
    gain_col, bias_col = column(gain[...]), column(bias[...])
    out_gain_col, out_bias_col = column(out_gain[...]), column(out_bias[...])
    masks = cell_masks(mask, rows)
    for row in range(rows):
        tri_hat, _ = norm_rows(row_pair(products, row - row % 2, block)[row % 2])
        scaled = (tri_hat * out_gain_col + out_bias_col).astype(BF16)
        d_gate_pre = (dot(out_flip, scaled, 1, 0) * gate_slope[row]).astype(BF16)
        d_zln_gate[row] = dot(w_gate[...], d_gate_pre, 1, 0)
        normed, inv_std = norm_rows(jnp.transpose(pair[row].astype(F32)))
        normed_in[row] = normed
        inv_in[row : row + 1] = inv_std
        zln = (normed * gain_col + bias_col).astype(BF16)
        proj = dot(w_flip, zln, 1, 0)
        for side in range(2):
            base = 2 * side * hidden
            sig = sigmoid(proj[base : base + hidden])
            masked = masks[row] * sig
            value = masked * (1.0 - sig) * proj[base + hidden : base + 2 * hidden]
            slopes[row, base : base + hidden, :] = value.astype(slopes.dtype)
            slopes[row, base + hidden : base + 2 * hidden, :] = masked.astype(slopes.dtype)


def finish_kernel(d_panels, slopes, d_zln_gate, normed_in, inv_in, gain, w_proj, grad):
    rows = grad.shape[0]
    count, depth, width = d_panels.shape
    block = depth // rows // 2
    hidden = count * block
    gain_col = column(gain[...])
    for row in range(rows):
        both = d_panels[:, row * 2 * block : (row + 1) * 2 * block, :].astype(F32)
        parts = []
        for side in range(2):
            d_value = both[:, side * block : (side + 1) * block, :].reshape(hidden, width)
            for base in (2 * side * hidden, (2 * side + 1) * hidden):
                slope = slopes[row, base : base + hidden, :].astype(F32)
                parts.append((d_value * slope).astype(BF16))
        d_zln = dot(w_proj[...], jnp.concatenate(parts, axis=0), 1, 0) + d_zln_gate[row]
        d_in = d_zln * gain_col
        normed = normed_in[row]
        mean_grad = jnp.mean(d_in, axis=0, keepdims=True)
        mean_cross = jnp.mean(d_in * normed, axis=0, keepdims=True)
        result = inv_in[row : row + 1] * (d_in - mean_grad - normed * mean_cross)
        grad[row] = jnp.transpose(result).astype(BF16)


def swap(values):
    return lax.all_to_all(values, "row", split_axis=0, concat_axis=0, tiled=True)


def kernel_shards(
    pair,
    cotangent,
    residue_mask,
    ln_in_gain,
    ln_in_bias,
    w_proj,
    w_gate,
    ln_out_gain,
    ln_out_bias,
    w_out,
):
    rows, width, channels = pair.shape
    hidden = w_out.shape[0]
    count = lax.axis_size("row")
    block = hidden // count
    total = rows * count
    shape = jax.ShapeDtypeStruct
    mask = residue_mask.reshape(1, width)
    gain, bias = ln_in_gain.reshape(1, channels), ln_in_bias.reshape(1, channels)
    out_gain, out_bias = ln_out_gain.reshape(1, hidden), ln_out_bias.reshape(1, hidden)
    cells = rows * width
    (panels,) = call(
        project_kernel,
        "project",
        [shape((count, rows * 2 * block, width), BF16)],
        [pair, mask, gain, bias, w_proj],
        fetched=range(5),
        flops=2 * cells * channels * 4 * hidden,
        limit=64 * 1024 * 1024 - 640 * 1024,
    )
    panels = swap(panels)
    d_hat_centered, gate_slope = call(
        prepare_kernel,
        "prepare",
        [shape((rows, hidden, width), F32), shape((rows, channels, width), F32)],
        [pair, cotangent, gain, bias, w_gate, out_gain, w_out],
        fetched=range(7),
        flops=2 * cells * channels * 2 * hidden,
    )
    wide = pltpu.VMEM((total * 2 * block, width), F32)
    narrow = pltpu.VMEM((total * block, width), F32)
    products, matrices = call(
        tri_kernel,
        "tri",
        [shape((count, rows * block, width), BF16), shape((2 * block, total, width), BF16)],
        [panels],
        scratch=[wide, narrow],
        flops=2 * block * total * width * total,
    )
    products = swap(products)
    (d_products,) = call(
        middle_kernel,
        "middle",
        [shape((count, rows * block, width), BF16)],
        [products, d_hat_centered],
        flops=20 * cells * hidden,
    )
    d_products = swap(d_products)
    (d_panels,) = call(
        products_kernel,
        "products",
        [shape((count, rows * 2 * block, width), BF16)],
        [d_products, matrices],
        scratch=[narrow, wide],
        flops=4 * block * total * width * total,
    )
    d_panels = swap(d_panels)
    slopes, d_zln_gate, normed_in, inv_in = call(
        slopes_kernel,
        "slopes",
        [
            shape((rows, 4 * hidden, width), BF16),
            shape((rows, channels, width), F32),
            shape((rows, channels, width), F32),
            shape((rows, width), F32),
        ],
        [
            products,
            gate_slope,
            pair,
            mask,
            gain,
            bias,
            w_proj,
            w_gate,
            out_gain,
            out_bias,
            w_out,
        ],
        fetched=range(2, 11),
        flops=2 * cells * channels * 6 * hidden,
    )
    (grad,) = call(
        finish_kernel,
        "finish",
        [shape(pair.shape, BF16)],
        [d_panels, slopes, d_zln_gate, normed_in, inv_in, gain, w_proj],
        fetched=(5, 6),
        flops=2 * cells * channels * 4 * hidden,
    )
    return grad


def normalize(values, reduce_axis):
    mean_value = jnp.mean(values, axis=reduce_axis, keepdims=True)
    centered = values - mean_value
    variance = jnp.mean(centered * centered, axis=reduce_axis, keepdims=True)
    inv_std = lax.rsqrt(variance + 1e-05)
    return (centered * inv_std, inv_std)


def norm_backward(upstream, normed, inv_std, reduce_axis):
    mean_grad = jnp.mean(upstream, axis=reduce_axis, keepdims=True)
    mean_cross = jnp.mean(upstream * normed, axis=reduce_axis, keepdims=True)
    return inv_std * (upstream - mean_grad - normed * mean_cross)


def shards(
    pair,
    cotangent,
    residue_mask,
    ln_in_gain,
    ln_in_bias,
    w_proj,
    w_gate,
    ln_out_gain,
    ln_out_bias,
    w_out,
):
    local_rows = pair.shape[0]
    local_cols = pair.shape[1]
    hidden = w_out.shape[0]
    chan_index = lax.axis_index("chan")
    row_start = lax.axis_index("row") * local_rows
    col_start = chan_index * local_cols
    mask_float = residue_mask.astype(jnp.float32)
    row_mask = lax.dynamic_slice_in_dim(mask_float, row_start, local_rows)
    col_mask = lax.dynamic_slice_in_dim(mask_float, col_start, local_cols)
    cell_mask = (row_mask[:, None] * col_mask[None, :])[None]
    normed, inv_std = normalize(pair.astype(jnp.float32), -1)
    normed_pair = (normed * ln_in_gain + ln_in_bias).astype(jnp.bfloat16)
    projected = jnp.einsum("rmc,ch->hrm", normed_pair, w_proj, preferred_element_type=jnp.float32)
    left_panel = (
        cell_mask * jax.nn.sigmoid(projected[:hidden]) * projected[hidden : 2 * hidden]
    ).astype(jnp.bfloat16)
    right_panel = (
        cell_mask * jax.nn.sigmoid(projected[2 * hidden : 3 * hidden]) * projected[3 * hidden :]
    ).astype(jnp.bfloat16)
    panels = lax.all_to_all(
        jnp.stack([left_panel, right_panel]), "row", split_axis=1, concat_axis=2, tiled=True
    )
    left_all = panels[0]
    right_all = panels[1]
    right_rows = lax.all_to_all(right_all, "chan", split_axis=1, concat_axis=2, tiled=True)
    partner = right_rows
    tri_part = jnp.einsum(
        "gik,gjk->gij",
        lax.all_gather(left_all, "chan", axis=2, tiled=True),
        partner,
        preferred_element_type=jnp.float32,
    ).astype(jnp.bfloat16)
    tri_cells = lax.all_to_all(tri_part, "row", split_axis=1, concat_axis=0, tiled=True)
    tri_hat, inv_tri = normalize(tri_cells.astype(jnp.float32), 0)
    scaled = (tri_hat * ln_out_gain[:, None, None] + ln_out_bias[:, None, None]).astype(
        jnp.bfloat16
    )
    proj_out = jnp.einsum("hrm,hc->rmc", scaled, w_out, preferred_element_type=jnp.float32)
    gate_value = jax.nn.sigmoid(
        jnp.einsum("rmc,cd->rmd", normed_pair, w_gate, preferred_element_type=jnp.float32)
    )
    cot_float = cotangent.astype(jnp.float32)
    d_gate_pre = (cot_float * proj_out * gate_value * (1.0 - gate_value)).astype(jnp.bfloat16)
    d_scaled = (cot_float * gate_value).astype(jnp.bfloat16)
    d_hat = jnp.einsum("rmc,hc->hrm", d_scaled, w_out, preferred_element_type=jnp.float32)
    d_hat = d_hat * ln_out_gain[:, None, None]
    d_tri = norm_backward(d_hat, tri_hat, inv_tri, 0).astype(jnp.bfloat16)
    d_tri_all = lax.all_to_all(d_tri, "row", split_axis=0, concat_axis=1, tiled=True)
    panel_piece = lax.all_gather(d_tri_all, "chan", axis=2, tiled=True)
    partner = right_all
    d_left = jnp.einsum("gij,gjk->gik", panel_piece, partner, preferred_element_type=jnp.float32)
    contribution = jnp.einsum(
        "gij,gik->gjk", panel_piece, left_all, preferred_element_type=jnp.float32
    )
    d_right = contribution
    d_left, d_right = (d_left, d_right)
    d_stack = jnp.stack([d_left, d_right]).astype(jnp.bfloat16)
    d_panels = lax.all_to_all(d_stack, "row", split_axis=2, concat_axis=1, tiled=True)

    def gating(d_value, gate_proj, value_proj):
        sigmoid_val = jax.nn.sigmoid(gate_proj)
        masked_grad = d_value.astype(jnp.float32) * cell_mask
        return (
            masked_grad * value_proj * sigmoid_val * (1.0 - sigmoid_val),
            masked_grad * sigmoid_val,
        )

    gate_left, value_left = gating(d_panels[0], projected[:hidden], projected[hidden : 2 * hidden])
    gate_right, value_right = gating(
        d_panels[1], projected[2 * hidden : 3 * hidden], projected[3 * hidden :]
    )
    d_proj = jnp.concatenate([gate_left, value_left, gate_right, value_right], axis=0).astype(
        jnp.bfloat16
    )
    d_normed = jnp.einsum("hrm,ch->rmc", d_proj, w_proj, preferred_element_type=jnp.float32)
    d_normed = d_normed + jnp.einsum(
        "rmd,cd->rmc", d_gate_pre, w_gate, preferred_element_type=jnp.float32
    )
    d_input = d_normed * ln_in_gain
    return norm_backward(d_input, normed, inv_std, -1).astype(jnp.bfloat16)


def solution(mesh):
    fits = mesh.shape["chan"] == 1 and mesh.shape["row"] <= 16
    return jax.shard_map(
        kernel_shards if fits else shards,
        mesh=mesh,
        in_specs=(
            P(("grp", "row"), "chan", None),
            P(("grp", "row"), "chan", None),
            P("grp"),
            P(),
            P(),
            P(),
            P(),
            P(),
            P(),
            P(),
        ),
        out_specs=P(("grp", "row"), "chan", None),
        check_vma=False,
    )
```

```python
import functools

import jax
import jax.numpy as jnp
from jax import lax
from jax.experimental import pallas as pl
from jax.experimental.pallas import tpu as pltpu
from jax.sharding import PartitionSpec as P

F32 = jnp.float32
BF16 = jnp.bfloat16
VMEM_LIMIT = 16 * 1024 * 1024


def dot(lhs, rhs, lhs_dim, rhs_dim):
    return lax.dot_general(
        lhs, rhs, (((lhs_dim,), (rhs_dim,)), ((), ())), preferred_element_type=F32
    )


def transposed(matrix):
    return jnp.transpose(matrix.astype(F32)).astype(BF16)


def sigmoid(values):
    return 1.0 / (1.0 + jnp.exp(-values))


def column(row):
    size = row.shape[1]
    return jnp.transpose(jnp.broadcast_to(row, (size, size)))


def norm_rows(values):
    centered = values - jnp.mean(values, axis=0, keepdims=True)
    variance = jnp.mean(centered * centered, axis=0, keepdims=True)
    inv_std = lax.rsqrt(variance + 1e-05)
    return centered * inv_std, inv_std


def call(kernel, name, outs, args, fetched=(), scratch=(), flops=0, limit=VMEM_LIMIT):
    moved = sum(a.size * a.dtype.itemsize for a in args) + sum(
        o.size * jnp.dtype(o.dtype).itemsize for o in outs
    )
    n_args, n_outs, n_fetched = len(args), len(outs), len(fetched)

    def body(*refs):
        ins = list(refs[:n_args])
        rest = refs[n_args + n_outs :]
        copies = []
        for n, place in enumerate(fetched):
            copies.append(pltpu.make_async_copy(ins[place], rest[n], rest[n_fetched].at[n]))
            ins[place] = rest[n]
        for copy in copies:
            copy.start()
        for copy in copies:
            copy.wait()
        kernel(*ins, *refs[n_args : n_args + n_outs], *rest[n_fetched + (n_fetched > 0) :])

    buffers = [pltpu.VMEM(args[place].shape, args[place].dtype) for place in fetched]
    if fetched:
        buffers.append(pltpu.SemaphoreType.DMA((n_fetched,)))
    return pl.pallas_call(
        body,
        name=name,
        out_shape=outs,
        in_specs=[
            pl.BlockSpec(memory_space=pltpu.HBM if n in fetched else pltpu.VMEM)
            for n in range(n_args)
        ],
        out_specs=[pl.BlockSpec(memory_space=pltpu.VMEM) for _ in outs],
        scratch_shapes=buffers + list(scratch),
        compiler_params=pltpu.CompilerParams(vmem_limit_bytes=limit),
        cost_estimate=pl.CostEstimate(flops=flops, bytes_accessed=moved, transcendentals=0),
    )(*args)


def cell_masks(mask, rows):
    columns = mask[...].astype(F32)
    shape = (rows, columns.shape[1])
    first = lax.axis_index("row") * rows
    own = lax.broadcasted_iota(jnp.int32, shape, 1) == (
        lax.broadcasted_iota(jnp.int32, shape, 0) + first
    )
    row_mask = jnp.sum(jnp.where(own, columns, 0.0), axis=1, keepdims=True)
    cells = row_mask * columns
    return [cells[row : row + 1] for row in range(rows)]


def project_kernel(pair, mask, gain, bias, w_proj, left_panel, right_panel):
    rows = pair.shape[0]
    hidden = w_proj.shape[1] // 4
    count, depth, width = left_panel.shape
    block = depth // rows
    halves = right_panel.shape[0] // count
    w_flip = transposed(w_proj[...])
    gain_col, bias_col = column(gain[...]), column(bias[...])
    masks = cell_masks(mask, rows)
    for row in range(rows):
        normed, _ = norm_rows(jnp.transpose(pair[row].astype(F32)))
        zln = (normed * gain_col + bias_col).astype(BF16)
        proj = dot(w_flip, zln, 1, 0)
        place = slice(row * block, (row + 1) * block)
        left = masks[row] * sigmoid(proj[:hidden]) * proj[hidden : 2 * hidden]
        left_panel[:, place, :] = left.reshape(count, block, width).astype(BF16)
        right = masks[row] * sigmoid(proj[2 * hidden : 3 * hidden]) * proj[3 * hidden :]
        right = right.reshape(count, block, width).astype(BF16)
        for half in range(halves):
            right_panel[half * count : (half + 1) * count, place, :] = right


def prepare_kernel(
    pair, cotangent, gain, bias, w_gate, out_gain, w_out, d_hat_centered, gate_slope
):
    gate_flip = transposed(w_gate[...])
    gain_col, bias_col = column(gain[...]), column(bias[...])
    out_gain_col = column(out_gain[...])
    for row in range(pair.shape[0]):
        normed, _ = norm_rows(jnp.transpose(pair[row].astype(F32)))
        zln = (normed * gain_col + bias_col).astype(BF16)
        gate = sigmoid(dot(gate_flip, zln, 1, 0))
        cot = jnp.transpose(cotangent[row].astype(F32))
        d_scaled = (cot * gate).astype(BF16)
        d_hat = dot(w_out[...], d_scaled, 1, 0) * out_gain_col
        d_hat_centered[row] = d_hat - jnp.mean(d_hat, axis=0, keepdims=True)
        gate_slope[row] = cot * gate * (1.0 - gate)


def spread(panel, wide):
    wide[...] = panel[...].astype(F32).reshape(wide.shape)


def tri_kernel(left_panel, right_panel, products, left_all, right_all, left_wide, right_wide):
    block, left_rows, _ = left_all.shape
    right_rows = right_all.shape[1]
    spread(left_panel, left_wide)
    spread(right_panel, right_wide)
    for h in range(block):
        left_all[h] = left_wide[pl.ds(h, left_rows, stride=block), :].astype(BF16)
        right_all[h] = right_wide[pl.ds(h, right_rows, stride=block), :].astype(BF16)
        left_wide[pl.ds(h, left_rows, stride=block), :] = dot(left_all[h], right_all[h], 1, 1)
    products[...] = left_wide[...].astype(BF16).reshape(products.shape)


def cell_row(ref, row, rows):
    count, depth, width = ref.shape
    block = depth // rows
    return ref[:, row * block : (row + 1) * block, :].astype(F32).reshape(count * block, width)


def middle_kernel(products, d_hat_centered, d_products):
    rows = d_hat_centered.shape[0]
    count, depth, width = products.shape
    block = depth // rows
    for row in range(rows):
        tri_hat, inv_std = norm_rows(cell_row(products, row, rows))
        d_hat = d_hat_centered[row]
        cross = jnp.mean(d_hat * tri_hat, axis=0, keepdims=True)
        d_tri = inv_std * (d_hat - tri_hat * cross)
        d_products[:, row * block : (row + 1) * block, :] = d_tri.reshape(
            count, block, width
        ).astype(BF16)


def products_kernel(
    d_products, left_all, right_all, d_left_panel, d_right_panel, left_wide, right_wide
):
    block, left_rows, _ = left_all.shape
    right_rows = right_all.shape[1]
    spread(d_products, left_wide)
    for h in range(block):
        d_tri = left_wide[pl.ds(h, left_rows, stride=block), :].astype(BF16)
        left_wide[pl.ds(h, left_rows, stride=block), :] = dot(d_tri, right_all[h], 1, 0)
        right_wide[pl.ds(h, right_rows, stride=block), :] = dot(d_tri, left_all[h], 0, 0)
    d_left_panel[...] = left_wide[...].astype(BF16).reshape(d_left_panel.shape)
    d_right_panel[...] = right_wide[...].astype(BF16).reshape(d_right_panel.shape)


def slopes_kernel(
    products,
    gate_slope,
    pair,
    mask,
    gain,
    bias,
    w_proj,
    w_gate,
    out_gain,
    out_bias,
    w_out,
    slopes,
    d_zln_gate,
    normed_in,
    inv_in,
):
    rows = pair.shape[0]
    hidden = w_out.shape[0]
    w_flip = transposed(w_proj[...])
    out_flip = transposed(w_out[...])
    gain_col, bias_col = column(gain[...]), column(bias[...])
    out_gain_col, out_bias_col = column(out_gain[...]), column(out_bias[...])
    masks = cell_masks(mask, rows)
    for row in range(rows):
        tri_hat, _ = norm_rows(cell_row(products, row, rows))
        scaled = (tri_hat * out_gain_col + out_bias_col).astype(BF16)
        d_gate_pre = (dot(out_flip, scaled, 1, 0) * gate_slope[row]).astype(BF16)
        d_zln_gate[row] = dot(w_gate[...], d_gate_pre, 1, 0)
        normed, inv_std = norm_rows(jnp.transpose(pair[row].astype(F32)))
        normed_in[row] = normed
        inv_in[row : row + 1] = inv_std
        zln = (normed * gain_col + bias_col).astype(BF16)
        proj = dot(w_flip, zln, 1, 0)
        for side in range(2):
            base = 2 * side * hidden
            sig = sigmoid(proj[base : base + hidden])
            masked = masks[row] * sig
            value = masked * (1.0 - sig) * proj[base + hidden : base + 2 * hidden]
            slopes[row, base : base + hidden, :] = value.astype(slopes.dtype)
            slopes[row, base + hidden : base + 2 * hidden, :] = masked.astype(slopes.dtype)


def finish_kernel(
    d_left_panel, d_right_panel, slopes, d_zln_gate, normed_in, inv_in, gain, w_proj, grad
):
    rows = grad.shape[0]
    count, depth, width = d_left_panel.shape
    hidden = count * depth // rows
    gain_col = column(gain[...])
    for row in range(rows):
        d_right = cell_row(d_right_panel, row, rows)
        d_right = sum(d_right[n : n + hidden] for n in range(0, d_right.shape[0], hidden))
        parts = []
        for side, d_value in enumerate((cell_row(d_left_panel, row, rows), d_right)):
            for base in (2 * side * hidden, (2 * side + 1) * hidden):
                slope = slopes[row, base : base + hidden, :].astype(F32)
                parts.append((d_value * slope).astype(BF16))
        d_zln = dot(w_proj[...], jnp.concatenate(parts, axis=0), 1, 0) + d_zln_gate[row]
        d_in = d_zln * gain_col
        normed = normed_in[row]
        mean_grad = jnp.mean(d_in, axis=0, keepdims=True)
        mean_cross = jnp.mean(d_in * normed, axis=0, keepdims=True)
        result = inv_in[row : row + 1] * (d_in - mean_grad - normed * mean_cross)
        grad[row] = jnp.transpose(result).astype(BF16)


def swap(values, halves=1):
    count = lax.axis_size("row") // halves
    groups = [[half * count + n for n in range(count)] for half in range(halves)]
    return lax.all_to_all(
        values,
        "row",
        split_axis=0,
        concat_axis=0,
        tiled=True,
        axis_index_groups=groups if halves > 1 else None,
    )


def kernel_shards(
    pair,
    cotangent,
    residue_mask,
    ln_in_gain,
    ln_in_bias,
    w_proj,
    w_gate,
    ln_out_gain,
    ln_out_bias,
    w_out,
):
    rows, width, channels = pair.shape
    hidden = w_out.shape[0]
    halves = 2
    devices = lax.axis_size("row")
    count = devices // halves
    block = hidden // count
    left_rows, right_rows = rows * count, rows * devices
    shape = jax.ShapeDtypeStruct
    panel = shape((count, rows * block, width), BF16)
    wide_panel = shape((devices, rows * block, width), BF16)
    mask = residue_mask.reshape(1, width)
    gain, bias = ln_in_gain.reshape(1, channels), ln_in_bias.reshape(1, channels)
    out_gain, out_bias = ln_out_gain.reshape(1, hidden), ln_out_bias.reshape(1, hidden)
    cells = rows * width
    left_panel, right_panel = call(
        project_kernel,
        "project",
        [panel, wide_panel],
        [pair, mask, gain, bias, w_proj],
        fetched=range(5),
        flops=2 * cells * channels * 4 * hidden,
        limit=64 * 1024 * 1024 - 896 * 1024,
    )
    right_panel = swap(right_panel)
    left_panel = swap(left_panel, halves)
    d_hat_centered, gate_slope = call(
        prepare_kernel,
        "prepare",
        [shape((rows, hidden, width), F32), shape((rows, channels, width), F32)],
        [pair, cotangent, gain, bias, w_gate, out_gain, w_out],
        fetched=range(7),
        flops=2 * cells * channels * 2 * hidden,
    )
    left_wide = pltpu.VMEM((left_rows * block, width), F32)
    right_wide = pltpu.VMEM((right_rows * block, width), F32)
    products, left_all, right_all = call(
        tri_kernel,
        "tri",
        [panel, shape((block, left_rows, width), BF16), shape((block, right_rows, width), BF16)],
        [left_panel, right_panel],
        scratch=[left_wide, right_wide],
        flops=2 * block * left_rows * width * right_rows,
    )
    products = swap(products, halves)
    (d_products,) = call(
        middle_kernel,
        "middle",
        [panel],
        [products, d_hat_centered],
        flops=20 * cells * hidden,
    )
    d_products = swap(d_products, halves)
    d_left_panel, d_right_panel = call(
        products_kernel,
        "products",
        [panel, wide_panel],
        [d_products, left_all, right_all],
        scratch=[left_wide, right_wide],
        flops=4 * block * left_rows * width * right_rows,
    )
    d_right_panel = swap(d_right_panel)
    d_left_panel = swap(d_left_panel, halves)
    slopes, d_zln_gate, normed_in, inv_in = call(
        slopes_kernel,
        "slopes",
        [
            shape((rows, 4 * hidden, width), BF16),
            shape((rows, channels, width), F32),
            shape((rows, channels, width), F32),
            shape((rows, width), F32),
        ],
        [
            products,
            gate_slope,
            pair,
            mask,
            gain,
            bias,
            w_proj,
            w_gate,
            out_gain,
            out_bias,
            w_out,
        ],
        fetched=range(2, 11),
        flops=2 * cells * channels * 6 * hidden,
    )
    (grad,) = call(
        finish_kernel,
        "finish",
        [shape(pair.shape, BF16)],
        [d_left_panel, d_right_panel, slopes, d_zln_gate, normed_in, inv_in, gain, w_proj],
        fetched=(6, 7),
        flops=2 * cells * channels * 4 * hidden,
    )
    return grad


def normalize(values, reduce_axis):
    mean_value = jnp.mean(values, axis=reduce_axis, keepdims=True)
    centered = values - mean_value
    variance = jnp.mean(centered * centered, axis=reduce_axis, keepdims=True)
    inv_std = lax.rsqrt(variance + 1e-05)
    return (centered * inv_std, inv_std)


def norm_backward(upstream, normed, inv_std, reduce_axis):
    mean_grad = jnp.mean(upstream, axis=reduce_axis, keepdims=True)
    mean_cross = jnp.mean(upstream * normed, axis=reduce_axis, keepdims=True)
    return inv_std * (upstream - mean_grad - normed * mean_cross)


def shards(
    pair,
    cotangent,
    residue_mask,
    ln_in_gain,
    ln_in_bias,
    w_proj,
    w_gate,
    ln_out_gain,
    ln_out_bias,
    w_out,
):
    local_rows = pair.shape[0]
    local_cols = pair.shape[1]
    hidden = w_out.shape[0]
    chan_index = lax.axis_index("chan")
    row_start = lax.axis_index("row") * local_rows
    col_start = chan_index * local_cols
    mask_float = residue_mask.astype(jnp.float32)
    row_mask = lax.dynamic_slice_in_dim(mask_float, row_start, local_rows)
    col_mask = lax.dynamic_slice_in_dim(mask_float, col_start, local_cols)
    cell_mask = (row_mask[:, None] * col_mask[None, :])[None]
    normed, inv_std = normalize(pair.astype(jnp.float32), -1)
    normed_pair = (normed * ln_in_gain + ln_in_bias).astype(jnp.bfloat16)
    projected = jnp.einsum("rmc,ch->hrm", normed_pair, w_proj, preferred_element_type=jnp.float32)
    left_panel = (
        cell_mask * jax.nn.sigmoid(projected[:hidden]) * projected[hidden : 2 * hidden]
    ).astype(jnp.bfloat16)
    right_panel = (
        cell_mask * jax.nn.sigmoid(projected[2 * hidden : 3 * hidden]) * projected[3 * hidden :]
    ).astype(jnp.bfloat16)
    panels = lax.all_to_all(
        jnp.stack([left_panel, right_panel]), "row", split_axis=1, concat_axis=2, tiled=True
    )
    left_all = panels[0]
    right_all = panels[1]
    right_rows = lax.all_to_all(right_all, "chan", split_axis=1, concat_axis=2, tiled=True)
    partner = right_rows
    tri_part = jnp.einsum(
        "gik,gjk->gij",
        lax.all_gather(left_all, "chan", axis=2, tiled=True),
        partner,
        preferred_element_type=jnp.float32,
    ).astype(jnp.bfloat16)
    tri_cells = lax.all_to_all(tri_part, "row", split_axis=1, concat_axis=0, tiled=True)
    tri_hat, inv_tri = normalize(tri_cells.astype(jnp.float32), 0)
    scaled = (tri_hat * ln_out_gain[:, None, None] + ln_out_bias[:, None, None]).astype(
        jnp.bfloat16
    )
    proj_out = jnp.einsum("hrm,hc->rmc", scaled, w_out, preferred_element_type=jnp.float32)
    gate_value = jax.nn.sigmoid(
        jnp.einsum("rmc,cd->rmd", normed_pair, w_gate, preferred_element_type=jnp.float32)
    )
    cot_float = cotangent.astype(jnp.float32)
    d_gate_pre = (cot_float * proj_out * gate_value * (1.0 - gate_value)).astype(jnp.bfloat16)
    d_scaled = (cot_float * gate_value).astype(jnp.bfloat16)
    d_hat = jnp.einsum("rmc,hc->hrm", d_scaled, w_out, preferred_element_type=jnp.float32)
    d_hat = d_hat * ln_out_gain[:, None, None]
    d_tri = norm_backward(d_hat, tri_hat, inv_tri, 0).astype(jnp.bfloat16)
    d_tri_all = lax.all_to_all(d_tri, "row", split_axis=0, concat_axis=1, tiled=True)
    panel_piece = lax.all_gather(d_tri_all, "chan", axis=2, tiled=True)
    partner = right_all
    d_left = jnp.einsum("gij,gjk->gik", panel_piece, partner, preferred_element_type=jnp.float32)
    contribution = jnp.einsum(
        "gij,gik->gjk", panel_piece, left_all, preferred_element_type=jnp.float32
    )
    d_right = contribution
    d_left, d_right = (d_left, d_right)
    d_stack = jnp.stack([d_left, d_right]).astype(jnp.bfloat16)
    d_panels = lax.all_to_all(d_stack, "row", split_axis=2, concat_axis=1, tiled=True)

    def gating(d_value, gate_proj, value_proj):
        sigmoid_val = jax.nn.sigmoid(gate_proj)
        masked_grad = d_value.astype(jnp.float32) * cell_mask
        return (
            masked_grad * value_proj * sigmoid_val * (1.0 - sigmoid_val),
            masked_grad * sigmoid_val,
        )

    gate_left, value_left = gating(d_panels[0], projected[:hidden], projected[hidden : 2 * hidden])
    gate_right, value_right = gating(
        d_panels[1], projected[2 * hidden : 3 * hidden], projected[3 * hidden :]
    )
    d_proj = jnp.concatenate([gate_left, value_left, gate_right, value_right], axis=0).astype(
        jnp.bfloat16
    )
    d_normed = jnp.einsum("hrm,ch->rmc", d_proj, w_proj, preferred_element_type=jnp.float32)
    d_normed = d_normed + jnp.einsum(
        "rmd,cd->rmc", d_gate_pre, w_gate, preferred_element_type=jnp.float32
    )
    d_input = d_normed * ln_in_gain
    return norm_backward(d_input, normed, inv_std, -1).astype(jnp.bfloat16)


def solution(mesh):
    fits = mesh.shape["chan"] == 1 and mesh.shape["row"] in (8, 16)
    return jax.shard_map(
        kernel_shards if fits else shards,
        mesh=mesh,
        in_specs=(
            P(("grp", "row"), "chan", None),
            P(("grp", "row"), "chan", None),
            P("grp"),
            P(),
            P(),
            P(),
            P(),
            P(),
            P(),
            P(),
        ),
        out_specs=P(("grp", "row"), "chan", None),
        check_vma=False,
    )
```

```python
import functools

import jax
import jax.numpy as jnp
from jax import lax
from jax.experimental import pallas as pl
from jax.experimental.pallas import tpu as pltpu
from jax.sharding import PartitionSpec as P

F32 = jnp.float32
BF16 = jnp.bfloat16
VMEM_LIMIT = 16 * 1024 * 1024


def dot(lhs, rhs, lhs_dim, rhs_dim):
    return lax.dot_general(
        lhs, rhs, (((lhs_dim,), (rhs_dim,)), ((), ())), preferred_element_type=F32
    )


def transposed(matrix):
    return jnp.transpose(matrix.astype(F32)).astype(BF16)


def sigmoid(values):
    return 1.0 / (1.0 + jnp.exp(-values))


def column(row):
    size = row.shape[1]
    return jnp.transpose(jnp.broadcast_to(row, (size, size)))


def norm_rows(values):
    centered = values - jnp.mean(values, axis=0, keepdims=True)
    variance = jnp.mean(centered * centered, axis=0, keepdims=True)
    inv_std = lax.rsqrt(variance + 1e-05)
    return centered * inv_std, inv_std


def call(kernel, name, outs, args, fetched=(), scratch=(), flops=0, limit=VMEM_LIMIT):
    moved = sum(a.size * a.dtype.itemsize for a in args) + sum(
        o.size * jnp.dtype(o.dtype).itemsize for o in outs
    )
    n_args, n_outs, n_fetched = len(args), len(outs), len(fetched)

    def body(*refs):
        ins = list(refs[:n_args])
        rest = refs[n_args + n_outs :]
        copies = []
        for n, place in enumerate(fetched):
            copies.append(pltpu.make_async_copy(ins[place], rest[n], rest[n_fetched].at[n]))
            ins[place] = rest[n]
        for copy in copies:
            copy.start()
        for copy in copies:
            copy.wait()
        kernel(*ins, *refs[n_args : n_args + n_outs], *rest[n_fetched + (n_fetched > 0) :])

    buffers = [pltpu.VMEM(args[place].shape, args[place].dtype) for place in fetched]
    if fetched:
        buffers.append(pltpu.SemaphoreType.DMA((n_fetched,)))
    return pl.pallas_call(
        body,
        name=name,
        out_shape=outs,
        in_specs=[
            pl.BlockSpec(memory_space=pltpu.HBM if n in fetched else pltpu.VMEM)
            for n in range(n_args)
        ],
        out_specs=[pl.BlockSpec(memory_space=pltpu.VMEM) for _ in outs],
        scratch_shapes=buffers + list(scratch),
        compiler_params=pltpu.CompilerParams(vmem_limit_bytes=limit),
        cost_estimate=pl.CostEstimate(flops=flops, bytes_accessed=moved, transcendentals=0),
    )(*args)


def cell_masks(mask, rows):
    columns = mask[...].astype(F32)
    shape = (rows, columns.shape[1])
    first = lax.axis_index("row") * rows
    own = lax.broadcasted_iota(jnp.int32, shape, 1) == (
        lax.broadcasted_iota(jnp.int32, shape, 0) + first
    )
    row_mask = jnp.sum(jnp.where(own, columns, 0.0), axis=1, keepdims=True)
    cells = row_mask * columns
    return [cells[row : row + 1] for row in range(rows)]


def partner(step, count):
    return lax.rem(lax.axis_index("row"), count) ^ step


def project_kernel(pair, mask, gain, bias, w_proj, right_panel, *refs):
    *pieces, left_panel = refs
    rows = pair.shape[0]
    hidden = w_proj.shape[1] // 4
    count, depth, width = left_panel.shape
    block = depth // rows
    halves = right_panel.shape[0] // count
    w_flip = transposed(w_proj[...])
    gain_col, bias_col = column(gain[...]), column(bias[...])
    masks = cell_masks(mask, rows)
    for row in range(rows):
        normed, _ = norm_rows(jnp.transpose(pair[row].astype(F32)))
        zln = (normed * gain_col + bias_col).astype(BF16)
        proj = dot(w_flip, zln, 1, 0)
        place = slice(row * block, (row + 1) * block)
        left = masks[row] * sigmoid(proj[:hidden]) * proj[hidden : 2 * hidden]
        left_panel[:, place, :] = left.reshape(count, block, width).astype(BF16)
        right = masks[row] * sigmoid(proj[2 * hidden : 3 * hidden]) * proj[3 * hidden :]
        right = right.reshape(count, block, width).astype(BF16)
        for half in range(halves):
            right_panel[half * count : (half + 1) * count, place, :] = right
    for step, piece in enumerate(pieces):
        piece[...] = left_panel[partner(step, count)]


def prepare_kernel(
    pair, cotangent, gain, bias, w_gate, out_gain, w_out, d_hat_centered, gate_slope
):
    gate_flip = transposed(w_gate[...])
    gain_col, bias_col = column(gain[...]), column(bias[...])
    out_gain_col = column(out_gain[...])
    for row in range(pair.shape[0]):
        normed, _ = norm_rows(jnp.transpose(pair[row].astype(F32)))
        zln = (normed * gain_col + bias_col).astype(BF16)
        gate = sigmoid(dot(gate_flip, zln, 1, 0))
        cot = jnp.transpose(cotangent[row].astype(F32))
        d_scaled = (cot * gate).astype(BF16)
        d_hat = dot(w_out[...], d_scaled, 1, 0) * out_gain_col
        d_hat_centered[row] = d_hat - jnp.mean(d_hat, axis=0, keepdims=True)
        gate_slope[row] = cot * gate * (1.0 - gate)


def spread(panel, wide):
    wide[...] = panel[...].astype(F32).reshape(wide.shape)


def tri_kernel(right_panel, *refs):
    *pieces, products, left_all, right_all, left_wide, right_wide = refs
    block, left_rows, _ = left_all.shape
    right_rows = right_all.shape[1]
    depth = pieces[0].shape[0]
    for step, piece in enumerate(pieces):
        start = pl.multiple_of(partner(step, len(pieces)) * depth, depth)
        left_wide[pl.ds(start, depth), :] = piece[...].astype(F32)
    spread(right_panel, right_wide)
    for h in range(block):
        left_all[h] = left_wide[pl.ds(h, left_rows, stride=block), :].astype(BF16)
        right_all[h] = right_wide[pl.ds(h, right_rows, stride=block), :].astype(BF16)
        left_wide[pl.ds(h, left_rows, stride=block), :] = dot(left_all[h], right_all[h], 1, 1)
    products[...] = left_wide[...].astype(BF16).reshape(products.shape)


def cell_row(ref, row, rows):
    count, depth, width = ref.shape
    block = depth // rows
    return ref[:, row * block : (row + 1) * block, :].astype(F32).reshape(count * block, width)


def middle_kernel(products, d_hat_centered, d_products):
    rows = d_hat_centered.shape[0]
    count, depth, width = products.shape
    block = depth // rows
    for row in range(rows):
        tri_hat, inv_std = norm_rows(cell_row(products, row, rows))
        d_hat = d_hat_centered[row]
        cross = jnp.mean(d_hat * tri_hat, axis=0, keepdims=True)
        d_tri = inv_std * (d_hat - tri_hat * cross)
        d_products[:, row * block : (row + 1) * block, :] = d_tri.reshape(
            count, block, width
        ).astype(BF16)


def products_kernel(d_products, left_all, right_all, d_right_panel, *refs):
    *pieces, left_wide, right_wide = refs
    block, left_rows, _ = left_all.shape
    right_rows = right_all.shape[1]
    spread(d_products, left_wide)
    for h in range(block):
        d_tri = left_wide[pl.ds(h, left_rows, stride=block), :].astype(BF16)
        left_wide[pl.ds(h, left_rows, stride=block), :] = dot(d_tri, right_all[h], 1, 0)
        right_wide[pl.ds(h, right_rows, stride=block), :] = dot(d_tri, left_all[h], 0, 0)
    depth = pieces[0].shape[0]
    for step, piece in enumerate(pieces):
        start = pl.multiple_of(partner(step, len(pieces)) * depth, depth)
        piece[...] = left_wide[pl.ds(start, depth), :].astype(BF16)
    d_right_panel[...] = right_wide[...].astype(BF16).reshape(d_right_panel.shape)


def slopes_kernel(
    products,
    gate_slope,
    pair,
    mask,
    gain,
    bias,
    w_proj,
    w_gate,
    out_gain,
    out_bias,
    w_out,
    slopes,
    d_zln_gate,
    normed_in,
    inv_in,
):
    rows = pair.shape[0]
    hidden = w_out.shape[0]
    w_flip = transposed(w_proj[...])
    out_flip = transposed(w_out[...])
    gain_col, bias_col = column(gain[...]), column(bias[...])
    out_gain_col, out_bias_col = column(out_gain[...]), column(out_bias[...])
    masks = cell_masks(mask, rows)
    for row in range(rows):
        tri_hat, _ = norm_rows(cell_row(products, row, rows))
        scaled = (tri_hat * out_gain_col + out_bias_col).astype(BF16)
        d_gate_pre = (dot(out_flip, scaled, 1, 0) * gate_slope[row]).astype(BF16)
        d_zln_gate[row] = dot(w_gate[...], d_gate_pre, 1, 0)
        normed, inv_std = norm_rows(jnp.transpose(pair[row].astype(F32)))
        normed_in[row] = normed
        inv_in[row : row + 1] = inv_std
        zln = (normed * gain_col + bias_col).astype(BF16)
        proj = dot(w_flip, zln, 1, 0)
        for side in range(2):
            base = 2 * side * hidden
            sig = sigmoid(proj[base : base + hidden])
            masked = masks[row] * sig
            value = masked * (1.0 - sig) * proj[base + hidden : base + 2 * hidden]
            slopes[row, base : base + hidden, :] = value.astype(slopes.dtype)
            slopes[row, base + hidden : base + 2 * hidden, :] = masked.astype(slopes.dtype)


def finish_kernel(d_right_panel, slopes, d_zln_gate, normed_in, inv_in, gain, w_proj, *refs):
    *pieces, grad, d_left_panel = refs
    for step, piece in enumerate(pieces):
        d_left_panel[partner(step, len(pieces))] = piece[...]
    rows = grad.shape[0]
    count, depth, width = d_left_panel.shape
    hidden = count * depth // rows
    gain_col = column(gain[...])
    for row in range(rows):
        d_right = cell_row(d_right_panel, row, rows)
        d_right = sum(d_right[n : n + hidden] for n in range(0, d_right.shape[0], hidden))
        parts = []
        for side, d_value in enumerate((cell_row(d_left_panel, row, rows), d_right)):
            for base in (2 * side * hidden, (2 * side + 1) * hidden):
                slope = slopes[row, base : base + hidden, :].astype(F32)
                parts.append((d_value * slope).astype(BF16))
        d_zln = dot(w_proj[...], jnp.concatenate(parts, axis=0), 1, 0) + d_zln_gate[row]
        d_in = d_zln * gain_col
        normed = normed_in[row]
        mean_grad = jnp.mean(d_in, axis=0, keepdims=True)
        mean_cross = jnp.mean(d_in * normed, axis=0, keepdims=True)
        result = inv_in[row : row + 1] * (d_in - mean_grad - normed * mean_cross)
        grad[row] = jnp.transpose(result).astype(BF16)


def swap(values):
    return lax.all_to_all(values, "row", split_axis=0, concat_axis=0, tiled=True)


def swap_half(values, count):
    devices = range(lax.axis_size("row"))
    groups = [[d for d in devices if d // count == half] for half in range(len(devices) // count)]
    return lax.all_to_all(
        values, "row", split_axis=0, concat_axis=0, tiled=True, axis_index_groups=groups
    )


def swap_pieces(pieces):
    devices = range(lax.axis_size("row"))
    return [pieces[0]] + [
        lax.ppermute(pieces[step], "row", [(d, d ^ step) for d in devices])
        for step in range(1, len(pieces))
    ]


def kernel_shards(
    pair,
    cotangent,
    residue_mask,
    ln_in_gain,
    ln_in_bias,
    w_proj,
    w_gate,
    ln_out_gain,
    ln_out_bias,
    w_out,
):
    rows, width, channels = pair.shape
    hidden = w_out.shape[0]
    halves = 2
    devices = lax.axis_size("row")
    count = devices // halves
    block = hidden // count
    left_rows, right_rows = rows * count, rows * devices
    shape = jax.ShapeDtypeStruct
    panel = shape((count, rows * block, width), BF16)
    wide_panel = shape((devices, rows * block, width), BF16)
    mask = residue_mask.reshape(1, width)
    gain, bias = ln_in_gain.reshape(1, channels), ln_in_bias.reshape(1, channels)
    out_gain, out_bias = ln_out_gain.reshape(1, hidden), ln_out_bias.reshape(1, hidden)
    cells = rows * width
    piece = shape((rows * block, width), BF16)
    left_panel = pltpu.VMEM(panel.shape, BF16)
    right_panel, *pieces = call(
        project_kernel,
        "project",
        [wide_panel] + [piece] * count,
        [pair, mask, gain, bias, w_proj],
        fetched=range(5),
        scratch=[left_panel],
        flops=2 * cells * channels * 4 * hidden,
        limit=64 * 1024 * 1024 - 896 * 1024,
    )
    right_panel = swap(right_panel)
    pieces = swap_pieces(pieces)
    d_hat_centered, gate_slope = call(
        prepare_kernel,
        "prepare",
        [shape((rows, hidden, width), F32), shape((rows, channels, width), F32)],
        [pair, cotangent, gain, bias, w_gate, out_gain, w_out],
        fetched=range(7),
        flops=2 * cells * channels * 2 * hidden,
    )
    left_wide = pltpu.VMEM((left_rows * block, width), F32)
    right_wide = pltpu.VMEM((right_rows * block, width), F32)
    products, left_all, right_all = call(
        tri_kernel,
        "tri",
        [panel, shape((block, left_rows, width), BF16), shape((block, right_rows, width), BF16)],
        [right_panel, *pieces],
        scratch=[left_wide, right_wide],
        flops=2 * block * left_rows * width * right_rows,
    )
    products = swap_half(products, count)
    (d_products,) = call(
        middle_kernel,
        "middle",
        [panel],
        [products, d_hat_centered],
        flops=20 * cells * hidden,
    )
    d_products = swap_half(d_products, count)
    d_right_panel, *d_pieces = call(
        products_kernel,
        "products",
        [wide_panel] + [piece] * count,
        [d_products, left_all, right_all],
        scratch=[left_wide, right_wide],
        flops=4 * block * left_rows * width * right_rows,
    )
    d_right_panel = swap(d_right_panel)
    d_pieces = swap_pieces(d_pieces)
    slopes, d_zln_gate, normed_in, inv_in = call(
        slopes_kernel,
        "slopes",
        [
            shape((rows, 4 * hidden, width), BF16),
            shape((rows, channels, width), F32),
            shape((rows, channels, width), F32),
            shape((rows, width), F32),
        ],
        [
            products,
            gate_slope,
            pair,
            mask,
            gain,
            bias,
            w_proj,
            w_gate,
            out_gain,
            out_bias,
            w_out,
        ],
        fetched=range(2, 11),
        flops=2 * cells * channels * 6 * hidden,
    )
    (grad,) = call(
        finish_kernel,
        "finish",
        [shape(pair.shape, BF16)],
        [d_right_panel, slopes, d_zln_gate, normed_in, inv_in, gain, w_proj, *d_pieces],
        fetched=(5, 6),
        scratch=[left_panel],
        flops=2 * cells * channels * 4 * hidden,
    )
    return grad


def normalize(values, reduce_axis):
    mean_value = jnp.mean(values, axis=reduce_axis, keepdims=True)
    centered = values - mean_value
    variance = jnp.mean(centered * centered, axis=reduce_axis, keepdims=True)
    inv_std = lax.rsqrt(variance + 1e-05)
    return (centered * inv_std, inv_std)


def norm_backward(upstream, normed, inv_std, reduce_axis):
    mean_grad = jnp.mean(upstream, axis=reduce_axis, keepdims=True)
    mean_cross = jnp.mean(upstream * normed, axis=reduce_axis, keepdims=True)
    return inv_std * (upstream - mean_grad - normed * mean_cross)


def shards(
    pair,
    cotangent,
    residue_mask,
    ln_in_gain,
    ln_in_bias,
    w_proj,
    w_gate,
    ln_out_gain,
    ln_out_bias,
    w_out,
):
    local_rows = pair.shape[0]
    local_cols = pair.shape[1]
    hidden = w_out.shape[0]
    chan_index = lax.axis_index("chan")
    row_start = lax.axis_index("row") * local_rows
    col_start = chan_index * local_cols
    mask_float = residue_mask.astype(jnp.float32)
    row_mask = lax.dynamic_slice_in_dim(mask_float, row_start, local_rows)
    col_mask = lax.dynamic_slice_in_dim(mask_float, col_start, local_cols)
    cell_mask = (row_mask[:, None] * col_mask[None, :])[None]
    normed, inv_std = normalize(pair.astype(jnp.float32), -1)
    normed_pair = (normed * ln_in_gain + ln_in_bias).astype(jnp.bfloat16)
    projected = jnp.einsum("rmc,ch->hrm", normed_pair, w_proj, preferred_element_type=jnp.float32)
    left_panel = (
        cell_mask * jax.nn.sigmoid(projected[:hidden]) * projected[hidden : 2 * hidden]
    ).astype(jnp.bfloat16)
    right_panel = (
        cell_mask * jax.nn.sigmoid(projected[2 * hidden : 3 * hidden]) * projected[3 * hidden :]
    ).astype(jnp.bfloat16)
    panels = lax.all_to_all(
        jnp.stack([left_panel, right_panel]), "row", split_axis=1, concat_axis=2, tiled=True
    )
    left_all = panels[0]
    right_all = panels[1]
    right_rows = lax.all_to_all(right_all, "chan", split_axis=1, concat_axis=2, tiled=True)
    partner = right_rows
    tri_part = jnp.einsum(
        "gik,gjk->gij",
        lax.all_gather(left_all, "chan", axis=2, tiled=True),
        partner,
        preferred_element_type=jnp.float32,
    ).astype(jnp.bfloat16)
    tri_cells = lax.all_to_all(tri_part, "row", split_axis=1, concat_axis=0, tiled=True)
    tri_hat, inv_tri = normalize(tri_cells.astype(jnp.float32), 0)
    scaled = (tri_hat * ln_out_gain[:, None, None] + ln_out_bias[:, None, None]).astype(
        jnp.bfloat16
    )
    proj_out = jnp.einsum("hrm,hc->rmc", scaled, w_out, preferred_element_type=jnp.float32)
    gate_value = jax.nn.sigmoid(
        jnp.einsum("rmc,cd->rmd", normed_pair, w_gate, preferred_element_type=jnp.float32)
    )
    cot_float = cotangent.astype(jnp.float32)
    d_gate_pre = (cot_float * proj_out * gate_value * (1.0 - gate_value)).astype(jnp.bfloat16)
    d_scaled = (cot_float * gate_value).astype(jnp.bfloat16)
    d_hat = jnp.einsum("rmc,hc->hrm", d_scaled, w_out, preferred_element_type=jnp.float32)
    d_hat = d_hat * ln_out_gain[:, None, None]
    d_tri = norm_backward(d_hat, tri_hat, inv_tri, 0).astype(jnp.bfloat16)
    d_tri_all = lax.all_to_all(d_tri, "row", split_axis=0, concat_axis=1, tiled=True)
    panel_piece = lax.all_gather(d_tri_all, "chan", axis=2, tiled=True)
    partner = right_all
    d_left = jnp.einsum("gij,gjk->gik", panel_piece, partner, preferred_element_type=jnp.float32)
    contribution = jnp.einsum(
        "gij,gik->gjk", panel_piece, left_all, preferred_element_type=jnp.float32
    )
    d_right = contribution
    d_left, d_right = (d_left, d_right)
    d_stack = jnp.stack([d_left, d_right]).astype(jnp.bfloat16)
    d_panels = lax.all_to_all(d_stack, "row", split_axis=2, concat_axis=1, tiled=True)

    def gating(d_value, gate_proj, value_proj):
        sigmoid_val = jax.nn.sigmoid(gate_proj)
        masked_grad = d_value.astype(jnp.float32) * cell_mask
        return (
            masked_grad * value_proj * sigmoid_val * (1.0 - sigmoid_val),
            masked_grad * sigmoid_val,
        )

    gate_left, value_left = gating(d_panels[0], projected[:hidden], projected[hidden : 2 * hidden])
    gate_right, value_right = gating(
        d_panels[1], projected[2 * hidden : 3 * hidden], projected[3 * hidden :]
    )
    d_proj = jnp.concatenate([gate_left, value_left, gate_right, value_right], axis=0).astype(
        jnp.bfloat16
    )
    d_normed = jnp.einsum("hrm,ch->rmc", d_proj, w_proj, preferred_element_type=jnp.float32)
    d_normed = d_normed + jnp.einsum(
        "rmd,cd->rmc", d_gate_pre, w_gate, preferred_element_type=jnp.float32
    )
    d_input = d_normed * ln_in_gain
    return norm_backward(d_input, normed, inv_std, -1).astype(jnp.bfloat16)


def solution(mesh):
    fits = mesh.shape["chan"] == 1 and mesh.shape["row"] in (8, 16)
    return jax.shard_map(
        kernel_shards if fits else shards,
        mesh=mesh,
        in_specs=(
            P(("grp", "row"), "chan", None),
            P(("grp", "row"), "chan", None),
            P("grp"),
            P(),
            P(),
            P(),
            P(),
            P(),
            P(),
            P(),
        ),
        out_specs=P(("grp", "row"), "chan", None),
        check_vma=False,
    )
```

```python
import functools

import jax
import jax.numpy as jnp
from jax import lax
from jax.experimental import pallas as pl
from jax.experimental.pallas import tpu as pltpu
from jax.sharding import PartitionSpec as P

F32 = jnp.float32
BF16 = jnp.bfloat16
VMEM_LIMIT = 16 * 1024 * 1024


def dot(lhs, rhs, lhs_dim, rhs_dim):
    return lax.dot_general(
        lhs, rhs, (((lhs_dim,), (rhs_dim,)), ((), ())), preferred_element_type=F32
    )


def transposed(matrix):
    return jnp.transpose(matrix.astype(F32)).astype(BF16)


def sigmoid(values):
    return 1.0 / (1.0 + jnp.exp(-values))


def column(row):
    size = row.shape[1]
    return jnp.transpose(jnp.broadcast_to(row, (size, size)))


def norm_rows(values):
    centered = values - jnp.mean(values, axis=0, keepdims=True)
    variance = jnp.mean(centered * centered, axis=0, keepdims=True)
    inv_std = lax.rsqrt(variance + 1e-05)
    return centered * inv_std, inv_std


def call(
    kernel, name, outs, args, fetched=(), unread=(), scratch=(), flops=0, limit=VMEM_LIMIT
):
    moved = sum(a.size * a.dtype.itemsize for a in args) + sum(
        o.size * jnp.dtype(o.dtype).itemsize for o in outs
    )
    n_args, n_outs, n_fetched = len(args), len(outs), len(fetched)

    def body(*refs):
        ins = list(refs[:n_args])
        rest = refs[n_args + n_outs :]
        copies = []
        for n, place in enumerate(fetched):
            copies.append(pltpu.make_async_copy(ins[place], rest[n], rest[n_fetched].at[n]))
            ins[place] = rest[n]
        for copy in copies:
            copy.start()
        for copy in copies:
            copy.wait()
        kernel(*ins, *refs[n_args : n_args + n_outs], *rest[n_fetched + (n_fetched > 0) :])

    buffers = [pltpu.VMEM(args[place].shape, args[place].dtype) for place in fetched]
    if fetched:
        buffers.append(pltpu.SemaphoreType.DMA((n_fetched,)))
    return pl.pallas_call(
        body,
        name=name,
        out_shape=outs,
        in_specs=[
            pl.BlockSpec(
                memory_space=pltpu.HBM if n in fetched else pl.ANY if n in unread else pltpu.VMEM
            )
            for n in range(n_args)
        ],
        out_specs=[pl.BlockSpec(memory_space=pltpu.VMEM) for _ in outs],
        scratch_shapes=buffers + list(scratch),
        compiler_params=pltpu.CompilerParams(vmem_limit_bytes=limit),
        cost_estimate=pl.CostEstimate(flops=flops, bytes_accessed=moved, transcendentals=0),
    )(*args)


def cell_masks(mask, rows):
    columns = mask[...].astype(F32)
    shape = (rows, columns.shape[1])
    first = lax.axis_index("row") * rows
    own = lax.broadcasted_iota(jnp.int32, shape, 1) == (
        lax.broadcasted_iota(jnp.int32, shape, 0) + first
    )
    row_mask = jnp.sum(jnp.where(own, columns, 0.0), axis=1, keepdims=True)
    cells = row_mask * columns
    return [cells[row : row + 1] for row in range(rows)]


def partner(step, count):
    return lax.rem(lax.axis_index("row"), count) ^ step


def gated_rows(pair, mask, gain, bias, w_proj, side):
    rows = pair.shape[0]
    hidden = w_proj.shape[1] // 4
    w_flip = transposed(w_proj[:, 2 * side * hidden : 2 * (side + 1) * hidden])
    gain_col, bias_col = column(gain[...]), column(bias[...])
    masks = cell_masks(mask, rows)
    for row in range(rows):
        normed, _ = norm_rows(jnp.transpose(pair[row].astype(F32)))
        zln = (normed * gain_col + bias_col).astype(BF16)
        proj = dot(w_flip, zln, 1, 0)
        yield row, masks[row] * sigmoid(proj[:hidden]) * proj[hidden:]


def project_right_kernel(pair, mask, gain, bias, w_proj, right_panel):
    rows = pair.shape[0]
    devices, depth, width = right_panel.shape
    block = depth // rows
    hidden = w_proj.shape[1] // 4
    count = hidden // block
    for row, right in gated_rows(pair, mask, gain, bias, w_proj, 1):
        right = right.reshape(count, block, width).astype(BF16)
        for start in range(0, devices, count):
            right_panel[start : start + count, row * block : (row + 1) * block, :] = right


def project_left_kernel(pair, mask, gain, bias, w_proj, after, *refs):
    del after
    *pieces, left_panel = refs
    rows = pair.shape[0]
    count, depth, width = left_panel.shape
    block = depth // rows
    for row, left in gated_rows(pair, mask, gain, bias, w_proj, 0):
        left = left.reshape(count, block, width).astype(BF16)
        left_panel[:, row * block : (row + 1) * block, :] = left
    for step, piece in enumerate(pieces):
        piece[...] = left_panel[partner(step, count)]


def prepare_kernel(
    pair, cotangent, gain, bias, w_gate, out_gain, w_out, d_hat_centered, gate_slope
):
    gate_flip = transposed(w_gate[...])
    gain_col, bias_col = column(gain[...]), column(bias[...])
    out_gain_col = column(out_gain[...])
    for row in range(pair.shape[0]):
        normed, _ = norm_rows(jnp.transpose(pair[row].astype(F32)))
        zln = (normed * gain_col + bias_col).astype(BF16)
        gate = sigmoid(dot(gate_flip, zln, 1, 0))
        cot = jnp.transpose(cotangent[row].astype(F32))
        d_scaled = (cot * gate).astype(BF16)
        d_hat = dot(w_out[...], d_scaled, 1, 0) * out_gain_col
        d_hat_centered[row] = d_hat - jnp.mean(d_hat, axis=0, keepdims=True)
        gate_slope[row] = cot * gate * (1.0 - gate)


def spread(panel, wide):
    wide[...] = panel[...].astype(F32).reshape(wide.shape)


def sort_left_kernel(*refs):
    *pieces, left_all, left_wide = refs
    block, left_rows, _ = left_all.shape
    depth = pieces[0].shape[0]
    for step, piece in enumerate(pieces):
        start = pl.multiple_of(partner(step, len(pieces)) * depth, depth)
        left_wide[pl.ds(start, depth), :] = piece[...].astype(F32)
    for h in range(block):
        left_all[h] = left_wide[pl.ds(h, left_rows, stride=block), :].astype(BF16)


def tri_kernel(right_panel, left_all, after, products, right_all, left_wide, right_wide):
    del after
    block, left_rows, _ = left_all.shape
    right_rows = right_all.shape[1]
    spread(right_panel, right_wide)
    for h in range(block):
        right = right_wide[pl.ds(h, right_rows, stride=block), :].astype(BF16)
        right_all[h] = right
        left_wide[pl.ds(h, left_rows, stride=block), :] = dot(left_all[h], right, 1, 1)
    products[...] = left_wide[...].astype(BF16).reshape(products.shape)


def cell_row(ref, row, rows):
    count, depth, width = ref.shape
    block = depth // rows
    return ref[:, row * block : (row + 1) * block, :].astype(F32).reshape(count * block, width)


def middle_kernel(products, d_hat_centered, d_products):
    rows = d_hat_centered.shape[0]
    count, depth, width = products.shape
    block = depth // rows
    for row in range(rows):
        tri_hat, inv_std = norm_rows(cell_row(products, row, rows))
        d_hat = d_hat_centered[row]
        cross = jnp.mean(d_hat * tri_hat, axis=0, keepdims=True)
        d_tri = inv_std * (d_hat - tri_hat * cross)
        d_products[:, row * block : (row + 1) * block, :] = d_tri.reshape(
            count, block, width
        ).astype(BF16)


def d_right_kernel(d_products, left_all, d_right_panel, d_tri_all, left_wide, right_wide):
    block, left_rows, _ = left_all.shape
    right_rows = right_wide.shape[0] // block
    spread(d_products, left_wide)
    for h in range(block):
        d_tri = left_wide[pl.ds(h, left_rows, stride=block), :].astype(BF16)
        d_tri_all[h] = d_tri
        right_wide[pl.ds(h, right_rows, stride=block), :] = dot(d_tri, left_all[h], 0, 0)
    d_right_panel[...] = right_wide[...].astype(BF16).reshape(d_right_panel.shape)


def d_left_kernel(d_tri_all, right_all, *refs):
    *pieces, left_wide = refs
    block, left_rows, _ = d_tri_all.shape
    for h in range(block):
        left_wide[pl.ds(h, left_rows, stride=block), :] = dot(d_tri_all[h], right_all[h], 1, 0)
    depth = pieces[0].shape[0]
    for step, piece in enumerate(pieces):
        start = pl.multiple_of(partner(step, len(pieces)) * depth, depth)
        piece[...] = left_wide[pl.ds(start, depth), :].astype(BF16)


def slopes_kernel(
    products,
    gate_slope,
    pair,
    mask,
    gain,
    bias,
    w_proj,
    out_gain,
    out_bias,
    w_out,
    slopes,
    d_gate_pre,
    normed_in,
    inv_in,
):
    rows = pair.shape[0]
    hidden = w_out.shape[0]
    w_flip = transposed(w_proj[...])
    out_flip = transposed(w_out[...])
    gain_col, bias_col = column(gain[...]), column(bias[...])
    out_gain_col, out_bias_col = column(out_gain[...]), column(out_bias[...])
    masks = cell_masks(mask, rows)
    for row in range(rows):
        tri_hat, _ = norm_rows(cell_row(products, row, rows))
        scaled = (tri_hat * out_gain_col + out_bias_col).astype(BF16)
        d_gate_pre[row] = (dot(out_flip, scaled, 1, 0) * gate_slope[row]).astype(BF16)
        normed, inv_std = norm_rows(jnp.transpose(pair[row].astype(F32)))
        normed_in[row] = normed.astype(normed_in.dtype)
        inv_in[row : row + 1] = inv_std
        zln = (normed * gain_col + bias_col).astype(BF16)
        proj = dot(w_flip, zln, 1, 0)
        for side in range(2):
            base = 2 * side * hidden
            sig = sigmoid(proj[base : base + hidden])
            masked = masks[row] * sig
            value = masked * (1.0 - sig) * proj[base + hidden : base + 2 * hidden]
            slopes[row, base : base + hidden, :] = value.astype(slopes.dtype)
            slopes[row, base + hidden : base + 2 * hidden, :] = masked.astype(slopes.dtype)


def finish_kernel(
    d_right_panel, slopes, d_gate_pre, normed_in, inv_in, gain, w_proj, w_gate, *refs
):
    *pieces, grad, d_left_panel = refs
    for step, piece in enumerate(pieces):
        d_left_panel[partner(step, len(pieces))] = piece[...]
    rows = grad.shape[0]
    count, depth, width = d_left_panel.shape
    hidden = count * depth // rows
    gain_col = column(gain[...])
    weights = jnp.concatenate([w_proj[...], w_gate[...]], axis=1)
    for row in range(rows):
        d_right = cell_row(d_right_panel, row, rows)
        d_right = sum(d_right[n : n + hidden] for n in range(0, d_right.shape[0], hidden))
        parts = []
        for side, d_value in enumerate((cell_row(d_left_panel, row, rows), d_right)):
            for base in (2 * side * hidden, (2 * side + 1) * hidden):
                slope = slopes[row, base : base + hidden, :].astype(F32)
                parts.append((d_value * slope).astype(BF16))
        parts.append(d_gate_pre[row])
        d_in = dot(weights, jnp.concatenate(parts, axis=0), 1, 0) * gain_col
        normed = normed_in[row].astype(F32)
        mean_grad = jnp.mean(d_in, axis=0, keepdims=True)
        mean_cross = jnp.mean(d_in * normed, axis=0, keepdims=True)
        result = inv_in[row : row + 1] * (d_in - mean_grad - normed * mean_cross)
        grad[row] = jnp.transpose(result).astype(BF16)


def swap(values):
    return lax.all_to_all(values, "row", split_axis=0, concat_axis=0, tiled=True)


def swap_half(values, count):
    devices = range(lax.axis_size("row"))
    groups = [[d for d in devices if d // count == half] for half in range(len(devices) // count)]
    return lax.all_to_all(
        values, "row", split_axis=0, concat_axis=0, tiled=True, axis_index_groups=groups
    )


def swap_pieces(pieces):
    devices = range(lax.axis_size("row"))
    return [pieces[0]] + [
        lax.ppermute(pieces[step], "row", [(d, d ^ step) for d in devices])
        for step in range(1, len(pieces))
    ]


def kernel_shards(
    pair,
    cotangent,
    residue_mask,
    ln_in_gain,
    ln_in_bias,
    w_proj,
    w_gate,
    ln_out_gain,
    ln_out_bias,
    w_out,
):
    rows, width, channels = pair.shape
    hidden = w_out.shape[0]
    halves = 2
    devices = lax.axis_size("row")
    count = devices // halves
    block = hidden // count
    left_rows, right_rows = rows * count, rows * devices
    shape = jax.ShapeDtypeStruct
    panel = shape((count, rows * block, width), BF16)
    wide_panel = shape((devices, rows * block, width), BF16)
    mask = residue_mask.reshape(1, width)
    gain, bias = ln_in_gain.reshape(1, channels), ln_in_bias.reshape(1, channels)
    out_gain, out_bias = ln_out_gain.reshape(1, hidden), ln_out_bias.reshape(1, hidden)
    cells = rows * width
    piece = shape((rows * block, width), BF16)
    left_panel = pltpu.VMEM(panel.shape, BF16)
    left_wide = pltpu.VMEM((left_rows * block, width), F32)
    right_wide = pltpu.VMEM((right_rows * block, width), F32)
    (own_right,) = call(
        project_right_kernel,
        "project_right",
        [wide_panel],
        [pair, mask, gain, bias, w_proj],
        fetched=range(5),
        flops=2 * cells * channels * 2 * hidden,
        limit=64 * 1024 * 1024 - 640 * 1024,
    )
    right_panel = swap(own_right)
    pieces = call(
        project_left_kernel,
        "project_left",
        [piece] * count,
        [pair, mask, gain, bias, w_proj, own_right],
        fetched=range(5),
        unread=(5,),
        scratch=[left_panel],
        flops=2 * cells * channels * 2 * hidden,
    )
    pieces = swap_pieces(pieces)
    (left_all,) = call(
        sort_left_kernel,
        "sort_left",
        [shape((block, left_rows, width), BF16)],
        pieces,
        scratch=[left_wide],
    )
    d_hat_centered, gate_slope = call(
        prepare_kernel,
        "prepare",
        [shape((rows, hidden, width), F32), shape((rows, channels, width), F32)],
        [pair, cotangent, gain, bias, w_gate, out_gain, w_out],
        fetched=range(7),
        flops=2 * cells * channels * 2 * hidden,
    )
    products, right_all = call(
        tri_kernel,
        "tri",
        [panel, shape((block, right_rows, width), BF16)],
        [right_panel, left_all, d_hat_centered],
        unread=(2,),
        scratch=[left_wide, right_wide],
        flops=2 * block * left_rows * width * right_rows,
    )
    products = swap_half(products, count)
    (d_products,) = call(
        middle_kernel,
        "middle",
        [panel],
        [products, d_hat_centered],
        flops=20 * cells * hidden,
    )
    d_products = swap_half(d_products, count)
    d_right_panel, d_tri_all = call(
        d_right_kernel,
        "d_right",
        [wide_panel, shape((block, left_rows, width), BF16)],
        [d_products, left_all],
        scratch=[left_wide, right_wide],
        flops=2 * block * left_rows * width * right_rows,
    )
    d_right_panel = swap(d_right_panel)
    d_pieces = call(
        d_left_kernel,
        "d_left",
        [piece] * count,
        [d_tri_all, right_all],
        scratch=[left_wide],
        flops=2 * block * left_rows * width * right_rows,
    )
    d_pieces = swap_pieces(d_pieces)
    slopes, d_gate_pre, normed_in, inv_in = call(
        slopes_kernel,
        "slopes",
        [
            shape((rows, 4 * hidden, width), BF16),
            shape((rows, channels, width), BF16),
            shape((rows, channels, width), BF16),
            shape((rows, width), F32),
        ],
        [
            products,
            gate_slope,
            pair,
            mask,
            gain,
            bias,
            w_proj,
            out_gain,
            out_bias,
            w_out,
        ],
        fetched=range(2, 10),
        flops=2 * cells * channels * 6 * hidden,
    )
    (grad,) = call(
        finish_kernel,
        "finish",
        [shape(pair.shape, BF16)],
        [d_right_panel, slopes, d_gate_pre, normed_in, inv_in, gain, w_proj, w_gate, *d_pieces],
        fetched=(5, 6, 7),
        scratch=[left_panel],
        flops=2 * cells * channels * 4 * hidden,
    )
    return grad


def normalize(values, reduce_axis):
    mean_value = jnp.mean(values, axis=reduce_axis, keepdims=True)
    centered = values - mean_value
    variance = jnp.mean(centered * centered, axis=reduce_axis, keepdims=True)
    inv_std = lax.rsqrt(variance + 1e-05)
    return (centered * inv_std, inv_std)


def norm_backward(upstream, normed, inv_std, reduce_axis):
    mean_grad = jnp.mean(upstream, axis=reduce_axis, keepdims=True)
    mean_cross = jnp.mean(upstream * normed, axis=reduce_axis, keepdims=True)
    return inv_std * (upstream - mean_grad - normed * mean_cross)


def shards(
    pair,
    cotangent,
    residue_mask,
    ln_in_gain,
    ln_in_bias,
    w_proj,
    w_gate,
    ln_out_gain,
    ln_out_bias,
    w_out,
):
    local_rows = pair.shape[0]
    local_cols = pair.shape[1]
    hidden = w_out.shape[0]
    chan_index = lax.axis_index("chan")
    row_start = lax.axis_index("row") * local_rows
    col_start = chan_index * local_cols
    mask_float = residue_mask.astype(jnp.float32)
    row_mask = lax.dynamic_slice_in_dim(mask_float, row_start, local_rows)
    col_mask = lax.dynamic_slice_in_dim(mask_float, col_start, local_cols)
    cell_mask = (row_mask[:, None] * col_mask[None, :])[None]
    normed, inv_std = normalize(pair.astype(jnp.float32), -1)
    normed_pair = (normed * ln_in_gain + ln_in_bias).astype(jnp.bfloat16)
    projected = jnp.einsum("rmc,ch->hrm", normed_pair, w_proj, preferred_element_type=jnp.float32)
    left_panel = (
        cell_mask * jax.nn.sigmoid(projected[:hidden]) * projected[hidden : 2 * hidden]
    ).astype(jnp.bfloat16)
    right_panel = (
        cell_mask * jax.nn.sigmoid(projected[2 * hidden : 3 * hidden]) * projected[3 * hidden :]
    ).astype(jnp.bfloat16)
    panels = lax.all_to_all(
        jnp.stack([left_panel, right_panel]), "row", split_axis=1, concat_axis=2, tiled=True
    )
    left_all = panels[0]
    right_all = panels[1]
    right_rows = lax.all_to_all(right_all, "chan", split_axis=1, concat_axis=2, tiled=True)
    partner = right_rows
    tri_part = jnp.einsum(
        "gik,gjk->gij",
        lax.all_gather(left_all, "chan", axis=2, tiled=True),
        partner,
        preferred_element_type=jnp.float32,
    ).astype(jnp.bfloat16)
    tri_cells = lax.all_to_all(tri_part, "row", split_axis=1, concat_axis=0, tiled=True)
    tri_hat, inv_tri = normalize(tri_cells.astype(jnp.float32), 0)
    scaled = (tri_hat * ln_out_gain[:, None, None] + ln_out_bias[:, None, None]).astype(
        jnp.bfloat16
    )
    proj_out = jnp.einsum("hrm,hc->rmc", scaled, w_out, preferred_element_type=jnp.float32)
    gate_value = jax.nn.sigmoid(
        jnp.einsum("rmc,cd->rmd", normed_pair, w_gate, preferred_element_type=jnp.float32)
    )
    cot_float = cotangent.astype(jnp.float32)
    d_gate_pre = (cot_float * proj_out * gate_value * (1.0 - gate_value)).astype(jnp.bfloat16)
    d_scaled = (cot_float * gate_value).astype(jnp.bfloat16)
    d_hat = jnp.einsum("rmc,hc->hrm", d_scaled, w_out, preferred_element_type=jnp.float32)
    d_hat = d_hat * ln_out_gain[:, None, None]
    d_tri = norm_backward(d_hat, tri_hat, inv_tri, 0).astype(jnp.bfloat16)
    d_tri_all = lax.all_to_all(d_tri, "row", split_axis=0, concat_axis=1, tiled=True)
    panel_piece = lax.all_gather(d_tri_all, "chan", axis=2, tiled=True)
    partner = right_all
    d_left = jnp.einsum("gij,gjk->gik", panel_piece, partner, preferred_element_type=jnp.float32)
    contribution = jnp.einsum(
        "gij,gik->gjk", panel_piece, left_all, preferred_element_type=jnp.float32
    )
    d_right = contribution
    d_left, d_right = (d_left, d_right)
    d_stack = jnp.stack([d_left, d_right]).astype(jnp.bfloat16)
    d_panels = lax.all_to_all(d_stack, "row", split_axis=2, concat_axis=1, tiled=True)

    def gating(d_value, gate_proj, value_proj):
        sigmoid_val = jax.nn.sigmoid(gate_proj)
        masked_grad = d_value.astype(jnp.float32) * cell_mask
        return (
            masked_grad * value_proj * sigmoid_val * (1.0 - sigmoid_val),
            masked_grad * sigmoid_val,
        )

    gate_left, value_left = gating(d_panels[0], projected[:hidden], projected[hidden : 2 * hidden])
    gate_right, value_right = gating(
        d_panels[1], projected[2 * hidden : 3 * hidden], projected[3 * hidden :]
    )
    d_proj = jnp.concatenate([gate_left, value_left, gate_right, value_right], axis=0).astype(
        jnp.bfloat16
    )
    d_normed = jnp.einsum("hrm,ch->rmc", d_proj, w_proj, preferred_element_type=jnp.float32)
    d_normed = d_normed + jnp.einsum(
        "rmd,cd->rmc", d_gate_pre, w_gate, preferred_element_type=jnp.float32
    )
    d_input = d_normed * ln_in_gain
    return norm_backward(d_input, normed, inv_std, -1).astype(jnp.bfloat16)


def solution(mesh):
    fits = mesh.shape["chan"] == 1 and mesh.shape["row"] in (8, 16)
    return jax.shard_map(
        kernel_shards if fits else shards,
        mesh=mesh,
        in_specs=(
            P(("grp", "row"), "chan", None),
            P(("grp", "row"), "chan", None),
            P("grp"),
            P(),
            P(),
            P(),
            P(),
            P(),
            P(),
            P(),
        ),
        out_specs=P(("grp", "row"), "chan", None),
        check_vma=False,
    )
```

```python
import functools

import jax
import jax.numpy as jnp
from jax import lax
from jax.experimental import pallas as pl
from jax.experimental.pallas import tpu as pltpu
from jax.sharding import PartitionSpec as P

F32 = jnp.float32
BF16 = jnp.bfloat16
VMEM_LIMIT = 16 * 1024 * 1024


def dot(lhs, rhs, lhs_dim, rhs_dim):
    return lax.dot_general(
        lhs, rhs, (((lhs_dim,), (rhs_dim,)), ((), ())), preferred_element_type=F32
    )


def transposed(matrix):
    return jnp.transpose(matrix.astype(F32)).astype(BF16)


def sigmoid(values):
    return 1.0 / (1.0 + jnp.exp(-values))


def column(row):
    size = row.shape[1]
    return jnp.transpose(jnp.broadcast_to(row, (size, size)))


def norm_rows(values):
    centered = values - jnp.mean(values, axis=0, keepdims=True)
    variance = jnp.mean(centered * centered, axis=0, keepdims=True)
    inv_std = lax.rsqrt(variance + 1e-05)
    return centered * inv_std, inv_std


def call(
    kernel, name, outs, args, fetched=(), unread=(), sent=(), scratch=(), flops=0, limit=VMEM_LIMIT
):
    moved = sum(a.size * a.dtype.itemsize for a in args) + sum(
        o.size * jnp.dtype(o.dtype).itemsize for o in outs
    )
    n_args, n_outs, n_fetched = len(args), len(outs), len(fetched)

    def body(*refs):
        ins = list(refs[:n_args])
        rest = refs[n_args + n_outs :]
        copies = []
        for n, place in enumerate(fetched):
            copies.append(pltpu.make_async_copy(ins[place], rest[n], rest[n_fetched].at[n]))
            ins[place] = rest[n]
        for copy in copies:
            copy.start()
        for copy in copies:
            copy.wait()
        kernel(*ins, *refs[n_args : n_args + n_outs], *rest[n_fetched + (n_fetched > 0) :])

    buffers = [pltpu.VMEM(args[place].shape, args[place].dtype) for place in fetched]
    if fetched:
        buffers.append(pltpu.SemaphoreType.DMA((n_fetched,)))
    return pl.pallas_call(
        body,
        name=name,
        out_shape=outs,
        in_specs=[
            pl.BlockSpec(
                memory_space=pltpu.HBM if n in fetched else pl.ANY if n in unread else pltpu.VMEM
            )
            for n in range(n_args)
        ],
        out_specs=[
            pl.BlockSpec(memory_space=pltpu.HBM if n in sent else pltpu.VMEM) for n in range(n_outs)
        ],
        scratch_shapes=buffers + list(scratch),
        compiler_params=pltpu.CompilerParams(vmem_limit_bytes=limit),
        cost_estimate=pl.CostEstimate(flops=flops, bytes_accessed=moved, transcendentals=0),
    )(*args)


def cell_masks(mask, rows):
    columns = mask[...].astype(F32)
    shape = (rows, columns.shape[1])
    first = lax.axis_index("row") * rows
    own = lax.broadcasted_iota(jnp.int32, shape, 1) == (
        lax.broadcasted_iota(jnp.int32, shape, 0) + first
    )
    row_mask = jnp.sum(jnp.where(own, columns, 0.0), axis=1, keepdims=True)
    cells = row_mask * columns
    return [cells[row : row + 1] for row in range(rows)]


def partner(step, count):
    return lax.rem(lax.axis_index("row"), count) ^ step


def gated_rows(pair, mask, gain, bias, w_proj, side):
    rows, width, _ = pair.shape
    hidden = w_proj.shape[1] // 4
    w_flip = transposed(w_proj[:, 2 * side * hidden : 2 * (side + 1) * hidden])
    gain_col, bias_col = column(gain[...]), column(bias[...])
    masks = cell_masks(mask, rows)
    for first in range(0, rows, 2):
        zlns = []
        for row in (first, first + 1):
            normed, _ = norm_rows(jnp.transpose(pair[row].astype(F32)))
            zlns.append((normed * gain_col + bias_col).astype(BF16))
        proj = dot(w_flip, jnp.concatenate(zlns, axis=1), 1, 0)
        gated = sigmoid(proj[:hidden]) * proj[hidden:]
        yield first, masks[first] * gated[:, :width]
        yield first + 1, masks[first + 1] * gated[:, width:]


def project_right_kernel(pair, mask, gain, bias, w_proj, right_panel, own_panel, sems):
    rows = pair.shape[0]
    count, depth, width = own_panel.shape
    block = depth // rows
    copies = []
    for row, right in gated_rows(pair, mask, gain, bias, w_proj, 1):
        place = pl.ds(row * block, block)
        own_panel[:, place, :] = right.reshape(count, block, width).astype(BF16)
        for half in range(right_panel.shape[0] // count):
            copy = pltpu.make_async_copy(
                own_panel.at[:, place, :],
                right_panel.at[pl.ds(half * count, count), place, :],
                sems.at[row, half],
            )
            copy.start()
            copies.append(copy)
    for copy in copies:
        copy.wait()


def project_left_kernel(pair, mask, gain, bias, w_proj, after, *refs):
    del after
    *pieces, left_panel = refs
    rows = pair.shape[0]
    count, depth, width = left_panel.shape
    block = depth // rows
    for row, left in gated_rows(pair, mask, gain, bias, w_proj, 0):
        left = left.reshape(count, block, width).astype(BF16)
        left_panel[:, row * block : (row + 1) * block, :] = left
    for step, piece in enumerate(pieces):
        piece[...] = left_panel[partner(step, count)]


def prepare_kernel(
    pair, cotangent, gain, bias, w_gate, out_gain, w_out, d_hat_centered, gate_slope
):
    gate_flip = transposed(w_gate[...])
    gain_col, bias_col = column(gain[...]), column(bias[...])
    out_gain_col = column(out_gain[...])
    for row in range(pair.shape[0]):
        normed, _ = norm_rows(jnp.transpose(pair[row].astype(F32)))
        zln = (normed * gain_col + bias_col).astype(BF16)
        gate = sigmoid(dot(gate_flip, zln, 1, 0))
        cot = jnp.transpose(cotangent[row].astype(F32))
        d_scaled = (cot * gate).astype(BF16)
        d_hat = dot(w_out[...], d_scaled, 1, 0) * out_gain_col
        d_hat_centered[row] = d_hat - jnp.mean(d_hat, axis=0, keepdims=True)
        gate_slope[row] = cot * gate * (1.0 - gate)


def spread(panel, wide):
    wide[...] = panel[...].astype(F32).reshape(wide.shape)


def sort_left_kernel(*refs):
    *pieces, left_all, left_wide = refs
    block, left_rows, _ = left_all.shape
    depth = pieces[0].shape[0]
    for step, piece in enumerate(pieces):
        start = pl.multiple_of(partner(step, len(pieces)) * depth, depth)
        left_wide[pl.ds(start, depth), :] = piece[...].astype(F32)
    for h in range(block):
        left_all[h] = left_wide[pl.ds(h, left_rows, stride=block), :].astype(BF16)


def tri_kernel(right_panel, left_all, after, products, right_all, left_wide, right_wide):
    del after
    block, left_rows, _ = left_all.shape
    right_rows = right_all.shape[1]
    spread(right_panel, right_wide)
    for h in range(block):
        right = right_wide[pl.ds(h, right_rows, stride=block), :].astype(BF16)
        right_all[h] = right
        left_wide[pl.ds(h, left_rows, stride=block), :] = dot(left_all[h], right, 1, 1)
    products[...] = left_wide[...].astype(BF16).reshape(products.shape)


def cell_row(ref, row, rows):
    count, depth, width = ref.shape
    block = depth // rows
    return ref[:, row * block : (row + 1) * block, :].astype(F32).reshape(count * block, width)


def middle_kernel(products, d_hat_centered, d_products):
    rows = d_hat_centered.shape[0]
    count, depth, width = products.shape
    block = depth // rows
    for row in range(rows):
        tri_hat, inv_std = norm_rows(cell_row(products, row, rows))
        d_hat = d_hat_centered[row]
        cross = jnp.mean(d_hat * tri_hat, axis=0, keepdims=True)
        d_tri = inv_std * (d_hat - tri_hat * cross)
        d_products[:, row * block : (row + 1) * block, :] = d_tri.reshape(
            count, block, width
        ).astype(BF16)


def d_right_kernel(
    d_products, left_all, d_right_panel, d_tri_all, left_wide, right_wide, panel, sems
):
    block, left_rows, _ = left_all.shape
    devices, depth, _ = panel.shape
    spread(d_products, left_wide)
    for h in range(block):
        d_tri = left_wide[pl.ds(h, left_rows, stride=block), :].astype(BF16)
        d_tri_all[h] = d_tri
        right_wide[pl.ds(h, devices * depth // block, stride=block), :] = dot(
            d_tri, left_all[h], 0, 0
        )
    copies = []
    for device in range(devices):
        panel[device] = right_wide[device * depth : (device + 1) * depth, :].astype(BF16)
        copy = pltpu.make_async_copy(panel.at[device], d_right_panel.at[device], sems.at[device])
        copy.start()
        copies.append(copy)
    for copy in copies:
        copy.wait()


def d_left_kernel(d_tri_all, right_all, *refs):
    *pieces, left_wide = refs
    block, left_rows, _ = d_tri_all.shape
    for h in range(block):
        left_wide[pl.ds(h, left_rows, stride=block), :] = dot(d_tri_all[h], right_all[h], 1, 0)
    depth = pieces[0].shape[0]
    for step, piece in enumerate(pieces):
        start = pl.multiple_of(partner(step, len(pieces)) * depth, depth)
        piece[...] = left_wide[pl.ds(start, depth), :].astype(BF16)


def slopes_kernel(
    products,
    gate_slope,
    pair,
    mask,
    gain,
    bias,
    w_proj,
    out_gain,
    out_bias,
    w_out,
    slopes,
    d_gate_pre,
    normed_in,
    inv_in,
):
    rows = pair.shape[0]
    hidden = w_out.shape[0]
    w_flip = transposed(w_proj[...])
    out_flip = transposed(w_out[...])
    gain_col, bias_col = column(gain[...]), column(bias[...])
    out_gain_col, out_bias_col = column(out_gain[...]), column(out_bias[...])
    masks = cell_masks(mask, rows)
    for row in range(rows):
        tri_hat, _ = norm_rows(cell_row(products, row, rows))
        scaled = (tri_hat * out_gain_col + out_bias_col).astype(BF16)
        d_gate_pre[row] = (dot(out_flip, scaled, 1, 0) * gate_slope[row]).astype(BF16)
        normed, inv_std = norm_rows(jnp.transpose(pair[row].astype(F32)))
        normed_in[row] = normed.astype(normed_in.dtype)
        inv_in[row : row + 1] = inv_std
        zln = (normed * gain_col + bias_col).astype(BF16)
        proj = dot(w_flip, zln, 1, 0)
        for side in range(2):
            base = 2 * side * hidden
            sig = sigmoid(proj[base : base + hidden])
            masked = masks[row] * sig
            value = masked * (1.0 - sig) * proj[base + hidden : base + 2 * hidden]
            slopes[row, base : base + hidden, :] = value.astype(slopes.dtype)
            slopes[row, base + hidden : base + 2 * hidden, :] = masked.astype(slopes.dtype)


def sort_d_left_kernel(*refs):
    *pieces, d_left_panel = refs
    for step, piece in enumerate(pieces):
        d_left_panel[partner(step, len(pieces))] = piece[...]


def finish_kernel(
    d_right_panel,
    d_left_panel,
    slopes,
    d_gate_pre,
    normed_in,
    inv_in,
    gain,
    w_proj,
    w_gate,
    grad,
    own_grad,
    sems,
):
    rows = grad.shape[0]
    count, depth, width = d_left_panel.shape
    hidden = count * depth // rows
    gain_col = column(gain[...])
    weights = jnp.concatenate([w_proj[...], w_gate[...]], axis=1)
    copies = []
    for first in range(0, rows, 2):
        stacks = []
        for row in (first, first + 1):
            d_right = cell_row(d_right_panel, row, rows)
            d_right = sum(d_right[n : n + hidden] for n in range(0, d_right.shape[0], hidden))
            parts = []
            for side, d_value in enumerate((cell_row(d_left_panel, row, rows), d_right)):
                for base in (2 * side * hidden, (2 * side + 1) * hidden):
                    slope = slopes[row, base : base + hidden, :].astype(F32)
                    parts.append((d_value * slope).astype(BF16))
            parts.append(d_gate_pre[row])
            stacks.append(jnp.concatenate(parts, axis=0))
        d_zln = dot(weights, jnp.concatenate(stacks, axis=1), 1, 0)
        for n, row in enumerate((first, first + 1)):
            d_in = d_zln[:, n * width : (n + 1) * width] * gain_col
            normed = normed_in[row].astype(F32)
            mean_grad = jnp.mean(d_in, axis=0, keepdims=True)
            mean_cross = jnp.mean(d_in * normed, axis=0, keepdims=True)
            result = inv_in[row : row + 1] * (d_in - mean_grad - normed * mean_cross)
            own_grad[row] = jnp.transpose(result).astype(BF16)
            copy = pltpu.make_async_copy(own_grad.at[row], grad.at[row], sems.at[row])
            copy.start()
            copies.append(copy)
    for copy in copies:
        copy.wait()


def swap(values):
    return lax.all_to_all(values, "row", split_axis=0, concat_axis=0, tiled=True)


def swap_half(values, count):
    devices = range(lax.axis_size("row"))
    groups = [[d for d in devices if d // count == half] for half in range(len(devices) // count)]
    return lax.all_to_all(
        values, "row", split_axis=0, concat_axis=0, tiled=True, axis_index_groups=groups
    )


def swap_pieces(pieces):
    devices = range(lax.axis_size("row"))
    return [pieces[0]] + [
        lax.ppermute(pieces[step], "row", [(d, d ^ step) for d in devices])
        for step in range(1, len(pieces))
    ]


def kernel_shards(
    pair,
    cotangent,
    residue_mask,
    ln_in_gain,
    ln_in_bias,
    w_proj,
    w_gate,
    ln_out_gain,
    ln_out_bias,
    w_out,
):
    rows, width, channels = pair.shape
    hidden = w_out.shape[0]
    halves = 2
    devices = lax.axis_size("row")
    count = devices // halves
    block = hidden // count
    left_rows, right_rows = rows * count, rows * devices
    shape = jax.ShapeDtypeStruct
    panel = shape((count, rows * block, width), BF16)
    wide_panel = shape((devices, rows * block, width), BF16)
    mask = residue_mask.reshape(1, width)
    gain, bias = ln_in_gain.reshape(1, channels), ln_in_bias.reshape(1, channels)
    out_gain, out_bias = ln_out_gain.reshape(1, hidden), ln_out_bias.reshape(1, hidden)
    cells = rows * width
    piece = shape((rows * block, width), BF16)
    left_panel = pltpu.VMEM(panel.shape, BF16)
    left_wide = pltpu.VMEM((left_rows * block, width), F32)
    right_wide = pltpu.VMEM((right_rows * block, width), F32)
    (own_right,) = call(
        project_right_kernel,
        "project_right",
        [wide_panel],
        [pair, mask, gain, bias, w_proj],
        fetched=range(5),
        sent=(0,),
        scratch=[left_panel, pltpu.SemaphoreType.DMA((rows, halves))],
        flops=2 * cells * channels * 2 * hidden,
        limit=64 * 1024 * 1024 - 640 * 1024,
    )
    right_panel = swap(own_right)
    pieces = call(
        project_left_kernel,
        "project_left",
        [piece] * count,
        [pair, mask, gain, bias, w_proj, own_right],
        fetched=range(5),
        unread=(5,),
        scratch=[left_panel],
        flops=2 * cells * channels * 2 * hidden,
    )
    pieces = swap_pieces(pieces)
    (left_all,) = call(
        sort_left_kernel,
        "sort_left",
        [shape((block, left_rows, width), BF16)],
        pieces,
        scratch=[left_wide],
    )
    d_hat_centered, gate_slope = call(
        prepare_kernel,
        "prepare",
        [shape((rows, hidden, width), F32), shape((rows, channels, width), F32)],
        [pair, cotangent, gain, bias, w_gate, out_gain, w_out],
        fetched=range(7),
        flops=2 * cells * channels * 2 * hidden,
    )
    products, right_all = call(
        tri_kernel,
        "tri",
        [panel, shape((block, right_rows, width), BF16)],
        [right_panel, left_all, d_hat_centered],
        unread=(2,),
        scratch=[left_wide, right_wide],
        flops=2 * block * left_rows * width * right_rows,
    )
    products = swap_half(products, count)
    (d_products,) = call(
        middle_kernel,
        "middle",
        [panel],
        [products, d_hat_centered],
        flops=20 * cells * hidden,
    )
    d_products = swap_half(d_products, count)
    d_right_panel, d_tri_all = call(
        d_right_kernel,
        "d_right",
        [wide_panel, shape((block, left_rows, width), BF16)],
        [d_products, left_all],
        sent=(0,),
        scratch=[
            left_wide,
            right_wide,
            pltpu.VMEM(wide_panel.shape, BF16),
            pltpu.SemaphoreType.DMA((devices,)),
        ],
        flops=2 * block * left_rows * width * right_rows,
    )
    d_right_panel = swap(d_right_panel)
    d_pieces = call(
        d_left_kernel,
        "d_left",
        [piece] * count,
        [d_tri_all, right_all],
        scratch=[left_wide],
        flops=2 * block * left_rows * width * right_rows,
    )
    d_pieces = swap_pieces(d_pieces)
    (d_left_panel,) = call(sort_d_left_kernel, "sort_d_left", [panel], d_pieces)
    slopes, d_gate_pre, normed_in, inv_in = call(
        slopes_kernel,
        "slopes",
        [
            shape((rows, 4 * hidden, width), BF16),
            shape((rows, channels, width), BF16),
            shape((rows, channels, width), BF16),
            shape((rows, width), F32),
        ],
        [
            products,
            gate_slope,
            pair,
            mask,
            gain,
            bias,
            w_proj,
            out_gain,
            out_bias,
            w_out,
        ],
        fetched=range(2, 10),
        flops=2 * cells * channels * 6 * hidden,
    )
    (grad,) = call(
        finish_kernel,
        "finish",
        [shape(pair.shape, BF16)],
        [
            d_right_panel,
            d_left_panel,
            slopes,
            d_gate_pre,
            normed_in,
            inv_in,
            gain,
            w_proj,
            w_gate,
        ],
        fetched=(6, 7, 8),
        sent=(0,),
        scratch=[pltpu.VMEM(pair.shape, BF16), pltpu.SemaphoreType.DMA((rows,))],
        flops=2 * cells * channels * 4 * hidden,
    )
    return grad


def normalize(values, reduce_axis):
    mean_value = jnp.mean(values, axis=reduce_axis, keepdims=True)
    centered = values - mean_value
    variance = jnp.mean(centered * centered, axis=reduce_axis, keepdims=True)
    inv_std = lax.rsqrt(variance + 1e-05)
    return (centered * inv_std, inv_std)


def norm_backward(upstream, normed, inv_std, reduce_axis):
    mean_grad = jnp.mean(upstream, axis=reduce_axis, keepdims=True)
    mean_cross = jnp.mean(upstream * normed, axis=reduce_axis, keepdims=True)
    return inv_std * (upstream - mean_grad - normed * mean_cross)


def shards(
    pair,
    cotangent,
    residue_mask,
    ln_in_gain,
    ln_in_bias,
    w_proj,
    w_gate,
    ln_out_gain,
    ln_out_bias,
    w_out,
):
    local_rows = pair.shape[0]
    local_cols = pair.shape[1]
    hidden = w_out.shape[0]
    chan_index = lax.axis_index("chan")
    row_start = lax.axis_index("row") * local_rows
    col_start = chan_index * local_cols
    mask_float = residue_mask.astype(jnp.float32)
    row_mask = lax.dynamic_slice_in_dim(mask_float, row_start, local_rows)
    col_mask = lax.dynamic_slice_in_dim(mask_float, col_start, local_cols)
    cell_mask = (row_mask[:, None] * col_mask[None, :])[None]
    normed, inv_std = normalize(pair.astype(jnp.float32), -1)
    normed_pair = (normed * ln_in_gain + ln_in_bias).astype(jnp.bfloat16)
    projected = jnp.einsum("rmc,ch->hrm", normed_pair, w_proj, preferred_element_type=jnp.float32)
    left_panel = (
        cell_mask * jax.nn.sigmoid(projected[:hidden]) * projected[hidden : 2 * hidden]
    ).astype(jnp.bfloat16)
    right_panel = (
        cell_mask * jax.nn.sigmoid(projected[2 * hidden : 3 * hidden]) * projected[3 * hidden :]
    ).astype(jnp.bfloat16)
    panels = lax.all_to_all(
        jnp.stack([left_panel, right_panel]), "row", split_axis=1, concat_axis=2, tiled=True
    )
    left_all = panels[0]
    right_all = panels[1]
    right_rows = lax.all_to_all(right_all, "chan", split_axis=1, concat_axis=2, tiled=True)
    partner = right_rows
    tri_part = jnp.einsum(
        "gik,gjk->gij",
        lax.all_gather(left_all, "chan", axis=2, tiled=True),
        partner,
        preferred_element_type=jnp.float32,
    ).astype(jnp.bfloat16)
    tri_cells = lax.all_to_all(tri_part, "row", split_axis=1, concat_axis=0, tiled=True)
    tri_hat, inv_tri = normalize(tri_cells.astype(jnp.float32), 0)
    scaled = (tri_hat * ln_out_gain[:, None, None] + ln_out_bias[:, None, None]).astype(
        jnp.bfloat16
    )
    proj_out = jnp.einsum("hrm,hc->rmc", scaled, w_out, preferred_element_type=jnp.float32)
    gate_value = jax.nn.sigmoid(
        jnp.einsum("rmc,cd->rmd", normed_pair, w_gate, preferred_element_type=jnp.float32)
    )
    cot_float = cotangent.astype(jnp.float32)
    d_gate_pre = (cot_float * proj_out * gate_value * (1.0 - gate_value)).astype(jnp.bfloat16)
    d_scaled = (cot_float * gate_value).astype(jnp.bfloat16)
    d_hat = jnp.einsum("rmc,hc->hrm", d_scaled, w_out, preferred_element_type=jnp.float32)
    d_hat = d_hat * ln_out_gain[:, None, None]
    d_tri = norm_backward(d_hat, tri_hat, inv_tri, 0).astype(jnp.bfloat16)
    d_tri_all = lax.all_to_all(d_tri, "row", split_axis=0, concat_axis=1, tiled=True)
    panel_piece = lax.all_gather(d_tri_all, "chan", axis=2, tiled=True)
    partner = right_all
    d_left = jnp.einsum("gij,gjk->gik", panel_piece, partner, preferred_element_type=jnp.float32)
    contribution = jnp.einsum(
        "gij,gik->gjk", panel_piece, left_all, preferred_element_type=jnp.float32
    )
    d_right = contribution
    d_left, d_right = (d_left, d_right)
    d_stack = jnp.stack([d_left, d_right]).astype(jnp.bfloat16)
    d_panels = lax.all_to_all(d_stack, "row", split_axis=2, concat_axis=1, tiled=True)

    def gating(d_value, gate_proj, value_proj):
        sigmoid_val = jax.nn.sigmoid(gate_proj)
        masked_grad = d_value.astype(jnp.float32) * cell_mask
        return (
            masked_grad * value_proj * sigmoid_val * (1.0 - sigmoid_val),
            masked_grad * sigmoid_val,
        )

    gate_left, value_left = gating(d_panels[0], projected[:hidden], projected[hidden : 2 * hidden])
    gate_right, value_right = gating(
        d_panels[1], projected[2 * hidden : 3 * hidden], projected[3 * hidden :]
    )
    d_proj = jnp.concatenate([gate_left, value_left, gate_right, value_right], axis=0).astype(
        jnp.bfloat16
    )
    d_normed = jnp.einsum("hrm,ch->rmc", d_proj, w_proj, preferred_element_type=jnp.float32)
    d_normed = d_normed + jnp.einsum(
        "rmd,cd->rmc", d_gate_pre, w_gate, preferred_element_type=jnp.float32
    )
    d_input = d_normed * ln_in_gain
    return norm_backward(d_input, normed, inv_std, -1).astype(jnp.bfloat16)


def solution(mesh):
    fits = mesh.shape["chan"] == 1 and mesh.shape["row"] in (8, 16)
    return jax.shard_map(
        kernel_shards if fits else shards,
        mesh=mesh,
        in_specs=(
            P(("grp", "row"), "chan", None),
            P(("grp", "row"), "chan", None),
            P("grp"),
            P(),
            P(),
            P(),
            P(),
            P(),
            P(),
            P(),
        ),
        out_specs=P(("grp", "row"), "chan", None),
        check_vma=False,
    )
```

```python
import functools

import jax
import jax.numpy as jnp
from jax import lax
from jax.experimental import pallas as pl
from jax.experimental.pallas import tpu as pltpu
from jax.sharding import PartitionSpec as P

F32 = jnp.float32
BF16 = jnp.bfloat16
VMEM_LIMIT = 16 * 1024 * 1024


def dot(lhs, rhs, lhs_dim, rhs_dim):
    return lax.dot_general(
        lhs, rhs, (((lhs_dim,), (rhs_dim,)), ((), ())), preferred_element_type=F32
    )


def transposed(matrix):
    return jnp.transpose(matrix.astype(F32)).astype(BF16)


def sigmoid(values):
    return 1.0 / (1.0 + jnp.exp(-values))


def column(row):
    size = row.shape[1]
    return jnp.transpose(jnp.broadcast_to(row, (size, size)))


def norm_rows(values):
    centered = values - jnp.mean(values, axis=0, keepdims=True)
    variance = jnp.mean(centered * centered, axis=0, keepdims=True)
    inv_std = lax.rsqrt(variance + 1e-05)
    return centered * inv_std, inv_std


def call(
    kernel, name, outs, args, fetched=(), unread=(), scratch=(), flops=0, limit=VMEM_LIMIT
):
    moved = sum(a.size * a.dtype.itemsize for a in args) + sum(
        o.size * jnp.dtype(o.dtype).itemsize for o in outs
    )
    n_args, n_outs, n_fetched = len(args), len(outs), len(fetched)

    def body(*refs):
        ins = list(refs[:n_args])
        rest = refs[n_args + n_outs :]
        copies = []
        for n, place in enumerate(fetched):
            copies.append(pltpu.make_async_copy(ins[place], rest[n], rest[n_fetched].at[n]))
            ins[place] = rest[n]
        for copy in copies:
            copy.start()
        for copy in copies:
            copy.wait()
        kernel(*ins, *refs[n_args : n_args + n_outs], *rest[n_fetched + (n_fetched > 0) :])

    buffers = [pltpu.VMEM(args[place].shape, args[place].dtype) for place in fetched]
    if fetched:
        buffers.append(pltpu.SemaphoreType.DMA((n_fetched,)))
    return pl.pallas_call(
        body,
        name=name,
        out_shape=outs,
        in_specs=[
            pl.BlockSpec(
                memory_space=pltpu.HBM if n in fetched else pl.ANY if n in unread else pltpu.VMEM
            )
            for n in range(n_args)
        ],
        out_specs=[pl.BlockSpec(memory_space=pltpu.VMEM) for _ in outs],
        scratch_shapes=buffers + list(scratch),
        compiler_params=pltpu.CompilerParams(vmem_limit_bytes=limit),
        cost_estimate=pl.CostEstimate(flops=flops, bytes_accessed=moved, transcendentals=0),
    )(*args)


def cell_masks(mask, rows):
    columns = mask[...].astype(F32)
    shape = (rows, columns.shape[1])
    first = lax.axis_index("row") * rows
    own = lax.broadcasted_iota(jnp.int32, shape, 1) == (
        lax.broadcasted_iota(jnp.int32, shape, 0) + first
    )
    row_mask = jnp.sum(jnp.where(own, columns, 0.0), axis=1, keepdims=True)
    cells = row_mask * columns
    return [cells[row : row + 1] for row in range(rows)]


def partner(step, count):
    return lax.rem(lax.axis_index("row"), count) ^ step


def gated_rows(pair, mask, gain, bias, w_proj, side):
    rows = pair.shape[0]
    hidden = w_proj.shape[1] // 4
    w_flip = transposed(w_proj[:, 2 * side * hidden : 2 * (side + 1) * hidden])
    gain_col, bias_col = column(gain[...]), column(bias[...])
    masks = cell_masks(mask, rows)
    for row in range(rows):
        normed, _ = norm_rows(jnp.transpose(pair[row].astype(F32)))
        zln = (normed * gain_col + bias_col).astype(BF16)
        proj = dot(w_flip, zln, 1, 0)
        yield row, masks[row] * sigmoid(proj[:hidden]) * proj[hidden:]


def project_right_kernel(pair, mask, gain, bias, w_proj, right_panel):
    rows = pair.shape[0]
    devices, depth, width = right_panel.shape
    block = depth // rows
    hidden = w_proj.shape[1] // 4
    count = hidden // block
    for row, right in gated_rows(pair, mask, gain, bias, w_proj, 1):
        right = right.reshape(count, block, width).astype(BF16)
        for start in range(0, devices, count):
            right_panel[start : start + count, row * block : (row + 1) * block, :] = right


def project_left_kernel(pair, mask, gain, bias, w_proj, after, *refs):
    del after
    *pieces, left_panel = refs
    rows = pair.shape[0]
    count, depth, width = left_panel.shape
    block = depth // rows
    for row, left in gated_rows(pair, mask, gain, bias, w_proj, 0):
        left = left.reshape(count, block, width).astype(BF16)
        left_panel[:, row * block : (row + 1) * block, :] = left
    for step, piece in enumerate(pieces):
        piece[...] = left_panel[partner(step, count)]


def prepare_kernel(
    pair, cotangent, gain, bias, w_gate, out_gain, w_out, d_hat_centered, gate_slope
):
    gate_flip = transposed(w_gate[...])
    gain_col, bias_col = column(gain[...]), column(bias[...])
    out_gain_col = column(out_gain[...])
    for row in range(pair.shape[0]):
        normed, _ = norm_rows(jnp.transpose(pair[row].astype(F32)))
        zln = (normed * gain_col + bias_col).astype(BF16)
        gate = sigmoid(dot(gate_flip, zln, 1, 0))
        cot = jnp.transpose(cotangent[row].astype(F32))
        d_scaled = (cot * gate).astype(BF16)
        d_hat = dot(w_out[...], d_scaled, 1, 0) * out_gain_col
        d_hat_centered[row] = d_hat - jnp.mean(d_hat, axis=0, keepdims=True)
        gate_slope[row] = cot * gate * (1.0 - gate)


def spread(panel, wide):
    wide[...] = panel[...].astype(F32).reshape(wide.shape)


def sort_left_kernel(*refs):
    *pieces, left_all, left_wide = refs
    block, left_rows, _ = left_all.shape
    depth = pieces[0].shape[0]
    for step, piece in enumerate(pieces):
        start = pl.multiple_of(partner(step, len(pieces)) * depth, depth)
        left_wide[pl.ds(start, depth), :] = piece[...].astype(F32)
    for h in range(block):
        left_all[h] = left_wide[pl.ds(h, left_rows, stride=block), :].astype(BF16)


def tri_kernel(right_panel, left_all, after, products, right_all, left_wide, right_wide):
    del after
    block, left_rows, _ = left_all.shape
    right_rows = right_all.shape[1]
    spread(right_panel, right_wide)
    for h in range(block):
        right = right_wide[pl.ds(h, right_rows, stride=block), :].astype(BF16)
        right_all[h] = right
        left_wide[pl.ds(h, left_rows, stride=block), :] = dot(left_all[h], right, 1, 1)
    products[...] = left_wide[...].astype(BF16).reshape(products.shape)


def cell_row(ref, row, rows):
    count, depth, width = ref.shape
    block = depth // rows
    return ref[:, row * block : (row + 1) * block, :].astype(F32).reshape(count * block, width)


def middle_kernel(products, d_hat_centered, d_products):
    rows = d_hat_centered.shape[0]
    count, depth, width = products.shape
    block = depth // rows
    for row in range(rows):
        tri_hat, inv_std = norm_rows(cell_row(products, row, rows))
        d_hat = d_hat_centered[row]
        cross = jnp.mean(d_hat * tri_hat, axis=0, keepdims=True)
        d_tri = inv_std * (d_hat - tri_hat * cross)
        d_products[:, row * block : (row + 1) * block, :] = d_tri.reshape(
            count, block, width
        ).astype(BF16)


def d_right_kernel(d_products, left_all, d_right_panel, d_tri_all, left_wide, right_wide):
    block, left_rows, _ = left_all.shape
    right_rows = right_wide.shape[0] // block
    spread(d_products, left_wide)
    for h in range(block):
        d_tri = left_wide[pl.ds(h, left_rows, stride=block), :].astype(BF16)
        d_tri_all[h] = d_tri
        right_wide[pl.ds(h, right_rows, stride=block), :] = dot(d_tri, left_all[h], 0, 0)
    d_right_panel[...] = right_wide[...].astype(BF16).reshape(d_right_panel.shape)


def d_left_kernel(d_tri_all, right_all, *refs):
    *pieces, left_wide = refs
    block, left_rows, _ = d_tri_all.shape
    for h in range(block):
        left_wide[pl.ds(h, left_rows, stride=block), :] = dot(d_tri_all[h], right_all[h], 1, 0)
    depth = pieces[0].shape[0]
    for step, piece in enumerate(pieces):
        start = pl.multiple_of(partner(step, len(pieces)) * depth, depth)
        piece[...] = left_wide[pl.ds(start, depth), :].astype(BF16)


def slopes_kernel(
    products,
    gate_slope,
    pair,
    mask,
    gain,
    bias,
    w_proj,
    w_gate,
    out_gain,
    out_bias,
    w_out,
    slopes,
    d_gate_pre,
    normed_in,
    inv_in,
    in_gain,
    weights,
):
    rows = pair.shape[0]
    hidden = w_out.shape[0]
    w_flip = transposed(w_proj[...])
    out_flip = transposed(w_out[...])
    gain_col, bias_col = column(gain[...]), column(bias[...])
    in_gain[...] = gain_col
    weights[...] = jnp.concatenate([w_proj[...], w_gate[...]], axis=1)
    out_gain_col, out_bias_col = column(out_gain[...]), column(out_bias[...])
    masks = cell_masks(mask, rows)
    for row in range(rows):
        tri_hat, _ = norm_rows(cell_row(products, row, rows))
        scaled = (tri_hat * out_gain_col + out_bias_col).astype(BF16)
        d_gate_pre[row] = (dot(out_flip, scaled, 1, 0) * gate_slope[row]).astype(BF16)
        normed, inv_std = norm_rows(jnp.transpose(pair[row].astype(F32)))
        normed_in[row] = normed.astype(normed_in.dtype)
        inv_in[row : row + 1] = inv_std
        zln = (normed * gain_col + bias_col).astype(BF16)
        proj = dot(w_flip, zln, 1, 0)
        for side in range(2):
            base = 2 * side * hidden
            sig = sigmoid(proj[base : base + hidden])
            masked = masks[row] * sig
            value = masked * (1.0 - sig) * proj[base + hidden : base + 2 * hidden]
            slopes[row, base : base + hidden, :] = value.astype(slopes.dtype)
            slopes[row, base + hidden : base + 2 * hidden, :] = masked.astype(slopes.dtype)


def sort_d_left_kernel(*refs):
    *pieces, d_left_panel = refs
    for step, piece in enumerate(pieces):
        d_left_panel[partner(step, len(pieces))] = piece[...]


def finish_kernel(
    d_right_panel, d_left_panel, slopes, d_gate_pre, normed_in, inv_in, gain_col, weights, grad
):
    rows = grad.shape[0]
    count, depth, width = d_left_panel.shape
    hidden = count * depth // rows
    for row in range(rows):
        d_right = cell_row(d_right_panel, row, rows)
        d_right = sum(d_right[n : n + hidden] for n in range(0, d_right.shape[0], hidden))
        parts = []
        for side, d_value in enumerate((cell_row(d_left_panel, row, rows), d_right)):
            for base in (2 * side * hidden, (2 * side + 1) * hidden):
                slope = slopes[row, base : base + hidden, :].astype(F32)
                parts.append((d_value * slope).astype(BF16))
        parts.append(d_gate_pre[row])
        d_in = dot(weights[...], jnp.concatenate(parts, axis=0), 1, 0) * gain_col[...]
        normed = normed_in[row].astype(F32)
        mean_grad = jnp.mean(d_in, axis=0, keepdims=True)
        mean_cross = jnp.mean(d_in * normed, axis=0, keepdims=True)
        result = inv_in[row : row + 1] * (d_in - mean_grad - normed * mean_cross)
        grad[row] = jnp.transpose(result).astype(BF16)


def swap(values):
    return lax.all_to_all(values, "row", split_axis=0, concat_axis=0, tiled=True)


def swap_half(values, count):
    devices = range(lax.axis_size("row"))
    groups = [[d for d in devices if d // count == half] for half in range(len(devices) // count)]
    return lax.all_to_all(
        values, "row", split_axis=0, concat_axis=0, tiled=True, axis_index_groups=groups
    )


def swap_pieces(pieces):
    devices = range(lax.axis_size("row"))
    return [pieces[0]] + [
        lax.ppermute(pieces[step], "row", [(d, d ^ step) for d in devices])
        for step in range(1, len(pieces))
    ]


def kernel_shards(
    pair,
    cotangent,
    residue_mask,
    ln_in_gain,
    ln_in_bias,
    w_proj,
    w_gate,
    ln_out_gain,
    ln_out_bias,
    w_out,
):
    rows, width, channels = pair.shape
    hidden = w_out.shape[0]
    halves = 2
    devices = lax.axis_size("row")
    count = devices // halves
    block = hidden // count
    left_rows, right_rows = rows * count, rows * devices
    shape = jax.ShapeDtypeStruct
    panel = shape((count, rows * block, width), BF16)
    wide_panel = shape((devices, rows * block, width), BF16)
    mask = residue_mask.reshape(1, width)
    gain, bias = ln_in_gain.reshape(1, channels), ln_in_bias.reshape(1, channels)
    out_gain, out_bias = ln_out_gain.reshape(1, hidden), ln_out_bias.reshape(1, hidden)
    cells = rows * width
    piece = shape((rows * block, width), BF16)
    left_panel = pltpu.VMEM(panel.shape, BF16)
    left_wide = pltpu.VMEM((left_rows * block, width), F32)
    right_wide = pltpu.VMEM((right_rows * block, width), F32)
    (own_right,) = call(
        project_right_kernel,
        "project_right",
        [wide_panel],
        [pair, mask, gain, bias, w_proj],
        fetched=range(5),
        flops=2 * cells * channels * 2 * hidden,
        limit=64 * 1024 * 1024 - 640 * 1024,
    )
    right_panel = swap(own_right)
    pieces = call(
        project_left_kernel,
        "project_left",
        [piece] * count,
        [pair, mask, gain, bias, w_proj, own_right],
        fetched=range(5),
        unread=(5,),
        scratch=[left_panel],
        flops=2 * cells * channels * 2 * hidden,
    )
    pieces = swap_pieces(pieces)
    (left_all,) = call(
        sort_left_kernel,
        "sort_left",
        [shape((block, left_rows, width), BF16)],
        pieces,
        scratch=[left_wide],
    )
    d_hat_centered, gate_slope = call(
        prepare_kernel,
        "prepare",
        [shape((rows, hidden, width), F32), shape((rows, channels, width), F32)],
        [pair, cotangent, gain, bias, w_gate, out_gain, w_out],
        fetched=range(7),
        flops=2 * cells * channels * 2 * hidden,
    )
    products, right_all = call(
        tri_kernel,
        "tri",
        [panel, shape((block, right_rows, width), BF16)],
        [right_panel, left_all, d_hat_centered],
        unread=(2,),
        scratch=[left_wide, right_wide],
        flops=2 * block * left_rows * width * right_rows,
    )
    products = swap_half(products, count)
    (d_products,) = call(
        middle_kernel,
        "middle",
        [panel],
        [products, d_hat_centered],
        flops=20 * cells * hidden,
    )
    d_products = swap_half(d_products, count)
    d_right_panel, d_tri_all = call(
        d_right_kernel,
        "d_right",
        [wide_panel, shape((block, left_rows, width), BF16)],
        [d_products, left_all],
        scratch=[left_wide, right_wide],
        flops=2 * block * left_rows * width * right_rows,
    )
    d_right_panel = swap(d_right_panel)
    d_pieces = call(
        d_left_kernel,
        "d_left",
        [piece] * count,
        [d_tri_all, right_all],
        scratch=[left_wide],
        flops=2 * block * left_rows * width * right_rows,
    )
    d_pieces = swap_pieces(d_pieces)
    (d_left_panel,) = call(sort_d_left_kernel, "sort_d_left", [panel], d_pieces)
    slopes, d_gate_pre, normed_in, inv_in, gain_col, weights = call(
        slopes_kernel,
        "slopes",
        [
            shape((rows, 4 * hidden, width), BF16),
            shape((rows, channels, width), BF16),
            shape((rows, channels, width), BF16),
            shape((rows, width), F32),
            shape((channels, channels), F32),
            shape((channels, 4 * hidden + channels), BF16),
        ],
        [
            products,
            gate_slope,
            pair,
            mask,
            gain,
            bias,
            w_proj,
            w_gate,
            out_gain,
            out_bias,
            w_out,
        ],
        fetched=range(2, 11),
        flops=2 * cells * channels * 6 * hidden,
    )
    (grad,) = call(
        finish_kernel,
        "finish",
        [shape(pair.shape, BF16)],
        [
            d_right_panel,
            d_left_panel,
            slopes,
            d_gate_pre,
            normed_in,
            inv_in,
            gain_col,
            weights,
        ],
        flops=2 * cells * channels * 4 * hidden,
    )
    return grad


def normalize(values, reduce_axis):
    mean_value = jnp.mean(values, axis=reduce_axis, keepdims=True)
    centered = values - mean_value
    variance = jnp.mean(centered * centered, axis=reduce_axis, keepdims=True)
    inv_std = lax.rsqrt(variance + 1e-05)
    return (centered * inv_std, inv_std)


def norm_backward(upstream, normed, inv_std, reduce_axis):
    mean_grad = jnp.mean(upstream, axis=reduce_axis, keepdims=True)
    mean_cross = jnp.mean(upstream * normed, axis=reduce_axis, keepdims=True)
    return inv_std * (upstream - mean_grad - normed * mean_cross)


def shards(
    pair,
    cotangent,
    residue_mask,
    ln_in_gain,
    ln_in_bias,
    w_proj,
    w_gate,
    ln_out_gain,
    ln_out_bias,
    w_out,
):
    local_rows = pair.shape[0]
    local_cols = pair.shape[1]
    hidden = w_out.shape[0]
    chan_index = lax.axis_index("chan")
    row_start = lax.axis_index("row") * local_rows
    col_start = chan_index * local_cols
    mask_float = residue_mask.astype(jnp.float32)
    row_mask = lax.dynamic_slice_in_dim(mask_float, row_start, local_rows)
    col_mask = lax.dynamic_slice_in_dim(mask_float, col_start, local_cols)
    cell_mask = (row_mask[:, None] * col_mask[None, :])[None]
    normed, inv_std = normalize(pair.astype(jnp.float32), -1)
    normed_pair = (normed * ln_in_gain + ln_in_bias).astype(jnp.bfloat16)
    projected = jnp.einsum("rmc,ch->hrm", normed_pair, w_proj, preferred_element_type=jnp.float32)
    left_panel = (
        cell_mask * jax.nn.sigmoid(projected[:hidden]) * projected[hidden : 2 * hidden]
    ).astype(jnp.bfloat16)
    right_panel = (
        cell_mask * jax.nn.sigmoid(projected[2 * hidden : 3 * hidden]) * projected[3 * hidden :]
    ).astype(jnp.bfloat16)
    panels = lax.all_to_all(
        jnp.stack([left_panel, right_panel]), "row", split_axis=1, concat_axis=2, tiled=True
    )
    left_all = panels[0]
    right_all = panels[1]
    right_rows = lax.all_to_all(right_all, "chan", split_axis=1, concat_axis=2, tiled=True)
    partner = right_rows
    tri_part = jnp.einsum(
        "gik,gjk->gij",
        lax.all_gather(left_all, "chan", axis=2, tiled=True),
        partner,
        preferred_element_type=jnp.float32,
    ).astype(jnp.bfloat16)
    tri_cells = lax.all_to_all(tri_part, "row", split_axis=1, concat_axis=0, tiled=True)
    tri_hat, inv_tri = normalize(tri_cells.astype(jnp.float32), 0)
    scaled = (tri_hat * ln_out_gain[:, None, None] + ln_out_bias[:, None, None]).astype(
        jnp.bfloat16
    )
    proj_out = jnp.einsum("hrm,hc->rmc", scaled, w_out, preferred_element_type=jnp.float32)
    gate_value = jax.nn.sigmoid(
        jnp.einsum("rmc,cd->rmd", normed_pair, w_gate, preferred_element_type=jnp.float32)
    )
    cot_float = cotangent.astype(jnp.float32)
    d_gate_pre = (cot_float * proj_out * gate_value * (1.0 - gate_value)).astype(jnp.bfloat16)
    d_scaled = (cot_float * gate_value).astype(jnp.bfloat16)
    d_hat = jnp.einsum("rmc,hc->hrm", d_scaled, w_out, preferred_element_type=jnp.float32)
    d_hat = d_hat * ln_out_gain[:, None, None]
    d_tri = norm_backward(d_hat, tri_hat, inv_tri, 0).astype(jnp.bfloat16)
    d_tri_all = lax.all_to_all(d_tri, "row", split_axis=0, concat_axis=1, tiled=True)
    panel_piece = lax.all_gather(d_tri_all, "chan", axis=2, tiled=True)
    partner = right_all
    d_left = jnp.einsum("gij,gjk->gik", panel_piece, partner, preferred_element_type=jnp.float32)
    contribution = jnp.einsum(
        "gij,gik->gjk", panel_piece, left_all, preferred_element_type=jnp.float32
    )
    d_right = contribution
    d_left, d_right = (d_left, d_right)
    d_stack = jnp.stack([d_left, d_right]).astype(jnp.bfloat16)
    d_panels = lax.all_to_all(d_stack, "row", split_axis=2, concat_axis=1, tiled=True)

    def gating(d_value, gate_proj, value_proj):
        sigmoid_val = jax.nn.sigmoid(gate_proj)
        masked_grad = d_value.astype(jnp.float32) * cell_mask
        return (
            masked_grad * value_proj * sigmoid_val * (1.0 - sigmoid_val),
            masked_grad * sigmoid_val,
        )

    gate_left, value_left = gating(d_panels[0], projected[:hidden], projected[hidden : 2 * hidden])
    gate_right, value_right = gating(
        d_panels[1], projected[2 * hidden : 3 * hidden], projected[3 * hidden :]
    )
    d_proj = jnp.concatenate([gate_left, value_left, gate_right, value_right], axis=0).astype(
        jnp.bfloat16
    )
    d_normed = jnp.einsum("hrm,ch->rmc", d_proj, w_proj, preferred_element_type=jnp.float32)
    d_normed = d_normed + jnp.einsum(
        "rmd,cd->rmc", d_gate_pre, w_gate, preferred_element_type=jnp.float32
    )
    d_input = d_normed * ln_in_gain
    return norm_backward(d_input, normed, inv_std, -1).astype(jnp.bfloat16)


def solution(mesh):
    fits = mesh.shape["chan"] == 1 and mesh.shape["row"] in (8, 16)
    return jax.shard_map(
        kernel_shards if fits else shards,
        mesh=mesh,
        in_specs=(
            P(("grp", "row"), "chan", None),
            P(("grp", "row"), "chan", None),
            P("grp"),
            P(),
            P(),
            P(),
            P(),
            P(),
            P(),
            P(),
        ),
        out_specs=P(("grp", "row"), "chan", None),
        check_vma=False,
    )
```

```python
import functools

import jax
import jax.numpy as jnp
from jax import lax
from jax.experimental import pallas as pl
from jax.experimental.pallas import tpu as pltpu
from jax.sharding import PartitionSpec as P

F32 = jnp.float32
BF16 = jnp.bfloat16
VMEM_LIMIT = 16 * 1024 * 1024


def dot(lhs, rhs, lhs_dim, rhs_dim):
    return lax.dot_general(
        lhs, rhs, (((lhs_dim,), (rhs_dim,)), ((), ())), preferred_element_type=F32
    )


def transposed(matrix):
    return jnp.transpose(matrix.astype(F32)).astype(BF16)


def sigmoid(values):
    return 1.0 / (1.0 + jnp.exp(-values))


def column(row):
    size = row.shape[1]
    return jnp.transpose(jnp.broadcast_to(row, (size, size)))


def norm_rows(values):
    centered = values - jnp.mean(values, axis=0, keepdims=True)
    variance = jnp.mean(centered * centered, axis=0, keepdims=True)
    inv_std = lax.rsqrt(variance + 1e-05)
    return centered * inv_std, inv_std


def call(
    kernel, name, outs, args, fetched=(), unread=(), scratch=(), flops=0, limit=VMEM_LIMIT
):
    moved = sum(a.size * a.dtype.itemsize for a in args) + sum(
        o.size * jnp.dtype(o.dtype).itemsize for o in outs
    )
    n_args, n_outs, n_fetched = len(args), len(outs), len(fetched)

    def body(*refs):
        ins = list(refs[:n_args])
        rest = refs[n_args + n_outs :]
        copies = []
        for n, place in enumerate(fetched):
            copies.append(pltpu.make_async_copy(ins[place], rest[n], rest[n_fetched].at[n]))
            ins[place] = rest[n]
        for copy in copies:
            copy.start()
        for copy in copies:
            copy.wait()
        kernel(*ins, *refs[n_args : n_args + n_outs], *rest[n_fetched + (n_fetched > 0) :])

    buffers = [pltpu.VMEM(args[place].shape, args[place].dtype) for place in fetched]
    if fetched:
        buffers.append(pltpu.SemaphoreType.DMA((n_fetched,)))
    return pl.pallas_call(
        body,
        name=name,
        out_shape=outs,
        in_specs=[
            pl.BlockSpec(
                memory_space=pltpu.HBM if n in fetched else pl.ANY if n in unread else pltpu.VMEM
            )
            for n in range(n_args)
        ],
        out_specs=[pl.BlockSpec(memory_space=pltpu.VMEM) for _ in outs],
        scratch_shapes=buffers + list(scratch),
        compiler_params=pltpu.CompilerParams(vmem_limit_bytes=limit),
        cost_estimate=pl.CostEstimate(flops=flops, bytes_accessed=moved, transcendentals=0),
    )(*args)


def cell_masks(mask, rows):
    columns = mask[...].astype(F32)
    shape = (rows, columns.shape[1])
    first = lax.axis_index("row") * rows
    own = lax.broadcasted_iota(jnp.int32, shape, 1) == (
        lax.broadcasted_iota(jnp.int32, shape, 0) + first
    )
    row_mask = jnp.sum(jnp.where(own, columns, 0.0), axis=1, keepdims=True)
    cells = row_mask * columns
    return [cells[row : row + 1] for row in range(rows)]


def wide_order(devices, count):
    return [half * count + place for place in range(count) for half in range(devices // count)]


def partner(step, count):
    return lax.rem(lax.axis_index("row"), count) ^ step


def gated_rows(pair, mask, gain, bias, w_proj, side):
    rows = pair.shape[0]
    hidden = w_proj.shape[1] // 4
    w_flip = transposed(w_proj[:, 2 * side * hidden : 2 * (side + 1) * hidden])
    gain_col, bias_col = column(gain[...]), column(bias[...])
    masks = cell_masks(mask, rows)
    for row in range(rows):
        normed, _ = norm_rows(jnp.transpose(pair[row].astype(F32)))
        zln = (normed * gain_col + bias_col).astype(BF16)
        proj = dot(w_flip, zln, 1, 0)
        yield row, masks[row] * sigmoid(proj[:hidden]) * proj[hidden:]


def project_right_kernel(pair, mask, gain, bias, w_proj, right_panel):
    rows = pair.shape[0]
    devices, depth, width = right_panel.shape
    block = depth // rows
    count = w_proj.shape[1] // 4 // block
    for row, right in gated_rows(pair, mask, gain, bias, w_proj, 1):
        right = right.reshape(count, block, width).astype(BF16)
        for rank in range(devices):
            place = wide_order(devices, count)[rank] % count
            right_panel[rank, row * block : (row + 1) * block, :] = right[place]


def project_left_kernel(pair, mask, gain, bias, w_proj, after, *refs):
    del after
    *pieces, left_panel = refs
    rows = pair.shape[0]
    count, depth, width = left_panel.shape
    block = depth // rows
    for row, left in gated_rows(pair, mask, gain, bias, w_proj, 0):
        left = left.reshape(count, block, width).astype(BF16)
        left_panel[:, row * block : (row + 1) * block, :] = left
    for step, piece in enumerate(pieces):
        piece[...] = left_panel[partner(step, count)]


def prepare_kernel(
    pair, cotangent, gain, bias, w_gate, out_gain, w_out, d_hat_centered, gate_slope
):
    gate_flip = transposed(w_gate[...])
    gain_col, bias_col = column(gain[...]), column(bias[...])
    out_gain_col = column(out_gain[...])
    for row in range(pair.shape[0]):
        normed, _ = norm_rows(jnp.transpose(pair[row].astype(F32)))
        zln = (normed * gain_col + bias_col).astype(BF16)
        gate = sigmoid(dot(gate_flip, zln, 1, 0))
        cot = jnp.transpose(cotangent[row].astype(F32))
        d_scaled = (cot * gate).astype(BF16)
        d_hat = dot(w_out[...], d_scaled, 1, 0) * out_gain_col
        d_hat_centered[row] = d_hat - jnp.mean(d_hat, axis=0, keepdims=True)
        gate_slope[row] = cot * gate * (1.0 - gate)


def spread(panel, wide):
    wide[...] = panel[...].astype(F32).reshape(wide.shape)


def wide_places(panel, count):
    devices, depth, _ = panel.shape
    for rank, device in enumerate(wide_order(devices, count)):
        yield rank, slice(device * depth, (device + 1) * depth)


def sort_left_kernel(*refs):
    *pieces, left_all, left_wide = refs
    block, left_rows, _ = left_all.shape
    depth = pieces[0].shape[0]
    for step, piece in enumerate(pieces):
        start = pl.multiple_of(partner(step, len(pieces)) * depth, depth)
        left_wide[pl.ds(start, depth), :] = piece[...].astype(F32)
    for h in range(block):
        left_all[h] = left_wide[pl.ds(h, left_rows, stride=block), :].astype(BF16)


def tri_kernel(right_panel, left_all, after, products, right_all, left_wide, right_wide):
    del after
    block, left_rows, _ = left_all.shape
    right_rows = right_all.shape[1]
    for rank, place in wide_places(right_panel, products.shape[0]):
        right_wide[place, :] = right_panel[rank].astype(F32)
    for h in range(block):
        right = right_wide[pl.ds(h, right_rows, stride=block), :].astype(BF16)
        right_all[h] = right
        left_wide[pl.ds(h, left_rows, stride=block), :] = dot(left_all[h], right, 1, 1)
    products[...] = left_wide[...].astype(BF16).reshape(products.shape)


def cell_row(ref, row, rows):
    count, depth, width = ref.shape
    block = depth // rows
    return ref[:, row * block : (row + 1) * block, :].astype(F32).reshape(count * block, width)


def middle_kernel(products, d_hat_centered, d_products):
    rows = d_hat_centered.shape[0]
    count, depth, width = products.shape
    block = depth // rows
    for row in range(rows):
        tri_hat, inv_std = norm_rows(cell_row(products, row, rows))
        d_hat = d_hat_centered[row]
        cross = jnp.mean(d_hat * tri_hat, axis=0, keepdims=True)
        d_tri = inv_std * (d_hat - tri_hat * cross)
        d_products[:, row * block : (row + 1) * block, :] = d_tri.reshape(
            count, block, width
        ).astype(BF16)


def d_right_kernel(d_products, left_all, d_right_panel, d_tri_all, left_wide, right_wide):
    block, left_rows, _ = left_all.shape
    right_rows = right_wide.shape[0] // block
    spread(d_products, left_wide)
    for h in range(block):
        d_tri = left_wide[pl.ds(h, left_rows, stride=block), :].astype(BF16)
        d_tri_all[h] = d_tri
        right_wide[pl.ds(h, right_rows, stride=block), :] = dot(d_tri, left_all[h], 0, 0)
    for rank, place in wide_places(d_right_panel, d_products.shape[0]):
        d_right_panel[rank] = right_wide[place, :].astype(BF16)


def d_left_kernel(d_tri_all, right_all, *refs):
    *pieces, left_wide = refs
    block, left_rows, _ = d_tri_all.shape
    for h in range(block):
        left_wide[pl.ds(h, left_rows, stride=block), :] = dot(d_tri_all[h], right_all[h], 1, 0)
    depth = pieces[0].shape[0]
    for step, piece in enumerate(pieces):
        start = pl.multiple_of(partner(step, len(pieces)) * depth, depth)
        piece[...] = left_wide[pl.ds(start, depth), :].astype(BF16)


def slopes_kernel(
    products,
    gate_slope,
    pair,
    mask,
    gain,
    bias,
    w_proj,
    w_gate,
    out_gain,
    out_bias,
    w_out,
    slopes,
    d_gate_pre,
    normed_in,
    inv_in,
    in_gain,
    weights,
):
    rows = pair.shape[0]
    hidden = w_out.shape[0]
    w_flip = transposed(w_proj[...])
    out_flip = transposed(w_out[...])
    gain_col, bias_col = column(gain[...]), column(bias[...])
    in_gain[...] = gain_col
    weights[...] = jnp.concatenate([w_proj[...], w_gate[...]], axis=1)
    out_gain_col, out_bias_col = column(out_gain[...]), column(out_bias[...])
    masks = cell_masks(mask, rows)
    for row in range(rows):
        tri_hat, _ = norm_rows(cell_row(products, row, rows))
        scaled = (tri_hat * out_gain_col + out_bias_col).astype(BF16)
        d_gate_pre[row] = (dot(out_flip, scaled, 1, 0) * gate_slope[row]).astype(BF16)
        normed, inv_std = norm_rows(jnp.transpose(pair[row].astype(F32)))
        normed_in[row] = normed.astype(normed_in.dtype)
        inv_in[row : row + 1] = inv_std
        zln = (normed * gain_col + bias_col).astype(BF16)
        proj = dot(w_flip, zln, 1, 0)
        for side in range(2):
            base = 2 * side * hidden
            sig = sigmoid(proj[base : base + hidden])
            masked = masks[row] * sig
            value = masked * (1.0 - sig) * proj[base + hidden : base + 2 * hidden]
            slopes[row, base : base + hidden, :] = value.astype(slopes.dtype)
            slopes[row, base + hidden : base + 2 * hidden, :] = masked.astype(slopes.dtype)


def sort_d_left_kernel(*refs):
    *pieces, d_left_panel = refs
    for step, piece in enumerate(pieces):
        d_left_panel[partner(step, len(pieces))] = piece[...]


def finish_kernel(
    d_right_panel, d_left_panel, slopes, d_gate_pre, normed_in, inv_in, gain_col, weights, grad
):
    rows = grad.shape[0]
    count, depth, width = d_left_panel.shape
    hidden = count * depth // rows
    for row in range(rows):
        d_right = cell_row(d_right_panel, row, rows)
        d_right = jnp.sum(d_right.reshape(count, -1, depth // rows, width), axis=1)
        parts = []
        for side, d_value in enumerate((cell_row(d_left_panel, row, rows), d_right.reshape(hidden, width))):
            for base in (2 * side * hidden, (2 * side + 1) * hidden):
                slope = slopes[row, base : base + hidden, :].astype(F32)
                parts.append((d_value * slope).astype(BF16))
        parts.append(d_gate_pre[row])
        d_in = dot(weights[...], jnp.concatenate(parts, axis=0), 1, 0) * gain_col[...]
        normed = normed_in[row].astype(F32)
        mean_grad = jnp.mean(d_in, axis=0, keepdims=True)
        mean_cross = jnp.mean(d_in * normed, axis=0, keepdims=True)
        result = inv_in[row : row + 1] * (d_in - mean_grad - normed * mean_cross)
        grad[row] = jnp.transpose(result).astype(BF16)


def swap(values, count):
    groups = [wide_order(lax.axis_size("row"), count)]
    return lax.all_to_all(
        values, "row", split_axis=0, concat_axis=0, tiled=True, axis_index_groups=groups
    )


def swap_half(values, count):
    devices = range(lax.axis_size("row"))
    groups = [[d for d in devices if d // count == half] for half in range(len(devices) // count)]
    return lax.all_to_all(
        values, "row", split_axis=0, concat_axis=0, tiled=True, axis_index_groups=groups
    )


def swap_pieces(pieces):
    devices = range(lax.axis_size("row"))
    return [pieces[0]] + [
        lax.ppermute(pieces[step], "row", [(d, d ^ step) for d in devices])
        for step in range(1, len(pieces))
    ]


def kernel_shards(
    pair,
    cotangent,
    residue_mask,
    ln_in_gain,
    ln_in_bias,
    w_proj,
    w_gate,
    ln_out_gain,
    ln_out_bias,
    w_out,
):
    rows, width, channels = pair.shape
    hidden = w_out.shape[0]
    halves = 2
    devices = lax.axis_size("row")
    count = devices // halves
    block = hidden // count
    left_rows, right_rows = rows * count, rows * devices
    shape = jax.ShapeDtypeStruct
    panel = shape((count, rows * block, width), BF16)
    wide_panel = shape((devices, rows * block, width), BF16)
    mask = residue_mask.reshape(1, width)
    gain, bias = ln_in_gain.reshape(1, channels), ln_in_bias.reshape(1, channels)
    out_gain, out_bias = ln_out_gain.reshape(1, hidden), ln_out_bias.reshape(1, hidden)
    cells = rows * width
    piece = shape((rows * block, width), BF16)
    left_panel = pltpu.VMEM(panel.shape, BF16)
    left_wide = pltpu.VMEM((left_rows * block, width), F32)
    right_wide = pltpu.VMEM((right_rows * block, width), F32)
    (own_right,) = call(
        project_right_kernel,
        "project_right",
        [wide_panel],
        [pair, mask, gain, bias, w_proj],
        fetched=range(5),
        flops=2 * cells * channels * 2 * hidden,
        limit=64 * 1024 * 1024 - 640 * 1024,
    )
    right_panel = swap(own_right, count)
    pieces = call(
        project_left_kernel,
        "project_left",
        [piece] * count,
        [pair, mask, gain, bias, w_proj, own_right],
        fetched=range(5),
        unread=(5,),
        scratch=[left_panel],
        flops=2 * cells * channels * 2 * hidden,
    )
    pieces = swap_pieces(pieces)
    (left_all,) = call(
        sort_left_kernel,
        "sort_left",
        [shape((block, left_rows, width), BF16)],
        pieces,
        scratch=[left_wide],
    )
    d_hat_centered, gate_slope = call(
        prepare_kernel,
        "prepare",
        [shape((rows, hidden, width), F32), shape((rows, channels, width), F32)],
        [pair, cotangent, gain, bias, w_gate, out_gain, w_out],
        fetched=range(7),
        flops=2 * cells * channels * 2 * hidden,
    )
    products, right_all = call(
        tri_kernel,
        "tri",
        [panel, shape((block, right_rows, width), BF16)],
        [right_panel, left_all, d_hat_centered],
        unread=(2,),
        scratch=[left_wide, right_wide],
        flops=2 * block * left_rows * width * right_rows,
    )
    products = swap_half(products, count)
    (d_products,) = call(
        middle_kernel,
        "middle",
        [panel],
        [products, d_hat_centered],
        flops=20 * cells * hidden,
    )
    d_products = swap_half(d_products, count)
    d_right_panel, d_tri_all = call(
        d_right_kernel,
        "d_right",
        [wide_panel, shape((block, left_rows, width), BF16)],
        [d_products, left_all],
        scratch=[left_wide, right_wide],
        flops=2 * block * left_rows * width * right_rows,
    )
    d_right_panel = swap(d_right_panel, count)
    d_pieces = call(
        d_left_kernel,
        "d_left",
        [piece] * count,
        [d_tri_all, right_all],
        scratch=[left_wide],
        flops=2 * block * left_rows * width * right_rows,
    )
    d_pieces = swap_pieces(d_pieces)
    (d_left_panel,) = call(sort_d_left_kernel, "sort_d_left", [panel], d_pieces)
    slopes, d_gate_pre, normed_in, inv_in, gain_col, weights = call(
        slopes_kernel,
        "slopes",
        [
            shape((rows, 4 * hidden, width), BF16),
            shape((rows, channels, width), BF16),
            shape((rows, channels, width), BF16),
            shape((rows, width), F32),
            shape((channels, channels), F32),
            shape((channels, 4 * hidden + channels), BF16),
        ],
        [
            products,
            gate_slope,
            pair,
            mask,
            gain,
            bias,
            w_proj,
            w_gate,
            out_gain,
            out_bias,
            w_out,
        ],
        fetched=range(2, 11),
        flops=2 * cells * channels * 6 * hidden,
    )
    (grad,) = call(
        finish_kernel,
        "finish",
        [shape(pair.shape, BF16)],
        [
            d_right_panel,
            d_left_panel,
            slopes,
            d_gate_pre,
            normed_in,
            inv_in,
            gain_col,
            weights,
        ],
        flops=2 * cells * channels * 4 * hidden,
    )
    return grad


def normalize(values, reduce_axis):
    mean_value = jnp.mean(values, axis=reduce_axis, keepdims=True)
    centered = values - mean_value
    variance = jnp.mean(centered * centered, axis=reduce_axis, keepdims=True)
    inv_std = lax.rsqrt(variance + 1e-05)
    return (centered * inv_std, inv_std)


def norm_backward(upstream, normed, inv_std, reduce_axis):
    mean_grad = jnp.mean(upstream, axis=reduce_axis, keepdims=True)
    mean_cross = jnp.mean(upstream * normed, axis=reduce_axis, keepdims=True)
    return inv_std * (upstream - mean_grad - normed * mean_cross)


def shards(
    pair,
    cotangent,
    residue_mask,
    ln_in_gain,
    ln_in_bias,
    w_proj,
    w_gate,
    ln_out_gain,
    ln_out_bias,
    w_out,
):
    local_rows = pair.shape[0]
    local_cols = pair.shape[1]
    hidden = w_out.shape[0]
    chan_index = lax.axis_index("chan")
    row_start = lax.axis_index("row") * local_rows
    col_start = chan_index * local_cols
    mask_float = residue_mask.astype(jnp.float32)
    row_mask = lax.dynamic_slice_in_dim(mask_float, row_start, local_rows)
    col_mask = lax.dynamic_slice_in_dim(mask_float, col_start, local_cols)
    cell_mask = (row_mask[:, None] * col_mask[None, :])[None]
    normed, inv_std = normalize(pair.astype(jnp.float32), -1)
    normed_pair = (normed * ln_in_gain + ln_in_bias).astype(jnp.bfloat16)
    projected = jnp.einsum("rmc,ch->hrm", normed_pair, w_proj, preferred_element_type=jnp.float32)
    left_panel = (
        cell_mask * jax.nn.sigmoid(projected[:hidden]) * projected[hidden : 2 * hidden]
    ).astype(jnp.bfloat16)
    right_panel = (
        cell_mask * jax.nn.sigmoid(projected[2 * hidden : 3 * hidden]) * projected[3 * hidden :]
    ).astype(jnp.bfloat16)
    panels = lax.all_to_all(
        jnp.stack([left_panel, right_panel]), "row", split_axis=1, concat_axis=2, tiled=True
    )
    left_all = panels[0]
    right_all = panels[1]
    right_rows = lax.all_to_all(right_all, "chan", split_axis=1, concat_axis=2, tiled=True)
    partner = right_rows
    tri_part = jnp.einsum(
        "gik,gjk->gij",
        lax.all_gather(left_all, "chan", axis=2, tiled=True),
        partner,
        preferred_element_type=jnp.float32,
    ).astype(jnp.bfloat16)
    tri_cells = lax.all_to_all(tri_part, "row", split_axis=1, concat_axis=0, tiled=True)
    tri_hat, inv_tri = normalize(tri_cells.astype(jnp.float32), 0)
    scaled = (tri_hat * ln_out_gain[:, None, None] + ln_out_bias[:, None, None]).astype(
        jnp.bfloat16
    )
    proj_out = jnp.einsum("hrm,hc->rmc", scaled, w_out, preferred_element_type=jnp.float32)
    gate_value = jax.nn.sigmoid(
        jnp.einsum("rmc,cd->rmd", normed_pair, w_gate, preferred_element_type=jnp.float32)
    )
    cot_float = cotangent.astype(jnp.float32)
    d_gate_pre = (cot_float * proj_out * gate_value * (1.0 - gate_value)).astype(jnp.bfloat16)
    d_scaled = (cot_float * gate_value).astype(jnp.bfloat16)
    d_hat = jnp.einsum("rmc,hc->hrm", d_scaled, w_out, preferred_element_type=jnp.float32)
    d_hat = d_hat * ln_out_gain[:, None, None]
    d_tri = norm_backward(d_hat, tri_hat, inv_tri, 0).astype(jnp.bfloat16)
    d_tri_all = lax.all_to_all(d_tri, "row", split_axis=0, concat_axis=1, tiled=True)
    panel_piece = lax.all_gather(d_tri_all, "chan", axis=2, tiled=True)
    partner = right_all
    d_left = jnp.einsum("gij,gjk->gik", panel_piece, partner, preferred_element_type=jnp.float32)
    contribution = jnp.einsum(
        "gij,gik->gjk", panel_piece, left_all, preferred_element_type=jnp.float32
    )
    d_right = contribution
    d_left, d_right = (d_left, d_right)
    d_stack = jnp.stack([d_left, d_right]).astype(jnp.bfloat16)
    d_panels = lax.all_to_all(d_stack, "row", split_axis=2, concat_axis=1, tiled=True)

    def gating(d_value, gate_proj, value_proj):
        sigmoid_val = jax.nn.sigmoid(gate_proj)
        masked_grad = d_value.astype(jnp.float32) * cell_mask
        return (
            masked_grad * value_proj * sigmoid_val * (1.0 - sigmoid_val),
            masked_grad * sigmoid_val,
        )

    gate_left, value_left = gating(d_panels[0], projected[:hidden], projected[hidden : 2 * hidden])
    gate_right, value_right = gating(
        d_panels[1], projected[2 * hidden : 3 * hidden], projected[3 * hidden :]
    )
    d_proj = jnp.concatenate([gate_left, value_left, gate_right, value_right], axis=0).astype(
        jnp.bfloat16
    )
    d_normed = jnp.einsum("hrm,ch->rmc", d_proj, w_proj, preferred_element_type=jnp.float32)
    d_normed = d_normed + jnp.einsum(
        "rmd,cd->rmc", d_gate_pre, w_gate, preferred_element_type=jnp.float32
    )
    d_input = d_normed * ln_in_gain
    return norm_backward(d_input, normed, inv_std, -1).astype(jnp.bfloat16)


def solution(mesh):
    fits = mesh.shape["chan"] == 1 and mesh.shape["row"] in (8, 16)
    return jax.shard_map(
        kernel_shards if fits else shards,
        mesh=mesh,
        in_specs=(
            P(("grp", "row"), "chan", None),
            P(("grp", "row"), "chan", None),
            P("grp"),
            P(),
            P(),
            P(),
            P(),
            P(),
            P(),
            P(),
        ),
        out_specs=P(("grp", "row"), "chan", None),
        check_vma=False,
    )
```

```python
import functools

import jax
import jax.numpy as jnp
from jax import lax
from jax.experimental import pallas as pl
from jax.experimental.pallas import tpu as pltpu
from jax.sharding import PartitionSpec as P

F32 = jnp.float32
BF16 = jnp.bfloat16
VMEM_LIMIT = 16 * 1024 * 1024


def dot(lhs, rhs, lhs_dim, rhs_dim):
    return lax.dot_general(
        lhs, rhs, (((lhs_dim,), (rhs_dim,)), ((), ())), preferred_element_type=F32
    )


def transposed(matrix):
    return jnp.transpose(matrix.astype(F32)).astype(BF16)


def sigmoid(values):
    return 1.0 / (1.0 + jnp.exp(-values))


def column(row):
    size = row.shape[1]
    return jnp.transpose(jnp.broadcast_to(row, (size, size)))


def norm_rows(values):
    centered = values - jnp.mean(values, axis=0, keepdims=True)
    variance = jnp.mean(centered * centered, axis=0, keepdims=True)
    inv_std = lax.rsqrt(variance + 1e-05)
    return centered * inv_std, inv_std


def call(
    kernel, name, outs, args, fetched=(), unread=(), scratch=(), flops=0, limit=VMEM_LIMIT
):
    moved = sum(a.size * a.dtype.itemsize for a in args) + sum(
        o.size * jnp.dtype(o.dtype).itemsize for o in outs
    )
    n_args, n_outs, n_fetched = len(args), len(outs), len(fetched)

    def body(*refs):
        ins = list(refs[:n_args])
        rest = refs[n_args + n_outs :]
        copies = []
        for n, place in enumerate(fetched):
            copies.append(pltpu.make_async_copy(ins[place], rest[n], rest[n_fetched].at[n]))
            ins[place] = rest[n]
        for copy in copies:
            copy.start()
        for copy in copies:
            copy.wait()
        kernel(*ins, *refs[n_args : n_args + n_outs], *rest[n_fetched + (n_fetched > 0) :])

    buffers = [pltpu.VMEM(args[place].shape, args[place].dtype) for place in fetched]
    if fetched:
        buffers.append(pltpu.SemaphoreType.DMA((n_fetched,)))
    return pl.pallas_call(
        body,
        name=name,
        out_shape=outs,
        in_specs=[
            pl.BlockSpec(
                memory_space=pltpu.HBM if n in fetched else pl.ANY if n in unread else pltpu.VMEM
            )
            for n in range(n_args)
        ],
        out_specs=[pl.BlockSpec(memory_space=pltpu.VMEM) for _ in outs],
        scratch_shapes=buffers + list(scratch),
        compiler_params=pltpu.CompilerParams(vmem_limit_bytes=limit),
        cost_estimate=pl.CostEstimate(flops=flops, bytes_accessed=moved, transcendentals=0),
    )(*args)


def cell_masks(mask, rows):
    columns = mask[...].astype(F32)
    shape = (rows, columns.shape[1])
    first = lax.axis_index("row") * rows
    own = lax.broadcasted_iota(jnp.int32, shape, 1) == (
        lax.broadcasted_iota(jnp.int32, shape, 0) + first
    )
    row_mask = jnp.sum(jnp.where(own, columns, 0.0), axis=1, keepdims=True)
    cells = row_mask * columns
    return [cells[row : row + 1] for row in range(rows)]


def wide_order(devices, count):
    inner = [(place + count // 2) % count for place in range(count)]
    return [device for place in range(count) for device in (inner[place], count + place)]


def partner(step, count):
    return lax.rem(lax.axis_index("row"), count) ^ step


def gated_rows(pair, mask, gain, bias, w_proj, side):
    rows = pair.shape[0]
    hidden = w_proj.shape[1] // 4
    w_flip = transposed(w_proj[:, 2 * side * hidden : 2 * (side + 1) * hidden])
    gain_col, bias_col = column(gain[...]), column(bias[...])
    masks = cell_masks(mask, rows)
    for row in range(rows):
        normed, _ = norm_rows(jnp.transpose(pair[row].astype(F32)))
        zln = (normed * gain_col + bias_col).astype(BF16)
        proj = dot(w_flip, zln, 1, 0)
        yield row, masks[row] * sigmoid(proj[:hidden]) * proj[hidden:]


def project_right_kernel(pair, mask, gain, bias, w_proj, right_panel):
    rows = pair.shape[0]
    devices, depth, width = right_panel.shape
    block = depth // rows
    count = w_proj.shape[1] // 4 // block
    for row, right in gated_rows(pair, mask, gain, bias, w_proj, 1):
        right = right.reshape(count, block, width).astype(BF16)
        for rank in range(devices):
            place = wide_order(devices, count)[rank] % count
            right_panel[rank, row * block : (row + 1) * block, :] = right[place]


def project_left_kernel(pair, mask, gain, bias, w_proj, after, *refs):
    del after
    *pieces, left_panel = refs
    rows = pair.shape[0]
    count, depth, width = left_panel.shape
    block = depth // rows
    for row, left in gated_rows(pair, mask, gain, bias, w_proj, 0):
        left = left.reshape(count, block, width).astype(BF16)
        left_panel[:, row * block : (row + 1) * block, :] = left
    for step, piece in enumerate(pieces):
        piece[...] = left_panel[partner(step, count)]


def prepare_kernel(
    pair, cotangent, gain, bias, w_gate, out_gain, w_out, d_hat_centered, gate_slope
):
    gate_flip = transposed(w_gate[...])
    gain_col, bias_col = column(gain[...]), column(bias[...])
    out_gain_col = column(out_gain[...])
    for row in range(pair.shape[0]):
        normed, _ = norm_rows(jnp.transpose(pair[row].astype(F32)))
        zln = (normed * gain_col + bias_col).astype(BF16)
        gate = sigmoid(dot(gate_flip, zln, 1, 0))
        cot = jnp.transpose(cotangent[row].astype(F32))
        d_scaled = (cot * gate).astype(BF16)
        d_hat = dot(w_out[...], d_scaled, 1, 0) * out_gain_col
        d_hat_centered[row] = d_hat - jnp.mean(d_hat, axis=0, keepdims=True)
        gate_slope[row] = cot * gate * (1.0 - gate)


def spread(panel, wide):
    wide[...] = panel[...].astype(F32).reshape(wide.shape)


def wide_places(panel, count):
    devices, depth, _ = panel.shape
    for rank, device in enumerate(wide_order(devices, count)):
        yield rank, slice(device * depth, (device + 1) * depth)


def sort_left_kernel(*refs):
    *pieces, left_all, left_wide = refs
    block, left_rows, _ = left_all.shape
    depth = pieces[0].shape[0]
    for step, piece in enumerate(pieces):
        start = pl.multiple_of(partner(step, len(pieces)) * depth, depth)
        left_wide[pl.ds(start, depth), :] = piece[...].astype(F32)
    for h in range(block):
        left_all[h] = left_wide[pl.ds(h, left_rows, stride=block), :].astype(BF16)


def tri_kernel(right_panel, left_all, after, products, right_all, left_wide, right_wide):
    del after
    block, left_rows, _ = left_all.shape
    right_rows = right_all.shape[1]
    for rank, place in wide_places(right_panel, products.shape[0]):
        right_wide[place, :] = right_panel[rank].astype(F32)
    for h in range(block):
        right = right_wide[pl.ds(h, right_rows, stride=block), :].astype(BF16)
        right_all[h] = right
        left_wide[pl.ds(h, left_rows, stride=block), :] = dot(left_all[h], right, 1, 1)
    products[...] = left_wide[...].astype(BF16).reshape(products.shape)


def cell_row(ref, row, rows):
    count, depth, width = ref.shape
    block = depth // rows
    return ref[:, row * block : (row + 1) * block, :].astype(F32).reshape(count * block, width)


def middle_kernel(products, d_hat_centered, d_products):
    rows = d_hat_centered.shape[0]
    count, depth, width = products.shape
    block = depth // rows
    for row in range(rows):
        tri_hat, inv_std = norm_rows(cell_row(products, row, rows))
        d_hat = d_hat_centered[row]
        cross = jnp.mean(d_hat * tri_hat, axis=0, keepdims=True)
        d_tri = inv_std * (d_hat - tri_hat * cross)
        d_products[:, row * block : (row + 1) * block, :] = d_tri.reshape(
            count, block, width
        ).astype(BF16)


def d_right_kernel(d_products, left_all, d_right_panel, d_tri_all, left_wide, right_wide):
    block, left_rows, _ = left_all.shape
    right_rows = right_wide.shape[0] // block
    spread(d_products, left_wide)
    for h in range(block):
        d_tri = left_wide[pl.ds(h, left_rows, stride=block), :].astype(BF16)
        d_tri_all[h] = d_tri
        right_wide[pl.ds(h, right_rows, stride=block), :] = dot(d_tri, left_all[h], 0, 0)
    for rank, place in wide_places(d_right_panel, d_products.shape[0]):
        d_right_panel[rank] = right_wide[place, :].astype(BF16)


def d_left_kernel(d_tri_all, right_all, *refs):
    *pieces, left_wide = refs
    block, left_rows, _ = d_tri_all.shape
    for h in range(block):
        left_wide[pl.ds(h, left_rows, stride=block), :] = dot(d_tri_all[h], right_all[h], 1, 0)
    depth = pieces[0].shape[0]
    for step, piece in enumerate(pieces):
        start = pl.multiple_of(partner(step, len(pieces)) * depth, depth)
        piece[...] = left_wide[pl.ds(start, depth), :].astype(BF16)


def slopes_kernel(
    products,
    gate_slope,
    pair,
    mask,
    gain,
    bias,
    w_proj,
    w_gate,
    out_gain,
    out_bias,
    w_out,
    slopes,
    d_gate_pre,
    normed_in,
    inv_in,
    in_gain,
    weights,
):
    rows = pair.shape[0]
    hidden = w_out.shape[0]
    w_flip = transposed(w_proj[...])
    out_flip = transposed(w_out[...])
    gain_col, bias_col = column(gain[...]), column(bias[...])
    in_gain[...] = gain_col
    weights[...] = jnp.concatenate([w_proj[...], w_gate[...]], axis=1)
    out_gain_col, out_bias_col = column(out_gain[...]), column(out_bias[...])
    masks = cell_masks(mask, rows)
    for row in range(rows):
        tri_hat, _ = norm_rows(cell_row(products, row, rows))
        scaled = (tri_hat * out_gain_col + out_bias_col).astype(BF16)
        d_gate_pre[row] = (dot(out_flip, scaled, 1, 0) * gate_slope[row]).astype(BF16)
        normed, inv_std = norm_rows(jnp.transpose(pair[row].astype(F32)))
        normed_in[row] = normed.astype(normed_in.dtype)
        inv_in[row : row + 1] = inv_std
        zln = (normed * gain_col + bias_col).astype(BF16)
        proj = dot(w_flip, zln, 1, 0)
        for side in range(2):
            base = 2 * side * hidden
            sig = sigmoid(proj[base : base + hidden])
            masked = masks[row] * sig
            value = masked * (1.0 - sig) * proj[base + hidden : base + 2 * hidden]
            slopes[row, base : base + hidden, :] = value.astype(slopes.dtype)
            slopes[row, base + hidden : base + 2 * hidden, :] = masked.astype(slopes.dtype)


def sort_d_left_kernel(*refs):
    *pieces, d_left_panel = refs
    for step, piece in enumerate(pieces):
        d_left_panel[partner(step, len(pieces))] = piece[...]


def both_halves(blocks, count):
    order = wide_order(2 * count, count)
    return jnp.stack(
        [blocks[order.index(place)] + blocks[order.index(count + place)] for place in range(count)]
    )


def finish_kernel(
    d_right_panel, d_left_panel, slopes, d_gate_pre, normed_in, inv_in, gain_col, weights, grad
):
    rows = grad.shape[0]
    count, depth, width = d_left_panel.shape
    hidden = count * depth // rows
    for row in range(rows):
        d_right = cell_row(d_right_panel, row, rows)
        d_right = both_halves(d_right.reshape(2 * count, depth // rows, width), count)
        parts = []
        for side, d_value in enumerate((cell_row(d_left_panel, row, rows), d_right.reshape(hidden, width))):
            for base in (2 * side * hidden, (2 * side + 1) * hidden):
                slope = slopes[row, base : base + hidden, :].astype(F32)
                parts.append((d_value * slope).astype(BF16))
        parts.append(d_gate_pre[row])
        d_in = dot(weights[...], jnp.concatenate(parts, axis=0), 1, 0) * gain_col[...]
        normed = normed_in[row].astype(F32)
        mean_grad = jnp.mean(d_in, axis=0, keepdims=True)
        mean_cross = jnp.mean(d_in * normed, axis=0, keepdims=True)
        result = inv_in[row : row + 1] * (d_in - mean_grad - normed * mean_cross)
        grad[row] = jnp.transpose(result).astype(BF16)


def swap(values, count):
    groups = [wide_order(lax.axis_size("row"), count)]
    return lax.all_to_all(
        values, "row", split_axis=0, concat_axis=0, tiled=True, axis_index_groups=groups
    )


def swap_half(values, count):
    devices = range(lax.axis_size("row"))
    groups = [[d for d in devices if d // count == half] for half in range(len(devices) // count)]
    return lax.all_to_all(
        values, "row", split_axis=0, concat_axis=0, tiled=True, axis_index_groups=groups
    )


def swap_pieces(pieces):
    devices = range(lax.axis_size("row"))
    return [pieces[0]] + [
        lax.ppermute(pieces[step], "row", [(d, d ^ step) for d in devices])
        for step in range(1, len(pieces))
    ]


def kernel_shards(
    pair,
    cotangent,
    residue_mask,
    ln_in_gain,
    ln_in_bias,
    w_proj,
    w_gate,
    ln_out_gain,
    ln_out_bias,
    w_out,
):
    rows, width, channels = pair.shape
    hidden = w_out.shape[0]
    halves = 2
    devices = lax.axis_size("row")
    count = devices // halves
    block = hidden // count
    left_rows, right_rows = rows * count, rows * devices
    shape = jax.ShapeDtypeStruct
    panel = shape((count, rows * block, width), BF16)
    wide_panel = shape((devices, rows * block, width), BF16)
    mask = residue_mask.reshape(1, width)
    gain, bias = ln_in_gain.reshape(1, channels), ln_in_bias.reshape(1, channels)
    out_gain, out_bias = ln_out_gain.reshape(1, hidden), ln_out_bias.reshape(1, hidden)
    cells = rows * width
    piece = shape((rows * block, width), BF16)
    left_panel = pltpu.VMEM(panel.shape, BF16)
    left_wide = pltpu.VMEM((left_rows * block, width), F32)
    right_wide = pltpu.VMEM((right_rows * block, width), F32)
    (own_right,) = call(
        project_right_kernel,
        "project_right",
        [wide_panel],
        [pair, mask, gain, bias, w_proj],
        fetched=range(5),
        flops=2 * cells * channels * 2 * hidden,
        limit=64 * 1024 * 1024 - 640 * 1024,
    )
    right_panel = swap(own_right, count)
    pieces = call(
        project_left_kernel,
        "project_left",
        [piece] * count,
        [pair, mask, gain, bias, w_proj, own_right],
        fetched=range(5),
        unread=(5,),
        scratch=[left_panel],
        flops=2 * cells * channels * 2 * hidden,
    )
    pieces = swap_pieces(pieces)
    (left_all,) = call(
        sort_left_kernel,
        "sort_left",
        [shape((block, left_rows, width), BF16)],
        pieces,
        scratch=[left_wide],
    )
    d_hat_centered, gate_slope = call(
        prepare_kernel,
        "prepare",
        [shape((rows, hidden, width), F32), shape((rows, channels, width), F32)],
        [pair, cotangent, gain, bias, w_gate, out_gain, w_out],
        fetched=range(7),
        flops=2 * cells * channels * 2 * hidden,
    )
    products, right_all = call(
        tri_kernel,
        "tri",
        [panel, shape((block, right_rows, width), BF16)],
        [right_panel, left_all, d_hat_centered],
        unread=(2,),
        scratch=[left_wide, right_wide],
        flops=2 * block * left_rows * width * right_rows,
    )
    products = swap_half(products, count)
    (d_products,) = call(
        middle_kernel,
        "middle",
        [panel],
        [products, d_hat_centered],
        flops=20 * cells * hidden,
    )
    d_products = swap_half(d_products, count)
    d_right_panel, d_tri_all = call(
        d_right_kernel,
        "d_right",
        [wide_panel, shape((block, left_rows, width), BF16)],
        [d_products, left_all],
        scratch=[left_wide, right_wide],
        flops=2 * block * left_rows * width * right_rows,
    )
    d_right_panel = swap(d_right_panel, count)
    d_pieces = call(
        d_left_kernel,
        "d_left",
        [piece] * count,
        [d_tri_all, right_all],
        scratch=[left_wide],
        flops=2 * block * left_rows * width * right_rows,
    )
    d_pieces = swap_pieces(d_pieces)
    (d_left_panel,) = call(sort_d_left_kernel, "sort_d_left", [panel], d_pieces)
    slopes, d_gate_pre, normed_in, inv_in, gain_col, weights = call(
        slopes_kernel,
        "slopes",
        [
            shape((rows, 4 * hidden, width), BF16),
            shape((rows, channels, width), BF16),
            shape((rows, channels, width), BF16),
            shape((rows, width), F32),
            shape((channels, channels), F32),
            shape((channels, 4 * hidden + channels), BF16),
        ],
        [
            products,
            gate_slope,
            pair,
            mask,
            gain,
            bias,
            w_proj,
            w_gate,
            out_gain,
            out_bias,
            w_out,
        ],
        fetched=range(2, 11),
        flops=2 * cells * channels * 6 * hidden,
    )
    (grad,) = call(
        finish_kernel,
        "finish",
        [shape(pair.shape, BF16)],
        [
            d_right_panel,
            d_left_panel,
            slopes,
            d_gate_pre,
            normed_in,
            inv_in,
            gain_col,
            weights,
        ],
        flops=2 * cells * channels * 4 * hidden,
    )
    return grad


def normalize(values, reduce_axis):
    mean_value = jnp.mean(values, axis=reduce_axis, keepdims=True)
    centered = values - mean_value
    variance = jnp.mean(centered * centered, axis=reduce_axis, keepdims=True)
    inv_std = lax.rsqrt(variance + 1e-05)
    return (centered * inv_std, inv_std)


def norm_backward(upstream, normed, inv_std, reduce_axis):
    mean_grad = jnp.mean(upstream, axis=reduce_axis, keepdims=True)
    mean_cross = jnp.mean(upstream * normed, axis=reduce_axis, keepdims=True)
    return inv_std * (upstream - mean_grad - normed * mean_cross)


def shards(
    pair,
    cotangent,
    residue_mask,
    ln_in_gain,
    ln_in_bias,
    w_proj,
    w_gate,
    ln_out_gain,
    ln_out_bias,
    w_out,
):
    local_rows = pair.shape[0]
    local_cols = pair.shape[1]
    hidden = w_out.shape[0]
    chan_index = lax.axis_index("chan")
    row_start = lax.axis_index("row") * local_rows
    col_start = chan_index * local_cols
    mask_float = residue_mask.astype(jnp.float32)
    row_mask = lax.dynamic_slice_in_dim(mask_float, row_start, local_rows)
    col_mask = lax.dynamic_slice_in_dim(mask_float, col_start, local_cols)
    cell_mask = (row_mask[:, None] * col_mask[None, :])[None]
    normed, inv_std = normalize(pair.astype(jnp.float32), -1)
    normed_pair = (normed * ln_in_gain + ln_in_bias).astype(jnp.bfloat16)
    projected = jnp.einsum("rmc,ch->hrm", normed_pair, w_proj, preferred_element_type=jnp.float32)
    left_panel = (
        cell_mask * jax.nn.sigmoid(projected[:hidden]) * projected[hidden : 2 * hidden]
    ).astype(jnp.bfloat16)
    right_panel = (
        cell_mask * jax.nn.sigmoid(projected[2 * hidden : 3 * hidden]) * projected[3 * hidden :]
    ).astype(jnp.bfloat16)
    panels = lax.all_to_all(
        jnp.stack([left_panel, right_panel]), "row", split_axis=1, concat_axis=2, tiled=True
    )
    left_all = panels[0]
    right_all = panels[1]
    right_rows = lax.all_to_all(right_all, "chan", split_axis=1, concat_axis=2, tiled=True)
    partner = right_rows
    tri_part = jnp.einsum(
        "gik,gjk->gij",
        lax.all_gather(left_all, "chan", axis=2, tiled=True),
        partner,
        preferred_element_type=jnp.float32,
    ).astype(jnp.bfloat16)
    tri_cells = lax.all_to_all(tri_part, "row", split_axis=1, concat_axis=0, tiled=True)
    tri_hat, inv_tri = normalize(tri_cells.astype(jnp.float32), 0)
    scaled = (tri_hat * ln_out_gain[:, None, None] + ln_out_bias[:, None, None]).astype(
        jnp.bfloat16
    )
    proj_out = jnp.einsum("hrm,hc->rmc", scaled, w_out, preferred_element_type=jnp.float32)
    gate_value = jax.nn.sigmoid(
        jnp.einsum("rmc,cd->rmd", normed_pair, w_gate, preferred_element_type=jnp.float32)
    )
    cot_float = cotangent.astype(jnp.float32)
    d_gate_pre = (cot_float * proj_out * gate_value * (1.0 - gate_value)).astype(jnp.bfloat16)
    d_scaled = (cot_float * gate_value).astype(jnp.bfloat16)
    d_hat = jnp.einsum("rmc,hc->hrm", d_scaled, w_out, preferred_element_type=jnp.float32)
    d_hat = d_hat * ln_out_gain[:, None, None]
    d_tri = norm_backward(d_hat, tri_hat, inv_tri, 0).astype(jnp.bfloat16)
    d_tri_all = lax.all_to_all(d_tri, "row", split_axis=0, concat_axis=1, tiled=True)
    panel_piece = lax.all_gather(d_tri_all, "chan", axis=2, tiled=True)
    partner = right_all
    d_left = jnp.einsum("gij,gjk->gik", panel_piece, partner, preferred_element_type=jnp.float32)
    contribution = jnp.einsum(
        "gij,gik->gjk", panel_piece, left_all, preferred_element_type=jnp.float32
    )
    d_right = contribution
    d_left, d_right = (d_left, d_right)
    d_stack = jnp.stack([d_left, d_right]).astype(jnp.bfloat16)
    d_panels = lax.all_to_all(d_stack, "row", split_axis=2, concat_axis=1, tiled=True)

    def gating(d_value, gate_proj, value_proj):
        sigmoid_val = jax.nn.sigmoid(gate_proj)
        masked_grad = d_value.astype(jnp.float32) * cell_mask
        return (
            masked_grad * value_proj * sigmoid_val * (1.0 - sigmoid_val),
            masked_grad * sigmoid_val,
        )

    gate_left, value_left = gating(d_panels[0], projected[:hidden], projected[hidden : 2 * hidden])
    gate_right, value_right = gating(
        d_panels[1], projected[2 * hidden : 3 * hidden], projected[3 * hidden :]
    )
    d_proj = jnp.concatenate([gate_left, value_left, gate_right, value_right], axis=0).astype(
        jnp.bfloat16
    )
    d_normed = jnp.einsum("hrm,ch->rmc", d_proj, w_proj, preferred_element_type=jnp.float32)
    d_normed = d_normed + jnp.einsum(
        "rmd,cd->rmc", d_gate_pre, w_gate, preferred_element_type=jnp.float32
    )
    d_input = d_normed * ln_in_gain
    return norm_backward(d_input, normed, inv_std, -1).astype(jnp.bfloat16)


def solution(mesh):
    fits = mesh.shape["chan"] == 1 and mesh.shape["row"] in (8, 16)
    return jax.shard_map(
        kernel_shards if fits else shards,
        mesh=mesh,
        in_specs=(
            P(("grp", "row"), "chan", None),
            P(("grp", "row"), "chan", None),
            P("grp"),
            P(),
            P(),
            P(),
            P(),
            P(),
            P(),
            P(),
        ),
        out_specs=P(("grp", "row"), "chan", None),
        check_vma=False,
    )
```

```python
import functools

import jax
import jax.numpy as jnp
from jax import lax
from jax.experimental import pallas as pl
from jax.experimental.pallas import tpu as pltpu
from jax.sharding import PartitionSpec as P

F32 = jnp.float32
BF16 = jnp.bfloat16
VMEM_LIMIT = 16 * 1024 * 1024


def dot(lhs, rhs, lhs_dim, rhs_dim):
    return lax.dot_general(
        lhs, rhs, (((lhs_dim,), (rhs_dim,)), ((), ())), preferred_element_type=F32
    )


def transposed(matrix):
    return jnp.transpose(matrix.astype(F32)).astype(BF16)


def sigmoid(values):
    return 1.0 / (1.0 + jnp.exp(-values))


def column(row):
    size = row.shape[1]
    return jnp.transpose(jnp.broadcast_to(row, (size, size)))


def norm_rows(values):
    centered = values - jnp.mean(values, axis=0, keepdims=True)
    variance = jnp.mean(centered * centered, axis=0, keepdims=True)
    inv_std = lax.rsqrt(variance + 1e-05)
    return centered * inv_std, inv_std


def call(
    kernel, name, outs, args, fetched=(), unread=(), scratch=(), flops=0, limit=VMEM_LIMIT
):
    moved = sum(a.size * a.dtype.itemsize for a in args) + sum(
        o.size * jnp.dtype(o.dtype).itemsize for o in outs
    )
    n_args, n_outs, n_fetched = len(args), len(outs), len(fetched)

    def body(*refs):
        ins = list(refs[:n_args])
        rest = refs[n_args + n_outs :]
        copies = []
        for n, place in enumerate(fetched):
            copies.append(pltpu.make_async_copy(ins[place], rest[n], rest[n_fetched].at[n]))
            ins[place] = rest[n]
        for copy in copies:
            copy.start()
        for copy in copies:
            copy.wait()
        kernel(*ins, *refs[n_args : n_args + n_outs], *rest[n_fetched + (n_fetched > 0) :])

    buffers = [pltpu.VMEM(args[place].shape, args[place].dtype) for place in fetched]
    if fetched:
        buffers.append(pltpu.SemaphoreType.DMA((n_fetched,)))
    return pl.pallas_call(
        body,
        name=name,
        out_shape=outs,
        in_specs=[
            pl.BlockSpec(
                memory_space=pltpu.HBM if n in fetched else pl.ANY if n in unread else pltpu.VMEM
            )
            for n in range(n_args)
        ],
        out_specs=[pl.BlockSpec(memory_space=pltpu.VMEM) for _ in outs],
        scratch_shapes=buffers + list(scratch),
        compiler_params=pltpu.CompilerParams(vmem_limit_bytes=limit),
        cost_estimate=pl.CostEstimate(flops=flops, bytes_accessed=moved, transcendentals=0),
    )(*args)


def cell_masks(mask, rows):
    columns = mask[...].astype(F32)
    shape = (rows, columns.shape[1])
    first = lax.axis_index("row") * rows
    own = lax.broadcasted_iota(jnp.int32, shape, 1) == (
        lax.broadcasted_iota(jnp.int32, shape, 0) + first
    )
    row_mask = jnp.sum(jnp.where(own, columns, 0.0), axis=1, keepdims=True)
    cells = row_mask * columns
    return [cells[row : row + 1] for row in range(rows)]


def wide_order(devices, count):
    inner = [(place + count // 2) % count for place in range(count)]
    return [device for place in range(count) for device in (inner[place], count + place)]


def partner(step, count):
    return lax.rem(lax.axis_index("row"), count) ^ step


def gated_rows(pair, mask, gain, bias, w_proj, side):
    rows = pair.shape[0]
    hidden = w_proj.shape[1] // 4
    w_flip = transposed(w_proj[:, 2 * side * hidden : 2 * (side + 1) * hidden])
    gain_col, bias_col = column(gain[...]), column(bias[...])
    masks = cell_masks(mask, rows)
    for row in range(rows):
        normed, _ = norm_rows(jnp.transpose(pair[row].astype(F32)))
        zln = (normed * gain_col + bias_col).astype(BF16)
        proj = dot(w_flip, zln, 1, 0)
        yield row, masks[row] * sigmoid(proj[:hidden]) * proj[hidden:]


def project_right_kernel(pair, mask, gain, bias, w_proj, right_panel):
    rows = pair.shape[0]
    devices, depth, width = right_panel.shape
    block = depth // rows
    count = w_proj.shape[1] // 4 // block
    for row, right in gated_rows(pair, mask, gain, bias, w_proj, 1):
        right = right.reshape(count, block, width).astype(BF16)
        for rank in range(devices):
            place = wide_order(devices, count)[rank] % count
            right_panel[rank, row * block : (row + 1) * block, :] = right[place]


def project_left_kernel(pair, mask, gain, bias, w_proj, after, *refs):
    del after
    *pieces, left_panel = refs
    rows = pair.shape[0]
    count, depth, width = left_panel.shape
    block = depth // rows
    for row, left in gated_rows(pair, mask, gain, bias, w_proj, 0):
        left = left.reshape(count, block, width).astype(BF16)
        left_panel[:, row * block : (row + 1) * block, :] = left
    for step, piece in enumerate(pieces):
        piece[...] = left_panel[partner(step, count)]


def prepare_kernel(
    pair, cotangent, gain, bias, w_gate, out_gain, w_out, d_hat_centered, gate_slope
):
    gate_flip = transposed(w_gate[...])
    gain_col, bias_col = column(gain[...]), column(bias[...])
    out_gain_col = column(out_gain[...])
    for row in range(pair.shape[0]):
        normed, _ = norm_rows(jnp.transpose(pair[row].astype(F32)))
        zln = (normed * gain_col + bias_col).astype(BF16)
        gate = sigmoid(dot(gate_flip, zln, 1, 0))
        cot = jnp.transpose(cotangent[row].astype(F32))
        d_scaled = (cot * gate).astype(BF16)
        d_hat = dot(w_out[...], d_scaled, 1, 0) * out_gain_col
        d_hat_centered[row] = d_hat - jnp.mean(d_hat, axis=0, keepdims=True)
        gate_slope[row] = cot * gate * (1.0 - gate)


def spread(panel, wide):
    wide[...] = panel[...].astype(F32).reshape(wide.shape)


def wide_places(panel, count):
    devices, depth, _ = panel.shape
    for rank, device in enumerate(wide_order(devices, count)):
        yield rank, slice(device * depth, (device + 1) * depth)


def sort_left_kernel(*refs):
    *pieces, left_all, left_wide = refs
    block, left_rows, _ = left_all.shape
    depth = pieces[0].shape[0]
    for step, piece in enumerate(pieces):
        start = pl.multiple_of(partner(step, len(pieces)) * depth, depth)
        left_wide[pl.ds(start, depth), :] = piece[...].astype(F32)
    for h in range(block):
        left_all[h] = left_wide[pl.ds(h, left_rows, stride=block), :].astype(BF16)


def tri_kernel(right_panel, left_all, after, products, right_all, left_wide, right_wide):
    del after
    block, left_rows, _ = left_all.shape
    right_rows = right_all.shape[1]
    for rank, place in wide_places(right_panel, products.shape[0]):
        right_wide[place, :] = right_panel[rank].astype(F32)
    for h in range(block):
        right = right_wide[pl.ds(h, right_rows, stride=block), :].astype(BF16)
        right_all[h] = right
        left_wide[pl.ds(h, left_rows, stride=block), :] = dot(left_all[h], right, 1, 1)
    products[...] = left_wide[...].astype(BF16).reshape(products.shape)


def cell_row(ref, row, rows):
    count, depth, width = ref.shape
    block = depth // rows
    return ref[:, row * block : (row + 1) * block, :].astype(F32).reshape(count * block, width)


def middle_kernel(products, d_hat_centered, d_products):
    rows = d_hat_centered.shape[0]
    count, depth, width = products.shape
    block = depth // rows
    for row in range(rows):
        tri_hat, inv_std = norm_rows(cell_row(products, row, rows))
        d_hat = d_hat_centered[row]
        cross = jnp.mean(d_hat * tri_hat, axis=0, keepdims=True)
        d_tri = inv_std * (d_hat - tri_hat * cross)
        d_products[:, row * block : (row + 1) * block, :] = d_tri.reshape(
            count, block, width
        ).astype(BF16)


def d_right_kernel(d_products, left_all, d_right_panel, d_tri_all, left_wide, right_wide):
    block, left_rows, _ = left_all.shape
    right_rows = right_wide.shape[0] // block
    spread(d_products, left_wide)
    for h in range(block):
        d_tri = left_wide[pl.ds(h, left_rows, stride=block), :].astype(BF16)
        d_tri_all[h] = d_tri
        right_wide[pl.ds(h, right_rows, stride=block), :] = dot(d_tri, left_all[h], 0, 0)
    for rank, place in wide_places(d_right_panel, d_products.shape[0]):
        d_right_panel[rank] = right_wide[place, :].astype(BF16)


def d_left_kernel(d_tri_all, right_all, *refs):
    *pieces, left_wide = refs
    block, left_rows, _ = d_tri_all.shape
    for h in range(block):
        left_wide[pl.ds(h, left_rows, stride=block), :] = dot(d_tri_all[h], right_all[h], 1, 0)
    depth = pieces[0].shape[0]
    for step, piece in enumerate(pieces):
        start = pl.multiple_of(partner(step, len(pieces)) * depth, depth)
        piece[...] = left_wide[pl.ds(start, depth), :].astype(BF16)


def gate_back_kernel(products, gate_slope, out_gain, out_bias, w_out, d_gate_pre):
    rows = gate_slope.shape[0]
    out_flip = transposed(w_out[...])
    out_gain_col, out_bias_col = column(out_gain[...]), column(out_bias[...])
    for row in range(rows):
        tri_hat, _ = norm_rows(cell_row(products, row, rows))
        scaled = (tri_hat * out_gain_col + out_bias_col).astype(BF16)
        d_gate_pre[row] = (dot(out_flip, scaled, 1, 0) * gate_slope[row]).astype(BF16)


def slopes_kernel(
    pair, mask, gain, bias, w_proj, w_gate, after, slopes, normed_in, inv_in, in_gain, weights
):
    del after
    rows = pair.shape[0]
    hidden = w_proj.shape[1] // 4
    w_flip = transposed(w_proj[...])
    gain_col, bias_col = column(gain[...]), column(bias[...])
    in_gain[...] = gain_col
    weights[...] = jnp.concatenate([w_proj[...], w_gate[...]], axis=1)
    masks = cell_masks(mask, rows)
    for row in range(rows):
        normed, inv_std = norm_rows(jnp.transpose(pair[row].astype(F32)))
        normed_in[row] = normed.astype(normed_in.dtype)
        inv_in[row : row + 1] = inv_std
        zln = (normed * gain_col + bias_col).astype(BF16)
        proj = dot(w_flip, zln, 1, 0)
        for side in range(2):
            base = 2 * side * hidden
            sig = sigmoid(proj[base : base + hidden])
            masked = masks[row] * sig
            value = masked * (1.0 - sig) * proj[base + hidden : base + 2 * hidden]
            slopes[row, base : base + hidden, :] = value.astype(slopes.dtype)
            slopes[row, base + hidden : base + 2 * hidden, :] = masked.astype(slopes.dtype)


def sort_d_left_kernel(*refs):
    *pieces, d_left_panel = refs
    for step, piece in enumerate(pieces):
        d_left_panel[partner(step, len(pieces))] = piece[...]


def both_halves(blocks, count):
    order = wide_order(2 * count, count)
    return jnp.stack(
        [blocks[order.index(place)] + blocks[order.index(count + place)] for place in range(count)]
    )


def finish_kernel(
    d_right_panel, d_left_panel, slopes, d_gate_pre, normed_in, inv_in, gain_col, weights, grad
):
    rows = grad.shape[0]
    count, depth, width = d_left_panel.shape
    hidden = count * depth // rows
    for row in range(rows):
        d_right = cell_row(d_right_panel, row, rows)
        d_right = both_halves(d_right.reshape(2 * count, depth // rows, width), count)
        parts = []
        for side, d_value in enumerate((cell_row(d_left_panel, row, rows), d_right.reshape(hidden, width))):
            for base in (2 * side * hidden, (2 * side + 1) * hidden):
                slope = slopes[row, base : base + hidden, :].astype(F32)
                parts.append((d_value * slope).astype(BF16))
        parts.append(d_gate_pre[row])
        d_in = dot(weights[...], jnp.concatenate(parts, axis=0), 1, 0) * gain_col[...]
        normed = normed_in[row].astype(F32)
        mean_grad = jnp.mean(d_in, axis=0, keepdims=True)
        mean_cross = jnp.mean(d_in * normed, axis=0, keepdims=True)
        result = inv_in[row : row + 1] * (d_in - mean_grad - normed * mean_cross)
        grad[row] = jnp.transpose(result).astype(BF16)


def swap(values, count):
    groups = [wide_order(lax.axis_size("row"), count)]
    return lax.all_to_all(
        values, "row", split_axis=0, concat_axis=0, tiled=True, axis_index_groups=groups
    )


def swap_half(values, count):
    devices = range(lax.axis_size("row"))
    groups = [[d for d in devices if d // count == half] for half in range(len(devices) // count)]
    return lax.all_to_all(
        values, "row", split_axis=0, concat_axis=0, tiled=True, axis_index_groups=groups
    )


def swap_pieces(pieces):
    devices = range(lax.axis_size("row"))
    swapped = [
        lax.ppermute(pieces[step], "row", [(d, d ^ step) for d in devices])
        for step in range(len(pieces) - 1, 0, -1)
    ]
    return [pieces[0]] + swapped[::-1]


def kernel_shards(
    pair,
    cotangent,
    residue_mask,
    ln_in_gain,
    ln_in_bias,
    w_proj,
    w_gate,
    ln_out_gain,
    ln_out_bias,
    w_out,
):
    rows, width, channels = pair.shape
    hidden = w_out.shape[0]
    halves = 2
    devices = lax.axis_size("row")
    count = devices // halves
    block = hidden // count
    left_rows, right_rows = rows * count, rows * devices
    shape = jax.ShapeDtypeStruct
    panel = shape((count, rows * block, width), BF16)
    wide_panel = shape((devices, rows * block, width), BF16)
    mask = residue_mask.reshape(1, width)
    gain, bias = ln_in_gain.reshape(1, channels), ln_in_bias.reshape(1, channels)
    out_gain, out_bias = ln_out_gain.reshape(1, hidden), ln_out_bias.reshape(1, hidden)
    cells = rows * width
    piece = shape((rows * block, width), BF16)
    left_panel = pltpu.VMEM(panel.shape, BF16)
    left_wide = pltpu.VMEM((left_rows * block, width), F32)
    right_wide = pltpu.VMEM((right_rows * block, width), F32)
    (own_right,) = call(
        project_right_kernel,
        "project_right",
        [wide_panel],
        [pair, mask, gain, bias, w_proj],
        fetched=range(5),
        flops=2 * cells * channels * 2 * hidden,
        limit=64 * 1024 * 1024 - 640 * 1024,
    )
    right_panel = swap(own_right, count)
    pieces = call(
        project_left_kernel,
        "project_left",
        [piece] * count,
        [pair, mask, gain, bias, w_proj, own_right],
        fetched=range(5),
        unread=(5,),
        scratch=[left_panel],
        flops=2 * cells * channels * 2 * hidden,
    )
    pieces = swap_pieces(pieces)
    (left_all,) = call(
        sort_left_kernel,
        "sort_left",
        [shape((block, left_rows, width), BF16)],
        pieces,
        scratch=[left_wide],
    )
    d_hat_centered, gate_slope = call(
        prepare_kernel,
        "prepare",
        [shape((rows, hidden, width), F32), shape((rows, channels, width), F32)],
        [pair, cotangent, gain, bias, w_gate, out_gain, w_out],
        fetched=range(7),
        flops=2 * cells * channels * 2 * hidden,
    )
    products, right_all = call(
        tri_kernel,
        "tri",
        [panel, shape((block, right_rows, width), BF16)],
        [right_panel, left_all, d_hat_centered],
        unread=(2,),
        scratch=[left_wide, right_wide],
        flops=2 * block * left_rows * width * right_rows,
    )
    products = swap_half(products, count)
    (d_products,) = call(
        middle_kernel,
        "middle",
        [panel],
        [products, d_hat_centered],
        flops=20 * cells * hidden,
    )
    d_products = swap_half(d_products, count)
    d_right_panel, d_tri_all = call(
        d_right_kernel,
        "d_right",
        [wide_panel, shape((block, left_rows, width), BF16)],
        [d_products, left_all],
        scratch=[left_wide, right_wide],
        flops=2 * block * left_rows * width * right_rows,
    )
    d_right_panel = swap(d_right_panel, count)
    d_pieces = call(
        d_left_kernel,
        "d_left",
        [piece] * count,
        [d_tri_all, right_all],
        scratch=[left_wide],
        flops=2 * block * left_rows * width * right_rows,
    )
    d_pieces = swap_pieces(d_pieces)
    (d_left_panel,) = call(sort_d_left_kernel, "sort_d_left", [panel], d_pieces)
    (d_gate_pre,) = call(
        gate_back_kernel,
        "gate_back",
        [shape((rows, channels, width), BF16)],
        [products, gate_slope, out_gain, out_bias, w_out],
        fetched=range(2, 5),
        flops=2 * cells * channels * hidden,
    )
    slopes, normed_in, inv_in, gain_col, weights = call(
        slopes_kernel,
        "slopes",
        [
            shape((rows, 4 * hidden, width), BF16),
            shape((rows, channels, width), BF16),
            shape((rows, width), F32),
            shape((channels, channels), F32),
            shape((channels, 4 * hidden + channels), BF16),
        ],
        [pair, mask, gain, bias, w_proj, w_gate, d_gate_pre],
        fetched=range(6),
        unread=(6,),
        flops=2 * cells * channels * 4 * hidden,
    )
    (grad,) = call(
        finish_kernel,
        "finish",
        [shape(pair.shape, BF16)],
        [
            d_right_panel,
            d_left_panel,
            slopes,
            d_gate_pre,
            normed_in,
            inv_in,
            gain_col,
            weights,
        ],
        flops=2 * cells * channels * 4 * hidden,
    )
    return grad


def normalize(values, reduce_axis):
    mean_value = jnp.mean(values, axis=reduce_axis, keepdims=True)
    centered = values - mean_value
    variance = jnp.mean(centered * centered, axis=reduce_axis, keepdims=True)
    inv_std = lax.rsqrt(variance + 1e-05)
    return (centered * inv_std, inv_std)


def norm_backward(upstream, normed, inv_std, reduce_axis):
    mean_grad = jnp.mean(upstream, axis=reduce_axis, keepdims=True)
    mean_cross = jnp.mean(upstream * normed, axis=reduce_axis, keepdims=True)
    return inv_std * (upstream - mean_grad - normed * mean_cross)


def shards(
    pair,
    cotangent,
    residue_mask,
    ln_in_gain,
    ln_in_bias,
    w_proj,
    w_gate,
    ln_out_gain,
    ln_out_bias,
    w_out,
):
    local_rows = pair.shape[0]
    local_cols = pair.shape[1]
    hidden = w_out.shape[0]
    chan_index = lax.axis_index("chan")
    row_start = lax.axis_index("row") * local_rows
    col_start = chan_index * local_cols
    mask_float = residue_mask.astype(jnp.float32)
    row_mask = lax.dynamic_slice_in_dim(mask_float, row_start, local_rows)
    col_mask = lax.dynamic_slice_in_dim(mask_float, col_start, local_cols)
    cell_mask = (row_mask[:, None] * col_mask[None, :])[None]
    normed, inv_std = normalize(pair.astype(jnp.float32), -1)
    normed_pair = (normed * ln_in_gain + ln_in_bias).astype(jnp.bfloat16)
    projected = jnp.einsum("rmc,ch->hrm", normed_pair, w_proj, preferred_element_type=jnp.float32)
    left_panel = (
        cell_mask * jax.nn.sigmoid(projected[:hidden]) * projected[hidden : 2 * hidden]
    ).astype(jnp.bfloat16)
    right_panel = (
        cell_mask * jax.nn.sigmoid(projected[2 * hidden : 3 * hidden]) * projected[3 * hidden :]
    ).astype(jnp.bfloat16)
    panels = lax.all_to_all(
        jnp.stack([left_panel, right_panel]), "row", split_axis=1, concat_axis=2, tiled=True
    )
    left_all = panels[0]
    right_all = panels[1]
    right_rows = lax.all_to_all(right_all, "chan", split_axis=1, concat_axis=2, tiled=True)
    partner = right_rows
    tri_part = jnp.einsum(
        "gik,gjk->gij",
        lax.all_gather(left_all, "chan", axis=2, tiled=True),
        partner,
        preferred_element_type=jnp.float32,
    ).astype(jnp.bfloat16)
    tri_cells = lax.all_to_all(tri_part, "row", split_axis=1, concat_axis=0, tiled=True)
    tri_hat, inv_tri = normalize(tri_cells.astype(jnp.float32), 0)
    scaled = (tri_hat * ln_out_gain[:, None, None] + ln_out_bias[:, None, None]).astype(
        jnp.bfloat16
    )
    proj_out = jnp.einsum("hrm,hc->rmc", scaled, w_out, preferred_element_type=jnp.float32)
    gate_value = jax.nn.sigmoid(
        jnp.einsum("rmc,cd->rmd", normed_pair, w_gate, preferred_element_type=jnp.float32)
    )
    cot_float = cotangent.astype(jnp.float32)
    d_gate_pre = (cot_float * proj_out * gate_value * (1.0 - gate_value)).astype(jnp.bfloat16)
    d_scaled = (cot_float * gate_value).astype(jnp.bfloat16)
    d_hat = jnp.einsum("rmc,hc->hrm", d_scaled, w_out, preferred_element_type=jnp.float32)
    d_hat = d_hat * ln_out_gain[:, None, None]
    d_tri = norm_backward(d_hat, tri_hat, inv_tri, 0).astype(jnp.bfloat16)
    d_tri_all = lax.all_to_all(d_tri, "row", split_axis=0, concat_axis=1, tiled=True)
    panel_piece = lax.all_gather(d_tri_all, "chan", axis=2, tiled=True)
    partner = right_all
    d_left = jnp.einsum("gij,gjk->gik", panel_piece, partner, preferred_element_type=jnp.float32)
    contribution = jnp.einsum(
        "gij,gik->gjk", panel_piece, left_all, preferred_element_type=jnp.float32
    )
    d_right = contribution
    d_left, d_right = (d_left, d_right)
    d_stack = jnp.stack([d_left, d_right]).astype(jnp.bfloat16)
    d_panels = lax.all_to_all(d_stack, "row", split_axis=2, concat_axis=1, tiled=True)

    def gating(d_value, gate_proj, value_proj):
        sigmoid_val = jax.nn.sigmoid(gate_proj)
        masked_grad = d_value.astype(jnp.float32) * cell_mask
        return (
            masked_grad * value_proj * sigmoid_val * (1.0 - sigmoid_val),
            masked_grad * sigmoid_val,
        )

    gate_left, value_left = gating(d_panels[0], projected[:hidden], projected[hidden : 2 * hidden])
    gate_right, value_right = gating(
        d_panels[1], projected[2 * hidden : 3 * hidden], projected[3 * hidden :]
    )
    d_proj = jnp.concatenate([gate_left, value_left, gate_right, value_right], axis=0).astype(
        jnp.bfloat16
    )
    d_normed = jnp.einsum("hrm,ch->rmc", d_proj, w_proj, preferred_element_type=jnp.float32)
    d_normed = d_normed + jnp.einsum(
        "rmd,cd->rmc", d_gate_pre, w_gate, preferred_element_type=jnp.float32
    )
    d_input = d_normed * ln_in_gain
    return norm_backward(d_input, normed, inv_std, -1).astype(jnp.bfloat16)


def solution(mesh):
    fits = mesh.shape["chan"] == 1 and mesh.shape["row"] in (8, 16)
    return jax.shard_map(
        kernel_shards if fits else shards,
        mesh=mesh,
        in_specs=(
            P(("grp", "row"), "chan", None),
            P(("grp", "row"), "chan", None),
            P("grp"),
            P(),
            P(),
            P(),
            P(),
            P(),
            P(),
            P(),
        ),
        out_specs=P(("grp", "row"), "chan", None),
        check_vma=False,
    )
```

```python
import functools

import jax
import jax.numpy as jnp
from jax import lax
from jax.experimental import pallas as pl
from jax.experimental.pallas import tpu as pltpu
from jax.sharding import PartitionSpec as P

F32 = jnp.float32
BF16 = jnp.bfloat16
VMEM_LIMIT = 16 * 1024 * 1024


def dot(lhs, rhs, lhs_dim, rhs_dim):
    return lax.dot_general(
        lhs, rhs, (((lhs_dim,), (rhs_dim,)), ((), ())), preferred_element_type=F32
    )


def transposed(matrix):
    return jnp.transpose(matrix.astype(F32)).astype(BF16)


def sigmoid(values):
    return 1.0 / (1.0 + jnp.exp(-values))


def column(row):
    size = row.shape[1]
    return jnp.transpose(jnp.broadcast_to(row, (size, size)))


def norm_rows(values):
    centered = values - jnp.mean(values, axis=0, keepdims=True)
    variance = jnp.mean(centered * centered, axis=0, keepdims=True)
    inv_std = lax.rsqrt(variance + 1e-05)
    return centered * inv_std, inv_std


def call(
    kernel, name, outs, args, fetched=(), unread=(), scratch=(), flops=0, limit=VMEM_LIMIT
):
    moved = sum(a.size * a.dtype.itemsize for a in args) + sum(
        o.size * jnp.dtype(o.dtype).itemsize for o in outs
    )
    n_args, n_outs, n_fetched = len(args), len(outs), len(fetched)

    def body(*refs):
        ins = list(refs[:n_args])
        rest = refs[n_args + n_outs :]
        copies = []
        for n, place in enumerate(fetched):
            copies.append(pltpu.make_async_copy(ins[place], rest[n], rest[n_fetched].at[n]))
            ins[place] = rest[n]
        for copy in copies:
            copy.start()
        for copy in copies:
            copy.wait()
        kernel(*ins, *refs[n_args : n_args + n_outs], *rest[n_fetched + (n_fetched > 0) :])

    buffers = [pltpu.VMEM(args[place].shape, args[place].dtype) for place in fetched]
    if fetched:
        buffers.append(pltpu.SemaphoreType.DMA((n_fetched,)))
    return pl.pallas_call(
        body,
        name=name,
        out_shape=outs,
        in_specs=[
            pl.BlockSpec(
                memory_space=pltpu.HBM if n in fetched else pl.ANY if n in unread else pltpu.VMEM
            )
            for n in range(n_args)
        ],
        out_specs=[pl.BlockSpec(memory_space=pltpu.VMEM) for _ in outs],
        scratch_shapes=buffers + list(scratch),
        compiler_params=pltpu.CompilerParams(vmem_limit_bytes=limit),
        cost_estimate=pl.CostEstimate(flops=flops, bytes_accessed=moved, transcendentals=0),
    )(*args)


def cell_masks(mask, rows):
    columns = mask[...].astype(F32)
    shape = (rows, columns.shape[1])
    first = lax.axis_index("row") * rows
    own = lax.broadcasted_iota(jnp.int32, shape, 1) == (
        lax.broadcasted_iota(jnp.int32, shape, 0) + first
    )
    row_mask = jnp.sum(jnp.where(own, columns, 0.0), axis=1, keepdims=True)
    cells = row_mask * columns
    return [cells[row : row + 1] for row in range(rows)]


def wide_order(devices, count):
    inner = [(place + count // 2) % count for place in range(count)]
    return [device for place in range(count) for device in (inner[place], count + place)]


def distance(step, count):
    return (count - step) % count


def partner(step, count):
    return lax.rem(lax.axis_index("row"), count) ^ distance(step, count)


def gated_rows(pair, mask, gain, bias, w_proj, side):
    rows = pair.shape[0]
    hidden = w_proj.shape[1] // 4
    w_flip = transposed(w_proj[:, 2 * side * hidden : 2 * (side + 1) * hidden])
    gain_col, bias_col = column(gain[...]), column(bias[...])
    masks = cell_masks(mask, rows)
    for row in range(rows):
        normed, _ = norm_rows(jnp.transpose(pair[row].astype(F32)))
        zln = (normed * gain_col + bias_col).astype(BF16)
        proj = dot(w_flip, zln, 1, 0)
        yield row, masks[row] * sigmoid(proj[:hidden]) * proj[hidden:]


def project_right_kernel(pair, mask, gain, bias, w_proj, right_panel):
    rows = pair.shape[0]
    devices, depth, width = right_panel.shape
    block = depth // rows
    count = w_proj.shape[1] // 4 // block
    for row, right in gated_rows(pair, mask, gain, bias, w_proj, 1):
        right = right.reshape(count, block, width).astype(BF16)
        for rank in range(devices):
            place = wide_order(devices, count)[rank] % count
            right_panel[rank, row * block : (row + 1) * block, :] = right[place]


def project_left_kernel(pair, mask, gain, bias, w_proj, after, *refs):
    del after
    *pieces, left_panel = refs
    rows = pair.shape[0]
    count, depth, width = left_panel.shape
    block = depth // rows
    for row, left in gated_rows(pair, mask, gain, bias, w_proj, 0):
        left = left.reshape(count, block, width).astype(BF16)
        left_panel[:, row * block : (row + 1) * block, :] = left
    for step, piece in enumerate(pieces):
        piece[...] = left_panel[partner(step, count)]


def prepare_kernel(
    pair, cotangent, gain, bias, w_gate, out_gain, w_out, d_hat_centered, gate_slope
):
    gate_flip = transposed(w_gate[...])
    gain_col, bias_col = column(gain[...]), column(bias[...])
    out_gain_col = column(out_gain[...])
    for row in range(pair.shape[0]):
        normed, _ = norm_rows(jnp.transpose(pair[row].astype(F32)))
        zln = (normed * gain_col + bias_col).astype(BF16)
        gate = sigmoid(dot(gate_flip, zln, 1, 0))
        cot = jnp.transpose(cotangent[row].astype(F32))
        d_scaled = (cot * gate).astype(BF16)
        d_hat = dot(w_out[...], d_scaled, 1, 0) * out_gain_col
        d_hat_centered[row] = d_hat - jnp.mean(d_hat, axis=0, keepdims=True)
        gate_slope[row] = cot * gate * (1.0 - gate)


def spread(panel, wide):
    wide[...] = panel[...].astype(F32).reshape(wide.shape)


def wide_places(panel, count):
    devices, depth, _ = panel.shape
    for rank, device in enumerate(wide_order(devices, count)):
        yield rank, slice(device * depth, (device + 1) * depth)


def sort_left_kernel(*refs):
    *pieces, left_all, left_wide = refs
    block, left_rows, _ = left_all.shape
    depth = pieces[0].shape[0]
    for step, piece in enumerate(pieces):
        start = pl.multiple_of(partner(step, len(pieces)) * depth, depth)
        left_wide[pl.ds(start, depth), :] = piece[...].astype(F32)
    for h in range(block):
        left_all[h] = left_wide[pl.ds(h, left_rows, stride=block), :].astype(BF16)


def tri_kernel(right_panel, left_all, after, products, right_all, left_wide, right_wide):
    del after
    block, left_rows, _ = left_all.shape
    right_rows = right_all.shape[1]
    for rank, place in wide_places(right_panel, products.shape[0]):
        right_wide[place, :] = right_panel[rank].astype(F32)
    for h in range(block):
        right = right_wide[pl.ds(h, right_rows, stride=block), :].astype(BF16)
        right_all[h] = right
        left_wide[pl.ds(h, left_rows, stride=block), :] = dot(left_all[h], right, 1, 1)
    products[...] = left_wide[...].astype(BF16).reshape(products.shape)


def cell_row(ref, row, rows):
    count, depth, width = ref.shape
    block = depth // rows
    return ref[:, row * block : (row + 1) * block, :].astype(F32).reshape(count * block, width)


def middle_kernel(products, d_hat_centered, d_products):
    rows = d_hat_centered.shape[0]
    count, depth, width = products.shape
    block = depth // rows
    for row in range(rows):
        tri_hat, inv_std = norm_rows(cell_row(products, row, rows))
        d_hat = d_hat_centered[row]
        cross = jnp.mean(d_hat * tri_hat, axis=0, keepdims=True)
        d_tri = inv_std * (d_hat - tri_hat * cross)
        d_products[:, row * block : (row + 1) * block, :] = d_tri.reshape(
            count, block, width
        ).astype(BF16)


def d_right_kernel(d_products, left_all, d_right_panel, d_tri_all, left_wide, right_wide):
    block, left_rows, _ = left_all.shape
    right_rows = right_wide.shape[0] // block
    spread(d_products, left_wide)
    for h in range(block):
        d_tri = left_wide[pl.ds(h, left_rows, stride=block), :].astype(BF16)
        d_tri_all[h] = d_tri
        right_wide[pl.ds(h, right_rows, stride=block), :] = dot(d_tri, left_all[h], 0, 0)
    for rank, place in wide_places(d_right_panel, d_products.shape[0]):
        d_right_panel[rank] = right_wide[place, :].astype(BF16)


def d_left_kernel(d_tri_all, right_all, *refs):
    *pieces, left_wide = refs
    block, left_rows, _ = d_tri_all.shape
    for h in range(block):
        left_wide[pl.ds(h, left_rows, stride=block), :] = dot(d_tri_all[h], right_all[h], 1, 0)
    depth = pieces[0].shape[0]
    for step, piece in enumerate(pieces):
        start = pl.multiple_of(partner(step, len(pieces)) * depth, depth)
        piece[...] = left_wide[pl.ds(start, depth), :].astype(BF16)


def gate_back_kernel(products, gate_slope, out_gain, out_bias, w_out, d_gate_pre):
    rows = gate_slope.shape[0]
    out_flip = transposed(w_out[...])
    out_gain_col, out_bias_col = column(out_gain[...]), column(out_bias[...])
    for row in range(rows):
        tri_hat, _ = norm_rows(cell_row(products, row, rows))
        scaled = (tri_hat * out_gain_col + out_bias_col).astype(BF16)
        d_gate_pre[row] = (dot(out_flip, scaled, 1, 0) * gate_slope[row]).astype(BF16)


def slopes_kernel(
    pair, mask, gain, bias, w_proj, w_gate, after, slopes, normed_in, inv_in, in_gain, weights
):
    del after
    rows = pair.shape[0]
    hidden = w_proj.shape[1] // 4
    w_flip = transposed(w_proj[...])
    gain_col, bias_col = column(gain[...]), column(bias[...])
    in_gain[...] = gain_col
    weights[...] = jnp.concatenate([w_proj[...], w_gate[...]], axis=1)
    masks = cell_masks(mask, rows)
    for row in range(rows):
        normed, inv_std = norm_rows(jnp.transpose(pair[row].astype(F32)))
        normed_in[row] = normed.astype(normed_in.dtype)
        inv_in[row : row + 1] = inv_std
        zln = (normed * gain_col + bias_col).astype(BF16)
        proj = dot(w_flip, zln, 1, 0)
        for side in range(2):
            base = 2 * side * hidden
            sig = sigmoid(proj[base : base + hidden])
            masked = masks[row] * sig
            value = masked * (1.0 - sig) * proj[base + hidden : base + 2 * hidden]
            slopes[row, base : base + hidden, :] = value.astype(slopes.dtype)
            slopes[row, base + hidden : base + 2 * hidden, :] = masked.astype(slopes.dtype)


def sort_d_left_kernel(*refs):
    *pieces, d_left_panel = refs
    for step, piece in enumerate(pieces):
        d_left_panel[partner(step, len(pieces))] = piece[...]


def both_halves(blocks, count):
    order = wide_order(2 * count, count)
    return jnp.stack(
        [blocks[order.index(place)] + blocks[order.index(count + place)] for place in range(count)]
    )


def finish_kernel(
    d_right_panel, d_left_panel, slopes, d_gate_pre, normed_in, inv_in, gain_col, weights, grad
):
    rows = grad.shape[0]
    count, depth, width = d_left_panel.shape
    hidden = count * depth // rows
    for row in range(rows):
        d_right = cell_row(d_right_panel, row, rows)
        d_right = both_halves(d_right.reshape(2 * count, depth // rows, width), count)
        parts = []
        for side, d_value in enumerate((cell_row(d_left_panel, row, rows), d_right.reshape(hidden, width))):
            for base in (2 * side * hidden, (2 * side + 1) * hidden):
                slope = slopes[row, base : base + hidden, :].astype(F32)
                parts.append((d_value * slope).astype(BF16))
        parts.append(d_gate_pre[row])
        d_in = dot(weights[...], jnp.concatenate(parts, axis=0), 1, 0) * gain_col[...]
        normed = normed_in[row].astype(F32)
        mean_grad = jnp.mean(d_in, axis=0, keepdims=True)
        mean_cross = jnp.mean(d_in * normed, axis=0, keepdims=True)
        result = inv_in[row : row + 1] * (d_in - mean_grad - normed * mean_cross)
        grad[row] = jnp.transpose(result).astype(BF16)


def swap(values, count):
    groups = [wide_order(lax.axis_size("row"), count)]
    return lax.all_to_all(
        values, "row", split_axis=0, concat_axis=0, tiled=True, axis_index_groups=groups
    )


def swap_half(values, count):
    devices = range(lax.axis_size("row"))
    groups = [[d for d in devices if d // count == half] for half in range(len(devices) // count)]
    return lax.all_to_all(
        values, "row", split_axis=0, concat_axis=0, tiled=True, axis_index_groups=groups
    )


def swap_pieces(pieces):
    devices = range(lax.axis_size("row"))
    count = len(pieces)
    return [pieces[0]] + [
        lax.ppermute(pieces[step], "row", [(d, d ^ distance(step, count)) for d in devices])
        for step in range(1, count)
    ]


def kernel_shards(
    pair,
    cotangent,
    residue_mask,
    ln_in_gain,
    ln_in_bias,
    w_proj,
    w_gate,
    ln_out_gain,
    ln_out_bias,
    w_out,
):
    rows, width, channels = pair.shape
    hidden = w_out.shape[0]
    halves = 2
    devices = lax.axis_size("row")
    count = devices // halves
    block = hidden // count
    left_rows, right_rows = rows * count, rows * devices
    shape = jax.ShapeDtypeStruct
    panel = shape((count, rows * block, width), BF16)
    wide_panel = shape((devices, rows * block, width), BF16)
    mask = residue_mask.reshape(1, width)
    gain, bias = ln_in_gain.reshape(1, channels), ln_in_bias.reshape(1, channels)
    out_gain, out_bias = ln_out_gain.reshape(1, hidden), ln_out_bias.reshape(1, hidden)
    cells = rows * width
    piece = shape((rows * block, width), BF16)
    left_panel = pltpu.VMEM(panel.shape, BF16)
    left_wide = pltpu.VMEM((left_rows * block, width), F32)
    right_wide = pltpu.VMEM((right_rows * block, width), F32)
    (own_right,) = call(
        project_right_kernel,
        "project_right",
        [wide_panel],
        [pair, mask, gain, bias, w_proj],
        fetched=range(5),
        flops=2 * cells * channels * 2 * hidden,
        limit=64 * 1024 * 1024 - 640 * 1024,
    )
    right_panel = swap(own_right, count)
    pieces = call(
        project_left_kernel,
        "project_left",
        [piece] * count,
        [pair, mask, gain, bias, w_proj, own_right],
        fetched=range(5),
        unread=(5,),
        scratch=[left_panel],
        flops=2 * cells * channels * 2 * hidden,
    )
    pieces = swap_pieces(pieces)
    (left_all,) = call(
        sort_left_kernel,
        "sort_left",
        [shape((block, left_rows, width), BF16)],
        pieces,
        scratch=[left_wide],
    )
    d_hat_centered, gate_slope = call(
        prepare_kernel,
        "prepare",
        [shape((rows, hidden, width), F32), shape((rows, channels, width), F32)],
        [pair, cotangent, gain, bias, w_gate, out_gain, w_out],
        fetched=range(7),
        flops=2 * cells * channels * 2 * hidden,
    )
    products, right_all = call(
        tri_kernel,
        "tri",
        [panel, shape((block, right_rows, width), BF16)],
        [right_panel, left_all, d_hat_centered],
        unread=(2,),
        scratch=[left_wide, right_wide],
        flops=2 * block * left_rows * width * right_rows,
    )
    products = swap_half(products, count)
    (d_products,) = call(
        middle_kernel,
        "middle",
        [panel],
        [products, d_hat_centered],
        flops=20 * cells * hidden,
    )
    d_products = swap_half(d_products, count)
    d_right_panel, d_tri_all = call(
        d_right_kernel,
        "d_right",
        [wide_panel, shape((block, left_rows, width), BF16)],
        [d_products, left_all],
        scratch=[left_wide, right_wide],
        flops=2 * block * left_rows * width * right_rows,
    )
    d_right_panel = swap(d_right_panel, count)
    d_pieces = call(
        d_left_kernel,
        "d_left",
        [piece] * count,
        [d_tri_all, right_all],
        scratch=[left_wide],
        flops=2 * block * left_rows * width * right_rows,
    )
    d_pieces = swap_pieces(d_pieces)
    (d_left_panel,) = call(sort_d_left_kernel, "sort_d_left", [panel], d_pieces)
    (d_gate_pre,) = call(
        gate_back_kernel,
        "gate_back",
        [shape((rows, channels, width), BF16)],
        [products, gate_slope, out_gain, out_bias, w_out],
        fetched=range(2, 5),
        flops=2 * cells * channels * hidden,
    )
    slopes, normed_in, inv_in, gain_col, weights = call(
        slopes_kernel,
        "slopes",
        [
            shape((rows, 4 * hidden, width), BF16),
            shape((rows, channels, width), BF16),
            shape((rows, width), F32),
            shape((channels, channels), F32),
            shape((channels, 4 * hidden + channels), BF16),
        ],
        [pair, mask, gain, bias, w_proj, w_gate, d_gate_pre],
        fetched=range(6),
        unread=(6,),
        flops=2 * cells * channels * 4 * hidden,
    )
    (grad,) = call(
        finish_kernel,
        "finish",
        [shape(pair.shape, BF16)],
        [
            d_right_panel,
            d_left_panel,
            slopes,
            d_gate_pre,
            normed_in,
            inv_in,
            gain_col,
            weights,
        ],
        flops=2 * cells * channels * 4 * hidden,
    )
    return grad


def normalize(values, reduce_axis):
    mean_value = jnp.mean(values, axis=reduce_axis, keepdims=True)
    centered = values - mean_value
    variance = jnp.mean(centered * centered, axis=reduce_axis, keepdims=True)
    inv_std = lax.rsqrt(variance + 1e-05)
    return (centered * inv_std, inv_std)


def norm_backward(upstream, normed, inv_std, reduce_axis):
    mean_grad = jnp.mean(upstream, axis=reduce_axis, keepdims=True)
    mean_cross = jnp.mean(upstream * normed, axis=reduce_axis, keepdims=True)
    return inv_std * (upstream - mean_grad - normed * mean_cross)


def shards(
    pair,
    cotangent,
    residue_mask,
    ln_in_gain,
    ln_in_bias,
    w_proj,
    w_gate,
    ln_out_gain,
    ln_out_bias,
    w_out,
):
    local_rows = pair.shape[0]
    local_cols = pair.shape[1]
    hidden = w_out.shape[0]
    chan_index = lax.axis_index("chan")
    row_start = lax.axis_index("row") * local_rows
    col_start = chan_index * local_cols
    mask_float = residue_mask.astype(jnp.float32)
    row_mask = lax.dynamic_slice_in_dim(mask_float, row_start, local_rows)
    col_mask = lax.dynamic_slice_in_dim(mask_float, col_start, local_cols)
    cell_mask = (row_mask[:, None] * col_mask[None, :])[None]
    normed, inv_std = normalize(pair.astype(jnp.float32), -1)
    normed_pair = (normed * ln_in_gain + ln_in_bias).astype(jnp.bfloat16)
    projected = jnp.einsum("rmc,ch->hrm", normed_pair, w_proj, preferred_element_type=jnp.float32)
    left_panel = (
        cell_mask * jax.nn.sigmoid(projected[:hidden]) * projected[hidden : 2 * hidden]
    ).astype(jnp.bfloat16)
    right_panel = (
        cell_mask * jax.nn.sigmoid(projected[2 * hidden : 3 * hidden]) * projected[3 * hidden :]
    ).astype(jnp.bfloat16)
    panels = lax.all_to_all(
        jnp.stack([left_panel, right_panel]), "row", split_axis=1, concat_axis=2, tiled=True
    )
    left_all = panels[0]
    right_all = panels[1]
    right_rows = lax.all_to_all(right_all, "chan", split_axis=1, concat_axis=2, tiled=True)
    partner = right_rows
    tri_part = jnp.einsum(
        "gik,gjk->gij",
        lax.all_gather(left_all, "chan", axis=2, tiled=True),
        partner,
        preferred_element_type=jnp.float32,
    ).astype(jnp.bfloat16)
    tri_cells = lax.all_to_all(tri_part, "row", split_axis=1, concat_axis=0, tiled=True)
    tri_hat, inv_tri = normalize(tri_cells.astype(jnp.float32), 0)
    scaled = (tri_hat * ln_out_gain[:, None, None] + ln_out_bias[:, None, None]).astype(
        jnp.bfloat16
    )
    proj_out = jnp.einsum("hrm,hc->rmc", scaled, w_out, preferred_element_type=jnp.float32)
    gate_value = jax.nn.sigmoid(
        jnp.einsum("rmc,cd->rmd", normed_pair, w_gate, preferred_element_type=jnp.float32)
    )
    cot_float = cotangent.astype(jnp.float32)
    d_gate_pre = (cot_float * proj_out * gate_value * (1.0 - gate_value)).astype(jnp.bfloat16)
    d_scaled = (cot_float * gate_value).astype(jnp.bfloat16)
    d_hat = jnp.einsum("rmc,hc->hrm", d_scaled, w_out, preferred_element_type=jnp.float32)
    d_hat = d_hat * ln_out_gain[:, None, None]
    d_tri = norm_backward(d_hat, tri_hat, inv_tri, 0).astype(jnp.bfloat16)
    d_tri_all = lax.all_to_all(d_tri, "row", split_axis=0, concat_axis=1, tiled=True)
    panel_piece = lax.all_gather(d_tri_all, "chan", axis=2, tiled=True)
    partner = right_all
    d_left = jnp.einsum("gij,gjk->gik", panel_piece, partner, preferred_element_type=jnp.float32)
    contribution = jnp.einsum(
        "gij,gik->gjk", panel_piece, left_all, preferred_element_type=jnp.float32
    )
    d_right = contribution
    d_left, d_right = (d_left, d_right)
    d_stack = jnp.stack([d_left, d_right]).astype(jnp.bfloat16)
    d_panels = lax.all_to_all(d_stack, "row", split_axis=2, concat_axis=1, tiled=True)

    def gating(d_value, gate_proj, value_proj):
        sigmoid_val = jax.nn.sigmoid(gate_proj)
        masked_grad = d_value.astype(jnp.float32) * cell_mask
        return (
            masked_grad * value_proj * sigmoid_val * (1.0 - sigmoid_val),
            masked_grad * sigmoid_val,
        )

    gate_left, value_left = gating(d_panels[0], projected[:hidden], projected[hidden : 2 * hidden])
    gate_right, value_right = gating(
        d_panels[1], projected[2 * hidden : 3 * hidden], projected[3 * hidden :]
    )
    d_proj = jnp.concatenate([gate_left, value_left, gate_right, value_right], axis=0).astype(
        jnp.bfloat16
    )
    d_normed = jnp.einsum("hrm,ch->rmc", d_proj, w_proj, preferred_element_type=jnp.float32)
    d_normed = d_normed + jnp.einsum(
        "rmd,cd->rmc", d_gate_pre, w_gate, preferred_element_type=jnp.float32
    )
    d_input = d_normed * ln_in_gain
    return norm_backward(d_input, normed, inv_std, -1).astype(jnp.bfloat16)


def solution(mesh):
    fits = mesh.shape["chan"] == 1 and mesh.shape["row"] in (8, 16)
    return jax.shard_map(
        kernel_shards if fits else shards,
        mesh=mesh,
        in_specs=(
            P(("grp", "row"), "chan", None),
            P(("grp", "row"), "chan", None),
            P("grp"),
            P(),
            P(),
            P(),
            P(),
            P(),
            P(),
            P(),
        ),
        out_specs=P(("grp", "row"), "chan", None),
        check_vma=False,
    )
```

```python
import functools

import jax
import jax.numpy as jnp
from jax import lax
from jax.experimental import pallas as pl
from jax.experimental.pallas import tpu as pltpu
from jax.sharding import PartitionSpec as P

F32 = jnp.float32
BF16 = jnp.bfloat16
VMEM_LIMIT = 16 * 1024 * 1024


def dot(lhs, rhs, lhs_dim, rhs_dim):
    return lax.dot_general(
        lhs, rhs, (((lhs_dim,), (rhs_dim,)), ((), ())), preferred_element_type=F32
    )


def transposed(matrix):
    return jnp.transpose(matrix.astype(F32)).astype(BF16)


def sigmoid(values):
    return 1.0 / (1.0 + jnp.exp(-values))


def column(row):
    size = row.shape[1]
    return jnp.transpose(jnp.broadcast_to(row, (size, size)))


def norm_rows(values):
    centered = values - jnp.mean(values, axis=0, keepdims=True)
    variance = jnp.mean(centered * centered, axis=0, keepdims=True)
    inv_std = lax.rsqrt(variance + 1e-05)
    return centered * inv_std, inv_std


def call(
    kernel, name, outs, args, fetched=(), unread=(), scratch=(), flops=0, limit=VMEM_LIMIT
):
    moved = sum(a.size * a.dtype.itemsize for a in args) + sum(
        o.size * jnp.dtype(o.dtype).itemsize for o in outs
    )
    n_args, n_outs, n_fetched = len(args), len(outs), len(fetched)

    def body(*refs):
        ins = list(refs[:n_args])
        rest = refs[n_args + n_outs :]
        copies = []
        for n, place in enumerate(fetched):
            copies.append(pltpu.make_async_copy(ins[place], rest[n], rest[n_fetched].at[n]))
            ins[place] = rest[n]
        for copy in copies:
            copy.start()
        for copy in copies:
            copy.wait()
        kernel(*ins, *refs[n_args : n_args + n_outs], *rest[n_fetched + (n_fetched > 0) :])

    buffers = [pltpu.VMEM(args[place].shape, args[place].dtype) for place in fetched]
    if fetched:
        buffers.append(pltpu.SemaphoreType.DMA((n_fetched,)))
    return pl.pallas_call(
        body,
        name=name,
        out_shape=outs,
        in_specs=[
            pl.BlockSpec(
                memory_space=pltpu.HBM if n in fetched else pl.ANY if n in unread else pltpu.VMEM
            )
            for n in range(n_args)
        ],
        out_specs=[pl.BlockSpec(memory_space=pltpu.VMEM) for _ in outs],
        scratch_shapes=buffers + list(scratch),
        compiler_params=pltpu.CompilerParams(vmem_limit_bytes=limit),
        cost_estimate=pl.CostEstimate(flops=flops, bytes_accessed=moved, transcendentals=0),
    )(*args)


def cell_masks(mask, rows):
    columns = mask[...].astype(F32)
    shape = (rows, columns.shape[1])
    first = lax.axis_index("row") * rows
    own = lax.broadcasted_iota(jnp.int32, shape, 1) == (
        lax.broadcasted_iota(jnp.int32, shape, 0) + first
    )
    row_mask = jnp.sum(jnp.where(own, columns, 0.0), axis=1, keepdims=True)
    cells = row_mask * columns
    return [cells[row : row + 1] for row in range(rows)]


def wide_order(devices, count):
    inner = [(place + count // 2) % count for place in range(count)]
    return [device for place in range(count) for device in (inner[place], count + place)]


def distance(step, count):
    far = sorted(range(3, count), key=lambda apart: -(apart // 2))
    return [*range(min(3, count)), *far][step]


def partner(step, count):
    return lax.rem(lax.axis_index("row"), count) ^ distance(step, count)


def gated_rows(pair, mask, gain, bias, w_proj, side):
    rows = pair.shape[0]
    hidden = w_proj.shape[1] // 4
    w_flip = transposed(w_proj[:, 2 * side * hidden : 2 * (side + 1) * hidden])
    gain_col, bias_col = column(gain[...]), column(bias[...])
    masks = cell_masks(mask, rows)
    for row in range(rows):
        normed, _ = norm_rows(jnp.transpose(pair[row].astype(F32)))
        zln = (normed * gain_col + bias_col).astype(BF16)
        proj = dot(w_flip, zln, 1, 0)
        yield row, masks[row] * sigmoid(proj[:hidden]) * proj[hidden:]


def project_right_kernel(pair, mask, gain, bias, w_proj, right_panel):
    rows = pair.shape[0]
    devices, depth, width = right_panel.shape
    block = depth // rows
    count = w_proj.shape[1] // 4 // block
    for row, right in gated_rows(pair, mask, gain, bias, w_proj, 1):
        right = right.reshape(count, block, width).astype(BF16)
        for rank in range(devices):
            place = wide_order(devices, count)[rank] % count
            right_panel[rank, row * block : (row + 1) * block, :] = right[place]


def project_left_kernel(pair, mask, gain, bias, w_proj, after, *refs):
    del after
    *pieces, left_panel = refs
    rows = pair.shape[0]
    count, depth, width = left_panel.shape
    block = depth // rows
    for row, left in gated_rows(pair, mask, gain, bias, w_proj, 0):
        left = left.reshape(count, block, width).astype(BF16)
        left_panel[:, row * block : (row + 1) * block, :] = left
    for step, piece in enumerate(pieces):
        piece[...] = left_panel[partner(step, count)]


def prepare_kernel(
    pair, cotangent, gain, bias, w_gate, out_gain, w_out, d_hat_centered, gate_slope
):
    gate_flip = transposed(w_gate[...])
    gain_col, bias_col = column(gain[...]), column(bias[...])
    out_gain_col = column(out_gain[...])
    for row in range(pair.shape[0]):
        normed, _ = norm_rows(jnp.transpose(pair[row].astype(F32)))
        zln = (normed * gain_col + bias_col).astype(BF16)
        gate = sigmoid(dot(gate_flip, zln, 1, 0))
        cot = jnp.transpose(cotangent[row].astype(F32))
        d_scaled = (cot * gate).astype(BF16)
        d_hat = dot(w_out[...], d_scaled, 1, 0) * out_gain_col
        d_hat_centered[row] = d_hat - jnp.mean(d_hat, axis=0, keepdims=True)
        gate_slope[row] = cot * gate * (1.0 - gate)


def spread(panel, wide):
    wide[...] = panel[...].astype(F32).reshape(wide.shape)


def wide_places(panel, count):
    devices, depth, _ = panel.shape
    for rank, device in enumerate(wide_order(devices, count)):
        yield rank, slice(device * depth, (device + 1) * depth)


def sort_left_kernel(*refs):
    *pieces, left_all, left_wide = refs
    block, left_rows, _ = left_all.shape
    depth = pieces[0].shape[0]
    for step, piece in enumerate(pieces):
        start = pl.multiple_of(partner(step, len(pieces)) * depth, depth)
        left_wide[pl.ds(start, depth), :] = piece[...].astype(F32)
    for h in range(block):
        left_all[h] = left_wide[pl.ds(h, left_rows, stride=block), :].astype(BF16)


def tri_kernel(right_panel, left_all, after, products, right_all, left_wide, right_wide):
    del after
    block, left_rows, _ = left_all.shape
    right_rows = right_all.shape[1]
    for rank, place in wide_places(right_panel, products.shape[0]):
        right_wide[place, :] = right_panel[rank].astype(F32)
    for h in range(block):
        right = right_wide[pl.ds(h, right_rows, stride=block), :].astype(BF16)
        right_all[h] = right
        left_wide[pl.ds(h, left_rows, stride=block), :] = dot(left_all[h], right, 1, 1)
    products[...] = left_wide[...].astype(BF16).reshape(products.shape)


def cell_row(ref, row, rows):
    count, depth, width = ref.shape
    block = depth // rows
    return ref[:, row * block : (row + 1) * block, :].astype(F32).reshape(count * block, width)


def middle_kernel(products, d_hat_centered, d_products):
    rows = d_hat_centered.shape[0]
    count, depth, width = products.shape
    block = depth // rows
    for row in range(rows):
        tri_hat, inv_std = norm_rows(cell_row(products, row, rows))
        d_hat = d_hat_centered[row]
        cross = jnp.mean(d_hat * tri_hat, axis=0, keepdims=True)
        d_tri = inv_std * (d_hat - tri_hat * cross)
        d_products[:, row * block : (row + 1) * block, :] = d_tri.reshape(
            count, block, width
        ).astype(BF16)


def d_right_kernel(d_products, left_all, d_right_panel, d_tri_all, left_wide, right_wide):
    block, left_rows, _ = left_all.shape
    right_rows = right_wide.shape[0] // block
    spread(d_products, left_wide)
    for h in range(block):
        d_tri = left_wide[pl.ds(h, left_rows, stride=block), :].astype(BF16)
        d_tri_all[h] = d_tri
        right_wide[pl.ds(h, right_rows, stride=block), :] = dot(d_tri, left_all[h], 0, 0)
    for rank, place in wide_places(d_right_panel, d_products.shape[0]):
        d_right_panel[rank] = right_wide[place, :].astype(BF16)


def d_left_kernel(d_tri_all, right_all, *refs):
    *pieces, left_wide = refs
    block, left_rows, _ = d_tri_all.shape
    for h in range(block):
        left_wide[pl.ds(h, left_rows, stride=block), :] = dot(d_tri_all[h], right_all[h], 1, 0)
    depth = pieces[0].shape[0]
    for step, piece in enumerate(pieces):
        start = pl.multiple_of(partner(step, len(pieces)) * depth, depth)
        piece[...] = left_wide[pl.ds(start, depth), :].astype(BF16)


def gate_back_kernel(products, gate_slope, out_gain, out_bias, w_out, d_gate_pre):
    rows = gate_slope.shape[0]
    out_flip = transposed(w_out[...])
    out_gain_col, out_bias_col = column(out_gain[...]), column(out_bias[...])
    for row in range(rows):
        tri_hat, _ = norm_rows(cell_row(products, row, rows))
        scaled = (tri_hat * out_gain_col + out_bias_col).astype(BF16)
        d_gate_pre[row] = (dot(out_flip, scaled, 1, 0) * gate_slope[row]).astype(BF16)


def slopes_kernel(
    pair, mask, gain, bias, w_proj, w_gate, after, slopes, normed_in, inv_in, in_gain, weights
):
    del after
    rows = pair.shape[0]
    hidden = w_proj.shape[1] // 4
    w_flip = transposed(w_proj[...])
    gain_col, bias_col = column(gain[...]), column(bias[...])
    in_gain[...] = gain_col
    weights[...] = jnp.concatenate([w_proj[...], w_gate[...]], axis=1)
    masks = cell_masks(mask, rows)
    for row in range(rows):
        normed, inv_std = norm_rows(jnp.transpose(pair[row].astype(F32)))
        normed_in[row] = normed.astype(normed_in.dtype)
        inv_in[row : row + 1] = inv_std
        zln = (normed * gain_col + bias_col).astype(BF16)
        proj = dot(w_flip, zln, 1, 0)
        for side in range(2):
            base = 2 * side * hidden
            sig = sigmoid(proj[base : base + hidden])
            masked = masks[row] * sig
            value = masked * (1.0 - sig) * proj[base + hidden : base + 2 * hidden]
            slopes[row, base : base + hidden, :] = value.astype(slopes.dtype)
            slopes[row, base + hidden : base + 2 * hidden, :] = masked.astype(slopes.dtype)


def sort_d_left_kernel(*refs):
    *pieces, d_left_panel = refs
    for step, piece in enumerate(pieces):
        d_left_panel[partner(step, len(pieces))] = piece[...]


def both_halves(blocks, count):
    order = wide_order(2 * count, count)
    return jnp.stack(
        [blocks[order.index(place)] + blocks[order.index(count + place)] for place in range(count)]
    )


def finish_kernel(
    d_right_panel, d_left_panel, slopes, d_gate_pre, normed_in, inv_in, gain_col, weights, grad
):
    rows = grad.shape[0]
    count, depth, width = d_left_panel.shape
    hidden = count * depth // rows
    for row in range(rows):
        d_right = cell_row(d_right_panel, row, rows)
        d_right = both_halves(d_right.reshape(2 * count, depth // rows, width), count)
        parts = []
        for side, d_value in enumerate((cell_row(d_left_panel, row, rows), d_right.reshape(hidden, width))):
            for base in (2 * side * hidden, (2 * side + 1) * hidden):
                slope = slopes[row, base : base + hidden, :].astype(F32)
                parts.append((d_value * slope).astype(BF16))
        parts.append(d_gate_pre[row])
        d_in = dot(weights[...], jnp.concatenate(parts, axis=0), 1, 0) * gain_col[...]
        normed = normed_in[row].astype(F32)
        mean_grad = jnp.mean(d_in, axis=0, keepdims=True)
        mean_cross = jnp.mean(d_in * normed, axis=0, keepdims=True)
        result = inv_in[row : row + 1] * (d_in - mean_grad - normed * mean_cross)
        grad[row] = jnp.transpose(result).astype(BF16)


def swap(values, count):
    groups = [wide_order(lax.axis_size("row"), count)]
    return lax.all_to_all(
        values, "row", split_axis=0, concat_axis=0, tiled=True, axis_index_groups=groups
    )


def swap_half(values, count):
    devices = range(lax.axis_size("row"))
    groups = [[d for d in devices if d // count == half] for half in range(len(devices) // count)]
    return lax.all_to_all(
        values, "row", split_axis=0, concat_axis=0, tiled=True, axis_index_groups=groups
    )


def swap_pieces(pieces):
    devices = range(lax.axis_size("row"))
    count = len(pieces)
    return [pieces[0]] + [
        lax.ppermute(pieces[step], "row", [(d, d ^ distance(step, count)) for d in devices])
        for step in range(1, count)
    ]


def kernel_shards(
    pair,
    cotangent,
    residue_mask,
    ln_in_gain,
    ln_in_bias,
    w_proj,
    w_gate,
    ln_out_gain,
    ln_out_bias,
    w_out,
):
    rows, width, channels = pair.shape
    hidden = w_out.shape[0]
    halves = 2
    devices = lax.axis_size("row")
    count = devices // halves
    block = hidden // count
    left_rows, right_rows = rows * count, rows * devices
    shape = jax.ShapeDtypeStruct
    panel = shape((count, rows * block, width), BF16)
    wide_panel = shape((devices, rows * block, width), BF16)
    mask = residue_mask.reshape(1, width)
    gain, bias = ln_in_gain.reshape(1, channels), ln_in_bias.reshape(1, channels)
    out_gain, out_bias = ln_out_gain.reshape(1, hidden), ln_out_bias.reshape(1, hidden)
    cells = rows * width
    piece = shape((rows * block, width), BF16)
    left_panel = pltpu.VMEM(panel.shape, BF16)
    left_wide = pltpu.VMEM((left_rows * block, width), F32)
    right_wide = pltpu.VMEM((right_rows * block, width), F32)
    (own_right,) = call(
        project_right_kernel,
        "project_right",
        [wide_panel],
        [pair, mask, gain, bias, w_proj],
        fetched=range(5),
        flops=2 * cells * channels * 2 * hidden,
        limit=64 * 1024 * 1024 - 640 * 1024,
    )
    right_panel = swap(own_right, count)
    pieces = call(
        project_left_kernel,
        "project_left",
        [piece] * count,
        [pair, mask, gain, bias, w_proj, own_right],
        fetched=range(5),
        unread=(5,),
        scratch=[left_panel],
        flops=2 * cells * channels * 2 * hidden,
    )
    pieces = swap_pieces(pieces)
    (left_all,) = call(
        sort_left_kernel,
        "sort_left",
        [shape((block, left_rows, width), BF16)],
        pieces,
        scratch=[left_wide],
    )
    d_hat_centered, gate_slope = call(
        prepare_kernel,
        "prepare",
        [shape((rows, hidden, width), F32), shape((rows, channels, width), F32)],
        [pair, cotangent, gain, bias, w_gate, out_gain, w_out],
        fetched=range(7),
        flops=2 * cells * channels * 2 * hidden,
    )
    products, right_all = call(
        tri_kernel,
        "tri",
        [panel, shape((block, right_rows, width), BF16)],
        [right_panel, left_all, d_hat_centered],
        unread=(2,),
        scratch=[left_wide, right_wide],
        flops=2 * block * left_rows * width * right_rows,
    )
    products = swap_half(products, count)
    (d_products,) = call(
        middle_kernel,
        "middle",
        [panel],
        [products, d_hat_centered],
        flops=20 * cells * hidden,
    )
    d_products = swap_half(d_products, count)
    d_right_panel, d_tri_all = call(
        d_right_kernel,
        "d_right",
        [wide_panel, shape((block, left_rows, width), BF16)],
        [d_products, left_all],
        scratch=[left_wide, right_wide],
        flops=2 * block * left_rows * width * right_rows,
    )
    d_right_panel = swap(d_right_panel, count)
    d_pieces = call(
        d_left_kernel,
        "d_left",
        [piece] * count,
        [d_tri_all, right_all],
        scratch=[left_wide],
        flops=2 * block * left_rows * width * right_rows,
    )
    d_pieces = swap_pieces(d_pieces)
    (d_left_panel,) = call(sort_d_left_kernel, "sort_d_left", [panel], d_pieces)
    (d_gate_pre,) = call(
        gate_back_kernel,
        "gate_back",
        [shape((rows, channels, width), BF16)],
        [products, gate_slope, out_gain, out_bias, w_out],
        fetched=range(2, 5),
        flops=2 * cells * channels * hidden,
    )
    slopes, normed_in, inv_in, gain_col, weights = call(
        slopes_kernel,
        "slopes",
        [
            shape((rows, 4 * hidden, width), BF16),
            shape((rows, channels, width), BF16),
            shape((rows, width), F32),
            shape((channels, channels), F32),
            shape((channels, 4 * hidden + channels), BF16),
        ],
        [pair, mask, gain, bias, w_proj, w_gate, d_gate_pre],
        fetched=range(6),
        unread=(6,),
        flops=2 * cells * channels * 4 * hidden,
    )
    (grad,) = call(
        finish_kernel,
        "finish",
        [shape(pair.shape, BF16)],
        [
            d_right_panel,
            d_left_panel,
            slopes,
            d_gate_pre,
            normed_in,
            inv_in,
            gain_col,
            weights,
        ],
        flops=2 * cells * channels * 4 * hidden,
    )
    return grad


def normalize(values, reduce_axis):
    mean_value = jnp.mean(values, axis=reduce_axis, keepdims=True)
    centered = values - mean_value
    variance = jnp.mean(centered * centered, axis=reduce_axis, keepdims=True)
    inv_std = lax.rsqrt(variance + 1e-05)
    return (centered * inv_std, inv_std)


def norm_backward(upstream, normed, inv_std, reduce_axis):
    mean_grad = jnp.mean(upstream, axis=reduce_axis, keepdims=True)
    mean_cross = jnp.mean(upstream * normed, axis=reduce_axis, keepdims=True)
    return inv_std * (upstream - mean_grad - normed * mean_cross)


def shards(
    pair,
    cotangent,
    residue_mask,
    ln_in_gain,
    ln_in_bias,
    w_proj,
    w_gate,
    ln_out_gain,
    ln_out_bias,
    w_out,
):
    local_rows = pair.shape[0]
    local_cols = pair.shape[1]
    hidden = w_out.shape[0]
    chan_index = lax.axis_index("chan")
    row_start = lax.axis_index("row") * local_rows
    col_start = chan_index * local_cols
    mask_float = residue_mask.astype(jnp.float32)
    row_mask = lax.dynamic_slice_in_dim(mask_float, row_start, local_rows)
    col_mask = lax.dynamic_slice_in_dim(mask_float, col_start, local_cols)
    cell_mask = (row_mask[:, None] * col_mask[None, :])[None]
    normed, inv_std = normalize(pair.astype(jnp.float32), -1)
    normed_pair = (normed * ln_in_gain + ln_in_bias).astype(jnp.bfloat16)
    projected = jnp.einsum("rmc,ch->hrm", normed_pair, w_proj, preferred_element_type=jnp.float32)
    left_panel = (
        cell_mask * jax.nn.sigmoid(projected[:hidden]) * projected[hidden : 2 * hidden]
    ).astype(jnp.bfloat16)
    right_panel = (
        cell_mask * jax.nn.sigmoid(projected[2 * hidden : 3 * hidden]) * projected[3 * hidden :]
    ).astype(jnp.bfloat16)
    panels = lax.all_to_all(
        jnp.stack([left_panel, right_panel]), "row", split_axis=1, concat_axis=2, tiled=True
    )
    left_all = panels[0]
    right_all = panels[1]
    right_rows = lax.all_to_all(right_all, "chan", split_axis=1, concat_axis=2, tiled=True)
    partner = right_rows
    tri_part = jnp.einsum(
        "gik,gjk->gij",
        lax.all_gather(left_all, "chan", axis=2, tiled=True),
        partner,
        preferred_element_type=jnp.float32,
    ).astype(jnp.bfloat16)
    tri_cells = lax.all_to_all(tri_part, "row", split_axis=1, concat_axis=0, tiled=True)
    tri_hat, inv_tri = normalize(tri_cells.astype(jnp.float32), 0)
    scaled = (tri_hat * ln_out_gain[:, None, None] + ln_out_bias[:, None, None]).astype(
        jnp.bfloat16
    )
    proj_out = jnp.einsum("hrm,hc->rmc", scaled, w_out, preferred_element_type=jnp.float32)
    gate_value = jax.nn.sigmoid(
        jnp.einsum("rmc,cd->rmd", normed_pair, w_gate, preferred_element_type=jnp.float32)
    )
    cot_float = cotangent.astype(jnp.float32)
    d_gate_pre = (cot_float * proj_out * gate_value * (1.0 - gate_value)).astype(jnp.bfloat16)
    d_scaled = (cot_float * gate_value).astype(jnp.bfloat16)
    d_hat = jnp.einsum("rmc,hc->hrm", d_scaled, w_out, preferred_element_type=jnp.float32)
    d_hat = d_hat * ln_out_gain[:, None, None]
    d_tri = norm_backward(d_hat, tri_hat, inv_tri, 0).astype(jnp.bfloat16)
    d_tri_all = lax.all_to_all(d_tri, "row", split_axis=0, concat_axis=1, tiled=True)
    panel_piece = lax.all_gather(d_tri_all, "chan", axis=2, tiled=True)
    partner = right_all
    d_left = jnp.einsum("gij,gjk->gik", panel_piece, partner, preferred_element_type=jnp.float32)
    contribution = jnp.einsum(
        "gij,gik->gjk", panel_piece, left_all, preferred_element_type=jnp.float32
    )
    d_right = contribution
    d_left, d_right = (d_left, d_right)
    d_stack = jnp.stack([d_left, d_right]).astype(jnp.bfloat16)
    d_panels = lax.all_to_all(d_stack, "row", split_axis=2, concat_axis=1, tiled=True)

    def gating(d_value, gate_proj, value_proj):
        sigmoid_val = jax.nn.sigmoid(gate_proj)
        masked_grad = d_value.astype(jnp.float32) * cell_mask
        return (
            masked_grad * value_proj * sigmoid_val * (1.0 - sigmoid_val),
            masked_grad * sigmoid_val,
        )

    gate_left, value_left = gating(d_panels[0], projected[:hidden], projected[hidden : 2 * hidden])
    gate_right, value_right = gating(
        d_panels[1], projected[2 * hidden : 3 * hidden], projected[3 * hidden :]
    )
    d_proj = jnp.concatenate([gate_left, value_left, gate_right, value_right], axis=0).astype(
        jnp.bfloat16
    )
    d_normed = jnp.einsum("hrm,ch->rmc", d_proj, w_proj, preferred_element_type=jnp.float32)
    d_normed = d_normed + jnp.einsum(
        "rmd,cd->rmc", d_gate_pre, w_gate, preferred_element_type=jnp.float32
    )
    d_input = d_normed * ln_in_gain
    return norm_backward(d_input, normed, inv_std, -1).astype(jnp.bfloat16)


def solution(mesh):
    fits = mesh.shape["chan"] == 1 and mesh.shape["row"] in (8, 16)
    return jax.shard_map(
        kernel_shards if fits else shards,
        mesh=mesh,
        in_specs=(
            P(("grp", "row"), "chan", None),
            P(("grp", "row"), "chan", None),
            P("grp"),
            P(),
            P(),
            P(),
            P(),
            P(),
            P(),
            P(),
        ),
        out_specs=P(("grp", "row"), "chan", None),
        check_vma=False,
    )
```

```python
import functools

import jax
import jax.numpy as jnp
from jax import lax
from jax.experimental import pallas as pl
from jax.experimental.pallas import tpu as pltpu
from jax.sharding import PartitionSpec as P

F32 = jnp.float32
BF16 = jnp.bfloat16
VMEM_LIMIT = 16 * 1024 * 1024


def dot(lhs, rhs, lhs_dim, rhs_dim):
    return lax.dot_general(
        lhs, rhs, (((lhs_dim,), (rhs_dim,)), ((), ())), preferred_element_type=F32
    )


def transposed(matrix):
    return jnp.transpose(matrix.astype(F32)).astype(BF16)


def sigmoid(values):
    return 1.0 / (1.0 + jnp.exp(-values))


def column(row):
    size = row.shape[1]
    return jnp.transpose(jnp.broadcast_to(row, (size, size)))


def norm_rows(values):
    centered = values - jnp.mean(values, axis=0, keepdims=True)
    variance = jnp.mean(centered * centered, axis=0, keepdims=True)
    inv_std = lax.rsqrt(variance + 1e-05)
    return centered * inv_std, inv_std


def call(
    kernel, name, outs, args, fetched=(), unread=(), scratch=(), flops=0, limit=VMEM_LIMIT
):
    moved = sum(a.size * a.dtype.itemsize for a in args) + sum(
        o.size * jnp.dtype(o.dtype).itemsize for o in outs
    )
    n_args, n_outs, n_fetched = len(args), len(outs), len(fetched)

    def body(*refs):
        ins = list(refs[:n_args])
        rest = refs[n_args + n_outs :]
        copies = []
        for n, place in enumerate(fetched):
            copies.append(pltpu.make_async_copy(ins[place], rest[n], rest[n_fetched].at[n]))
            ins[place] = rest[n]
        for copy in copies:
            copy.start()
        for copy in copies:
            copy.wait()
        kernel(*ins, *refs[n_args : n_args + n_outs], *rest[n_fetched + (n_fetched > 0) :])

    buffers = [pltpu.VMEM(args[place].shape, args[place].dtype) for place in fetched]
    if fetched:
        buffers.append(pltpu.SemaphoreType.DMA((n_fetched,)))
    return pl.pallas_call(
        body,
        name=name,
        out_shape=outs,
        in_specs=[
            pl.BlockSpec(
                memory_space=pltpu.HBM if n in fetched else pl.ANY if n in unread else pltpu.VMEM
            )
            for n in range(n_args)
        ],
        out_specs=[pl.BlockSpec(memory_space=pltpu.VMEM) for _ in outs],
        scratch_shapes=buffers + list(scratch),
        compiler_params=pltpu.CompilerParams(vmem_limit_bytes=limit),
        cost_estimate=pl.CostEstimate(flops=flops, bytes_accessed=moved, transcendentals=0),
    )(*args)


def cell_masks(mask, rows):
    columns = mask[...].astype(F32)
    shape = (rows, columns.shape[1])
    first = lax.axis_index("row") * rows
    own = lax.broadcasted_iota(jnp.int32, shape, 1) == (
        lax.broadcasted_iota(jnp.int32, shape, 0) + first
    )
    row_mask = jnp.sum(jnp.where(own, columns, 0.0), axis=1, keepdims=True)
    cells = row_mask * columns
    return [cells[row : row + 1] for row in range(rows)]


def wide_order(devices, count):
    order = []
    for place in range(count):
        order += [count + (place ^ 2), place ^ (count // 2)]
    return order


def distance(step, count):
    far = sorted(range(3, count), key=lambda apart: -(apart // 2))
    return [*range(min(3, count)), *far][step]


def partner(step, count):
    return lax.rem(lax.axis_index("row"), count) ^ distance(step, count)


def gated_rows(pair, mask, gain, bias, w_proj, side):
    rows = pair.shape[0]
    hidden = w_proj.shape[1] // 4
    w_flip = transposed(w_proj[:, 2 * side * hidden : 2 * (side + 1) * hidden])
    gain_col, bias_col = column(gain[...]), column(bias[...])
    masks = cell_masks(mask, rows)
    for row in range(rows):
        normed, _ = norm_rows(jnp.transpose(pair[row].astype(F32)))
        zln = (normed * gain_col + bias_col).astype(BF16)
        proj = dot(w_flip, zln, 1, 0)
        yield row, masks[row] * sigmoid(proj[:hidden]) * proj[hidden:]


def project_right_kernel(pair, mask, gain, bias, w_proj, right_panel):
    rows = pair.shape[0]
    devices, depth, width = right_panel.shape
    block = depth // rows
    count = w_proj.shape[1] // 4 // block
    for row, right in gated_rows(pair, mask, gain, bias, w_proj, 1):
        right = right.reshape(count, block, width).astype(BF16)
        for rank in range(devices):
            place = wide_order(devices, count)[rank] % count
            right_panel[rank, row * block : (row + 1) * block, :] = right[place]


def project_left_kernel(pair, mask, gain, bias, w_proj, after, *refs):
    del after
    *pieces, left_panel = refs
    rows = pair.shape[0]
    count, depth, width = left_panel.shape
    block = depth // rows
    for row, left in gated_rows(pair, mask, gain, bias, w_proj, 0):
        left = left.reshape(count, block, width).astype(BF16)
        left_panel[:, row * block : (row + 1) * block, :] = left
    for step, piece in enumerate(pieces):
        piece[...] = left_panel[partner(step, count)]


def prepare_kernel(
    pair, cotangent, gain, bias, w_gate, out_gain, w_out, d_hat_centered, gate_slope
):
    gate_flip = transposed(w_gate[...])
    gain_col, bias_col = column(gain[...]), column(bias[...])
    out_gain_col = column(out_gain[...])
    for row in range(pair.shape[0]):
        normed, _ = norm_rows(jnp.transpose(pair[row].astype(F32)))
        zln = (normed * gain_col + bias_col).astype(BF16)
        gate = sigmoid(dot(gate_flip, zln, 1, 0))
        cot = jnp.transpose(cotangent[row].astype(F32))
        d_scaled = (cot * gate).astype(BF16)
        d_hat = dot(w_out[...], d_scaled, 1, 0) * out_gain_col
        d_hat_centered[row] = d_hat - jnp.mean(d_hat, axis=0, keepdims=True)
        gate_slope[row] = cot * gate * (1.0 - gate)


def spread(panel, wide):
    wide[...] = panel[...].astype(F32).reshape(wide.shape)


def wide_places(panel, count):
    devices, depth, _ = panel.shape
    for rank, device in enumerate(wide_order(devices, count)):
        yield rank, slice(device * depth, (device + 1) * depth)


def sort_left_kernel(*refs):
    *pieces, left_all, left_wide = refs
    block, left_rows, _ = left_all.shape
    depth = pieces[0].shape[0]
    for step, piece in enumerate(pieces):
        start = pl.multiple_of(partner(step, len(pieces)) * depth, depth)
        left_wide[pl.ds(start, depth), :] = piece[...].astype(F32)
    for h in range(block):
        left_all[h] = left_wide[pl.ds(h, left_rows, stride=block), :].astype(BF16)


def tri_kernel(right_panel, left_all, after, products, right_all, left_wide, right_wide):
    del after
    block, left_rows, _ = left_all.shape
    right_rows = right_all.shape[1]
    for rank, place in wide_places(right_panel, products.shape[0]):
        right_wide[place, :] = right_panel[rank].astype(F32)
    for h in range(block):
        right = right_wide[pl.ds(h, right_rows, stride=block), :].astype(BF16)
        right_all[h] = right
        left_wide[pl.ds(h, left_rows, stride=block), :] = dot(left_all[h], right, 1, 1)
    products[...] = left_wide[...].astype(BF16).reshape(products.shape)


def cell_row(ref, row, rows):
    count, depth, width = ref.shape
    block = depth // rows
    return ref[:, row * block : (row + 1) * block, :].astype(F32).reshape(count * block, width)


def middle_kernel(products, d_hat_centered, d_products):
    rows = d_hat_centered.shape[0]
    count, depth, width = products.shape
    block = depth // rows
    for row in range(rows):
        tri_hat, inv_std = norm_rows(cell_row(products, row, rows))
        d_hat = d_hat_centered[row]
        cross = jnp.mean(d_hat * tri_hat, axis=0, keepdims=True)
        d_tri = inv_std * (d_hat - tri_hat * cross)
        d_products[:, row * block : (row + 1) * block, :] = d_tri.reshape(
            count, block, width
        ).astype(BF16)


def d_right_kernel(d_products, left_all, d_right_panel, d_tri_all, left_wide, right_wide):
    block, left_rows, _ = left_all.shape
    right_rows = right_wide.shape[0] // block
    spread(d_products, left_wide)
    for h in range(block):
        d_tri = left_wide[pl.ds(h, left_rows, stride=block), :].astype(BF16)
        d_tri_all[h] = d_tri
        right_wide[pl.ds(h, right_rows, stride=block), :] = dot(d_tri, left_all[h], 0, 0)
    for rank, place in wide_places(d_right_panel, d_products.shape[0]):
        d_right_panel[rank] = right_wide[place, :].astype(BF16)


def d_left_kernel(d_tri_all, right_all, *refs):
    *pieces, left_wide = refs
    block, left_rows, _ = d_tri_all.shape
    for h in range(block):
        left_wide[pl.ds(h, left_rows, stride=block), :] = dot(d_tri_all[h], right_all[h], 1, 0)
    depth = pieces[0].shape[0]
    for step, piece in enumerate(pieces):
        start = pl.multiple_of(partner(step, len(pieces)) * depth, depth)
        piece[...] = left_wide[pl.ds(start, depth), :].astype(BF16)


def gate_back_kernel(products, gate_slope, out_gain, out_bias, w_out, d_gate_pre):
    rows = gate_slope.shape[0]
    out_flip = transposed(w_out[...])
    out_gain_col, out_bias_col = column(out_gain[...]), column(out_bias[...])
    for row in range(rows):
        tri_hat, _ = norm_rows(cell_row(products, row, rows))
        scaled = (tri_hat * out_gain_col + out_bias_col).astype(BF16)
        d_gate_pre[row] = (dot(out_flip, scaled, 1, 0) * gate_slope[row]).astype(BF16)


def slopes_kernel(
    pair, mask, gain, bias, w_proj, w_gate, after, slopes, normed_in, inv_in, in_gain, weights
):
    del after
    rows = pair.shape[0]
    hidden = w_proj.shape[1] // 4
    w_flip = transposed(w_proj[...])
    gain_col, bias_col = column(gain[...]), column(bias[...])
    in_gain[...] = gain_col
    weights[...] = jnp.concatenate([w_proj[...], w_gate[...]], axis=1)
    masks = cell_masks(mask, rows)
    for row in range(rows):
        normed, inv_std = norm_rows(jnp.transpose(pair[row].astype(F32)))
        normed_in[row] = normed.astype(normed_in.dtype)
        inv_in[row : row + 1] = inv_std
        zln = (normed * gain_col + bias_col).astype(BF16)
        proj = dot(w_flip, zln, 1, 0)
        for side in range(2):
            base = 2 * side * hidden
            sig = sigmoid(proj[base : base + hidden])
            masked = masks[row] * sig
            value = masked * (1.0 - sig) * proj[base + hidden : base + 2 * hidden]
            slopes[row, base : base + hidden, :] = value.astype(slopes.dtype)
            slopes[row, base + hidden : base + 2 * hidden, :] = masked.astype(slopes.dtype)


def sort_d_left_kernel(*refs):
    *pieces, d_left_panel = refs
    for step, piece in enumerate(pieces):
        d_left_panel[partner(step, len(pieces))] = piece[...]


def both_halves(blocks, count):
    order = wide_order(2 * count, count)
    return jnp.stack(
        [blocks[order.index(place)] + blocks[order.index(count + place)] for place in range(count)]
    )


def finish_kernel(
    d_right_panel, d_left_panel, slopes, d_gate_pre, normed_in, inv_in, gain_col, weights, grad
):
    rows = grad.shape[0]
    count, depth, width = d_left_panel.shape
    hidden = count * depth // rows
    for row in range(rows):
        d_right = cell_row(d_right_panel, row, rows)
        d_right = both_halves(d_right.reshape(2 * count, depth // rows, width), count)
        parts = []
        for side, d_value in enumerate((cell_row(d_left_panel, row, rows), d_right.reshape(hidden, width))):
            for base in (2 * side * hidden, (2 * side + 1) * hidden):
                slope = slopes[row, base : base + hidden, :].astype(F32)
                parts.append((d_value * slope).astype(BF16))
        parts.append(d_gate_pre[row])
        d_in = dot(weights[...], jnp.concatenate(parts, axis=0), 1, 0) * gain_col[...]
        normed = normed_in[row].astype(F32)
        mean_grad = jnp.mean(d_in, axis=0, keepdims=True)
        mean_cross = jnp.mean(d_in * normed, axis=0, keepdims=True)
        result = inv_in[row : row + 1] * (d_in - mean_grad - normed * mean_cross)
        grad[row] = jnp.transpose(result).astype(BF16)


def swap(values, count):
    groups = [wide_order(lax.axis_size("row"), count)]
    return lax.all_to_all(
        values, "row", split_axis=0, concat_axis=0, tiled=True, axis_index_groups=groups
    )


def swap_half(values, count):
    devices = range(lax.axis_size("row"))
    groups = [[d for d in devices if d // count == half] for half in range(len(devices) // count)]
    return lax.all_to_all(
        values, "row", split_axis=0, concat_axis=0, tiled=True, axis_index_groups=groups
    )


def swap_pieces(pieces):
    devices = range(lax.axis_size("row"))
    count = len(pieces)
    return [pieces[0]] + [
        lax.ppermute(pieces[step], "row", [(d, d ^ distance(step, count)) for d in devices])
        for step in range(1, count)
    ]


def kernel_shards(
    pair,
    cotangent,
    residue_mask,
    ln_in_gain,
    ln_in_bias,
    w_proj,
    w_gate,
    ln_out_gain,
    ln_out_bias,
    w_out,
):
    rows, width, channels = pair.shape
    hidden = w_out.shape[0]
    halves = 2
    devices = lax.axis_size("row")
    count = devices // halves
    block = hidden // count
    left_rows, right_rows = rows * count, rows * devices
    shape = jax.ShapeDtypeStruct
    panel = shape((count, rows * block, width), BF16)
    wide_panel = shape((devices, rows * block, width), BF16)
    mask = residue_mask.reshape(1, width)
    gain, bias = ln_in_gain.reshape(1, channels), ln_in_bias.reshape(1, channels)
    out_gain, out_bias = ln_out_gain.reshape(1, hidden), ln_out_bias.reshape(1, hidden)
    cells = rows * width
    piece = shape((rows * block, width), BF16)
    left_panel = pltpu.VMEM(panel.shape, BF16)
    left_wide = pltpu.VMEM((left_rows * block, width), F32)
    right_wide = pltpu.VMEM((right_rows * block, width), F32)
    (own_right,) = call(
        project_right_kernel,
        "project_right",
        [wide_panel],
        [pair, mask, gain, bias, w_proj],
        fetched=range(5),
        flops=2 * cells * channels * 2 * hidden,
        limit=64 * 1024 * 1024 - 640 * 1024,
    )
    right_panel = swap(own_right, count)
    pieces = call(
        project_left_kernel,
        "project_left",
        [piece] * count,
        [pair, mask, gain, bias, w_proj, own_right],
        fetched=range(5),
        unread=(5,),
        scratch=[left_panel],
        flops=2 * cells * channels * 2 * hidden,
    )
    pieces = swap_pieces(pieces)
    (left_all,) = call(
        sort_left_kernel,
        "sort_left",
        [shape((block, left_rows, width), BF16)],
        pieces,
        scratch=[left_wide],
    )
    d_hat_centered, gate_slope = call(
        prepare_kernel,
        "prepare",
        [shape((rows, hidden, width), F32), shape((rows, channels, width), F32)],
        [pair, cotangent, gain, bias, w_gate, out_gain, w_out],
        fetched=range(7),
        flops=2 * cells * channels * 2 * hidden,
    )
    products, right_all = call(
        tri_kernel,
        "tri",
        [panel, shape((block, right_rows, width), BF16)],
        [right_panel, left_all, d_hat_centered],
        unread=(2,),
        scratch=[left_wide, right_wide],
        flops=2 * block * left_rows * width * right_rows,
    )
    products = swap_half(products, count)
    (d_products,) = call(
        middle_kernel,
        "middle",
        [panel],
        [products, d_hat_centered],
        flops=20 * cells * hidden,
    )
    d_products = swap_half(d_products, count)
    d_right_panel, d_tri_all = call(
        d_right_kernel,
        "d_right",
        [wide_panel, shape((block, left_rows, width), BF16)],
        [d_products, left_all],
        scratch=[left_wide, right_wide],
        flops=2 * block * left_rows * width * right_rows,
    )
    d_right_panel = swap(d_right_panel, count)
    d_pieces = call(
        d_left_kernel,
        "d_left",
        [piece] * count,
        [d_tri_all, right_all],
        scratch=[left_wide],
        flops=2 * block * left_rows * width * right_rows,
    )
    d_pieces = swap_pieces(d_pieces)
    (d_left_panel,) = call(sort_d_left_kernel, "sort_d_left", [panel], d_pieces)
    (d_gate_pre,) = call(
        gate_back_kernel,
        "gate_back",
        [shape((rows, channels, width), BF16)],
        [products, gate_slope, out_gain, out_bias, w_out],
        fetched=range(2, 5),
        flops=2 * cells * channels * hidden,
    )
    slopes, normed_in, inv_in, gain_col, weights = call(
        slopes_kernel,
        "slopes",
        [
            shape((rows, 4 * hidden, width), BF16),
            shape((rows, channels, width), BF16),
            shape((rows, width), F32),
            shape((channels, channels), F32),
            shape((channels, 4 * hidden + channels), BF16),
        ],
        [pair, mask, gain, bias, w_proj, w_gate, d_gate_pre],
        fetched=range(6),
        unread=(6,),
        flops=2 * cells * channels * 4 * hidden,
    )
    (grad,) = call(
        finish_kernel,
        "finish",
        [shape(pair.shape, BF16)],
        [
            d_right_panel,
            d_left_panel,
            slopes,
            d_gate_pre,
            normed_in,
            inv_in,
            gain_col,
            weights,
        ],
        flops=2 * cells * channels * 4 * hidden,
    )
    return grad


def normalize(values, reduce_axis):
    mean_value = jnp.mean(values, axis=reduce_axis, keepdims=True)
    centered = values - mean_value
    variance = jnp.mean(centered * centered, axis=reduce_axis, keepdims=True)
    inv_std = lax.rsqrt(variance + 1e-05)
    return (centered * inv_std, inv_std)


def norm_backward(upstream, normed, inv_std, reduce_axis):
    mean_grad = jnp.mean(upstream, axis=reduce_axis, keepdims=True)
    mean_cross = jnp.mean(upstream * normed, axis=reduce_axis, keepdims=True)
    return inv_std * (upstream - mean_grad - normed * mean_cross)


def shards(
    pair,
    cotangent,
    residue_mask,
    ln_in_gain,
    ln_in_bias,
    w_proj,
    w_gate,
    ln_out_gain,
    ln_out_bias,
    w_out,
):
    local_rows = pair.shape[0]
    local_cols = pair.shape[1]
    hidden = w_out.shape[0]
    chan_index = lax.axis_index("chan")
    row_start = lax.axis_index("row") * local_rows
    col_start = chan_index * local_cols
    mask_float = residue_mask.astype(jnp.float32)
    row_mask = lax.dynamic_slice_in_dim(mask_float, row_start, local_rows)
    col_mask = lax.dynamic_slice_in_dim(mask_float, col_start, local_cols)
    cell_mask = (row_mask[:, None] * col_mask[None, :])[None]
    normed, inv_std = normalize(pair.astype(jnp.float32), -1)
    normed_pair = (normed * ln_in_gain + ln_in_bias).astype(jnp.bfloat16)
    projected = jnp.einsum("rmc,ch->hrm", normed_pair, w_proj, preferred_element_type=jnp.float32)
    left_panel = (
        cell_mask * jax.nn.sigmoid(projected[:hidden]) * projected[hidden : 2 * hidden]
    ).astype(jnp.bfloat16)
    right_panel = (
        cell_mask * jax.nn.sigmoid(projected[2 * hidden : 3 * hidden]) * projected[3 * hidden :]
    ).astype(jnp.bfloat16)
    panels = lax.all_to_all(
        jnp.stack([left_panel, right_panel]), "row", split_axis=1, concat_axis=2, tiled=True
    )
    left_all = panels[0]
    right_all = panels[1]
    right_rows = lax.all_to_all(right_all, "chan", split_axis=1, concat_axis=2, tiled=True)
    partner = right_rows
    tri_part = jnp.einsum(
        "gik,gjk->gij",
        lax.all_gather(left_all, "chan", axis=2, tiled=True),
        partner,
        preferred_element_type=jnp.float32,
    ).astype(jnp.bfloat16)
    tri_cells = lax.all_to_all(tri_part, "row", split_axis=1, concat_axis=0, tiled=True)
    tri_hat, inv_tri = normalize(tri_cells.astype(jnp.float32), 0)
    scaled = (tri_hat * ln_out_gain[:, None, None] + ln_out_bias[:, None, None]).astype(
        jnp.bfloat16
    )
    proj_out = jnp.einsum("hrm,hc->rmc", scaled, w_out, preferred_element_type=jnp.float32)
    gate_value = jax.nn.sigmoid(
        jnp.einsum("rmc,cd->rmd", normed_pair, w_gate, preferred_element_type=jnp.float32)
    )
    cot_float = cotangent.astype(jnp.float32)
    d_gate_pre = (cot_float * proj_out * gate_value * (1.0 - gate_value)).astype(jnp.bfloat16)
    d_scaled = (cot_float * gate_value).astype(jnp.bfloat16)
    d_hat = jnp.einsum("rmc,hc->hrm", d_scaled, w_out, preferred_element_type=jnp.float32)
    d_hat = d_hat * ln_out_gain[:, None, None]
    d_tri = norm_backward(d_hat, tri_hat, inv_tri, 0).astype(jnp.bfloat16)
    d_tri_all = lax.all_to_all(d_tri, "row", split_axis=0, concat_axis=1, tiled=True)
    panel_piece = lax.all_gather(d_tri_all, "chan", axis=2, tiled=True)
    partner = right_all
    d_left = jnp.einsum("gij,gjk->gik", panel_piece, partner, preferred_element_type=jnp.float32)
    contribution = jnp.einsum(
        "gij,gik->gjk", panel_piece, left_all, preferred_element_type=jnp.float32
    )
    d_right = contribution
    d_left, d_right = (d_left, d_right)
    d_stack = jnp.stack([d_left, d_right]).astype(jnp.bfloat16)
    d_panels = lax.all_to_all(d_stack, "row", split_axis=2, concat_axis=1, tiled=True)

    def gating(d_value, gate_proj, value_proj):
        sigmoid_val = jax.nn.sigmoid(gate_proj)
        masked_grad = d_value.astype(jnp.float32) * cell_mask
        return (
            masked_grad * value_proj * sigmoid_val * (1.0 - sigmoid_val),
            masked_grad * sigmoid_val,
        )

    gate_left, value_left = gating(d_panels[0], projected[:hidden], projected[hidden : 2 * hidden])
    gate_right, value_right = gating(
        d_panels[1], projected[2 * hidden : 3 * hidden], projected[3 * hidden :]
    )
    d_proj = jnp.concatenate([gate_left, value_left, gate_right, value_right], axis=0).astype(
        jnp.bfloat16
    )
    d_normed = jnp.einsum("hrm,ch->rmc", d_proj, w_proj, preferred_element_type=jnp.float32)
    d_normed = d_normed + jnp.einsum(
        "rmd,cd->rmc", d_gate_pre, w_gate, preferred_element_type=jnp.float32
    )
    d_input = d_normed * ln_in_gain
    return norm_backward(d_input, normed, inv_std, -1).astype(jnp.bfloat16)


def solution(mesh):
    fits = mesh.shape["chan"] == 1 and mesh.shape["row"] in (8, 16)
    return jax.shard_map(
        kernel_shards if fits else shards,
        mesh=mesh,
        in_specs=(
            P(("grp", "row"), "chan", None),
            P(("grp", "row"), "chan", None),
            P("grp"),
            P(),
            P(),
            P(),
            P(),
            P(),
            P(),
            P(),
        ),
        out_specs=P(("grp", "row"), "chan", None),
        check_vma=False,
    )
```

```python
import functools

import jax
import jax.numpy as jnp
from jax import lax
from jax.experimental import pallas as pl
from jax.experimental.pallas import tpu as pltpu
from jax.sharding import PartitionSpec as P

F32 = jnp.float32
BF16 = jnp.bfloat16
VMEM_LIMIT = 16 * 1024 * 1024


def dot(lhs, rhs, lhs_dim, rhs_dim):
    return lax.dot_general(
        lhs, rhs, (((lhs_dim,), (rhs_dim,)), ((), ())), preferred_element_type=F32
    )


def transposed(matrix):
    return jnp.transpose(matrix.astype(F32)).astype(BF16)


def sigmoid(values):
    return 1.0 / (1.0 + jnp.exp(-values))


def column(row):
    size = row.shape[1]
    return jnp.transpose(jnp.broadcast_to(row, (size, size)))


def norm_rows(values):
    centered = values - jnp.mean(values, axis=0, keepdims=True)
    variance = jnp.mean(centered * centered, axis=0, keepdims=True)
    inv_std = lax.rsqrt(variance + 1e-05)
    return centered * inv_std, inv_std


def call(
    kernel, name, outs, args, fetched=(), unread=(), scratch=(), flops=0, limit=VMEM_LIMIT
):
    moved = sum(a.size * a.dtype.itemsize for a in args) + sum(
        o.size * jnp.dtype(o.dtype).itemsize for o in outs
    )
    n_args, n_outs, n_fetched = len(args), len(outs), len(fetched)

    def body(*refs):
        ins = list(refs[:n_args])
        rest = refs[n_args + n_outs :]
        copies = []
        for n, place in enumerate(fetched):
            copies.append(pltpu.make_async_copy(ins[place], rest[n], rest[n_fetched].at[n]))
            ins[place] = rest[n]
        for copy in copies:
            copy.start()
        for copy in copies:
            copy.wait()
        kernel(*ins, *refs[n_args : n_args + n_outs], *rest[n_fetched + (n_fetched > 0) :])

    buffers = [pltpu.VMEM(args[place].shape, args[place].dtype) for place in fetched]
    if fetched:
        buffers.append(pltpu.SemaphoreType.DMA((n_fetched,)))
    return pl.pallas_call(
        body,
        name=name,
        out_shape=outs,
        in_specs=[
            pl.BlockSpec(
                memory_space=pltpu.HBM if n in fetched else pl.ANY if n in unread else pltpu.VMEM
            )
            for n in range(n_args)
        ],
        out_specs=[pl.BlockSpec(memory_space=pltpu.VMEM) for _ in outs],
        scratch_shapes=buffers + list(scratch),
        compiler_params=pltpu.CompilerParams(vmem_limit_bytes=limit),
        cost_estimate=pl.CostEstimate(flops=flops, bytes_accessed=moved, transcendentals=0),
    )(*args)


def cell_masks(mask, rows):
    columns = mask[...].astype(F32)
    shape = (rows, columns.shape[1])
    first = lax.axis_index("row") * rows
    own = lax.broadcasted_iota(jnp.int32, shape, 1) == (
        lax.broadcasted_iota(jnp.int32, shape, 0) + first
    )
    row_mask = jnp.sum(jnp.where(own, columns, 0.0), axis=1, keepdims=True)
    cells = row_mask * columns
    return [cells[row : row + 1] for row in range(rows)]


def wide_order(devices, count, back):
    order = []
    for place in range(count):
        if back:
            order += [place ^ (count // 2), count + place]
        else:
            order += [count + (place ^ 2), place ^ (count // 2)]
    return order


def distance(step, count):
    far = sorted(range(3, count), key=lambda apart: -(apart // 2))
    return [*range(min(3, count)), *far][step]


def partner(step, count):
    return lax.rem(lax.axis_index("row"), count) ^ distance(step, count)


def gated_rows(pair, mask, gain, bias, w_proj, side):
    rows = pair.shape[0]
    hidden = w_proj.shape[1] // 4
    w_flip = transposed(w_proj[:, 2 * side * hidden : 2 * (side + 1) * hidden])
    gain_col, bias_col = column(gain[...]), column(bias[...])
    masks = cell_masks(mask, rows)
    for row in range(rows):
        normed, _ = norm_rows(jnp.transpose(pair[row].astype(F32)))
        zln = (normed * gain_col + bias_col).astype(BF16)
        proj = dot(w_flip, zln, 1, 0)
        yield row, masks[row] * sigmoid(proj[:hidden]) * proj[hidden:]


def project_right_kernel(pair, mask, gain, bias, w_proj, right_panel):
    rows = pair.shape[0]
    devices, depth, width = right_panel.shape
    block = depth // rows
    count = w_proj.shape[1] // 4 // block
    for row, right in gated_rows(pair, mask, gain, bias, w_proj, 1):
        right = right.reshape(count, block, width).astype(BF16)
        for rank in range(devices):
            place = wide_order(devices, count, False)[rank] % count
            right_panel[rank, row * block : (row + 1) * block, :] = right[place]


def project_left_kernel(pair, mask, gain, bias, w_proj, after, *refs):
    del after
    *pieces, left_panel = refs
    rows = pair.shape[0]
    count, depth, width = left_panel.shape
    block = depth // rows
    for row, left in gated_rows(pair, mask, gain, bias, w_proj, 0):
        left = left.reshape(count, block, width).astype(BF16)
        left_panel[:, row * block : (row + 1) * block, :] = left
    for step, piece in enumerate(pieces):
        piece[...] = left_panel[partner(step, count)]


def prepare_kernel(
    pair, cotangent, gain, bias, w_gate, out_gain, w_out, d_hat_centered, gate_slope
):
    gate_flip = transposed(w_gate[...])
    gain_col, bias_col = column(gain[...]), column(bias[...])
    out_gain_col = column(out_gain[...])
    for row in range(pair.shape[0]):
        normed, _ = norm_rows(jnp.transpose(pair[row].astype(F32)))
        zln = (normed * gain_col + bias_col).astype(BF16)
        gate = sigmoid(dot(gate_flip, zln, 1, 0))
        cot = jnp.transpose(cotangent[row].astype(F32))
        d_scaled = (cot * gate).astype(BF16)
        d_hat = dot(w_out[...], d_scaled, 1, 0) * out_gain_col
        d_hat_centered[row] = d_hat - jnp.mean(d_hat, axis=0, keepdims=True)
        gate_slope[row] = cot * gate * (1.0 - gate)


def spread(panel, wide):
    wide[...] = panel[...].astype(F32).reshape(wide.shape)


def wide_places(panel, count, back):
    devices, depth, _ = panel.shape
    for rank, device in enumerate(wide_order(devices, count, back)):
        yield rank, slice(device * depth, (device + 1) * depth)


def sort_left_kernel(*refs):
    *pieces, left_all, left_wide = refs
    block, left_rows, _ = left_all.shape
    depth = pieces[0].shape[0]
    for step, piece in enumerate(pieces):
        start = pl.multiple_of(partner(step, len(pieces)) * depth, depth)
        left_wide[pl.ds(start, depth), :] = piece[...].astype(F32)
    for h in range(block):
        left_all[h] = left_wide[pl.ds(h, left_rows, stride=block), :].astype(BF16)


def tri_kernel(right_panel, left_all, after, products, right_all, left_wide, right_wide):
    del after
    block, left_rows, _ = left_all.shape
    right_rows = right_all.shape[1]
    for rank, place in wide_places(right_panel, products.shape[0], False):
        right_wide[place, :] = right_panel[rank].astype(F32)
    for h in range(block):
        right = right_wide[pl.ds(h, right_rows, stride=block), :].astype(BF16)
        right_all[h] = right
        left_wide[pl.ds(h, left_rows, stride=block), :] = dot(left_all[h], right, 1, 1)
    products[...] = left_wide[...].astype(BF16).reshape(products.shape)


def cell_row(ref, row, rows):
    count, depth, width = ref.shape
    block = depth // rows
    return ref[:, row * block : (row + 1) * block, :].astype(F32).reshape(count * block, width)


def middle_kernel(products, d_hat_centered, d_products):
    rows = d_hat_centered.shape[0]
    count, depth, width = products.shape
    block = depth // rows
    for row in range(rows):
        tri_hat, inv_std = norm_rows(cell_row(products, row, rows))
        d_hat = d_hat_centered[row]
        cross = jnp.mean(d_hat * tri_hat, axis=0, keepdims=True)
        d_tri = inv_std * (d_hat - tri_hat * cross)
        d_products[:, row * block : (row + 1) * block, :] = d_tri.reshape(
            count, block, width
        ).astype(BF16)


def d_right_kernel(d_products, left_all, d_right_panel, d_tri_all, left_wide, right_wide):
    block, left_rows, _ = left_all.shape
    right_rows = right_wide.shape[0] // block
    spread(d_products, left_wide)
    for h in range(block):
        d_tri = left_wide[pl.ds(h, left_rows, stride=block), :].astype(BF16)
        d_tri_all[h] = d_tri
        right_wide[pl.ds(h, right_rows, stride=block), :] = dot(d_tri, left_all[h], 0, 0)
    for rank, place in wide_places(d_right_panel, d_products.shape[0], True):
        d_right_panel[rank] = right_wide[place, :].astype(BF16)


def d_left_kernel(d_tri_all, right_all, *refs):
    *pieces, left_wide = refs
    block, left_rows, _ = d_tri_all.shape
    for h in range(block):
        left_wide[pl.ds(h, left_rows, stride=block), :] = dot(d_tri_all[h], right_all[h], 1, 0)
    depth = pieces[0].shape[0]
    for step, piece in enumerate(pieces):
        start = pl.multiple_of(partner(step, len(pieces)) * depth, depth)
        piece[...] = left_wide[pl.ds(start, depth), :].astype(BF16)


def gate_back_kernel(products, gate_slope, out_gain, out_bias, w_out, d_gate_pre):
    rows = gate_slope.shape[0]
    out_flip = transposed(w_out[...])
    out_gain_col, out_bias_col = column(out_gain[...]), column(out_bias[...])
    for row in range(rows):
        tri_hat, _ = norm_rows(cell_row(products, row, rows))
        scaled = (tri_hat * out_gain_col + out_bias_col).astype(BF16)
        d_gate_pre[row] = (dot(out_flip, scaled, 1, 0) * gate_slope[row]).astype(BF16)


def slopes_kernel(
    pair, mask, gain, bias, w_proj, w_gate, after, slopes, normed_in, inv_in, in_gain, weights
):
    del after
    rows = pair.shape[0]
    hidden = w_proj.shape[1] // 4
    w_flip = transposed(w_proj[...])
    gain_col, bias_col = column(gain[...]), column(bias[...])
    in_gain[...] = gain_col
    weights[...] = jnp.concatenate([w_proj[...], w_gate[...]], axis=1)
    masks = cell_masks(mask, rows)
    for row in range(rows):
        normed, inv_std = norm_rows(jnp.transpose(pair[row].astype(F32)))
        normed_in[row] = normed.astype(normed_in.dtype)
        inv_in[row : row + 1] = inv_std
        zln = (normed * gain_col + bias_col).astype(BF16)
        proj = dot(w_flip, zln, 1, 0)
        for side in range(2):
            base = 2 * side * hidden
            sig = sigmoid(proj[base : base + hidden])
            masked = masks[row] * sig
            value = masked * (1.0 - sig) * proj[base + hidden : base + 2 * hidden]
            slopes[row, base : base + hidden, :] = value.astype(slopes.dtype)
            slopes[row, base + hidden : base + 2 * hidden, :] = masked.astype(slopes.dtype)


def sort_d_left_kernel(*refs):
    *pieces, d_left_panel = refs
    for step, piece in enumerate(pieces):
        d_left_panel[partner(step, len(pieces))] = piece[...]


def both_halves(blocks, count):
    order = wide_order(2 * count, count, True)
    return jnp.stack(
        [blocks[order.index(place)] + blocks[order.index(count + place)] for place in range(count)]
    )


def finish_kernel(
    d_right_panel, d_left_panel, slopes, d_gate_pre, normed_in, inv_in, gain_col, weights, grad
):
    rows = grad.shape[0]
    count, depth, width = d_left_panel.shape
    hidden = count * depth // rows
    for row in range(rows):
        d_right = cell_row(d_right_panel, row, rows)
        d_right = both_halves(d_right.reshape(2 * count, depth // rows, width), count)
        parts = []
        for side, d_value in enumerate((cell_row(d_left_panel, row, rows), d_right.reshape(hidden, width))):
            for base in (2 * side * hidden, (2 * side + 1) * hidden):
                slope = slopes[row, base : base + hidden, :].astype(F32)
                parts.append((d_value * slope).astype(BF16))
        parts.append(d_gate_pre[row])
        d_in = dot(weights[...], jnp.concatenate(parts, axis=0), 1, 0) * gain_col[...]
        normed = normed_in[row].astype(F32)
        mean_grad = jnp.mean(d_in, axis=0, keepdims=True)
        mean_cross = jnp.mean(d_in * normed, axis=0, keepdims=True)
        result = inv_in[row : row + 1] * (d_in - mean_grad - normed * mean_cross)
        grad[row] = jnp.transpose(result).astype(BF16)


def swap(values, count, back):
    groups = [wide_order(lax.axis_size("row"), count, back)]
    return lax.all_to_all(
        values, "row", split_axis=0, concat_axis=0, tiled=True, axis_index_groups=groups
    )


def swap_half(values, count):
    devices = range(lax.axis_size("row"))
    groups = [[d for d in devices if d // count == half] for half in range(len(devices) // count)]
    return lax.all_to_all(
        values, "row", split_axis=0, concat_axis=0, tiled=True, axis_index_groups=groups
    )


def swap_pieces(pieces):
    devices = range(lax.axis_size("row"))
    count = len(pieces)
    return [pieces[0]] + [
        lax.ppermute(pieces[step], "row", [(d, d ^ distance(step, count)) for d in devices])
        for step in range(1, count)
    ]


def kernel_shards(
    pair,
    cotangent,
    residue_mask,
    ln_in_gain,
    ln_in_bias,
    w_proj,
    w_gate,
    ln_out_gain,
    ln_out_bias,
    w_out,
):
    rows, width, channels = pair.shape
    hidden = w_out.shape[0]
    halves = 2
    devices = lax.axis_size("row")
    count = devices // halves
    block = hidden // count
    left_rows, right_rows = rows * count, rows * devices
    shape = jax.ShapeDtypeStruct
    panel = shape((count, rows * block, width), BF16)
    wide_panel = shape((devices, rows * block, width), BF16)
    mask = residue_mask.reshape(1, width)
    gain, bias = ln_in_gain.reshape(1, channels), ln_in_bias.reshape(1, channels)
    out_gain, out_bias = ln_out_gain.reshape(1, hidden), ln_out_bias.reshape(1, hidden)
    cells = rows * width
    piece = shape((rows * block, width), BF16)
    left_panel = pltpu.VMEM(panel.shape, BF16)
    left_wide = pltpu.VMEM((left_rows * block, width), F32)
    right_wide = pltpu.VMEM((right_rows * block, width), F32)
    (own_right,) = call(
        project_right_kernel,
        "project_right",
        [wide_panel],
        [pair, mask, gain, bias, w_proj],
        fetched=range(5),
        flops=2 * cells * channels * 2 * hidden,
        limit=64 * 1024 * 1024 - 640 * 1024,
    )
    right_panel = swap(own_right, count, False)
    pieces = call(
        project_left_kernel,
        "project_left",
        [piece] * count,
        [pair, mask, gain, bias, w_proj, own_right],
        fetched=range(5),
        unread=(5,),
        scratch=[left_panel],
        flops=2 * cells * channels * 2 * hidden,
    )
    pieces = swap_pieces(pieces)
    (left_all,) = call(
        sort_left_kernel,
        "sort_left",
        [shape((block, left_rows, width), BF16)],
        pieces,
        scratch=[left_wide],
    )
    d_hat_centered, gate_slope = call(
        prepare_kernel,
        "prepare",
        [shape((rows, hidden, width), F32), shape((rows, channels, width), F32)],
        [pair, cotangent, gain, bias, w_gate, out_gain, w_out],
        fetched=range(7),
        flops=2 * cells * channels * 2 * hidden,
    )
    products, right_all = call(
        tri_kernel,
        "tri",
        [panel, shape((block, right_rows, width), BF16)],
        [right_panel, left_all, d_hat_centered],
        unread=(2,),
        scratch=[left_wide, right_wide],
        flops=2 * block * left_rows * width * right_rows,
    )
    products = swap_half(products, count)
    (d_products,) = call(
        middle_kernel,
        "middle",
        [panel],
        [products, d_hat_centered],
        flops=20 * cells * hidden,
    )
    d_products = swap_half(d_products, count)
    d_right_panel, d_tri_all = call(
        d_right_kernel,
        "d_right",
        [wide_panel, shape((block, left_rows, width), BF16)],
        [d_products, left_all],
        scratch=[left_wide, right_wide],
        flops=2 * block * left_rows * width * right_rows,
    )
    d_right_panel = swap(d_right_panel, count, True)
    d_pieces = call(
        d_left_kernel,
        "d_left",
        [piece] * count,
        [d_tri_all, right_all],
        scratch=[left_wide],
        flops=2 * block * left_rows * width * right_rows,
    )
    d_pieces = swap_pieces(d_pieces)
    (d_left_panel,) = call(sort_d_left_kernel, "sort_d_left", [panel], d_pieces)
    (d_gate_pre,) = call(
        gate_back_kernel,
        "gate_back",
        [shape((rows, channels, width), BF16)],
        [products, gate_slope, out_gain, out_bias, w_out],
        fetched=range(2, 5),
        flops=2 * cells * channels * hidden,
    )
    slopes, normed_in, inv_in, gain_col, weights = call(
        slopes_kernel,
        "slopes",
        [
            shape((rows, 4 * hidden, width), BF16),
            shape((rows, channels, width), BF16),
            shape((rows, width), F32),
            shape((channels, channels), F32),
            shape((channels, 4 * hidden + channels), BF16),
        ],
        [pair, mask, gain, bias, w_proj, w_gate, d_gate_pre],
        fetched=range(6),
        unread=(6,),
        flops=2 * cells * channels * 4 * hidden,
    )
    (grad,) = call(
        finish_kernel,
        "finish",
        [shape(pair.shape, BF16)],
        [
            d_right_panel,
            d_left_panel,
            slopes,
            d_gate_pre,
            normed_in,
            inv_in,
            gain_col,
            weights,
        ],
        flops=2 * cells * channels * 4 * hidden,
    )
    return grad


def normalize(values, reduce_axis):
    mean_value = jnp.mean(values, axis=reduce_axis, keepdims=True)
    centered = values - mean_value
    variance = jnp.mean(centered * centered, axis=reduce_axis, keepdims=True)
    inv_std = lax.rsqrt(variance + 1e-05)
    return (centered * inv_std, inv_std)


def norm_backward(upstream, normed, inv_std, reduce_axis):
    mean_grad = jnp.mean(upstream, axis=reduce_axis, keepdims=True)
    mean_cross = jnp.mean(upstream * normed, axis=reduce_axis, keepdims=True)
    return inv_std * (upstream - mean_grad - normed * mean_cross)


def shards(
    pair,
    cotangent,
    residue_mask,
    ln_in_gain,
    ln_in_bias,
    w_proj,
    w_gate,
    ln_out_gain,
    ln_out_bias,
    w_out,
):
    local_rows = pair.shape[0]
    local_cols = pair.shape[1]
    hidden = w_out.shape[0]
    chan_index = lax.axis_index("chan")
    row_start = lax.axis_index("row") * local_rows
    col_start = chan_index * local_cols
    mask_float = residue_mask.astype(jnp.float32)
    row_mask = lax.dynamic_slice_in_dim(mask_float, row_start, local_rows)
    col_mask = lax.dynamic_slice_in_dim(mask_float, col_start, local_cols)
    cell_mask = (row_mask[:, None] * col_mask[None, :])[None]
    normed, inv_std = normalize(pair.astype(jnp.float32), -1)
    normed_pair = (normed * ln_in_gain + ln_in_bias).astype(jnp.bfloat16)
    projected = jnp.einsum("rmc,ch->hrm", normed_pair, w_proj, preferred_element_type=jnp.float32)
    left_panel = (
        cell_mask * jax.nn.sigmoid(projected[:hidden]) * projected[hidden : 2 * hidden]
    ).astype(jnp.bfloat16)
    right_panel = (
        cell_mask * jax.nn.sigmoid(projected[2 * hidden : 3 * hidden]) * projected[3 * hidden :]
    ).astype(jnp.bfloat16)
    panels = lax.all_to_all(
        jnp.stack([left_panel, right_panel]), "row", split_axis=1, concat_axis=2, tiled=True
    )
    left_all = panels[0]
    right_all = panels[1]
    right_rows = lax.all_to_all(right_all, "chan", split_axis=1, concat_axis=2, tiled=True)
    partner = right_rows
    tri_part = jnp.einsum(
        "gik,gjk->gij",
        lax.all_gather(left_all, "chan", axis=2, tiled=True),
        partner,
        preferred_element_type=jnp.float32,
    ).astype(jnp.bfloat16)
    tri_cells = lax.all_to_all(tri_part, "row", split_axis=1, concat_axis=0, tiled=True)
    tri_hat, inv_tri = normalize(tri_cells.astype(jnp.float32), 0)
    scaled = (tri_hat * ln_out_gain[:, None, None] + ln_out_bias[:, None, None]).astype(
        jnp.bfloat16
    )
    proj_out = jnp.einsum("hrm,hc->rmc", scaled, w_out, preferred_element_type=jnp.float32)
    gate_value = jax.nn.sigmoid(
        jnp.einsum("rmc,cd->rmd", normed_pair, w_gate, preferred_element_type=jnp.float32)
    )
    cot_float = cotangent.astype(jnp.float32)
    d_gate_pre = (cot_float * proj_out * gate_value * (1.0 - gate_value)).astype(jnp.bfloat16)
    d_scaled = (cot_float * gate_value).astype(jnp.bfloat16)
    d_hat = jnp.einsum("rmc,hc->hrm", d_scaled, w_out, preferred_element_type=jnp.float32)
    d_hat = d_hat * ln_out_gain[:, None, None]
    d_tri = norm_backward(d_hat, tri_hat, inv_tri, 0).astype(jnp.bfloat16)
    d_tri_all = lax.all_to_all(d_tri, "row", split_axis=0, concat_axis=1, tiled=True)
    panel_piece = lax.all_gather(d_tri_all, "chan", axis=2, tiled=True)
    partner = right_all
    d_left = jnp.einsum("gij,gjk->gik", panel_piece, partner, preferred_element_type=jnp.float32)
    contribution = jnp.einsum(
        "gij,gik->gjk", panel_piece, left_all, preferred_element_type=jnp.float32
    )
    d_right = contribution
    d_left, d_right = (d_left, d_right)
    d_stack = jnp.stack([d_left, d_right]).astype(jnp.bfloat16)
    d_panels = lax.all_to_all(d_stack, "row", split_axis=2, concat_axis=1, tiled=True)

    def gating(d_value, gate_proj, value_proj):
        sigmoid_val = jax.nn.sigmoid(gate_proj)
        masked_grad = d_value.astype(jnp.float32) * cell_mask
        return (
            masked_grad * value_proj * sigmoid_val * (1.0 - sigmoid_val),
            masked_grad * sigmoid_val,
        )

    gate_left, value_left = gating(d_panels[0], projected[:hidden], projected[hidden : 2 * hidden])
    gate_right, value_right = gating(
        d_panels[1], projected[2 * hidden : 3 * hidden], projected[3 * hidden :]
    )
    d_proj = jnp.concatenate([gate_left, value_left, gate_right, value_right], axis=0).astype(
        jnp.bfloat16
    )
    d_normed = jnp.einsum("hrm,ch->rmc", d_proj, w_proj, preferred_element_type=jnp.float32)
    d_normed = d_normed + jnp.einsum(
        "rmd,cd->rmc", d_gate_pre, w_gate, preferred_element_type=jnp.float32
    )
    d_input = d_normed * ln_in_gain
    return norm_backward(d_input, normed, inv_std, -1).astype(jnp.bfloat16)


def solution(mesh):
    fits = mesh.shape["chan"] == 1 and mesh.shape["row"] in (8, 16)
    return jax.shard_map(
        kernel_shards if fits else shards,
        mesh=mesh,
        in_specs=(
            P(("grp", "row"), "chan", None),
            P(("grp", "row"), "chan", None),
            P("grp"),
            P(),
            P(),
            P(),
            P(),
            P(),
            P(),
            P(),
        ),
        out_specs=P(("grp", "row"), "chan", None),
        check_vma=False,
    )
```

```python
import functools

import jax
import jax.numpy as jnp
from jax import lax
from jax.experimental import pallas as pl
from jax.experimental.pallas import tpu as pltpu
from jax.sharding import PartitionSpec as P

F32 = jnp.float32
BF16 = jnp.bfloat16
VMEM_LIMIT = 16 * 1024 * 1024


def dot(lhs, rhs, lhs_dim, rhs_dim):
    return lax.dot_general(
        lhs, rhs, (((lhs_dim,), (rhs_dim,)), ((), ())), preferred_element_type=F32
    )


def transposed(matrix):
    return jnp.transpose(matrix.astype(F32)).astype(BF16)


def sigmoid(values):
    return 1.0 / (1.0 + jnp.exp(-values))


def column(row):
    size = row.shape[1]
    return jnp.transpose(jnp.broadcast_to(row, (size, size)))


def norm_rows(values):
    centered = values - jnp.mean(values, axis=0, keepdims=True)
    variance = jnp.mean(centered * centered, axis=0, keepdims=True)
    inv_std = lax.rsqrt(variance + 1e-05)
    return centered * inv_std, inv_std


def call(
    kernel, name, outs, args, fetched=(), unread=(), scratch=(), flops=0, limit=VMEM_LIMIT
):
    moved = sum(a.size * a.dtype.itemsize for a in args) + sum(
        o.size * jnp.dtype(o.dtype).itemsize for o in outs
    )
    n_args, n_outs, n_fetched = len(args), len(outs), len(fetched)

    def body(*refs):
        ins = list(refs[:n_args])
        rest = refs[n_args + n_outs :]
        copies = []
        for n, place in enumerate(fetched):
            copies.append(pltpu.make_async_copy(ins[place], rest[n], rest[n_fetched].at[n]))
            ins[place] = rest[n]
        for copy in copies:
            copy.start()
        for copy in copies:
            copy.wait()
        kernel(*ins, *refs[n_args : n_args + n_outs], *rest[n_fetched + (n_fetched > 0) :])

    buffers = [pltpu.VMEM(args[place].shape, args[place].dtype) for place in fetched]
    if fetched:
        buffers.append(pltpu.SemaphoreType.DMA((n_fetched,)))
    return pl.pallas_call(
        body,
        name=name,
        out_shape=outs,
        in_specs=[
            pl.BlockSpec(
                memory_space=pltpu.HBM if n in fetched else pl.ANY if n in unread else pltpu.VMEM
            )
            for n in range(n_args)
        ],
        out_specs=[pl.BlockSpec(memory_space=pltpu.VMEM) for _ in outs],
        scratch_shapes=buffers + list(scratch),
        compiler_params=pltpu.CompilerParams(vmem_limit_bytes=limit),
        cost_estimate=pl.CostEstimate(flops=flops, bytes_accessed=moved, transcendentals=0),
    )(*args)


def cell_masks(mask, rows):
    columns = mask[...].astype(F32)
    shape = (rows, columns.shape[1])
    first = lax.axis_index("row") * rows
    own = lax.broadcasted_iota(jnp.int32, shape, 1) == (
        lax.broadcasted_iota(jnp.int32, shape, 0) + first
    )
    row_mask = jnp.sum(jnp.where(own, columns, 0.0), axis=1, keepdims=True)
    cells = row_mask * columns
    return [cells[row : row + 1] for row in range(rows)]


def wide_order(devices, count, back):
    order = []
    for place in range(count):
        if back:
            order += [place ^ (count // 2), count + place]
        else:
            order += [count + (place ^ 2), place ^ (count // 2)]
    return order


def distances(count, beside):
    far = sorted(range(2, count), key=lambda apart: -(apart // 2))
    if beside:
        return [0, 1, 2] + [apart for apart in far if apart != 2]
    return [0] + far + [1]


def partners(count, beside):
    place = lax.rem(lax.axis_index("row"), count)
    return [place ^ apart for apart in distances(count, beside)]


def gather(pieces, panel, beside):
    for place, piece in zip(partners(len(pieces), beside), pieces):
        panel[place] = piece[...]


def spread(pieces, wide, beside):
    depth = pieces[0].shape[0]
    for place, piece in zip(partners(len(pieces), beside), pieces):
        wide[pl.ds(pl.multiple_of(place * depth, depth), depth), :] = piece[...].astype(F32)


def hand_out(wide, pieces, beside):
    depth = pieces[0].shape[0]
    for place, piece in zip(partners(len(pieces), beside), pieces):
        piece[...] = wide[pl.ds(pl.multiple_of(place * depth, depth), depth), :].astype(BF16)


def gated_rows(pair, mask, gain, bias, w_proj, side):
    rows = pair.shape[0]
    hidden = w_proj.shape[1] // 4
    w_flip = transposed(w_proj[:, 2 * side * hidden : 2 * (side + 1) * hidden])
    gain_col, bias_col = column(gain[...]), column(bias[...])
    masks = cell_masks(mask, rows)
    for row in range(rows):
        normed, _ = norm_rows(jnp.transpose(pair[row].astype(F32)))
        zln = (normed * gain_col + bias_col).astype(BF16)
        proj = dot(w_flip, zln, 1, 0)
        yield row, masks[row] * sigmoid(proj[:hidden]) * proj[hidden:]


def project_right_kernel(pair, mask, gain, bias, w_proj, right_panel):
    rows = pair.shape[0]
    devices, depth, width = right_panel.shape
    block = depth // rows
    count = w_proj.shape[1] // 4 // block
    for row, right in gated_rows(pair, mask, gain, bias, w_proj, 1):
        right = right.reshape(count, block, width).astype(BF16)
        for rank in range(devices):
            place = wide_order(devices, count, False)[rank] % count
            right_panel[rank, row * block : (row + 1) * block, :] = right[place]


def project_left_kernel(pair, mask, gain, bias, w_proj, after, *refs):
    del after
    *pieces, left_panel = refs
    rows = pair.shape[0]
    count, depth, width = left_panel.shape
    block = depth // rows
    for row, left in gated_rows(pair, mask, gain, bias, w_proj, 0):
        left = left.reshape(count, block, width).astype(BF16)
        left_panel[:, row * block : (row + 1) * block, :] = left
    for place, piece in zip(partners(count, True), pieces):
        piece[...] = left_panel[place]


def prepare_kernel(
    pair, cotangent, gain, bias, w_gate, out_gain, w_out, d_hat_centered, gate_slope
):
    gate_flip = transposed(w_gate[...])
    gain_col, bias_col = column(gain[...]), column(bias[...])
    out_gain_col = column(out_gain[...])
    for row in range(pair.shape[0]):
        normed, _ = norm_rows(jnp.transpose(pair[row].astype(F32)))
        zln = (normed * gain_col + bias_col).astype(BF16)
        gate = sigmoid(dot(gate_flip, zln, 1, 0))
        cot = jnp.transpose(cotangent[row].astype(F32))
        d_scaled = (cot * gate).astype(BF16)
        d_hat = dot(w_out[...], d_scaled, 1, 0) * out_gain_col
        d_hat_centered[row] = d_hat - jnp.mean(d_hat, axis=0, keepdims=True)
        gate_slope[row] = cot * gate * (1.0 - gate)


def wide_places(panel, count, back):
    devices, depth, _ = panel.shape
    for rank, device in enumerate(wide_order(devices, count, back)):
        yield rank, slice(device * depth, (device + 1) * depth)


def sort_left_kernel(*refs):
    *pieces, left_all, left_wide = refs
    block, left_rows, _ = left_all.shape
    spread(pieces, left_wide, True)
    for h in range(block):
        left_all[h] = left_wide[pl.ds(h, left_rows, stride=block), :].astype(BF16)


def tri_kernel(right_panel, left_all, after, *refs):
    del after
    right_all, *pieces, left_wide, right_wide = refs
    block, left_rows, _ = left_all.shape
    right_rows = right_all.shape[1]
    for rank, place in wide_places(right_panel, len(pieces), False):
        right_wide[place, :] = right_panel[rank].astype(F32)
    for h in range(block):
        right = right_wide[pl.ds(h, right_rows, stride=block), :].astype(BF16)
        right_all[h] = right
        left_wide[pl.ds(h, left_rows, stride=block), :] = dot(left_all[h], right, 1, 1)
    hand_out(left_wide, pieces, False)


def cell_row(ref, row, rows):
    count, depth, width = ref.shape
    block = depth // rows
    return ref[:, row * block : (row + 1) * block, :].astype(F32).reshape(count * block, width)


def middle_kernel(d_hat_centered, *refs):
    count = (len(refs) - 2) // 2
    products, pieces = refs[:count], refs[count : 2 * count]
    panel, d_panel = refs[2 * count :]
    rows = d_hat_centered.shape[0]
    _, depth, width = panel.shape
    block = depth // rows
    gather(products, panel, False)
    for row in range(rows):
        tri_hat, inv_std = norm_rows(cell_row(panel, row, rows))
        d_hat = d_hat_centered[row]
        cross = jnp.mean(d_hat * tri_hat, axis=0, keepdims=True)
        d_tri = inv_std * (d_hat - tri_hat * cross)
        d_panel[:, row * block : (row + 1) * block, :] = d_tri.reshape(
            count, block, width
        ).astype(BF16)
    for place, piece in zip(partners(count, False), pieces):
        piece[...] = d_panel[place]


def d_right_kernel(left_all, *refs):
    *d_products, d_right_panel, d_tri_all, left_wide, right_wide = refs
    block, left_rows, _ = left_all.shape
    right_rows = right_wide.shape[0] // block
    spread(d_products, left_wide, False)
    for h in range(block):
        d_tri = left_wide[pl.ds(h, left_rows, stride=block), :].astype(BF16)
        d_tri_all[h] = d_tri
        right_wide[pl.ds(h, right_rows, stride=block), :] = dot(d_tri, left_all[h], 0, 0)
    for rank, place in wide_places(d_right_panel, len(d_products), True):
        d_right_panel[rank] = right_wide[place, :].astype(BF16)


def d_left_kernel(d_tri_all, right_all, *refs):
    *pieces, left_wide = refs
    block, left_rows, _ = d_tri_all.shape
    for h in range(block):
        left_wide[pl.ds(h, left_rows, stride=block), :] = dot(d_tri_all[h], right_all[h], 1, 0)
    hand_out(left_wide, pieces, True)


def gate_back_kernel(gate_slope, out_gain, out_bias, w_out, *refs):
    *products, d_gate_pre, panel = refs
    rows = gate_slope.shape[0]
    gather(products, panel, False)
    out_flip = transposed(w_out[...])
    out_gain_col, out_bias_col = column(out_gain[...]), column(out_bias[...])
    for row in range(rows):
        tri_hat, _ = norm_rows(cell_row(panel, row, rows))
        scaled = (tri_hat * out_gain_col + out_bias_col).astype(BF16)
        d_gate_pre[row] = (dot(out_flip, scaled, 1, 0) * gate_slope[row]).astype(BF16)


def slopes_kernel(
    pair, mask, gain, bias, w_proj, w_gate, after, slopes, normed_in, inv_in, in_gain, weights
):
    del after
    rows = pair.shape[0]
    hidden = w_proj.shape[1] // 4
    w_flip = transposed(w_proj[...])
    gain_col, bias_col = column(gain[...]), column(bias[...])
    in_gain[...] = gain_col
    weights[...] = jnp.concatenate([w_proj[...], w_gate[...]], axis=1)
    masks = cell_masks(mask, rows)
    for row in range(rows):
        normed, inv_std = norm_rows(jnp.transpose(pair[row].astype(F32)))
        normed_in[row] = normed.astype(normed_in.dtype)
        inv_in[row : row + 1] = inv_std
        zln = (normed * gain_col + bias_col).astype(BF16)
        proj = dot(w_flip, zln, 1, 0)
        for side in range(2):
            base = 2 * side * hidden
            sig = sigmoid(proj[base : base + hidden])
            masked = masks[row] * sig
            value = masked * (1.0 - sig) * proj[base + hidden : base + 2 * hidden]
            slopes[row, base : base + hidden, :] = value.astype(slopes.dtype)
            slopes[row, base + hidden : base + 2 * hidden, :] = masked.astype(slopes.dtype)


def sort_d_left_kernel(*refs):
    *pieces, d_left_panel = refs
    gather(pieces, d_left_panel, True)


def both_halves(blocks, count):
    order = wide_order(2 * count, count, True)
    return jnp.stack(
        [blocks[order.index(place)] + blocks[order.index(count + place)] for place in range(count)]
    )


def finish_kernel(
    d_right_panel, d_left_panel, slopes, d_gate_pre, normed_in, inv_in, gain_col, weights, grad
):
    rows = grad.shape[0]
    count, depth, width = d_left_panel.shape
    hidden = count * depth // rows
    for row in range(rows):
        d_right = cell_row(d_right_panel, row, rows)
        d_right = both_halves(d_right.reshape(2 * count, depth // rows, width), count)
        parts = []
        for side, d_value in enumerate((cell_row(d_left_panel, row, rows), d_right.reshape(hidden, width))):
            for base in (2 * side * hidden, (2 * side + 1) * hidden):
                slope = slopes[row, base : base + hidden, :].astype(F32)
                parts.append((d_value * slope).astype(BF16))
        parts.append(d_gate_pre[row])
        d_in = dot(weights[...], jnp.concatenate(parts, axis=0), 1, 0) * gain_col[...]
        normed = normed_in[row].astype(F32)
        mean_grad = jnp.mean(d_in, axis=0, keepdims=True)
        mean_cross = jnp.mean(d_in * normed, axis=0, keepdims=True)
        result = inv_in[row : row + 1] * (d_in - mean_grad - normed * mean_cross)
        grad[row] = jnp.transpose(result).astype(BF16)


def swap(values, count, back):
    groups = [wide_order(lax.axis_size("row"), count, back)]
    return lax.all_to_all(
        values, "row", split_axis=0, concat_axis=0, tiled=True, axis_index_groups=groups
    )


def swap_pieces(pieces, beside):
    devices = range(lax.axis_size("row"))
    apart = distances(len(pieces), beside)
    return [pieces[0]] + [
        lax.ppermute(pieces[step], "row", [(d, d ^ apart[step]) for d in devices])
        for step in range(1, len(pieces))
    ]


def kernel_shards(
    pair,
    cotangent,
    residue_mask,
    ln_in_gain,
    ln_in_bias,
    w_proj,
    w_gate,
    ln_out_gain,
    ln_out_bias,
    w_out,
):
    rows, width, channels = pair.shape
    hidden = w_out.shape[0]
    halves = 2
    devices = lax.axis_size("row")
    count = devices // halves
    block = hidden // count
    left_rows, right_rows = rows * count, rows * devices
    shape = jax.ShapeDtypeStruct
    panel = shape((count, rows * block, width), BF16)
    wide_panel = shape((devices, rows * block, width), BF16)
    mask = residue_mask.reshape(1, width)
    gain, bias = ln_in_gain.reshape(1, channels), ln_in_bias.reshape(1, channels)
    out_gain, out_bias = ln_out_gain.reshape(1, hidden), ln_out_bias.reshape(1, hidden)
    cells = rows * width
    piece = shape((rows * block, width), BF16)
    left_panel = pltpu.VMEM(panel.shape, BF16)
    left_wide = pltpu.VMEM((left_rows * block, width), F32)
    right_wide = pltpu.VMEM((right_rows * block, width), F32)
    (own_right,) = call(
        project_right_kernel,
        "project_right",
        [wide_panel],
        [pair, mask, gain, bias, w_proj],
        fetched=range(5),
        flops=2 * cells * channels * 2 * hidden,
        limit=64 * 1024 * 1024 - 640 * 1024,
    )
    right_panel = swap(own_right, count, False)
    pieces = call(
        project_left_kernel,
        "project_left",
        [piece] * count,
        [pair, mask, gain, bias, w_proj, own_right],
        fetched=range(5),
        unread=(5,),
        scratch=[left_panel],
        flops=2 * cells * channels * 2 * hidden,
    )
    pieces = swap_pieces(pieces, True)
    (left_all,) = call(
        sort_left_kernel,
        "sort_left",
        [shape((block, left_rows, width), BF16)],
        pieces,
        scratch=[left_wide],
    )
    d_hat_centered, gate_slope = call(
        prepare_kernel,
        "prepare",
        [shape((rows, hidden, width), F32), shape((rows, channels, width), F32)],
        [pair, cotangent, gain, bias, w_gate, out_gain, w_out],
        fetched=range(7),
        flops=2 * cells * channels * 2 * hidden,
    )
    right_all, *products = call(
        tri_kernel,
        "tri",
        [shape((block, right_rows, width), BF16)] + [piece] * count,
        [right_panel, left_all, d_hat_centered],
        unread=(2,),
        scratch=[left_wide, right_wide],
        flops=2 * block * left_rows * width * right_rows,
    )
    products = swap_pieces(products, False)
    d_products = call(
        middle_kernel,
        "middle",
        [piece] * count,
        [d_hat_centered, *products],
        scratch=[left_panel, left_panel],
        flops=20 * cells * hidden,
    )
    d_products = swap_pieces(d_products, False)
    d_right_panel, d_tri_all = call(
        d_right_kernel,
        "d_right",
        [wide_panel, shape((block, left_rows, width), BF16)],
        [left_all, *d_products],
        scratch=[left_wide, right_wide],
        flops=2 * block * left_rows * width * right_rows,
    )
    d_right_panel = swap(d_right_panel, count, True)
    d_pieces = call(
        d_left_kernel,
        "d_left",
        [piece] * count,
        [d_tri_all, right_all],
        scratch=[left_wide],
        flops=2 * block * left_rows * width * right_rows,
    )
    d_pieces = swap_pieces(d_pieces, True)
    (d_left_panel,) = call(sort_d_left_kernel, "sort_d_left", [panel], d_pieces)
    (d_gate_pre,) = call(
        gate_back_kernel,
        "gate_back",
        [shape((rows, channels, width), BF16)],
        [gate_slope, out_gain, out_bias, w_out, *products],
        fetched=range(1, 4),
        scratch=[left_panel],
        flops=2 * cells * channels * hidden,
    )
    slopes, normed_in, inv_in, gain_col, weights = call(
        slopes_kernel,
        "slopes",
        [
            shape((rows, 4 * hidden, width), BF16),
            shape((rows, channels, width), BF16),
            shape((rows, width), F32),
            shape((channels, channels), F32),
            shape((channels, 4 * hidden + channels), BF16),
        ],
        [pair, mask, gain, bias, w_proj, w_gate, d_gate_pre],
        fetched=range(6),
        unread=(6,),
        flops=2 * cells * channels * 4 * hidden,
    )
    (grad,) = call(
        finish_kernel,
        "finish",
        [shape(pair.shape, BF16)],
        [
            d_right_panel,
            d_left_panel,
            slopes,
            d_gate_pre,
            normed_in,
            inv_in,
            gain_col,
            weights,
        ],
        flops=2 * cells * channels * 4 * hidden,
    )
    return grad


def normalize(values, reduce_axis):
    mean_value = jnp.mean(values, axis=reduce_axis, keepdims=True)
    centered = values - mean_value
    variance = jnp.mean(centered * centered, axis=reduce_axis, keepdims=True)
    inv_std = lax.rsqrt(variance + 1e-05)
    return (centered * inv_std, inv_std)


def norm_backward(upstream, normed, inv_std, reduce_axis):
    mean_grad = jnp.mean(upstream, axis=reduce_axis, keepdims=True)
    mean_cross = jnp.mean(upstream * normed, axis=reduce_axis, keepdims=True)
    return inv_std * (upstream - mean_grad - normed * mean_cross)


def shards(
    pair,
    cotangent,
    residue_mask,
    ln_in_gain,
    ln_in_bias,
    w_proj,
    w_gate,
    ln_out_gain,
    ln_out_bias,
    w_out,
):
    local_rows = pair.shape[0]
    local_cols = pair.shape[1]
    hidden = w_out.shape[0]
    chan_index = lax.axis_index("chan")
    row_start = lax.axis_index("row") * local_rows
    col_start = chan_index * local_cols
    mask_float = residue_mask.astype(jnp.float32)
    row_mask = lax.dynamic_slice_in_dim(mask_float, row_start, local_rows)
    col_mask = lax.dynamic_slice_in_dim(mask_float, col_start, local_cols)
    cell_mask = (row_mask[:, None] * col_mask[None, :])[None]
    normed, inv_std = normalize(pair.astype(jnp.float32), -1)
    normed_pair = (normed * ln_in_gain + ln_in_bias).astype(jnp.bfloat16)
    projected = jnp.einsum("rmc,ch->hrm", normed_pair, w_proj, preferred_element_type=jnp.float32)
    left_panel = (
        cell_mask * jax.nn.sigmoid(projected[:hidden]) * projected[hidden : 2 * hidden]
    ).astype(jnp.bfloat16)
    right_panel = (
        cell_mask * jax.nn.sigmoid(projected[2 * hidden : 3 * hidden]) * projected[3 * hidden :]
    ).astype(jnp.bfloat16)
    panels = lax.all_to_all(
        jnp.stack([left_panel, right_panel]), "row", split_axis=1, concat_axis=2, tiled=True
    )
    left_all = panels[0]
    right_all = panels[1]
    right_rows = lax.all_to_all(right_all, "chan", split_axis=1, concat_axis=2, tiled=True)
    partner = right_rows
    tri_part = jnp.einsum(
        "gik,gjk->gij",
        lax.all_gather(left_all, "chan", axis=2, tiled=True),
        partner,
        preferred_element_type=jnp.float32,
    ).astype(jnp.bfloat16)
    tri_cells = lax.all_to_all(tri_part, "row", split_axis=1, concat_axis=0, tiled=True)
    tri_hat, inv_tri = normalize(tri_cells.astype(jnp.float32), 0)
    scaled = (tri_hat * ln_out_gain[:, None, None] + ln_out_bias[:, None, None]).astype(
        jnp.bfloat16
    )
    proj_out = jnp.einsum("hrm,hc->rmc", scaled, w_out, preferred_element_type=jnp.float32)
    gate_value = jax.nn.sigmoid(
        jnp.einsum("rmc,cd->rmd", normed_pair, w_gate, preferred_element_type=jnp.float32)
    )
    cot_float = cotangent.astype(jnp.float32)
    d_gate_pre = (cot_float * proj_out * gate_value * (1.0 - gate_value)).astype(jnp.bfloat16)
    d_scaled = (cot_float * gate_value).astype(jnp.bfloat16)
    d_hat = jnp.einsum("rmc,hc->hrm", d_scaled, w_out, preferred_element_type=jnp.float32)
    d_hat = d_hat * ln_out_gain[:, None, None]
    d_tri = norm_backward(d_hat, tri_hat, inv_tri, 0).astype(jnp.bfloat16)
    d_tri_all = lax.all_to_all(d_tri, "row", split_axis=0, concat_axis=1, tiled=True)
    panel_piece = lax.all_gather(d_tri_all, "chan", axis=2, tiled=True)
    partner = right_all
    d_left = jnp.einsum("gij,gjk->gik", panel_piece, partner, preferred_element_type=jnp.float32)
    contribution = jnp.einsum(
        "gij,gik->gjk", panel_piece, left_all, preferred_element_type=jnp.float32
    )
    d_right = contribution
    d_left, d_right = (d_left, d_right)
    d_stack = jnp.stack([d_left, d_right]).astype(jnp.bfloat16)
    d_panels = lax.all_to_all(d_stack, "row", split_axis=2, concat_axis=1, tiled=True)

    def gating(d_value, gate_proj, value_proj):
        sigmoid_val = jax.nn.sigmoid(gate_proj)
        masked_grad = d_value.astype(jnp.float32) * cell_mask
        return (
            masked_grad * value_proj * sigmoid_val * (1.0 - sigmoid_val),
            masked_grad * sigmoid_val,
        )

    gate_left, value_left = gating(d_panels[0], projected[:hidden], projected[hidden : 2 * hidden])
    gate_right, value_right = gating(
        d_panels[1], projected[2 * hidden : 3 * hidden], projected[3 * hidden :]
    )
    d_proj = jnp.concatenate([gate_left, value_left, gate_right, value_right], axis=0).astype(
        jnp.bfloat16
    )
    d_normed = jnp.einsum("hrm,ch->rmc", d_proj, w_proj, preferred_element_type=jnp.float32)
    d_normed = d_normed + jnp.einsum(
        "rmd,cd->rmc", d_gate_pre, w_gate, preferred_element_type=jnp.float32
    )
    d_input = d_normed * ln_in_gain
    return norm_backward(d_input, normed, inv_std, -1).astype(jnp.bfloat16)


def solution(mesh):
    fits = mesh.shape["chan"] == 1 and mesh.shape["row"] in (8, 16)
    return jax.shard_map(
        kernel_shards if fits else shards,
        mesh=mesh,
        in_specs=(
            P(("grp", "row"), "chan", None),
            P(("grp", "row"), "chan", None),
            P("grp"),
            P(),
            P(),
            P(),
            P(),
            P(),
            P(),
            P(),
        ),
        out_specs=P(("grp", "row"), "chan", None),
        check_vma=False,
    )
```

```python
import functools

import jax
import jax.numpy as jnp
from jax import lax
from jax.experimental import pallas as pl
from jax.experimental.pallas import tpu as pltpu
from jax.sharding import PartitionSpec as P

F32 = jnp.float32
BF16 = jnp.bfloat16
VMEM_LIMIT = 16 * 1024 * 1024


def dot(lhs, rhs, lhs_dim, rhs_dim):
    return lax.dot_general(
        lhs, rhs, (((lhs_dim,), (rhs_dim,)), ((), ())), preferred_element_type=F32
    )


def transposed(matrix):
    return jnp.transpose(matrix.astype(F32)).astype(BF16)


def sigmoid(values):
    return 0.5 + 0.5 * jnp.tanh(0.5 * values)


def column(row):
    size = row.shape[1]
    return jnp.transpose(jnp.broadcast_to(row, (size, size)))


def norm_rows(values):
    centered = values - jnp.mean(values, axis=0, keepdims=True)
    variance = jnp.mean(centered * centered, axis=0, keepdims=True)
    inv_std = lax.rsqrt(variance + 1e-05)
    return centered * inv_std, inv_std


def call(
    kernel, name, outs, args, fetched=(), columns={}, unread=(), scratch=(), flops=0, limit=VMEM_LIMIT
):
    moved = sum(a.size * a.dtype.itemsize for a in args) + sum(
        o.size * jnp.dtype(o.dtype).itemsize for o in outs
    )
    n_args, n_outs, n_fetched = len(args), len(outs), len(fetched)

    def body(*refs):
        ins = list(refs[:n_args])
        rest = refs[n_args + n_outs :]
        copies = []
        for n, place in enumerate(fetched):
            source = ins[place].at[:, columns[place]] if place in columns else ins[place]
            copies.append(pltpu.make_async_copy(source, rest[n], rest[n_fetched].at[n]))
            ins[place] = rest[n]
        for copy in copies:
            copy.start()
        for copy in copies:
            copy.wait()
        kernel(*ins, *refs[n_args : n_args + n_outs], *rest[n_fetched + (n_fetched > 0) :])

    buffers = [
        pltpu.VMEM(
            (*args[place].shape[:-1], columns[place].size) if place in columns else args[place].shape,
            args[place].dtype,
        )
        for place in fetched
    ]
    if fetched:
        buffers.append(pltpu.SemaphoreType.DMA((n_fetched,)))
    return pl.pallas_call(
        body,
        name=name,
        out_shape=outs,
        in_specs=[
            pl.BlockSpec(
                memory_space=pltpu.HBM if n in fetched else pl.ANY if n in unread else pltpu.VMEM
            )
            for n in range(n_args)
        ],
        out_specs=[pl.BlockSpec(memory_space=pltpu.VMEM) for _ in outs],
        scratch_shapes=buffers + list(scratch),
        compiler_params=pltpu.CompilerParams(vmem_limit_bytes=limit),
        cost_estimate=pl.CostEstimate(flops=flops, bytes_accessed=moved, transcendentals=0),
    )(*args)


def cell_masks(mask, rows):
    columns = mask[...].astype(F32)
    shape = (rows, columns.shape[1])
    first = lax.axis_index("row") * rows
    own = lax.broadcasted_iota(jnp.int32, shape, 1) == (
        lax.broadcasted_iota(jnp.int32, shape, 0) + first
    )
    row_mask = jnp.sum(jnp.where(own, columns, 0.0), axis=1, keepdims=True)
    cells = row_mask * columns
    return [cells[row : row + 1] for row in range(rows)]


def wide_order(devices, count, back):
    order = []
    for place in range(count):
        if back:
            order += [place ^ (count // 2), count + place]
        else:
            order += [count + (place ^ 2), place ^ (count // 2)]
    return order


def distance(step, count):
    far = sorted(range(3, count), key=lambda apart: -(apart // 2))
    return [*range(min(3, count)), *far][step]


def partner(step, count):
    return lax.rem(lax.axis_index("row"), count) ^ distance(step, count)


def gated_rows(pair, mask, gain, bias, w_side):
    rows = pair.shape[0]
    hidden = w_side.shape[1] // 2
    w_flip = transposed(w_side[...])
    gain_col, bias_col = column(gain[...]), column(bias[...])
    masks = cell_masks(mask, rows)
    for row in range(rows):
        normed, _ = norm_rows(jnp.transpose(pair[row].astype(F32)))
        zln = (normed * gain_col + bias_col).astype(BF16)
        proj = dot(w_flip, zln, 1, 0)
        yield row, masks[row] * sigmoid(proj[:hidden]) * proj[hidden:]


def project_right_kernel(pair, mask, gain, bias, w_side, right_panel):
    rows = pair.shape[0]
    devices, depth, width = right_panel.shape
    block = depth // rows
    count = w_side.shape[1] // 2 // block
    for row, right in gated_rows(pair, mask, gain, bias, w_side):
        right = right.reshape(count, block, width).astype(BF16)
        for rank in range(devices):
            place = wide_order(devices, count, False)[rank] % count
            right_panel[rank, row * block : (row + 1) * block, :] = right[place]


def project_left_kernel(pair, mask, gain, bias, w_side, after, *refs):
    del after
    *pieces, left_panel = refs
    rows = pair.shape[0]
    count, depth, width = left_panel.shape
    block = depth // rows
    for row, left in gated_rows(pair, mask, gain, bias, w_side):
        left = left.reshape(count, block, width).astype(BF16)
        left_panel[:, row * block : (row + 1) * block, :] = left
    for step, piece in enumerate(pieces):
        piece[...] = left_panel[partner(step, count)]


def prepare_kernel(
    pair, cotangent, gain, bias, w_gate, out_gain, w_out, d_hat_centered, gate_slope
):
    gate_flip = transposed(w_gate[...])
    gain_col, bias_col = column(gain[...]), column(bias[...])
    out_gain_col = column(out_gain[...])
    for row in range(pair.shape[0]):
        normed, _ = norm_rows(jnp.transpose(pair[row].astype(F32)))
        zln = (normed * gain_col + bias_col).astype(BF16)
        gate = sigmoid(dot(gate_flip, zln, 1, 0))
        cot = jnp.transpose(cotangent[row].astype(F32))
        d_scaled = (cot * gate).astype(BF16)
        d_hat = dot(w_out[...], d_scaled, 1, 0) * out_gain_col
        d_hat_centered[row] = d_hat - jnp.mean(d_hat, axis=0, keepdims=True)
        gate_slope[row] = cot * gate * (1.0 - gate)


def spread(panel, wide):
    wide[...] = panel[...].astype(F32).reshape(wide.shape)


def wide_places(panel, count, back):
    devices, depth, _ = panel.shape
    for rank, device in enumerate(wide_order(devices, count, back)):
        yield rank, slice(device * depth, (device + 1) * depth)


def sort_left_kernel(*refs):
    *pieces, left_all, left_wide = refs
    block, left_rows, _ = left_all.shape
    depth = pieces[0].shape[0]
    for step, piece in enumerate(pieces):
        start = pl.multiple_of(partner(step, len(pieces)) * depth, depth)
        left_wide[pl.ds(start, depth), :] = piece[...].astype(F32)
    for h in range(block):
        left_all[h] = left_wide[pl.ds(h, left_rows, stride=block), :].astype(BF16)


def tri_kernel(right_panel, left_all, after, products, right_all, left_wide, right_wide):
    del after
    block, left_rows, _ = left_all.shape
    right_rows = right_all.shape[1]
    for rank, place in wide_places(right_panel, products.shape[0], False):
        right_wide[place, :] = right_panel[rank].astype(F32)
    for h in range(block):
        right = right_wide[pl.ds(h, right_rows, stride=block), :].astype(BF16)
        right_all[h] = right
        left_wide[pl.ds(h, left_rows, stride=block), :] = dot(left_all[h], right, 1, 1)
    products[...] = left_wide[...].astype(BF16).reshape(products.shape)


def cell_row(ref, row, rows):
    count, depth, width = ref.shape
    block = depth // rows
    return ref[:, row * block : (row + 1) * block, :].astype(F32).reshape(count * block, width)


def middle_kernel(products, d_hat_centered, d_products):
    rows = d_hat_centered.shape[0]
    count, depth, width = products.shape
    block = depth // rows
    for row in range(rows):
        tri_hat, inv_std = norm_rows(cell_row(products, row, rows))
        d_hat = d_hat_centered[row]
        cross = jnp.mean(d_hat * tri_hat, axis=0, keepdims=True)
        d_tri = inv_std * (d_hat - tri_hat * cross)
        d_products[:, row * block : (row + 1) * block, :] = d_tri.reshape(
            count, block, width
        ).astype(BF16)


def d_right_kernel(d_products, left_all, d_right_panel, d_tri_all, left_wide, right_wide):
    block, left_rows, _ = left_all.shape
    right_rows = right_wide.shape[0] // block
    spread(d_products, left_wide)
    for h in range(block):
        d_tri = left_wide[pl.ds(h, left_rows, stride=block), :].astype(BF16)
        d_tri_all[h] = d_tri
        right_wide[pl.ds(h, right_rows, stride=block), :] = dot(d_tri, left_all[h], 0, 0)
    for rank, place in wide_places(d_right_panel, d_products.shape[0], True):
        d_right_panel[rank] = right_wide[place, :].astype(BF16)


def d_left_kernel(d_tri_all, right_all, *refs):
    *pieces, left_wide = refs
    block, left_rows, _ = d_tri_all.shape
    for h in range(block):
        left_wide[pl.ds(h, left_rows, stride=block), :] = dot(d_tri_all[h], right_all[h], 1, 0)
    depth = pieces[0].shape[0]
    for step, piece in enumerate(pieces):
        start = pl.multiple_of(partner(step, len(pieces)) * depth, depth)
        piece[...] = left_wide[pl.ds(start, depth), :].astype(BF16)


def gate_back_kernel(products, gate_slope, out_gain, out_bias, w_out, d_gate_pre):
    rows = gate_slope.shape[0]
    out_flip = transposed(w_out[...])
    out_gain_col, out_bias_col = column(out_gain[...]), column(out_bias[...])
    for row in range(rows):
        tri_hat, _ = norm_rows(cell_row(products, row, rows))
        scaled = (tri_hat * out_gain_col + out_bias_col).astype(BF16)
        d_gate_pre[row] = (dot(out_flip, scaled, 1, 0) * gate_slope[row]).astype(BF16)


def slopes_kernel(
    pair, mask, gain, bias, w_proj, w_gate, after, slopes, normed_in, inv_in, in_gain, weights
):
    del after
    rows = pair.shape[0]
    hidden = w_proj.shape[1] // 4
    w_flip = transposed(w_proj[...])
    gain_col, bias_col = column(gain[...]), column(bias[...])
    in_gain[...] = gain_col
    weights[...] = jnp.concatenate([w_proj[...], w_gate[...]], axis=1)
    masks = cell_masks(mask, rows)
    for row in range(rows):
        normed, inv_std = norm_rows(jnp.transpose(pair[row].astype(F32)))
        normed_in[row] = normed.astype(normed_in.dtype)
        inv_in[row : row + 1] = inv_std
        zln = (normed * gain_col + bias_col).astype(BF16)
        proj = dot(w_flip, zln, 1, 0)
        for side in range(2):
            base = 2 * side * hidden
            sig = sigmoid(proj[base : base + hidden])
            masked = masks[row] * sig
            value = masked * (1.0 - sig) * proj[base + hidden : base + 2 * hidden]
            slopes[row, base : base + hidden, :] = value.astype(slopes.dtype)
            slopes[row, base + hidden : base + 2 * hidden, :] = masked.astype(slopes.dtype)


def sort_d_left_kernel(*refs):
    *pieces, d_left_panel = refs
    for step, piece in enumerate(pieces):
        d_left_panel[partner(step, len(pieces))] = piece[...]


def both_halves(blocks, count):
    order = wide_order(2 * count, count, True)
    return jnp.stack(
        [blocks[order.index(place)] + blocks[order.index(count + place)] for place in range(count)]
    )


def finish_kernel(
    d_right_panel, d_left_panel, slopes, d_gate_pre, normed_in, inv_in, gain_col, weights, grad
):
    rows = grad.shape[0]
    count, depth, width = d_left_panel.shape
    hidden = count * depth // rows
    for row in range(rows):
        d_right = cell_row(d_right_panel, row, rows)
        d_right = both_halves(d_right.reshape(2 * count, depth // rows, width), count)
        parts = []
        for side, d_value in enumerate((cell_row(d_left_panel, row, rows), d_right.reshape(hidden, width))):
            for base in (2 * side * hidden, (2 * side + 1) * hidden):
                slope = slopes[row, base : base + hidden, :].astype(F32)
                parts.append((d_value * slope).astype(BF16))
        parts.append(d_gate_pre[row])
        d_in = dot(weights[...], jnp.concatenate(parts, axis=0), 1, 0) * gain_col[...]
        normed = normed_in[row].astype(F32)
        mean_grad = jnp.mean(d_in, axis=0, keepdims=True)
        mean_cross = jnp.mean(d_in * normed, axis=0, keepdims=True)
        result = inv_in[row : row + 1] * (d_in - mean_grad - normed * mean_cross)
        grad[row] = jnp.transpose(result).astype(BF16)


def swap(values, count, back):
    groups = [wide_order(lax.axis_size("row"), count, back)]
    return lax.all_to_all(
        values, "row", split_axis=0, concat_axis=0, tiled=True, axis_index_groups=groups
    )


def swap_half(values, count):
    devices = range(lax.axis_size("row"))
    groups = [[d for d in devices if d // count == half] for half in range(len(devices) // count)]
    return lax.all_to_all(
        values, "row", split_axis=0, concat_axis=0, tiled=True, axis_index_groups=groups
    )


def swap_pieces(pieces):
    devices = range(lax.axis_size("row"))
    count = len(pieces)
    return [pieces[0]] + [
        lax.ppermute(pieces[step], "row", [(d, d ^ distance(step, count)) for d in devices])
        for step in range(1, count)
    ]


def kernel_shards(
    pair,
    cotangent,
    residue_mask,
    ln_in_gain,
    ln_in_bias,
    w_proj,
    w_gate,
    ln_out_gain,
    ln_out_bias,
    w_out,
):
    rows, width, channels = pair.shape
    hidden = w_out.shape[0]
    halves = 2
    devices = lax.axis_size("row")
    count = devices // halves
    block = hidden // count
    left_rows, right_rows = rows * count, rows * devices
    shape = jax.ShapeDtypeStruct
    panel = shape((count, rows * block, width), BF16)
    wide_panel = shape((devices, rows * block, width), BF16)
    mask = residue_mask.reshape(1, width)
    gain, bias = ln_in_gain.reshape(1, channels), ln_in_bias.reshape(1, channels)
    out_gain, out_bias = ln_out_gain.reshape(1, hidden), ln_out_bias.reshape(1, hidden)
    cells = rows * width
    piece = shape((rows * block, width), BF16)
    left_panel = pltpu.VMEM(panel.shape, BF16)
    left_wide = pltpu.VMEM((left_rows * block, width), F32)
    right_wide = pltpu.VMEM((right_rows * block, width), F32)
    (own_right,) = call(
        project_right_kernel,
        "project_right",
        [wide_panel],
        [pair, mask, gain, bias, w_proj],
        fetched=range(5),
        columns={4: pl.ds(2 * hidden, 2 * hidden)},
        flops=2 * cells * channels * 2 * hidden,
        limit=64 * 1024 * 1024 - 640 * 1024,
    )
    right_panel = swap(own_right, count, False)
    pieces = call(
        project_left_kernel,
        "project_left",
        [piece] * count,
        [pair, mask, gain, bias, w_proj, own_right],
        fetched=range(5),
        columns={4: pl.ds(0, 2 * hidden)},
        unread=(5,),
        scratch=[left_panel],
        flops=2 * cells * channels * 2 * hidden,
    )
    pieces = swap_pieces(pieces)
    (left_all,) = call(
        sort_left_kernel,
        "sort_left",
        [shape((block, left_rows, width), BF16)],
        pieces,
        scratch=[left_wide],
    )
    d_hat_centered, gate_slope = call(
        prepare_kernel,
        "prepare",
        [shape((rows, hidden, width), F32), shape((rows, channels, width), F32)],
        [pair, cotangent, gain, bias, w_gate, out_gain, w_out],
        fetched=range(7),
        flops=2 * cells * channels * 2 * hidden,
    )
    products, right_all = call(
        tri_kernel,
        "tri",
        [panel, shape((block, right_rows, width), BF16)],
        [right_panel, left_all, d_hat_centered],
        unread=(2,),
        scratch=[left_wide, right_wide],
        flops=2 * block * left_rows * width * right_rows,
    )
    products = swap_half(products, count)
    (d_products,) = call(
        middle_kernel,
        "middle",
        [panel],
        [products, d_hat_centered],
        flops=20 * cells * hidden,
    )
    d_products = swap_half(d_products, count)
    d_right_panel, d_tri_all = call(
        d_right_kernel,
        "d_right",
        [wide_panel, shape((block, left_rows, width), BF16)],
        [d_products, left_all],
        scratch=[left_wide, right_wide],
        flops=2 * block * left_rows * width * right_rows,
    )
    d_right_panel = swap(d_right_panel, count, True)
    d_pieces = call(
        d_left_kernel,
        "d_left",
        [piece] * count,
        [d_tri_all, right_all],
        scratch=[left_wide],
        flops=2 * block * left_rows * width * right_rows,
    )
    d_pieces = swap_pieces(d_pieces)
    (d_left_panel,) = call(sort_d_left_kernel, "sort_d_left", [panel], d_pieces)
    (d_gate_pre,) = call(
        gate_back_kernel,
        "gate_back",
        [shape((rows, channels, width), BF16)],
        [products, gate_slope, out_gain, out_bias, w_out],
        fetched=range(2, 5),
        flops=2 * cells * channels * hidden,
    )
    slopes, normed_in, inv_in, gain_col, weights = call(
        slopes_kernel,
        "slopes",
        [
            shape((rows, 4 * hidden, width), BF16),
            shape((rows, channels, width), BF16),
            shape((rows, width), F32),
            shape((channels, channels), F32),
            shape((channels, 4 * hidden + channels), BF16),
        ],
        [pair, mask, gain, bias, w_proj, w_gate, d_gate_pre],
        fetched=range(6),
        unread=(6,),
        flops=2 * cells * channels * 4 * hidden,
    )
    (grad,) = call(
        finish_kernel,
        "finish",
        [shape(pair.shape, BF16)],
        [
            d_right_panel,
            d_left_panel,
            slopes,
            d_gate_pre,
            normed_in,
            inv_in,
            gain_col,
            weights,
        ],
        flops=2 * cells * channels * 4 * hidden,
    )
    return grad


def normalize(values, reduce_axis):
    mean_value = jnp.mean(values, axis=reduce_axis, keepdims=True)
    centered = values - mean_value
    variance = jnp.mean(centered * centered, axis=reduce_axis, keepdims=True)
    inv_std = lax.rsqrt(variance + 1e-05)
    return (centered * inv_std, inv_std)


def norm_backward(upstream, normed, inv_std, reduce_axis):
    mean_grad = jnp.mean(upstream, axis=reduce_axis, keepdims=True)
    mean_cross = jnp.mean(upstream * normed, axis=reduce_axis, keepdims=True)
    return inv_std * (upstream - mean_grad - normed * mean_cross)


def shards(
    pair,
    cotangent,
    residue_mask,
    ln_in_gain,
    ln_in_bias,
    w_proj,
    w_gate,
    ln_out_gain,
    ln_out_bias,
    w_out,
):
    local_rows = pair.shape[0]
    local_cols = pair.shape[1]
    hidden = w_out.shape[0]
    chan_index = lax.axis_index("chan")
    row_start = lax.axis_index("row") * local_rows
    col_start = chan_index * local_cols
    mask_float = residue_mask.astype(jnp.float32)
    row_mask = lax.dynamic_slice_in_dim(mask_float, row_start, local_rows)
    col_mask = lax.dynamic_slice_in_dim(mask_float, col_start, local_cols)
    cell_mask = (row_mask[:, None] * col_mask[None, :])[None]
    normed, inv_std = normalize(pair.astype(jnp.float32), -1)
    normed_pair = (normed * ln_in_gain + ln_in_bias).astype(jnp.bfloat16)
    projected = jnp.einsum("rmc,ch->hrm", normed_pair, w_proj, preferred_element_type=jnp.float32)
    left_panel = (
        cell_mask * jax.nn.sigmoid(projected[:hidden]) * projected[hidden : 2 * hidden]
    ).astype(jnp.bfloat16)
    right_panel = (
        cell_mask * jax.nn.sigmoid(projected[2 * hidden : 3 * hidden]) * projected[3 * hidden :]
    ).astype(jnp.bfloat16)
    panels = lax.all_to_all(
        jnp.stack([left_panel, right_panel]), "row", split_axis=1, concat_axis=2, tiled=True
    )
    left_all = panels[0]
    right_all = panels[1]
    right_rows = lax.all_to_all(right_all, "chan", split_axis=1, concat_axis=2, tiled=True)
    partner = right_rows
    tri_part = jnp.einsum(
        "gik,gjk->gij",
        lax.all_gather(left_all, "chan", axis=2, tiled=True),
        partner,
        preferred_element_type=jnp.float32,
    ).astype(jnp.bfloat16)
    tri_cells = lax.all_to_all(tri_part, "row", split_axis=1, concat_axis=0, tiled=True)
    tri_hat, inv_tri = normalize(tri_cells.astype(jnp.float32), 0)
    scaled = (tri_hat * ln_out_gain[:, None, None] + ln_out_bias[:, None, None]).astype(
        jnp.bfloat16
    )
    proj_out = jnp.einsum("hrm,hc->rmc", scaled, w_out, preferred_element_type=jnp.float32)
    gate_value = jax.nn.sigmoid(
        jnp.einsum("rmc,cd->rmd", normed_pair, w_gate, preferred_element_type=jnp.float32)
    )
    cot_float = cotangent.astype(jnp.float32)
    d_gate_pre = (cot_float * proj_out * gate_value * (1.0 - gate_value)).astype(jnp.bfloat16)
    d_scaled = (cot_float * gate_value).astype(jnp.bfloat16)
    d_hat = jnp.einsum("rmc,hc->hrm", d_scaled, w_out, preferred_element_type=jnp.float32)
    d_hat = d_hat * ln_out_gain[:, None, None]
    d_tri = norm_backward(d_hat, tri_hat, inv_tri, 0).astype(jnp.bfloat16)
    d_tri_all = lax.all_to_all(d_tri, "row", split_axis=0, concat_axis=1, tiled=True)
    panel_piece = lax.all_gather(d_tri_all, "chan", axis=2, tiled=True)
    partner = right_all
    d_left = jnp.einsum("gij,gjk->gik", panel_piece, partner, preferred_element_type=jnp.float32)
    contribution = jnp.einsum(
        "gij,gik->gjk", panel_piece, left_all, preferred_element_type=jnp.float32
    )
    d_right = contribution
    d_left, d_right = (d_left, d_right)
    d_stack = jnp.stack([d_left, d_right]).astype(jnp.bfloat16)
    d_panels = lax.all_to_all(d_stack, "row", split_axis=2, concat_axis=1, tiled=True)

    def gating(d_value, gate_proj, value_proj):
        sigmoid_val = jax.nn.sigmoid(gate_proj)
        masked_grad = d_value.astype(jnp.float32) * cell_mask
        return (
            masked_grad * value_proj * sigmoid_val * (1.0 - sigmoid_val),
            masked_grad * sigmoid_val,
        )

    gate_left, value_left = gating(d_panels[0], projected[:hidden], projected[hidden : 2 * hidden])
    gate_right, value_right = gating(
        d_panels[1], projected[2 * hidden : 3 * hidden], projected[3 * hidden :]
    )
    d_proj = jnp.concatenate([gate_left, value_left, gate_right, value_right], axis=0).astype(
        jnp.bfloat16
    )
    d_normed = jnp.einsum("hrm,ch->rmc", d_proj, w_proj, preferred_element_type=jnp.float32)
    d_normed = d_normed + jnp.einsum(
        "rmd,cd->rmc", d_gate_pre, w_gate, preferred_element_type=jnp.float32
    )
    d_input = d_normed * ln_in_gain
    return norm_backward(d_input, normed, inv_std, -1).astype(jnp.bfloat16)


def solution(mesh):
    fits = mesh.shape["chan"] == 1 and mesh.shape["row"] in (8, 16)
    return jax.shard_map(
        kernel_shards if fits else shards,
        mesh=mesh,
        in_specs=(
            P(("grp", "row"), "chan", None),
            P(("grp", "row"), "chan", None),
            P("grp"),
            P(),
            P(),
            P(),
            P(),
            P(),
            P(),
            P(),
        ),
        out_specs=P(("grp", "row"), "chan", None),
        check_vma=False,
    )
```

```python
import functools

import jax
import jax.numpy as jnp
from jax import lax
from jax.experimental import pallas as pl
from jax.experimental.pallas import tpu as pltpu
from jax.sharding import PartitionSpec as P

F32 = jnp.float32
BF16 = jnp.bfloat16
VMEM_LIMIT = 16 * 1024 * 1024


def dot(lhs, rhs, lhs_dim, rhs_dim):
    return lax.dot_general(
        lhs, rhs, (((lhs_dim,), (rhs_dim,)), ((), ())), preferred_element_type=F32
    )


def transposed(matrix):
    return jnp.transpose(matrix.astype(F32)).astype(BF16)


def sigmoid(values):
    return 1.0 / (1.0 + jnp.exp(-values))


def column(row):
    size = row.shape[1]
    return jnp.transpose(jnp.broadcast_to(row, (size, size)))


def norm_rows(values):
    centered = values - jnp.mean(values, axis=0, keepdims=True)
    variance = jnp.mean(centered * centered, axis=0, keepdims=True)
    inv_std = lax.rsqrt(variance + 1e-05)
    return centered * inv_std, inv_std


def call(
    kernel, name, outs, args, fetched=(), unread=(), scratch=(), flops=0, limit=VMEM_LIMIT
):
    moved = sum(a.size * a.dtype.itemsize for a in args) + sum(
        o.size * jnp.dtype(o.dtype).itemsize for o in outs
    )
    n_args, n_outs, n_fetched = len(args), len(outs), len(fetched)

    def body(*refs):
        ins = list(refs[:n_args])
        rest = refs[n_args + n_outs :]
        copies = []
        for n, place in enumerate(fetched):
            copies.append(pltpu.make_async_copy(ins[place], rest[n], rest[n_fetched].at[n]))
            ins[place] = rest[n]
        for copy in copies:
            copy.start()
        for copy in copies:
            copy.wait()
        kernel(*ins, *refs[n_args : n_args + n_outs], *rest[n_fetched + (n_fetched > 0) :])

    buffers = [pltpu.VMEM(args[place].shape, args[place].dtype) for place in fetched]
    if fetched:
        buffers.append(pltpu.SemaphoreType.DMA((n_fetched,)))
    return pl.pallas_call(
        body,
        name=name,
        out_shape=outs,
        in_specs=[
            pl.BlockSpec(
                memory_space=pltpu.HBM if n in fetched else pl.ANY if n in unread else pltpu.VMEM
            )
            for n in range(n_args)
        ],
        out_specs=[pl.BlockSpec(memory_space=pltpu.VMEM) for _ in outs],
        scratch_shapes=buffers + list(scratch),
        compiler_params=pltpu.CompilerParams(vmem_limit_bytes=limit),
        cost_estimate=pl.CostEstimate(flops=flops, bytes_accessed=moved, transcendentals=0),
    )(*args)


def cell_masks(mask, rows):
    columns = mask[...].astype(F32)
    shape = (rows, columns.shape[1])
    first = lax.axis_index("row") * rows
    own = lax.broadcasted_iota(jnp.int32, shape, 1) == (
        lax.broadcasted_iota(jnp.int32, shape, 0) + first
    )
    row_mask = jnp.sum(jnp.where(own, columns, 0.0), axis=1, keepdims=True)
    cells = row_mask * columns
    return [cells[row : row + 1] for row in range(rows)]


def wide_order(devices, count, back):
    order = []
    for place in range(count):
        if back:
            order += [place ^ (count // 2), count + place]
        else:
            order += [count + (place ^ 2), place ^ (count // 2)]
    return order


def half_order(count):
    return [*range(0, count, 2), *range(1, count, 2)]


def distance(step, count):
    far = sorted(range(3, count), key=lambda apart: -(apart // 2))
    return [*range(min(3, count)), *far][step]


def partner(step, count):
    return lax.rem(lax.axis_index("row"), count) ^ distance(step, count)


def gated_rows(pair, mask, gain, bias, w_proj, side):
    rows = pair.shape[0]
    hidden = w_proj.shape[1] // 4
    w_flip = transposed(w_proj[:, 2 * side * hidden : 2 * (side + 1) * hidden])
    gain_col, bias_col = column(gain[...]), column(bias[...])
    masks = cell_masks(mask, rows)
    for row in range(rows):
        normed, _ = norm_rows(jnp.transpose(pair[row].astype(F32)))
        zln = (normed * gain_col + bias_col).astype(BF16)
        proj = dot(w_flip, zln, 1, 0)
        yield row, masks[row] * sigmoid(proj[:hidden]) * proj[hidden:]


def project_right_kernel(pair, mask, gain, bias, w_proj, right_panel):
    rows = pair.shape[0]
    devices, depth, width = right_panel.shape
    block = depth // rows
    count = w_proj.shape[1] // 4 // block
    for row, right in gated_rows(pair, mask, gain, bias, w_proj, 1):
        right = right.reshape(count, block, width).astype(BF16)
        for rank in range(devices):
            place = wide_order(devices, count, False)[rank] % count
            right_panel[rank, row * block : (row + 1) * block, :] = right[place]


def project_left_kernel(pair, mask, gain, bias, w_proj, after, *refs):
    del after
    *pieces, left_panel = refs
    rows = pair.shape[0]
    count, depth, width = left_panel.shape
    block = depth // rows
    for row, left in gated_rows(pair, mask, gain, bias, w_proj, 0):
        left = left.reshape(count, block, width).astype(BF16)
        left_panel[:, row * block : (row + 1) * block, :] = left
    for step, piece in enumerate(pieces):
        piece[...] = left_panel[partner(step, count)]


def prepare_kernel(
    pair, cotangent, gain, bias, w_gate, out_gain, w_out, d_hat_centered, gate_slope
):
    gate_flip = transposed(w_gate[...])
    gain_col, bias_col = column(gain[...]), column(bias[...])
    out_gain_col = column(out_gain[...])
    for row in range(pair.shape[0]):
        normed, _ = norm_rows(jnp.transpose(pair[row].astype(F32)))
        zln = (normed * gain_col + bias_col).astype(BF16)
        gate = sigmoid(dot(gate_flip, zln, 1, 0))
        cot = jnp.transpose(cotangent[row].astype(F32))
        d_scaled = (cot * gate).astype(BF16)
        d_hat = dot(w_out[...], d_scaled, 1, 0) * out_gain_col
        d_hat_centered[row] = d_hat - jnp.mean(d_hat, axis=0, keepdims=True)
        gate_slope[row] = cot * gate * (1.0 - gate)


def half_places(panel):
    count, depth, _ = panel.shape
    for rank, place in enumerate(half_order(count)):
        yield rank, slice(place * depth, (place + 1) * depth)


def wide_places(panel, count, back):
    devices, depth, _ = panel.shape
    for rank, device in enumerate(wide_order(devices, count, back)):
        yield rank, slice(device * depth, (device + 1) * depth)


def sort_left_kernel(*refs):
    *pieces, left_all, left_wide = refs
    block, left_rows, _ = left_all.shape
    depth = pieces[0].shape[0]
    for step, piece in enumerate(pieces):
        start = pl.multiple_of(partner(step, len(pieces)) * depth, depth)
        left_wide[pl.ds(start, depth), :] = piece[...].astype(F32)
    for h in range(block):
        left_all[h] = left_wide[pl.ds(h, left_rows, stride=block), :].astype(BF16)


def tri_kernel(right_panel, left_all, after, products, right_all, left_wide, right_wide):
    del after
    block, left_rows, _ = left_all.shape
    right_rows = right_all.shape[1]
    for rank, place in wide_places(right_panel, products.shape[0], False):
        right_wide[place, :] = right_panel[rank].astype(F32)
    for h in range(block):
        right = right_wide[pl.ds(h, right_rows, stride=block), :].astype(BF16)
        right_all[h] = right
        left_wide[pl.ds(h, left_rows, stride=block), :] = dot(left_all[h], right, 1, 1)
    for rank, place in half_places(products):
        products[rank] = left_wide[place, :].astype(BF16)


def cell_row(ref, row, rows, order=None):
    count, depth, width = ref.shape
    block = depth // rows
    part = ref[:, row * block : (row + 1) * block, :].astype(F32)
    if order:
        part = jnp.stack([part[order.index(place)] for place in range(count)])
    return part.reshape(count * block, width)


def middle_kernel(products, d_hat_centered, d_products):
    rows = d_hat_centered.shape[0]
    count, depth, width = products.shape
    block = depth // rows
    order = half_order(count)
    for row in range(rows):
        tri_hat, inv_std = norm_rows(cell_row(products, row, rows, order))
        d_hat = d_hat_centered[row]
        cross = jnp.mean(d_hat * tri_hat, axis=0, keepdims=True)
        d_tri = inv_std * (d_hat - tri_hat * cross)
        d_tri = d_tri.reshape(count, block, width).astype(BF16)
        for rank, place in enumerate(order):
            d_products[rank, row * block : (row + 1) * block, :] = d_tri[place]


def d_right_kernel(d_products, left_all, d_right_panel, d_tri_all, left_wide, right_wide):
    block, left_rows, _ = left_all.shape
    right_rows = right_wide.shape[0] // block
    for rank, place in half_places(d_products):
        left_wide[place, :] = d_products[rank].astype(F32)
    for h in range(block):
        d_tri = left_wide[pl.ds(h, left_rows, stride=block), :].astype(BF16)
        d_tri_all[h] = d_tri
        right_wide[pl.ds(h, right_rows, stride=block), :] = dot(d_tri, left_all[h], 0, 0)
    for rank, place in wide_places(d_right_panel, d_products.shape[0], True):
        d_right_panel[rank] = right_wide[place, :].astype(BF16)


def d_left_kernel(d_tri_all, right_all, *refs):
    *pieces, left_wide = refs
    block, left_rows, _ = d_tri_all.shape
    for h in range(block):
        left_wide[pl.ds(h, left_rows, stride=block), :] = dot(d_tri_all[h], right_all[h], 1, 0)
    depth = pieces[0].shape[0]
    for step, piece in enumerate(pieces):
        start = pl.multiple_of(partner(step, len(pieces)) * depth, depth)
        piece[...] = left_wide[pl.ds(start, depth), :].astype(BF16)


def gate_back_kernel(products, gate_slope, out_gain, out_bias, w_out, d_gate_pre):
    rows = gate_slope.shape[0]
    out_flip = transposed(w_out[...])
    out_gain_col, out_bias_col = column(out_gain[...]), column(out_bias[...])
    for row in range(rows):
        tri_hat, _ = norm_rows(cell_row(products, row, rows, half_order(products.shape[0])))
        scaled = (tri_hat * out_gain_col + out_bias_col).astype(BF16)
        d_gate_pre[row] = (dot(out_flip, scaled, 1, 0) * gate_slope[row]).astype(BF16)


def slopes_kernel(
    pair, mask, gain, bias, w_proj, w_gate, after, slopes, normed_in, inv_in, in_gain, weights
):
    del after
    rows = pair.shape[0]
    hidden = w_proj.shape[1] // 4
    w_flip = transposed(w_proj[...])
    gain_col, bias_col = column(gain[...]), column(bias[...])
    in_gain[...] = gain_col
    weights[...] = jnp.concatenate([w_proj[...], w_gate[...]], axis=1)
    masks = cell_masks(mask, rows)
    for row in range(rows):
        normed, inv_std = norm_rows(jnp.transpose(pair[row].astype(F32)))
        normed_in[row] = normed.astype(normed_in.dtype)
        inv_in[row : row + 1] = inv_std
        zln = (normed * gain_col + bias_col).astype(BF16)
        proj = dot(w_flip, zln, 1, 0)
        for side in range(2):
            base = 2 * side * hidden
            sig = sigmoid(proj[base : base + hidden])
            masked = masks[row] * sig
            value = masked * (1.0 - sig) * proj[base + hidden : base + 2 * hidden]
            slopes[row, base : base + hidden, :] = value.astype(slopes.dtype)
            slopes[row, base + hidden : base + 2 * hidden, :] = masked.astype(slopes.dtype)


def sort_d_left_kernel(*refs):
    *pieces, d_left_panel = refs
    for step, piece in enumerate(pieces):
        d_left_panel[partner(step, len(pieces))] = piece[...]


def both_halves(blocks, count):
    order = wide_order(2 * count, count, True)
    return jnp.stack(
        [blocks[order.index(place)] + blocks[order.index(count + place)] for place in range(count)]
    )


def finish_kernel(
    d_right_panel, d_left_panel, slopes, d_gate_pre, normed_in, inv_in, gain_col, weights, grad
):
    rows = grad.shape[0]
    count, depth, width = d_left_panel.shape
    hidden = count * depth // rows
    for row in range(rows):
        d_right = cell_row(d_right_panel, row, rows)
        d_right = both_halves(d_right.reshape(2 * count, depth // rows, width), count)
        parts = []
        for side, d_value in enumerate((cell_row(d_left_panel, row, rows), d_right.reshape(hidden, width))):
            for base in (2 * side * hidden, (2 * side + 1) * hidden):
                slope = slopes[row, base : base + hidden, :].astype(F32)
                parts.append((d_value * slope).astype(BF16))
        parts.append(d_gate_pre[row])
        d_in = dot(weights[...], jnp.concatenate(parts, axis=0), 1, 0) * gain_col[...]
        normed = normed_in[row].astype(F32)
        mean_grad = jnp.mean(d_in, axis=0, keepdims=True)
        mean_cross = jnp.mean(d_in * normed, axis=0, keepdims=True)
        result = inv_in[row : row + 1] * (d_in - mean_grad - normed * mean_cross)
        grad[row] = jnp.transpose(result).astype(BF16)


def swap(values, count, back):
    groups = [wide_order(lax.axis_size("row"), count, back)]
    return lax.all_to_all(
        values, "row", split_axis=0, concat_axis=0, tiled=True, axis_index_groups=groups
    )


def swap_half(values, count):
    devices = range(lax.axis_size("row"))
    order = half_order(count)
    groups = [[start + place for place in order] for start in range(0, len(devices), count)]
    return lax.all_to_all(
        values, "row", split_axis=0, concat_axis=0, tiled=True, axis_index_groups=groups
    )


def swap_pieces(pieces):
    devices = range(lax.axis_size("row"))
    count = len(pieces)
    return [pieces[0]] + [
        lax.ppermute(pieces[step], "row", [(d, d ^ distance(step, count)) for d in devices])
        for step in range(1, count)
    ]


def kernel_shards(
    pair,
    cotangent,
    residue_mask,
    ln_in_gain,
    ln_in_bias,
    w_proj,
    w_gate,
    ln_out_gain,
    ln_out_bias,
    w_out,
):
    rows, width, channels = pair.shape
    hidden = w_out.shape[0]
    halves = 2
    devices = lax.axis_size("row")
    count = devices // halves
    block = hidden // count
    left_rows, right_rows = rows * count, rows * devices
    shape = jax.ShapeDtypeStruct
    panel = shape((count, rows * block, width), BF16)
    wide_panel = shape((devices, rows * block, width), BF16)
    mask = residue_mask.reshape(1, width)
    gain, bias = ln_in_gain.reshape(1, channels), ln_in_bias.reshape(1, channels)
    out_gain, out_bias = ln_out_gain.reshape(1, hidden), ln_out_bias.reshape(1, hidden)
    cells = rows * width
    piece = shape((rows * block, width), BF16)
    left_panel = pltpu.VMEM(panel.shape, BF16)
    left_wide = pltpu.VMEM((left_rows * block, width), F32)
    right_wide = pltpu.VMEM((right_rows * block, width), F32)
    (own_right,) = call(
        project_right_kernel,
        "project_right",
        [wide_panel],
        [pair, mask, gain, bias, w_proj],
        fetched=range(5),
        flops=2 * cells * channels * 2 * hidden,
        limit=64 * 1024 * 1024 - 640 * 1024,
    )
    right_panel = swap(own_right, count, False)
    pieces = call(
        project_left_kernel,
        "project_left",
        [piece] * count,
        [pair, mask, gain, bias, w_proj, own_right],
        fetched=range(5),
        unread=(5,),
        scratch=[left_panel],
        flops=2 * cells * channels * 2 * hidden,
    )
    pieces = swap_pieces(pieces)
    (left_all,) = call(
        sort_left_kernel,
        "sort_left",
        [shape((block, left_rows, width), BF16)],
        pieces,
        scratch=[left_wide],
    )
    d_hat_centered, gate_slope = call(
        prepare_kernel,
        "prepare",
        [shape((rows, hidden, width), F32), shape((rows, channels, width), F32)],
        [pair, cotangent, gain, bias, w_gate, out_gain, w_out],
        fetched=range(7),
        flops=2 * cells * channels * 2 * hidden,
    )
    products, right_all = call(
        tri_kernel,
        "tri",
        [panel, shape((block, right_rows, width), BF16)],
        [right_panel, left_all, d_hat_centered],
        unread=(2,),
        scratch=[left_wide, right_wide],
        flops=2 * block * left_rows * width * right_rows,
    )
    products = swap_half(products, count)
    (d_products,) = call(
        middle_kernel,
        "middle",
        [panel],
        [products, d_hat_centered],
        flops=20 * cells * hidden,
    )
    d_products = swap_half(d_products, count)
    d_right_panel, d_tri_all = call(
        d_right_kernel,
        "d_right",
        [wide_panel, shape((block, left_rows, width), BF16)],
        [d_products, left_all],
        scratch=[left_wide, right_wide],
        flops=2 * block * left_rows * width * right_rows,
    )
    d_right_panel = swap(d_right_panel, count, True)
    d_pieces = call(
        d_left_kernel,
        "d_left",
        [piece] * count,
        [d_tri_all, right_all],
        scratch=[left_wide],
        flops=2 * block * left_rows * width * right_rows,
    )
    d_pieces = swap_pieces(d_pieces)
    (d_left_panel,) = call(sort_d_left_kernel, "sort_d_left", [panel], d_pieces)
    (d_gate_pre,) = call(
        gate_back_kernel,
        "gate_back",
        [shape((rows, channels, width), BF16)],
        [products, gate_slope, out_gain, out_bias, w_out],
        fetched=range(2, 5),
        flops=2 * cells * channels * hidden,
    )
    slopes, normed_in, inv_in, gain_col, weights = call(
        slopes_kernel,
        "slopes",
        [
            shape((rows, 4 * hidden, width), BF16),
            shape((rows, channels, width), BF16),
            shape((rows, width), F32),
            shape((channels, channels), F32),
            shape((channels, 4 * hidden + channels), BF16),
        ],
        [pair, mask, gain, bias, w_proj, w_gate, d_gate_pre],
        fetched=range(6),
        unread=(6,),
        flops=2 * cells * channels * 4 * hidden,
    )
    (grad,) = call(
        finish_kernel,
        "finish",
        [shape(pair.shape, BF16)],
        [
            d_right_panel,
            d_left_panel,
            slopes,
            d_gate_pre,
            normed_in,
            inv_in,
            gain_col,
            weights,
        ],
        flops=2 * cells * channels * 4 * hidden,
    )
    return grad


def normalize(values, reduce_axis):
    mean_value = jnp.mean(values, axis=reduce_axis, keepdims=True)
    centered = values - mean_value
    variance = jnp.mean(centered * centered, axis=reduce_axis, keepdims=True)
    inv_std = lax.rsqrt(variance + 1e-05)
    return (centered * inv_std, inv_std)


def norm_backward(upstream, normed, inv_std, reduce_axis):
    mean_grad = jnp.mean(upstream, axis=reduce_axis, keepdims=True)
    mean_cross = jnp.mean(upstream * normed, axis=reduce_axis, keepdims=True)
    return inv_std * (upstream - mean_grad - normed * mean_cross)


def shards(
    pair,
    cotangent,
    residue_mask,
    ln_in_gain,
    ln_in_bias,
    w_proj,
    w_gate,
    ln_out_gain,
    ln_out_bias,
    w_out,
):
    local_rows = pair.shape[0]
    local_cols = pair.shape[1]
    hidden = w_out.shape[0]
    chan_index = lax.axis_index("chan")
    row_start = lax.axis_index("row") * local_rows
    col_start = chan_index * local_cols
    mask_float = residue_mask.astype(jnp.float32)
    row_mask = lax.dynamic_slice_in_dim(mask_float, row_start, local_rows)
    col_mask = lax.dynamic_slice_in_dim(mask_float, col_start, local_cols)
    cell_mask = (row_mask[:, None] * col_mask[None, :])[None]
    normed, inv_std = normalize(pair.astype(jnp.float32), -1)
    normed_pair = (normed * ln_in_gain + ln_in_bias).astype(jnp.bfloat16)
    projected = jnp.einsum("rmc,ch->hrm", normed_pair, w_proj, preferred_element_type=jnp.float32)
    left_panel = (
        cell_mask * jax.nn.sigmoid(projected[:hidden]) * projected[hidden : 2 * hidden]
    ).astype(jnp.bfloat16)
    right_panel = (
        cell_mask * jax.nn.sigmoid(projected[2 * hidden : 3 * hidden]) * projected[3 * hidden :]
    ).astype(jnp.bfloat16)
    panels = lax.all_to_all(
        jnp.stack([left_panel, right_panel]), "row", split_axis=1, concat_axis=2, tiled=True
    )
    left_all = panels[0]
    right_all = panels[1]
    right_rows = lax.all_to_all(right_all, "chan", split_axis=1, concat_axis=2, tiled=True)
    partner = right_rows
    tri_part = jnp.einsum(
        "gik,gjk->gij",
        lax.all_gather(left_all, "chan", axis=2, tiled=True),
        partner,
        preferred_element_type=jnp.float32,
    ).astype(jnp.bfloat16)
    tri_cells = lax.all_to_all(tri_part, "row", split_axis=1, concat_axis=0, tiled=True)
    tri_hat, inv_tri = normalize(tri_cells.astype(jnp.float32), 0)
    scaled = (tri_hat * ln_out_gain[:, None, None] + ln_out_bias[:, None, None]).astype(
        jnp.bfloat16
    )
    proj_out = jnp.einsum("hrm,hc->rmc", scaled, w_out, preferred_element_type=jnp.float32)
    gate_value = jax.nn.sigmoid(
        jnp.einsum("rmc,cd->rmd", normed_pair, w_gate, preferred_element_type=jnp.float32)
    )
    cot_float = cotangent.astype(jnp.float32)
    d_gate_pre = (cot_float * proj_out * gate_value * (1.0 - gate_value)).astype(jnp.bfloat16)
    d_scaled = (cot_float * gate_value).astype(jnp.bfloat16)
    d_hat = jnp.einsum("rmc,hc->hrm", d_scaled, w_out, preferred_element_type=jnp.float32)
    d_hat = d_hat * ln_out_gain[:, None, None]
    d_tri = norm_backward(d_hat, tri_hat, inv_tri, 0).astype(jnp.bfloat16)
    d_tri_all = lax.all_to_all(d_tri, "row", split_axis=0, concat_axis=1, tiled=True)
    panel_piece = lax.all_gather(d_tri_all, "chan", axis=2, tiled=True)
    partner = right_all
    d_left = jnp.einsum("gij,gjk->gik", panel_piece, partner, preferred_element_type=jnp.float32)
    contribution = jnp.einsum(
        "gij,gik->gjk", panel_piece, left_all, preferred_element_type=jnp.float32
    )
    d_right = contribution
    d_left, d_right = (d_left, d_right)
    d_stack = jnp.stack([d_left, d_right]).astype(jnp.bfloat16)
    d_panels = lax.all_to_all(d_stack, "row", split_axis=2, concat_axis=1, tiled=True)

    def gating(d_value, gate_proj, value_proj):
        sigmoid_val = jax.nn.sigmoid(gate_proj)
        masked_grad = d_value.astype(jnp.float32) * cell_mask
        return (
            masked_grad * value_proj * sigmoid_val * (1.0 - sigmoid_val),
            masked_grad * sigmoid_val,
        )

    gate_left, value_left = gating(d_panels[0], projected[:hidden], projected[hidden : 2 * hidden])
    gate_right, value_right = gating(
        d_panels[1], projected[2 * hidden : 3 * hidden], projected[3 * hidden :]
    )
    d_proj = jnp.concatenate([gate_left, value_left, gate_right, value_right], axis=0).astype(
        jnp.bfloat16
    )
    d_normed = jnp.einsum("hrm,ch->rmc", d_proj, w_proj, preferred_element_type=jnp.float32)
    d_normed = d_normed + jnp.einsum(
        "rmd,cd->rmc", d_gate_pre, w_gate, preferred_element_type=jnp.float32
    )
    d_input = d_normed * ln_in_gain
    return norm_backward(d_input, normed, inv_std, -1).astype(jnp.bfloat16)


def solution(mesh):
    fits = mesh.shape["chan"] == 1 and mesh.shape["row"] in (8, 16)
    return jax.shard_map(
        kernel_shards if fits else shards,
        mesh=mesh,
        in_specs=(
            P(("grp", "row"), "chan", None),
            P(("grp", "row"), "chan", None),
            P("grp"),
            P(),
            P(),
            P(),
            P(),
            P(),
            P(),
            P(),
        ),
        out_specs=P(("grp", "row"), "chan", None),
        check_vma=False,
    )
```

```python
import functools

import jax
import jax.numpy as jnp
from jax import lax
from jax.experimental import pallas as pl
from jax.experimental.pallas import tpu as pltpu
from jax.sharding import PartitionSpec as P

F32 = jnp.float32
BF16 = jnp.bfloat16
VMEM_LIMIT = 16 * 1024 * 1024


def dot(lhs, rhs, lhs_dim, rhs_dim):
    return lax.dot_general(
        lhs, rhs, (((lhs_dim,), (rhs_dim,)), ((), ())), preferred_element_type=F32
    )


def transposed(matrix):
    return jnp.transpose(matrix.astype(F32)).astype(BF16)


def sigmoid(values):
    return 1.0 / (1.0 + jnp.exp(-values))


def column(row):
    size = row.shape[1]
    return jnp.transpose(jnp.broadcast_to(row, (size, size)))


def norm_rows(values):
    centered = values - jnp.mean(values, axis=0, keepdims=True)
    variance = jnp.mean(centered * centered, axis=0, keepdims=True)
    inv_std = lax.rsqrt(variance + 1e-05)
    return centered * inv_std, inv_std


def call(
    kernel, name, outs, args, fetched=(), unread=(), scratch=(), flops=0, limit=VMEM_LIMIT
):
    moved = sum(a.size * a.dtype.itemsize for a in args) + sum(
        o.size * jnp.dtype(o.dtype).itemsize for o in outs
    )
    n_args, n_outs, n_fetched = len(args), len(outs), len(fetched)

    def body(*refs):
        ins = list(refs[:n_args])
        rest = refs[n_args + n_outs :]
        copies = []
        for n, place in enumerate(fetched):
            copies.append(pltpu.make_async_copy(ins[place], rest[n], rest[n_fetched].at[n]))
            ins[place] = rest[n]
        for copy in copies:
            copy.start()
        for copy in copies:
            copy.wait()
        kernel(*ins, *refs[n_args : n_args + n_outs], *rest[n_fetched + (n_fetched > 0) :])

    buffers = [pltpu.VMEM(args[place].shape, args[place].dtype) for place in fetched]
    if fetched:
        buffers.append(pltpu.SemaphoreType.DMA((n_fetched,)))
    return pl.pallas_call(
        body,
        name=name,
        out_shape=outs,
        in_specs=[
            pl.BlockSpec(
                memory_space=pltpu.HBM if n in fetched else pl.ANY if n in unread else pltpu.VMEM
            )
            for n in range(n_args)
        ],
        out_specs=[pl.BlockSpec(memory_space=pltpu.VMEM) for _ in outs],
        scratch_shapes=buffers + list(scratch),
        compiler_params=pltpu.CompilerParams(vmem_limit_bytes=limit),
        cost_estimate=pl.CostEstimate(flops=flops, bytes_accessed=moved, transcendentals=0),
    )(*args)


def cell_masks(mask, rows):
    columns = mask[...].astype(F32)
    shape = (rows, columns.shape[1])
    first = lax.axis_index("row") * rows
    own = lax.broadcasted_iota(jnp.int32, shape, 1) == (
        lax.broadcasted_iota(jnp.int32, shape, 0) + first
    )
    row_mask = jnp.sum(jnp.where(own, columns, 0.0), axis=1, keepdims=True)
    cells = row_mask * columns
    return [cells[row : row + 1] for row in range(rows)]


def wide_order(devices, count, back):
    order = []
    for place in range(count):
        if back:
            order += [place ^ (count // 2), count + place]
        else:
            order += [count + (place ^ 2), place ^ (count // 2)]
    return order


def half_order(count):
    return [place + plane for place in range(count // 2) for plane in (0, count // 2)]


def distance(step, count):
    far = sorted(range(3, count), key=lambda apart: -(apart // 2))
    return [*range(min(3, count)), *far][step]


def partner(step, count):
    return lax.rem(lax.axis_index("row"), count) ^ distance(step, count)


def gated_rows(pair, mask, gain, bias, w_proj, side):
    rows = pair.shape[0]
    hidden = w_proj.shape[1] // 4
    w_flip = transposed(w_proj[:, 2 * side * hidden : 2 * (side + 1) * hidden])
    gain_col, bias_col = column(gain[...]), column(bias[...])
    masks = cell_masks(mask, rows)
    for row in range(rows):
        normed, _ = norm_rows(jnp.transpose(pair[row].astype(F32)))
        zln = (normed * gain_col + bias_col).astype(BF16)
        proj = dot(w_flip, zln, 1, 0)
        yield row, masks[row] * sigmoid(proj[:hidden]) * proj[hidden:]


def project_right_kernel(pair, mask, gain, bias, w_proj, right_panel):
    rows = pair.shape[0]
    devices, depth, width = right_panel.shape
    block = depth // rows
    count = w_proj.shape[1] // 4 // block
    for row, right in gated_rows(pair, mask, gain, bias, w_proj, 1):
        right = right.reshape(count, block, width).astype(BF16)
        for rank in range(devices):
            place = wide_order(devices, count, False)[rank] % count
            right_panel[rank, row * block : (row + 1) * block, :] = right[place]


def project_left_kernel(pair, mask, gain, bias, w_proj, after, *refs):
    del after
    *pieces, left_panel = refs
    rows = pair.shape[0]
    count, depth, width = left_panel.shape
    block = depth // rows
    for row, left in gated_rows(pair, mask, gain, bias, w_proj, 0):
        left = left.reshape(count, block, width).astype(BF16)
        left_panel[:, row * block : (row + 1) * block, :] = left
    for step, piece in enumerate(pieces):
        piece[...] = left_panel[partner(step, count)]


def prepare_kernel(
    pair, cotangent, gain, bias, w_gate, out_gain, w_out, d_hat_centered, gate_slope
):
    gate_flip = transposed(w_gate[...])
    gain_col, bias_col = column(gain[...]), column(bias[...])
    out_gain_col = column(out_gain[...])
    for row in range(pair.shape[0]):
        normed, _ = norm_rows(jnp.transpose(pair[row].astype(F32)))
        zln = (normed * gain_col + bias_col).astype(BF16)
        gate = sigmoid(dot(gate_flip, zln, 1, 0))
        cot = jnp.transpose(cotangent[row].astype(F32))
        d_scaled = (cot * gate).astype(BF16)
        d_hat = dot(w_out[...], d_scaled, 1, 0) * out_gain_col
        d_hat_centered[row] = d_hat - jnp.mean(d_hat, axis=0, keepdims=True)
        gate_slope[row] = cot * gate * (1.0 - gate)


def half_places(panel):
    count, depth, _ = panel.shape
    for rank, place in enumerate(half_order(count)):
        yield rank, slice(place * depth, (place + 1) * depth)


def wide_places(panel, count, back):
    devices, depth, _ = panel.shape
    for rank, device in enumerate(wide_order(devices, count, back)):
        yield rank, slice(device * depth, (device + 1) * depth)


def sort_left_kernel(*refs):
    *pieces, left_all, left_wide = refs
    block, left_rows, _ = left_all.shape
    depth = pieces[0].shape[0]
    for step, piece in enumerate(pieces):
        start = pl.multiple_of(partner(step, len(pieces)) * depth, depth)
        left_wide[pl.ds(start, depth), :] = piece[...].astype(F32)
    for h in range(block):
        left_all[h] = left_wide[pl.ds(h, left_rows, stride=block), :].astype(BF16)


def tri_kernel(right_panel, left_all, after, products, right_all, left_wide, right_wide):
    del after
    block, left_rows, _ = left_all.shape
    right_rows = right_all.shape[1]
    for rank, place in wide_places(right_panel, products.shape[0], False):
        right_wide[place, :] = right_panel[rank].astype(F32)
    for h in range(block):
        right = right_wide[pl.ds(h, right_rows, stride=block), :].astype(BF16)
        right_all[h] = right
        left_wide[pl.ds(h, left_rows, stride=block), :] = dot(left_all[h], right, 1, 1)
    for rank, place in half_places(products):
        products[rank] = left_wide[place, :].astype(BF16)


def cell_row(ref, row, rows, order=None):
    count, depth, width = ref.shape
    block = depth // rows
    part = ref[:, row * block : (row + 1) * block, :].astype(F32)
    if order:
        part = jnp.stack([part[order.index(place)] for place in range(count)])
    return part.reshape(count * block, width)


def middle_kernel(products, d_hat_centered, d_products):
    rows = d_hat_centered.shape[0]
    count, depth, width = products.shape
    block = depth // rows
    order = half_order(count)
    for row in range(rows):
        tri_hat, inv_std = norm_rows(cell_row(products, row, rows, order))
        d_hat = d_hat_centered[row]
        cross = jnp.mean(d_hat * tri_hat, axis=0, keepdims=True)
        d_tri = inv_std * (d_hat - tri_hat * cross)
        d_tri = d_tri.reshape(count, block, width).astype(BF16)
        for rank, place in enumerate(order):
            d_products[rank, row * block : (row + 1) * block, :] = d_tri[place]


def d_right_kernel(d_products, left_all, d_right_panel, d_tri_all, left_wide, right_wide):
    block, left_rows, _ = left_all.shape
    right_rows = right_wide.shape[0] // block
    for rank, place in half_places(d_products):
        left_wide[place, :] = d_products[rank].astype(F32)
    for h in range(block):
        d_tri = left_wide[pl.ds(h, left_rows, stride=block), :].astype(BF16)
        d_tri_all[h] = d_tri
        right_wide[pl.ds(h, right_rows, stride=block), :] = dot(d_tri, left_all[h], 0, 0)
    for rank, place in wide_places(d_right_panel, d_products.shape[0], True):
        d_right_panel[rank] = right_wide[place, :].astype(BF16)


def d_left_kernel(d_tri_all, right_all, *refs):
    *pieces, left_wide = refs
    block, left_rows, _ = d_tri_all.shape
    for h in range(block):
        left_wide[pl.ds(h, left_rows, stride=block), :] = dot(d_tri_all[h], right_all[h], 1, 0)
    depth = pieces[0].shape[0]
    for step, piece in enumerate(pieces):
        start = pl.multiple_of(partner(step, len(pieces)) * depth, depth)
        piece[...] = left_wide[pl.ds(start, depth), :].astype(BF16)


def gate_back_kernel(products, gate_slope, out_gain, out_bias, w_out, d_gate_pre):
    rows = gate_slope.shape[0]
    out_flip = transposed(w_out[...])
    out_gain_col, out_bias_col = column(out_gain[...]), column(out_bias[...])
    for row in range(rows):
        tri_hat, _ = norm_rows(cell_row(products, row, rows, half_order(products.shape[0])))
        scaled = (tri_hat * out_gain_col + out_bias_col).astype(BF16)
        d_gate_pre[row] = (dot(out_flip, scaled, 1, 0) * gate_slope[row]).astype(BF16)


def slopes_kernel(
    pair, mask, gain, bias, w_proj, w_gate, after, slopes, normed_in, inv_in, in_gain, weights
):
    del after
    rows = pair.shape[0]
    hidden = w_proj.shape[1] // 4
    w_flip = transposed(w_proj[...])
    gain_col, bias_col = column(gain[...]), column(bias[...])
    in_gain[...] = gain_col
    weights[...] = jnp.concatenate([w_proj[...], w_gate[...]], axis=1)
    masks = cell_masks(mask, rows)
    for row in range(rows):
        normed, inv_std = norm_rows(jnp.transpose(pair[row].astype(F32)))
        normed_in[row] = normed.astype(normed_in.dtype)
        inv_in[row : row + 1] = inv_std
        zln = (normed * gain_col + bias_col).astype(BF16)
        proj = dot(w_flip, zln, 1, 0)
        for side in range(2):
            base = 2 * side * hidden
            sig = sigmoid(proj[base : base + hidden])
            masked = masks[row] * sig
            value = masked * (1.0 - sig) * proj[base + hidden : base + 2 * hidden]
            slopes[row, base : base + hidden, :] = value.astype(slopes.dtype)
            slopes[row, base + hidden : base + 2 * hidden, :] = masked.astype(slopes.dtype)


def sort_d_left_kernel(*refs):
    *pieces, d_left_panel = refs
    for step, piece in enumerate(pieces):
        d_left_panel[partner(step, len(pieces))] = piece[...]


def both_halves(blocks, count):
    order = wide_order(2 * count, count, True)
    return jnp.stack(
        [blocks[order.index(place)] + blocks[order.index(count + place)] for place in range(count)]
    )


def finish_kernel(
    d_right_panel, d_left_panel, slopes, d_gate_pre, normed_in, inv_in, gain_col, weights, grad
):
    rows = grad.shape[0]
    count, depth, width = d_left_panel.shape
    hidden = count * depth // rows
    for row in range(rows):
        d_right = cell_row(d_right_panel, row, rows)
        d_right = both_halves(d_right.reshape(2 * count, depth // rows, width), count)
        parts = []
        for side, d_value in enumerate((cell_row(d_left_panel, row, rows), d_right.reshape(hidden, width))):
            for base in (2 * side * hidden, (2 * side + 1) * hidden):
                slope = slopes[row, base : base + hidden, :].astype(F32)
                parts.append((d_value * slope).astype(BF16))
        parts.append(d_gate_pre[row])
        d_in = dot(weights[...], jnp.concatenate(parts, axis=0), 1, 0) * gain_col[...]
        normed = normed_in[row].astype(F32)
        mean_grad = jnp.mean(d_in, axis=0, keepdims=True)
        mean_cross = jnp.mean(d_in * normed, axis=0, keepdims=True)
        result = inv_in[row : row + 1] * (d_in - mean_grad - normed * mean_cross)
        grad[row] = jnp.transpose(result).astype(BF16)


def swap(values, count, back):
    groups = [wide_order(lax.axis_size("row"), count, back)]
    return lax.all_to_all(
        values, "row", split_axis=0, concat_axis=0, tiled=True, axis_index_groups=groups
    )


def swap_half(values, count):
    devices = range(lax.axis_size("row"))
    order = half_order(count)
    groups = [[start + place for place in order] for start in range(0, len(devices), count)]
    return lax.all_to_all(
        values, "row", split_axis=0, concat_axis=0, tiled=True, axis_index_groups=groups
    )


def swap_pieces(pieces):
    devices = range(lax.axis_size("row"))
    count = len(pieces)
    return [pieces[0]] + [
        lax.ppermute(pieces[step], "row", [(d, d ^ distance(step, count)) for d in devices])
        for step in range(1, count)
    ]


def kernel_shards(
    pair,
    cotangent,
    residue_mask,
    ln_in_gain,
    ln_in_bias,
    w_proj,
    w_gate,
    ln_out_gain,
    ln_out_bias,
    w_out,
):
    rows, width, channels = pair.shape
    hidden = w_out.shape[0]
    halves = 2
    devices = lax.axis_size("row")
    count = devices // halves
    block = hidden // count
    left_rows, right_rows = rows * count, rows * devices
    shape = jax.ShapeDtypeStruct
    panel = shape((count, rows * block, width), BF16)
    wide_panel = shape((devices, rows * block, width), BF16)
    mask = residue_mask.reshape(1, width)
    gain, bias = ln_in_gain.reshape(1, channels), ln_in_bias.reshape(1, channels)
    out_gain, out_bias = ln_out_gain.reshape(1, hidden), ln_out_bias.reshape(1, hidden)
    cells = rows * width
    piece = shape((rows * block, width), BF16)
    left_panel = pltpu.VMEM(panel.shape, BF16)
    left_wide = pltpu.VMEM((left_rows * block, width), F32)
    right_wide = pltpu.VMEM((right_rows * block, width), F32)
    (own_right,) = call(
        project_right_kernel,
        "project_right",
        [wide_panel],
        [pair, mask, gain, bias, w_proj],
        fetched=range(5),
        flops=2 * cells * channels * 2 * hidden,
        limit=64 * 1024 * 1024 - 640 * 1024,
    )
    right_panel = swap(own_right, count, False)
    pieces = call(
        project_left_kernel,
        "project_left",
        [piece] * count,
        [pair, mask, gain, bias, w_proj, own_right],
        fetched=range(5),
        unread=(5,),
        scratch=[left_panel],
        flops=2 * cells * channels * 2 * hidden,
    )
    pieces = swap_pieces(pieces)
    (left_all,) = call(
        sort_left_kernel,
        "sort_left",
        [shape((block, left_rows, width), BF16)],
        pieces,
        scratch=[left_wide],
    )
    d_hat_centered, gate_slope = call(
        prepare_kernel,
        "prepare",
        [shape((rows, hidden, width), F32), shape((rows, channels, width), F32)],
        [pair, cotangent, gain, bias, w_gate, out_gain, w_out],
        fetched=range(7),
        flops=2 * cells * channels * 2 * hidden,
    )
    products, right_all = call(
        tri_kernel,
        "tri",
        [panel, shape((block, right_rows, width), BF16)],
        [right_panel, left_all, d_hat_centered],
        unread=(2,),
        scratch=[left_wide, right_wide],
        flops=2 * block * left_rows * width * right_rows,
    )
    products = swap_half(products, count)
    (d_products,) = call(
        middle_kernel,
        "middle",
        [panel],
        [products, d_hat_centered],
        flops=20 * cells * hidden,
    )
    d_products = swap_half(d_products, count)
    d_right_panel, d_tri_all = call(
        d_right_kernel,
        "d_right",
        [wide_panel, shape((block, left_rows, width), BF16)],
        [d_products, left_all],
        scratch=[left_wide, right_wide],
        flops=2 * block * left_rows * width * right_rows,
    )
    d_right_panel = swap(d_right_panel, count, True)
    d_pieces = call(
        d_left_kernel,
        "d_left",
        [piece] * count,
        [d_tri_all, right_all],
        scratch=[left_wide],
        flops=2 * block * left_rows * width * right_rows,
    )
    d_pieces = swap_pieces(d_pieces)
    (d_left_panel,) = call(sort_d_left_kernel, "sort_d_left", [panel], d_pieces)
    (d_gate_pre,) = call(
        gate_back_kernel,
        "gate_back",
        [shape((rows, channels, width), BF16)],
        [products, gate_slope, out_gain, out_bias, w_out],
        fetched=range(2, 5),
        flops=2 * cells * channels * hidden,
    )
    slopes, normed_in, inv_in, gain_col, weights = call(
        slopes_kernel,
        "slopes",
        [
            shape((rows, 4 * hidden, width), BF16),
            shape((rows, channels, width), BF16),
            shape((rows, width), F32),
            shape((channels, channels), F32),
            shape((channels, 4 * hidden + channels), BF16),
        ],
        [pair, mask, gain, bias, w_proj, w_gate, d_gate_pre],
        fetched=range(6),
        unread=(6,),
        flops=2 * cells * channels * 4 * hidden,
    )
    (grad,) = call(
        finish_kernel,
        "finish",
        [shape(pair.shape, BF16)],
        [
            d_right_panel,
            d_left_panel,
            slopes,
            d_gate_pre,
            normed_in,
            inv_in,
            gain_col,
            weights,
        ],
        flops=2 * cells * channels * 4 * hidden,
    )
    return grad


def normalize(values, reduce_axis):
    mean_value = jnp.mean(values, axis=reduce_axis, keepdims=True)
    centered = values - mean_value
    variance = jnp.mean(centered * centered, axis=reduce_axis, keepdims=True)
    inv_std = lax.rsqrt(variance + 1e-05)
    return (centered * inv_std, inv_std)


def norm_backward(upstream, normed, inv_std, reduce_axis):
    mean_grad = jnp.mean(upstream, axis=reduce_axis, keepdims=True)
    mean_cross = jnp.mean(upstream * normed, axis=reduce_axis, keepdims=True)
    return inv_std * (upstream - mean_grad - normed * mean_cross)


def shards(
    pair,
    cotangent,
    residue_mask,
    ln_in_gain,
    ln_in_bias,
    w_proj,
    w_gate,
    ln_out_gain,
    ln_out_bias,
    w_out,
):
    local_rows = pair.shape[0]
    local_cols = pair.shape[1]
    hidden = w_out.shape[0]
    chan_index = lax.axis_index("chan")
    row_start = lax.axis_index("row") * local_rows
    col_start = chan_index * local_cols
    mask_float = residue_mask.astype(jnp.float32)
    row_mask = lax.dynamic_slice_in_dim(mask_float, row_start, local_rows)
    col_mask = lax.dynamic_slice_in_dim(mask_float, col_start, local_cols)
    cell_mask = (row_mask[:, None] * col_mask[None, :])[None]
    normed, inv_std = normalize(pair.astype(jnp.float32), -1)
    normed_pair = (normed * ln_in_gain + ln_in_bias).astype(jnp.bfloat16)
    projected = jnp.einsum("rmc,ch->hrm", normed_pair, w_proj, preferred_element_type=jnp.float32)
    left_panel = (
        cell_mask * jax.nn.sigmoid(projected[:hidden]) * projected[hidden : 2 * hidden]
    ).astype(jnp.bfloat16)
    right_panel = (
        cell_mask * jax.nn.sigmoid(projected[2 * hidden : 3 * hidden]) * projected[3 * hidden :]
    ).astype(jnp.bfloat16)
    panels = lax.all_to_all(
        jnp.stack([left_panel, right_panel]), "row", split_axis=1, concat_axis=2, tiled=True
    )
    left_all = panels[0]
    right_all = panels[1]
    right_rows = lax.all_to_all(right_all, "chan", split_axis=1, concat_axis=2, tiled=True)
    partner = right_rows
    tri_part = jnp.einsum(
        "gik,gjk->gij",
        lax.all_gather(left_all, "chan", axis=2, tiled=True),
        partner,
        preferred_element_type=jnp.float32,
    ).astype(jnp.bfloat16)
    tri_cells = lax.all_to_all(tri_part, "row", split_axis=1, concat_axis=0, tiled=True)
    tri_hat, inv_tri = normalize(tri_cells.astype(jnp.float32), 0)
    scaled = (tri_hat * ln_out_gain[:, None, None] + ln_out_bias[:, None, None]).astype(
        jnp.bfloat16
    )
    proj_out = jnp.einsum("hrm,hc->rmc", scaled, w_out, preferred_element_type=jnp.float32)
    gate_value = jax.nn.sigmoid(
        jnp.einsum("rmc,cd->rmd", normed_pair, w_gate, preferred_element_type=jnp.float32)
    )
    cot_float = cotangent.astype(jnp.float32)
    d_gate_pre = (cot_float * proj_out * gate_value * (1.0 - gate_value)).astype(jnp.bfloat16)
    d_scaled = (cot_float * gate_value).astype(jnp.bfloat16)
    d_hat = jnp.einsum("rmc,hc->hrm", d_scaled, w_out, preferred_element_type=jnp.float32)
    d_hat = d_hat * ln_out_gain[:, None, None]
    d_tri = norm_backward(d_hat, tri_hat, inv_tri, 0).astype(jnp.bfloat16)
    d_tri_all = lax.all_to_all(d_tri, "row", split_axis=0, concat_axis=1, tiled=True)
    panel_piece = lax.all_gather(d_tri_all, "chan", axis=2, tiled=True)
    partner = right_all
    d_left = jnp.einsum("gij,gjk->gik", panel_piece, partner, preferred_element_type=jnp.float32)
    contribution = jnp.einsum(
        "gij,gik->gjk", panel_piece, left_all, preferred_element_type=jnp.float32
    )
    d_right = contribution
    d_left, d_right = (d_left, d_right)
    d_stack = jnp.stack([d_left, d_right]).astype(jnp.bfloat16)
    d_panels = lax.all_to_all(d_stack, "row", split_axis=2, concat_axis=1, tiled=True)

    def gating(d_value, gate_proj, value_proj):
        sigmoid_val = jax.nn.sigmoid(gate_proj)
        masked_grad = d_value.astype(jnp.float32) * cell_mask
        return (
            masked_grad * value_proj * sigmoid_val * (1.0 - sigmoid_val),
            masked_grad * sigmoid_val,
        )

    gate_left, value_left = gating(d_panels[0], projected[:hidden], projected[hidden : 2 * hidden])
    gate_right, value_right = gating(
        d_panels[1], projected[2 * hidden : 3 * hidden], projected[3 * hidden :]
    )
    d_proj = jnp.concatenate([gate_left, value_left, gate_right, value_right], axis=0).astype(
        jnp.bfloat16
    )
    d_normed = jnp.einsum("hrm,ch->rmc", d_proj, w_proj, preferred_element_type=jnp.float32)
    d_normed = d_normed + jnp.einsum(
        "rmd,cd->rmc", d_gate_pre, w_gate, preferred_element_type=jnp.float32
    )
    d_input = d_normed * ln_in_gain
    return norm_backward(d_input, normed, inv_std, -1).astype(jnp.bfloat16)


def solution(mesh):
    fits = mesh.shape["chan"] == 1 and mesh.shape["row"] in (8, 16)
    return jax.shard_map(
        kernel_shards if fits else shards,
        mesh=mesh,
        in_specs=(
            P(("grp", "row"), "chan", None),
            P(("grp", "row"), "chan", None),
            P("grp"),
            P(),
            P(),
            P(),
            P(),
            P(),
            P(),
            P(),
        ),
        out_specs=P(("grp", "row"), "chan", None),
        check_vma=False,
    )
```

```python
import functools

import jax
import jax.numpy as jnp
from jax import lax
from jax.experimental import pallas as pl
from jax.experimental.pallas import tpu as pltpu
from jax.sharding import PartitionSpec as P

F32 = jnp.float32
BF16 = jnp.bfloat16
VMEM_LIMIT = 16 * 1024 * 1024


def dot(lhs, rhs, lhs_dim, rhs_dim):
    return lax.dot_general(
        lhs, rhs, (((lhs_dim,), (rhs_dim,)), ((), ())), preferred_element_type=F32
    )


def transposed(matrix):
    return jnp.transpose(matrix.astype(F32)).astype(BF16)


def sigmoid(values):
    return 1.0 / (1.0 + jnp.exp(-values))


def column(row):
    size = row.shape[1]
    return jnp.transpose(jnp.broadcast_to(row, (size, size)))


def norm_rows(values):
    centered = values - jnp.mean(values, axis=0, keepdims=True)
    variance = jnp.mean(centered * centered, axis=0, keepdims=True)
    inv_std = lax.rsqrt(variance + 1e-05)
    return centered * inv_std, inv_std


def call(
    kernel, name, outs, args, fetched=(), unread=(), scratch=(), flops=0, limit=VMEM_LIMIT
):
    moved = sum(a.size * a.dtype.itemsize for a in args) + sum(
        o.size * jnp.dtype(o.dtype).itemsize for o in outs
    )
    n_args, n_outs, n_fetched = len(args), len(outs), len(fetched)

    def body(*refs):
        ins = list(refs[:n_args])
        rest = refs[n_args + n_outs :]
        copies = []
        for n, place in enumerate(fetched):
            copies.append(pltpu.make_async_copy(ins[place], rest[n], rest[n_fetched].at[n]))
            ins[place] = rest[n]
        for copy in copies:
            copy.start()
        for copy in copies:
            copy.wait()
        kernel(*ins, *refs[n_args : n_args + n_outs], *rest[n_fetched + (n_fetched > 0) :])

    buffers = [pltpu.VMEM(args[place].shape, args[place].dtype) for place in fetched]
    if fetched:
        buffers.append(pltpu.SemaphoreType.DMA((n_fetched,)))
    return pl.pallas_call(
        body,
        name=name,
        out_shape=outs,
        in_specs=[
            pl.BlockSpec(
                memory_space=pltpu.HBM if n in fetched else pl.ANY if n in unread else pltpu.VMEM
            )
            for n in range(n_args)
        ],
        out_specs=[pl.BlockSpec(memory_space=pltpu.VMEM) for _ in outs],
        scratch_shapes=buffers + list(scratch),
        compiler_params=pltpu.CompilerParams(vmem_limit_bytes=limit),
        cost_estimate=pl.CostEstimate(flops=flops, bytes_accessed=moved, transcendentals=0),
    )(*args)


def cell_masks(mask, rows):
    columns = mask[...].astype(F32)
    shape = (rows, columns.shape[1])
    first = lax.axis_index("row") * rows
    own = lax.broadcasted_iota(jnp.int32, shape, 1) == (
        lax.broadcasted_iota(jnp.int32, shape, 0) + first
    )
    row_mask = jnp.sum(jnp.where(own, columns, 0.0), axis=1, keepdims=True)
    cells = row_mask * columns
    return [cells[row : row + 1] for row in range(rows)]


def wide_order(devices, count, back):
    first = count // 2 if back else count
    return [(first + n) % devices for n in range(devices)]


def distance(step, count):
    far = sorted(range(3, count), key=lambda apart: -(apart // 2))
    return [*range(min(3, count)), *far][step]


def partner(step, count):
    return lax.rem(lax.axis_index("row"), count) ^ distance(step, count)


def gated_rows(pair, mask, gain, bias, w_proj, side):
    rows = pair.shape[0]
    hidden = w_proj.shape[1] // 4
    w_flip = transposed(w_proj[:, 2 * side * hidden : 2 * (side + 1) * hidden])
    gain_col, bias_col = column(gain[...]), column(bias[...])
    masks = cell_masks(mask, rows)
    for row in range(rows):
        normed, _ = norm_rows(jnp.transpose(pair[row].astype(F32)))
        zln = (normed * gain_col + bias_col).astype(BF16)
        proj = dot(w_flip, zln, 1, 0)
        yield row, masks[row] * sigmoid(proj[:hidden]) * proj[hidden:]


def project_right_kernel(pair, mask, gain, bias, w_proj, right_panel):
    rows = pair.shape[0]
    devices, depth, width = right_panel.shape
    block = depth // rows
    count = w_proj.shape[1] // 4 // block
    for row, right in gated_rows(pair, mask, gain, bias, w_proj, 1):
        right = right.reshape(count, block, width).astype(BF16)
        for rank in range(devices):
            place = wide_order(devices, count, False)[rank] % count
            right_panel[rank, row * block : (row + 1) * block, :] = right[place]


def project_left_kernel(pair, mask, gain, bias, w_proj, after, *refs):
    del after
    *pieces, left_panel = refs
    rows = pair.shape[0]
    count, depth, width = left_panel.shape
    block = depth // rows
    for row, left in gated_rows(pair, mask, gain, bias, w_proj, 0):
        left = left.reshape(count, block, width).astype(BF16)
        left_panel[:, row * block : (row + 1) * block, :] = left
    for step, piece in enumerate(pieces):
        piece[...] = left_panel[partner(step, count)]


def prepare_kernel(
    pair, cotangent, gain, bias, w_gate, out_gain, w_out, d_hat_centered, gate_slope
):
    gate_flip = transposed(w_gate[...])
    gain_col, bias_col = column(gain[...]), column(bias[...])
    out_gain_col = column(out_gain[...])
    for row in range(pair.shape[0]):
        normed, _ = norm_rows(jnp.transpose(pair[row].astype(F32)))
        zln = (normed * gain_col + bias_col).astype(BF16)
        gate = sigmoid(dot(gate_flip, zln, 1, 0))
        cot = jnp.transpose(cotangent[row].astype(F32))
        d_scaled = (cot * gate).astype(BF16)
        d_hat = dot(w_out[...], d_scaled, 1, 0) * out_gain_col
        d_hat_centered[row] = d_hat - jnp.mean(d_hat, axis=0, keepdims=True)
        gate_slope[row] = cot * gate * (1.0 - gate)


def spread(panel, wide):
    wide[...] = panel[...].astype(F32).reshape(wide.shape)


def wide_places(panel, count, back):
    devices, depth, _ = panel.shape
    for rank, device in enumerate(wide_order(devices, count, back)):
        yield rank, slice(device * depth, (device + 1) * depth)


def sort_left_kernel(*refs):
    *pieces, left_all, left_wide = refs
    block, left_rows, _ = left_all.shape
    depth = pieces[0].shape[0]
    for step, piece in enumerate(pieces):
        start = pl.multiple_of(partner(step, len(pieces)) * depth, depth)
        left_wide[pl.ds(start, depth), :] = piece[...].astype(F32)
    for h in range(block):
        left_all[h] = left_wide[pl.ds(h, left_rows, stride=block), :].astype(BF16)


def tri_kernel(right_panel, left_all, after, products, right_all, left_wide, right_wide):
    del after
    block, left_rows, _ = left_all.shape
    right_rows = right_all.shape[1]
    for rank, place in wide_places(right_panel, products.shape[0], False):
        right_wide[place, :] = right_panel[rank].astype(F32)
    for h in range(block):
        right = right_wide[pl.ds(h, right_rows, stride=block), :].astype(BF16)
        right_all[h] = right
        left_wide[pl.ds(h, left_rows, stride=block), :] = dot(left_all[h], right, 1, 1)
    products[...] = left_wide[...].astype(BF16).reshape(products.shape)


def cell_row(ref, row, rows):
    count, depth, width = ref.shape
    block = depth // rows
    return ref[:, row * block : (row + 1) * block, :].astype(F32).reshape(count * block, width)


def middle_kernel(products, d_hat_centered, d_products):
    rows = d_hat_centered.shape[0]
    count, depth, width = products.shape
    block = depth // rows
    for row in range(rows):
        tri_hat, inv_std = norm_rows(cell_row(products, row, rows))
        d_hat = d_hat_centered[row]
        cross = jnp.mean(d_hat * tri_hat, axis=0, keepdims=True)
        d_tri = inv_std * (d_hat - tri_hat * cross)
        d_products[:, row * block : (row + 1) * block, :] = d_tri.reshape(
            count, block, width
        ).astype(BF16)


def d_right_kernel(d_products, left_all, d_right_panel, d_tri_all, left_wide, right_wide):
    block, left_rows, _ = left_all.shape
    right_rows = right_wide.shape[0] // block
    spread(d_products, left_wide)
    for h in range(block):
        d_tri = left_wide[pl.ds(h, left_rows, stride=block), :].astype(BF16)
        d_tri_all[h] = d_tri
        right_wide[pl.ds(h, right_rows, stride=block), :] = dot(d_tri, left_all[h], 0, 0)
    for rank, place in wide_places(d_right_panel, d_products.shape[0], True):
        d_right_panel[rank] = right_wide[place, :].astype(BF16)


def d_left_kernel(d_tri_all, right_all, *refs):
    *pieces, left_wide = refs
    block, left_rows, _ = d_tri_all.shape
    for h in range(block):
        left_wide[pl.ds(h, left_rows, stride=block), :] = dot(d_tri_all[h], right_all[h], 1, 0)
    depth = pieces[0].shape[0]
    for step, piece in enumerate(pieces):
        start = pl.multiple_of(partner(step, len(pieces)) * depth, depth)
        piece[...] = left_wide[pl.ds(start, depth), :].astype(BF16)


def gate_back_kernel(products, gate_slope, out_gain, out_bias, w_out, d_gate_pre):
    rows = gate_slope.shape[0]
    out_flip = transposed(w_out[...])
    out_gain_col, out_bias_col = column(out_gain[...]), column(out_bias[...])
    for row in range(rows):
        tri_hat, _ = norm_rows(cell_row(products, row, rows))
        scaled = (tri_hat * out_gain_col + out_bias_col).astype(BF16)
        d_gate_pre[row] = (dot(out_flip, scaled, 1, 0) * gate_slope[row]).astype(BF16)


def slopes_kernel(
    pair, mask, gain, bias, w_proj, w_gate, after, slopes, normed_in, inv_in, in_gain, weights
):
    del after
    rows = pair.shape[0]
    hidden = w_proj.shape[1] // 4
    w_flip = transposed(w_proj[...])
    gain_col, bias_col = column(gain[...]), column(bias[...])
    in_gain[...] = gain_col
    weights[...] = jnp.concatenate([w_proj[...], w_gate[...]], axis=1)
    masks = cell_masks(mask, rows)
    for row in range(rows):
        normed, inv_std = norm_rows(jnp.transpose(pair[row].astype(F32)))
        normed_in[row] = normed.astype(normed_in.dtype)
        inv_in[row : row + 1] = inv_std
        zln = (normed * gain_col + bias_col).astype(BF16)
        proj = dot(w_flip, zln, 1, 0)
        for side in range(2):
            base = 2 * side * hidden
            sig = sigmoid(proj[base : base + hidden])
            masked = masks[row] * sig
            value = masked * (1.0 - sig) * proj[base + hidden : base + 2 * hidden]
            slopes[row, base : base + hidden, :] = value.astype(slopes.dtype)
            slopes[row, base + hidden : base + 2 * hidden, :] = masked.astype(slopes.dtype)


def sort_d_left_kernel(*refs):
    *pieces, d_left_panel = refs
    for step, piece in enumerate(pieces):
        d_left_panel[partner(step, len(pieces))] = piece[...]


def both_halves(blocks, count):
    order = wide_order(2 * count, count, True)
    return jnp.stack(
        [blocks[order.index(place)] + blocks[order.index(count + place)] for place in range(count)]
    )


def finish_kernel(
    d_right_panel, d_left_panel, slopes, d_gate_pre, normed_in, inv_in, gain_col, weights, grad
):
    rows = grad.shape[0]
    count, depth, width = d_left_panel.shape
    hidden = count * depth // rows
    for row in range(rows):
        d_right = cell_row(d_right_panel, row, rows)
        d_right = both_halves(d_right.reshape(2 * count, depth // rows, width), count)
        parts = []
        for side, d_value in enumerate((cell_row(d_left_panel, row, rows), d_right.reshape(hidden, width))):
            for base in (2 * side * hidden, (2 * side + 1) * hidden):
                slope = slopes[row, base : base + hidden, :].astype(F32)
                parts.append((d_value * slope).astype(BF16))
        parts.append(d_gate_pre[row])
        d_in = dot(weights[...], jnp.concatenate(parts, axis=0), 1, 0) * gain_col[...]
        normed = normed_in[row].astype(F32)
        mean_grad = jnp.mean(d_in, axis=0, keepdims=True)
        mean_cross = jnp.mean(d_in * normed, axis=0, keepdims=True)
        result = inv_in[row : row + 1] * (d_in - mean_grad - normed * mean_cross)
        grad[row] = jnp.transpose(result).astype(BF16)


def swap(values, count, back):
    groups = [wide_order(lax.axis_size("row"), count, back)]
    return lax.all_to_all(
        values, "row", split_axis=0, concat_axis=0, tiled=True, axis_index_groups=groups
    )


def swap_half(values, count):
    devices = range(lax.axis_size("row"))
    groups = [[d for d in devices if d // count == half] for half in range(len(devices) // count)]
    return lax.all_to_all(
        values, "row", split_axis=0, concat_axis=0, tiled=True, axis_index_groups=groups
    )


def swap_pieces(pieces):
    devices = range(lax.axis_size("row"))
    count = len(pieces)
    return [pieces[0]] + [
        lax.ppermute(pieces[step], "row", [(d, d ^ distance(step, count)) for d in devices])
        for step in range(1, count)
    ]


def kernel_shards(
    pair,
    cotangent,
    residue_mask,
    ln_in_gain,
    ln_in_bias,
    w_proj,
    w_gate,
    ln_out_gain,
    ln_out_bias,
    w_out,
):
    rows, width, channels = pair.shape
    hidden = w_out.shape[0]
    halves = 2
    devices = lax.axis_size("row")
    count = devices // halves
    block = hidden // count
    left_rows, right_rows = rows * count, rows * devices
    shape = jax.ShapeDtypeStruct
    panel = shape((count, rows * block, width), BF16)
    wide_panel = shape((devices, rows * block, width), BF16)
    mask = residue_mask.reshape(1, width)
    gain, bias = ln_in_gain.reshape(1, channels), ln_in_bias.reshape(1, channels)
    out_gain, out_bias = ln_out_gain.reshape(1, hidden), ln_out_bias.reshape(1, hidden)
    cells = rows * width
    piece = shape((rows * block, width), BF16)
    left_panel = pltpu.VMEM(panel.shape, BF16)
    left_wide = pltpu.VMEM((left_rows * block, width), F32)
    right_wide = pltpu.VMEM((right_rows * block, width), F32)
    (own_right,) = call(
        project_right_kernel,
        "project_right",
        [wide_panel],
        [pair, mask, gain, bias, w_proj],
        fetched=range(5),
        flops=2 * cells * channels * 2 * hidden,
        limit=64 * 1024 * 1024 - 640 * 1024,
    )
    right_panel = swap(own_right, count, False)
    pieces = call(
        project_left_kernel,
        "project_left",
        [piece] * count,
        [pair, mask, gain, bias, w_proj, own_right],
        fetched=range(5),
        unread=(5,),
        scratch=[left_panel],
        flops=2 * cells * channels * 2 * hidden,
    )
    pieces = swap_pieces(pieces)
    (left_all,) = call(
        sort_left_kernel,
        "sort_left",
        [shape((block, left_rows, width), BF16)],
        pieces,
        scratch=[left_wide],
    )
    d_hat_centered, gate_slope = call(
        prepare_kernel,
        "prepare",
        [shape((rows, hidden, width), F32), shape((rows, channels, width), F32)],
        [pair, cotangent, gain, bias, w_gate, out_gain, w_out],
        fetched=range(7),
        flops=2 * cells * channels * 2 * hidden,
    )
    products, right_all = call(
        tri_kernel,
        "tri",
        [panel, shape((block, right_rows, width), BF16)],
        [right_panel, left_all, d_hat_centered],
        unread=(2,),
        scratch=[left_wide, right_wide],
        flops=2 * block * left_rows * width * right_rows,
    )
    products = swap_half(products, count)
    (d_products,) = call(
        middle_kernel,
        "middle",
        [panel],
        [products, d_hat_centered],
        flops=20 * cells * hidden,
    )
    d_products = swap_half(d_products, count)
    d_right_panel, d_tri_all = call(
        d_right_kernel,
        "d_right",
        [wide_panel, shape((block, left_rows, width), BF16)],
        [d_products, left_all],
        scratch=[left_wide, right_wide],
        flops=2 * block * left_rows * width * right_rows,
    )
    d_right_panel = swap(d_right_panel, count, True)
    d_pieces = call(
        d_left_kernel,
        "d_left",
        [piece] * count,
        [d_tri_all, right_all],
        scratch=[left_wide],
        flops=2 * block * left_rows * width * right_rows,
    )
    d_pieces = swap_pieces(d_pieces)
    (d_left_panel,) = call(sort_d_left_kernel, "sort_d_left", [panel], d_pieces)
    (d_gate_pre,) = call(
        gate_back_kernel,
        "gate_back",
        [shape((rows, channels, width), BF16)],
        [products, gate_slope, out_gain, out_bias, w_out],
        fetched=range(2, 5),
        flops=2 * cells * channels * hidden,
    )
    slopes, normed_in, inv_in, gain_col, weights = call(
        slopes_kernel,
        "slopes",
        [
            shape((rows, 4 * hidden, width), BF16),
            shape((rows, channels, width), BF16),
            shape((rows, width), F32),
            shape((channels, channels), F32),
            shape((channels, 4 * hidden + channels), BF16),
        ],
        [pair, mask, gain, bias, w_proj, w_gate, d_gate_pre],
        fetched=range(6),
        unread=(6,),
        flops=2 * cells * channels * 4 * hidden,
    )
    (grad,) = call(
        finish_kernel,
        "finish",
        [shape(pair.shape, BF16)],
        [
            d_right_panel,
            d_left_panel,
            slopes,
            d_gate_pre,
            normed_in,
            inv_in,
            gain_col,
            weights,
        ],
        flops=2 * cells * channels * 4 * hidden,
    )
    return grad


def normalize(values, reduce_axis):
    mean_value = jnp.mean(values, axis=reduce_axis, keepdims=True)
    centered = values - mean_value
    variance = jnp.mean(centered * centered, axis=reduce_axis, keepdims=True)
    inv_std = lax.rsqrt(variance + 1e-05)
    return (centered * inv_std, inv_std)


def norm_backward(upstream, normed, inv_std, reduce_axis):
    mean_grad = jnp.mean(upstream, axis=reduce_axis, keepdims=True)
    mean_cross = jnp.mean(upstream * normed, axis=reduce_axis, keepdims=True)
    return inv_std * (upstream - mean_grad - normed * mean_cross)


def shards(
    pair,
    cotangent,
    residue_mask,
    ln_in_gain,
    ln_in_bias,
    w_proj,
    w_gate,
    ln_out_gain,
    ln_out_bias,
    w_out,
):
    local_rows = pair.shape[0]
    local_cols = pair.shape[1]
    hidden = w_out.shape[0]
    chan_index = lax.axis_index("chan")
    row_start = lax.axis_index("row") * local_rows
    col_start = chan_index * local_cols
    mask_float = residue_mask.astype(jnp.float32)
    row_mask = lax.dynamic_slice_in_dim(mask_float, row_start, local_rows)
    col_mask = lax.dynamic_slice_in_dim(mask_float, col_start, local_cols)
    cell_mask = (row_mask[:, None] * col_mask[None, :])[None]
    normed, inv_std = normalize(pair.astype(jnp.float32), -1)
    normed_pair = (normed * ln_in_gain + ln_in_bias).astype(jnp.bfloat16)
    projected = jnp.einsum("rmc,ch->hrm", normed_pair, w_proj, preferred_element_type=jnp.float32)
    left_panel = (
        cell_mask * jax.nn.sigmoid(projected[:hidden]) * projected[hidden : 2 * hidden]
    ).astype(jnp.bfloat16)
    right_panel = (
        cell_mask * jax.nn.sigmoid(projected[2 * hidden : 3 * hidden]) * projected[3 * hidden :]
    ).astype(jnp.bfloat16)
    panels = lax.all_to_all(
        jnp.stack([left_panel, right_panel]), "row", split_axis=1, concat_axis=2, tiled=True
    )
    left_all = panels[0]
    right_all = panels[1]
    right_rows = lax.all_to_all(right_all, "chan", split_axis=1, concat_axis=2, tiled=True)
    partner = right_rows
    tri_part = jnp.einsum(
        "gik,gjk->gij",
        lax.all_gather(left_all, "chan", axis=2, tiled=True),
        partner,
        preferred_element_type=jnp.float32,
    ).astype(jnp.bfloat16)
    tri_cells = lax.all_to_all(tri_part, "row", split_axis=1, concat_axis=0, tiled=True)
    tri_hat, inv_tri = normalize(tri_cells.astype(jnp.float32), 0)
    scaled = (tri_hat * ln_out_gain[:, None, None] + ln_out_bias[:, None, None]).astype(
        jnp.bfloat16
    )
    proj_out = jnp.einsum("hrm,hc->rmc", scaled, w_out, preferred_element_type=jnp.float32)
    gate_value = jax.nn.sigmoid(
        jnp.einsum("rmc,cd->rmd", normed_pair, w_gate, preferred_element_type=jnp.float32)
    )
    cot_float = cotangent.astype(jnp.float32)
    d_gate_pre = (cot_float * proj_out * gate_value * (1.0 - gate_value)).astype(jnp.bfloat16)
    d_scaled = (cot_float * gate_value).astype(jnp.bfloat16)
    d_hat = jnp.einsum("rmc,hc->hrm", d_scaled, w_out, preferred_element_type=jnp.float32)
    d_hat = d_hat * ln_out_gain[:, None, None]
    d_tri = norm_backward(d_hat, tri_hat, inv_tri, 0).astype(jnp.bfloat16)
    d_tri_all = lax.all_to_all(d_tri, "row", split_axis=0, concat_axis=1, tiled=True)
    panel_piece = lax.all_gather(d_tri_all, "chan", axis=2, tiled=True)
    partner = right_all
    d_left = jnp.einsum("gij,gjk->gik", panel_piece, partner, preferred_element_type=jnp.float32)
    contribution = jnp.einsum(
        "gij,gik->gjk", panel_piece, left_all, preferred_element_type=jnp.float32
    )
    d_right = contribution
    d_left, d_right = (d_left, d_right)
    d_stack = jnp.stack([d_left, d_right]).astype(jnp.bfloat16)
    d_panels = lax.all_to_all(d_stack, "row", split_axis=2, concat_axis=1, tiled=True)

    def gating(d_value, gate_proj, value_proj):
        sigmoid_val = jax.nn.sigmoid(gate_proj)
        masked_grad = d_value.astype(jnp.float32) * cell_mask
        return (
            masked_grad * value_proj * sigmoid_val * (1.0 - sigmoid_val),
            masked_grad * sigmoid_val,
        )

    gate_left, value_left = gating(d_panels[0], projected[:hidden], projected[hidden : 2 * hidden])
    gate_right, value_right = gating(
        d_panels[1], projected[2 * hidden : 3 * hidden], projected[3 * hidden :]
    )
    d_proj = jnp.concatenate([gate_left, value_left, gate_right, value_right], axis=0).astype(
        jnp.bfloat16
    )
    d_normed = jnp.einsum("hrm,ch->rmc", d_proj, w_proj, preferred_element_type=jnp.float32)
    d_normed = d_normed + jnp.einsum(
        "rmd,cd->rmc", d_gate_pre, w_gate, preferred_element_type=jnp.float32
    )
    d_input = d_normed * ln_in_gain
    return norm_backward(d_input, normed, inv_std, -1).astype(jnp.bfloat16)


def solution(mesh):
    fits = mesh.shape["chan"] == 1 and mesh.shape["row"] in (8, 16)
    return jax.shard_map(
        kernel_shards if fits else shards,
        mesh=mesh,
        in_specs=(
            P(("grp", "row"), "chan", None),
            P(("grp", "row"), "chan", None),
            P("grp"),
            P(),
            P(),
            P(),
            P(),
            P(),
            P(),
            P(),
        ),
        out_specs=P(("grp", "row"), "chan", None),
        check_vma=False,
    )
```

```python
import functools

import jax
import jax.numpy as jnp
from jax import lax
from jax.experimental import pallas as pl
from jax.experimental.pallas import tpu as pltpu
from jax.sharding import PartitionSpec as P

F32 = jnp.float32
BF16 = jnp.bfloat16
VMEM_LIMIT = 16 * 1024 * 1024


def dot(lhs, rhs, lhs_dim, rhs_dim):
    return lax.dot_general(
        lhs, rhs, (((lhs_dim,), (rhs_dim,)), ((), ())), preferred_element_type=F32
    )


def transposed(matrix):
    return jnp.transpose(matrix.astype(F32)).astype(BF16)


def sigmoid(values):
    return 1.0 / (1.0 + jnp.exp(-values))


def column(row):
    size = row.shape[1]
    return jnp.transpose(jnp.broadcast_to(row, (size, size)))


def norm_rows(values):
    centered = values - jnp.mean(values, axis=0, keepdims=True)
    variance = jnp.mean(centered * centered, axis=0, keepdims=True)
    inv_std = lax.rsqrt(variance + 1e-05)
    return centered * inv_std, inv_std


def call(
    kernel, name, outs, args, fetched=(), unread=(), scratch=(), flops=0, limit=VMEM_LIMIT
):
    moved = sum(a.size * a.dtype.itemsize for a in args) + sum(
        o.size * jnp.dtype(o.dtype).itemsize for o in outs
    )
    n_args, n_outs, n_fetched = len(args), len(outs), len(fetched)

    def body(*refs):
        ins = list(refs[:n_args])
        rest = refs[n_args + n_outs :]
        copies = []
        for n, place in enumerate(fetched):
            copies.append(pltpu.make_async_copy(ins[place], rest[n], rest[n_fetched].at[n]))
            ins[place] = rest[n]
        for copy in copies:
            copy.start()
        for copy in copies:
            copy.wait()
        kernel(*ins, *refs[n_args : n_args + n_outs], *rest[n_fetched + (n_fetched > 0) :])

    buffers = [pltpu.VMEM(args[place].shape, args[place].dtype) for place in fetched]
    if fetched:
        buffers.append(pltpu.SemaphoreType.DMA((n_fetched,)))
    return pl.pallas_call(
        body,
        name=name,
        out_shape=outs,
        in_specs=[
            pl.BlockSpec(
                memory_space=pltpu.HBM if n in fetched else pl.ANY if n in unread else pltpu.VMEM
            )
            for n in range(n_args)
        ],
        out_specs=[pl.BlockSpec(memory_space=pltpu.VMEM) for _ in outs],
        scratch_shapes=buffers + list(scratch),
        compiler_params=pltpu.CompilerParams(vmem_limit_bytes=limit),
        cost_estimate=pl.CostEstimate(flops=flops, bytes_accessed=moved, transcendentals=0),
    )(*args)


HALVES = 2
PLANES = 2


def reorder(columns):
    size = columns.shape[0] // (HALVES * PLANES)
    parts = [columns[n * size : (n + 1) * size] for n in (0, 2, 1, 3)]
    return jnp.concatenate(parts, axis=0)


def on_lanes(cells):
    return jnp.transpose(reorder(cells.astype(F32)))


def lane_of(shape):
    return lax.broadcasted_iota(jnp.int32, shape, len(shape) - 1)


def own_plane(per_plane):
    return lax.rem(lax.div(lax.axis_index("row"), per_plane), PLANES)


def cell_masks(mask, rows):
    columns = mask[...].astype(F32)
    width = columns.shape[1]
    shape = (rows, width)
    first = lax.axis_index("row") * rows
    lane = lane_of(shape)
    own = lane == lax.broadcasted_iota(jnp.int32, shape, 0) + first
    row_mask = jnp.sum(jnp.where(own, columns, 0.0), axis=1, keepdims=True)
    cells = row_mask * columns
    size = width // (HALVES * PLANES)
    later, earlier = pltpu.roll(cells, width - size, 1), pltpu.roll(cells, size, 1)
    segment = lax.div(lane, size)
    cells = jnp.where(segment == 1, later, jnp.where(segment == 2, earlier, cells))
    return [cells[row : row + 1] for row in range(rows)]


def pack(first, second, plane):
    half = first.shape[1] // 2
    lane = lane_of(first.shape)
    zero = lane * 0 + plane == 0
    first = jnp.where(zero, pltpu.roll(first, half, 1), first)
    second = jnp.where(zero, second, pltpu.roll(second, half, 1))
    return jnp.where(lane < half, first, second)


def unpack(own, packed, is_first, plane):
    half = own.shape[1] // 2
    lane = lane_of(own.shape)
    zero = lane * 0 + plane == 0
    moved = pltpu.roll(packed, half, 1)
    other = jnp.where(zero, moved, packed) if is_first else jnp.where(zero, packed, moved)
    return jnp.where(lax.div(lane, half) == plane, own, other)


def distances(count, beside):
    far = sorted(range(2, count), key=lambda apart: -(apart // 2))
    if beside:
        return [0, 1, 2] + [apart for apart in far if apart != 2]
    return [0] + far + [1]


def partners(count, beside):
    place = lax.rem(lax.axis_index("row"), count)
    return [place ^ apart for apart in distances(count, beside)]


def gather(pieces, panel, beside):
    for place, piece in zip(partners(len(pieces), beside), pieces):
        panel[place] = piece[...]


def spread(pieces, wide, beside):
    depth = pieces[0].shape[0]
    for place, piece in zip(partners(len(pieces), beside), pieces):
        wide[pl.ds(pl.multiple_of(place * depth, depth), depth), :] = piece[...].astype(F32)


def hand_out(wide, pieces, beside):
    depth = pieces[0].shape[0]
    for place, piece in zip(partners(len(pieces), beside), pieces):
        piece[...] = wide[pl.ds(pl.multiple_of(place * depth, depth), depth), :].astype(BF16)


def gated_rows(pair, mask, gain, bias, w_proj, side):
    rows = pair.shape[0]
    hidden = w_proj.shape[1] // 4
    w_flip = transposed(w_proj[:, 2 * side * hidden : 2 * (side + 1) * hidden])
    gain_col, bias_col = column(gain[...]), column(bias[...])
    masks = cell_masks(mask, rows)
    for row in range(rows):
        normed, _ = norm_rows(on_lanes(pair[row]))
        zln = (normed * gain_col + bias_col).astype(BF16)
        proj = dot(w_flip, zln, 1, 0)
        yield row, masks[row] * sigmoid(proj[:hidden]) * proj[hidden:]


def project_right_kernel(pair, mask, gain, bias, w_proj, right_panel):
    rows = pair.shape[0]
    devices, depth, width = right_panel.shape
    block = depth // rows
    for row, right in gated_rows(pair, mask, gain, bias, w_proj, 1):
        right = right.reshape(devices // HALVES, block, width).astype(BF16)
        for half in range(HALVES):
            start = half * (devices // HALVES)
            right_panel[
                start : start + devices // HALVES, row * block : (row + 1) * block, :
            ] = right


def project_left_kernel(pair, mask, gain, bias, w_proj, after, *refs):
    del after
    *pieces, left_panel = refs
    rows = pair.shape[0]
    per_plane, depth, width = left_panel.shape
    block = depth // rows
    for row, left in gated_rows(pair, mask, gain, bias, w_proj, 0):
        left = left.reshape(per_plane, block, width).astype(BF16)
        left_panel[:, row * block : (row + 1) * block, :] = left
    for place, piece in zip(partners(len(pieces), True), pieces):
        piece[...] = left_panel[lax.rem(place, per_plane)]


def pack_rows(cells, packed, per_plane):
    rows, channels, _ = cells.shape
    plane = own_plane(per_plane)
    for row in range(rows // 2):
        both = pack(cells[row], cells[row + rows // 2], plane)
        packed[row * channels : (row + 1) * channels, :] = both.astype(BF16)


def unpack_row(own, packed, row, rows, per_plane):
    channels = own.shape[0]
    place = row % (rows // 2) * channels
    other = packed[place : place + channels, :].astype(F32)
    return unpack(own, other, row < rows // 2, own_plane(per_plane))


def prepare_kernel(
    pair, cotangent, gain, bias, w_gate, out_gain, w_out, after, d_hat_centered, gate_slope, d_hat_sent
):
    del after
    gate_flip = transposed(w_gate[...])
    gain_col, bias_col = column(gain[...]), column(bias[...])
    out_gain_col = column(out_gain[...])
    for row in range(pair.shape[0]):
        normed, _ = norm_rows(on_lanes(pair[row]))
        zln = (normed * gain_col + bias_col).astype(BF16)
        gate = sigmoid(dot(gate_flip, zln, 1, 0))
        cot = on_lanes(cotangent[row])
        d_scaled = (cot * gate).astype(BF16)
        d_hat = dot(w_out[...], d_scaled, 1, 0) * out_gain_col
        d_hat_centered[row] = d_hat - jnp.mean(d_hat, axis=0, keepdims=True)
        gate_slope[row] = cot * gate * (1.0 - gate)
    pack_rows(d_hat_centered, d_hat_sent, pair.shape[1] // (HALVES * PLANES) // pair.shape[0])


def sort_left_kernel(*refs):
    *pieces, left_all, left_wide = refs
    block, left_rows, _ = left_all.shape
    spread(pieces, left_wide, True)
    for h in range(block):
        left_all[h] = left_wide[pl.ds(h, left_rows, stride=block), :].astype(BF16)


def twice(matrix):
    return jnp.concatenate([matrix, matrix], axis=0)


def tri_kernel(right_panel, left_all, after, right_all, *refs):
    del after
    *pieces, right_wide, tri_wide = refs
    block, right_rows, width = right_all.shape
    cells = left_all.shape[1] // PLANES
    low = lane_of((cells, width)) < width // 2
    right_wide[...] = right_panel[...].astype(F32).reshape(right_wide.shape)
    for h in range(block):
        right = right_wide[pl.ds(h, right_rows, stride=block), :].astype(BF16)
        right_all[h] = right
        tri = dot(left_all[h], twice(right), 1, 1)
        tri_wide[pl.ds(h, cells, stride=block), :] = jnp.where(low, tri[:cells], tri[cells:])
    hand_out(tri_wide, pieces, False)


def cell_row(ref, row, rows):
    count, depth, width = ref.shape
    block = depth // rows
    return ref[:, row * block : (row + 1) * block, :].astype(F32).reshape(count * block, width)


def middle_kernel(d_hat_centered, d_hat_other, *refs):
    per_plane = (len(refs) - 2) // 2
    products, pieces = refs[:per_plane], refs[per_plane : 2 * per_plane]
    panel, d_panel = refs[2 * per_plane :]
    rows = d_hat_centered.shape[0]
    _, depth, width = panel.shape
    block = depth // rows
    gather(products, panel, False)
    for row in range(rows):
        tri_hat, inv_std = norm_rows(cell_row(panel, row, rows))
        d_hat = unpack_row(d_hat_centered[row], d_hat_other, row, rows, per_plane)
        cross = jnp.mean(d_hat * tri_hat, axis=0, keepdims=True)
        d_tri = inv_std * (d_hat - tri_hat * cross)
        d_panel[:, row * block : (row + 1) * block, :] = d_tri.reshape(
            per_plane, block, width
        ).astype(BF16)
    for place, piece in zip(partners(per_plane, False), pieces):
        piece[...] = d_panel[place]


def d_right_kernel(left_all, *refs):
    *d_products, d_right_panel, d_tri_all, tri_wide, right_wide = refs
    block, _, width = left_all.shape
    cells = d_tri_all.shape[1] // PLANES
    right_rows = right_wide.shape[0] // block
    low = lane_of((cells, width)) < width // 2
    spread(d_products, tri_wide, False)
    for h in range(block):
        d_tri = tri_wide[pl.ds(h, cells, stride=block), :]
        parts = [jnp.where(low, d_tri, 0.0), jnp.where(low, 0.0, d_tri)]
        d_tri = jnp.concatenate(parts, axis=0).astype(BF16)
        d_tri_all[h] = d_tri
        d_right = dot(d_tri, left_all[h], 0, 0)
        right_wide[pl.ds(h, right_rows, stride=block), :] = (
            d_right[:right_rows] + d_right[right_rows:]
        )
    d_right_panel[...] = right_wide[...].astype(BF16).reshape(d_right_panel.shape)


def d_left_kernel(d_tri_all, right_all, *refs):
    *pieces, left_wide = refs
    block, left_rows, _ = d_tri_all.shape
    for h in range(block):
        left_wide[pl.ds(h, left_rows, stride=block), :] = dot(
            d_tri_all[h], twice(right_all[h]), 1, 0
        )
    hand_out(left_wide, pieces, True)


def pack_tri_kernel(after, *refs):
    del after
    *products, tri_sent, panel, cells = refs
    rows = cells.shape[0]
    gather(products, panel, False)
    for row in range(rows):
        cells[row] = cell_row(panel, row, rows)
    pack_rows(cells, tri_sent, len(products))


def gate_back_kernel(gate_slope, out_gain, out_bias, w_out, tri_other, *refs):
    *products, d_gate_pre, panel = refs
    rows = gate_slope.shape[0]
    gather(products, panel, False)
    out_flip = transposed(w_out[...])
    out_gain_col, out_bias_col = column(out_gain[...]), column(out_bias[...])
    for row in range(rows):
        own = cell_row(panel, row, rows)
        tri_hat, _ = norm_rows(unpack_row(own, tri_other, row, rows, len(products)))
        scaled = (tri_hat * out_gain_col + out_bias_col).astype(BF16)
        d_gate_pre[row] = (dot(out_flip, scaled, 1, 0) * gate_slope[row]).astype(BF16)


def slopes_kernel(
    pair, mask, gain, bias, w_proj, w_gate, after, slopes, normed_in, inv_in, in_gain, weights
):
    del after
    rows = pair.shape[0]
    hidden = w_proj.shape[1] // 4
    w_flip = transposed(w_proj[...])
    gain_col, bias_col = column(gain[...]), column(bias[...])
    in_gain[...] = gain_col
    weights[...] = jnp.concatenate([w_proj[...], w_gate[...]], axis=1)
    masks = cell_masks(mask, rows)
    for row in range(rows):
        normed, inv_std = norm_rows(on_lanes(pair[row]))
        normed_in[row] = normed.astype(normed_in.dtype)
        inv_in[row : row + 1] = inv_std
        zln = (normed * gain_col + bias_col).astype(BF16)
        proj = dot(w_flip, zln, 1, 0)
        for side in range(2):
            base = 2 * side * hidden
            sig = sigmoid(proj[base : base + hidden])
            masked = masks[row] * sig
            value = masked * (1.0 - sig) * proj[base + hidden : base + 2 * hidden]
            slopes[row, base : base + hidden, :] = value.astype(slopes.dtype)
            slopes[row, base + hidden : base + 2 * hidden, :] = masked.astype(slopes.dtype)


def sort_d_left_kernel(*refs):
    *pieces, d_left_panel = refs
    gather(pieces, d_left_panel, True)


def finish_kernel(
    d_right_panel, d_left_panel, slopes, d_gate_pre, normed_in, inv_in, gain_col, weights, grad
):
    rows = grad.shape[0]
    hidden = slopes.shape[1] // 4
    for row in range(rows):
        parts = []
        for side, panel in enumerate((d_left_panel, d_right_panel)):
            d_value = cell_row(panel, row, rows)
            d_value = d_value[:hidden] + d_value[hidden:]
            for base in (2 * side * hidden, (2 * side + 1) * hidden):
                slope = slopes[row, base : base + hidden, :].astype(F32)
                parts.append((d_value * slope).astype(BF16))
        parts.append(d_gate_pre[row])
        d_in = dot(weights[...], jnp.concatenate(parts, axis=0), 1, 0) * gain_col[...]
        normed = normed_in[row].astype(F32)
        mean_grad = jnp.mean(d_in, axis=0, keepdims=True)
        mean_cross = jnp.mean(d_in * normed, axis=0, keepdims=True)
        result = inv_in[row : row + 1] * (d_in - mean_grad - normed * mean_cross)
        grad[row] = reorder(jnp.transpose(result)).astype(BF16)


def swap(values, per_plane):
    groups = [
        [(half * PLANES + plane) * per_plane + n for half in range(HALVES) for n in range(per_plane)]
        for plane in range(PLANES)
    ]
    return lax.all_to_all(
        values, "row", split_axis=0, concat_axis=0, tiled=True, axis_index_groups=groups
    )


def swap_with(values, apart):
    devices = range(lax.axis_size("row"))
    return lax.ppermute(values, "row", [(d, d ^ apart) for d in devices])


def swap_pieces(pieces, beside):
    apart = distances(len(pieces), beside)
    return [pieces[0]] + [
        swap_with(pieces[step], apart[step]) for step in range(1, len(pieces))
    ]


def kernel_shards(
    pair,
    cotangent,
    residue_mask,
    ln_in_gain,
    ln_in_bias,
    w_proj,
    w_gate,
    ln_out_gain,
    ln_out_bias,
    w_out,
):
    rows, width, channels = pair.shape
    hidden = w_out.shape[0]
    per_plane = lax.axis_size("row") // (HALVES * PLANES)
    count = per_plane * PLANES
    block = hidden // per_plane
    left_rows, right_rows = rows * count, rows * per_plane * HALVES
    shape = jax.ShapeDtypeStruct
    piece = shape((rows * block, width), BF16)
    wide_panel = shape((per_plane * HALVES, rows * block, width), BF16)
    swapped = shape((rows // 2 * hidden, width), BF16)
    mask = residue_mask.reshape(1, width)
    gain, bias = ln_in_gain.reshape(1, channels), ln_in_bias.reshape(1, channels)
    out_gain, out_bias = ln_out_gain.reshape(1, hidden), ln_out_bias.reshape(1, hidden)
    cells = rows * width
    plane_panel = pltpu.VMEM((per_plane, rows * block, width), BF16)
    left_wide = pltpu.VMEM((left_rows * block, width), F32)
    right_wide = pltpu.VMEM((right_rows * block, width), F32)
    tri_wide = pltpu.VMEM((rows * per_plane * block, width), F32)
    (own_right,) = call(
        project_right_kernel,
        "project_right",
        [wide_panel],
        [pair, mask, gain, bias, w_proj],
        fetched=range(5),
        flops=2 * cells * channels * 2 * hidden,
        limit=64 * 1024 * 1024 - 640 * 1024,
    )
    right_panel = swap(own_right, per_plane)
    pieces = call(
        project_left_kernel,
        "project_left",
        [piece] * count,
        [pair, mask, gain, bias, w_proj, own_right],
        fetched=range(5),
        unread=(5,),
        scratch=[plane_panel],
        flops=2 * cells * channels * 2 * hidden,
    )
    pieces = swap_pieces(pieces, True)
    (left_all,) = call(
        sort_left_kernel,
        "sort_left",
        [shape((block, left_rows, width), BF16)],
        pieces,
        scratch=[left_wide],
    )
    d_hat_centered, gate_slope, d_hat_sent = call(
        prepare_kernel,
        "prepare",
        [shape((rows, hidden, width), F32), shape((rows, channels, width), F32), swapped],
        [pair, cotangent, gain, bias, w_gate, out_gain, w_out, own_right],
        fetched=range(7),
        unread=(7,),
        flops=2 * cells * channels * 2 * hidden,
    )
    d_hat_other = swap_with(d_hat_sent, per_plane)
    right_all, *products = call(
        tri_kernel,
        "tri",
        [shape((block, right_rows, width), BF16)] + [piece] * per_plane,
        [right_panel, left_all, d_hat_other],
        unread=(2,),
        scratch=[right_wide, tri_wide],
        flops=2 * block * left_rows * width * right_rows,
    )
    products = swap_pieces(products, False)
    d_products = call(
        middle_kernel,
        "middle",
        [piece] * per_plane,
        [d_hat_centered, d_hat_other, *products],
        scratch=[plane_panel, plane_panel],
        flops=20 * cells * hidden,
    )
    d_products = swap_pieces(d_products, False)
    own_d_right, d_tri_all = call(
        d_right_kernel,
        "d_right",
        [wide_panel, shape((block, left_rows, width), BF16)],
        [left_all, *d_products],
        scratch=[tri_wide, right_wide],
        flops=2 * block * left_rows * width * right_rows,
    )
    d_right_panel = swap(own_d_right, per_plane)
    d_pieces = call(
        d_left_kernel,
        "d_left",
        [piece] * count,
        [d_tri_all, right_all],
        scratch=[left_wide],
        flops=2 * block * left_rows * width * right_rows,
    )
    d_pieces = swap_pieces(d_pieces, True)
    d_left_panel = shape((count, rows * block, width), BF16)
    (d_left_panel,) = call(sort_d_left_kernel, "sort_d_left", [d_left_panel], d_pieces)
    (tri_sent,) = call(
        pack_tri_kernel,
        "pack_tri",
        [swapped],
        [own_d_right, *products],
        unread=(0,),
        scratch=[plane_panel, pltpu.VMEM((rows, hidden, width), F32)],
    )
    tri_other = swap_with(tri_sent, per_plane)
    (d_gate_pre,) = call(
        gate_back_kernel,
        "gate_back",
        [shape((rows, channels, width), BF16)],
        [gate_slope, out_gain, out_bias, w_out, tri_other, *products],
        fetched=range(1, 4),
        scratch=[plane_panel],
        flops=2 * cells * channels * hidden,
    )
    slopes, normed_in, inv_in, gain_col, weights = call(
        slopes_kernel,
        "slopes",
        [
            shape((rows, 4 * hidden, width), BF16),
            shape((rows, channels, width), BF16),
            shape((rows, width), F32),
            shape((channels, channels), F32),
            shape((channels, 4 * hidden + channels), BF16),
        ],
        [pair, mask, gain, bias, w_proj, w_gate, d_gate_pre],
        fetched=range(6),
        unread=(6,),
        flops=2 * cells * channels * 4 * hidden,
    )
    (grad,) = call(
        finish_kernel,
        "finish",
        [shape(pair.shape, BF16)],
        [
            d_right_panel,
            d_left_panel,
            slopes,
            d_gate_pre,
            normed_in,
            inv_in,
            gain_col,
            weights,
        ],
        flops=2 * cells * channels * 4 * hidden,
    )
    return grad


def normalize(values, reduce_axis):
    mean_value = jnp.mean(values, axis=reduce_axis, keepdims=True)
    centered = values - mean_value
    variance = jnp.mean(centered * centered, axis=reduce_axis, keepdims=True)
    inv_std = lax.rsqrt(variance + 1e-05)
    return (centered * inv_std, inv_std)


def norm_backward(upstream, normed, inv_std, reduce_axis):
    mean_grad = jnp.mean(upstream, axis=reduce_axis, keepdims=True)
    mean_cross = jnp.mean(upstream * normed, axis=reduce_axis, keepdims=True)
    return inv_std * (upstream - mean_grad - normed * mean_cross)


def shards(
    pair,
    cotangent,
    residue_mask,
    ln_in_gain,
    ln_in_bias,
    w_proj,
    w_gate,
    ln_out_gain,
    ln_out_bias,
    w_out,
):
    local_rows = pair.shape[0]
    local_cols = pair.shape[1]
    hidden = w_out.shape[0]
    chan_index = lax.axis_index("chan")
    row_start = lax.axis_index("row") * local_rows
    col_start = chan_index * local_cols
    mask_float = residue_mask.astype(jnp.float32)
    row_mask = lax.dynamic_slice_in_dim(mask_float, row_start, local_rows)
    col_mask = lax.dynamic_slice_in_dim(mask_float, col_start, local_cols)
    cell_mask = (row_mask[:, None] * col_mask[None, :])[None]
    normed, inv_std = normalize(pair.astype(jnp.float32), -1)
    normed_pair = (normed * ln_in_gain + ln_in_bias).astype(jnp.bfloat16)
    projected = jnp.einsum("rmc,ch->hrm", normed_pair, w_proj, preferred_element_type=jnp.float32)
    left_panel = (
        cell_mask * jax.nn.sigmoid(projected[:hidden]) * projected[hidden : 2 * hidden]
    ).astype(jnp.bfloat16)
    right_panel = (
        cell_mask * jax.nn.sigmoid(projected[2 * hidden : 3 * hidden]) * projected[3 * hidden :]
    ).astype(jnp.bfloat16)
    panels = lax.all_to_all(
        jnp.stack([left_panel, right_panel]), "row", split_axis=1, concat_axis=2, tiled=True
    )
    left_all = panels[0]
    right_all = panels[1]
    right_rows = lax.all_to_all(right_all, "chan", split_axis=1, concat_axis=2, tiled=True)
    partner = right_rows
    tri_part = jnp.einsum(
        "gik,gjk->gij",
        lax.all_gather(left_all, "chan", axis=2, tiled=True),
        partner,
        preferred_element_type=jnp.float32,
    ).astype(jnp.bfloat16)
    tri_cells = lax.all_to_all(tri_part, "row", split_axis=1, concat_axis=0, tiled=True)
    tri_hat, inv_tri = normalize(tri_cells.astype(jnp.float32), 0)
    scaled = (tri_hat * ln_out_gain[:, None, None] + ln_out_bias[:, None, None]).astype(
        jnp.bfloat16
    )
    proj_out = jnp.einsum("hrm,hc->rmc", scaled, w_out, preferred_element_type=jnp.float32)
    gate_value = jax.nn.sigmoid(
        jnp.einsum("rmc,cd->rmd", normed_pair, w_gate, preferred_element_type=jnp.float32)
    )
    cot_float = cotangent.astype(jnp.float32)
    d_gate_pre = (cot_float * proj_out * gate_value * (1.0 - gate_value)).astype(jnp.bfloat16)
    d_scaled = (cot_float * gate_value).astype(jnp.bfloat16)
    d_hat = jnp.einsum("rmc,hc->hrm", d_scaled, w_out, preferred_element_type=jnp.float32)
    d_hat = d_hat * ln_out_gain[:, None, None]
    d_tri = norm_backward(d_hat, tri_hat, inv_tri, 0).astype(jnp.bfloat16)
    d_tri_all = lax.all_to_all(d_tri, "row", split_axis=0, concat_axis=1, tiled=True)
    panel_piece = lax.all_gather(d_tri_all, "chan", axis=2, tiled=True)
    partner = right_all
    d_left = jnp.einsum("gij,gjk->gik", panel_piece, partner, preferred_element_type=jnp.float32)
    contribution = jnp.einsum(
        "gij,gik->gjk", panel_piece, left_all, preferred_element_type=jnp.float32
    )
    d_right = contribution
    d_left, d_right = (d_left, d_right)
    d_stack = jnp.stack([d_left, d_right]).astype(jnp.bfloat16)
    d_panels = lax.all_to_all(d_stack, "row", split_axis=2, concat_axis=1, tiled=True)

    def gating(d_value, gate_proj, value_proj):
        sigmoid_val = jax.nn.sigmoid(gate_proj)
        masked_grad = d_value.astype(jnp.float32) * cell_mask
        return (
            masked_grad * value_proj * sigmoid_val * (1.0 - sigmoid_val),
            masked_grad * sigmoid_val,
        )

    gate_left, value_left = gating(d_panels[0], projected[:hidden], projected[hidden : 2 * hidden])
    gate_right, value_right = gating(
        d_panels[1], projected[2 * hidden : 3 * hidden], projected[3 * hidden :]
    )
    d_proj = jnp.concatenate([gate_left, value_left, gate_right, value_right], axis=0).astype(
        jnp.bfloat16
    )
    d_normed = jnp.einsum("hrm,ch->rmc", d_proj, w_proj, preferred_element_type=jnp.float32)
    d_normed = d_normed + jnp.einsum(
        "rmd,cd->rmc", d_gate_pre, w_gate, preferred_element_type=jnp.float32
    )
    d_input = d_normed * ln_in_gain
    return norm_backward(d_input, normed, inv_std, -1).astype(jnp.bfloat16)


def solution(mesh):
    fits = mesh.shape["chan"] == 1 and mesh.shape["row"] == 16
    return jax.shard_map(
        kernel_shards if fits else shards,
        mesh=mesh,
        in_specs=(
            P(("grp", "row"), "chan", None),
            P(("grp", "row"), "chan", None),
            P("grp"),
            P(),
            P(),
            P(),
            P(),
            P(),
            P(),
            P(),
        ),
        out_specs=P(("grp", "row"), "chan", None),
        check_vma=False,
    )
```

```python
import functools

import jax
import jax.numpy as jnp
from jax import lax
from jax.experimental import pallas as pl
from jax.experimental.pallas import tpu as pltpu
from jax.sharding import PartitionSpec as P

F32 = jnp.float32
BF16 = jnp.bfloat16
VMEM_LIMIT = 16 * 1024 * 1024


def dot(lhs, rhs, lhs_dim, rhs_dim):
    return lax.dot_general(
        lhs, rhs, (((lhs_dim,), (rhs_dim,)), ((), ())), preferred_element_type=F32
    )


def transposed(matrix):
    return jnp.transpose(matrix.astype(F32)).astype(BF16)


def sigmoid(values):
    return 1.0 / (1.0 + jnp.exp(-values))


def column(row):
    size = row.shape[1]
    return jnp.transpose(jnp.broadcast_to(row, (size, size)))


def norm_rows(values):
    centered = values - jnp.mean(values, axis=0, keepdims=True)
    variance = jnp.mean(centered * centered, axis=0, keepdims=True)
    inv_std = lax.rsqrt(variance + 1e-05)
    return centered * inv_std, inv_std


def call(
    kernel, name, outs, args, fetched=(), unread=(), scratch=(), flops=0, limit=VMEM_LIMIT
):
    moved = sum(a.size * a.dtype.itemsize for a in args) + sum(
        o.size * jnp.dtype(o.dtype).itemsize for o in outs
    )
    n_args, n_outs, n_fetched = len(args), len(outs), len(fetched)

    def body(*refs):
        ins = list(refs[:n_args])
        rest = refs[n_args + n_outs :]
        copies = []
        for n, place in enumerate(fetched):
            copies.append(pltpu.make_async_copy(ins[place], rest[n], rest[n_fetched].at[n]))
            ins[place] = rest[n]
        for copy in copies:
            copy.start()
        for copy in copies:
            copy.wait()
        kernel(*ins, *refs[n_args : n_args + n_outs], *rest[n_fetched + (n_fetched > 0) :])

    buffers = [pltpu.VMEM(args[place].shape, args[place].dtype) for place in fetched]
    if fetched:
        buffers.append(pltpu.SemaphoreType.DMA((n_fetched,)))
    return pl.pallas_call(
        body,
        name=name,
        out_shape=outs,
        in_specs=[
            pl.BlockSpec(
                memory_space=pltpu.HBM if n in fetched else pl.ANY if n in unread else pltpu.VMEM
            )
            for n in range(n_args)
        ],
        out_specs=[pl.BlockSpec(memory_space=pltpu.VMEM) for _ in outs],
        scratch_shapes=buffers + list(scratch),
        compiler_params=pltpu.CompilerParams(vmem_limit_bytes=limit),
        cost_estimate=pl.CostEstimate(flops=flops, bytes_accessed=moved, transcendentals=0),
    )(*args)


def cell_masks(mask, rows):
    columns = mask[...].astype(F32)
    shape = (rows, columns.shape[1])
    first = lax.axis_index("row") * rows
    own = lax.broadcasted_iota(jnp.int32, shape, 1) == (
        lax.broadcasted_iota(jnp.int32, shape, 0) + first
    )
    row_mask = jnp.sum(jnp.where(own, columns, 0.0), axis=1, keepdims=True)
    cells = row_mask * columns
    return [cells[row : row + 1] for row in range(rows)]


def wide_order(devices, count, back):
    order = []
    for place in range(count):
        if back:
            inner = place ^ (count // 2)
            order += [inner if place < count // 2 else inner ^ 2, count + place]
        else:
            order += [count + (place ^ 2), place ^ (count // 2)]
    return order


def distance(step, count):
    far = sorted(range(3, count), key=lambda apart: -(apart // 2))
    return [*range(min(3, count)), *far][step]


def partner(step, count):
    return lax.rem(lax.axis_index("row"), count) ^ distance(step, count)


def gated_rows(pair, mask, gain, bias, w_proj, side):
    rows = pair.shape[0]
    hidden = w_proj.shape[1] // 4
    w_flip = transposed(w_proj[:, 2 * side * hidden : 2 * (side + 1) * hidden])
    gain_col, bias_col = column(gain[...]), column(bias[...])
    masks = cell_masks(mask, rows)
    for row in range(rows):
        normed, _ = norm_rows(jnp.transpose(pair[row].astype(F32)))
        zln = (normed * gain_col + bias_col).astype(BF16)
        proj = dot(w_flip, zln, 1, 0)
        yield row, masks[row] * sigmoid(proj[:hidden]) * proj[hidden:]


def project_right_kernel(pair, mask, gain, bias, w_proj, right_panel):
    rows = pair.shape[0]
    devices, depth, width = right_panel.shape
    block = depth // rows
    count = w_proj.shape[1] // 4 // block
    for row, right in gated_rows(pair, mask, gain, bias, w_proj, 1):
        right = right.reshape(count, block, width).astype(BF16)
        for rank in range(devices):
            place = wide_order(devices, count, False)[rank] % count
            right_panel[rank, row * block : (row + 1) * block, :] = right[place]


def project_left_kernel(pair, mask, gain, bias, w_proj, after, *refs):
    del after
    *pieces, left_panel = refs
    rows = pair.shape[0]
    count, depth, width = left_panel.shape
    block = depth // rows
    for row, left in gated_rows(pair, mask, gain, bias, w_proj, 0):
        left = left.reshape(count, block, width).astype(BF16)
        left_panel[:, row * block : (row + 1) * block, :] = left
    for step, piece in enumerate(pieces):
        piece[...] = left_panel[partner(step, count)]


def prepare_kernel(
    pair, cotangent, gain, bias, w_gate, out_gain, w_out, d_hat_centered, gate_slope
):
    gate_flip = transposed(w_gate[...])
    gain_col, bias_col = column(gain[...]), column(bias[...])
    out_gain_col = column(out_gain[...])
    for row in range(pair.shape[0]):
        normed, _ = norm_rows(jnp.transpose(pair[row].astype(F32)))
        zln = (normed * gain_col + bias_col).astype(BF16)
        gate = sigmoid(dot(gate_flip, zln, 1, 0))
        cot = jnp.transpose(cotangent[row].astype(F32))
        d_scaled = (cot * gate).astype(BF16)
        d_hat = dot(w_out[...], d_scaled, 1, 0) * out_gain_col
        d_hat_centered[row] = d_hat - jnp.mean(d_hat, axis=0, keepdims=True)
        gate_slope[row] = cot * gate * (1.0 - gate)


def spread(panel, wide):
    wide[...] = panel[...].astype(F32).reshape(wide.shape)


def wide_places(panel, count, back):
    devices, depth, _ = panel.shape
    for rank, device in enumerate(wide_order(devices, count, back)):
        yield rank, slice(device * depth, (device + 1) * depth)


def sort_left_kernel(*refs):
    *pieces, left_all, left_wide = refs
    block, left_rows, _ = left_all.shape
    depth = pieces[0].shape[0]
    for step, piece in enumerate(pieces):
        start = pl.multiple_of(partner(step, len(pieces)) * depth, depth)
        left_wide[pl.ds(start, depth), :] = piece[...].astype(F32)
    for h in range(block):
        left_all[h] = left_wide[pl.ds(h, left_rows, stride=block), :].astype(BF16)


def tri_kernel(right_panel, left_all, after, products, right_all, left_wide, right_wide):
    del after
    block, left_rows, _ = left_all.shape
    right_rows = right_all.shape[1]
    for rank, place in wide_places(right_panel, products.shape[0], False):
        right_wide[place, :] = right_panel[rank].astype(F32)
    for h in range(block):
        right = right_wide[pl.ds(h, right_rows, stride=block), :].astype(BF16)
        right_all[h] = right
        left_wide[pl.ds(h, left_rows, stride=block), :] = dot(left_all[h], right, 1, 1)
    products[...] = left_wide[...].astype(BF16).reshape(products.shape)


def cell_row(ref, row, rows):
    count, depth, width = ref.shape
    block = depth // rows
    return ref[:, row * block : (row + 1) * block, :].astype(F32).reshape(count * block, width)


def middle_kernel(products, d_hat_centered, d_products):
    rows = d_hat_centered.shape[0]
    count, depth, width = products.shape
    block = depth // rows
    for row in range(rows):
        tri_hat, inv_std = norm_rows(cell_row(products, row, rows))
        d_hat = d_hat_centered[row]
        cross = jnp.mean(d_hat * tri_hat, axis=0, keepdims=True)
        d_tri = inv_std * (d_hat - tri_hat * cross)
        d_products[:, row * block : (row + 1) * block, :] = d_tri.reshape(
            count, block, width
        ).astype(BF16)


def d_right_kernel(d_products, left_all, d_right_panel, d_tri_all, left_wide, right_wide):
    block, left_rows, _ = left_all.shape
    right_rows = right_wide.shape[0] // block
    spread(d_products, left_wide)
    for h in range(block):
        d_tri = left_wide[pl.ds(h, left_rows, stride=block), :].astype(BF16)
        d_tri_all[h] = d_tri
        right_wide[pl.ds(h, right_rows, stride=block), :] = dot(d_tri, left_all[h], 0, 0)
    for rank, place in wide_places(d_right_panel, d_products.shape[0], True):
        d_right_panel[rank] = right_wide[place, :].astype(BF16)


def d_left_kernel(d_tri_all, right_all, *refs):
    *pieces, left_wide = refs
    block, left_rows, _ = d_tri_all.shape
    for h in range(block):
        left_wide[pl.ds(h, left_rows, stride=block), :] = dot(d_tri_all[h], right_all[h], 1, 0)
    depth = pieces[0].shape[0]
    for step, piece in enumerate(pieces):
        start = pl.multiple_of(partner(step, len(pieces)) * depth, depth)
        piece[...] = left_wide[pl.ds(start, depth), :].astype(BF16)


def gate_back_kernel(products, gate_slope, out_gain, out_bias, w_out, d_gate_pre):
    rows = gate_slope.shape[0]
    out_flip = transposed(w_out[...])
    out_gain_col, out_bias_col = column(out_gain[...]), column(out_bias[...])
    for row in range(rows):
        tri_hat, _ = norm_rows(cell_row(products, row, rows))
        scaled = (tri_hat * out_gain_col + out_bias_col).astype(BF16)
        d_gate_pre[row] = (dot(out_flip, scaled, 1, 0) * gate_slope[row]).astype(BF16)


def slopes_kernel(
    pair, mask, gain, bias, w_proj, w_gate, after, slopes, normed_in, inv_in, in_gain, weights
):
    del after
    rows = pair.shape[0]
    hidden = w_proj.shape[1] // 4
    w_flip = transposed(w_proj[...])
    gain_col, bias_col = column(gain[...]), column(bias[...])
    in_gain[...] = gain_col
    weights[...] = jnp.concatenate([w_proj[...], w_gate[...]], axis=1)
    masks = cell_masks(mask, rows)
    for row in range(rows):
        normed, inv_std = norm_rows(jnp.transpose(pair[row].astype(F32)))
        normed_in[row] = normed.astype(normed_in.dtype)
        inv_in[row : row + 1] = inv_std
        zln = (normed * gain_col + bias_col).astype(BF16)
        proj = dot(w_flip, zln, 1, 0)
        for side in range(2):
            base = 2 * side * hidden
            sig = sigmoid(proj[base : base + hidden])
            masked = masks[row] * sig
            value = masked * (1.0 - sig) * proj[base + hidden : base + 2 * hidden]
            slopes[row, base : base + hidden, :] = value.astype(slopes.dtype)
            slopes[row, base + hidden : base + 2 * hidden, :] = masked.astype(slopes.dtype)


def sort_d_left_kernel(*refs):
    *pieces, d_left_panel = refs
    for step, piece in enumerate(pieces):
        d_left_panel[partner(step, len(pieces))] = piece[...]


def both_halves(blocks, count):
    order = wide_order(2 * count, count, True)
    return jnp.stack(
        [blocks[order.index(place)] + blocks[order.index(count + place)] for place in range(count)]
    )


def finish_kernel(
    d_right_panel, d_left_panel, slopes, d_gate_pre, normed_in, inv_in, gain_col, weights, grad
):
    rows = grad.shape[0]
    count, depth, width = d_left_panel.shape
    hidden = count * depth // rows
    for row in range(rows):
        d_right = cell_row(d_right_panel, row, rows)
        d_right = both_halves(d_right.reshape(2 * count, depth // rows, width), count)
        parts = []
        for side, d_value in enumerate((cell_row(d_left_panel, row, rows), d_right.reshape(hidden, width))):
            for base in (2 * side * hidden, (2 * side + 1) * hidden):
                slope = slopes[row, base : base + hidden, :].astype(F32)
                parts.append((d_value * slope).astype(BF16))
        parts.append(d_gate_pre[row])
        d_in = dot(weights[...], jnp.concatenate(parts, axis=0), 1, 0) * gain_col[...]
        normed = normed_in[row].astype(F32)
        mean_grad = jnp.mean(d_in, axis=0, keepdims=True)
        mean_cross = jnp.mean(d_in * normed, axis=0, keepdims=True)
        result = inv_in[row : row + 1] * (d_in - mean_grad - normed * mean_cross)
        grad[row] = jnp.transpose(result).astype(BF16)


def swap(values, count, back):
    groups = [wide_order(lax.axis_size("row"), count, back)]
    return lax.all_to_all(
        values, "row", split_axis=0, concat_axis=0, tiled=True, axis_index_groups=groups
    )


def swap_half(values, count):
    devices = range(lax.axis_size("row"))
    groups = [[d for d in devices if d // count == half] for half in range(len(devices) // count)]
    return lax.all_to_all(
        values, "row", split_axis=0, concat_axis=0, tiled=True, axis_index_groups=groups
    )


def swap_pieces(pieces):
    devices = range(lax.axis_size("row"))
    count = len(pieces)
    return [pieces[0]] + [
        lax.ppermute(pieces[step], "row", [(d, d ^ distance(step, count)) for d in devices])
        for step in range(1, count)
    ]


def kernel_shards(
    pair,
    cotangent,
    residue_mask,
    ln_in_gain,
    ln_in_bias,
    w_proj,
    w_gate,
    ln_out_gain,
    ln_out_bias,
    w_out,
):
    rows, width, channels = pair.shape
    hidden = w_out.shape[0]
    halves = 2
    devices = lax.axis_size("row")
    count = devices // halves
    block = hidden // count
    left_rows, right_rows = rows * count, rows * devices
    shape = jax.ShapeDtypeStruct
    panel = shape((count, rows * block, width), BF16)
    wide_panel = shape((devices, rows * block, width), BF16)
    mask = residue_mask.reshape(1, width)
    gain, bias = ln_in_gain.reshape(1, channels), ln_in_bias.reshape(1, channels)
    out_gain, out_bias = ln_out_gain.reshape(1, hidden), ln_out_bias.reshape(1, hidden)
    cells = rows * width
    piece = shape((rows * block, width), BF16)
    left_panel = pltpu.VMEM(panel.shape, BF16)
    left_wide = pltpu.VMEM((left_rows * block, width), F32)
    right_wide = pltpu.VMEM((right_rows * block, width), F32)
    (own_right,) = call(
        project_right_kernel,
        "project_right",
        [wide_panel],
        [pair, mask, gain, bias, w_proj],
        fetched=range(5),
        flops=2 * cells * channels * 2 * hidden,
        limit=64 * 1024 * 1024 - 640 * 1024,
    )
    right_panel = swap(own_right, count, False)
    pieces = call(
        project_left_kernel,
        "project_left",
        [piece] * count,
        [pair, mask, gain, bias, w_proj, own_right],
        fetched=range(5),
        unread=(5,),
        scratch=[left_panel],
        flops=2 * cells * channels * 2 * hidden,
    )
    pieces = swap_pieces(pieces)
    (left_all,) = call(
        sort_left_kernel,
        "sort_left",
        [shape((block, left_rows, width), BF16)],
        pieces,
        scratch=[left_wide],
    )
    d_hat_centered, gate_slope = call(
        prepare_kernel,
        "prepare",
        [shape((rows, hidden, width), F32), shape((rows, channels, width), F32)],
        [pair, cotangent, gain, bias, w_gate, out_gain, w_out],
        fetched=range(7),
        flops=2 * cells * channels * 2 * hidden,
    )
    products, right_all = call(
        tri_kernel,
        "tri",
        [panel, shape((block, right_rows, width), BF16)],
        [right_panel, left_all, d_hat_centered],
        unread=(2,),
        scratch=[left_wide, right_wide],
        flops=2 * block * left_rows * width * right_rows,
    )
    products = swap_half(products, count)
    (d_products,) = call(
        middle_kernel,
        "middle",
        [panel],
        [products, d_hat_centered],
        flops=20 * cells * hidden,
    )
    d_products = swap_half(d_products, count)
    d_right_panel, d_tri_all = call(
        d_right_kernel,
        "d_right",
        [wide_panel, shape((block, left_rows, width), BF16)],
        [d_products, left_all],
        scratch=[left_wide, right_wide],
        flops=2 * block * left_rows * width * right_rows,
    )
    d_right_panel = swap(d_right_panel, count, True)
    d_pieces = call(
        d_left_kernel,
        "d_left",
        [piece] * count,
        [d_tri_all, right_all],
        scratch=[left_wide],
        flops=2 * block * left_rows * width * right_rows,
    )
    d_pieces = swap_pieces(d_pieces)
    (d_left_panel,) = call(sort_d_left_kernel, "sort_d_left", [panel], d_pieces)
    (d_gate_pre,) = call(
        gate_back_kernel,
        "gate_back",
        [shape((rows, channels, width), BF16)],
        [products, gate_slope, out_gain, out_bias, w_out],
        fetched=range(2, 5),
        flops=2 * cells * channels * hidden,
    )
    slopes, normed_in, inv_in, gain_col, weights = call(
        slopes_kernel,
        "slopes",
        [
            shape((rows, 4 * hidden, width), BF16),
            shape((rows, channels, width), BF16),
            shape((rows, width), F32),
            shape((channels, channels), F32),
            shape((channels, 4 * hidden + channels), BF16),
        ],
        [pair, mask, gain, bias, w_proj, w_gate, d_gate_pre],
        fetched=range(6),
        unread=(6,),
        flops=2 * cells * channels * 4 * hidden,
    )
    (grad,) = call(
        finish_kernel,
        "finish",
        [shape(pair.shape, BF16)],
        [
            d_right_panel,
            d_left_panel,
            slopes,
            d_gate_pre,
            normed_in,
            inv_in,
            gain_col,
            weights,
        ],
        flops=2 * cells * channels * 4 * hidden,
    )
    return grad


def normalize(values, reduce_axis):
    mean_value = jnp.mean(values, axis=reduce_axis, keepdims=True)
    centered = values - mean_value
    variance = jnp.mean(centered * centered, axis=reduce_axis, keepdims=True)
    inv_std = lax.rsqrt(variance + 1e-05)
    return (centered * inv_std, inv_std)


def norm_backward(upstream, normed, inv_std, reduce_axis):
    mean_grad = jnp.mean(upstream, axis=reduce_axis, keepdims=True)
    mean_cross = jnp.mean(upstream * normed, axis=reduce_axis, keepdims=True)
    return inv_std * (upstream - mean_grad - normed * mean_cross)


def shards(
    pair,
    cotangent,
    residue_mask,
    ln_in_gain,
    ln_in_bias,
    w_proj,
    w_gate,
    ln_out_gain,
    ln_out_bias,
    w_out,
):
    local_rows = pair.shape[0]
    local_cols = pair.shape[1]
    hidden = w_out.shape[0]
    chan_index = lax.axis_index("chan")
    row_start = lax.axis_index("row") * local_rows
    col_start = chan_index * local_cols
    mask_float = residue_mask.astype(jnp.float32)
    row_mask = lax.dynamic_slice_in_dim(mask_float, row_start, local_rows)
    col_mask = lax.dynamic_slice_in_dim(mask_float, col_start, local_cols)
    cell_mask = (row_mask[:, None] * col_mask[None, :])[None]
    normed, inv_std = normalize(pair.astype(jnp.float32), -1)
    normed_pair = (normed * ln_in_gain + ln_in_bias).astype(jnp.bfloat16)
    projected = jnp.einsum("rmc,ch->hrm", normed_pair, w_proj, preferred_element_type=jnp.float32)
    left_panel = (
        cell_mask * jax.nn.sigmoid(projected[:hidden]) * projected[hidden : 2 * hidden]
    ).astype(jnp.bfloat16)
    right_panel = (
        cell_mask * jax.nn.sigmoid(projected[2 * hidden : 3 * hidden]) * projected[3 * hidden :]
    ).astype(jnp.bfloat16)
    panels = lax.all_to_all(
        jnp.stack([left_panel, right_panel]), "row", split_axis=1, concat_axis=2, tiled=True
    )
    left_all = panels[0]
    right_all = panels[1]
    right_rows = lax.all_to_all(right_all, "chan", split_axis=1, concat_axis=2, tiled=True)
    partner = right_rows
    tri_part = jnp.einsum(
        "gik,gjk->gij",
        lax.all_gather(left_all, "chan", axis=2, tiled=True),
        partner,
        preferred_element_type=jnp.float32,
    ).astype(jnp.bfloat16)
    tri_cells = lax.all_to_all(tri_part, "row", split_axis=1, concat_axis=0, tiled=True)
    tri_hat, inv_tri = normalize(tri_cells.astype(jnp.float32), 0)
    scaled = (tri_hat * ln_out_gain[:, None, None] + ln_out_bias[:, None, None]).astype(
        jnp.bfloat16
    )
    proj_out = jnp.einsum("hrm,hc->rmc", scaled, w_out, preferred_element_type=jnp.float32)
    gate_value = jax.nn.sigmoid(
        jnp.einsum("rmc,cd->rmd", normed_pair, w_gate, preferred_element_type=jnp.float32)
    )
    cot_float = cotangent.astype(jnp.float32)
    d_gate_pre = (cot_float * proj_out * gate_value * (1.0 - gate_value)).astype(jnp.bfloat16)
    d_scaled = (cot_float * gate_value).astype(jnp.bfloat16)
    d_hat = jnp.einsum("rmc,hc->hrm", d_scaled, w_out, preferred_element_type=jnp.float32)
    d_hat = d_hat * ln_out_gain[:, None, None]
    d_tri = norm_backward(d_hat, tri_hat, inv_tri, 0).astype(jnp.bfloat16)
    d_tri_all = lax.all_to_all(d_tri, "row", split_axis=0, concat_axis=1, tiled=True)
    panel_piece = lax.all_gather(d_tri_all, "chan", axis=2, tiled=True)
    partner = right_all
    d_left = jnp.einsum("gij,gjk->gik", panel_piece, partner, preferred_element_type=jnp.float32)
    contribution = jnp.einsum(
        "gij,gik->gjk", panel_piece, left_all, preferred_element_type=jnp.float32
    )
    d_right = contribution
    d_left, d_right = (d_left, d_right)
    d_stack = jnp.stack([d_left, d_right]).astype(jnp.bfloat16)
    d_panels = lax.all_to_all(d_stack, "row", split_axis=2, concat_axis=1, tiled=True)

    def gating(d_value, gate_proj, value_proj):
        sigmoid_val = jax.nn.sigmoid(gate_proj)
        masked_grad = d_value.astype(jnp.float32) * cell_mask
        return (
            masked_grad * value_proj * sigmoid_val * (1.0 - sigmoid_val),
            masked_grad * sigmoid_val,
        )

    gate_left, value_left = gating(d_panels[0], projected[:hidden], projected[hidden : 2 * hidden])
    gate_right, value_right = gating(
        d_panels[1], projected[2 * hidden : 3 * hidden], projected[3 * hidden :]
    )
    d_proj = jnp.concatenate([gate_left, value_left, gate_right, value_right], axis=0).astype(
        jnp.bfloat16
    )
    d_normed = jnp.einsum("hrm,ch->rmc", d_proj, w_proj, preferred_element_type=jnp.float32)
    d_normed = d_normed + jnp.einsum(
        "rmd,cd->rmc", d_gate_pre, w_gate, preferred_element_type=jnp.float32
    )
    d_input = d_normed * ln_in_gain
    return norm_backward(d_input, normed, inv_std, -1).astype(jnp.bfloat16)


def solution(mesh):
    fits = mesh.shape["chan"] == 1 and mesh.shape["row"] in (8, 16)
    return jax.shard_map(
        kernel_shards if fits else shards,
        mesh=mesh,
        in_specs=(
            P(("grp", "row"), "chan", None),
            P(("grp", "row"), "chan", None),
            P("grp"),
            P(),
            P(),
            P(),
            P(),
            P(),
            P(),
            P(),
        ),
        out_specs=P(("grp", "row"), "chan", None),
        check_vma=False,
    )
```

```python
import functools

import jax
import jax.numpy as jnp
from jax import lax
from jax.experimental import pallas as pl
from jax.experimental.pallas import tpu as pltpu
from jax.sharding import PartitionSpec as P

F32 = jnp.float32
BF16 = jnp.bfloat16
VMEM_LIMIT = 16 * 1024 * 1024


def dot(lhs, rhs, lhs_dim, rhs_dim):
    return lax.dot_general(
        lhs, rhs, (((lhs_dim,), (rhs_dim,)), ((), ())), preferred_element_type=F32
    )


def transposed(matrix):
    return jnp.transpose(matrix.astype(F32)).astype(BF16)


def sigmoid(values):
    return 1.0 / (1.0 + jnp.exp(-values))


def column(row):
    size = row.shape[1]
    return jnp.transpose(jnp.broadcast_to(row, (size, size)))


def norm_rows(values):
    centered = values - jnp.mean(values, axis=0, keepdims=True)
    variance = jnp.mean(centered * centered, axis=0, keepdims=True)
    inv_std = lax.rsqrt(variance + 1e-05)
    return centered * inv_std, inv_std


def call(
    kernel, name, outs, args, fetched=(), unread=(), scratch=(), flops=0, limit=VMEM_LIMIT
):
    moved = sum(a.size * a.dtype.itemsize for a in args) + sum(
        o.size * jnp.dtype(o.dtype).itemsize for o in outs
    )
    n_args, n_outs, n_fetched = len(args), len(outs), len(fetched)

    def body(*refs):
        ins = list(refs[:n_args])
        rest = refs[n_args + n_outs :]
        copies = []
        for n, place in enumerate(fetched):
            copies.append(pltpu.make_async_copy(ins[place], rest[n], rest[n_fetched].at[n]))
            ins[place] = rest[n]
        for copy in copies:
            copy.start()
        for copy in copies:
            copy.wait()
        kernel(*ins, *refs[n_args : n_args + n_outs], *rest[n_fetched + (n_fetched > 0) :])

    buffers = [pltpu.VMEM(args[place].shape, args[place].dtype) for place in fetched]
    if fetched:
        buffers.append(pltpu.SemaphoreType.DMA((n_fetched,)))
    return pl.pallas_call(
        body,
        name=name,
        out_shape=outs,
        in_specs=[
            pl.BlockSpec(
                memory_space=pltpu.HBM if n in fetched else pl.ANY if n in unread else pltpu.VMEM
            )
            for n in range(n_args)
        ],
        out_specs=[pl.BlockSpec(memory_space=pltpu.VMEM) for _ in outs],
        scratch_shapes=buffers + list(scratch),
        compiler_params=pltpu.CompilerParams(vmem_limit_bytes=limit),
        cost_estimate=pl.CostEstimate(flops=flops, bytes_accessed=moved, transcendentals=0),
    )(*args)


def cell_masks(mask, rows):
    columns = mask[...].astype(F32)
    shape = (rows, columns.shape[1])
    first = lax.axis_index("row") * rows
    own = lax.broadcasted_iota(jnp.int32, shape, 1) == (
        lax.broadcasted_iota(jnp.int32, shape, 0) + first
    )
    row_mask = jnp.sum(jnp.where(own, columns, 0.0), axis=1, keepdims=True)
    cells = row_mask * columns
    return [cells[row : row + 1] for row in range(rows)]


def wide_order(devices, count, back):
    order = []
    for place in range(count):
        if back:
            order += [place ^ (count // 2), count + place]
        else:
            order += [count + (place ^ 2), place ^ (count // 2)]
    return order


def distance(step, count):
    far = sorted(range(3, count), key=lambda apart: apart < count // 2)
    return [*range(min(3, count)), *far][step]


def partner(step, count):
    return lax.rem(lax.axis_index("row"), count) ^ distance(step, count)


def gated_rows(pair, mask, gain, bias, w_proj, side):
    rows = pair.shape[0]
    hidden = w_proj.shape[1] // 4
    w_flip = transposed(w_proj[:, 2 * side * hidden : 2 * (side + 1) * hidden])
    gain_col, bias_col = column(gain[...]), column(bias[...])
    masks = cell_masks(mask, rows)
    for row in range(rows):
        normed, _ = norm_rows(jnp.transpose(pair[row].astype(F32)))
        zln = (normed * gain_col + bias_col).astype(BF16)
        proj = dot(w_flip, zln, 1, 0)
        yield row, masks[row] * sigmoid(proj[:hidden]) * proj[hidden:]


def project_right_kernel(pair, mask, gain, bias, w_proj, right_panel):
    rows = pair.shape[0]
    devices, depth, width = right_panel.shape
    block = depth // rows
    count = w_proj.shape[1] // 4 // block
    for row, right in gated_rows(pair, mask, gain, bias, w_proj, 1):
        right = right.reshape(count, block, width).astype(BF16)
        for rank in range(devices):
            place = wide_order(devices, count, False)[rank] % count
            right_panel[rank, row * block : (row + 1) * block, :] = right[place]


def project_left_kernel(pair, mask, gain, bias, w_proj, after, *refs):
    del after
    *pieces, left_panel = refs
    rows = pair.shape[0]
    count, depth, width = left_panel.shape
    block = depth // rows
    for row, left in gated_rows(pair, mask, gain, bias, w_proj, 0):
        left = left.reshape(count, block, width).astype(BF16)
        left_panel[:, row * block : (row + 1) * block, :] = left
    for step, piece in enumerate(pieces):
        piece[...] = left_panel[partner(step, count)]


def prepare_kernel(
    pair, cotangent, gain, bias, w_gate, out_gain, w_out, d_hat_centered, gate_slope
):
    gate_flip = transposed(w_gate[...])
    gain_col, bias_col = column(gain[...]), column(bias[...])
    out_gain_col = column(out_gain[...])
    for row in range(pair.shape[0]):
        normed, _ = norm_rows(jnp.transpose(pair[row].astype(F32)))
        zln = (normed * gain_col + bias_col).astype(BF16)
        gate = sigmoid(dot(gate_flip, zln, 1, 0))
        cot = jnp.transpose(cotangent[row].astype(F32))
        d_scaled = (cot * gate).astype(BF16)
        d_hat = dot(w_out[...], d_scaled, 1, 0) * out_gain_col
        d_hat_centered[row] = d_hat - jnp.mean(d_hat, axis=0, keepdims=True)
        gate_slope[row] = cot * gate * (1.0 - gate)


def spread(panel, wide):
    wide[...] = panel[...].astype(F32).reshape(wide.shape)


def wide_places(panel, count, back):
    devices, depth, _ = panel.shape
    for rank, device in enumerate(wide_order(devices, count, back)):
        yield rank, slice(device * depth, (device + 1) * depth)


def sort_left_kernel(*refs):
    *pieces, left_all, left_wide = refs
    block, left_rows, _ = left_all.shape
    depth = pieces[0].shape[0]
    for step, piece in enumerate(pieces):
        start = pl.multiple_of(partner(step, len(pieces)) * depth, depth)
        left_wide[pl.ds(start, depth), :] = piece[...].astype(F32)
    for h in range(block):
        left_all[h] = left_wide[pl.ds(h, left_rows, stride=block), :].astype(BF16)


def tri_kernel(right_panel, left_all, after, products, right_all, left_wide, right_wide):
    del after
    block, left_rows, _ = left_all.shape
    right_rows = right_all.shape[1]
    for rank, place in wide_places(right_panel, products.shape[0], False):
        right_wide[place, :] = right_panel[rank].astype(F32)
    for h in range(block):
        right = right_wide[pl.ds(h, right_rows, stride=block), :].astype(BF16)
        right_all[h] = right
        left_wide[pl.ds(h, left_rows, stride=block), :] = dot(left_all[h], right, 1, 1)
    products[...] = left_wide[...].astype(BF16).reshape(products.shape)


def cell_row(ref, row, rows):
    count, depth, width = ref.shape
    block = depth // rows
    return ref[:, row * block : (row + 1) * block, :].astype(F32).reshape(count * block, width)


def middle_kernel(products, d_hat_centered, d_products):
    rows = d_hat_centered.shape[0]
    count, depth, width = products.shape
    block = depth // rows
    for row in range(rows):
        tri_hat, inv_std = norm_rows(cell_row(products, row, rows))
        d_hat = d_hat_centered[row]
        cross = jnp.mean(d_hat * tri_hat, axis=0, keepdims=True)
        d_tri = inv_std * (d_hat - tri_hat * cross)
        d_products[:, row * block : (row + 1) * block, :] = d_tri.reshape(
            count, block, width
        ).astype(BF16)


def d_right_kernel(d_products, left_all, d_right_panel, d_tri_all, left_wide, right_wide):
    block, left_rows, _ = left_all.shape
    right_rows = right_wide.shape[0] // block
    spread(d_products, left_wide)
    for h in range(block):
        d_tri = left_wide[pl.ds(h, left_rows, stride=block), :].astype(BF16)
        d_tri_all[h] = d_tri
        right_wide[pl.ds(h, right_rows, stride=block), :] = dot(d_tri, left_all[h], 0, 0)
    for rank, place in wide_places(d_right_panel, d_products.shape[0], True):
        d_right_panel[rank] = right_wide[place, :].astype(BF16)


def d_left_kernel(d_tri_all, right_all, *refs):
    *pieces, left_wide = refs
    block, left_rows, _ = d_tri_all.shape
    for h in range(block):
        left_wide[pl.ds(h, left_rows, stride=block), :] = dot(d_tri_all[h], right_all[h], 1, 0)
    depth = pieces[0].shape[0]
    for step, piece in enumerate(pieces):
        start = pl.multiple_of(partner(step, len(pieces)) * depth, depth)
        piece[...] = left_wide[pl.ds(start, depth), :].astype(BF16)


def gate_back_kernel(products, gate_slope, out_gain, out_bias, w_out, d_gate_pre):
    rows = gate_slope.shape[0]
    out_flip = transposed(w_out[...])
    out_gain_col, out_bias_col = column(out_gain[...]), column(out_bias[...])
    for row in range(rows):
        tri_hat, _ = norm_rows(cell_row(products, row, rows))
        scaled = (tri_hat * out_gain_col + out_bias_col).astype(BF16)
        d_gate_pre[row] = (dot(out_flip, scaled, 1, 0) * gate_slope[row]).astype(BF16)


def slopes_kernel(
    pair, mask, gain, bias, w_proj, w_gate, after, slopes, normed_in, inv_in, in_gain, weights
):
    del after
    rows = pair.shape[0]
    hidden = w_proj.shape[1] // 4
    w_flip = transposed(w_proj[...])
    gain_col, bias_col = column(gain[...]), column(bias[...])
    in_gain[...] = gain_col
    weights[...] = jnp.concatenate([w_proj[...], w_gate[...]], axis=1)
    masks = cell_masks(mask, rows)
    for row in range(rows):
        normed, inv_std = norm_rows(jnp.transpose(pair[row].astype(F32)))
        normed_in[row] = normed.astype(normed_in.dtype)
        inv_in[row : row + 1] = inv_std
        zln = (normed * gain_col + bias_col).astype(BF16)
        proj = dot(w_flip, zln, 1, 0)
        for side in range(2):
            base = 2 * side * hidden
            sig = sigmoid(proj[base : base + hidden])
            masked = masks[row] * sig
            value = masked * (1.0 - sig) * proj[base + hidden : base + 2 * hidden]
            slopes[row, base : base + hidden, :] = value.astype(slopes.dtype)
            slopes[row, base + hidden : base + 2 * hidden, :] = masked.astype(slopes.dtype)


def sort_d_left_kernel(*refs):
    *pieces, d_left_panel = refs
    for step, piece in enumerate(pieces):
        d_left_panel[partner(step, len(pieces))] = piece[...]


def both_halves(blocks, count):
    order = wide_order(2 * count, count, True)
    return jnp.stack(
        [blocks[order.index(place)] + blocks[order.index(count + place)] for place in range(count)]
    )


def finish_kernel(
    d_right_panel, d_left_panel, slopes, d_gate_pre, normed_in, inv_in, gain_col, weights, grad
):
    rows = grad.shape[0]
    count, depth, width = d_left_panel.shape
    hidden = count * depth // rows
    for row in range(rows):
        d_right = cell_row(d_right_panel, row, rows)
        d_right = both_halves(d_right.reshape(2 * count, depth // rows, width), count)
        parts = []
        for side, d_value in enumerate((cell_row(d_left_panel, row, rows), d_right.reshape(hidden, width))):
            for base in (2 * side * hidden, (2 * side + 1) * hidden):
                slope = slopes[row, base : base + hidden, :].astype(F32)
                parts.append((d_value * slope).astype(BF16))
        parts.append(d_gate_pre[row])
        d_in = dot(weights[...], jnp.concatenate(parts, axis=0), 1, 0) * gain_col[...]
        normed = normed_in[row].astype(F32)
        mean_grad = jnp.mean(d_in, axis=0, keepdims=True)
        mean_cross = jnp.mean(d_in * normed, axis=0, keepdims=True)
        result = inv_in[row : row + 1] * (d_in - mean_grad - normed * mean_cross)
        grad[row] = jnp.transpose(result).astype(BF16)


def swap(values, count, back):
    groups = [wide_order(lax.axis_size("row"), count, back)]
    return lax.all_to_all(
        values, "row", split_axis=0, concat_axis=0, tiled=True, axis_index_groups=groups
    )


def swap_half(values, count):
    devices = range(lax.axis_size("row"))
    groups = [[d for d in devices if d // count == half] for half in range(len(devices) // count)]
    return lax.all_to_all(
        values, "row", split_axis=0, concat_axis=0, tiled=True, axis_index_groups=groups
    )


def swap_pieces(pieces):
    devices = range(lax.axis_size("row"))
    count = len(pieces)
    return [pieces[0]] + [
        lax.ppermute(pieces[step], "row", [(d, d ^ distance(step, count)) for d in devices])
        for step in range(1, count)
    ]


def kernel_shards(
    pair,
    cotangent,
    residue_mask,
    ln_in_gain,
    ln_in_bias,
    w_proj,
    w_gate,
    ln_out_gain,
    ln_out_bias,
    w_out,
):
    rows, width, channels = pair.shape
    hidden = w_out.shape[0]
    halves = 2
    devices = lax.axis_size("row")
    count = devices // halves
    block = hidden // count
    left_rows, right_rows = rows * count, rows * devices
    shape = jax.ShapeDtypeStruct
    panel = shape((count, rows * block, width), BF16)
    wide_panel = shape((devices, rows * block, width), BF16)
    mask = residue_mask.reshape(1, width)
    gain, bias = ln_in_gain.reshape(1, channels), ln_in_bias.reshape(1, channels)
    out_gain, out_bias = ln_out_gain.reshape(1, hidden), ln_out_bias.reshape(1, hidden)
    cells = rows * width
    piece = shape((rows * block, width), BF16)
    left_panel = pltpu.VMEM(panel.shape, BF16)
    left_wide = pltpu.VMEM((left_rows * block, width), F32)
    right_wide = pltpu.VMEM((right_rows * block, width), F32)
    (own_right,) = call(
        project_right_kernel,
        "project_right",
        [wide_panel],
        [pair, mask, gain, bias, w_proj],
        fetched=range(5),
        flops=2 * cells * channels * 2 * hidden,
        limit=64 * 1024 * 1024 - 640 * 1024,
    )
    right_panel = swap(own_right, count, False)
    pieces = call(
        project_left_kernel,
        "project_left",
        [piece] * count,
        [pair, mask, gain, bias, w_proj, own_right],
        fetched=range(5),
        unread=(5,),
        scratch=[left_panel],
        flops=2 * cells * channels * 2 * hidden,
    )
    pieces = swap_pieces(pieces)
    (left_all,) = call(
        sort_left_kernel,
        "sort_left",
        [shape((block, left_rows, width), BF16)],
        pieces,
        scratch=[left_wide],
    )
    d_hat_centered, gate_slope = call(
        prepare_kernel,
        "prepare",
        [shape((rows, hidden, width), F32), shape((rows, channels, width), F32)],
        [pair, cotangent, gain, bias, w_gate, out_gain, w_out],
        fetched=range(7),
        flops=2 * cells * channels * 2 * hidden,
    )
    products, right_all = call(
        tri_kernel,
        "tri",
        [panel, shape((block, right_rows, width), BF16)],
        [right_panel, left_all, d_hat_centered],
        unread=(2,),
        scratch=[left_wide, right_wide],
        flops=2 * block * left_rows * width * right_rows,
    )
    products = swap_half(products, count)
    (d_products,) = call(
        middle_kernel,
        "middle",
        [panel],
        [products, d_hat_centered],
        flops=20 * cells * hidden,
    )
    d_products = swap_half(d_products, count)
    d_right_panel, d_tri_all = call(
        d_right_kernel,
        "d_right",
        [wide_panel, shape((block, left_rows, width), BF16)],
        [d_products, left_all],
        scratch=[left_wide, right_wide],
        flops=2 * block * left_rows * width * right_rows,
    )
    d_right_panel = swap(d_right_panel, count, True)
    d_pieces = call(
        d_left_kernel,
        "d_left",
        [piece] * count,
        [d_tri_all, right_all],
        scratch=[left_wide],
        flops=2 * block * left_rows * width * right_rows,
    )
    d_pieces = swap_pieces(d_pieces)
    (d_left_panel,) = call(sort_d_left_kernel, "sort_d_left", [panel], d_pieces)
    (d_gate_pre,) = call(
        gate_back_kernel,
        "gate_back",
        [shape((rows, channels, width), BF16)],
        [products, gate_slope, out_gain, out_bias, w_out],
        fetched=range(2, 5),
        flops=2 * cells * channels * hidden,
    )
    slopes, normed_in, inv_in, gain_col, weights = call(
        slopes_kernel,
        "slopes",
        [
            shape((rows, 4 * hidden, width), BF16),
            shape((rows, channels, width), BF16),
            shape((rows, width), F32),
            shape((channels, channels), F32),
            shape((channels, 4 * hidden + channels), BF16),
        ],
        [pair, mask, gain, bias, w_proj, w_gate, d_gate_pre],
        fetched=range(6),
        unread=(6,),
        flops=2 * cells * channels * 4 * hidden,
    )
    (grad,) = call(
        finish_kernel,
        "finish",
        [shape(pair.shape, BF16)],
        [
            d_right_panel,
            d_left_panel,
            slopes,
            d_gate_pre,
            normed_in,
            inv_in,
            gain_col,
            weights,
        ],
        flops=2 * cells * channels * 4 * hidden,
    )
    return grad


def normalize(values, reduce_axis):
    mean_value = jnp.mean(values, axis=reduce_axis, keepdims=True)
    centered = values - mean_value
    variance = jnp.mean(centered * centered, axis=reduce_axis, keepdims=True)
    inv_std = lax.rsqrt(variance + 1e-05)
    return (centered * inv_std, inv_std)


def norm_backward(upstream, normed, inv_std, reduce_axis):
    mean_grad = jnp.mean(upstream, axis=reduce_axis, keepdims=True)
    mean_cross = jnp.mean(upstream * normed, axis=reduce_axis, keepdims=True)
    return inv_std * (upstream - mean_grad - normed * mean_cross)


def shards(
    pair,
    cotangent,
    residue_mask,
    ln_in_gain,
    ln_in_bias,
    w_proj,
    w_gate,
    ln_out_gain,
    ln_out_bias,
    w_out,
):
    local_rows = pair.shape[0]
    local_cols = pair.shape[1]
    hidden = w_out.shape[0]
    chan_index = lax.axis_index("chan")
    row_start = lax.axis_index("row") * local_rows
    col_start = chan_index * local_cols
    mask_float = residue_mask.astype(jnp.float32)
    row_mask = lax.dynamic_slice_in_dim(mask_float, row_start, local_rows)
    col_mask = lax.dynamic_slice_in_dim(mask_float, col_start, local_cols)
    cell_mask = (row_mask[:, None] * col_mask[None, :])[None]
    normed, inv_std = normalize(pair.astype(jnp.float32), -1)
    normed_pair = (normed * ln_in_gain + ln_in_bias).astype(jnp.bfloat16)
    projected = jnp.einsum("rmc,ch->hrm", normed_pair, w_proj, preferred_element_type=jnp.float32)
    left_panel = (
        cell_mask * jax.nn.sigmoid(projected[:hidden]) * projected[hidden : 2 * hidden]
    ).astype(jnp.bfloat16)
    right_panel = (
        cell_mask * jax.nn.sigmoid(projected[2 * hidden : 3 * hidden]) * projected[3 * hidden :]
    ).astype(jnp.bfloat16)
    panels = lax.all_to_all(
        jnp.stack([left_panel, right_panel]), "row", split_axis=1, concat_axis=2, tiled=True
    )
    left_all = panels[0]
    right_all = panels[1]
    right_rows = lax.all_to_all(right_all, "chan", split_axis=1, concat_axis=2, tiled=True)
    partner = right_rows
    tri_part = jnp.einsum(
        "gik,gjk->gij",
        lax.all_gather(left_all, "chan", axis=2, tiled=True),
        partner,
        preferred_element_type=jnp.float32,
    ).astype(jnp.bfloat16)
    tri_cells = lax.all_to_all(tri_part, "row", split_axis=1, concat_axis=0, tiled=True)
    tri_hat, inv_tri = normalize(tri_cells.astype(jnp.float32), 0)
    scaled = (tri_hat * ln_out_gain[:, None, None] + ln_out_bias[:, None, None]).astype(
        jnp.bfloat16
    )
    proj_out = jnp.einsum("hrm,hc->rmc", scaled, w_out, preferred_element_type=jnp.float32)
    gate_value = jax.nn.sigmoid(
        jnp.einsum("rmc,cd->rmd", normed_pair, w_gate, preferred_element_type=jnp.float32)
    )
    cot_float = cotangent.astype(jnp.float32)
    d_gate_pre = (cot_float * proj_out * gate_value * (1.0 - gate_value)).astype(jnp.bfloat16)
    d_scaled = (cot_float * gate_value).astype(jnp.bfloat16)
    d_hat = jnp.einsum("rmc,hc->hrm", d_scaled, w_out, preferred_element_type=jnp.float32)
    d_hat = d_hat * ln_out_gain[:, None, None]
    d_tri = norm_backward(d_hat, tri_hat, inv_tri, 0).astype(jnp.bfloat16)
    d_tri_all = lax.all_to_all(d_tri, "row", split_axis=0, concat_axis=1, tiled=True)
    panel_piece = lax.all_gather(d_tri_all, "chan", axis=2, tiled=True)
    partner = right_all
    d_left = jnp.einsum("gij,gjk->gik", panel_piece, partner, preferred_element_type=jnp.float32)
    contribution = jnp.einsum(
        "gij,gik->gjk", panel_piece, left_all, preferred_element_type=jnp.float32
    )
    d_right = contribution
    d_left, d_right = (d_left, d_right)
    d_stack = jnp.stack([d_left, d_right]).astype(jnp.bfloat16)
    d_panels = lax.all_to_all(d_stack, "row", split_axis=2, concat_axis=1, tiled=True)

    def gating(d_value, gate_proj, value_proj):
        sigmoid_val = jax.nn.sigmoid(gate_proj)
        masked_grad = d_value.astype(jnp.float32) * cell_mask
        return (
            masked_grad * value_proj * sigmoid_val * (1.0 - sigmoid_val),
            masked_grad * sigmoid_val,
        )

    gate_left, value_left = gating(d_panels[0], projected[:hidden], projected[hidden : 2 * hidden])
    gate_right, value_right = gating(
        d_panels[1], projected[2 * hidden : 3 * hidden], projected[3 * hidden :]
    )
    d_proj = jnp.concatenate([gate_left, value_left, gate_right, value_right], axis=0).astype(
        jnp.bfloat16
    )
    d_normed = jnp.einsum("hrm,ch->rmc", d_proj, w_proj, preferred_element_type=jnp.float32)
    d_normed = d_normed + jnp.einsum(
        "rmd,cd->rmc", d_gate_pre, w_gate, preferred_element_type=jnp.float32
    )
    d_input = d_normed * ln_in_gain
    return norm_backward(d_input, normed, inv_std, -1).astype(jnp.bfloat16)


def solution(mesh):
    fits = mesh.shape["chan"] == 1 and mesh.shape["row"] in (8, 16)
    return jax.shard_map(
        kernel_shards if fits else shards,
        mesh=mesh,
        in_specs=(
            P(("grp", "row"), "chan", None),
            P(("grp", "row"), "chan", None),
            P("grp"),
            P(),
            P(),
            P(),
            P(),
            P(),
            P(),
            P(),
        ),
        out_specs=P(("grp", "row"), "chan", None),
        check_vma=False,
    )
```

```python
import functools

import jax
import jax.numpy as jnp
from jax import lax
from jax.experimental import pallas as pl
from jax.experimental.pallas import tpu as pltpu
from jax.sharding import PartitionSpec as P

F32 = jnp.float32
BF16 = jnp.bfloat16
VMEM_LIMIT = 16 * 1024 * 1024


def dot(lhs, rhs, lhs_dim, rhs_dim):
    return lax.dot_general(
        lhs, rhs, (((lhs_dim,), (rhs_dim,)), ((), ())), preferred_element_type=F32
    )


def transposed(matrix):
    return jnp.transpose(matrix.astype(F32)).astype(BF16)


def sigmoid(values):
    return 1.0 / (1.0 + jnp.exp(-values))


def column(row):
    size = row.shape[1]
    return jnp.transpose(jnp.broadcast_to(row, (size, size)))


def norm_rows(values):
    centered = values - jnp.mean(values, axis=0, keepdims=True)
    variance = jnp.mean(centered * centered, axis=0, keepdims=True)
    inv_std = lax.rsqrt(variance + 1e-05)
    return centered * inv_std, inv_std


def call(
    kernel, name, outs, args, fetched=(), unread=(), scratch=(), flops=0, limit=VMEM_LIMIT
):
    moved = sum(a.size * a.dtype.itemsize for a in args) + sum(
        o.size * jnp.dtype(o.dtype).itemsize for o in outs
    )
    n_args, n_outs, n_fetched = len(args), len(outs), len(fetched)

    def body(*refs):
        ins = list(refs[:n_args])
        rest = refs[n_args + n_outs :]
        copies = []
        for n, place in enumerate(fetched):
            copies.append(pltpu.make_async_copy(ins[place], rest[n], rest[n_fetched].at[n]))
            ins[place] = rest[n]
        for copy in copies:
            copy.start()
        for copy in copies:
            copy.wait()
        kernel(*ins, *refs[n_args : n_args + n_outs], *rest[n_fetched + (n_fetched > 0) :])

    buffers = [pltpu.VMEM(args[place].shape, args[place].dtype) for place in fetched]
    if fetched:
        buffers.append(pltpu.SemaphoreType.DMA((n_fetched,)))
    return pl.pallas_call(
        body,
        name=name,
        out_shape=outs,
        in_specs=[
            pl.BlockSpec(
                memory_space=pltpu.HBM if n in fetched else pl.ANY if n in unread else pltpu.VMEM
            )
            for n in range(n_args)
        ],
        out_specs=[pl.BlockSpec(memory_space=pltpu.VMEM) for _ in outs],
        scratch_shapes=buffers + list(scratch),
        compiler_params=pltpu.CompilerParams(vmem_limit_bytes=limit),
        cost_estimate=pl.CostEstimate(flops=flops, bytes_accessed=moved, transcendentals=0),
    )(*args)


def cell_masks(mask, rows):
    columns = mask[...].astype(F32)
    shape = (rows, columns.shape[1])
    first = lax.axis_index("row") * rows
    own = lax.broadcasted_iota(jnp.int32, shape, 1) == (
        lax.broadcasted_iota(jnp.int32, shape, 0) + first
    )
    row_mask = jnp.sum(jnp.where(own, columns, 0.0), axis=1, keepdims=True)
    cells = row_mask * columns
    return [cells[row : row + 1] for row in range(rows)]


def wide_order(devices, count, back):
    order = []
    for place in range(count):
        if back:
            order += [place ^ (count // 2), count + place]
        else:
            order += [count + (place ^ 2), place ^ (count // 2)]
    return order


def distance(step, count):
    far = sorted(range(3, count), key=lambda apart: -(apart // 2))
    return [*range(min(3, count)), *far][step]


def partner(step, count):
    return lax.rem(lax.axis_index("row"), count) ^ distance(step, count)


def gated_rows(pair, mask, gain, bias, w_proj, side):
    rows = pair.shape[0]
    hidden = w_proj.shape[1] // 4
    w_flip = transposed(w_proj[:, 2 * side * hidden : 2 * (side + 1) * hidden])
    gain_col, bias_col = column(gain[...]), column(bias[...])
    masks = cell_masks(mask, rows)
    for row in range(rows):
        normed, _ = norm_rows(jnp.transpose(pair[row].astype(F32)))
        zln = (normed * gain_col + bias_col).astype(BF16)
        proj = dot(w_flip, zln, 1, 0)
        yield row, masks[row] * sigmoid(proj[:hidden]) * proj[hidden:]


def project_right_kernel(pair, mask, gain, bias, w_proj, right_panel):
    rows = pair.shape[0]
    devices, depth, width = right_panel.shape
    block = depth // rows
    count = w_proj.shape[1] // 4 // block
    for row, right in gated_rows(pair, mask, gain, bias, w_proj, 1):
        right = right.reshape(count, block, width).astype(BF16)
        for rank in range(devices):
            place = wide_order(devices, count, False)[rank] % count
            right_panel[rank, row * block : (row + 1) * block, :] = right[place]


def project_left_kernel(pair, mask, gain, bias, w_proj, after, *refs):
    del after
    *pieces, left_panel = refs
    rows = pair.shape[0]
    count, depth, width = left_panel.shape
    block = depth // rows
    for row, left in gated_rows(pair, mask, gain, bias, w_proj, 0):
        left = left.reshape(count, block, width).astype(BF16)
        left_panel[:, row * block : (row + 1) * block, :] = left
    for step, piece in enumerate(pieces):
        piece[...] = left_panel[partner(step, count)]


def prepare_kernel(
    pair, cotangent, gain, bias, w_gate, out_gain, w_out, d_hat_centered, gate_slope
):
    gate_flip = transposed(w_gate[...])
    gain_col, bias_col = column(gain[...]), column(bias[...])
    out_gain_col = column(out_gain[...])
    for row in range(pair.shape[0]):
        normed, _ = norm_rows(jnp.transpose(pair[row].astype(F32)))
        zln = (normed * gain_col + bias_col).astype(BF16)
        gate = sigmoid(dot(gate_flip, zln, 1, 0))
        cot = jnp.transpose(cotangent[row].astype(F32))
        d_scaled = (cot * gate).astype(BF16)
        d_hat = dot(w_out[...], d_scaled, 1, 0) * out_gain_col
        d_hat_centered[row] = d_hat - jnp.mean(d_hat, axis=0, keepdims=True)
        gate_slope[row] = cot * gate * (1.0 - gate)


def spread(panel, wide):
    wide[...] = panel[...].astype(F32).reshape(wide.shape)


def wide_places(panel, count, back):
    devices, depth, _ = panel.shape
    for rank, device in enumerate(wide_order(devices, count, back)):
        yield rank, slice(device * depth, (device + 1) * depth)


def sort_left_kernel(*refs):
    *pieces, left_all, left_pairs, left_wide = refs
    block, left_rows, _ = left_all.shape
    depth = pieces[0].shape[0]
    for step, piece in enumerate(pieces):
        start = pl.multiple_of(partner(step, len(pieces)) * depth, depth)
        left_wide[pl.ds(start, depth), :] = piece[...].astype(F32)
    for h in range(block):
        left_all[h] = left_wide[pl.ds(h, left_rows, stride=block), :].astype(BF16)
    empty = jnp.zeros(left_all.shape[1:], BF16)
    for n in range(block // 2):
        left_pairs[n, :left_rows, :] = jnp.concatenate([left_all[2 * n], empty], axis=1)
        left_pairs[n, left_rows:, :] = jnp.concatenate([empty, left_all[2 * n + 1]], axis=1)


def tri_kernel(right_panel, left_all, after, products, right_all, left_wide, right_wide):
    del after
    block, left_rows, _ = left_all.shape
    right_rows = right_all.shape[1]
    for rank, place in wide_places(right_panel, products.shape[0], False):
        right_wide[place, :] = right_panel[rank].astype(F32)
    for h in range(block):
        right = right_wide[pl.ds(h, right_rows, stride=block), :].astype(BF16)
        right_all[h] = right
        left_wide[pl.ds(h, left_rows, stride=block), :] = dot(left_all[h], right, 1, 1)
    products[...] = left_wide[...].astype(BF16).reshape(products.shape)


def cell_row(ref, row, rows):
    count, depth, width = ref.shape
    block = depth // rows
    return ref[:, row * block : (row + 1) * block, :].astype(F32).reshape(count * block, width)


def middle_kernel(products, d_hat_centered, d_products):
    rows = d_hat_centered.shape[0]
    count, depth, width = products.shape
    block = depth // rows
    for row in range(rows):
        tri_hat, inv_std = norm_rows(cell_row(products, row, rows))
        d_hat = d_hat_centered[row]
        cross = jnp.mean(d_hat * tri_hat, axis=0, keepdims=True)
        d_tri = inv_std * (d_hat - tri_hat * cross)
        d_products[:, row * block : (row + 1) * block, :] = d_tri.reshape(
            count, block, width
        ).astype(BF16)


def d_right_kernel(d_products, left_pairs, d_right_panel, d_tri_all, left_wide, right_wide):
    block, left_rows, width = d_tri_all.shape
    right_rows = right_wide.shape[0] // block
    spread(d_products, left_wide)
    for n in range(block // 2):
        pair = (2 * n, 2 * n + 1)
        d_tri = [left_wide[pl.ds(h, left_rows, stride=block), :] for h in pair]
        d_tri = jnp.concatenate(d_tri, axis=0).astype(BF16)
        d_right = dot(d_tri, left_pairs[n], 0, 0)
        for side, h in enumerate(pair):
            d_tri_all[h] = d_tri[side * left_rows : (side + 1) * left_rows]
            right_wide[pl.ds(h, right_rows, stride=block), :] = d_right[
                :, side * width : (side + 1) * width
            ]
    for rank, place in wide_places(d_right_panel, d_products.shape[0], True):
        d_right_panel[rank] = right_wide[place, :].astype(BF16)


def d_left_kernel(d_tri_all, right_all, *refs):
    *pieces, left_wide = refs
    block, left_rows, _ = d_tri_all.shape
    for h in range(block):
        left_wide[pl.ds(h, left_rows, stride=block), :] = dot(d_tri_all[h], right_all[h], 1, 0)
    depth = pieces[0].shape[0]
    for step, piece in enumerate(pieces):
        start = pl.multiple_of(partner(step, len(pieces)) * depth, depth)
        piece[...] = left_wide[pl.ds(start, depth), :].astype(BF16)


def gate_back_kernel(products, gate_slope, out_gain, out_bias, w_out, d_gate_pre):
    rows = gate_slope.shape[0]
    out_flip = transposed(w_out[...])
    out_gain_col, out_bias_col = column(out_gain[...]), column(out_bias[...])
    for row in range(rows):
        tri_hat, _ = norm_rows(cell_row(products, row, rows))
        scaled = (tri_hat * out_gain_col + out_bias_col).astype(BF16)
        d_gate_pre[row] = (dot(out_flip, scaled, 1, 0) * gate_slope[row]).astype(BF16)


def slopes_kernel(
    pair, mask, gain, bias, w_proj, w_gate, after, slopes, normed_in, inv_in, in_gain, weights
):
    del after
    rows = pair.shape[0]
    hidden = w_proj.shape[1] // 4
    w_flip = transposed(w_proj[...])
    gain_col, bias_col = column(gain[...]), column(bias[...])
    in_gain[...] = gain_col
    weights[...] = jnp.concatenate([w_proj[...], w_gate[...]], axis=1)
    masks = cell_masks(mask, rows)
    for row in range(rows):
        normed, inv_std = norm_rows(jnp.transpose(pair[row].astype(F32)))
        normed_in[row] = normed.astype(normed_in.dtype)
        inv_in[row : row + 1] = inv_std
        zln = (normed * gain_col + bias_col).astype(BF16)
        proj = dot(w_flip, zln, 1, 0)
        for side in range(2):
            base = 2 * side * hidden
            sig = sigmoid(proj[base : base + hidden])
            masked = masks[row] * sig
            value = masked * (1.0 - sig) * proj[base + hidden : base + 2 * hidden]
            slopes[row, base : base + hidden, :] = value.astype(slopes.dtype)
            slopes[row, base + hidden : base + 2 * hidden, :] = masked.astype(slopes.dtype)


def sort_d_left_kernel(*refs):
    *pieces, d_left_panel = refs
    for step, piece in enumerate(pieces):
        d_left_panel[partner(step, len(pieces))] = piece[...]


def both_halves(blocks, count):
    order = wide_order(2 * count, count, True)
    return jnp.stack(
        [blocks[order.index(place)] + blocks[order.index(count + place)] for place in range(count)]
    )


def finish_kernel(
    d_right_panel, d_left_panel, slopes, d_gate_pre, normed_in, inv_in, gain_col, weights, grad
):
    rows = grad.shape[0]
    count, depth, width = d_left_panel.shape
    hidden = count * depth // rows
    for row in range(rows):
        d_right = cell_row(d_right_panel, row, rows)
        d_right = both_halves(d_right.reshape(2 * count, depth // rows, width), count)
        parts = []
        for side, d_value in enumerate((cell_row(d_left_panel, row, rows), d_right.reshape(hidden, width))):
            for base in (2 * side * hidden, (2 * side + 1) * hidden):
                slope = slopes[row, base : base + hidden, :].astype(F32)
                parts.append((d_value * slope).astype(BF16))
        parts.append(d_gate_pre[row])
        d_in = dot(weights[...], jnp.concatenate(parts, axis=0), 1, 0) * gain_col[...]
        normed = normed_in[row].astype(F32)
        mean_grad = jnp.mean(d_in, axis=0, keepdims=True)
        mean_cross = jnp.mean(d_in * normed, axis=0, keepdims=True)
        result = inv_in[row : row + 1] * (d_in - mean_grad - normed * mean_cross)
        grad[row] = jnp.transpose(result).astype(BF16)


def swap(values, count, back):
    groups = [wide_order(lax.axis_size("row"), count, back)]
    return lax.all_to_all(
        values, "row", split_axis=0, concat_axis=0, tiled=True, axis_index_groups=groups
    )


def swap_half(values, count):
    devices = range(lax.axis_size("row"))
    groups = [[d for d in devices if d // count == half] for half in range(len(devices) // count)]
    return lax.all_to_all(
        values, "row", split_axis=0, concat_axis=0, tiled=True, axis_index_groups=groups
    )


def swap_pieces(pieces):
    devices = range(lax.axis_size("row"))
    count = len(pieces)
    return [pieces[0]] + [
        lax.ppermute(pieces[step], "row", [(d, d ^ distance(step, count)) for d in devices])
        for step in range(1, count)
    ]


def kernel_shards(
    pair,
    cotangent,
    residue_mask,
    ln_in_gain,
    ln_in_bias,
    w_proj,
    w_gate,
    ln_out_gain,
    ln_out_bias,
    w_out,
):
    rows, width, channels = pair.shape
    hidden = w_out.shape[0]
    halves = 2
    devices = lax.axis_size("row")
    count = devices // halves
    block = hidden // count
    left_rows, right_rows = rows * count, rows * devices
    shape = jax.ShapeDtypeStruct
    panel = shape((count, rows * block, width), BF16)
    wide_panel = shape((devices, rows * block, width), BF16)
    mask = residue_mask.reshape(1, width)
    gain, bias = ln_in_gain.reshape(1, channels), ln_in_bias.reshape(1, channels)
    out_gain, out_bias = ln_out_gain.reshape(1, hidden), ln_out_bias.reshape(1, hidden)
    cells = rows * width
    piece = shape((rows * block, width), BF16)
    left_panel = pltpu.VMEM(panel.shape, BF16)
    left_wide = pltpu.VMEM((left_rows * block, width), F32)
    right_wide = pltpu.VMEM((right_rows * block, width), F32)
    (own_right,) = call(
        project_right_kernel,
        "project_right",
        [wide_panel],
        [pair, mask, gain, bias, w_proj],
        fetched=range(5),
        flops=2 * cells * channels * 2 * hidden,
        limit=64 * 1024 * 1024 - 640 * 1024,
    )
    right_panel = swap(own_right, count, False)
    pieces = call(
        project_left_kernel,
        "project_left",
        [piece] * count,
        [pair, mask, gain, bias, w_proj, own_right],
        fetched=range(5),
        unread=(5,),
        scratch=[left_panel],
        flops=2 * cells * channels * 2 * hidden,
    )
    pieces = swap_pieces(pieces)
    left_all, left_pairs = call(
        sort_left_kernel,
        "sort_left",
        [
            shape((block, left_rows, width), BF16),
            shape((block // 2, 2 * left_rows, 2 * width), BF16),
        ],
        pieces,
        scratch=[left_wide],
    )
    d_hat_centered, gate_slope = call(
        prepare_kernel,
        "prepare",
        [shape((rows, hidden, width), F32), shape((rows, channels, width), F32)],
        [pair, cotangent, gain, bias, w_gate, out_gain, w_out],
        fetched=range(7),
        flops=2 * cells * channels * 2 * hidden,
    )
    products, right_all = call(
        tri_kernel,
        "tri",
        [panel, shape((block, right_rows, width), BF16)],
        [right_panel, left_all, d_hat_centered],
        unread=(2,),
        scratch=[left_wide, right_wide],
        flops=2 * block * left_rows * width * right_rows,
    )
    products = swap_half(products, count)
    (d_products,) = call(
        middle_kernel,
        "middle",
        [panel],
        [products, d_hat_centered],
        flops=20 * cells * hidden,
    )
    d_products = swap_half(d_products, count)
    d_right_panel, d_tri_all = call(
        d_right_kernel,
        "d_right",
        [wide_panel, shape((block, left_rows, width), BF16)],
        [d_products, left_pairs],
        scratch=[left_wide, right_wide],
        flops=2 * block * left_rows * width * right_rows,
    )
    d_right_panel = swap(d_right_panel, count, True)
    d_pieces = call(
        d_left_kernel,
        "d_left",
        [piece] * count,
        [d_tri_all, right_all],
        scratch=[left_wide],
        flops=2 * block * left_rows * width * right_rows,
    )
    d_pieces = swap_pieces(d_pieces)
    (d_left_panel,) = call(sort_d_left_kernel, "sort_d_left", [panel], d_pieces)
    (d_gate_pre,) = call(
        gate_back_kernel,
        "gate_back",
        [shape((rows, channels, width), BF16)],
        [products, gate_slope, out_gain, out_bias, w_out],
        fetched=range(2, 5),
        flops=2 * cells * channels * hidden,
    )
    slopes, normed_in, inv_in, gain_col, weights = call(
        slopes_kernel,
        "slopes",
        [
            shape((rows, 4 * hidden, width), BF16),
            shape((rows, channels, width), BF16),
            shape((rows, width), F32),
            shape((channels, channels), F32),
            shape((channels, 4 * hidden + channels), BF16),
        ],
        [pair, mask, gain, bias, w_proj, w_gate, d_gate_pre],
        fetched=range(6),
        unread=(6,),
        flops=2 * cells * channels * 4 * hidden,
    )
    (grad,) = call(
        finish_kernel,
        "finish",
        [shape(pair.shape, BF16)],
        [
            d_right_panel,
            d_left_panel,
            slopes,
            d_gate_pre,
            normed_in,
            inv_in,
            gain_col,
            weights,
        ],
        flops=2 * cells * channels * 4 * hidden,
    )
    return grad


def normalize(values, reduce_axis):
    mean_value = jnp.mean(values, axis=reduce_axis, keepdims=True)
    centered = values - mean_value
    variance = jnp.mean(centered * centered, axis=reduce_axis, keepdims=True)
    inv_std = lax.rsqrt(variance + 1e-05)
    return (centered * inv_std, inv_std)


def norm_backward(upstream, normed, inv_std, reduce_axis):
    mean_grad = jnp.mean(upstream, axis=reduce_axis, keepdims=True)
    mean_cross = jnp.mean(upstream * normed, axis=reduce_axis, keepdims=True)
    return inv_std * (upstream - mean_grad - normed * mean_cross)


def shards(
    pair,
    cotangent,
    residue_mask,
    ln_in_gain,
    ln_in_bias,
    w_proj,
    w_gate,
    ln_out_gain,
    ln_out_bias,
    w_out,
):
    local_rows = pair.shape[0]
    local_cols = pair.shape[1]
    hidden = w_out.shape[0]
    chan_index = lax.axis_index("chan")
    row_start = lax.axis_index("row") * local_rows
    col_start = chan_index * local_cols
    mask_float = residue_mask.astype(jnp.float32)
    row_mask = lax.dynamic_slice_in_dim(mask_float, row_start, local_rows)
    col_mask = lax.dynamic_slice_in_dim(mask_float, col_start, local_cols)
    cell_mask = (row_mask[:, None] * col_mask[None, :])[None]
    normed, inv_std = normalize(pair.astype(jnp.float32), -1)
    normed_pair = (normed * ln_in_gain + ln_in_bias).astype(jnp.bfloat16)
    projected = jnp.einsum("rmc,ch->hrm", normed_pair, w_proj, preferred_element_type=jnp.float32)
    left_panel = (
        cell_mask * jax.nn.sigmoid(projected[:hidden]) * projected[hidden : 2 * hidden]
    ).astype(jnp.bfloat16)
    right_panel = (
        cell_mask * jax.nn.sigmoid(projected[2 * hidden : 3 * hidden]) * projected[3 * hidden :]
    ).astype(jnp.bfloat16)
    panels = lax.all_to_all(
        jnp.stack([left_panel, right_panel]), "row", split_axis=1, concat_axis=2, tiled=True
    )
    left_all = panels[0]
    right_all = panels[1]
    right_rows = lax.all_to_all(right_all, "chan", split_axis=1, concat_axis=2, tiled=True)
    partner = right_rows
    tri_part = jnp.einsum(
        "gik,gjk->gij",
        lax.all_gather(left_all, "chan", axis=2, tiled=True),
        partner,
        preferred_element_type=jnp.float32,
    ).astype(jnp.bfloat16)
    tri_cells = lax.all_to_all(tri_part, "row", split_axis=1, concat_axis=0, tiled=True)
    tri_hat, inv_tri = normalize(tri_cells.astype(jnp.float32), 0)
    scaled = (tri_hat * ln_out_gain[:, None, None] + ln_out_bias[:, None, None]).astype(
        jnp.bfloat16
    )
    proj_out = jnp.einsum("hrm,hc->rmc", scaled, w_out, preferred_element_type=jnp.float32)
    gate_value = jax.nn.sigmoid(
        jnp.einsum("rmc,cd->rmd", normed_pair, w_gate, preferred_element_type=jnp.float32)
    )
    cot_float = cotangent.astype(jnp.float32)
    d_gate_pre = (cot_float * proj_out * gate_value * (1.0 - gate_value)).astype(jnp.bfloat16)
    d_scaled = (cot_float * gate_value).astype(jnp.bfloat16)
    d_hat = jnp.einsum("rmc,hc->hrm", d_scaled, w_out, preferred_element_type=jnp.float32)
    d_hat = d_hat * ln_out_gain[:, None, None]
    d_tri = norm_backward(d_hat, tri_hat, inv_tri, 0).astype(jnp.bfloat16)
    d_tri_all = lax.all_to_all(d_tri, "row", split_axis=0, concat_axis=1, tiled=True)
    panel_piece = lax.all_gather(d_tri_all, "chan", axis=2, tiled=True)
    partner = right_all
    d_left = jnp.einsum("gij,gjk->gik", panel_piece, partner, preferred_element_type=jnp.float32)
    contribution = jnp.einsum(
        "gij,gik->gjk", panel_piece, left_all, preferred_element_type=jnp.float32
    )
    d_right = contribution
    d_left, d_right = (d_left, d_right)
    d_stack = jnp.stack([d_left, d_right]).astype(jnp.bfloat16)
    d_panels = lax.all_to_all(d_stack, "row", split_axis=2, concat_axis=1, tiled=True)

    def gating(d_value, gate_proj, value_proj):
        sigmoid_val = jax.nn.sigmoid(gate_proj)
        masked_grad = d_value.astype(jnp.float32) * cell_mask
        return (
            masked_grad * value_proj * sigmoid_val * (1.0 - sigmoid_val),
            masked_grad * sigmoid_val,
        )

    gate_left, value_left = gating(d_panels[0], projected[:hidden], projected[hidden : 2 * hidden])
    gate_right, value_right = gating(
        d_panels[1], projected[2 * hidden : 3 * hidden], projected[3 * hidden :]
    )
    d_proj = jnp.concatenate([gate_left, value_left, gate_right, value_right], axis=0).astype(
        jnp.bfloat16
    )
    d_normed = jnp.einsum("hrm,ch->rmc", d_proj, w_proj, preferred_element_type=jnp.float32)
    d_normed = d_normed + jnp.einsum(
        "rmd,cd->rmc", d_gate_pre, w_gate, preferred_element_type=jnp.float32
    )
    d_input = d_normed * ln_in_gain
    return norm_backward(d_input, normed, inv_std, -1).astype(jnp.bfloat16)


def solution(mesh):
    fits = mesh.shape["chan"] == 1 and mesh.shape["row"] in (8, 16)
    return jax.shard_map(
        kernel_shards if fits else shards,
        mesh=mesh,
        in_specs=(
            P(("grp", "row"), "chan", None),
            P(("grp", "row"), "chan", None),
            P("grp"),
            P(),
            P(),
            P(),
            P(),
            P(),
            P(),
            P(),
        ),
        out_specs=P(("grp", "row"), "chan", None),
        check_vma=False,
    )
```

```python
import functools

import jax
import jax.numpy as jnp
from jax import lax
from jax.experimental import pallas as pl
from jax.experimental.pallas import tpu as pltpu
from jax.sharding import PartitionSpec as P

F32 = jnp.float32
BF16 = jnp.bfloat16
VMEM_LIMIT = 16 * 1024 * 1024


def dot(lhs, rhs, lhs_dim, rhs_dim):
    return lax.dot_general(
        lhs, rhs, (((lhs_dim,), (rhs_dim,)), ((), ())), preferred_element_type=F32
    )


def transposed(matrix):
    return jnp.transpose(matrix.astype(F32)).astype(BF16)


def sigmoid(values):
    return 1.0 / (1.0 + jnp.exp(-values))


def column(row):
    size = row.shape[1]
    return jnp.transpose(jnp.broadcast_to(row, (size, size)))


def norm_rows(values):
    centered = values - jnp.mean(values, axis=0, keepdims=True)
    variance = jnp.mean(centered * centered, axis=0, keepdims=True)
    inv_std = lax.rsqrt(variance + 1e-05)
    return centered * inv_std, inv_std


def call(
    kernel, name, outs, args, fetched=(), unread=(), scratch=(), flops=0, limit=VMEM_LIMIT
):
    moved = sum(a.size * a.dtype.itemsize for a in args) + sum(
        o.size * jnp.dtype(o.dtype).itemsize for o in outs
    )
    n_args, n_outs, n_fetched = len(args), len(outs), len(fetched)

    def body(*refs):
        ins = list(refs[:n_args])
        rest = refs[n_args + n_outs :]
        copies = []
        for n, place in enumerate(fetched):
            copies.append(pltpu.make_async_copy(ins[place], rest[n], rest[n_fetched].at[n]))
            ins[place] = rest[n]
        for copy in copies:
            copy.start()
        for copy in copies:
            copy.wait()
        kernel(*ins, *refs[n_args : n_args + n_outs], *rest[n_fetched + (n_fetched > 0) :])

    buffers = [pltpu.VMEM(args[place].shape, args[place].dtype) for place in fetched]
    if fetched:
        buffers.append(pltpu.SemaphoreType.DMA((n_fetched,)))
    return pl.pallas_call(
        body,
        name=name,
        out_shape=outs,
        in_specs=[
            pl.BlockSpec(
                memory_space=pltpu.HBM if n in fetched else pl.ANY if n in unread else pltpu.VMEM
            )
            for n in range(n_args)
        ],
        out_specs=[pl.BlockSpec(memory_space=pltpu.VMEM) for _ in outs],
        scratch_shapes=buffers + list(scratch),
        compiler_params=pltpu.CompilerParams(vmem_limit_bytes=limit),
        cost_estimate=pl.CostEstimate(flops=flops, bytes_accessed=moved, transcendentals=0),
    )(*args)


def cell_masks(mask, rows):
    columns = mask[...].astype(F32)
    shape = (rows, columns.shape[1])
    first = lax.axis_index("row") * rows
    own = lax.broadcasted_iota(jnp.int32, shape, 1) == (
        lax.broadcasted_iota(jnp.int32, shape, 0) + first
    )
    row_mask = jnp.sum(jnp.where(own, columns, 0.0), axis=1, keepdims=True)
    cells = row_mask * columns
    return [cells[row : row + 1] for row in range(rows)]


def wide_order(devices, count, back):
    order = []
    for place in range(count):
        if back:
            order += [place ^ (count // 2), count + place]
        else:
            order += [count + (place ^ 2), place ^ (count // 2)]
    return order


def distance(step, count):
    far = sorted(range(3, count), reverse=True)
    return [*range(min(3, count)), *far][step]


def partner(step, count):
    return lax.rem(lax.axis_index("row"), count) ^ distance(step, count)


def gated_rows(pair, mask, gain, bias, w_proj, side):
    rows = pair.shape[0]
    hidden = w_proj.shape[1] // 4
    w_flip = transposed(w_proj[:, 2 * side * hidden : 2 * (side + 1) * hidden])
    gain_col, bias_col = column(gain[...]), column(bias[...])
    masks = cell_masks(mask, rows)
    for row in range(rows):
        normed, _ = norm_rows(jnp.transpose(pair[row].astype(F32)))
        zln = (normed * gain_col + bias_col).astype(BF16)
        proj = dot(w_flip, zln, 1, 0)
        yield row, masks[row] * sigmoid(proj[:hidden]) * proj[hidden:]


def project_right_kernel(pair, mask, gain, bias, w_proj, right_panel):
    rows = pair.shape[0]
    devices, depth, width = right_panel.shape
    block = depth // rows
    count = w_proj.shape[1] // 4 // block
    for row, right in gated_rows(pair, mask, gain, bias, w_proj, 1):
        right = right.reshape(count, block, width).astype(BF16)
        for rank in range(devices):
            place = wide_order(devices, count, False)[rank] % count
            right_panel[rank, row * block : (row + 1) * block, :] = right[place]


def project_left_kernel(pair, mask, gain, bias, w_proj, after, *refs):
    del after
    *pieces, left_panel = refs
    rows = pair.shape[0]
    count, depth, width = left_panel.shape
    block = depth // rows
    for row, left in gated_rows(pair, mask, gain, bias, w_proj, 0):
        left = left.reshape(count, block, width).astype(BF16)
        left_panel[:, row * block : (row + 1) * block, :] = left
    for step, piece in enumerate(pieces):
        piece[...] = left_panel[partner(step, count)]


def prepare_kernel(
    pair, cotangent, gain, bias, w_gate, out_gain, w_out, d_hat_centered, gate_slope
):
    gate_flip = transposed(w_gate[...])
    gain_col, bias_col = column(gain[...]), column(bias[...])
    out_gain_col = column(out_gain[...])
    for row in range(pair.shape[0]):
        normed, _ = norm_rows(jnp.transpose(pair[row].astype(F32)))
        zln = (normed * gain_col + bias_col).astype(BF16)
        gate = sigmoid(dot(gate_flip, zln, 1, 0))
        cot = jnp.transpose(cotangent[row].astype(F32))
        d_scaled = (cot * gate).astype(BF16)
        d_hat = dot(w_out[...], d_scaled, 1, 0) * out_gain_col
        d_hat_centered[row] = d_hat - jnp.mean(d_hat, axis=0, keepdims=True)
        gate_slope[row] = cot * gate * (1.0 - gate)


def spread(panel, wide):
    wide[...] = panel[...].astype(F32).reshape(wide.shape)


def wide_places(panel, count, back):
    devices, depth, _ = panel.shape
    for rank, device in enumerate(wide_order(devices, count, back)):
        yield rank, slice(device * depth, (device + 1) * depth)


def sort_left_kernel(*refs):
    *pieces, left_all, left_pairs, left_wide = refs
    block, left_rows, _ = left_all.shape
    depth = pieces[0].shape[0]
    for step, piece in enumerate(pieces):
        start = pl.multiple_of(partner(step, len(pieces)) * depth, depth)
        left_wide[pl.ds(start, depth), :] = piece[...].astype(F32)
    for h in range(block):
        left_all[h] = left_wide[pl.ds(h, left_rows, stride=block), :].astype(BF16)
    empty = jnp.zeros(left_all.shape[1:], BF16)
    for n in range(block // 2):
        left_pairs[n, :left_rows, :] = jnp.concatenate([left_all[2 * n], empty], axis=1)
        left_pairs[n, left_rows:, :] = jnp.concatenate([empty, left_all[2 * n + 1]], axis=1)


def tri_kernel(right_panel, left_all, after, products, right_all, left_wide, right_wide):
    del after
    block, left_rows, _ = left_all.shape
    right_rows = right_all.shape[1]
    for rank, place in wide_places(right_panel, products.shape[0], False):
        right_wide[place, :] = right_panel[rank].astype(F32)
    for h in range(block):
        right = right_wide[pl.ds(h, right_rows, stride=block), :].astype(BF16)
        right_all[h] = right
        left_wide[pl.ds(h, left_rows, stride=block), :] = dot(left_all[h], right, 1, 1)
    products[...] = left_wide[...].astype(BF16).reshape(products.shape)


def cell_row(ref, row, rows):
    count, depth, width = ref.shape
    block = depth // rows
    return ref[:, row * block : (row + 1) * block, :].astype(F32).reshape(count * block, width)


def middle_kernel(products, d_hat_centered, d_products):
    rows = d_hat_centered.shape[0]
    count, depth, width = products.shape
    block = depth // rows
    for row in range(rows):
        tri_hat, inv_std = norm_rows(cell_row(products, row, rows))
        d_hat = d_hat_centered[row]
        cross = jnp.mean(d_hat * tri_hat, axis=0, keepdims=True)
        d_tri = inv_std * (d_hat - tri_hat * cross)
        d_products[:, row * block : (row + 1) * block, :] = d_tri.reshape(
            count, block, width
        ).astype(BF16)


def d_right_kernel(d_products, left_pairs, d_right_panel, d_tri_all, left_wide, right_wide):
    block, left_rows, width = d_tri_all.shape
    right_rows = right_wide.shape[0] // block
    spread(d_products, left_wide)
    for n in range(block // 2):
        pair = (2 * n, 2 * n + 1)
        d_tri = [left_wide[pl.ds(h, left_rows, stride=block), :] for h in pair]
        d_tri = jnp.concatenate(d_tri, axis=0).astype(BF16)
        d_right = dot(d_tri, left_pairs[n], 0, 0)
        for side, h in enumerate(pair):
            d_tri_all[h] = d_tri[side * left_rows : (side + 1) * left_rows]
            right_wide[pl.ds(h, right_rows, stride=block), :] = d_right[
                :, side * width : (side + 1) * width
            ]
    for rank, place in wide_places(d_right_panel, d_products.shape[0], True):
        d_right_panel[rank] = right_wide[place, :].astype(BF16)


def d_left_kernel(d_tri_all, right_all, *refs):
    *pieces, left_wide = refs
    block, left_rows, _ = d_tri_all.shape
    for h in range(block):
        left_wide[pl.ds(h, left_rows, stride=block), :] = dot(d_tri_all[h], right_all[h], 1, 0)
    depth = pieces[0].shape[0]
    for step, piece in enumerate(pieces):
        start = pl.multiple_of(partner(step, len(pieces)) * depth, depth)
        piece[...] = left_wide[pl.ds(start, depth), :].astype(BF16)


def gate_back_kernel(products, gate_slope, out_gain, out_bias, w_out, d_gate_pre):
    rows = gate_slope.shape[0]
    out_flip = transposed(w_out[...])
    out_gain_col, out_bias_col = column(out_gain[...]), column(out_bias[...])
    for row in range(rows):
        tri_hat, _ = norm_rows(cell_row(products, row, rows))
        scaled = (tri_hat * out_gain_col + out_bias_col).astype(BF16)
        d_gate_pre[row] = (dot(out_flip, scaled, 1, 0) * gate_slope[row]).astype(BF16)


def slopes_kernel(
    pair, mask, gain, bias, w_proj, w_gate, after, slopes, normed_in, inv_in, in_gain, weights
):
    del after
    rows = pair.shape[0]
    hidden = w_proj.shape[1] // 4
    w_flip = transposed(w_proj[...])
    gain_col, bias_col = column(gain[...]), column(bias[...])
    in_gain[...] = gain_col
    weights[...] = jnp.concatenate([w_proj[...], w_gate[...]], axis=1)
    masks = cell_masks(mask, rows)
    for row in range(rows):
        normed, inv_std = norm_rows(jnp.transpose(pair[row].astype(F32)))
        normed_in[row] = normed.astype(normed_in.dtype)
        inv_in[row : row + 1] = inv_std
        zln = (normed * gain_col + bias_col).astype(BF16)
        proj = dot(w_flip, zln, 1, 0)
        for side in range(2):
            base = 2 * side * hidden
            sig = sigmoid(proj[base : base + hidden])
            masked = masks[row] * sig
            value = masked * (1.0 - sig) * proj[base + hidden : base + 2 * hidden]
            slopes[row, base : base + hidden, :] = value.astype(slopes.dtype)
            slopes[row, base + hidden : base + 2 * hidden, :] = masked.astype(slopes.dtype)


def sort_d_left_kernel(*refs):
    *pieces, d_left_panel = refs
    for step, piece in enumerate(pieces):
        d_left_panel[partner(step, len(pieces))] = piece[...]


def both_halves(blocks, count):
    order = wide_order(2 * count, count, True)
    return jnp.stack(
        [blocks[order.index(place)] + blocks[order.index(count + place)] for place in range(count)]
    )


def finish_kernel(
    d_right_panel, d_left_panel, slopes, d_gate_pre, normed_in, inv_in, gain_col, weights, grad
):
    rows = grad.shape[0]
    count, depth, width = d_left_panel.shape
    hidden = count * depth // rows
    for row in range(rows):
        d_right = cell_row(d_right_panel, row, rows)
        d_right = both_halves(d_right.reshape(2 * count, depth // rows, width), count)
        parts = []
        for side, d_value in enumerate((cell_row(d_left_panel, row, rows), d_right.reshape(hidden, width))):
            for base in (2 * side * hidden, (2 * side + 1) * hidden):
                slope = slopes[row, base : base + hidden, :].astype(F32)
                parts.append((d_value * slope).astype(BF16))
        parts.append(d_gate_pre[row])
        d_in = dot(weights[...], jnp.concatenate(parts, axis=0), 1, 0) * gain_col[...]
        normed = normed_in[row].astype(F32)
        mean_grad = jnp.mean(d_in, axis=0, keepdims=True)
        mean_cross = jnp.mean(d_in * normed, axis=0, keepdims=True)
        result = inv_in[row : row + 1] * (d_in - mean_grad - normed * mean_cross)
        grad[row] = jnp.transpose(result).astype(BF16)


def swap(values, count, back):
    groups = [wide_order(lax.axis_size("row"), count, back)]
    return lax.all_to_all(
        values, "row", split_axis=0, concat_axis=0, tiled=True, axis_index_groups=groups
    )


def swap_half(values, count):
    devices = range(lax.axis_size("row"))
    groups = [[d for d in devices if d // count == half] for half in range(len(devices) // count)]
    return lax.all_to_all(
        values, "row", split_axis=0, concat_axis=0, tiled=True, axis_index_groups=groups
    )


def swap_pieces(pieces):
    devices = range(lax.axis_size("row"))
    count = len(pieces)
    return [pieces[0]] + [
        lax.ppermute(pieces[step], "row", [(d, d ^ distance(step, count)) for d in devices])
        for step in range(1, count)
    ]


def kernel_shards(
    pair,
    cotangent,
    residue_mask,
    ln_in_gain,
    ln_in_bias,
    w_proj,
    w_gate,
    ln_out_gain,
    ln_out_bias,
    w_out,
):
    rows, width, channels = pair.shape
    hidden = w_out.shape[0]
    halves = 2
    devices = lax.axis_size("row")
    count = devices // halves
    block = hidden // count
    left_rows, right_rows = rows * count, rows * devices
    shape = jax.ShapeDtypeStruct
    panel = shape((count, rows * block, width), BF16)
    wide_panel = shape((devices, rows * block, width), BF16)
    mask = residue_mask.reshape(1, width)
    gain, bias = ln_in_gain.reshape(1, channels), ln_in_bias.reshape(1, channels)
    out_gain, out_bias = ln_out_gain.reshape(1, hidden), ln_out_bias.reshape(1, hidden)
    cells = rows * width
    piece = shape((rows * block, width), BF16)
    left_panel = pltpu.VMEM(panel.shape, BF16)
    left_wide = pltpu.VMEM((left_rows * block, width), F32)
    right_wide = pltpu.VMEM((right_rows * block, width), F32)
    (own_right,) = call(
        project_right_kernel,
        "project_right",
        [wide_panel],
        [pair, mask, gain, bias, w_proj],
        fetched=range(5),
        flops=2 * cells * channels * 2 * hidden,
        limit=64 * 1024 * 1024 - 640 * 1024,
    )
    right_panel = swap(own_right, count, False)
    pieces = call(
        project_left_kernel,
        "project_left",
        [piece] * count,
        [pair, mask, gain, bias, w_proj, own_right],
        fetched=range(5),
        unread=(5,),
        scratch=[left_panel],
        flops=2 * cells * channels * 2 * hidden,
    )
    pieces = swap_pieces(pieces)
    left_all, left_pairs = call(
        sort_left_kernel,
        "sort_left",
        [
            shape((block, left_rows, width), BF16),
            shape((block // 2, 2 * left_rows, 2 * width), BF16),
        ],
        pieces,
        scratch=[left_wide],
    )
    d_hat_centered, gate_slope = call(
        prepare_kernel,
        "prepare",
        [shape((rows, hidden, width), F32), shape((rows, channels, width), F32)],
        [pair, cotangent, gain, bias, w_gate, out_gain, w_out],
        fetched=range(7),
        flops=2 * cells * channels * 2 * hidden,
    )
    products, right_all = call(
        tri_kernel,
        "tri",
        [panel, shape((block, right_rows, width), BF16)],
        [right_panel, left_all, d_hat_centered],
        unread=(2,),
        scratch=[left_wide, right_wide],
        flops=2 * block * left_rows * width * right_rows,
    )
    products = swap_half(products, count)
    (d_products,) = call(
        middle_kernel,
        "middle",
        [panel],
        [products, d_hat_centered],
        flops=20 * cells * hidden,
    )
    d_products = swap_half(d_products, count)
    d_right_panel, d_tri_all = call(
        d_right_kernel,
        "d_right",
        [wide_panel, shape((block, left_rows, width), BF16)],
        [d_products, left_pairs],
        scratch=[left_wide, right_wide],
        flops=2 * block * left_rows * width * right_rows,
    )
    d_right_panel = swap(d_right_panel, count, True)
    d_pieces = call(
        d_left_kernel,
        "d_left",
        [piece] * count,
        [d_tri_all, right_all],
        scratch=[left_wide],
        flops=2 * block * left_rows * width * right_rows,
    )
    d_pieces = swap_pieces(d_pieces)
    (d_left_panel,) = call(sort_d_left_kernel, "sort_d_left", [panel], d_pieces)
    (d_gate_pre,) = call(
        gate_back_kernel,
        "gate_back",
        [shape((rows, channels, width), BF16)],
        [products, gate_slope, out_gain, out_bias, w_out],
        fetched=range(2, 5),
        flops=2 * cells * channels * hidden,
    )
    slopes, normed_in, inv_in, gain_col, weights = call(
        slopes_kernel,
        "slopes",
        [
            shape((rows, 4 * hidden, width), BF16),
            shape((rows, channels, width), BF16),
            shape((rows, width), F32),
            shape((channels, channels), F32),
            shape((channels, 4 * hidden + channels), BF16),
        ],
        [pair, mask, gain, bias, w_proj, w_gate, d_gate_pre],
        fetched=range(6),
        unread=(6,),
        flops=2 * cells * channels * 4 * hidden,
    )
    (grad,) = call(
        finish_kernel,
        "finish",
        [shape(pair.shape, BF16)],
        [
            d_right_panel,
            d_left_panel,
            slopes,
            d_gate_pre,
            normed_in,
            inv_in,
            gain_col,
            weights,
        ],
        flops=2 * cells * channels * 4 * hidden,
    )
    return grad


def normalize(values, reduce_axis):
    mean_value = jnp.mean(values, axis=reduce_axis, keepdims=True)
    centered = values - mean_value
    variance = jnp.mean(centered * centered, axis=reduce_axis, keepdims=True)
    inv_std = lax.rsqrt(variance + 1e-05)
    return (centered * inv_std, inv_std)


def norm_backward(upstream, normed, inv_std, reduce_axis):
    mean_grad = jnp.mean(upstream, axis=reduce_axis, keepdims=True)
    mean_cross = jnp.mean(upstream * normed, axis=reduce_axis, keepdims=True)
    return inv_std * (upstream - mean_grad - normed * mean_cross)


def shards(
    pair,
    cotangent,
    residue_mask,
    ln_in_gain,
    ln_in_bias,
    w_proj,
    w_gate,
    ln_out_gain,
    ln_out_bias,
    w_out,
):
    local_rows = pair.shape[0]
    local_cols = pair.shape[1]
    hidden = w_out.shape[0]
    chan_index = lax.axis_index("chan")
    row_start = lax.axis_index("row") * local_rows
    col_start = chan_index * local_cols
    mask_float = residue_mask.astype(jnp.float32)
    row_mask = lax.dynamic_slice_in_dim(mask_float, row_start, local_rows)
    col_mask = lax.dynamic_slice_in_dim(mask_float, col_start, local_cols)
    cell_mask = (row_mask[:, None] * col_mask[None, :])[None]
    normed, inv_std = normalize(pair.astype(jnp.float32), -1)
    normed_pair = (normed * ln_in_gain + ln_in_bias).astype(jnp.bfloat16)
    projected = jnp.einsum("rmc,ch->hrm", normed_pair, w_proj, preferred_element_type=jnp.float32)
    left_panel = (
        cell_mask * jax.nn.sigmoid(projected[:hidden]) * projected[hidden : 2 * hidden]
    ).astype(jnp.bfloat16)
    right_panel = (
        cell_mask * jax.nn.sigmoid(projected[2 * hidden : 3 * hidden]) * projected[3 * hidden :]
    ).astype(jnp.bfloat16)
    panels = lax.all_to_all(
        jnp.stack([left_panel, right_panel]), "row", split_axis=1, concat_axis=2, tiled=True
    )
    left_all = panels[0]
    right_all = panels[1]
    right_rows = lax.all_to_all(right_all, "chan", split_axis=1, concat_axis=2, tiled=True)
    partner = right_rows
    tri_part = jnp.einsum(
        "gik,gjk->gij",
        lax.all_gather(left_all, "chan", axis=2, tiled=True),
        partner,
        preferred_element_type=jnp.float32,
    ).astype(jnp.bfloat16)
    tri_cells = lax.all_to_all(tri_part, "row", split_axis=1, concat_axis=0, tiled=True)
    tri_hat, inv_tri = normalize(tri_cells.astype(jnp.float32), 0)
    scaled = (tri_hat * ln_out_gain[:, None, None] + ln_out_bias[:, None, None]).astype(
        jnp.bfloat16
    )
    proj_out = jnp.einsum("hrm,hc->rmc", scaled, w_out, preferred_element_type=jnp.float32)
    gate_value = jax.nn.sigmoid(
        jnp.einsum("rmc,cd->rmd", normed_pair, w_gate, preferred_element_type=jnp.float32)
    )
    cot_float = cotangent.astype(jnp.float32)
    d_gate_pre = (cot_float * proj_out * gate_value * (1.0 - gate_value)).astype(jnp.bfloat16)
    d_scaled = (cot_float * gate_value).astype(jnp.bfloat16)
    d_hat = jnp.einsum("rmc,hc->hrm", d_scaled, w_out, preferred_element_type=jnp.float32)
    d_hat = d_hat * ln_out_gain[:, None, None]
    d_tri = norm_backward(d_hat, tri_hat, inv_tri, 0).astype(jnp.bfloat16)
    d_tri_all = lax.all_to_all(d_tri, "row", split_axis=0, concat_axis=1, tiled=True)
    panel_piece = lax.all_gather(d_tri_all, "chan", axis=2, tiled=True)
    partner = right_all
    d_left = jnp.einsum("gij,gjk->gik", panel_piece, partner, preferred_element_type=jnp.float32)
    contribution = jnp.einsum(
        "gij,gik->gjk", panel_piece, left_all, preferred_element_type=jnp.float32
    )
    d_right = contribution
    d_left, d_right = (d_left, d_right)
    d_stack = jnp.stack([d_left, d_right]).astype(jnp.bfloat16)
    d_panels = lax.all_to_all(d_stack, "row", split_axis=2, concat_axis=1, tiled=True)

    def gating(d_value, gate_proj, value_proj):
        sigmoid_val = jax.nn.sigmoid(gate_proj)
        masked_grad = d_value.astype(jnp.float32) * cell_mask
        return (
            masked_grad * value_proj * sigmoid_val * (1.0 - sigmoid_val),
            masked_grad * sigmoid_val,
        )

    gate_left, value_left = gating(d_panels[0], projected[:hidden], projected[hidden : 2 * hidden])
    gate_right, value_right = gating(
        d_panels[1], projected[2 * hidden : 3 * hidden], projected[3 * hidden :]
    )
    d_proj = jnp.concatenate([gate_left, value_left, gate_right, value_right], axis=0).astype(
        jnp.bfloat16
    )
    d_normed = jnp.einsum("hrm,ch->rmc", d_proj, w_proj, preferred_element_type=jnp.float32)
    d_normed = d_normed + jnp.einsum(
        "rmd,cd->rmc", d_gate_pre, w_gate, preferred_element_type=jnp.float32
    )
    d_input = d_normed * ln_in_gain
    return norm_backward(d_input, normed, inv_std, -1).astype(jnp.bfloat16)


def solution(mesh):
    fits = mesh.shape["chan"] == 1 and mesh.shape["row"] in (8, 16)
    return jax.shard_map(
        kernel_shards if fits else shards,
        mesh=mesh,
        in_specs=(
            P(("grp", "row"), "chan", None),
            P(("grp", "row"), "chan", None),
            P("grp"),
            P(),
            P(),
            P(),
            P(),
            P(),
            P(),
            P(),
        ),
        out_specs=P(("grp", "row"), "chan", None),
        check_vma=False,
    )
```

```python
import functools

import jax
import jax.numpy as jnp
from jax import lax
from jax.experimental import pallas as pl
from jax.experimental.pallas import tpu as pltpu
from jax.sharding import PartitionSpec as P

F32 = jnp.float32
BF16 = jnp.bfloat16
VMEM_LIMIT = 16 * 1024 * 1024


def dot(lhs, rhs, lhs_dim, rhs_dim):
    return lax.dot_general(
        lhs, rhs, (((lhs_dim,), (rhs_dim,)), ((), ())), preferred_element_type=F32
    )


def transposed(matrix):
    return jnp.transpose(matrix.astype(F32)).astype(BF16)


def sigmoid(values):
    return 1.0 / (1.0 + jnp.exp(-values))


def column(row):
    size = row.shape[1]
    return jnp.transpose(jnp.broadcast_to(row, (size, size)))


def norm_rows(values):
    centered = values - jnp.mean(values, axis=0, keepdims=True)
    variance = jnp.mean(centered * centered, axis=0, keepdims=True)
    inv_std = lax.rsqrt(variance + 1e-05)
    return centered * inv_std, inv_std


def call(
    kernel, name, outs, args, fetched=(), columns={}, unread=(), scratch=(), flops=0, limit=VMEM_LIMIT
):
    moved = sum(a.size * a.dtype.itemsize for a in args) + sum(
        o.size * jnp.dtype(o.dtype).itemsize for o in outs
    )
    n_args, n_outs, n_fetched = len(args), len(outs), len(fetched)

    def body(*refs):
        ins = list(refs[:n_args])
        rest = refs[n_args + n_outs :]
        copies = []
        for n, place in enumerate(fetched):
            source = ins[place].at[:, columns[place]] if place in columns else ins[place]
            copies.append(pltpu.make_async_copy(source, rest[n], rest[n_fetched].at[n]))
            ins[place] = rest[n]
        for copy in copies:
            copy.start()
        for copy in copies:
            copy.wait()
        kernel(*ins, *refs[n_args : n_args + n_outs], *rest[n_fetched + (n_fetched > 0) :])

    buffers = [
        pltpu.VMEM(
            (*args[place].shape[:-1], columns[place].size) if place in columns else args[place].shape,
            args[place].dtype,
        )
        for place in fetched
    ]
    if fetched:
        buffers.append(pltpu.SemaphoreType.DMA((n_fetched,)))
    return pl.pallas_call(
        body,
        name=name,
        out_shape=outs,
        in_specs=[
            pl.BlockSpec(
                memory_space=pltpu.HBM if n in fetched else pl.ANY if n in unread else pltpu.VMEM
            )
            for n in range(n_args)
        ],
        out_specs=[pl.BlockSpec(memory_space=pltpu.VMEM) for _ in outs],
        scratch_shapes=buffers + list(scratch),
        compiler_params=pltpu.CompilerParams(vmem_limit_bytes=limit),
        cost_estimate=pl.CostEstimate(flops=flops, bytes_accessed=moved, transcendentals=0),
    )(*args)


def cell_masks(mask, rows):
    columns = mask[...].astype(F32)
    shape = (rows, columns.shape[1])
    first = lax.axis_index("row") * rows
    own = lax.broadcasted_iota(jnp.int32, shape, 1) == (
        lax.broadcasted_iota(jnp.int32, shape, 0) + first
    )
    row_mask = jnp.sum(jnp.where(own, columns, 0.0), axis=1, keepdims=True)
    cells = row_mask * columns
    return [cells[row : row + 1] for row in range(rows)]


def wide_order(devices, count, back):
    order = []
    for place in range(count):
        if back:
            order += [place ^ (count // 2), count + place]
        else:
            order += [count + (place ^ 2), place ^ (count // 2)]
    return order


def distance(step, count):
    far = sorted(range(3, count), key=lambda apart: -(apart // 2))
    return [*range(min(3, count)), *far][step]


def partner(step, count):
    return lax.rem(lax.axis_index("row"), count) ^ distance(step, count)


def gated_rows(pair, mask, gain, bias, w_side):
    rows = pair.shape[0]
    hidden = w_side.shape[1] // 2
    w_flip = transposed(w_side[...])
    gain_col, bias_col = column(gain[...]), column(bias[...])
    masks = cell_masks(mask, rows)
    for row in range(rows):
        normed, _ = norm_rows(jnp.transpose(pair[row].astype(F32)))
        zln = (normed * gain_col + bias_col).astype(BF16)
        proj = dot(w_flip, zln, 1, 0)
        yield row, masks[row] * sigmoid(proj[:hidden]) * proj[hidden:]


def project_right_kernel(pair, mask, gain, bias, w_side, right_panel):
    rows = pair.shape[0]
    devices, depth, width = right_panel.shape
    block = depth // rows
    count = w_side.shape[1] // 2 // block
    for row, right in gated_rows(pair, mask, gain, bias, w_side):
        right = right.reshape(count, block, width).astype(BF16)
        for rank in range(devices):
            place = wide_order(devices, count, False)[rank] % count
            right_panel[rank, row * block : (row + 1) * block, :] = right[place]


def project_left_kernel(pair, mask, gain, bias, w_side, after, *refs):
    del after
    *pieces, left_panel = refs
    rows = pair.shape[0]
    count, depth, width = left_panel.shape
    block = depth // rows
    for row, left in gated_rows(pair, mask, gain, bias, w_side):
        left = left.reshape(count, block, width).astype(BF16)
        left_panel[:, row * block : (row + 1) * block, :] = left
    for step, piece in enumerate(pieces):
        piece[...] = left_panel[partner(step, count)]


def prepare_kernel(
    pair, cotangent, gain, bias, w_gate, out_gain, w_out, d_hat_centered, gate_slope
):
    gate_flip = transposed(w_gate[...])
    gain_col, bias_col = column(gain[...]), column(bias[...])
    out_gain_col = column(out_gain[...])
    for row in range(pair.shape[0]):
        normed, _ = norm_rows(jnp.transpose(pair[row].astype(F32)))
        zln = (normed * gain_col + bias_col).astype(BF16)
        gate = sigmoid(dot(gate_flip, zln, 1, 0))
        cot = jnp.transpose(cotangent[row].astype(F32))
        d_scaled = (cot * gate).astype(BF16)
        d_hat = dot(w_out[...], d_scaled, 1, 0) * out_gain_col
        d_hat_centered[row] = d_hat - jnp.mean(d_hat, axis=0, keepdims=True)
        gate_slope[row] = cot * gate * (1.0 - gate)


def spread(panel, wide):
    wide[...] = panel[...].astype(F32).reshape(wide.shape)


def wide_places(panel, count, back):
    devices, depth, _ = panel.shape
    for rank, device in enumerate(wide_order(devices, count, back)):
        yield rank, slice(device * depth, (device + 1) * depth)


def sort_left_kernel(*refs):
    *pieces, left_all, left_pairs, left_wide = refs
    block, left_rows, _ = left_all.shape
    depth = pieces[0].shape[0]
    for step, piece in enumerate(pieces):
        start = pl.multiple_of(partner(step, len(pieces)) * depth, depth)
        left_wide[pl.ds(start, depth), :] = piece[...].astype(F32)
    for h in range(block):
        left_all[h] = left_wide[pl.ds(h, left_rows, stride=block), :].astype(BF16)
    empty = jnp.zeros(left_all.shape[1:], BF16)
    for n in range(block // 2):
        left_pairs[n, :left_rows, :] = jnp.concatenate([left_all[2 * n], empty], axis=1)
        left_pairs[n, left_rows:, :] = jnp.concatenate([empty, left_all[2 * n + 1]], axis=1)


def tri_kernel(right_panel, left_all, after, products, right_all, left_wide, right_wide):
    del after
    block, left_rows, _ = left_all.shape
    right_rows = right_all.shape[1]
    for rank, place in wide_places(right_panel, products.shape[0], False):
        right_wide[place, :] = right_panel[rank].astype(F32)
    for h in range(block):
        right = right_wide[pl.ds(h, right_rows, stride=block), :].astype(BF16)
        right_all[h] = right
        left_wide[pl.ds(h, left_rows, stride=block), :] = dot(left_all[h], right, 1, 1)
    products[...] = left_wide[...].astype(BF16).reshape(products.shape)


def cell_row(ref, row, rows):
    count, depth, width = ref.shape
    block = depth // rows
    return ref[:, row * block : (row + 1) * block, :].astype(F32).reshape(count * block, width)


def middle_kernel(products, d_hat_centered, d_products):
    rows = d_hat_centered.shape[0]
    count, depth, width = products.shape
    block = depth // rows
    for row in range(rows):
        tri_hat, inv_std = norm_rows(cell_row(products, row, rows))
        d_hat = d_hat_centered[row]
        cross = jnp.mean(d_hat * tri_hat, axis=0, keepdims=True)
        d_tri = inv_std * (d_hat - tri_hat * cross)
        d_products[:, row * block : (row + 1) * block, :] = d_tri.reshape(
            count, block, width
        ).astype(BF16)


def d_right_kernel(d_products, left_pairs, d_right_panel, d_tri_all, left_wide, right_wide):
    block, left_rows, width = d_tri_all.shape
    right_rows = right_wide.shape[0] // block
    spread(d_products, left_wide)
    for n in range(block // 2):
        pair = (2 * n, 2 * n + 1)
        d_tri = [left_wide[pl.ds(h, left_rows, stride=block), :] for h in pair]
        d_tri = jnp.concatenate(d_tri, axis=0).astype(BF16)
        d_right = dot(d_tri, left_pairs[n], 0, 0)
        for side, h in enumerate(pair):
            d_tri_all[h] = d_tri[side * left_rows : (side + 1) * left_rows]
            right_wide[pl.ds(h, right_rows, stride=block), :] = d_right[
                :, side * width : (side + 1) * width
            ]
    for rank, place in wide_places(d_right_panel, d_products.shape[0], True):
        d_right_panel[rank] = right_wide[place, :].astype(BF16)


def d_left_kernel(d_tri_all, right_all, *refs):
    *pieces, left_wide = refs
    block, left_rows, _ = d_tri_all.shape
    for h in range(block):
        left_wide[pl.ds(h, left_rows, stride=block), :] = dot(d_tri_all[h], right_all[h], 1, 0)
    depth = pieces[0].shape[0]
    for step, piece in enumerate(pieces):
        start = pl.multiple_of(partner(step, len(pieces)) * depth, depth)
        piece[...] = left_wide[pl.ds(start, depth), :].astype(BF16)


def gate_back_kernel(products, gate_slope, out_gain, out_bias, w_out, d_gate_pre):
    rows = gate_slope.shape[0]
    out_flip = transposed(w_out[...])
    out_gain_col, out_bias_col = column(out_gain[...]), column(out_bias[...])
    for row in range(rows):
        tri_hat, _ = norm_rows(cell_row(products, row, rows))
        scaled = (tri_hat * out_gain_col + out_bias_col).astype(BF16)
        d_gate_pre[row] = (dot(out_flip, scaled, 1, 0) * gate_slope[row]).astype(BF16)


def slopes_kernel(
    pair, mask, gain, bias, w_proj, w_gate, after, slopes, normed_in, inv_in, in_gain, weights
):
    del after
    rows = pair.shape[0]
    hidden = w_proj.shape[1] // 4
    w_flip = transposed(w_proj[...])
    gain_col, bias_col = column(gain[...]), column(bias[...])
    in_gain[...] = gain_col
    weights[...] = jnp.concatenate([w_proj[...], w_gate[...]], axis=1)
    masks = cell_masks(mask, rows)
    for row in range(rows):
        normed, inv_std = norm_rows(jnp.transpose(pair[row].astype(F32)))
        normed_in[row] = normed.astype(normed_in.dtype)
        inv_in[row : row + 1] = inv_std
        zln = (normed * gain_col + bias_col).astype(BF16)
        proj = dot(w_flip, zln, 1, 0)
        for side in range(2):
            base = 2 * side * hidden
            sig = sigmoid(proj[base : base + hidden])
            masked = masks[row] * sig
            value = masked * (1.0 - sig) * proj[base + hidden : base + 2 * hidden]
            slopes[row, base : base + hidden, :] = value.astype(slopes.dtype)
            slopes[row, base + hidden : base + 2 * hidden, :] = masked.astype(slopes.dtype)


def sort_d_left_kernel(*refs):
    *pieces, d_left_panel = refs
    for step, piece in enumerate(pieces):
        d_left_panel[partner(step, len(pieces))] = piece[...]


def both_halves(blocks, count):
    order = wide_order(2 * count, count, True)
    return jnp.stack(
        [blocks[order.index(place)] + blocks[order.index(count + place)] for place in range(count)]
    )


def finish_kernel(
    d_right_panel, d_left_panel, slopes, d_gate_pre, normed_in, inv_in, gain_col, weights, grad
):
    rows = grad.shape[0]
    count, depth, width = d_left_panel.shape
    hidden = count * depth // rows
    for row in range(rows):
        d_right = cell_row(d_right_panel, row, rows)
        d_right = both_halves(d_right.reshape(2 * count, depth // rows, width), count)
        parts = []
        for side, d_value in enumerate((cell_row(d_left_panel, row, rows), d_right.reshape(hidden, width))):
            for base in (2 * side * hidden, (2 * side + 1) * hidden):
                slope = slopes[row, base : base + hidden, :].astype(F32)
                parts.append((d_value * slope).astype(BF16))
        parts.append(d_gate_pre[row])
        d_in = dot(weights[...], jnp.concatenate(parts, axis=0), 1, 0) * gain_col[...]
        normed = normed_in[row].astype(F32)
        mean_grad = jnp.mean(d_in, axis=0, keepdims=True)
        mean_cross = jnp.mean(d_in * normed, axis=0, keepdims=True)
        result = inv_in[row : row + 1] * (d_in - mean_grad - normed * mean_cross)
        grad[row] = jnp.transpose(result).astype(BF16)


def swap(values, count, back):
    groups = [wide_order(lax.axis_size("row"), count, back)]
    return lax.all_to_all(
        values, "row", split_axis=0, concat_axis=0, tiled=True, axis_index_groups=groups
    )


def swap_half(values, count):
    devices = range(lax.axis_size("row"))
    groups = [[d for d in devices if d // count == half] for half in range(len(devices) // count)]
    return lax.all_to_all(
        values, "row", split_axis=0, concat_axis=0, tiled=True, axis_index_groups=groups
    )


def swap_pieces(pieces):
    devices = range(lax.axis_size("row"))
    count = len(pieces)
    return [pieces[0]] + [
        lax.ppermute(pieces[step], "row", [(d, d ^ distance(step, count)) for d in devices])
        for step in range(1, count)
    ]


def kernel_shards(
    pair,
    cotangent,
    residue_mask,
    ln_in_gain,
    ln_in_bias,
    w_proj,
    w_gate,
    ln_out_gain,
    ln_out_bias,
    w_out,
):
    rows, width, channels = pair.shape
    hidden = w_out.shape[0]
    halves = 2
    devices = lax.axis_size("row")
    count = devices // halves
    block = hidden // count
    left_rows, right_rows = rows * count, rows * devices
    shape = jax.ShapeDtypeStruct
    panel = shape((count, rows * block, width), BF16)
    wide_panel = shape((devices, rows * block, width), BF16)
    mask = residue_mask.reshape(1, width)
    gain, bias = ln_in_gain.reshape(1, channels), ln_in_bias.reshape(1, channels)
    out_gain, out_bias = ln_out_gain.reshape(1, hidden), ln_out_bias.reshape(1, hidden)
    cells = rows * width
    piece = shape((rows * block, width), BF16)
    left_panel = pltpu.VMEM(panel.shape, BF16)
    left_wide = pltpu.VMEM((left_rows * block, width), F32)
    right_wide = pltpu.VMEM((right_rows * block, width), F32)
    (own_right,) = call(
        project_right_kernel,
        "project_right",
        [wide_panel],
        [pair, mask, gain, bias, w_proj],
        fetched=range(5),
        columns={4: pl.ds(2 * hidden, 2 * hidden)},
        flops=2 * cells * channels * 2 * hidden,
        limit=64 * 1024 * 1024 - 640 * 1024,
    )
    right_panel = swap(own_right, count, False)
    pieces = call(
        project_left_kernel,
        "project_left",
        [piece] * count,
        [pair, mask, gain, bias, w_proj, own_right],
        fetched=range(5),
        columns={4: pl.ds(0, 2 * hidden)},
        unread=(5,),
        scratch=[left_panel],
        flops=2 * cells * channels * 2 * hidden,
    )
    pieces = swap_pieces(pieces)
    left_all, left_pairs = call(
        sort_left_kernel,
        "sort_left",
        [
            shape((block, left_rows, width), BF16),
            shape((block // 2, 2 * left_rows, 2 * width), BF16),
        ],
        pieces,
        scratch=[left_wide],
    )
    d_hat_centered, gate_slope = call(
        prepare_kernel,
        "prepare",
        [shape((rows, hidden, width), F32), shape((rows, channels, width), F32)],
        [pair, cotangent, gain, bias, w_gate, out_gain, w_out],
        fetched=range(7),
        flops=2 * cells * channels * 2 * hidden,
    )
    products, right_all = call(
        tri_kernel,
        "tri",
        [panel, shape((block, right_rows, width), BF16)],
        [right_panel, left_all, d_hat_centered],
        unread=(2,),
        scratch=[left_wide, right_wide],
        flops=2 * block * left_rows * width * right_rows,
    )
    products = swap_half(products, count)
    (d_products,) = call(
        middle_kernel,
        "middle",
        [panel],
        [products, d_hat_centered],
        flops=20 * cells * hidden,
    )
    d_products = swap_half(d_products, count)
    d_right_panel, d_tri_all = call(
        d_right_kernel,
        "d_right",
        [wide_panel, shape((block, left_rows, width), BF16)],
        [d_products, left_pairs],
        scratch=[left_wide, right_wide],
        flops=2 * block * left_rows * width * right_rows,
    )
    d_right_panel = swap(d_right_panel, count, True)
    d_pieces = call(
        d_left_kernel,
        "d_left",
        [piece] * count,
        [d_tri_all, right_all],
        scratch=[left_wide],
        flops=2 * block * left_rows * width * right_rows,
    )
    d_pieces = swap_pieces(d_pieces)
    (d_left_panel,) = call(sort_d_left_kernel, "sort_d_left", [panel], d_pieces)
    (d_gate_pre,) = call(
        gate_back_kernel,
        "gate_back",
        [shape((rows, channels, width), BF16)],
        [products, gate_slope, out_gain, out_bias, w_out],
        fetched=range(2, 5),
        flops=2 * cells * channels * hidden,
    )
    slopes, normed_in, inv_in, gain_col, weights = call(
        slopes_kernel,
        "slopes",
        [
            shape((rows, 4 * hidden, width), BF16),
            shape((rows, channels, width), BF16),
            shape((rows, width), F32),
            shape((channels, channels), F32),
            shape((channels, 4 * hidden + channels), BF16),
        ],
        [pair, mask, gain, bias, w_proj, w_gate, d_gate_pre],
        fetched=range(6),
        unread=(6,),
        flops=2 * cells * channels * 4 * hidden,
    )
    (grad,) = call(
        finish_kernel,
        "finish",
        [shape(pair.shape, BF16)],
        [
            d_right_panel,
            d_left_panel,
            slopes,
            d_gate_pre,
            normed_in,
            inv_in,
            gain_col,
            weights,
        ],
        flops=2 * cells * channels * 4 * hidden,
    )
    return grad


def normalize(values, reduce_axis):
    mean_value = jnp.mean(values, axis=reduce_axis, keepdims=True)
    centered = values - mean_value
    variance = jnp.mean(centered * centered, axis=reduce_axis, keepdims=True)
    inv_std = lax.rsqrt(variance + 1e-05)
    return (centered * inv_std, inv_std)


def norm_backward(upstream, normed, inv_std, reduce_axis):
    mean_grad = jnp.mean(upstream, axis=reduce_axis, keepdims=True)
    mean_cross = jnp.mean(upstream * normed, axis=reduce_axis, keepdims=True)
    return inv_std * (upstream - mean_grad - normed * mean_cross)


def shards(
    pair,
    cotangent,
    residue_mask,
    ln_in_gain,
    ln_in_bias,
    w_proj,
    w_gate,
    ln_out_gain,
    ln_out_bias,
    w_out,
):
    local_rows = pair.shape[0]
    local_cols = pair.shape[1]
    hidden = w_out.shape[0]
    chan_index = lax.axis_index("chan")
    row_start = lax.axis_index("row") * local_rows
    col_start = chan_index * local_cols
    mask_float = residue_mask.astype(jnp.float32)
    row_mask = lax.dynamic_slice_in_dim(mask_float, row_start, local_rows)
    col_mask = lax.dynamic_slice_in_dim(mask_float, col_start, local_cols)
    cell_mask = (row_mask[:, None] * col_mask[None, :])[None]
    normed, inv_std = normalize(pair.astype(jnp.float32), -1)
    normed_pair = (normed * ln_in_gain + ln_in_bias).astype(jnp.bfloat16)
    projected = jnp.einsum("rmc,ch->hrm", normed_pair, w_proj, preferred_element_type=jnp.float32)
    left_panel = (
        cell_mask * jax.nn.sigmoid(projected[:hidden]) * projected[hidden : 2 * hidden]
    ).astype(jnp.bfloat16)
    right_panel = (
        cell_mask * jax.nn.sigmoid(projected[2 * hidden : 3 * hidden]) * projected[3 * hidden :]
    ).astype(jnp.bfloat16)
    panels = lax.all_to_all(
        jnp.stack([left_panel, right_panel]), "row", split_axis=1, concat_axis=2, tiled=True
    )
    left_all = panels[0]
    right_all = panels[1]
    right_rows = lax.all_to_all(right_all, "chan", split_axis=1, concat_axis=2, tiled=True)
    partner = right_rows
    tri_part = jnp.einsum(
        "gik,gjk->gij",
        lax.all_gather(left_all, "chan", axis=2, tiled=True),
        partner,
        preferred_element_type=jnp.float32,
    ).astype(jnp.bfloat16)
    tri_cells = lax.all_to_all(tri_part, "row", split_axis=1, concat_axis=0, tiled=True)
    tri_hat, inv_tri = normalize(tri_cells.astype(jnp.float32), 0)
    scaled = (tri_hat * ln_out_gain[:, None, None] + ln_out_bias[:, None, None]).astype(
        jnp.bfloat16
    )
    proj_out = jnp.einsum("hrm,hc->rmc", scaled, w_out, preferred_element_type=jnp.float32)
    gate_value = jax.nn.sigmoid(
        jnp.einsum("rmc,cd->rmd", normed_pair, w_gate, preferred_element_type=jnp.float32)
    )
    cot_float = cotangent.astype(jnp.float32)
    d_gate_pre = (cot_float * proj_out * gate_value * (1.0 - gate_value)).astype(jnp.bfloat16)
    d_scaled = (cot_float * gate_value).astype(jnp.bfloat16)
    d_hat = jnp.einsum("rmc,hc->hrm", d_scaled, w_out, preferred_element_type=jnp.float32)
    d_hat = d_hat * ln_out_gain[:, None, None]
    d_tri = norm_backward(d_hat, tri_hat, inv_tri, 0).astype(jnp.bfloat16)
    d_tri_all = lax.all_to_all(d_tri, "row", split_axis=0, concat_axis=1, tiled=True)
    panel_piece = lax.all_gather(d_tri_all, "chan", axis=2, tiled=True)
    partner = right_all
    d_left = jnp.einsum("gij,gjk->gik", panel_piece, partner, preferred_element_type=jnp.float32)
    contribution = jnp.einsum(
        "gij,gik->gjk", panel_piece, left_all, preferred_element_type=jnp.float32
    )
    d_right = contribution
    d_left, d_right = (d_left, d_right)
    d_stack = jnp.stack([d_left, d_right]).astype(jnp.bfloat16)
    d_panels = lax.all_to_all(d_stack, "row", split_axis=2, concat_axis=1, tiled=True)

    def gating(d_value, gate_proj, value_proj):
        sigmoid_val = jax.nn.sigmoid(gate_proj)
        masked_grad = d_value.astype(jnp.float32) * cell_mask
        return (
            masked_grad * value_proj * sigmoid_val * (1.0 - sigmoid_val),
            masked_grad * sigmoid_val,
        )

    gate_left, value_left = gating(d_panels[0], projected[:hidden], projected[hidden : 2 * hidden])
    gate_right, value_right = gating(
        d_panels[1], projected[2 * hidden : 3 * hidden], projected[3 * hidden :]
    )
    d_proj = jnp.concatenate([gate_left, value_left, gate_right, value_right], axis=0).astype(
        jnp.bfloat16
    )
    d_normed = jnp.einsum("hrm,ch->rmc", d_proj, w_proj, preferred_element_type=jnp.float32)
    d_normed = d_normed + jnp.einsum(
        "rmd,cd->rmc", d_gate_pre, w_gate, preferred_element_type=jnp.float32
    )
    d_input = d_normed * ln_in_gain
    return norm_backward(d_input, normed, inv_std, -1).astype(jnp.bfloat16)


def solution(mesh):
    fits = mesh.shape["chan"] == 1 and mesh.shape["row"] in (8, 16)
    return jax.shard_map(
        kernel_shards if fits else shards,
        mesh=mesh,
        in_specs=(
            P(("grp", "row"), "chan", None),
            P(("grp", "row"), "chan", None),
            P("grp"),
            P(),
            P(),
            P(),
            P(),
            P(),
            P(),
            P(),
        ),
        out_specs=P(("grp", "row"), "chan", None),
        check_vma=False,
    )
```

```python
import functools

import jax
import jax.numpy as jnp
from jax import lax
from jax.experimental import pallas as pl
from jax.experimental.pallas import tpu as pltpu
from jax.sharding import PartitionSpec as P

F32 = jnp.float32
BF16 = jnp.bfloat16
VMEM_LIMIT = 16 * 1024 * 1024


def dot(lhs, rhs, lhs_dim, rhs_dim):
    return lax.dot_general(
        lhs, rhs, (((lhs_dim,), (rhs_dim,)), ((), ())), preferred_element_type=F32
    )


def transposed(matrix):
    return jnp.transpose(matrix.astype(F32)).astype(BF16)


def sigmoid(values):
    return 1.0 / (1.0 + jnp.exp(-values))


def column(row):
    size = row.shape[1]
    return jnp.transpose(jnp.broadcast_to(row, (size, size)))


def norm_rows(values):
    centered = values - jnp.mean(values, axis=0, keepdims=True)
    variance = jnp.mean(centered * centered, axis=0, keepdims=True)
    inv_std = lax.rsqrt(variance + 1e-05)
    return centered * inv_std, inv_std


def call(
    kernel, name, outs, args, fetched=(), columns={}, unread=(), scratch=(), flops=0, limit=VMEM_LIMIT
):
    moved = sum(a.size * a.dtype.itemsize for a in args) + sum(
        o.size * jnp.dtype(o.dtype).itemsize for o in outs
    )
    n_args, n_outs, n_fetched = len(args), len(outs), len(fetched)

    def body(*refs):
        ins = list(refs[:n_args])
        rest = refs[n_args + n_outs :]
        copies = []
        for n, place in enumerate(fetched):
            source = ins[place].at[:, columns[place]] if place in columns else ins[place]
            copies.append(pltpu.make_async_copy(source, rest[n], rest[n_fetched].at[n]))
            ins[place] = rest[n]
        for copy in copies:
            copy.start()
        for copy in copies:
            copy.wait()
        kernel(*ins, *refs[n_args : n_args + n_outs], *rest[n_fetched + (n_fetched > 0) :])

    buffers = [
        pltpu.VMEM(
            (*args[place].shape[:-1], columns[place].size) if place in columns else args[place].shape,
            args[place].dtype,
        )
        for place in fetched
    ]
    if fetched:
        buffers.append(pltpu.SemaphoreType.DMA((n_fetched,)))
    return pl.pallas_call(
        body,
        name=name,
        out_shape=outs,
        in_specs=[
            pl.BlockSpec(
                memory_space=pltpu.HBM if n in fetched else pl.ANY if n in unread else pltpu.VMEM
            )
            for n in range(n_args)
        ],
        out_specs=[pl.BlockSpec(memory_space=pltpu.VMEM) for _ in outs],
        scratch_shapes=buffers + list(scratch),
        compiler_params=pltpu.CompilerParams(vmem_limit_bytes=limit),
        cost_estimate=pl.CostEstimate(flops=flops, bytes_accessed=moved, transcendentals=0),
    )(*args)


def cell_masks(mask, rows):
    columns = mask[...].astype(F32)
    shape = (rows, columns.shape[1])
    first = lax.axis_index("row") * rows
    own = lax.broadcasted_iota(jnp.int32, shape, 1) == (
        lax.broadcasted_iota(jnp.int32, shape, 0) + first
    )
    row_mask = jnp.sum(jnp.where(own, columns, 0.0), axis=1, keepdims=True)
    cells = row_mask * columns
    return [cells[row : row + 1] for row in range(rows)]


def wide_order(devices, count, back):
    order = []
    for place in range(count):
        if not back:
            order += [count + (place ^ 2), place ^ (count // 2)]
        elif place < count // 2:
            order += [place + count // 2, place + count, place, place + count + count // 2]
    return order


def distance(step, count):
    far = sorted(range(3, count), key=lambda apart: -(apart // 2))
    return [*range(min(3, count)), *far][step]


def partner(step, count):
    return lax.rem(lax.axis_index("row"), count) ^ distance(step, count)


def gated_rows(pair, mask, gain, bias, w_side):
    rows = pair.shape[0]
    hidden = w_side.shape[1] // 2
    w_flip = transposed(w_side[...])
    gain_col, bias_col = column(gain[...]), column(bias[...])
    masks = cell_masks(mask, rows)
    for row in range(rows):
        normed, _ = norm_rows(jnp.transpose(pair[row].astype(F32)))
        zln = (normed * gain_col + bias_col).astype(BF16)
        proj = dot(w_flip, zln, 1, 0)
        yield row, masks[row] * sigmoid(proj[:hidden]) * proj[hidden:]


def project_right_kernel(pair, mask, gain, bias, w_side, right_panel):
    rows = pair.shape[0]
    devices, depth, width = right_panel.shape
    block = depth // rows
    count = w_side.shape[1] // 2 // block
    for row, right in gated_rows(pair, mask, gain, bias, w_side):
        right = right.reshape(count, block, width).astype(BF16)
        for rank in range(devices):
            place = wide_order(devices, count, False)[rank] % count
            right_panel[rank, row * block : (row + 1) * block, :] = right[place]


def project_left_kernel(pair, mask, gain, bias, w_side, after, *refs):
    del after
    *pieces, left_panel = refs
    rows = pair.shape[0]
    count, depth, width = left_panel.shape
    block = depth // rows
    for row, left in gated_rows(pair, mask, gain, bias, w_side):
        left = left.reshape(count, block, width).astype(BF16)
        left_panel[:, row * block : (row + 1) * block, :] = left
    for step, piece in enumerate(pieces):
        piece[...] = left_panel[partner(step, count)]


def prepare_kernel(
    pair, cotangent, gain, bias, w_gate, out_gain, w_out, d_hat_centered, gate_slope
):
    gate_flip = transposed(w_gate[...])
    gain_col, bias_col = column(gain[...]), column(bias[...])
    out_gain_col = column(out_gain[...])
    for row in range(pair.shape[0]):
        normed, _ = norm_rows(jnp.transpose(pair[row].astype(F32)))
        zln = (normed * gain_col + bias_col).astype(BF16)
        gate = sigmoid(dot(gate_flip, zln, 1, 0))
        cot = jnp.transpose(cotangent[row].astype(F32))
        d_scaled = (cot * gate).astype(BF16)
        d_hat = dot(w_out[...], d_scaled, 1, 0) * out_gain_col
        d_hat_centered[row] = d_hat - jnp.mean(d_hat, axis=0, keepdims=True)
        gate_slope[row] = cot * gate * (1.0 - gate)


def spread(panel, wide):
    wide[...] = panel[...].astype(F32).reshape(wide.shape)


def wide_places(panel, count, back):
    devices, depth, _ = panel.shape
    for rank, device in enumerate(wide_order(devices, count, back)):
        yield rank, slice(device * depth, (device + 1) * depth)


def sort_left_kernel(*refs):
    *pieces, left_all, left_pairs, left_wide = refs
    block, left_rows, _ = left_all.shape
    depth = pieces[0].shape[0]
    for step, piece in enumerate(pieces):
        start = pl.multiple_of(partner(step, len(pieces)) * depth, depth)
        left_wide[pl.ds(start, depth), :] = piece[...].astype(F32)
    for h in range(block):
        left_all[h] = left_wide[pl.ds(h, left_rows, stride=block), :].astype(BF16)
    empty = jnp.zeros(left_all.shape[1:], BF16)
    for n in range(block // 2):
        left_pairs[n, :left_rows, :] = jnp.concatenate([left_all[2 * n], empty], axis=1)
        left_pairs[n, left_rows:, :] = jnp.concatenate([empty, left_all[2 * n + 1]], axis=1)


def tri_kernel(right_panel, left_all, after, products, right_all, left_wide, right_wide):
    del after
    block, left_rows, _ = left_all.shape
    right_rows = right_all.shape[1]
    for rank, place in wide_places(right_panel, products.shape[0], False):
        right_wide[place, :] = right_panel[rank].astype(F32)
    for h in range(block):
        right = right_wide[pl.ds(h, right_rows, stride=block), :].astype(BF16)
        right_all[h] = right
        left_wide[pl.ds(h, left_rows, stride=block), :] = dot(left_all[h], right, 1, 1)
    products[...] = left_wide[...].astype(BF16).reshape(products.shape)


def cell_row(ref, row, rows):
    count, depth, width = ref.shape
    block = depth // rows
    return ref[:, row * block : (row + 1) * block, :].astype(F32).reshape(count * block, width)


def middle_kernel(products, d_hat_centered, d_products):
    rows = d_hat_centered.shape[0]
    count, depth, width = products.shape
    block = depth // rows
    for row in range(rows):
        tri_hat, inv_std = norm_rows(cell_row(products, row, rows))
        d_hat = d_hat_centered[row]
        cross = jnp.mean(d_hat * tri_hat, axis=0, keepdims=True)
        d_tri = inv_std * (d_hat - tri_hat * cross)
        d_products[:, row * block : (row + 1) * block, :] = d_tri.reshape(
            count, block, width
        ).astype(BF16)


def d_right_kernel(d_products, left_pairs, d_right_panel, d_tri_all, left_wide, right_wide):
    block, left_rows, width = d_tri_all.shape
    right_rows = right_wide.shape[0] // block
    spread(d_products, left_wide)
    for n in range(block // 2):
        pair = (2 * n, 2 * n + 1)
        d_tri = [left_wide[pl.ds(h, left_rows, stride=block), :] for h in pair]
        d_tri = jnp.concatenate(d_tri, axis=0).astype(BF16)
        d_right = dot(d_tri, left_pairs[n], 0, 0)
        for side, h in enumerate(pair):
            d_tri_all[h] = d_tri[side * left_rows : (side + 1) * left_rows]
            right_wide[pl.ds(h, right_rows, stride=block), :] = d_right[
                :, side * width : (side + 1) * width
            ]
    for rank, place in wide_places(d_right_panel, d_products.shape[0], True):
        d_right_panel[rank] = right_wide[place, :].astype(BF16)


def d_left_kernel(d_tri_all, right_all, *refs):
    *pieces, left_wide = refs
    block, left_rows, _ = d_tri_all.shape
    for h in range(block):
        left_wide[pl.ds(h, left_rows, stride=block), :] = dot(d_tri_all[h], right_all[h], 1, 0)
    depth = pieces[0].shape[0]
    for step, piece in enumerate(pieces):
        start = pl.multiple_of(partner(step, len(pieces)) * depth, depth)
        piece[...] = left_wide[pl.ds(start, depth), :].astype(BF16)


def gate_back_kernel(products, gate_slope, out_gain, out_bias, w_out, d_gate_pre):
    rows = gate_slope.shape[0]
    out_flip = transposed(w_out[...])
    out_gain_col, out_bias_col = column(out_gain[...]), column(out_bias[...])
    for row in range(rows):
        tri_hat, _ = norm_rows(cell_row(products, row, rows))
        scaled = (tri_hat * out_gain_col + out_bias_col).astype(BF16)
        d_gate_pre[row] = (dot(out_flip, scaled, 1, 0) * gate_slope[row]).astype(BF16)


def slopes_kernel(
    pair, mask, gain, bias, w_proj, w_gate, after, slopes, normed_in, inv_in, in_gain, weights
):
    del after
    rows = pair.shape[0]
    hidden = w_proj.shape[1] // 4
    w_flip = transposed(w_proj[...])
    gain_col, bias_col = column(gain[...]), column(bias[...])
    in_gain[...] = gain_col
    weights[...] = jnp.concatenate([w_proj[...], w_gate[...]], axis=1)
    masks = cell_masks(mask, rows)
    for row in range(rows):
        normed, inv_std = norm_rows(jnp.transpose(pair[row].astype(F32)))
        normed_in[row] = normed.astype(normed_in.dtype)
        inv_in[row : row + 1] = inv_std
        zln = (normed * gain_col + bias_col).astype(BF16)
        proj = dot(w_flip, zln, 1, 0)
        for side in range(2):
            base = 2 * side * hidden
            sig = sigmoid(proj[base : base + hidden])
            masked = masks[row] * sig
            value = masked * (1.0 - sig) * proj[base + hidden : base + 2 * hidden]
            slopes[row, base : base + hidden, :] = value.astype(slopes.dtype)
            slopes[row, base + hidden : base + 2 * hidden, :] = masked.astype(slopes.dtype)


def sort_d_left_kernel(*refs):
    *pieces, d_left_panel = refs
    for step, piece in enumerate(pieces):
        d_left_panel[partner(step, len(pieces))] = piece[...]


def both_halves(blocks, count):
    order = wide_order(2 * count, count, True)
    return jnp.stack(
        [blocks[order.index(place)] + blocks[order.index(count + place)] for place in range(count)]
    )


def finish_kernel(
    d_right_panel, d_left_panel, slopes, d_gate_pre, normed_in, inv_in, gain_col, weights, grad
):
    rows = grad.shape[0]
    count, depth, width = d_left_panel.shape
    hidden = count * depth // rows
    for row in range(rows):
        d_right = cell_row(d_right_panel, row, rows)
        d_right = both_halves(d_right.reshape(2 * count, depth // rows, width), count)
        parts = []
        for side, d_value in enumerate((cell_row(d_left_panel, row, rows), d_right.reshape(hidden, width))):
            for base in (2 * side * hidden, (2 * side + 1) * hidden):
                slope = slopes[row, base : base + hidden, :].astype(F32)
                parts.append((d_value * slope).astype(BF16))
        parts.append(d_gate_pre[row])
        d_in = dot(weights[...], jnp.concatenate(parts, axis=0), 1, 0) * gain_col[...]
        normed = normed_in[row].astype(F32)
        mean_grad = jnp.mean(d_in, axis=0, keepdims=True)
        mean_cross = jnp.mean(d_in * normed, axis=0, keepdims=True)
        result = inv_in[row : row + 1] * (d_in - mean_grad - normed * mean_cross)
        grad[row] = jnp.transpose(result).astype(BF16)


def swap(values, count, back):
    groups = [wide_order(lax.axis_size("row"), count, back)]
    return lax.all_to_all(
        values, "row", split_axis=0, concat_axis=0, tiled=True, axis_index_groups=groups
    )


def swap_half(values, count):
    devices = range(lax.axis_size("row"))
    groups = [[d for d in devices if d // count == half] for half in range(len(devices) // count)]
    return lax.all_to_all(
        values, "row", split_axis=0, concat_axis=0, tiled=True, axis_index_groups=groups
    )


def swap_pieces(pieces):
    devices = range(lax.axis_size("row"))
    count = len(pieces)
    return [pieces[0]] + [
        lax.ppermute(pieces[step], "row", [(d, d ^ distance(step, count)) for d in devices])
        for step in range(1, count)
    ]


def kernel_shards(
    pair,
    cotangent,
    residue_mask,
    ln_in_gain,
    ln_in_bias,
    w_proj,
    w_gate,
    ln_out_gain,
    ln_out_bias,
    w_out,
):
    rows, width, channels = pair.shape
    hidden = w_out.shape[0]
    halves = 2
    devices = lax.axis_size("row")
    count = devices // halves
    block = hidden // count
    left_rows, right_rows = rows * count, rows * devices
    shape = jax.ShapeDtypeStruct
    panel = shape((count, rows * block, width), BF16)
    wide_panel = shape((devices, rows * block, width), BF16)
    mask = residue_mask.reshape(1, width)
    gain, bias = ln_in_gain.reshape(1, channels), ln_in_bias.reshape(1, channels)
    out_gain, out_bias = ln_out_gain.reshape(1, hidden), ln_out_bias.reshape(1, hidden)
    cells = rows * width
    piece = shape((rows * block, width), BF16)
    left_panel = pltpu.VMEM(panel.shape, BF16)
    left_wide = pltpu.VMEM((left_rows * block, width), F32)
    right_wide = pltpu.VMEM((right_rows * block, width), F32)
    (own_right,) = call(
        project_right_kernel,
        "project_right",
        [wide_panel],
        [pair, mask, gain, bias, w_proj],
        fetched=range(5),
        columns={4: pl.ds(2 * hidden, 2 * hidden)},
        flops=2 * cells * channels * 2 * hidden,
        limit=64 * 1024 * 1024 - 640 * 1024,
    )
    right_panel = swap(own_right, count, False)
    pieces = call(
        project_left_kernel,
        "project_left",
        [piece] * count,
        [pair, mask, gain, bias, w_proj, own_right],
        fetched=range(5),
        columns={4: pl.ds(0, 2 * hidden)},
        unread=(5,),
        scratch=[left_panel],
        flops=2 * cells * channels * 2 * hidden,
    )
    pieces = swap_pieces(pieces)
    left_all, left_pairs = call(
        sort_left_kernel,
        "sort_left",
        [
            shape((block, left_rows, width), BF16),
            shape((block // 2, 2 * left_rows, 2 * width), BF16),
        ],
        pieces,
        scratch=[left_wide],
    )
    d_hat_centered, gate_slope = call(
        prepare_kernel,
        "prepare",
        [shape((rows, hidden, width), F32), shape((rows, channels, width), F32)],
        [pair, cotangent, gain, bias, w_gate, out_gain, w_out],
        fetched=range(7),
        flops=2 * cells * channels * 2 * hidden,
    )
    products, right_all = call(
        tri_kernel,
        "tri",
        [panel, shape((block, right_rows, width), BF16)],
        [right_panel, left_all, d_hat_centered],
        unread=(2,),
        scratch=[left_wide, right_wide],
        flops=2 * block * left_rows * width * right_rows,
    )
    products = swap_half(products, count)
    (d_products,) = call(
        middle_kernel,
        "middle",
        [panel],
        [products, d_hat_centered],
        flops=20 * cells * hidden,
    )
    d_products = swap_half(d_products, count)
    d_right_panel, d_tri_all = call(
        d_right_kernel,
        "d_right",
        [wide_panel, shape((block, left_rows, width), BF16)],
        [d_products, left_pairs],
        scratch=[left_wide, right_wide],
        flops=2 * block * left_rows * width * right_rows,
    )
    d_right_panel = swap(d_right_panel, count, True)
    d_pieces = call(
        d_left_kernel,
        "d_left",
        [piece] * count,
        [d_tri_all, right_all],
        scratch=[left_wide],
        flops=2 * block * left_rows * width * right_rows,
    )
    d_pieces = swap_pieces(d_pieces)
    (d_left_panel,) = call(sort_d_left_kernel, "sort_d_left", [panel], d_pieces)
    (d_gate_pre,) = call(
        gate_back_kernel,
        "gate_back",
        [shape((rows, channels, width), BF16)],
        [products, gate_slope, out_gain, out_bias, w_out],
        fetched=range(2, 5),
        flops=2 * cells * channels * hidden,
    )
    slopes, normed_in, inv_in, gain_col, weights = call(
        slopes_kernel,
        "slopes",
        [
            shape((rows, 4 * hidden, width), BF16),
            shape((rows, channels, width), BF16),
            shape((rows, width), F32),
            shape((channels, channels), F32),
            shape((channels, 4 * hidden + channels), BF16),
        ],
        [pair, mask, gain, bias, w_proj, w_gate, d_gate_pre],
        fetched=range(6),
        unread=(6,),
        flops=2 * cells * channels * 4 * hidden,
    )
    (grad,) = call(
        finish_kernel,
        "finish",
        [shape(pair.shape, BF16)],
        [
            d_right_panel,
            d_left_panel,
            slopes,
            d_gate_pre,
            normed_in,
            inv_in,
            gain_col,
            weights,
        ],
        flops=2 * cells * channels * 4 * hidden,
    )
    return grad


def normalize(values, reduce_axis):
    mean_value = jnp.mean(values, axis=reduce_axis, keepdims=True)
    centered = values - mean_value
    variance = jnp.mean(centered * centered, axis=reduce_axis, keepdims=True)
    inv_std = lax.rsqrt(variance + 1e-05)
    return (centered * inv_std, inv_std)


def norm_backward(upstream, normed, inv_std, reduce_axis):
    mean_grad = jnp.mean(upstream, axis=reduce_axis, keepdims=True)
    mean_cross = jnp.mean(upstream * normed, axis=reduce_axis, keepdims=True)
    return inv_std * (upstream - mean_grad - normed * mean_cross)


def shards(
    pair,
    cotangent,
    residue_mask,
    ln_in_gain,
    ln_in_bias,
    w_proj,
    w_gate,
    ln_out_gain,
    ln_out_bias,
    w_out,
):
    local_rows = pair.shape[0]
    local_cols = pair.shape[1]
    hidden = w_out.shape[0]
    chan_index = lax.axis_index("chan")
    row_start = lax.axis_index("row") * local_rows
    col_start = chan_index * local_cols
    mask_float = residue_mask.astype(jnp.float32)
    row_mask = lax.dynamic_slice_in_dim(mask_float, row_start, local_rows)
    col_mask = lax.dynamic_slice_in_dim(mask_float, col_start, local_cols)
    cell_mask = (row_mask[:, None] * col_mask[None, :])[None]
    normed, inv_std = normalize(pair.astype(jnp.float32), -1)
    normed_pair = (normed * ln_in_gain + ln_in_bias).astype(jnp.bfloat16)
    projected = jnp.einsum("rmc,ch->hrm", normed_pair, w_proj, preferred_element_type=jnp.float32)
    left_panel = (
        cell_mask * jax.nn.sigmoid(projected[:hidden]) * projected[hidden : 2 * hidden]
    ).astype(jnp.bfloat16)
    right_panel = (
        cell_mask * jax.nn.sigmoid(projected[2 * hidden : 3 * hidden]) * projected[3 * hidden :]
    ).astype(jnp.bfloat16)
    panels = lax.all_to_all(
        jnp.stack([left_panel, right_panel]), "row", split_axis=1, concat_axis=2, tiled=True
    )
    left_all = panels[0]
    right_all = panels[1]
    right_rows = lax.all_to_all(right_all, "chan", split_axis=1, concat_axis=2, tiled=True)
    partner = right_rows
    tri_part = jnp.einsum(
        "gik,gjk->gij",
        lax.all_gather(left_all, "chan", axis=2, tiled=True),
        partner,
        preferred_element_type=jnp.float32,
    ).astype(jnp.bfloat16)
    tri_cells = lax.all_to_all(tri_part, "row", split_axis=1, concat_axis=0, tiled=True)
    tri_hat, inv_tri = normalize(tri_cells.astype(jnp.float32), 0)
    scaled = (tri_hat * ln_out_gain[:, None, None] + ln_out_bias[:, None, None]).astype(
        jnp.bfloat16
    )
    proj_out = jnp.einsum("hrm,hc->rmc", scaled, w_out, preferred_element_type=jnp.float32)
    gate_value = jax.nn.sigmoid(
        jnp.einsum("rmc,cd->rmd", normed_pair, w_gate, preferred_element_type=jnp.float32)
    )
    cot_float = cotangent.astype(jnp.float32)
    d_gate_pre = (cot_float * proj_out * gate_value * (1.0 - gate_value)).astype(jnp.bfloat16)
    d_scaled = (cot_float * gate_value).astype(jnp.bfloat16)
    d_hat = jnp.einsum("rmc,hc->hrm", d_scaled, w_out, preferred_element_type=jnp.float32)
    d_hat = d_hat * ln_out_gain[:, None, None]
    d_tri = norm_backward(d_hat, tri_hat, inv_tri, 0).astype(jnp.bfloat16)
    d_tri_all = lax.all_to_all(d_tri, "row", split_axis=0, concat_axis=1, tiled=True)
    panel_piece = lax.all_gather(d_tri_all, "chan", axis=2, tiled=True)
    partner = right_all
    d_left = jnp.einsum("gij,gjk->gik", panel_piece, partner, preferred_element_type=jnp.float32)
    contribution = jnp.einsum(
        "gij,gik->gjk", panel_piece, left_all, preferred_element_type=jnp.float32
    )
    d_right = contribution
    d_left, d_right = (d_left, d_right)
    d_stack = jnp.stack([d_left, d_right]).astype(jnp.bfloat16)
    d_panels = lax.all_to_all(d_stack, "row", split_axis=2, concat_axis=1, tiled=True)

    def gating(d_value, gate_proj, value_proj):
        sigmoid_val = jax.nn.sigmoid(gate_proj)
        masked_grad = d_value.astype(jnp.float32) * cell_mask
        return (
            masked_grad * value_proj * sigmoid_val * (1.0 - sigmoid_val),
            masked_grad * sigmoid_val,
        )

    gate_left, value_left = gating(d_panels[0], projected[:hidden], projected[hidden : 2 * hidden])
    gate_right, value_right = gating(
        d_panels[1], projected[2 * hidden : 3 * hidden], projected[3 * hidden :]
    )
    d_proj = jnp.concatenate([gate_left, value_left, gate_right, value_right], axis=0).astype(
        jnp.bfloat16
    )
    d_normed = jnp.einsum("hrm,ch->rmc", d_proj, w_proj, preferred_element_type=jnp.float32)
    d_normed = d_normed + jnp.einsum(
        "rmd,cd->rmc", d_gate_pre, w_gate, preferred_element_type=jnp.float32
    )
    d_input = d_normed * ln_in_gain
    return norm_backward(d_input, normed, inv_std, -1).astype(jnp.bfloat16)


def solution(mesh):
    fits = mesh.shape["chan"] == 1 and mesh.shape["row"] in (8, 16)
    return jax.shard_map(
        kernel_shards if fits else shards,
        mesh=mesh,
        in_specs=(
            P(("grp", "row"), "chan", None),
            P(("grp", "row"), "chan", None),
            P("grp"),
            P(),
            P(),
            P(),
            P(),
            P(),
            P(),
            P(),
        ),
        out_specs=P(("grp", "row"), "chan", None),
        check_vma=False,
    )
```

```python
import functools

import jax
import jax.numpy as jnp
from jax import lax
from jax.experimental import pallas as pl
from jax.experimental.pallas import tpu as pltpu
from jax.sharding import PartitionSpec as P

F32 = jnp.float32
BF16 = jnp.bfloat16
VMEM_LIMIT = 16 * 1024 * 1024


def dot(lhs, rhs, lhs_dim, rhs_dim):
    return lax.dot_general(
        lhs, rhs, (((lhs_dim,), (rhs_dim,)), ((), ())), preferred_element_type=F32
    )


def transposed(matrix):
    return jnp.transpose(matrix.astype(F32)).astype(BF16)


def sigmoid(values):
    return 1.0 / (1.0 + jnp.exp(-values))


def column(row):
    size = row.shape[1]
    return jnp.transpose(jnp.broadcast_to(row, (size, size)))


def norm_rows(values):
    centered = values - jnp.mean(values, axis=0, keepdims=True)
    variance = jnp.mean(centered * centered, axis=0, keepdims=True)
    inv_std = lax.rsqrt(variance + 1e-05)
    return centered * inv_std, inv_std


def call(
    kernel, name, outs, args, fetched=(), columns={}, unread=(), scratch=(), flops=0, limit=VMEM_LIMIT
):
    moved = sum(a.size * a.dtype.itemsize for a in args) + sum(
        o.size * jnp.dtype(o.dtype).itemsize for o in outs
    )
    n_args, n_outs, n_fetched = len(args), len(outs), len(fetched)

    def body(*refs):
        ins = list(refs[:n_args])
        rest = refs[n_args + n_outs :]
        copies = []
        for n, place in enumerate(fetched):
            source = ins[place].at[:, columns[place]] if place in columns else ins[place]
            copies.append(pltpu.make_async_copy(source, rest[n], rest[n_fetched].at[n]))
            ins[place] = rest[n]
        for copy in copies:
            copy.start()
        for copy in copies:
            copy.wait()
        kernel(*ins, *refs[n_args : n_args + n_outs], *rest[n_fetched + (n_fetched > 0) :])

    buffers = [
        pltpu.VMEM(
            (*args[place].shape[:-1], columns[place].size) if place in columns else args[place].shape,
            args[place].dtype,
        )
        for place in fetched
    ]
    if fetched:
        buffers.append(pltpu.SemaphoreType.DMA((n_fetched,)))
    return pl.pallas_call(
        body,
        name=name,
        out_shape=outs,
        in_specs=[
            pl.BlockSpec(
                memory_space=pltpu.HBM if n in fetched else pl.ANY if n in unread else pltpu.VMEM
            )
            for n in range(n_args)
        ],
        out_specs=[pl.BlockSpec(memory_space=pltpu.VMEM) for _ in outs],
        scratch_shapes=buffers + list(scratch),
        compiler_params=pltpu.CompilerParams(vmem_limit_bytes=limit),
        cost_estimate=pl.CostEstimate(flops=flops, bytes_accessed=moved, transcendentals=0),
    )(*args)


def cell_masks(mask, rows):
    columns = mask[...].astype(F32)
    shape = (rows, columns.shape[1])
    first = lax.axis_index("row") * rows
    own = lax.broadcasted_iota(jnp.int32, shape, 1) == (
        lax.broadcasted_iota(jnp.int32, shape, 0) + first
    )
    row_mask = jnp.sum(jnp.where(own, columns, 0.0), axis=1, keepdims=True)
    cells = row_mask * columns
    return [cells[row : row + 1] for row in range(rows)]


def wide_order(devices, count, back):
    order = []
    for place in range(count):
        if back:
            order += [place ^ (count // 2), count + place]
        else:
            order += [count + (place ^ 2), place ^ (count // 2) ^ 2]
    return order


def distance(step, count):
    far = sorted(range(3, count), key=lambda apart: -(apart // 2))
    return [*range(min(3, count)), *far][step]


def partner(step, count):
    return lax.rem(lax.axis_index("row"), count) ^ distance(step, count)


def gated_rows(pair, mask, gain, bias, w_side):
    rows = pair.shape[0]
    hidden = w_side.shape[1] // 2
    w_flip = transposed(w_side[...])
    gain_col, bias_col = column(gain[...]), column(bias[...])
    masks = cell_masks(mask, rows)
    for row in range(rows):
        normed, _ = norm_rows(jnp.transpose(pair[row].astype(F32)))
        zln = (normed * gain_col + bias_col).astype(BF16)
        proj = dot(w_flip, zln, 1, 0)
        yield row, masks[row] * sigmoid(proj[:hidden]) * proj[hidden:]


def project_right_kernel(pair, mask, gain, bias, w_side, right_panel):
    rows = pair.shape[0]
    devices, depth, width = right_panel.shape
    block = depth // rows
    count = w_side.shape[1] // 2 // block
    for row, right in gated_rows(pair, mask, gain, bias, w_side):
        right = right.reshape(count, block, width).astype(BF16)
        for rank in range(devices):
            place = wide_order(devices, count, False)[rank] % count
            right_panel[rank, row * block : (row + 1) * block, :] = right[place]


def project_left_kernel(pair, mask, gain, bias, w_side, after, *refs):
    del after
    *pieces, left_panel = refs
    rows = pair.shape[0]
    count, depth, width = left_panel.shape
    block = depth // rows
    for row, left in gated_rows(pair, mask, gain, bias, w_side):
        left = left.reshape(count, block, width).astype(BF16)
        left_panel[:, row * block : (row + 1) * block, :] = left
    for step, piece in enumerate(pieces):
        piece[...] = left_panel[partner(step, count)]


def prepare_kernel(
    pair, cotangent, gain, bias, w_gate, out_gain, w_out, d_hat_centered, gate_slope
):
    gate_flip = transposed(w_gate[...])
    gain_col, bias_col = column(gain[...]), column(bias[...])
    out_gain_col = column(out_gain[...])
    for row in range(pair.shape[0]):
        normed, _ = norm_rows(jnp.transpose(pair[row].astype(F32)))
        zln = (normed * gain_col + bias_col).astype(BF16)
        gate = sigmoid(dot(gate_flip, zln, 1, 0))
        cot = jnp.transpose(cotangent[row].astype(F32))
        d_scaled = (cot * gate).astype(BF16)
        d_hat = dot(w_out[...], d_scaled, 1, 0) * out_gain_col
        d_hat_centered[row] = d_hat - jnp.mean(d_hat, axis=0, keepdims=True)
        gate_slope[row] = cot * gate * (1.0 - gate)


def spread(panel, wide):
    wide[...] = panel[...].astype(F32).reshape(wide.shape)


def wide_places(panel, count, back):
    devices, depth, _ = panel.shape
    for rank, device in enumerate(wide_order(devices, count, back)):
        yield rank, slice(device * depth, (device + 1) * depth)


def sort_left_kernel(*refs):
    *pieces, left_all, left_pairs, left_wide = refs
    block, left_rows, _ = left_all.shape
    depth = pieces[0].shape[0]
    for step, piece in enumerate(pieces):
        start = pl.multiple_of(partner(step, len(pieces)) * depth, depth)
        left_wide[pl.ds(start, depth), :] = piece[...].astype(F32)
    for h in range(block):
        left_all[h] = left_wide[pl.ds(h, left_rows, stride=block), :].astype(BF16)
    empty = jnp.zeros(left_all.shape[1:], BF16)
    for n in range(block // 2):
        left_pairs[n, :left_rows, :] = jnp.concatenate([left_all[2 * n], empty], axis=1)
        left_pairs[n, left_rows:, :] = jnp.concatenate([empty, left_all[2 * n + 1]], axis=1)


def tri_kernel(right_panel, left_all, after, products, right_all, left_wide, right_wide):
    del after
    block, left_rows, _ = left_all.shape
    right_rows = right_all.shape[1]
    for rank, place in wide_places(right_panel, products.shape[0], False):
        right_wide[place, :] = right_panel[rank].astype(F32)
    for h in range(block):
        right = right_wide[pl.ds(h, right_rows, stride=block), :].astype(BF16)
        right_all[h] = right
        left_wide[pl.ds(h, left_rows, stride=block), :] = dot(left_all[h], right, 1, 1)
    products[...] = left_wide[...].astype(BF16).reshape(products.shape)


def cell_row(ref, row, rows):
    count, depth, width = ref.shape
    block = depth // rows
    return ref[:, row * block : (row + 1) * block, :].astype(F32).reshape(count * block, width)


def middle_kernel(products, d_hat_centered, d_products):
    rows = d_hat_centered.shape[0]
    count, depth, width = products.shape
    block = depth // rows
    for row in range(rows):
        tri_hat, inv_std = norm_rows(cell_row(products, row, rows))
        d_hat = d_hat_centered[row]
        cross = jnp.mean(d_hat * tri_hat, axis=0, keepdims=True)
        d_tri = inv_std * (d_hat - tri_hat * cross)
        d_products[:, row * block : (row + 1) * block, :] = d_tri.reshape(
            count, block, width
        ).astype(BF16)


def d_right_kernel(d_products, left_pairs, d_right_panel, d_tri_all, left_wide, right_wide):
    block, left_rows, width = d_tri_all.shape
    right_rows = right_wide.shape[0] // block
    spread(d_products, left_wide)
    for n in range(block // 2):
        pair = (2 * n, 2 * n + 1)
        d_tri = [left_wide[pl.ds(h, left_rows, stride=block), :] for h in pair]
        d_tri = jnp.concatenate(d_tri, axis=0).astype(BF16)
        d_right = dot(d_tri, left_pairs[n], 0, 0)
        for side, h in enumerate(pair):
            d_tri_all[h] = d_tri[side * left_rows : (side + 1) * left_rows]
            right_wide[pl.ds(h, right_rows, stride=block), :] = d_right[
                :, side * width : (side + 1) * width
            ]
    for rank, place in wide_places(d_right_panel, d_products.shape[0], True):
        d_right_panel[rank] = right_wide[place, :].astype(BF16)


def d_left_kernel(d_tri_all, right_all, *refs):
    *pieces, left_wide = refs
    block, left_rows, _ = d_tri_all.shape
    for h in range(block):
        left_wide[pl.ds(h, left_rows, stride=block), :] = dot(d_tri_all[h], right_all[h], 1, 0)
    depth = pieces[0].shape[0]
    for step, piece in enumerate(pieces):
        start = pl.multiple_of(partner(step, len(pieces)) * depth, depth)
        piece[...] = left_wide[pl.ds(start, depth), :].astype(BF16)


def gate_back_kernel(products, gate_slope, out_gain, out_bias, w_out, d_gate_pre):
    rows = gate_slope.shape[0]
    out_flip = transposed(w_out[...])
    out_gain_col, out_bias_col = column(out_gain[...]), column(out_bias[...])
    for row in range(rows):
        tri_hat, _ = norm_rows(cell_row(products, row, rows))
        scaled = (tri_hat * out_gain_col + out_bias_col).astype(BF16)
        d_gate_pre[row] = (dot(out_flip, scaled, 1, 0) * gate_slope[row]).astype(BF16)


def slopes_kernel(
    pair, mask, gain, bias, w_proj, w_gate, after, slopes, normed_in, inv_in, in_gain, weights
):
    del after
    rows = pair.shape[0]
    hidden = w_proj.shape[1] // 4
    w_flip = transposed(w_proj[...])
    gain_col, bias_col = column(gain[...]), column(bias[...])
    in_gain[...] = gain_col
    weights[...] = jnp.concatenate([w_proj[...], w_gate[...]], axis=1)
    masks = cell_masks(mask, rows)
    for row in range(rows):
        normed, inv_std = norm_rows(jnp.transpose(pair[row].astype(F32)))
        normed_in[row] = normed.astype(normed_in.dtype)
        inv_in[row : row + 1] = inv_std
        zln = (normed * gain_col + bias_col).astype(BF16)
        proj = dot(w_flip, zln, 1, 0)
        for side in range(2):
            base = 2 * side * hidden
            sig = sigmoid(proj[base : base + hidden])
            masked = masks[row] * sig
            value = masked * (1.0 - sig) * proj[base + hidden : base + 2 * hidden]
            slopes[row, base : base + hidden, :] = value.astype(slopes.dtype)
            slopes[row, base + hidden : base + 2 * hidden, :] = masked.astype(slopes.dtype)


def sort_d_left_kernel(*refs):
    *pieces, d_left_panel = refs
    for step, piece in enumerate(pieces):
        d_left_panel[partner(step, len(pieces))] = piece[...]


def both_halves(blocks, count):
    order = wide_order(2 * count, count, True)
    return jnp.stack(
        [blocks[order.index(place)] + blocks[order.index(count + place)] for place in range(count)]
    )


def finish_kernel(
    d_right_panel, d_left_panel, slopes, d_gate_pre, normed_in, inv_in, gain_col, weights, grad
):
    rows = grad.shape[0]
    count, depth, width = d_left_panel.shape
    hidden = count * depth // rows
    for row in range(rows):
        d_right = cell_row(d_right_panel, row, rows)
        d_right = both_halves(d_right.reshape(2 * count, depth // rows, width), count)
        parts = []
        for side, d_value in enumerate((cell_row(d_left_panel, row, rows), d_right.reshape(hidden, width))):
            for base in (2 * side * hidden, (2 * side + 1) * hidden):
                slope = slopes[row, base : base + hidden, :].astype(F32)
                parts.append((d_value * slope).astype(BF16))
        parts.append(d_gate_pre[row])
        d_in = dot(weights[...], jnp.concatenate(parts, axis=0), 1, 0) * gain_col[...]
        normed = normed_in[row].astype(F32)
        mean_grad = jnp.mean(d_in, axis=0, keepdims=True)
        mean_cross = jnp.mean(d_in * normed, axis=0, keepdims=True)
        result = inv_in[row : row + 1] * (d_in - mean_grad - normed * mean_cross)
        grad[row] = jnp.transpose(result).astype(BF16)


def swap(values, count, back):
    groups = [wide_order(lax.axis_size("row"), count, back)]
    return lax.all_to_all(
        values, "row", split_axis=0, concat_axis=0, tiled=True, axis_index_groups=groups
    )


def swap_half(values, count):
    devices = range(lax.axis_size("row"))
    groups = [[d for d in devices if d // count == half] for half in range(len(devices) // count)]
    return lax.all_to_all(
        values, "row", split_axis=0, concat_axis=0, tiled=True, axis_index_groups=groups
    )


def swap_pieces(pieces):
    devices = range(lax.axis_size("row"))
    count = len(pieces)
    return [pieces[0]] + [
        lax.ppermute(pieces[step], "row", [(d, d ^ distance(step, count)) for d in devices])
        for step in range(1, count)
    ]


def kernel_shards(
    pair,
    cotangent,
    residue_mask,
    ln_in_gain,
    ln_in_bias,
    w_proj,
    w_gate,
    ln_out_gain,
    ln_out_bias,
    w_out,
):
    rows, width, channels = pair.shape
    hidden = w_out.shape[0]
    halves = 2
    devices = lax.axis_size("row")
    count = devices // halves
    block = hidden // count
    left_rows, right_rows = rows * count, rows * devices
    shape = jax.ShapeDtypeStruct
    panel = shape((count, rows * block, width), BF16)
    wide_panel = shape((devices, rows * block, width), BF16)
    mask = residue_mask.reshape(1, width)
    gain, bias = ln_in_gain.reshape(1, channels), ln_in_bias.reshape(1, channels)
    out_gain, out_bias = ln_out_gain.reshape(1, hidden), ln_out_bias.reshape(1, hidden)
    cells = rows * width
    piece = shape((rows * block, width), BF16)
    left_panel = pltpu.VMEM(panel.shape, BF16)
    left_wide = pltpu.VMEM((left_rows * block, width), F32)
    right_wide = pltpu.VMEM((right_rows * block, width), F32)
    (own_right,) = call(
        project_right_kernel,
        "project_right",
        [wide_panel],
        [pair, mask, gain, bias, w_proj],
        fetched=range(5),
        columns={4: pl.ds(2 * hidden, 2 * hidden)},
        flops=2 * cells * channels * 2 * hidden,
        limit=64 * 1024 * 1024 - 640 * 1024,
    )
    right_panel = swap(own_right, count, False)
    pieces = call(
        project_left_kernel,
        "project_left",
        [piece] * count,
        [pair, mask, gain, bias, w_proj, own_right],
        fetched=range(5),
        columns={4: pl.ds(0, 2 * hidden)},
        unread=(5,),
        scratch=[left_panel],
        flops=2 * cells * channels * 2 * hidden,
    )
    pieces = swap_pieces(pieces)
    left_all, left_pairs = call(
        sort_left_kernel,
        "sort_left",
        [
            shape((block, left_rows, width), BF16),
            shape((block // 2, 2 * left_rows, 2 * width), BF16),
        ],
        pieces,
        scratch=[left_wide],
    )
    d_hat_centered, gate_slope = call(
        prepare_kernel,
        "prepare",
        [shape((rows, hidden, width), F32), shape((rows, channels, width), F32)],
        [pair, cotangent, gain, bias, w_gate, out_gain, w_out],
        fetched=range(7),
        flops=2 * cells * channels * 2 * hidden,
    )
    products, right_all = call(
        tri_kernel,
        "tri",
        [panel, shape((block, right_rows, width), BF16)],
        [right_panel, left_all, d_hat_centered],
        unread=(2,),
        scratch=[left_wide, right_wide],
        flops=2 * block * left_rows * width * right_rows,
    )
    products = swap_half(products, count)
    (d_products,) = call(
        middle_kernel,
        "middle",
        [panel],
        [products, d_hat_centered],
        flops=20 * cells * hidden,
    )
    d_products = swap_half(d_products, count)
    d_right_panel, d_tri_all = call(
        d_right_kernel,
        "d_right",
        [wide_panel, shape((block, left_rows, width), BF16)],
        [d_products, left_pairs],
        scratch=[left_wide, right_wide],
        flops=2 * block * left_rows * width * right_rows,
    )
    d_right_panel = swap(d_right_panel, count, True)
    d_pieces = call(
        d_left_kernel,
        "d_left",
        [piece] * count,
        [d_tri_all, right_all],
        scratch=[left_wide],
        flops=2 * block * left_rows * width * right_rows,
    )
    d_pieces = swap_pieces(d_pieces)
    (d_left_panel,) = call(sort_d_left_kernel, "sort_d_left", [panel], d_pieces)
    (d_gate_pre,) = call(
        gate_back_kernel,
        "gate_back",
        [shape((rows, channels, width), BF16)],
        [products, gate_slope, out_gain, out_bias, w_out],
        fetched=range(2, 5),
        flops=2 * cells * channels * hidden,
    )
    slopes, normed_in, inv_in, gain_col, weights = call(
        slopes_kernel,
        "slopes",
        [
            shape((rows, 4 * hidden, width), BF16),
            shape((rows, channels, width), BF16),
            shape((rows, width), F32),
            shape((channels, channels), F32),
            shape((channels, 4 * hidden + channels), BF16),
        ],
        [pair, mask, gain, bias, w_proj, w_gate, d_gate_pre],
        fetched=range(6),
        unread=(6,),
        flops=2 * cells * channels * 4 * hidden,
    )
    (grad,) = call(
        finish_kernel,
        "finish",
        [shape(pair.shape, BF16)],
        [
            d_right_panel,
            d_left_panel,
            slopes,
            d_gate_pre,
            normed_in,
            inv_in,
            gain_col,
            weights,
        ],
        flops=2 * cells * channels * 4 * hidden,
    )
    return grad


def normalize(values, reduce_axis):
    mean_value = jnp.mean(values, axis=reduce_axis, keepdims=True)
    centered = values - mean_value
    variance = jnp.mean(centered * centered, axis=reduce_axis, keepdims=True)
    inv_std = lax.rsqrt(variance + 1e-05)
    return (centered * inv_std, inv_std)


def norm_backward(upstream, normed, inv_std, reduce_axis):
    mean_grad = jnp.mean(upstream, axis=reduce_axis, keepdims=True)
    mean_cross = jnp.mean(upstream * normed, axis=reduce_axis, keepdims=True)
    return inv_std * (upstream - mean_grad - normed * mean_cross)


def shards(
    pair,
    cotangent,
    residue_mask,
    ln_in_gain,
    ln_in_bias,
    w_proj,
    w_gate,
    ln_out_gain,
    ln_out_bias,
    w_out,
):
    local_rows = pair.shape[0]
    local_cols = pair.shape[1]
    hidden = w_out.shape[0]
    chan_index = lax.axis_index("chan")
    row_start = lax.axis_index("row") * local_rows
    col_start = chan_index * local_cols
    mask_float = residue_mask.astype(jnp.float32)
    row_mask = lax.dynamic_slice_in_dim(mask_float, row_start, local_rows)
    col_mask = lax.dynamic_slice_in_dim(mask_float, col_start, local_cols)
    cell_mask = (row_mask[:, None] * col_mask[None, :])[None]
    normed, inv_std = normalize(pair.astype(jnp.float32), -1)
    normed_pair = (normed * ln_in_gain + ln_in_bias).astype(jnp.bfloat16)
    projected = jnp.einsum("rmc,ch->hrm", normed_pair, w_proj, preferred_element_type=jnp.float32)
    left_panel = (
        cell_mask * jax.nn.sigmoid(projected[:hidden]) * projected[hidden : 2 * hidden]
    ).astype(jnp.bfloat16)
    right_panel = (
        cell_mask * jax.nn.sigmoid(projected[2 * hidden : 3 * hidden]) * projected[3 * hidden :]
    ).astype(jnp.bfloat16)
    panels = lax.all_to_all(
        jnp.stack([left_panel, right_panel]), "row", split_axis=1, concat_axis=2, tiled=True
    )
    left_all = panels[0]
    right_all = panels[1]
    right_rows = lax.all_to_all(right_all, "chan", split_axis=1, concat_axis=2, tiled=True)
    partner = right_rows
    tri_part = jnp.einsum(
        "gik,gjk->gij",
        lax.all_gather(left_all, "chan", axis=2, tiled=True),
        partner,
        preferred_element_type=jnp.float32,
    ).astype(jnp.bfloat16)
    tri_cells = lax.all_to_all(tri_part, "row", split_axis=1, concat_axis=0, tiled=True)
    tri_hat, inv_tri = normalize(tri_cells.astype(jnp.float32), 0)
    scaled = (tri_hat * ln_out_gain[:, None, None] + ln_out_bias[:, None, None]).astype(
        jnp.bfloat16
    )
    proj_out = jnp.einsum("hrm,hc->rmc", scaled, w_out, preferred_element_type=jnp.float32)
    gate_value = jax.nn.sigmoid(
        jnp.einsum("rmc,cd->rmd", normed_pair, w_gate, preferred_element_type=jnp.float32)
    )
    cot_float = cotangent.astype(jnp.float32)
    d_gate_pre = (cot_float * proj_out * gate_value * (1.0 - gate_value)).astype(jnp.bfloat16)
    d_scaled = (cot_float * gate_value).astype(jnp.bfloat16)
    d_hat = jnp.einsum("rmc,hc->hrm", d_scaled, w_out, preferred_element_type=jnp.float32)
    d_hat = d_hat * ln_out_gain[:, None, None]
    d_tri = norm_backward(d_hat, tri_hat, inv_tri, 0).astype(jnp.bfloat16)
    d_tri_all = lax.all_to_all(d_tri, "row", split_axis=0, concat_axis=1, tiled=True)
    panel_piece = lax.all_gather(d_tri_all, "chan", axis=2, tiled=True)
    partner = right_all
    d_left = jnp.einsum("gij,gjk->gik", panel_piece, partner, preferred_element_type=jnp.float32)
    contribution = jnp.einsum(
        "gij,gik->gjk", panel_piece, left_all, preferred_element_type=jnp.float32
    )
    d_right = contribution
    d_left, d_right = (d_left, d_right)
    d_stack = jnp.stack([d_left, d_right]).astype(jnp.bfloat16)
    d_panels = lax.all_to_all(d_stack, "row", split_axis=2, concat_axis=1, tiled=True)

    def gating(d_value, gate_proj, value_proj):
        sigmoid_val = jax.nn.sigmoid(gate_proj)
        masked_grad = d_value.astype(jnp.float32) * cell_mask
        return (
            masked_grad * value_proj * sigmoid_val * (1.0 - sigmoid_val),
            masked_grad * sigmoid_val,
        )

    gate_left, value_left = gating(d_panels[0], projected[:hidden], projected[hidden : 2 * hidden])
    gate_right, value_right = gating(
        d_panels[1], projected[2 * hidden : 3 * hidden], projected[3 * hidden :]
    )
    d_proj = jnp.concatenate([gate_left, value_left, gate_right, value_right], axis=0).astype(
        jnp.bfloat16
    )
    d_normed = jnp.einsum("hrm,ch->rmc", d_proj, w_proj, preferred_element_type=jnp.float32)
    d_normed = d_normed + jnp.einsum(
        "rmd,cd->rmc", d_gate_pre, w_gate, preferred_element_type=jnp.float32
    )
    d_input = d_normed * ln_in_gain
    return norm_backward(d_input, normed, inv_std, -1).astype(jnp.bfloat16)


def solution(mesh):
    fits = mesh.shape["chan"] == 1 and mesh.shape["row"] in (8, 16)
    return jax.shard_map(
        kernel_shards if fits else shards,
        mesh=mesh,
        in_specs=(
            P(("grp", "row"), "chan", None),
            P(("grp", "row"), "chan", None),
            P("grp"),
            P(),
            P(),
            P(),
            P(),
            P(),
            P(),
            P(),
        ),
        out_specs=P(("grp", "row"), "chan", None),
        check_vma=False,
    )
```

```python
import functools

import jax
import jax.numpy as jnp
from jax import lax
from jax.experimental import pallas as pl
from jax.experimental.pallas import tpu as pltpu
from jax.sharding import PartitionSpec as P

F32 = jnp.float32
BF16 = jnp.bfloat16
VMEM_LIMIT = 16 * 1024 * 1024


def dot(lhs, rhs, lhs_dim, rhs_dim):
    return lax.dot_general(
        lhs, rhs, (((lhs_dim,), (rhs_dim,)), ((), ())), preferred_element_type=F32
    )


def transposed(matrix):
    return jnp.transpose(matrix.astype(F32)).astype(BF16)


def sigmoid(values):
    return 1.0 / (1.0 + jnp.exp(-values))


def column(row):
    size = row.shape[1]
    return jnp.transpose(jnp.broadcast_to(row, (size, size)))


def norm_rows(values):
    centered = values - jnp.mean(values, axis=0, keepdims=True)
    variance = jnp.mean(centered * centered, axis=0, keepdims=True)
    inv_std = lax.rsqrt(variance + 1e-05)
    return centered * inv_std, inv_std


def call(
    kernel, name, outs, args, fetched=(), unread=(), scratch=(), flops=0, limit=VMEM_LIMIT
):
    moved = sum(a.size * a.dtype.itemsize for a in args) + sum(
        o.size * jnp.dtype(o.dtype).itemsize for o in outs
    )
    n_args, n_outs, n_fetched = len(args), len(outs), len(fetched)

    def body(*refs):
        ins = list(refs[:n_args])
        rest = refs[n_args + n_outs :]
        copies = []
        for n, place in enumerate(fetched):
            copies.append(pltpu.make_async_copy(ins[place], rest[n], rest[n_fetched].at[n]))
            ins[place] = rest[n]
        for copy in copies:
            copy.start()
        for copy in copies:
            copy.wait()
        kernel(*ins, *refs[n_args : n_args + n_outs], *rest[n_fetched + (n_fetched > 0) :])

    buffers = [pltpu.VMEM(args[place].shape, args[place].dtype) for place in fetched]
    if fetched:
        buffers.append(pltpu.SemaphoreType.DMA((n_fetched,)))
    return pl.pallas_call(
        body,
        name=name,
        out_shape=outs,
        in_specs=[
            pl.BlockSpec(
                memory_space=pltpu.HBM if n in fetched else pl.ANY if n in unread else pltpu.VMEM
            )
            for n in range(n_args)
        ],
        out_specs=[pl.BlockSpec(memory_space=pltpu.VMEM) for _ in outs],
        scratch_shapes=buffers + list(scratch),
        compiler_params=pltpu.CompilerParams(vmem_limit_bytes=limit),
        cost_estimate=pl.CostEstimate(flops=flops, bytes_accessed=moved, transcendentals=0),
    )(*args)


def cell_masks(mask, rows):
    columns = mask[...].astype(F32)
    shape = (rows, columns.shape[1])
    first = lax.axis_index("row") * rows
    own = lax.broadcasted_iota(jnp.int32, shape, 1) == (
        lax.broadcasted_iota(jnp.int32, shape, 0) + first
    )
    row_mask = jnp.sum(jnp.where(own, columns, 0.0), axis=1, keepdims=True)
    cells = row_mask * columns
    return [cells[row : row + 1] for row in range(rows)]


def wide_order(devices, count, back):
    order = []
    for place in range(count):
        if back:
            order += [place ^ (count // 2), count + place]
        else:
            order += [count + (place ^ 2), place ^ (count // 2)]
    return order


def distance(step, count):
    far = sorted(range(2, count), key=lambda apart: -(apart // 2))
    return [0, 1, *far][step]


def partner(step, count):
    return lax.rem(lax.axis_index("row"), count) ^ distance(step, count)


def gated_rows(pair, mask, gain, bias, w_proj, side):
    rows = pair.shape[0]
    hidden = w_proj.shape[1] // 4
    w_flip = transposed(w_proj[:, 2 * side * hidden : 2 * (side + 1) * hidden])
    gain_col, bias_col = column(gain[...]), column(bias[...])
    masks = cell_masks(mask, rows)
    for row in range(rows):
        normed, _ = norm_rows(jnp.transpose(pair[row].astype(F32)))
        zln = (normed * gain_col + bias_col).astype(BF16)
        proj = dot(w_flip, zln, 1, 0)
        yield row, masks[row] * sigmoid(proj[:hidden]) * proj[hidden:]


def project_right_kernel(pair, mask, gain, bias, w_proj, right_panel):
    rows = pair.shape[0]
    devices, depth, width = right_panel.shape
    block = depth // rows
    count = w_proj.shape[1] // 4 // block
    for row, right in gated_rows(pair, mask, gain, bias, w_proj, 1):
        right = right.reshape(count, block, width).astype(BF16)
        for rank in range(devices):
            place = wide_order(devices, count, False)[rank] % count
            right_panel[rank, row * block : (row + 1) * block, :] = right[place]


def project_left_kernel(pair, mask, gain, bias, w_proj, after, *refs):
    del after
    *pieces, left_panel = refs
    rows = pair.shape[0]
    count, depth, width = left_panel.shape
    block = depth // rows
    for row, left in gated_rows(pair, mask, gain, bias, w_proj, 0):
        left = left.reshape(count, block, width).astype(BF16)
        left_panel[:, row * block : (row + 1) * block, :] = left
    for step, piece in enumerate(pieces):
        piece[...] = left_panel[partner(step, count)]


def prepare_kernel(
    pair, cotangent, gain, bias, w_gate, out_gain, w_out, d_hat_centered, gate_slope
):
    gate_flip = transposed(w_gate[...])
    gain_col, bias_col = column(gain[...]), column(bias[...])
    out_gain_col = column(out_gain[...])
    for row in range(pair.shape[0]):
        normed, _ = norm_rows(jnp.transpose(pair[row].astype(F32)))
        zln = (normed * gain_col + bias_col).astype(BF16)
        gate = sigmoid(dot(gate_flip, zln, 1, 0))
        cot = jnp.transpose(cotangent[row].astype(F32))
        d_scaled = (cot * gate).astype(BF16)
        d_hat = dot(w_out[...], d_scaled, 1, 0) * out_gain_col
        d_hat_centered[row] = d_hat - jnp.mean(d_hat, axis=0, keepdims=True)
        gate_slope[row] = cot * gate * (1.0 - gate)


def spread(panel, wide):
    wide[...] = panel[...].astype(F32).reshape(wide.shape)


def wide_places(panel, count, back):
    devices, depth, _ = panel.shape
    for rank, device in enumerate(wide_order(devices, count, back)):
        yield rank, slice(device * depth, (device + 1) * depth)


def sort_left_kernel(*refs):
    *pieces, left_all, left_wide = refs
    block, left_rows, _ = left_all.shape
    depth = pieces[0].shape[0]
    for step, piece in enumerate(pieces):
        start = pl.multiple_of(partner(step, len(pieces)) * depth, depth)
        left_wide[pl.ds(start, depth), :] = piece[...].astype(F32)
    for h in range(block):
        left_all[h] = left_wide[pl.ds(h, left_rows, stride=block), :].astype(BF16)


def tri_kernel(right_panel, left_all, after, products, right_all, left_wide, right_wide):
    del after
    block, left_rows, _ = left_all.shape
    right_rows = right_all.shape[1]
    for rank, place in wide_places(right_panel, products.shape[0], False):
        right_wide[place, :] = right_panel[rank].astype(F32)
    for h in range(block):
        right = right_wide[pl.ds(h, right_rows, stride=block), :].astype(BF16)
        right_all[h] = right
        left_wide[pl.ds(h, left_rows, stride=block), :] = dot(left_all[h], right, 1, 1)
    products[...] = left_wide[...].astype(BF16).reshape(products.shape)


def cell_row(ref, row, rows):
    count, depth, width = ref.shape
    block = depth // rows
    return ref[:, row * block : (row + 1) * block, :].astype(F32).reshape(count * block, width)


def middle_kernel(products, d_hat_centered, d_products):
    rows = d_hat_centered.shape[0]
    count, depth, width = products.shape
    block = depth // rows
    for row in range(rows):
        tri_hat, inv_std = norm_rows(cell_row(products, row, rows))
        d_hat = d_hat_centered[row]
        cross = jnp.mean(d_hat * tri_hat, axis=0, keepdims=True)
        d_tri = inv_std * (d_hat - tri_hat * cross)
        d_products[:, row * block : (row + 1) * block, :] = d_tri.reshape(
            count, block, width
        ).astype(BF16)


def d_right_kernel(d_products, left_all, d_right_panel, d_tri_all, left_wide, right_wide):
    block, left_rows, _ = left_all.shape
    right_rows = right_wide.shape[0] // block
    spread(d_products, left_wide)
    for h in range(block):
        d_tri = left_wide[pl.ds(h, left_rows, stride=block), :].astype(BF16)
        d_tri_all[h] = d_tri
        right_wide[pl.ds(h, right_rows, stride=block), :] = dot(d_tri, left_all[h], 0, 0)
    for rank, place in wide_places(d_right_panel, d_products.shape[0], True):
        d_right_panel[rank] = right_wide[place, :].astype(BF16)


def d_left_kernel(d_tri_all, right_all, *refs):
    *pieces, left_wide = refs
    block, left_rows, _ = d_tri_all.shape
    for h in range(block):
        left_wide[pl.ds(h, left_rows, stride=block), :] = dot(d_tri_all[h], right_all[h], 1, 0)
    depth = pieces[0].shape[0]
    for step, piece in enumerate(pieces):
        start = pl.multiple_of(partner(step, len(pieces)) * depth, depth)
        piece[...] = left_wide[pl.ds(start, depth), :].astype(BF16)


def gate_back_kernel(products, gate_slope, out_gain, out_bias, w_out, d_gate_pre):
    rows = gate_slope.shape[0]
    out_flip = transposed(w_out[...])
    out_gain_col, out_bias_col = column(out_gain[...]), column(out_bias[...])
    for row in range(rows):
        tri_hat, _ = norm_rows(cell_row(products, row, rows))
        scaled = (tri_hat * out_gain_col + out_bias_col).astype(BF16)
        d_gate_pre[row] = (dot(out_flip, scaled, 1, 0) * gate_slope[row]).astype(BF16)


def slopes_kernel(
    pair, mask, gain, bias, w_proj, w_gate, after, slopes, normed_in, inv_in, in_gain, weights
):
    del after
    rows = pair.shape[0]
    hidden = w_proj.shape[1] // 4
    w_flip = transposed(w_proj[...])
    gain_col, bias_col = column(gain[...]), column(bias[...])
    in_gain[...] = gain_col
    weights[...] = jnp.concatenate([w_proj[...], w_gate[...]], axis=1)
    masks = cell_masks(mask, rows)
    for row in range(rows):
        normed, inv_std = norm_rows(jnp.transpose(pair[row].astype(F32)))
        normed_in[row] = normed.astype(normed_in.dtype)
        inv_in[row : row + 1] = inv_std
        zln = (normed * gain_col + bias_col).astype(BF16)
        proj = dot(w_flip, zln, 1, 0)
        for side in range(2):
            base = 2 * side * hidden
            sig = sigmoid(proj[base : base + hidden])
            masked = masks[row] * sig
            value = masked * (1.0 - sig) * proj[base + hidden : base + 2 * hidden]
            slopes[row, base : base + hidden, :] = value.astype(slopes.dtype)
            slopes[row, base + hidden : base + 2 * hidden, :] = masked.astype(slopes.dtype)


def sort_d_left_kernel(*refs):
    *pieces, d_left_panel = refs
    for step, piece in enumerate(pieces):
        d_left_panel[partner(step, len(pieces))] = piece[...]


def both_halves(blocks, count):
    order = wide_order(2 * count, count, True)
    return jnp.stack(
        [blocks[order.index(place)] + blocks[order.index(count + place)] for place in range(count)]
    )


def finish_kernel(
    d_right_panel, d_left_panel, slopes, d_gate_pre, normed_in, inv_in, gain_col, weights, grad
):
    rows = grad.shape[0]
    count, depth, width = d_left_panel.shape
    hidden = count * depth // rows
    for row in range(rows):
        d_right = cell_row(d_right_panel, row, rows)
        d_right = both_halves(d_right.reshape(2 * count, depth // rows, width), count)
        parts = []
        for side, d_value in enumerate((cell_row(d_left_panel, row, rows), d_right.reshape(hidden, width))):
            for base in (2 * side * hidden, (2 * side + 1) * hidden):
                slope = slopes[row, base : base + hidden, :].astype(F32)
                parts.append((d_value * slope).astype(BF16))
        parts.append(d_gate_pre[row])
        d_in = dot(weights[...], jnp.concatenate(parts, axis=0), 1, 0) * gain_col[...]
        normed = normed_in[row].astype(F32)
        mean_grad = jnp.mean(d_in, axis=0, keepdims=True)
        mean_cross = jnp.mean(d_in * normed, axis=0, keepdims=True)
        result = inv_in[row : row + 1] * (d_in - mean_grad - normed * mean_cross)
        grad[row] = jnp.transpose(result).astype(BF16)


def swap(values, count, back):
    groups = [wide_order(lax.axis_size("row"), count, back)]
    return lax.all_to_all(
        values, "row", split_axis=0, concat_axis=0, tiled=True, axis_index_groups=groups
    )


def swap_half(values, count):
    devices = range(lax.axis_size("row"))
    groups = [[d for d in devices if d // count == half] for half in range(len(devices) // count)]
    return lax.all_to_all(
        values, "row", split_axis=0, concat_axis=0, tiled=True, axis_index_groups=groups
    )


def swap_pieces(pieces):
    devices = range(lax.axis_size("row"))
    count = len(pieces)
    return [pieces[0]] + [
        lax.ppermute(pieces[step], "row", [(d, d ^ distance(step, count)) for d in devices])
        for step in range(1, count)
    ]


def kernel_shards(
    pair,
    cotangent,
    residue_mask,
    ln_in_gain,
    ln_in_bias,
    w_proj,
    w_gate,
    ln_out_gain,
    ln_out_bias,
    w_out,
):
    rows, width, channels = pair.shape
    hidden = w_out.shape[0]
    halves = 2
    devices = lax.axis_size("row")
    count = devices // halves
    block = hidden // count
    left_rows, right_rows = rows * count, rows * devices
    shape = jax.ShapeDtypeStruct
    panel = shape((count, rows * block, width), BF16)
    wide_panel = shape((devices, rows * block, width), BF16)
    mask = residue_mask.reshape(1, width)
    gain, bias = ln_in_gain.reshape(1, channels), ln_in_bias.reshape(1, channels)
    out_gain, out_bias = ln_out_gain.reshape(1, hidden), ln_out_bias.reshape(1, hidden)
    cells = rows * width
    piece = shape((rows * block, width), BF16)
    left_panel = pltpu.VMEM(panel.shape, BF16)
    left_wide = pltpu.VMEM((left_rows * block, width), F32)
    right_wide = pltpu.VMEM((right_rows * block, width), F32)
    (own_right,) = call(
        project_right_kernel,
        "project_right",
        [wide_panel],
        [pair, mask, gain, bias, w_proj],
        fetched=range(5),
        flops=2 * cells * channels * 2 * hidden,
        limit=64 * 1024 * 1024 - 640 * 1024,
    )
    right_panel = swap(own_right, count, False)
    pieces = call(
        project_left_kernel,
        "project_left",
        [piece] * count,
        [pair, mask, gain, bias, w_proj, own_right],
        fetched=range(5),
        unread=(5,),
        scratch=[left_panel],
        flops=2 * cells * channels * 2 * hidden,
    )
    pieces = swap_pieces(pieces)
    (left_all,) = call(
        sort_left_kernel,
        "sort_left",
        [shape((block, left_rows, width), BF16)],
        pieces,
        scratch=[left_wide],
    )
    d_hat_centered, gate_slope = call(
        prepare_kernel,
        "prepare",
        [shape((rows, hidden, width), F32), shape((rows, channels, width), F32)],
        [pair, cotangent, gain, bias, w_gate, out_gain, w_out],
        fetched=range(7),
        flops=2 * cells * channels * 2 * hidden,
    )
    products, right_all = call(
        tri_kernel,
        "tri",
        [panel, shape((block, right_rows, width), BF16)],
        [right_panel, left_all, d_hat_centered],
        unread=(2,),
        scratch=[left_wide, right_wide],
        flops=2 * block * left_rows * width * right_rows,
    )
    products = swap_half(products, count)
    (d_products,) = call(
        middle_kernel,
        "middle",
        [panel],
        [products, d_hat_centered],
        flops=20 * cells * hidden,
    )
    d_products = swap_half(d_products, count)
    d_right_panel, d_tri_all = call(
        d_right_kernel,
        "d_right",
        [wide_panel, shape((block, left_rows, width), BF16)],
        [d_products, left_all],
        scratch=[left_wide, right_wide],
        flops=2 * block * left_rows * width * right_rows,
    )
    d_right_panel = swap(d_right_panel, count, True)
    d_pieces = call(
        d_left_kernel,
        "d_left",
        [piece] * count,
        [d_tri_all, right_all],
        scratch=[left_wide],
        flops=2 * block * left_rows * width * right_rows,
    )
    d_pieces = swap_pieces(d_pieces)
    (d_left_panel,) = call(sort_d_left_kernel, "sort_d_left", [panel], d_pieces)
    (d_gate_pre,) = call(
        gate_back_kernel,
        "gate_back",
        [shape((rows, channels, width), BF16)],
        [products, gate_slope, out_gain, out_bias, w_out],
        fetched=range(2, 5),
        flops=2 * cells * channels * hidden,
    )
    slopes, normed_in, inv_in, gain_col, weights = call(
        slopes_kernel,
        "slopes",
        [
            shape((rows, 4 * hidden, width), BF16),
            shape((rows, channels, width), BF16),
            shape((rows, width), F32),
            shape((channels, channels), F32),
            shape((channels, 4 * hidden + channels), BF16),
        ],
        [pair, mask, gain, bias, w_proj, w_gate, d_gate_pre],
        fetched=range(6),
        unread=(6,),
        flops=2 * cells * channels * 4 * hidden,
    )
    (grad,) = call(
        finish_kernel,
        "finish",
        [shape(pair.shape, BF16)],
        [
            d_right_panel,
            d_left_panel,
            slopes,
            d_gate_pre,
            normed_in,
            inv_in,
            gain_col,
            weights,
        ],
        flops=2 * cells * channels * 4 * hidden,
    )
    return grad


def normalize(values, reduce_axis):
    mean_value = jnp.mean(values, axis=reduce_axis, keepdims=True)
    centered = values - mean_value
    variance = jnp.mean(centered * centered, axis=reduce_axis, keepdims=True)
    inv_std = lax.rsqrt(variance + 1e-05)
    return (centered * inv_std, inv_std)


def norm_backward(upstream, normed, inv_std, reduce_axis):
    mean_grad = jnp.mean(upstream, axis=reduce_axis, keepdims=True)
    mean_cross = jnp.mean(upstream * normed, axis=reduce_axis, keepdims=True)
    return inv_std * (upstream - mean_grad - normed * mean_cross)


def shards(
    pair,
    cotangent,
    residue_mask,
    ln_in_gain,
    ln_in_bias,
    w_proj,
    w_gate,
    ln_out_gain,
    ln_out_bias,
    w_out,
):
    local_rows = pair.shape[0]
    local_cols = pair.shape[1]
    hidden = w_out.shape[0]
    chan_index = lax.axis_index("chan")
    row_start = lax.axis_index("row") * local_rows
    col_start = chan_index * local_cols
    mask_float = residue_mask.astype(jnp.float32)
    row_mask = lax.dynamic_slice_in_dim(mask_float, row_start, local_rows)
    col_mask = lax.dynamic_slice_in_dim(mask_float, col_start, local_cols)
    cell_mask = (row_mask[:, None] * col_mask[None, :])[None]
    normed, inv_std = normalize(pair.astype(jnp.float32), -1)
    normed_pair = (normed * ln_in_gain + ln_in_bias).astype(jnp.bfloat16)
    projected = jnp.einsum("rmc,ch->hrm", normed_pair, w_proj, preferred_element_type=jnp.float32)
    left_panel = (
        cell_mask * jax.nn.sigmoid(projected[:hidden]) * projected[hidden : 2 * hidden]
    ).astype(jnp.bfloat16)
    right_panel = (
        cell_mask * jax.nn.sigmoid(projected[2 * hidden : 3 * hidden]) * projected[3 * hidden :]
    ).astype(jnp.bfloat16)
    panels = lax.all_to_all(
        jnp.stack([left_panel, right_panel]), "row", split_axis=1, concat_axis=2, tiled=True
    )
    left_all = panels[0]
    right_all = panels[1]
    right_rows = lax.all_to_all(right_all, "chan", split_axis=1, concat_axis=2, tiled=True)
    partner = right_rows
    tri_part = jnp.einsum(
        "gik,gjk->gij",
        lax.all_gather(left_all, "chan", axis=2, tiled=True),
        partner,
        preferred_element_type=jnp.float32,
    ).astype(jnp.bfloat16)
    tri_cells = lax.all_to_all(tri_part, "row", split_axis=1, concat_axis=0, tiled=True)
    tri_hat, inv_tri = normalize(tri_cells.astype(jnp.float32), 0)
    scaled = (tri_hat * ln_out_gain[:, None, None] + ln_out_bias[:, None, None]).astype(
        jnp.bfloat16
    )
    proj_out = jnp.einsum("hrm,hc->rmc", scaled, w_out, preferred_element_type=jnp.float32)
    gate_value = jax.nn.sigmoid(
        jnp.einsum("rmc,cd->rmd", normed_pair, w_gate, preferred_element_type=jnp.float32)
    )
    cot_float = cotangent.astype(jnp.float32)
    d_gate_pre = (cot_float * proj_out * gate_value * (1.0 - gate_value)).astype(jnp.bfloat16)
    d_scaled = (cot_float * gate_value).astype(jnp.bfloat16)
    d_hat = jnp.einsum("rmc,hc->hrm", d_scaled, w_out, preferred_element_type=jnp.float32)
    d_hat = d_hat * ln_out_gain[:, None, None]
    d_tri = norm_backward(d_hat, tri_hat, inv_tri, 0).astype(jnp.bfloat16)
    d_tri_all = lax.all_to_all(d_tri, "row", split_axis=0, concat_axis=1, tiled=True)
    panel_piece = lax.all_gather(d_tri_all, "chan", axis=2, tiled=True)
    partner = right_all
    d_left = jnp.einsum("gij,gjk->gik", panel_piece, partner, preferred_element_type=jnp.float32)
    contribution = jnp.einsum(
        "gij,gik->gjk", panel_piece, left_all, preferred_element_type=jnp.float32
    )
    d_right = contribution
    d_left, d_right = (d_left, d_right)
    d_stack = jnp.stack([d_left, d_right]).astype(jnp.bfloat16)
    d_panels = lax.all_to_all(d_stack, "row", split_axis=2, concat_axis=1, tiled=True)

    def gating(d_value, gate_proj, value_proj):
        sigmoid_val = jax.nn.sigmoid(gate_proj)
        masked_grad = d_value.astype(jnp.float32) * cell_mask
        return (
            masked_grad * value_proj * sigmoid_val * (1.0 - sigmoid_val),
            masked_grad * sigmoid_val,
        )

    gate_left, value_left = gating(d_panels[0], projected[:hidden], projected[hidden : 2 * hidden])
    gate_right, value_right = gating(
        d_panels[1], projected[2 * hidden : 3 * hidden], projected[3 * hidden :]
    )
    d_proj = jnp.concatenate([gate_left, value_left, gate_right, value_right], axis=0).astype(
        jnp.bfloat16
    )
    d_normed = jnp.einsum("hrm,ch->rmc", d_proj, w_proj, preferred_element_type=jnp.float32)
    d_normed = d_normed + jnp.einsum(
        "rmd,cd->rmc", d_gate_pre, w_gate, preferred_element_type=jnp.float32
    )
    d_input = d_normed * ln_in_gain
    return norm_backward(d_input, normed, inv_std, -1).astype(jnp.bfloat16)


def solution(mesh):
    fits = mesh.shape["chan"] == 1 and mesh.shape["row"] in (8, 16)
    return jax.shard_map(
        kernel_shards if fits else shards,
        mesh=mesh,
        in_specs=(
            P(("grp", "row"), "chan", None),
            P(("grp", "row"), "chan", None),
            P("grp"),
            P(),
            P(),
            P(),
            P(),
            P(),
            P(),
            P(),
        ),
        out_specs=P(("grp", "row"), "chan", None),
        check_vma=False,
    )
```

```python
import functools

import jax
import jax.numpy as jnp
from jax import lax
from jax.experimental import pallas as pl
from jax.experimental.pallas import tpu as pltpu
from jax.sharding import PartitionSpec as P

F32 = jnp.float32
BF16 = jnp.bfloat16
VMEM_LIMIT = 16 * 1024 * 1024


def dot(lhs, rhs, lhs_dim, rhs_dim):
    return lax.dot_general(
        lhs, rhs, (((lhs_dim,), (rhs_dim,)), ((), ())), preferred_element_type=F32
    )


def transposed(matrix):
    return jnp.transpose(matrix.astype(F32)).astype(BF16)


def sigmoid(values):
    return 1.0 / (1.0 + jnp.exp(-values))


def column(row):
    size = row.shape[1]
    return jnp.transpose(jnp.broadcast_to(row, (size, size)))


def norm_rows(values):
    centered = values - jnp.mean(values, axis=0, keepdims=True)
    variance = jnp.mean(centered * centered, axis=0, keepdims=True)
    inv_std = lax.rsqrt(variance + 1e-05)
    return centered * inv_std, inv_std


def call(
    kernel, name, outs, args, fetched=(), unread=(), scratch=(), flops=0, limit=VMEM_LIMIT
):
    moved = sum(a.size * a.dtype.itemsize for a in args) + sum(
        o.size * jnp.dtype(o.dtype).itemsize for o in outs
    )
    n_args, n_outs, n_fetched = len(args), len(outs), len(fetched)

    def body(*refs):
        ins = list(refs[:n_args])
        rest = refs[n_args + n_outs :]
        copies = []
        for n, place in enumerate(fetched):
            copies.append(pltpu.make_async_copy(ins[place], rest[n], rest[n_fetched].at[n]))
            ins[place] = rest[n]
        for copy in copies:
            copy.start()
        for copy in copies:
            copy.wait()
        kernel(*ins, *refs[n_args : n_args + n_outs], *rest[n_fetched + (n_fetched > 0) :])

    buffers = [pltpu.VMEM(args[place].shape, args[place].dtype) for place in fetched]
    if fetched:
        buffers.append(pltpu.SemaphoreType.DMA((n_fetched,)))
    return pl.pallas_call(
        body,
        name=name,
        out_shape=outs,
        in_specs=[
            pl.BlockSpec(
                memory_space=pltpu.HBM if n in fetched else pl.ANY if n in unread else pltpu.VMEM
            )
            for n in range(n_args)
        ],
        out_specs=[pl.BlockSpec(memory_space=pltpu.VMEM) for _ in outs],
        scratch_shapes=buffers + list(scratch),
        compiler_params=pltpu.CompilerParams(vmem_limit_bytes=limit),
        cost_estimate=pl.CostEstimate(flops=flops, bytes_accessed=moved, transcendentals=0),
    )(*args)


def cell_masks(mask, rows):
    columns = mask[...].astype(F32)
    shape = (rows, columns.shape[1])
    first = lax.axis_index("row") * rows
    own = lax.broadcasted_iota(jnp.int32, shape, 1) == (
        lax.broadcasted_iota(jnp.int32, shape, 0) + first
    )
    row_mask = jnp.sum(jnp.where(own, columns, 0.0), axis=1, keepdims=True)
    cells = row_mask * columns
    return [cells[row : row + 1] for row in range(rows)]


def wide_order(devices, count, back):
    order = []
    for place in range(count):
        if back:
            order += [place ^ (count // 2), count + place]
        else:
            order += [count + (place ^ 2), place ^ (count // 2)]
    return order


def distance(step, count):
    far = sorted(range(3, count), key=lambda apart: -(apart // 2))
    return [*range(min(3, count)), *far][step]


def partner(step, count):
    return lax.rem(lax.axis_index("row"), count) ^ distance(step, count)


def gated_rows(pair, mask, gain, bias, w_proj, side):
    rows = pair.shape[0]
    hidden = w_proj.shape[1] // 4
    w_flip = transposed(w_proj[:, 2 * side * hidden : 2 * (side + 1) * hidden])
    gain_col, bias_col = column(gain[...]), column(bias[...])
    masks = cell_masks(mask, rows)
    for row in range(rows):
        normed, _ = norm_rows(jnp.transpose(pair[row].astype(F32)))
        zln = (normed * gain_col + bias_col).astype(BF16)
        proj = dot(w_flip, zln, 1, 0)
        yield row, masks[row] * sigmoid(proj[:hidden]) * proj[hidden:]


def project_right_kernel(pair, mask, gain, bias, w_proj, right_panel):
    rows = pair.shape[0]
    devices, depth, width = right_panel.shape
    block = depth // rows
    count = w_proj.shape[1] // 4 // block
    for row, right in gated_rows(pair, mask, gain, bias, w_proj, 1):
        right = right.reshape(count, block, width).astype(BF16)
        for rank in range(devices):
            place = wide_order(devices, count, False)[rank] % count
            right_panel[rank, row * block : (row + 1) * block, :] = right[place]


def project_left_kernel(pair, mask, gain, bias, w_proj, after, *refs):
    del after
    *pieces, left_panel = refs
    rows = pair.shape[0]
    count, depth, width = left_panel.shape
    block = depth // rows
    for row, left in gated_rows(pair, mask, gain, bias, w_proj, 0):
        left = left.reshape(count, block, width).astype(BF16)
        left_panel[:, row * block : (row + 1) * block, :] = left
    for step, piece in enumerate(pieces):
        piece[...] = left_panel[partner(step, count)]


def prepare_kernel(
    pair, cotangent, gain, bias, w_gate, out_gain, w_out, d_hat_centered, gate_slope
):
    gate_flip = transposed(w_gate[...])
    gain_col, bias_col = column(gain[...]), column(bias[...])
    out_gain_col = column(out_gain[...])
    for row in range(pair.shape[0]):
        normed, _ = norm_rows(jnp.transpose(pair[row].astype(F32)))
        zln = (normed * gain_col + bias_col).astype(BF16)
        gate = sigmoid(dot(gate_flip, zln, 1, 0))
        cot = jnp.transpose(cotangent[row].astype(F32))
        d_scaled = (cot * gate).astype(BF16)
        d_hat = dot(w_out[...], d_scaled, 1, 0) * out_gain_col
        d_hat_centered[row] = d_hat - jnp.mean(d_hat, axis=0, keepdims=True)
        gate_slope[row] = cot * gate * (1.0 - gate)


def spread(panel, wide):
    wide[...] = panel[...].astype(F32).reshape(wide.shape)


def wide_places(panel, count, back):
    devices, depth, _ = panel.shape
    for rank, device in enumerate(wide_order(devices, count, back)):
        yield rank, slice(device * depth, (device + 1) * depth)


def sort_left_kernel(*refs):
    *pieces, left_all, left_wide = refs
    block, left_rows, _ = left_all.shape
    depth = pieces[0].shape[0]
    for step, piece in enumerate(pieces):
        start = pl.multiple_of(partner(step, len(pieces)) * depth, depth)
        left_wide[pl.ds(start, depth), :] = piece[...].astype(F32)
    for h in range(block):
        left_all[h] = left_wide[pl.ds(h, left_rows, stride=block), :].astype(BF16)


def tri_kernel(right_panel, left_all, after, products, right_all, left_wide, right_wide):
    del after
    block, left_rows, _ = left_all.shape
    right_rows = right_all.shape[1]
    for rank, place in wide_places(right_panel, products.shape[0], False):
        right_wide[place, :] = right_panel[rank].astype(F32)
    for h in range(block):
        right = right_wide[pl.ds(h, right_rows, stride=block), :].astype(BF16)
        right_all[h] = right
        left_wide[pl.ds(h, left_rows, stride=block), :] = dot(left_all[h], right, 1, 1)
    products[...] = left_wide[...].astype(BF16).reshape(products.shape)


def cell_row(ref, row, rows):
    count, depth, width = ref.shape
    block = depth // rows
    return ref[:, row * block : (row + 1) * block, :].astype(F32).reshape(count * block, width)


def middle_kernel(products, d_hat_centered, d_products):
    rows = d_hat_centered.shape[0]
    count, depth, width = products.shape
    block = depth // rows
    for row in range(rows):
        tri_hat, inv_std = norm_rows(cell_row(products, row, rows))
        d_hat = d_hat_centered[row]
        cross = jnp.mean(d_hat * tri_hat, axis=0, keepdims=True)
        d_tri = inv_std * (d_hat - tri_hat * cross)
        d_products[:, row * block : (row + 1) * block, :] = d_tri.reshape(
            count, block, width
        ).astype(BF16)


def d_right_kernel(d_products, left_all, d_right_panel, d_tri_all, left_wide, right_wide):
    block, left_rows, _ = left_all.shape
    right_rows = right_wide.shape[0] // block
    spread(d_products, left_wide)
    for h in range(block):
        d_tri = left_wide[pl.ds(h, left_rows, stride=block), :].astype(BF16)
        d_tri_all[h] = d_tri
        right_wide[pl.ds(h, right_rows, stride=block), :] = dot(d_tri, left_all[h], 0, 0)
    for rank, place in wide_places(d_right_panel, d_products.shape[0], True):
        d_right_panel[rank] = right_wide[place, :].astype(BF16)


def d_left_kernel(d_tri_all, right_all, *refs):
    *pieces, left_wide = refs
    block, left_rows, _ = d_tri_all.shape
    for h in range(block):
        left_wide[pl.ds(h, left_rows, stride=block), :] = dot(d_tri_all[h], right_all[h], 1, 0)
    depth = pieces[0].shape[0]
    for step, piece in enumerate(pieces):
        start = pl.multiple_of(partner(step, len(pieces)) * depth, depth)
        piece[...] = left_wide[pl.ds(start, depth), :].astype(BF16)


def gate_back_kernel(products, gate_slope, out_gain, out_bias, w_out, d_gate_pre):
    rows = gate_slope.shape[0]
    out_flip = transposed(w_out[...])
    out_gain_col, out_bias_col = column(out_gain[...]), column(out_bias[...])
    for row in range(rows):
        tri_hat, _ = norm_rows(cell_row(products, row, rows))
        scaled = (tri_hat * out_gain_col + out_bias_col).astype(BF16)
        d_gate_pre[row] = (dot(out_flip, scaled, 1, 0) * gate_slope[row]).astype(BF16)


def slopes_kernel(
    pair, mask, gain, bias, w_proj, w_gate, after, slopes, normed_in, inv_in, in_gain, weights
):
    del after
    rows = pair.shape[0]
    hidden = w_proj.shape[1] // 4
    w_flip = transposed(w_proj[...])
    gain_col, bias_col = column(gain[...]), column(bias[...])
    in_gain[...] = gain_col
    weights[...] = jnp.concatenate([w_proj[...], w_gate[...]], axis=1)
    masks = cell_masks(mask, rows)
    for row in range(rows):
        normed, inv_std = norm_rows(jnp.transpose(pair[row].astype(F32)))
        normed_in[row] = normed.astype(normed_in.dtype)
        inv_in[row : row + 1] = inv_std
        zln = (normed * gain_col + bias_col).astype(BF16)
        proj = dot(w_flip, zln, 1, 0)
        for side in range(2):
            base = 2 * side * hidden
            sig = sigmoid(proj[base : base + hidden])
            masked = masks[row] * sig
            value = masked * (1.0 - sig) * proj[base + hidden : base + 2 * hidden]
            slopes[row, base : base + hidden, :] = value.astype(slopes.dtype)
            slopes[row, base + hidden : base + 2 * hidden, :] = masked.astype(slopes.dtype)


def sloped(d_value, slopes, row, side):
    hidden = d_value.shape[0]
    parts = []
    for base in (2 * side * hidden, (2 * side + 1) * hidden):
        slope = slopes[row, base : base + hidden, :].astype(F32)
        parts.append((d_value * slope).astype(BF16))
    return jnp.concatenate(parts, axis=0)


def finish_left_kernel(slopes, d_gate_pre, weights, *refs):
    *pieces, d_zln_left, panel = refs
    rows = d_zln_left.shape[0]
    for step, piece in enumerate(pieces):
        panel[partner(step, len(pieces))] = piece[...]
    half = slopes.shape[1] // 2
    own = jnp.concatenate([weights[:, :half], weights[:, 2 * half :]], axis=1)
    for row in range(rows):
        d_proj = sloped(cell_row(panel, row, rows), slopes, row, 0)
        d_zln_left[row] = dot(own, jnp.concatenate([d_proj, d_gate_pre[row]], axis=0), 1, 0)


def both_halves(blocks, count):
    order = wide_order(2 * count, count, True)
    return jnp.stack(
        [blocks[order.index(place)] + blocks[order.index(count + place)] for place in range(count)]
    )


def finish_kernel(
    d_right_panel, d_zln_left, slopes, normed_in, inv_in, gain_col, weights, grad
):
    rows = grad.shape[0]
    devices, depth, width = d_right_panel.shape
    half = slopes.shape[1] // 2
    for row in range(rows):
        d_right = cell_row(d_right_panel, row, rows)
        d_right = both_halves(d_right.reshape(devices, depth // rows, width), devices // 2)
        d_proj = sloped(d_right.reshape(half // 2, width), slopes, row, 1)
        d_zln = d_zln_left[row] + dot(weights[:, half : 2 * half], d_proj, 1, 0)
        d_in = d_zln * gain_col[...]
        normed = normed_in[row].astype(F32)
        mean_grad = jnp.mean(d_in, axis=0, keepdims=True)
        mean_cross = jnp.mean(d_in * normed, axis=0, keepdims=True)
        result = inv_in[row : row + 1] * (d_in - mean_grad - normed * mean_cross)
        grad[row] = jnp.transpose(result).astype(BF16)


def swap(values, count, back):
    groups = [wide_order(lax.axis_size("row"), count, back)]
    return lax.all_to_all(
        values, "row", split_axis=0, concat_axis=0, tiled=True, axis_index_groups=groups
    )


def swap_half(values, count):
    devices = range(lax.axis_size("row"))
    groups = [[d for d in devices if d // count == half] for half in range(len(devices) // count)]
    return lax.all_to_all(
        values, "row", split_axis=0, concat_axis=0, tiled=True, axis_index_groups=groups
    )


def swap_pieces(pieces):
    devices = range(lax.axis_size("row"))
    count = len(pieces)
    return [pieces[0]] + [
        lax.ppermute(pieces[step], "row", [(d, d ^ distance(step, count)) for d in devices])
        for step in range(1, count)
    ]


def kernel_shards(
    pair,
    cotangent,
    residue_mask,
    ln_in_gain,
    ln_in_bias,
    w_proj,
    w_gate,
    ln_out_gain,
    ln_out_bias,
    w_out,
):
    rows, width, channels = pair.shape
    hidden = w_out.shape[0]
    halves = 2
    devices = lax.axis_size("row")
    count = devices // halves
    block = hidden // count
    left_rows, right_rows = rows * count, rows * devices
    shape = jax.ShapeDtypeStruct
    panel = shape((count, rows * block, width), BF16)
    wide_panel = shape((devices, rows * block, width), BF16)
    mask = residue_mask.reshape(1, width)
    gain, bias = ln_in_gain.reshape(1, channels), ln_in_bias.reshape(1, channels)
    out_gain, out_bias = ln_out_gain.reshape(1, hidden), ln_out_bias.reshape(1, hidden)
    cells = rows * width
    piece = shape((rows * block, width), BF16)
    left_panel = pltpu.VMEM(panel.shape, BF16)
    left_wide = pltpu.VMEM((left_rows * block, width), F32)
    right_wide = pltpu.VMEM((right_rows * block, width), F32)
    (own_right,) = call(
        project_right_kernel,
        "project_right",
        [wide_panel],
        [pair, mask, gain, bias, w_proj],
        fetched=range(5),
        flops=2 * cells * channels * 2 * hidden,
        limit=64 * 1024 * 1024 - 640 * 1024,
    )
    right_panel = swap(own_right, count, False)
    pieces = call(
        project_left_kernel,
        "project_left",
        [piece] * count,
        [pair, mask, gain, bias, w_proj, own_right],
        fetched=range(5),
        unread=(5,),
        scratch=[left_panel],
        flops=2 * cells * channels * 2 * hidden,
    )
    pieces = swap_pieces(pieces)
    (left_all,) = call(
        sort_left_kernel,
        "sort_left",
        [shape((block, left_rows, width), BF16)],
        pieces,
        scratch=[left_wide],
    )
    d_hat_centered, gate_slope = call(
        prepare_kernel,
        "prepare",
        [shape((rows, hidden, width), F32), shape((rows, channels, width), F32)],
        [pair, cotangent, gain, bias, w_gate, out_gain, w_out],
        fetched=range(7),
        flops=2 * cells * channels * 2 * hidden,
    )
    products, right_all = call(
        tri_kernel,
        "tri",
        [panel, shape((block, right_rows, width), BF16)],
        [right_panel, left_all, d_hat_centered],
        unread=(2,),
        scratch=[left_wide, right_wide],
        flops=2 * block * left_rows * width * right_rows,
    )
    products = swap_half(products, count)
    (d_products,) = call(
        middle_kernel,
        "middle",
        [panel],
        [products, d_hat_centered],
        flops=20 * cells * hidden,
    )
    d_products = swap_half(d_products, count)
    d_right_panel, d_tri_all = call(
        d_right_kernel,
        "d_right",
        [wide_panel, shape((block, left_rows, width), BF16)],
        [d_products, left_all],
        scratch=[left_wide, right_wide],
        flops=2 * block * left_rows * width * right_rows,
    )
    d_right_panel = swap(d_right_panel, count, True)
    d_pieces = call(
        d_left_kernel,
        "d_left",
        [piece] * count,
        [d_tri_all, right_all],
        scratch=[left_wide],
        flops=2 * block * left_rows * width * right_rows,
    )
    d_pieces = swap_pieces(d_pieces)
    (d_gate_pre,) = call(
        gate_back_kernel,
        "gate_back",
        [shape((rows, channels, width), BF16)],
        [products, gate_slope, out_gain, out_bias, w_out],
        fetched=range(2, 5),
        flops=2 * cells * channels * hidden,
    )
    slopes, normed_in, inv_in, gain_col, weights = call(
        slopes_kernel,
        "slopes",
        [
            shape((rows, 4 * hidden, width), BF16),
            shape((rows, channels, width), BF16),
            shape((rows, width), F32),
            shape((channels, channels), F32),
            shape((channels, 4 * hidden + channels), BF16),
        ],
        [pair, mask, gain, bias, w_proj, w_gate, d_gate_pre],
        fetched=range(6),
        unread=(6,),
        flops=2 * cells * channels * 4 * hidden,
    )
    (d_zln_left,) = call(
        finish_left_kernel,
        "finish_left",
        [shape((rows, channels, width), F32)],
        [slopes, d_gate_pre, weights, *d_pieces],
        scratch=[left_panel],
        flops=2 * cells * channels * 3 * hidden,
    )
    (grad,) = call(
        finish_kernel,
        "finish",
        [shape(pair.shape, BF16)],
        [
            d_right_panel,
            d_zln_left,
            slopes,
            normed_in,
            inv_in,
            gain_col,
            weights,
        ],
        flops=2 * cells * channels * 4 * hidden,
    )
    return grad


def normalize(values, reduce_axis):
    mean_value = jnp.mean(values, axis=reduce_axis, keepdims=True)
    centered = values - mean_value
    variance = jnp.mean(centered * centered, axis=reduce_axis, keepdims=True)
    inv_std = lax.rsqrt(variance + 1e-05)
    return (centered * inv_std, inv_std)


def norm_backward(upstream, normed, inv_std, reduce_axis):
    mean_grad = jnp.mean(upstream, axis=reduce_axis, keepdims=True)
    mean_cross = jnp.mean(upstream * normed, axis=reduce_axis, keepdims=True)
    return inv_std * (upstream - mean_grad - normed * mean_cross)


def shards(
    pair,
    cotangent,
    residue_mask,
    ln_in_gain,
    ln_in_bias,
    w_proj,
    w_gate,
    ln_out_gain,
    ln_out_bias,
    w_out,
):
    local_rows = pair.shape[0]
    local_cols = pair.shape[1]
    hidden = w_out.shape[0]
    chan_index = lax.axis_index("chan")
    row_start = lax.axis_index("row") * local_rows
    col_start = chan_index * local_cols
    mask_float = residue_mask.astype(jnp.float32)
    row_mask = lax.dynamic_slice_in_dim(mask_float, row_start, local_rows)
    col_mask = lax.dynamic_slice_in_dim(mask_float, col_start, local_cols)
    cell_mask = (row_mask[:, None] * col_mask[None, :])[None]
    normed, inv_std = normalize(pair.astype(jnp.float32), -1)
    normed_pair = (normed * ln_in_gain + ln_in_bias).astype(jnp.bfloat16)
    projected = jnp.einsum("rmc,ch->hrm", normed_pair, w_proj, preferred_element_type=jnp.float32)
    left_panel = (
        cell_mask * jax.nn.sigmoid(projected[:hidden]) * projected[hidden : 2 * hidden]
    ).astype(jnp.bfloat16)
    right_panel = (
        cell_mask * jax.nn.sigmoid(projected[2 * hidden : 3 * hidden]) * projected[3 * hidden :]
    ).astype(jnp.bfloat16)
    panels = lax.all_to_all(
        jnp.stack([left_panel, right_panel]), "row", split_axis=1, concat_axis=2, tiled=True
    )
    left_all = panels[0]
    right_all = panels[1]
    right_rows = lax.all_to_all(right_all, "chan", split_axis=1, concat_axis=2, tiled=True)
    partner = right_rows
    tri_part = jnp.einsum(
        "gik,gjk->gij",
        lax.all_gather(left_all, "chan", axis=2, tiled=True),
        partner,
        preferred_element_type=jnp.float32,
    ).astype(jnp.bfloat16)
    tri_cells = lax.all_to_all(tri_part, "row", split_axis=1, concat_axis=0, tiled=True)
    tri_hat, inv_tri = normalize(tri_cells.astype(jnp.float32), 0)
    scaled = (tri_hat * ln_out_gain[:, None, None] + ln_out_bias[:, None, None]).astype(
        jnp.bfloat16
    )
    proj_out = jnp.einsum("hrm,hc->rmc", scaled, w_out, preferred_element_type=jnp.float32)
    gate_value = jax.nn.sigmoid(
        jnp.einsum("rmc,cd->rmd", normed_pair, w_gate, preferred_element_type=jnp.float32)
    )
    cot_float = cotangent.astype(jnp.float32)
    d_gate_pre = (cot_float * proj_out * gate_value * (1.0 - gate_value)).astype(jnp.bfloat16)
    d_scaled = (cot_float * gate_value).astype(jnp.bfloat16)
    d_hat = jnp.einsum("rmc,hc->hrm", d_scaled, w_out, preferred_element_type=jnp.float32)
    d_hat = d_hat * ln_out_gain[:, None, None]
    d_tri = norm_backward(d_hat, tri_hat, inv_tri, 0).astype(jnp.bfloat16)
    d_tri_all = lax.all_to_all(d_tri, "row", split_axis=0, concat_axis=1, tiled=True)
    panel_piece = lax.all_gather(d_tri_all, "chan", axis=2, tiled=True)
    partner = right_all
    d_left = jnp.einsum("gij,gjk->gik", panel_piece, partner, preferred_element_type=jnp.float32)
    contribution = jnp.einsum(
        "gij,gik->gjk", panel_piece, left_all, preferred_element_type=jnp.float32
    )
    d_right = contribution
    d_left, d_right = (d_left, d_right)
    d_stack = jnp.stack([d_left, d_right]).astype(jnp.bfloat16)
    d_panels = lax.all_to_all(d_stack, "row", split_axis=2, concat_axis=1, tiled=True)

    def gating(d_value, gate_proj, value_proj):
        sigmoid_val = jax.nn.sigmoid(gate_proj)
        masked_grad = d_value.astype(jnp.float32) * cell_mask
        return (
            masked_grad * value_proj * sigmoid_val * (1.0 - sigmoid_val),
            masked_grad * sigmoid_val,
        )

    gate_left, value_left = gating(d_panels[0], projected[:hidden], projected[hidden : 2 * hidden])
    gate_right, value_right = gating(
        d_panels[1], projected[2 * hidden : 3 * hidden], projected[3 * hidden :]
    )
    d_proj = jnp.concatenate([gate_left, value_left, gate_right, value_right], axis=0).astype(
        jnp.bfloat16
    )
    d_normed = jnp.einsum("hrm,ch->rmc", d_proj, w_proj, preferred_element_type=jnp.float32)
    d_normed = d_normed + jnp.einsum(
        "rmd,cd->rmc", d_gate_pre, w_gate, preferred_element_type=jnp.float32
    )
    d_input = d_normed * ln_in_gain
    return norm_backward(d_input, normed, inv_std, -1).astype(jnp.bfloat16)


def solution(mesh):
    fits = mesh.shape["chan"] == 1 and mesh.shape["row"] in (8, 16)
    return jax.shard_map(
        kernel_shards if fits else shards,
        mesh=mesh,
        in_specs=(
            P(("grp", "row"), "chan", None),
            P(("grp", "row"), "chan", None),
            P("grp"),
            P(),
            P(),
            P(),
            P(),
            P(),
            P(),
            P(),
        ),
        out_specs=P(("grp", "row"), "chan", None),
        check_vma=False,
    )
```

```python
import functools

import jax
import jax.numpy as jnp
from jax import lax
from jax.experimental import pallas as pl
from jax.experimental.pallas import tpu as pltpu
from jax.sharding import PartitionSpec as P

F32 = jnp.float32
BF16 = jnp.bfloat16
VMEM_LIMIT = 16 * 1024 * 1024


def dot(lhs, rhs, lhs_dim, rhs_dim):
    return lax.dot_general(
        lhs, rhs, (((lhs_dim,), (rhs_dim,)), ((), ())), preferred_element_type=F32
    )


def transposed(matrix):
    return jnp.transpose(matrix.astype(F32)).astype(BF16)


def sigmoid(values):
    return 1.0 / (1.0 + jnp.exp(-values))


def column(row):
    size = row.shape[1]
    return jnp.transpose(jnp.broadcast_to(row, (size, size)))


def norm_rows(values):
    centered = values - jnp.mean(values, axis=0, keepdims=True)
    variance = jnp.mean(centered * centered, axis=0, keepdims=True)
    inv_std = lax.rsqrt(variance + 1e-05)
    return centered * inv_std, inv_std


def call(
    kernel, name, outs, args, fetched=(), columns={}, unread=(), scratch=(), flops=0, limit=VMEM_LIMIT
):
    moved = sum(a.size * a.dtype.itemsize for a in args) + sum(
        o.size * jnp.dtype(o.dtype).itemsize for o in outs
    )
    n_args, n_outs, n_fetched = len(args), len(outs), len(fetched)

    def body(*refs):
        ins = list(refs[:n_args])
        rest = refs[n_args + n_outs :]
        copies = []
        for n, place in enumerate(fetched):
            source = ins[place].at[:, columns[place]] if place in columns else ins[place]
            copies.append(pltpu.make_async_copy(source, rest[n], rest[n_fetched].at[n]))
            ins[place] = rest[n]
        for copy in copies:
            copy.start()
        for copy in copies:
            copy.wait()
        kernel(*ins, *refs[n_args : n_args + n_outs], *rest[n_fetched + (n_fetched > 0) :])

    buffers = [
        pltpu.VMEM(
            (*args[place].shape[:-1], columns[place].size) if place in columns else args[place].shape,
            args[place].dtype,
        )
        for place in fetched
    ]
    if fetched:
        buffers.append(pltpu.SemaphoreType.DMA((n_fetched,)))
    return pl.pallas_call(
        body,
        name=name,
        out_shape=outs,
        in_specs=[
            pl.BlockSpec(
                memory_space=pltpu.HBM if n in fetched else pl.ANY if n in unread else pltpu.VMEM
            )
            for n in range(n_args)
        ],
        out_specs=[pl.BlockSpec(memory_space=pltpu.VMEM) for _ in outs],
        scratch_shapes=buffers + list(scratch),
        compiler_params=pltpu.CompilerParams(vmem_limit_bytes=limit),
        cost_estimate=pl.CostEstimate(flops=flops, bytes_accessed=moved, transcendentals=0),
    )(*args)


def cell_masks(mask, rows):
    columns = mask[...].astype(F32)
    shape = (rows, columns.shape[1])
    first = lax.axis_index("row") * rows
    own = lax.broadcasted_iota(jnp.int32, shape, 1) == (
        lax.broadcasted_iota(jnp.int32, shape, 0) + first
    )
    row_mask = jnp.sum(jnp.where(own, columns, 0.0), axis=1, keepdims=True)
    cells = row_mask * columns
    return [cells[row : row + 1] for row in range(rows)]


def wide_order(devices, count, back):
    order = []
    for place in range(count):
        if back:
            order += [place ^ (count // 2), count + place]
        else:
            order += [count + (place ^ 2), place ^ (count // 2)]
    return order


def distance(step, count):
    far = sorted(range(3, count), key=lambda apart: -(apart // 2))
    return [*range(min(3, count)), *far][step]


def partner(step, count):
    return lax.rem(lax.axis_index("row"), count) ^ distance(step, count)


def gated_rows(pair, mask, gain, bias, w_side):
    rows = pair.shape[0]
    hidden = w_side.shape[1] // 2
    w_flip = transposed(w_side[...])
    gain_col, bias_col = column(gain[...]), column(bias[...])
    masks = cell_masks(mask, rows)
    for row in range(rows):
        normed, _ = norm_rows(jnp.transpose(pair[row].astype(F32)))
        zln = (normed * gain_col + bias_col).astype(BF16)
        proj = dot(w_flip, zln, 1, 0)
        yield row, masks[row] * sigmoid(proj[:hidden]) * proj[hidden:]


def project_right_kernel(pair, mask, gain, bias, w_side, right_panel):
    rows = pair.shape[0]
    devices, depth, width = right_panel.shape
    block = depth // rows
    count = w_side.shape[1] // 2 // block
    for row, right in gated_rows(pair, mask, gain, bias, w_side):
        right = right.reshape(count, block, width).astype(BF16)
        for rank in range(devices):
            place = wide_order(devices, count, False)[rank] % count
            right_panel[rank, row * block : (row + 1) * block, :] = right[place]


def project_left_kernel(pair, mask, gain, bias, w_side, after, *refs):
    del after
    *pieces, left_panel = refs
    rows = pair.shape[0]
    count, depth, width = left_panel.shape
    block = depth // rows
    for row, left in gated_rows(pair, mask, gain, bias, w_side):
        left = left.reshape(count, block, width).astype(BF16)
        left_panel[:, row * block : (row + 1) * block, :] = left
    for step, piece in enumerate(pieces):
        piece[...] = left_panel[partner(step, count)]


def prepare_kernel(
    pair, cotangent, gain, bias, w_gate, out_gain, w_out, d_hat_centered, gate_slope
):
    gate_flip = transposed(w_gate[...])
    gain_col, bias_col = column(gain[...]), column(bias[...])
    out_gain_col = column(out_gain[...])
    for row in range(pair.shape[0]):
        normed, _ = norm_rows(jnp.transpose(pair[row].astype(F32)))
        zln = (normed * gain_col + bias_col).astype(BF16)
        gate = sigmoid(dot(gate_flip, zln, 1, 0))
        cot = jnp.transpose(cotangent[row].astype(F32))
        d_scaled = (cot * gate).astype(BF16)
        d_hat = dot(w_out[...], d_scaled, 1, 0) * out_gain_col
        d_hat_centered[row] = d_hat - jnp.mean(d_hat, axis=0, keepdims=True)
        gate_slope[row] = cot * gate * (1.0 - gate)


def spread(panel, wide):
    wide[...] = panel[...].astype(F32).reshape(wide.shape)


def wide_places(panel, count, back):
    devices, depth, _ = panel.shape
    for rank, device in enumerate(wide_order(devices, count, back)):
        yield rank, slice(device * depth, (device + 1) * depth)


def sort_left_kernel(*refs):
    *pieces, left_all, left_pairs, left_wide = refs
    block, left_rows, _ = left_all.shape
    depth = pieces[0].shape[0]
    for step, piece in enumerate(pieces):
        start = pl.multiple_of(partner(step, len(pieces)) * depth, depth)
        left_wide[pl.ds(start, depth), :] = piece[...].astype(F32)
    for h in range(block):
        left_all[h] = left_wide[pl.ds(h, left_rows, stride=block), :].astype(BF16)
    empty = jnp.zeros(left_all.shape[1:], BF16)
    for n in range(block // 2):
        left_pairs[n, :left_rows, :] = jnp.concatenate([left_all[2 * n], empty], axis=1)
        left_pairs[n, left_rows:, :] = jnp.concatenate([empty, left_all[2 * n + 1]], axis=1)


def tri_kernel(right_panel, left_all, after, products, right_all, left_wide, right_wide):
    del after
    block, left_rows, _ = left_all.shape
    right_rows = right_all.shape[1]
    for rank, place in wide_places(right_panel, products.shape[0], False):
        right_wide[place, :] = right_panel[rank].astype(F32)
    for h in range(block):
        right = right_wide[pl.ds(h, right_rows, stride=block), :].astype(BF16)
        right_all[h] = right
        left_wide[pl.ds(h, left_rows, stride=block), :] = dot(left_all[h], right, 1, 1)
    products[...] = left_wide[...].astype(BF16).reshape(products.shape)


def cell_row(ref, row, rows):
    count, depth, width = ref.shape
    block = depth // rows
    return ref[:, row * block : (row + 1) * block, :].astype(F32).reshape(count * block, width)


def middle_kernel(products, d_hat_centered, d_products):
    rows = d_hat_centered.shape[0]
    count, depth, width = products.shape
    block = depth // rows
    for row in range(rows):
        tri_hat, inv_std = norm_rows(cell_row(products, row, rows))
        d_hat = d_hat_centered[row]
        cross = jnp.mean(d_hat * tri_hat, axis=0, keepdims=True)
        d_tri = inv_std * (d_hat - tri_hat * cross)
        d_products[:, row * block : (row + 1) * block, :] = d_tri.reshape(
            count, block, width
        ).astype(BF16)


def d_right_kernel(d_products, left_pairs, d_right_panel, d_tri_all, left_wide, right_wide):
    block, left_rows, width = d_tri_all.shape
    right_rows = right_wide.shape[0] // block
    spread(d_products, left_wide)
    for n in range(block // 2):
        pair = (2 * n, 2 * n + 1)
        d_tri = [left_wide[pl.ds(h, left_rows, stride=block), :] for h in pair]
        d_tri = jnp.concatenate(d_tri, axis=0).astype(BF16)
        d_right = dot(d_tri, left_pairs[n], 0, 0)
        for side, h in enumerate(pair):
            d_tri_all[h] = d_tri[side * left_rows : (side + 1) * left_rows]
            right_wide[pl.ds(h, right_rows, stride=block), :] = d_right[
                :, side * width : (side + 1) * width
            ]
    for rank, place in wide_places(d_right_panel, d_products.shape[0], True):
        d_right_panel[rank] = right_wide[place, :].astype(BF16)


def d_left_kernel(d_tri_all, right_all, *refs):
    *pieces, left_wide = refs
    block, left_rows, _ = d_tri_all.shape
    for h in range(block):
        left_wide[pl.ds(h, left_rows, stride=block), :] = dot(d_tri_all[h], right_all[h], 1, 0)
    depth = pieces[0].shape[0]
    for step, piece in enumerate(pieces):
        start = pl.multiple_of(partner(step, len(pieces)) * depth, depth)
        piece[...] = left_wide[pl.ds(start, depth), :].astype(BF16)


def gate_back_kernel(products, gate_slope, out_gain, out_bias, w_out, d_gate_pre):
    rows = gate_slope.shape[0]
    out_flip = transposed(w_out[...])
    out_gain_col, out_bias_col = column(out_gain[...]), column(out_bias[...])
    for row in range(rows):
        tri_hat, _ = norm_rows(cell_row(products, row, rows))
        scaled = (tri_hat * out_gain_col + out_bias_col).astype(BF16)
        d_gate_pre[row] = (dot(out_flip, scaled, 1, 0) * gate_slope[row]).astype(BF16)


def slopes_kernel(
    pair, mask, gain, bias, w_proj, w_gate, after, slopes, normed_in, inv_in, in_gain, weights
):
    del after
    rows = pair.shape[0]
    hidden = w_proj.shape[1] // 4
    w_flip = transposed(w_proj[...])
    gain_col, bias_col = column(gain[...]), column(bias[...])
    in_gain[...] = gain_col
    weights[...] = jnp.concatenate([w_proj[...], w_gate[...]], axis=1)
    masks = cell_masks(mask, rows)
    for row in range(rows):
        normed, inv_std = norm_rows(jnp.transpose(pair[row].astype(F32)))
        normed_in[row] = normed.astype(normed_in.dtype)
        inv_in[row : row + 1] = inv_std
        zln = (normed * gain_col + bias_col).astype(BF16)
        proj = dot(w_flip, zln, 1, 0)
        for side in range(2):
            base = 2 * side * hidden
            sig = sigmoid(proj[base : base + hidden])
            masked = masks[row] * sig
            value = masked * (1.0 - sig) * proj[base + hidden : base + 2 * hidden]
            slopes[row, base : base + hidden, :] = value.astype(slopes.dtype)
            slopes[row, base + hidden : base + 2 * hidden, :] = masked.astype(slopes.dtype)


def sloped(d_value, slopes, row, side):
    hidden = d_value.shape[0]
    parts = []
    for base in (2 * side * hidden, (2 * side + 1) * hidden):
        slope = slopes[row, base : base + hidden, :].astype(F32)
        parts.append((d_value * slope).astype(BF16))
    return jnp.concatenate(parts, axis=0)


def finish_left_kernel(slopes, d_gate_pre, weights, *refs):
    *pieces, d_zln_left, panel = refs
    rows = d_zln_left.shape[0]
    for step, piece in enumerate(pieces):
        panel[partner(step, len(pieces))] = piece[...]
    half = slopes.shape[1] // 2
    own = jnp.concatenate([weights[:, :half], weights[:, 2 * half :]], axis=1)
    for row in range(rows):
        d_proj = sloped(cell_row(panel, row, rows), slopes, row, 0)
        d_zln_left[row] = dot(own, jnp.concatenate([d_proj, d_gate_pre[row]], axis=0), 1, 0)


def both_halves(blocks, count):
    order = wide_order(2 * count, count, True)
    return jnp.stack(
        [blocks[order.index(place)] + blocks[order.index(count + place)] for place in range(count)]
    )


def finish_kernel(
    d_right_panel, d_zln_left, slopes, normed_in, inv_in, gain_col, weights, grad
):
    rows = grad.shape[0]
    devices, depth, width = d_right_panel.shape
    half = slopes.shape[1] // 2
    for row in range(rows):
        d_right = cell_row(d_right_panel, row, rows)
        d_right = both_halves(d_right.reshape(devices, depth // rows, width), devices // 2)
        d_proj = sloped(d_right.reshape(half // 2, width), slopes, row, 1)
        d_zln = d_zln_left[row] + dot(weights[:, half : 2 * half], d_proj, 1, 0)
        d_in = d_zln * gain_col[...]
        normed = normed_in[row].astype(F32)
        mean_grad = jnp.mean(d_in, axis=0, keepdims=True)
        mean_cross = jnp.mean(d_in * normed, axis=0, keepdims=True)
        result = inv_in[row : row + 1] * (d_in - mean_grad - normed * mean_cross)
        grad[row] = jnp.transpose(result).astype(BF16)


def swap(values, count, back):
    groups = [wide_order(lax.axis_size("row"), count, back)]
    return lax.all_to_all(
        values, "row", split_axis=0, concat_axis=0, tiled=True, axis_index_groups=groups
    )


def swap_half(values, count):
    devices = range(lax.axis_size("row"))
    groups = [[d for d in devices if d // count == half] for half in range(len(devices) // count)]
    return lax.all_to_all(
        values, "row", split_axis=0, concat_axis=0, tiled=True, axis_index_groups=groups
    )


def swap_pieces(pieces):
    devices = range(lax.axis_size("row"))
    count = len(pieces)
    return [pieces[0]] + [
        lax.ppermute(pieces[step], "row", [(d, d ^ distance(step, count)) for d in devices])
        for step in range(1, count)
    ]


def kernel_shards(
    pair,
    cotangent,
    residue_mask,
    ln_in_gain,
    ln_in_bias,
    w_proj,
    w_gate,
    ln_out_gain,
    ln_out_bias,
    w_out,
):
    rows, width, channels = pair.shape
    hidden = w_out.shape[0]
    halves = 2
    devices = lax.axis_size("row")
    count = devices // halves
    block = hidden // count
    left_rows, right_rows = rows * count, rows * devices
    shape = jax.ShapeDtypeStruct
    panel = shape((count, rows * block, width), BF16)
    wide_panel = shape((devices, rows * block, width), BF16)
    mask = residue_mask.reshape(1, width)
    gain, bias = ln_in_gain.reshape(1, channels), ln_in_bias.reshape(1, channels)
    out_gain, out_bias = ln_out_gain.reshape(1, hidden), ln_out_bias.reshape(1, hidden)
    cells = rows * width
    piece = shape((rows * block, width), BF16)
    left_panel = pltpu.VMEM(panel.shape, BF16)
    left_wide = pltpu.VMEM((left_rows * block, width), F32)
    right_wide = pltpu.VMEM((right_rows * block, width), F32)
    (own_right,) = call(
        project_right_kernel,
        "project_right",
        [wide_panel],
        [pair, mask, gain, bias, w_proj],
        fetched=range(5),
        columns={4: pl.ds(2 * hidden, 2 * hidden)},
        flops=2 * cells * channels * 2 * hidden,
        limit=64 * 1024 * 1024 - 640 * 1024,
    )
    right_panel = swap(own_right, count, False)
    pieces = call(
        project_left_kernel,
        "project_left",
        [piece] * count,
        [pair, mask, gain, bias, w_proj, own_right],
        fetched=range(5),
        columns={4: pl.ds(0, 2 * hidden)},
        unread=(5,),
        scratch=[left_panel],
        flops=2 * cells * channels * 2 * hidden,
    )
    pieces = swap_pieces(pieces)
    left_all, left_pairs = call(
        sort_left_kernel,
        "sort_left",
        [
            shape((block, left_rows, width), BF16),
            shape((block // 2, 2 * left_rows, 2 * width), BF16),
        ],
        pieces,
        scratch=[left_wide],
    )
    d_hat_centered, gate_slope = call(
        prepare_kernel,
        "prepare",
        [shape((rows, hidden, width), F32), shape((rows, channels, width), F32)],
        [pair, cotangent, gain, bias, w_gate, out_gain, w_out],
        fetched=range(7),
        flops=2 * cells * channels * 2 * hidden,
    )
    products, right_all = call(
        tri_kernel,
        "tri",
        [panel, shape((block, right_rows, width), BF16)],
        [right_panel, left_all, d_hat_centered],
        unread=(2,),
        scratch=[left_wide, right_wide],
        flops=2 * block * left_rows * width * right_rows,
    )
    products = swap_half(products, count)
    (d_products,) = call(
        middle_kernel,
        "middle",
        [panel],
        [products, d_hat_centered],
        flops=20 * cells * hidden,
    )
    d_products = swap_half(d_products, count)
    d_right_panel, d_tri_all = call(
        d_right_kernel,
        "d_right",
        [wide_panel, shape((block, left_rows, width), BF16)],
        [d_products, left_pairs],
        scratch=[left_wide, right_wide],
        flops=2 * block * left_rows * width * right_rows,
    )
    d_right_panel = swap(d_right_panel, count, True)
    d_pieces = call(
        d_left_kernel,
        "d_left",
        [piece] * count,
        [d_tri_all, right_all],
        scratch=[left_wide],
        flops=2 * block * left_rows * width * right_rows,
    )
    d_pieces = swap_pieces(d_pieces)
    (d_gate_pre,) = call(
        gate_back_kernel,
        "gate_back",
        [shape((rows, channels, width), BF16)],
        [products, gate_slope, out_gain, out_bias, w_out],
        fetched=range(2, 5),
        flops=2 * cells * channels * hidden,
    )
    slopes, normed_in, inv_in, gain_col, weights = call(
        slopes_kernel,
        "slopes",
        [
            shape((rows, 4 * hidden, width), BF16),
            shape((rows, channels, width), BF16),
            shape((rows, width), F32),
            shape((channels, channels), F32),
            shape((channels, 4 * hidden + channels), BF16),
        ],
        [pair, mask, gain, bias, w_proj, w_gate, d_gate_pre],
        fetched=range(6),
        unread=(6,),
        flops=2 * cells * channels * 4 * hidden,
    )
    (d_zln_left,) = call(
        finish_left_kernel,
        "finish_left",
        [shape((rows, channels, width), F32)],
        [slopes, d_gate_pre, weights, *d_pieces],
        scratch=[left_panel],
        flops=2 * cells * channels * 3 * hidden,
    )
    (grad,) = call(
        finish_kernel,
        "finish",
        [shape(pair.shape, BF16)],
        [
            d_right_panel,
            d_zln_left,
            slopes,
            normed_in,
            inv_in,
            gain_col,
            weights,
        ],
        flops=2 * cells * channels * 4 * hidden,
    )
    return grad


def normalize(values, reduce_axis):
    mean_value = jnp.mean(values, axis=reduce_axis, keepdims=True)
    centered = values - mean_value
    variance = jnp.mean(centered * centered, axis=reduce_axis, keepdims=True)
    inv_std = lax.rsqrt(variance + 1e-05)
    return (centered * inv_std, inv_std)


def norm_backward(upstream, normed, inv_std, reduce_axis):
    mean_grad = jnp.mean(upstream, axis=reduce_axis, keepdims=True)
    mean_cross = jnp.mean(upstream * normed, axis=reduce_axis, keepdims=True)
    return inv_std * (upstream - mean_grad - normed * mean_cross)


def shards(
    pair,
    cotangent,
    residue_mask,
    ln_in_gain,
    ln_in_bias,
    w_proj,
    w_gate,
    ln_out_gain,
    ln_out_bias,
    w_out,
):
    local_rows = pair.shape[0]
    local_cols = pair.shape[1]
    hidden = w_out.shape[0]
    chan_index = lax.axis_index("chan")
    row_start = lax.axis_index("row") * local_rows
    col_start = chan_index * local_cols
    mask_float = residue_mask.astype(jnp.float32)
    row_mask = lax.dynamic_slice_in_dim(mask_float, row_start, local_rows)
    col_mask = lax.dynamic_slice_in_dim(mask_float, col_start, local_cols)
    cell_mask = (row_mask[:, None] * col_mask[None, :])[None]
    normed, inv_std = normalize(pair.astype(jnp.float32), -1)
    normed_pair = (normed * ln_in_gain + ln_in_bias).astype(jnp.bfloat16)
    projected = jnp.einsum("rmc,ch->hrm", normed_pair, w_proj, preferred_element_type=jnp.float32)
    left_panel = (
        cell_mask * jax.nn.sigmoid(projected[:hidden]) * projected[hidden : 2 * hidden]
    ).astype(jnp.bfloat16)
    right_panel = (
        cell_mask * jax.nn.sigmoid(projected[2 * hidden : 3 * hidden]) * projected[3 * hidden :]
    ).astype(jnp.bfloat16)
    panels = lax.all_to_all(
        jnp.stack([left_panel, right_panel]), "row", split_axis=1, concat_axis=2, tiled=True
    )
    left_all = panels[0]
    right_all = panels[1]
    right_rows = lax.all_to_all(right_all, "chan", split_axis=1, concat_axis=2, tiled=True)
    partner = right_rows
    tri_part = jnp.einsum(
        "gik,gjk->gij",
        lax.all_gather(left_all, "chan", axis=2, tiled=True),
        partner,
        preferred_element_type=jnp.float32,
    ).astype(jnp.bfloat16)
    tri_cells = lax.all_to_all(tri_part, "row", split_axis=1, concat_axis=0, tiled=True)
    tri_hat, inv_tri = normalize(tri_cells.astype(jnp.float32), 0)
    scaled = (tri_hat * ln_out_gain[:, None, None] + ln_out_bias[:, None, None]).astype(
        jnp.bfloat16
    )
    proj_out = jnp.einsum("hrm,hc->rmc", scaled, w_out, preferred_element_type=jnp.float32)
    gate_value = jax.nn.sigmoid(
        jnp.einsum("rmc,cd->rmd", normed_pair, w_gate, preferred_element_type=jnp.float32)
    )
    cot_float = cotangent.astype(jnp.float32)
    d_gate_pre = (cot_float * proj_out * gate_value * (1.0 - gate_value)).astype(jnp.bfloat16)
    d_scaled = (cot_float * gate_value).astype(jnp.bfloat16)
    d_hat = jnp.einsum("rmc,hc->hrm", d_scaled, w_out, preferred_element_type=jnp.float32)
    d_hat = d_hat * ln_out_gain[:, None, None]
    d_tri = norm_backward(d_hat, tri_hat, inv_tri, 0).astype(jnp.bfloat16)
    d_tri_all = lax.all_to_all(d_tri, "row", split_axis=0, concat_axis=1, tiled=True)
    panel_piece = lax.all_gather(d_tri_all, "chan", axis=2, tiled=True)
    partner = right_all
    d_left = jnp.einsum("gij,gjk->gik", panel_piece, partner, preferred_element_type=jnp.float32)
    contribution = jnp.einsum(
        "gij,gik->gjk", panel_piece, left_all, preferred_element_type=jnp.float32
    )
    d_right = contribution
    d_left, d_right = (d_left, d_right)
    d_stack = jnp.stack([d_left, d_right]).astype(jnp.bfloat16)
    d_panels = lax.all_to_all(d_stack, "row", split_axis=2, concat_axis=1, tiled=True)

    def gating(d_value, gate_proj, value_proj):
        sigmoid_val = jax.nn.sigmoid(gate_proj)
        masked_grad = d_value.astype(jnp.float32) * cell_mask
        return (
            masked_grad * value_proj * sigmoid_val * (1.0 - sigmoid_val),
            masked_grad * sigmoid_val,
        )

    gate_left, value_left = gating(d_panels[0], projected[:hidden], projected[hidden : 2 * hidden])
    gate_right, value_right = gating(
        d_panels[1], projected[2 * hidden : 3 * hidden], projected[3 * hidden :]
    )
    d_proj = jnp.concatenate([gate_left, value_left, gate_right, value_right], axis=0).astype(
        jnp.bfloat16
    )
    d_normed = jnp.einsum("hrm,ch->rmc", d_proj, w_proj, preferred_element_type=jnp.float32)
    d_normed = d_normed + jnp.einsum(
        "rmd,cd->rmc", d_gate_pre, w_gate, preferred_element_type=jnp.float32
    )
    d_input = d_normed * ln_in_gain
    return norm_backward(d_input, normed, inv_std, -1).astype(jnp.bfloat16)


def solution(mesh):
    fits = mesh.shape["chan"] == 1 and mesh.shape["row"] in (8, 16)
    return jax.shard_map(
        kernel_shards if fits else shards,
        mesh=mesh,
        in_specs=(
            P(("grp", "row"), "chan", None),
            P(("grp", "row"), "chan", None),
            P("grp"),
            P(),
            P(),
            P(),
            P(),
            P(),
            P(),
            P(),
        ),
        out_specs=P(("grp", "row"), "chan", None),
        check_vma=False,
    )
```

```python
import functools

import jax
import jax.numpy as jnp
from jax import lax
from jax.experimental import pallas as pl
from jax.experimental.pallas import tpu as pltpu
from jax.sharding import PartitionSpec as P

F32 = jnp.float32
BF16 = jnp.bfloat16
VMEM_LIMIT = 16 * 1024 * 1024


def dot(lhs, rhs, lhs_dim, rhs_dim):
    return lax.dot_general(
        lhs, rhs, (((lhs_dim,), (rhs_dim,)), ((), ())), preferred_element_type=F32
    )


def transposed(matrix):
    return jnp.transpose(matrix.astype(F32)).astype(BF16)


def sigmoid(values):
    return 1.0 / (1.0 + jnp.exp(-values))


def column(row):
    size = row.shape[1]
    return jnp.transpose(jnp.broadcast_to(row, (size, size)))


def norm_rows(values):
    centered = values - jnp.mean(values, axis=0, keepdims=True)
    variance = jnp.mean(centered * centered, axis=0, keepdims=True)
    inv_std = lax.rsqrt(variance + 1e-05)
    return centered * inv_std, inv_std


def call(
    kernel, name, outs, args, fetched=(), columns={}, unread=(), scratch=(), flops=0, limit=VMEM_LIMIT
):
    moved = sum(a.size * a.dtype.itemsize for a in args) + sum(
        o.size * jnp.dtype(o.dtype).itemsize for o in outs
    )
    n_args, n_outs, n_fetched = len(args), len(outs), len(fetched)

    def body(*refs):
        ins = list(refs[:n_args])
        rest = refs[n_args + n_outs :]
        copies = []
        for n, place in enumerate(fetched):
            source = ins[place].at[:, columns[place]] if place in columns else ins[place]
            copies.append(pltpu.make_async_copy(source, rest[n], rest[n_fetched].at[n]))
            ins[place] = rest[n]
        for copy in copies:
            copy.start()
        for copy in copies:
            copy.wait()
        kernel(*ins, *refs[n_args : n_args + n_outs], *rest[n_fetched + (n_fetched > 0) :])

    buffers = [
        pltpu.VMEM(
            (*args[place].shape[:-1], columns[place].size) if place in columns else args[place].shape,
            args[place].dtype,
        )
        for place in fetched
    ]
    if fetched:
        buffers.append(pltpu.SemaphoreType.DMA((n_fetched,)))
    return pl.pallas_call(
        body,
        name=name,
        out_shape=outs,
        in_specs=[
            pl.BlockSpec(
                memory_space=pltpu.HBM if n in fetched else pl.ANY if n in unread else pltpu.VMEM
            )
            for n in range(n_args)
        ],
        out_specs=[pl.BlockSpec(memory_space=pltpu.VMEM) for _ in outs],
        scratch_shapes=buffers + list(scratch),
        compiler_params=pltpu.CompilerParams(vmem_limit_bytes=limit),
        cost_estimate=pl.CostEstimate(flops=flops, bytes_accessed=moved, transcendentals=0),
    )(*args)


def cell_masks(mask, rows):
    columns = mask[...].astype(F32)
    shape = (rows, columns.shape[1])
    first = lax.axis_index("row") * rows
    own = lax.broadcasted_iota(jnp.int32, shape, 1) == (
        lax.broadcasted_iota(jnp.int32, shape, 0) + first
    )
    row_mask = jnp.sum(jnp.where(own, columns, 0.0), axis=1, keepdims=True)
    cells = row_mask * columns
    return [cells[row : row + 1] for row in range(rows)]


def wide_order(devices, count, back):
    order = []
    for place in range(count):
        if back:
            order += [place ^ (count // 2), count + place]
        else:
            order += [count + (place ^ 2), place ^ (count // 2)]
    return order


def distance(step, count):
    far = sorted(range(3, count), key=lambda apart: -(apart // 2))
    return [*range(min(3, count)), *far][step]


def partner(step, count):
    return lax.rem(lax.axis_index("row"), count) ^ distance(step, count)


def gated_rows(pair, mask, gain, bias, w_side):
    rows = pair.shape[0]
    hidden = w_side.shape[1] // 2
    w_flip = transposed(w_side[...])
    gain_col, bias_col = column(gain[...]), column(bias[...])
    masks = cell_masks(mask, rows)
    for row in range(rows):
        normed, _ = norm_rows(jnp.transpose(pair[row].astype(F32)))
        zln = (normed * gain_col + bias_col).astype(BF16)
        proj = dot(w_flip, zln, 1, 0)
        yield row, masks[row] * sigmoid(proj[:hidden]) * proj[hidden:]


def project_right_kernel(pair, mask, gain, bias, w_side, right_panel):
    rows = pair.shape[0]
    devices, depth, width = right_panel.shape
    block = depth // rows
    count = w_side.shape[1] // 2 // block
    for row, right in gated_rows(pair, mask, gain, bias, w_side):
        right = right.reshape(count, block, width).astype(BF16)
        for rank in range(devices):
            place = wide_order(devices, count, False)[rank] % count
            right_panel[rank, row * block : (row + 1) * block, :] = right[place]


def project_left_kernel(pair, mask, gain, bias, w_side, after, *refs):
    del after
    *pieces, left_panel = refs
    rows = pair.shape[0]
    count, depth, width = left_panel.shape
    block = depth // rows
    for row, left in gated_rows(pair, mask, gain, bias, w_side):
        left = left.reshape(count, block, width).astype(BF16)
        left_panel[:, row * block : (row + 1) * block, :] = left
    for step, piece in enumerate(pieces):
        piece[...] = left_panel[partner(step, count)]


def prepare_kernel(
    pair, cotangent, gain, bias, w_gate, out_gain, w_out, d_hat_centered, gate_slope
):
    gate_flip = transposed(w_gate[...])
    gain_col, bias_col = column(gain[...]), column(bias[...])
    out_gain_col = column(out_gain[...])
    for row in range(pair.shape[0]):
        normed, _ = norm_rows(jnp.transpose(pair[row].astype(F32)))
        zln = (normed * gain_col + bias_col).astype(BF16)
        gate = sigmoid(dot(gate_flip, zln, 1, 0))
        cot = jnp.transpose(cotangent[row].astype(F32))
        d_scaled = (cot * gate).astype(BF16)
        d_hat = dot(w_out[...], d_scaled, 1, 0) * out_gain_col
        d_hat_centered[row] = d_hat - jnp.mean(d_hat, axis=0, keepdims=True)
        gate_slope[row] = cot * gate * (1.0 - gate)


def spread(panel, wide):
    wide[...] = panel[...].astype(F32).reshape(wide.shape)


def wide_places(panel, count, back):
    devices, depth, _ = panel.shape
    for rank, device in enumerate(wide_order(devices, count, back)):
        yield rank, slice(device * depth, (device + 1) * depth)


def sort_left_kernel(*refs):
    *pieces, left_all, left_wide = refs
    block, left_rows, _ = left_all.shape
    depth = pieces[0].shape[0]
    for step, piece in enumerate(pieces):
        start = pl.multiple_of(partner(step, len(pieces)) * depth, depth)
        left_wide[pl.ds(start, depth), :] = piece[...].astype(F32)
    for h in range(block):
        left_all[h] = left_wide[pl.ds(h, left_rows, stride=block), :].astype(BF16)


def tri_kernel(right_panel, left_all, after, products, right_all, left_wide, right_wide):
    del after
    block, left_rows, _ = left_all.shape
    right_rows = right_all.shape[1]
    for rank, place in wide_places(right_panel, products.shape[0], False):
        right_wide[place, :] = right_panel[rank].astype(F32)
    for h in range(block):
        right = right_wide[pl.ds(h, right_rows, stride=block), :].astype(BF16)
        right_all[h] = right
        left_wide[pl.ds(h, left_rows, stride=block), :] = dot(left_all[h], right, 1, 1)
    products[...] = left_wide[...].astype(BF16).reshape(products.shape)


def cell_row(ref, row, rows):
    count, depth, width = ref.shape
    block = depth // rows
    return ref[:, row * block : (row + 1) * block, :].astype(F32).reshape(count * block, width)


def middle_kernel(products, d_hat_centered, d_products):
    rows = d_hat_centered.shape[0]
    count, depth, width = products.shape
    block = depth // rows
    for row in range(rows):
        tri_hat, inv_std = norm_rows(cell_row(products, row, rows))
        d_hat = d_hat_centered[row]
        cross = jnp.mean(d_hat * tri_hat, axis=0, keepdims=True)
        d_tri = inv_std * (d_hat - tri_hat * cross)
        d_products[:, row * block : (row + 1) * block, :] = d_tri.reshape(
            count, block, width
        ).astype(BF16)


def d_right_kernel(d_products, left_all, d_right_panel, d_tri_all, left_wide, right_wide):
    block, left_rows, _ = left_all.shape
    right_rows = right_wide.shape[0] // block
    spread(d_products, left_wide)
    for h in range(block):
        d_tri = left_wide[pl.ds(h, left_rows, stride=block), :].astype(BF16)
        d_tri_all[h] = d_tri
        right_wide[pl.ds(h, right_rows, stride=block), :] = dot(d_tri, left_all[h], 0, 0)
    for rank, place in wide_places(d_right_panel, d_products.shape[0], True):
        d_right_panel[rank] = right_wide[place, :].astype(BF16)


def d_left_kernel(d_tri_all, right_all, *refs):
    *pieces, left_wide = refs
    block, left_rows, _ = d_tri_all.shape
    for h in range(block):
        left_wide[pl.ds(h, left_rows, stride=block), :] = dot(d_tri_all[h], right_all[h], 1, 0)
    depth = pieces[0].shape[0]
    for step, piece in enumerate(pieces):
        start = pl.multiple_of(partner(step, len(pieces)) * depth, depth)
        piece[...] = left_wide[pl.ds(start, depth), :].astype(BF16)


def gate_back_kernel(products, gate_slope, out_gain, out_bias, w_out, d_gate_pre):
    rows = gate_slope.shape[0]
    out_flip = transposed(w_out[...])
    out_gain_col, out_bias_col = column(out_gain[...]), column(out_bias[...])
    for row in range(rows):
        tri_hat, _ = norm_rows(cell_row(products, row, rows))
        scaled = (tri_hat * out_gain_col + out_bias_col).astype(BF16)
        d_gate_pre[row] = (dot(out_flip, scaled, 1, 0) * gate_slope[row]).astype(BF16)


def slopes_kernel(
    pair, mask, gain, bias, w_proj, w_gate, after, slopes, normed_in, inv_in, in_gain, weights
):
    del after
    rows = pair.shape[0]
    hidden = w_proj.shape[1] // 4
    w_flip = transposed(w_proj[...])
    gain_col, bias_col = column(gain[...]), column(bias[...])
    in_gain[...] = gain_col
    weights[...] = jnp.concatenate([w_proj[...], w_gate[...]], axis=1)
    masks = cell_masks(mask, rows)
    for row in range(rows):
        normed, inv_std = norm_rows(jnp.transpose(pair[row].astype(F32)))
        normed_in[row] = normed.astype(normed_in.dtype)
        inv_in[row : row + 1] = inv_std
        zln = (normed * gain_col + bias_col).astype(BF16)
        proj = dot(w_flip, zln, 1, 0)
        for side in range(2):
            base = 2 * side * hidden
            sig = sigmoid(proj[base : base + hidden])
            masked = masks[row] * sig
            value = masked * (1.0 - sig) * proj[base + hidden : base + 2 * hidden]
            slopes[row, base : base + hidden, :] = value.astype(slopes.dtype)
            slopes[row, base + hidden : base + 2 * hidden, :] = masked.astype(slopes.dtype)


def sloped(d_value, slopes, row, side):
    hidden = d_value.shape[0]
    parts = []
    for base in (2 * side * hidden, (2 * side + 1) * hidden):
        slope = slopes[row, base : base + hidden, :].astype(F32)
        parts.append((d_value * slope).astype(BF16))
    return jnp.concatenate(parts, axis=0)


def finish_left_kernel(slopes, d_gate_pre, weights, *refs):
    *pieces, d_zln_left, panel = refs
    rows = d_zln_left.shape[0]
    for step, piece in enumerate(pieces):
        panel[partner(step, len(pieces))] = piece[...]
    half = slopes.shape[1] // 2
    own = jnp.concatenate([weights[:, :half], weights[:, 2 * half :]], axis=1)
    for row in range(rows):
        d_proj = sloped(cell_row(panel, row, rows), slopes, row, 0)
        d_zln_left[row] = dot(own, jnp.concatenate([d_proj, d_gate_pre[row]], axis=0), 1, 0)


def both_halves(blocks, count):
    order = wide_order(2 * count, count, True)
    return jnp.stack(
        [blocks[order.index(place)] + blocks[order.index(count + place)] for place in range(count)]
    )


def finish_kernel(
    d_right_panel, d_zln_left, slopes, normed_in, inv_in, gain_col, weights, grad
):
    rows = grad.shape[0]
    devices, depth, width = d_right_panel.shape
    half = slopes.shape[1] // 2
    for row in range(rows):
        d_right = cell_row(d_right_panel, row, rows)
        d_right = both_halves(d_right.reshape(devices, depth // rows, width), devices // 2)
        d_proj = sloped(d_right.reshape(half // 2, width), slopes, row, 1)
        d_zln = d_zln_left[row] + dot(weights[:, half : 2 * half], d_proj, 1, 0)
        d_in = d_zln * gain_col[...]
        normed = normed_in[row].astype(F32)
        mean_grad = jnp.mean(d_in, axis=0, keepdims=True)
        mean_cross = jnp.mean(d_in * normed, axis=0, keepdims=True)
        result = inv_in[row : row + 1] * (d_in - mean_grad - normed * mean_cross)
        grad[row] = jnp.transpose(result).astype(BF16)


def swap(values, count, back):
    groups = [wide_order(lax.axis_size("row"), count, back)]
    return lax.all_to_all(
        values, "row", split_axis=0, concat_axis=0, tiled=True, axis_index_groups=groups
    )


def swap_half(values, count):
    devices = range(lax.axis_size("row"))
    groups = [[d for d in devices if d // count == half] for half in range(len(devices) // count)]
    return lax.all_to_all(
        values, "row", split_axis=0, concat_axis=0, tiled=True, axis_index_groups=groups
    )


def swap_pieces(pieces):
    devices = range(lax.axis_size("row"))
    count = len(pieces)
    return [pieces[0]] + [
        lax.ppermute(pieces[step], "row", [(d, d ^ distance(step, count)) for d in devices])
        for step in range(1, count)
    ]


def kernel_shards(
    pair,
    cotangent,
    residue_mask,
    ln_in_gain,
    ln_in_bias,
    w_proj,
    w_gate,
    ln_out_gain,
    ln_out_bias,
    w_out,
):
    rows, width, channels = pair.shape
    hidden = w_out.shape[0]
    halves = 2
    devices = lax.axis_size("row")
    count = devices // halves
    block = hidden // count
    left_rows, right_rows = rows * count, rows * devices
    shape = jax.ShapeDtypeStruct
    panel = shape((count, rows * block, width), BF16)
    wide_panel = shape((devices, rows * block, width), BF16)
    mask = residue_mask.reshape(1, width)
    gain, bias = ln_in_gain.reshape(1, channels), ln_in_bias.reshape(1, channels)
    out_gain, out_bias = ln_out_gain.reshape(1, hidden), ln_out_bias.reshape(1, hidden)
    cells = rows * width
    piece = shape((rows * block, width), BF16)
    left_panel = pltpu.VMEM(panel.shape, BF16)
    left_wide = pltpu.VMEM((left_rows * block, width), F32)
    right_wide = pltpu.VMEM((right_rows * block, width), F32)
    (own_right,) = call(
        project_right_kernel,
        "project_right",
        [wide_panel],
        [pair, mask, gain, bias, w_proj],
        fetched=range(5),
        columns={4: pl.ds(2 * hidden, 2 * hidden)},
        flops=2 * cells * channels * 2 * hidden,
        limit=64 * 1024 * 1024 - 640 * 1024,
    )
    right_panel = swap(own_right, count, False)
    pieces = call(
        project_left_kernel,
        "project_left",
        [piece] * count,
        [pair, mask, gain, bias, w_proj, own_right],
        fetched=range(5),
        columns={4: pl.ds(0, 2 * hidden)},
        unread=(5,),
        scratch=[left_panel],
        flops=2 * cells * channels * 2 * hidden,
    )
    pieces = swap_pieces(pieces)
    (left_all,) = call(
        sort_left_kernel,
        "sort_left",
        [shape((block, left_rows, width), BF16)],
        pieces,
        scratch=[left_wide],
    )
    d_hat_centered, gate_slope = call(
        prepare_kernel,
        "prepare",
        [shape((rows, hidden, width), F32), shape((rows, channels, width), F32)],
        [pair, cotangent, gain, bias, w_gate, out_gain, w_out],
        fetched=range(7),
        flops=2 * cells * channels * 2 * hidden,
    )
    products, right_all = call(
        tri_kernel,
        "tri",
        [panel, shape((block, right_rows, width), BF16)],
        [right_panel, left_all, d_hat_centered],
        unread=(2,),
        scratch=[left_wide, right_wide],
        flops=2 * block * left_rows * width * right_rows,
    )
    products = swap_half(products, count)
    (d_products,) = call(
        middle_kernel,
        "middle",
        [panel],
        [products, d_hat_centered],
        flops=20 * cells * hidden,
    )
    d_products = swap_half(d_products, count)
    d_right_panel, d_tri_all = call(
        d_right_kernel,
        "d_right",
        [wide_panel, shape((block, left_rows, width), BF16)],
        [d_products, left_all],
        scratch=[left_wide, right_wide],
        flops=2 * block * left_rows * width * right_rows,
    )
    d_right_panel = swap(d_right_panel, count, True)
    d_pieces = call(
        d_left_kernel,
        "d_left",
        [piece] * count,
        [d_tri_all, right_all],
        scratch=[left_wide],
        flops=2 * block * left_rows * width * right_rows,
    )
    d_pieces = swap_pieces(d_pieces)
    (d_gate_pre,) = call(
        gate_back_kernel,
        "gate_back",
        [shape((rows, channels, width), BF16)],
        [products, gate_slope, out_gain, out_bias, w_out],
        fetched=range(2, 5),
        flops=2 * cells * channels * hidden,
    )
    slopes, normed_in, inv_in, gain_col, weights = call(
        slopes_kernel,
        "slopes",
        [
            shape((rows, 4 * hidden, width), BF16),
            shape((rows, channels, width), BF16),
            shape((rows, width), F32),
            shape((channels, channels), F32),
            shape((channels, 4 * hidden + channels), BF16),
        ],
        [pair, mask, gain, bias, w_proj, w_gate, d_gate_pre],
        fetched=range(6),
        unread=(6,),
        flops=2 * cells * channels * 4 * hidden,
    )
    (d_zln_left,) = call(
        finish_left_kernel,
        "finish_left",
        [shape((rows, channels, width), F32)],
        [slopes, d_gate_pre, weights, *d_pieces],
        scratch=[left_panel],
        flops=2 * cells * channels * 3 * hidden,
    )
    (grad,) = call(
        finish_kernel,
        "finish",
        [shape(pair.shape, BF16)],
        [
            d_right_panel,
            d_zln_left,
            slopes,
            normed_in,
            inv_in,
            gain_col,
            weights,
        ],
        flops=2 * cells * channels * 4 * hidden,
    )
    return grad


def normalize(values, reduce_axis):
    mean_value = jnp.mean(values, axis=reduce_axis, keepdims=True)
    centered = values - mean_value
    variance = jnp.mean(centered * centered, axis=reduce_axis, keepdims=True)
    inv_std = lax.rsqrt(variance + 1e-05)
    return (centered * inv_std, inv_std)


def norm_backward(upstream, normed, inv_std, reduce_axis):
    mean_grad = jnp.mean(upstream, axis=reduce_axis, keepdims=True)
    mean_cross = jnp.mean(upstream * normed, axis=reduce_axis, keepdims=True)
    return inv_std * (upstream - mean_grad - normed * mean_cross)


def shards(
    pair,
    cotangent,
    residue_mask,
    ln_in_gain,
    ln_in_bias,
    w_proj,
    w_gate,
    ln_out_gain,
    ln_out_bias,
    w_out,
):
    local_rows = pair.shape[0]
    local_cols = pair.shape[1]
    hidden = w_out.shape[0]
    chan_index = lax.axis_index("chan")
    row_start = lax.axis_index("row") * local_rows
    col_start = chan_index * local_cols
    mask_float = residue_mask.astype(jnp.float32)
    row_mask = lax.dynamic_slice_in_dim(mask_float, row_start, local_rows)
    col_mask = lax.dynamic_slice_in_dim(mask_float, col_start, local_cols)
    cell_mask = (row_mask[:, None] * col_mask[None, :])[None]
    normed, inv_std = normalize(pair.astype(jnp.float32), -1)
    normed_pair = (normed * ln_in_gain + ln_in_bias).astype(jnp.bfloat16)
    projected = jnp.einsum("rmc,ch->hrm", normed_pair, w_proj, preferred_element_type=jnp.float32)
    left_panel = (
        cell_mask * jax.nn.sigmoid(projected[:hidden]) * projected[hidden : 2 * hidden]
    ).astype(jnp.bfloat16)
    right_panel = (
        cell_mask * jax.nn.sigmoid(projected[2 * hidden : 3 * hidden]) * projected[3 * hidden :]
    ).astype(jnp.bfloat16)
    panels = lax.all_to_all(
        jnp.stack([left_panel, right_panel]), "row", split_axis=1, concat_axis=2, tiled=True
    )
    left_all = panels[0]
    right_all = panels[1]
    right_rows = lax.all_to_all(right_all, "chan", split_axis=1, concat_axis=2, tiled=True)
    partner = right_rows
    tri_part = jnp.einsum(
        "gik,gjk->gij",
        lax.all_gather(left_all, "chan", axis=2, tiled=True),
        partner,
        preferred_element_type=jnp.float32,
    ).astype(jnp.bfloat16)
    tri_cells = lax.all_to_all(tri_part, "row", split_axis=1, concat_axis=0, tiled=True)
    tri_hat, inv_tri = normalize(tri_cells.astype(jnp.float32), 0)
    scaled = (tri_hat * ln_out_gain[:, None, None] + ln_out_bias[:, None, None]).astype(
        jnp.bfloat16
    )
    proj_out = jnp.einsum("hrm,hc->rmc", scaled, w_out, preferred_element_type=jnp.float32)
    gate_value = jax.nn.sigmoid(
        jnp.einsum("rmc,cd->rmd", normed_pair, w_gate, preferred_element_type=jnp.float32)
    )
    cot_float = cotangent.astype(jnp.float32)
    d_gate_pre = (cot_float * proj_out * gate_value * (1.0 - gate_value)).astype(jnp.bfloat16)
    d_scaled = (cot_float * gate_value).astype(jnp.bfloat16)
    d_hat = jnp.einsum("rmc,hc->hrm", d_scaled, w_out, preferred_element_type=jnp.float32)
    d_hat = d_hat * ln_out_gain[:, None, None]
    d_tri = norm_backward(d_hat, tri_hat, inv_tri, 0).astype(jnp.bfloat16)
    d_tri_all = lax.all_to_all(d_tri, "row", split_axis=0, concat_axis=1, tiled=True)
    panel_piece = lax.all_gather(d_tri_all, "chan", axis=2, tiled=True)
    partner = right_all
    d_left = jnp.einsum("gij,gjk->gik", panel_piece, partner, preferred_element_type=jnp.float32)
    contribution = jnp.einsum(
        "gij,gik->gjk", panel_piece, left_all, preferred_element_type=jnp.float32
    )
    d_right = contribution
    d_left, d_right = (d_left, d_right)
    d_stack = jnp.stack([d_left, d_right]).astype(jnp.bfloat16)
    d_panels = lax.all_to_all(d_stack, "row", split_axis=2, concat_axis=1, tiled=True)

    def gating(d_value, gate_proj, value_proj):
        sigmoid_val = jax.nn.sigmoid(gate_proj)
        masked_grad = d_value.astype(jnp.float32) * cell_mask
        return (
            masked_grad * value_proj * sigmoid_val * (1.0 - sigmoid_val),
            masked_grad * sigmoid_val,
        )

    gate_left, value_left = gating(d_panels[0], projected[:hidden], projected[hidden : 2 * hidden])
    gate_right, value_right = gating(
        d_panels[1], projected[2 * hidden : 3 * hidden], projected[3 * hidden :]
    )
    d_proj = jnp.concatenate([gate_left, value_left, gate_right, value_right], axis=0).astype(
        jnp.bfloat16
    )
    d_normed = jnp.einsum("hrm,ch->rmc", d_proj, w_proj, preferred_element_type=jnp.float32)
    d_normed = d_normed + jnp.einsum(
        "rmd,cd->rmc", d_gate_pre, w_gate, preferred_element_type=jnp.float32
    )
    d_input = d_normed * ln_in_gain
    return norm_backward(d_input, normed, inv_std, -1).astype(jnp.bfloat16)


def solution(mesh):
    fits = mesh.shape["chan"] == 1 and mesh.shape["row"] in (8, 16)
    return jax.shard_map(
        kernel_shards if fits else shards,
        mesh=mesh,
        in_specs=(
            P(("grp", "row"), "chan", None),
            P(("grp", "row"), "chan", None),
            P("grp"),
            P(),
            P(),
            P(),
            P(),
            P(),
            P(),
            P(),
        ),
        out_specs=P(("grp", "row"), "chan", None),
        check_vma=False,
    )
```

```python
import functools

import jax
import jax.numpy as jnp
from jax import lax
from jax.experimental import pallas as pl
from jax.experimental.pallas import tpu as pltpu
from jax.sharding import PartitionSpec as P

F32 = jnp.float32
BF16 = jnp.bfloat16
VMEM_LIMIT = 16 * 1024 * 1024


def dot(lhs, rhs, lhs_dim, rhs_dim):
    return lax.dot_general(
        lhs, rhs, (((lhs_dim,), (rhs_dim,)), ((), ())), preferred_element_type=F32
    )


def transposed(matrix):
    return jnp.transpose(matrix.astype(F32)).astype(BF16)


def sigmoid(values):
    return 1.0 / (1.0 + jnp.exp(-values))


def column(row):
    size = row.shape[1]
    return jnp.transpose(jnp.broadcast_to(row, (size, size)))


def norm_rows(values):
    centered = values - jnp.mean(values, axis=0, keepdims=True)
    variance = jnp.mean(centered * centered, axis=0, keepdims=True)
    inv_std = lax.rsqrt(variance + 1e-05)
    return centered * inv_std, inv_std


def call(
    kernel, name, outs, args, fetched=(), columns={}, unread=(), scratch=(), flops=0, limit=VMEM_LIMIT
):
    moved = sum(a.size * a.dtype.itemsize for a in args) + sum(
        o.size * jnp.dtype(o.dtype).itemsize for o in outs
    )
    n_args, n_outs, n_fetched = len(args), len(outs), len(fetched)

    def body(*refs):
        ins = list(refs[:n_args])
        rest = refs[n_args + n_outs :]
        copies = []
        for n, place in enumerate(fetched):
            source = ins[place].at[:, columns[place]] if place in columns else ins[place]
            copies.append(pltpu.make_async_copy(source, rest[n], rest[n_fetched].at[n]))
            ins[place] = rest[n]
        for copy in copies:
            copy.start()
        for copy in copies:
            copy.wait()
        kernel(*ins, *refs[n_args : n_args + n_outs], *rest[n_fetched + (n_fetched > 0) :])

    buffers = [
        pltpu.VMEM(
            (*args[place].shape[:-1], columns[place].size) if place in columns else args[place].shape,
            args[place].dtype,
        )
        for place in fetched
    ]
    if fetched:
        buffers.append(pltpu.SemaphoreType.DMA((n_fetched,)))
    return pl.pallas_call(
        body,
        name=name,
        out_shape=outs,
        in_specs=[
            pl.BlockSpec(
                memory_space=pltpu.HBM if n in fetched else pl.ANY if n in unread else pltpu.VMEM
            )
            for n in range(n_args)
        ],
        out_specs=[pl.BlockSpec(memory_space=pltpu.VMEM) for _ in outs],
        scratch_shapes=buffers + list(scratch),
        compiler_params=pltpu.CompilerParams(vmem_limit_bytes=limit),
        cost_estimate=pl.CostEstimate(flops=flops, bytes_accessed=moved, transcendentals=0),
    )(*args)


def cell_masks(mask, rows):
    columns = mask[...].astype(F32)
    shape = (rows, columns.shape[1])
    first = lax.axis_index("row") * rows
    own = lax.broadcasted_iota(jnp.int32, shape, 1) == (
        lax.broadcasted_iota(jnp.int32, shape, 0) + first
    )
    row_mask = jnp.sum(jnp.where(own, columns, 0.0), axis=1, keepdims=True)
    cells = row_mask * columns
    return [cells[row : row + 1] for row in range(rows)]


def wide_order(devices, count, back):
    order = []
    for place in range(count):
        if back:
            order += [place ^ (count // 2), count + place]
        else:
            order += [count + (place ^ 2), place ^ (count // 2)]
    return order


def distance(step, count):
    far = sorted(range(3, count), key=lambda apart: -(apart // 2))
    return [*range(min(3, count)), *far][step]


def partner(step, count):
    return lax.rem(lax.axis_index("row"), count) ^ distance(step, count)


def gated_rows(pair, mask, gain, bias, w_side):
    rows = pair.shape[0]
    hidden = w_side.shape[1] // 2
    w_flip = transposed(w_side[...])
    gain_col, bias_col = column(gain[...]), column(bias[...])
    masks = cell_masks(mask, rows)
    for row in range(rows):
        normed, _ = norm_rows(jnp.transpose(pair[row].astype(F32)))
        zln = (normed * gain_col + bias_col).astype(BF16)
        proj = dot(w_flip, zln, 1, 0)
        yield row, masks[row] * sigmoid(proj[:hidden]) * proj[hidden:]


def project_right_kernel(pair, mask, gain, bias, w_side, right_panel):
    rows = pair.shape[0]
    devices, depth, width = right_panel.shape
    block = depth // rows
    count = w_side.shape[1] // 2 // block
    for row, right in gated_rows(pair, mask, gain, bias, w_side):
        right = right.reshape(count, block, width).astype(BF16)
        for rank in range(devices):
            place = wide_order(devices, count, False)[rank] % count
            right_panel[rank, row * block : (row + 1) * block, :] = right[place]


def project_left_kernel(pair, mask, gain, bias, w_side, after, *refs):
    del after
    *pieces, left_panel = refs
    rows = pair.shape[0]
    count, depth, width = left_panel.shape
    block = depth // rows
    for row, left in gated_rows(pair, mask, gain, bias, w_side):
        left = left.reshape(count, block, width).astype(BF16)
        left_panel[:, row * block : (row + 1) * block, :] = left
    for step, piece in enumerate(pieces):
        piece[...] = left_panel[partner(step, count)]


def prepare_kernel(
    pair, cotangent, gain, bias, w_gate, out_gain, w_out, d_hat_centered, gate_slope
):
    gate_flip = transposed(w_gate[...])
    gain_col, bias_col = column(gain[...]), column(bias[...])
    out_gain_col = column(out_gain[...])
    for row in range(pair.shape[0]):
        normed, _ = norm_rows(jnp.transpose(pair[row].astype(F32)))
        zln = (normed * gain_col + bias_col).astype(BF16)
        gate = sigmoid(dot(gate_flip, zln, 1, 0))
        cot = jnp.transpose(cotangent[row].astype(F32))
        d_scaled = (cot * gate).astype(BF16)
        d_hat = dot(w_out[...], d_scaled, 1, 0) * out_gain_col
        d_hat_centered[row] = d_hat - jnp.mean(d_hat, axis=0, keepdims=True)
        gate_slope[row] = cot * gate * (1.0 - gate)


def spread(panel, wide):
    wide[...] = panel[...].astype(F32).reshape(wide.shape)


def wide_places(panel, count, back):
    devices, depth, _ = panel.shape
    for rank, device in enumerate(wide_order(devices, count, back)):
        yield rank, slice(device * depth, (device + 1) * depth)


def sort_left_kernel(*refs):
    *pieces, left_pairs, left_wide = refs
    pairs, both_rows, both_width = left_pairs.shape
    left_rows, block = both_rows // 2, 2 * pairs
    depth = pieces[0].shape[0]
    for step, piece in enumerate(pieces):
        start = pl.multiple_of(partner(step, len(pieces)) * depth, depth)
        left_wide[pl.ds(start, depth), :] = piece[...].astype(F32)
    empty = jnp.zeros((left_rows, both_width // 2), BF16)
    for n in range(pairs):
        left = [left_wide[pl.ds(h, left_rows, stride=block), :] for h in (2 * n, 2 * n + 1)]
        left = [value.astype(BF16) for value in left]
        left_pairs[n, :left_rows, :] = jnp.concatenate([left[0], empty], axis=1)
        left_pairs[n, left_rows:, :] = jnp.concatenate([empty, left[1]], axis=1)


def left_of(left_pairs, h):
    _, both_rows, both_width = left_pairs.shape
    rows, width, side = both_rows // 2, both_width // 2, h % 2
    return left_pairs[
        h // 2, side * rows : (side + 1) * rows, side * width : (side + 1) * width
    ]


def tri_kernel(right_panel, left_pairs, after, products, right_all, left_wide, right_wide):
    del after
    block, left_rows = 2 * left_pairs.shape[0], left_pairs.shape[1] // 2
    right_rows = right_all.shape[1]
    for rank, place in wide_places(right_panel, products.shape[0], False):
        right_wide[place, :] = right_panel[rank].astype(F32)
    for h in range(block):
        right = right_wide[pl.ds(h, right_rows, stride=block), :].astype(BF16)
        right_all[h] = right
        left_wide[pl.ds(h, left_rows, stride=block), :] = dot(left_of(left_pairs, h), right, 1, 1)
    products[...] = left_wide[...].astype(BF16).reshape(products.shape)


def cell_row(ref, row, rows):
    count, depth, width = ref.shape
    block = depth // rows
    return ref[:, row * block : (row + 1) * block, :].astype(F32).reshape(count * block, width)


def middle_kernel(products, d_hat_centered, d_products):
    rows = d_hat_centered.shape[0]
    count, depth, width = products.shape
    block = depth // rows
    for row in range(rows):
        tri_hat, inv_std = norm_rows(cell_row(products, row, rows))
        d_hat = d_hat_centered[row]
        cross = jnp.mean(d_hat * tri_hat, axis=0, keepdims=True)
        d_tri = inv_std * (d_hat - tri_hat * cross)
        d_products[:, row * block : (row + 1) * block, :] = d_tri.reshape(
            count, block, width
        ).astype(BF16)


def d_right_kernel(d_products, left_pairs, d_right_panel, d_tri_all, left_wide, right_wide):
    block, left_rows, width = d_tri_all.shape
    right_rows = right_wide.shape[0] // block
    spread(d_products, left_wide)
    for n in range(block // 2):
        pair = (2 * n, 2 * n + 1)
        d_tri = [left_wide[pl.ds(h, left_rows, stride=block), :] for h in pair]
        d_tri = jnp.concatenate(d_tri, axis=0).astype(BF16)
        d_right = dot(d_tri, left_pairs[n], 0, 0)
        for side, h in enumerate(pair):
            d_tri_all[h] = d_tri[side * left_rows : (side + 1) * left_rows]
            right_wide[pl.ds(h, right_rows, stride=block), :] = d_right[
                :, side * width : (side + 1) * width
            ]
    for rank, place in wide_places(d_right_panel, d_products.shape[0], True):
        d_right_panel[rank] = right_wide[place, :].astype(BF16)


def d_left_kernel(d_tri_all, right_all, *refs):
    *pieces, left_wide = refs
    block, left_rows, _ = d_tri_all.shape
    for h in range(block):
        left_wide[pl.ds(h, left_rows, stride=block), :] = dot(d_tri_all[h], right_all[h], 1, 0)
    depth = pieces[0].shape[0]
    for step, piece in enumerate(pieces):
        start = pl.multiple_of(partner(step, len(pieces)) * depth, depth)
        piece[...] = left_wide[pl.ds(start, depth), :].astype(BF16)


def gate_back_kernel(products, gate_slope, out_gain, out_bias, w_out, d_gate_pre):
    rows = gate_slope.shape[0]
    out_flip = transposed(w_out[...])
    out_gain_col, out_bias_col = column(out_gain[...]), column(out_bias[...])
    for row in range(rows):
        tri_hat, _ = norm_rows(cell_row(products, row, rows))
        scaled = (tri_hat * out_gain_col + out_bias_col).astype(BF16)
        d_gate_pre[row] = (dot(out_flip, scaled, 1, 0) * gate_slope[row]).astype(BF16)


def slopes_kernel(
    pair, mask, gain, bias, w_proj, w_gate, after, slopes, normed_in, inv_in, in_gain, weights
):
    del after
    rows = pair.shape[0]
    hidden = w_proj.shape[1] // 4
    w_flip = transposed(w_proj[...])
    gain_col, bias_col = column(gain[...]), column(bias[...])
    in_gain[...] = gain_col
    weights[...] = jnp.concatenate([w_proj[...], w_gate[...]], axis=1)
    masks = cell_masks(mask, rows)
    for row in range(rows):
        normed, inv_std = norm_rows(jnp.transpose(pair[row].astype(F32)))
        normed_in[row] = normed.astype(normed_in.dtype)
        inv_in[row : row + 1] = inv_std
        zln = (normed * gain_col + bias_col).astype(BF16)
        proj = dot(w_flip, zln, 1, 0)
        for side in range(2):
            base = 2 * side * hidden
            sig = sigmoid(proj[base : base + hidden])
            masked = masks[row] * sig
            value = masked * (1.0 - sig) * proj[base + hidden : base + 2 * hidden]
            slopes[row, base : base + hidden, :] = value.astype(slopes.dtype)
            slopes[row, base + hidden : base + 2 * hidden, :] = masked.astype(slopes.dtype)


def sloped(d_value, slopes, row, side):
    hidden = d_value.shape[0]
    parts = []
    for base in (2 * side * hidden, (2 * side + 1) * hidden):
        slope = slopes[row, base : base + hidden, :].astype(F32)
        parts.append((d_value * slope).astype(BF16))
    return jnp.concatenate(parts, axis=0)


def finish_left_kernel(slopes, d_gate_pre, weights, *refs):
    *pieces, d_zln_left, panel = refs
    rows = d_zln_left.shape[0]
    for step, piece in enumerate(pieces):
        panel[partner(step, len(pieces))] = piece[...]
    half = slopes.shape[1] // 2
    own = jnp.concatenate([weights[:, :half], weights[:, 2 * half :]], axis=1)
    for row in range(rows):
        d_proj = sloped(cell_row(panel, row, rows), slopes, row, 0)
        d_zln_left[row] = dot(own, jnp.concatenate([d_proj, d_gate_pre[row]], axis=0), 1, 0)


def both_halves(blocks, count):
    order = wide_order(2 * count, count, True)
    return jnp.stack(
        [blocks[order.index(place)] + blocks[order.index(count + place)] for place in range(count)]
    )


def finish_kernel(
    d_right_panel, d_zln_left, slopes, normed_in, inv_in, gain_col, weights, grad
):
    rows = grad.shape[0]
    devices, depth, width = d_right_panel.shape
    half = slopes.shape[1] // 2
    for row in range(rows):
        d_right = cell_row(d_right_panel, row, rows)
        d_right = both_halves(d_right.reshape(devices, depth // rows, width), devices // 2)
        d_proj = sloped(d_right.reshape(half // 2, width), slopes, row, 1)
        d_zln = d_zln_left[row] + dot(weights[:, half : 2 * half], d_proj, 1, 0)
        d_in = d_zln * gain_col[...]
        normed = normed_in[row].astype(F32)
        mean_grad = jnp.mean(d_in, axis=0, keepdims=True)
        mean_cross = jnp.mean(d_in * normed, axis=0, keepdims=True)
        result = inv_in[row : row + 1] * (d_in - mean_grad - normed * mean_cross)
        grad[row] = jnp.transpose(result).astype(BF16)


def swap(values, count, back):
    groups = [wide_order(lax.axis_size("row"), count, back)]
    return lax.all_to_all(
        values, "row", split_axis=0, concat_axis=0, tiled=True, axis_index_groups=groups
    )


def swap_half(values, count):
    devices = range(lax.axis_size("row"))
    groups = [[d for d in devices if d // count == half] for half in range(len(devices) // count)]
    return lax.all_to_all(
        values, "row", split_axis=0, concat_axis=0, tiled=True, axis_index_groups=groups
    )


def swap_pieces(pieces):
    devices = range(lax.axis_size("row"))
    count = len(pieces)
    return [pieces[0]] + [
        lax.ppermute(pieces[step], "row", [(d, d ^ distance(step, count)) for d in devices])
        for step in range(1, count)
    ]


def kernel_shards(
    pair,
    cotangent,
    residue_mask,
    ln_in_gain,
    ln_in_bias,
    w_proj,
    w_gate,
    ln_out_gain,
    ln_out_bias,
    w_out,
):
    rows, width, channels = pair.shape
    hidden = w_out.shape[0]
    halves = 2
    devices = lax.axis_size("row")
    count = devices // halves
    block = hidden // count
    left_rows, right_rows = rows * count, rows * devices
    shape = jax.ShapeDtypeStruct
    panel = shape((count, rows * block, width), BF16)
    wide_panel = shape((devices, rows * block, width), BF16)
    mask = residue_mask.reshape(1, width)
    gain, bias = ln_in_gain.reshape(1, channels), ln_in_bias.reshape(1, channels)
    out_gain, out_bias = ln_out_gain.reshape(1, hidden), ln_out_bias.reshape(1, hidden)
    cells = rows * width
    piece = shape((rows * block, width), BF16)
    left_panel = pltpu.VMEM(panel.shape, BF16)
    left_wide = pltpu.VMEM((left_rows * block, width), F32)
    right_wide = pltpu.VMEM((right_rows * block, width), F32)
    (own_right,) = call(
        project_right_kernel,
        "project_right",
        [wide_panel],
        [pair, mask, gain, bias, w_proj],
        fetched=range(5),
        columns={4: pl.ds(2 * hidden, 2 * hidden)},
        flops=2 * cells * channels * 2 * hidden,
        limit=64 * 1024 * 1024 - 640 * 1024,
    )
    right_panel = swap(own_right, count, False)
    pieces = call(
        project_left_kernel,
        "project_left",
        [piece] * count,
        [pair, mask, gain, bias, w_proj, own_right],
        fetched=range(5),
        columns={4: pl.ds(0, 2 * hidden)},
        unread=(5,),
        scratch=[left_panel],
        flops=2 * cells * channels * 2 * hidden,
    )
    pieces = swap_pieces(pieces)
    (left_pairs,) = call(
        sort_left_kernel,
        "sort_left",
        [shape((block // 2, 2 * left_rows, 2 * width), BF16)],
        pieces,
        scratch=[left_wide],
    )
    d_hat_centered, gate_slope = call(
        prepare_kernel,
        "prepare",
        [shape((rows, hidden, width), F32), shape((rows, channels, width), F32)],
        [pair, cotangent, gain, bias, w_gate, out_gain, w_out],
        fetched=range(7),
        flops=2 * cells * channels * 2 * hidden,
    )
    products, right_all = call(
        tri_kernel,
        "tri",
        [panel, shape((block, right_rows, width), BF16)],
        [right_panel, left_pairs, d_hat_centered],
        unread=(2,),
        scratch=[left_wide, right_wide],
        flops=2 * block * left_rows * width * right_rows,
    )
    products = swap_half(products, count)
    (d_products,) = call(
        middle_kernel,
        "middle",
        [panel],
        [products, d_hat_centered],
        flops=20 * cells * hidden,
    )
    d_products = swap_half(d_products, count)
    d_right_panel, d_tri_all = call(
        d_right_kernel,
        "d_right",
        [wide_panel, shape((block, left_rows, width), BF16)],
        [d_products, left_pairs],
        scratch=[left_wide, right_wide],
        flops=2 * block * left_rows * width * right_rows,
    )
    d_right_panel = swap(d_right_panel, count, True)
    d_pieces = call(
        d_left_kernel,
        "d_left",
        [piece] * count,
        [d_tri_all, right_all],
        scratch=[left_wide],
        flops=2 * block * left_rows * width * right_rows,
    )
    d_pieces = swap_pieces(d_pieces)
    (d_gate_pre,) = call(
        gate_back_kernel,
        "gate_back",
        [shape((rows, channels, width), BF16)],
        [products, gate_slope, out_gain, out_bias, w_out],
        fetched=range(2, 5),
        flops=2 * cells * channels * hidden,
    )
    slopes, normed_in, inv_in, gain_col, weights = call(
        slopes_kernel,
        "slopes",
        [
            shape((rows, 4 * hidden, width), BF16),
            shape((rows, channels, width), BF16),
            shape((rows, width), F32),
            shape((channels, channels), F32),
            shape((channels, 4 * hidden + channels), BF16),
        ],
        [pair, mask, gain, bias, w_proj, w_gate, d_gate_pre],
        fetched=range(6),
        unread=(6,),
        flops=2 * cells * channels * 4 * hidden,
    )
    (d_zln_left,) = call(
        finish_left_kernel,
        "finish_left",
        [shape((rows, channels, width), F32)],
        [slopes, d_gate_pre, weights, *d_pieces],
        scratch=[left_panel],
        flops=2 * cells * channels * 3 * hidden,
    )
    (grad,) = call(
        finish_kernel,
        "finish",
        [shape(pair.shape, BF16)],
        [
            d_right_panel,
            d_zln_left,
            slopes,
            normed_in,
            inv_in,
            gain_col,
            weights,
        ],
        flops=2 * cells * channels * 4 * hidden,
    )
    return grad


def normalize(values, reduce_axis):
    mean_value = jnp.mean(values, axis=reduce_axis, keepdims=True)
    centered = values - mean_value
    variance = jnp.mean(centered * centered, axis=reduce_axis, keepdims=True)
    inv_std = lax.rsqrt(variance + 1e-05)
    return (centered * inv_std, inv_std)


def norm_backward(upstream, normed, inv_std, reduce_axis):
    mean_grad = jnp.mean(upstream, axis=reduce_axis, keepdims=True)
    mean_cross = jnp.mean(upstream * normed, axis=reduce_axis, keepdims=True)
    return inv_std * (upstream - mean_grad - normed * mean_cross)


def shards(
    pair,
    cotangent,
    residue_mask,
    ln_in_gain,
    ln_in_bias,
    w_proj,
    w_gate,
    ln_out_gain,
    ln_out_bias,
    w_out,
):
    local_rows = pair.shape[0]
    local_cols = pair.shape[1]
    hidden = w_out.shape[0]
    chan_index = lax.axis_index("chan")
    row_start = lax.axis_index("row") * local_rows
    col_start = chan_index * local_cols
    mask_float = residue_mask.astype(jnp.float32)
    row_mask = lax.dynamic_slice_in_dim(mask_float, row_start, local_rows)
    col_mask = lax.dynamic_slice_in_dim(mask_float, col_start, local_cols)
    cell_mask = (row_mask[:, None] * col_mask[None, :])[None]
    normed, inv_std = normalize(pair.astype(jnp.float32), -1)
    normed_pair = (normed * ln_in_gain + ln_in_bias).astype(jnp.bfloat16)
    projected = jnp.einsum("rmc,ch->hrm", normed_pair, w_proj, preferred_element_type=jnp.float32)
    left_panel = (
        cell_mask * jax.nn.sigmoid(projected[:hidden]) * projected[hidden : 2 * hidden]
    ).astype(jnp.bfloat16)
    right_panel = (
        cell_mask * jax.nn.sigmoid(projected[2 * hidden : 3 * hidden]) * projected[3 * hidden :]
    ).astype(jnp.bfloat16)
    panels = lax.all_to_all(
        jnp.stack([left_panel, right_panel]), "row", split_axis=1, concat_axis=2, tiled=True
    )
    left_all = panels[0]
    right_all = panels[1]
    right_rows = lax.all_to_all(right_all, "chan", split_axis=1, concat_axis=2, tiled=True)
    partner = right_rows
    tri_part = jnp.einsum(
        "gik,gjk->gij",
        lax.all_gather(left_all, "chan", axis=2, tiled=True),
        partner,
        preferred_element_type=jnp.float32,
    ).astype(jnp.bfloat16)
    tri_cells = lax.all_to_all(tri_part, "row", split_axis=1, concat_axis=0, tiled=True)
    tri_hat, inv_tri = normalize(tri_cells.astype(jnp.float32), 0)
    scaled = (tri_hat * ln_out_gain[:, None, None] + ln_out_bias[:, None, None]).astype(
        jnp.bfloat16
    )
    proj_out = jnp.einsum("hrm,hc->rmc", scaled, w_out, preferred_element_type=jnp.float32)
    gate_value = jax.nn.sigmoid(
        jnp.einsum("rmc,cd->rmd", normed_pair, w_gate, preferred_element_type=jnp.float32)
    )
    cot_float = cotangent.astype(jnp.float32)
    d_gate_pre = (cot_float * proj_out * gate_value * (1.0 - gate_value)).astype(jnp.bfloat16)
    d_scaled = (cot_float * gate_value).astype(jnp.bfloat16)
    d_hat = jnp.einsum("rmc,hc->hrm", d_scaled, w_out, preferred_element_type=jnp.float32)
    d_hat = d_hat * ln_out_gain[:, None, None]
    d_tri = norm_backward(d_hat, tri_hat, inv_tri, 0).astype(jnp.bfloat16)
    d_tri_all = lax.all_to_all(d_tri, "row", split_axis=0, concat_axis=1, tiled=True)
    panel_piece = lax.all_gather(d_tri_all, "chan", axis=2, tiled=True)
    partner = right_all
    d_left = jnp.einsum("gij,gjk->gik", panel_piece, partner, preferred_element_type=jnp.float32)
    contribution = jnp.einsum(
        "gij,gik->gjk", panel_piece, left_all, preferred_element_type=jnp.float32
    )
    d_right = contribution
    d_left, d_right = (d_left, d_right)
    d_stack = jnp.stack([d_left, d_right]).astype(jnp.bfloat16)
    d_panels = lax.all_to_all(d_stack, "row", split_axis=2, concat_axis=1, tiled=True)

    def gating(d_value, gate_proj, value_proj):
        sigmoid_val = jax.nn.sigmoid(gate_proj)
        masked_grad = d_value.astype(jnp.float32) * cell_mask
        return (
            masked_grad * value_proj * sigmoid_val * (1.0 - sigmoid_val),
            masked_grad * sigmoid_val,
        )

    gate_left, value_left = gating(d_panels[0], projected[:hidden], projected[hidden : 2 * hidden])
    gate_right, value_right = gating(
        d_panels[1], projected[2 * hidden : 3 * hidden], projected[3 * hidden :]
    )
    d_proj = jnp.concatenate([gate_left, value_left, gate_right, value_right], axis=0).astype(
        jnp.bfloat16
    )
    d_normed = jnp.einsum("hrm,ch->rmc", d_proj, w_proj, preferred_element_type=jnp.float32)
    d_normed = d_normed + jnp.einsum(
        "rmd,cd->rmc", d_gate_pre, w_gate, preferred_element_type=jnp.float32
    )
    d_input = d_normed * ln_in_gain
    return norm_backward(d_input, normed, inv_std, -1).astype(jnp.bfloat16)


def solution(mesh):
    fits = mesh.shape["chan"] == 1 and mesh.shape["row"] in (8, 16)
    return jax.shard_map(
        kernel_shards if fits else shards,
        mesh=mesh,
        in_specs=(
            P(("grp", "row"), "chan", None),
            P(("grp", "row"), "chan", None),
            P("grp"),
            P(),
            P(),
            P(),
            P(),
            P(),
            P(),
            P(),
        ),
        out_specs=P(("grp", "row"), "chan", None),
        check_vma=False,
    )
```

```python
import functools

import jax
import jax.numpy as jnp
from jax import lax
from jax.experimental import pallas as pl
from jax.experimental.pallas import tpu as pltpu
from jax.sharding import PartitionSpec as P

F32 = jnp.float32
BF16 = jnp.bfloat16
VMEM_LIMIT = 16 * 1024 * 1024


def dot(lhs, rhs, lhs_dim, rhs_dim):
    return lax.dot_general(
        lhs, rhs, (((lhs_dim,), (rhs_dim,)), ((), ())), preferred_element_type=F32
    )


def transposed(matrix):
    return jnp.transpose(matrix.astype(F32)).astype(BF16)


def sigmoid(values):
    return 1.0 / (1.0 + jnp.exp(-values))


def column(row):
    size = row.shape[1]
    return jnp.transpose(jnp.broadcast_to(row, (size, size)))


def norm_rows(values):
    centered = values - jnp.mean(values, axis=0, keepdims=True)
    variance = jnp.mean(centered * centered, axis=0, keepdims=True)
    inv_std = lax.rsqrt(variance + 1e-05)
    return centered * inv_std, inv_std


def call(
    kernel, name, outs, args, fetched=(), columns={}, unread=(), scratch=(), flops=0, limit=VMEM_LIMIT
):
    moved = sum(a.size * a.dtype.itemsize for a in args) + sum(
        o.size * jnp.dtype(o.dtype).itemsize for o in outs
    )
    n_args, n_outs, n_fetched = len(args), len(outs), len(fetched)

    def body(*refs):
        ins = list(refs[:n_args])
        rest = refs[n_args + n_outs :]
        copies = []
        for n, place in enumerate(fetched):
            source = ins[place].at[:, columns[place]] if place in columns else ins[place]
            copies.append(pltpu.make_async_copy(source, rest[n], rest[n_fetched].at[n]))
            ins[place] = rest[n]
        for copy in copies:
            copy.start()
        for copy in copies:
            copy.wait()
        kernel(*ins, *refs[n_args : n_args + n_outs], *rest[n_fetched + (n_fetched > 0) :])

    buffers = [
        pltpu.VMEM(
            (*args[place].shape[:-1], columns[place].size) if place in columns else args[place].shape,
            args[place].dtype,
        )
        for place in fetched
    ]
    if fetched:
        buffers.append(pltpu.SemaphoreType.DMA((n_fetched,)))
    return pl.pallas_call(
        body,
        name=name,
        out_shape=outs,
        in_specs=[
            pl.BlockSpec(
                memory_space=pltpu.HBM if n in fetched else pl.ANY if n in unread else pltpu.VMEM
            )
            for n in range(n_args)
        ],
        out_specs=[pl.BlockSpec(memory_space=pltpu.VMEM) for _ in outs],
        scratch_shapes=buffers + list(scratch),
        compiler_params=pltpu.CompilerParams(vmem_limit_bytes=limit),
        cost_estimate=pl.CostEstimate(flops=flops, bytes_accessed=moved, transcendentals=0),
    )(*args)


def cell_masks(mask, rows):
    columns = mask[...].astype(F32)
    shape = (rows, columns.shape[1])
    first = lax.axis_index("row") * rows
    own = lax.broadcasted_iota(jnp.int32, shape, 1) == (
        lax.broadcasted_iota(jnp.int32, shape, 0) + first
    )
    row_mask = jnp.sum(jnp.where(own, columns, 0.0), axis=1, keepdims=True)
    cells = row_mask * columns
    return [cells[row : row + 1] for row in range(rows)]


def wide_order(devices, count, back):
    order = []
    for place in range(count):
        if back:
            order += [place ^ (count // 2), count + place]
        else:
            order += [count + (place ^ 2), place ^ (count // 2)]
    return order


def distance(step, count):
    far = sorted(range(3, count), key=lambda apart: -(apart // 2))
    return [*range(min(3, count)), *far][step]


def partner(step, count):
    return lax.rem(lax.axis_index("row"), count) ^ distance(step, count)


def gated_rows(pair, mask, gain, bias, w_side):
    rows = pair.shape[0]
    hidden = w_side.shape[1] // 2
    w_flip = transposed(w_side[...])
    gain_col, bias_col = column(gain[...]), column(bias[...])
    masks = cell_masks(mask, rows)
    for row in range(rows):
        normed, _ = norm_rows(jnp.transpose(pair[row].astype(F32)))
        zln = (normed * gain_col + bias_col).astype(BF16)
        proj = dot(w_flip, zln, 1, 0)
        yield row, masks[row] * proj[hidden:] / (1.0 + jnp.exp(-proj[:hidden]))


def project_right_kernel(pair, mask, gain, bias, w_side, right_panel):
    rows = pair.shape[0]
    devices, depth, width = right_panel.shape
    block = depth // rows
    count = w_side.shape[1] // 2 // block
    for row, right in gated_rows(pair, mask, gain, bias, w_side):
        right = right.reshape(count, block, width).astype(BF16)
        for rank in range(devices):
            place = wide_order(devices, count, False)[rank] % count
            right_panel[rank, row * block : (row + 1) * block, :] = right[place]


def project_left_kernel(pair, mask, gain, bias, w_side, after, *refs):
    del after
    *pieces, left_panel = refs
    rows = pair.shape[0]
    count, depth, width = left_panel.shape
    block = depth // rows
    for row, left in gated_rows(pair, mask, gain, bias, w_side):
        left = left.reshape(count, block, width).astype(BF16)
        left_panel[:, row * block : (row + 1) * block, :] = left
    for step, piece in enumerate(pieces):
        piece[...] = left_panel[partner(step, count)]


def prepare_kernel(
    pair, cotangent, gain, bias, w_gate, out_gain, w_out, d_hat_centered, gate_slope
):
    gate_flip = transposed(w_gate[...])
    gain_col, bias_col = column(gain[...]), column(bias[...])
    out_gain_col = column(out_gain[...])
    for row in range(pair.shape[0]):
        normed, _ = norm_rows(jnp.transpose(pair[row].astype(F32)))
        zln = (normed * gain_col + bias_col).astype(BF16)
        gate = sigmoid(dot(gate_flip, zln, 1, 0))
        cot = jnp.transpose(cotangent[row].astype(F32))
        d_scaled = (cot * gate).astype(BF16)
        d_hat = dot(w_out[...], d_scaled, 1, 0) * out_gain_col
        d_hat_centered[row] = d_hat - jnp.mean(d_hat, axis=0, keepdims=True)
        gate_slope[row] = cot * gate * (1.0 - gate)


def spread(panel, wide):
    wide[...] = panel[...].astype(F32).reshape(wide.shape)


def wide_places(panel, count, back):
    devices, depth, _ = panel.shape
    for rank, device in enumerate(wide_order(devices, count, back)):
        yield rank, slice(device * depth, (device + 1) * depth)


def sort_left_kernel(*refs):
    *pieces, left_pairs, left_wide = refs
    pairs, both_rows, both_width = left_pairs.shape
    left_rows, block = both_rows // 2, 2 * pairs
    depth = pieces[0].shape[0]
    for step, piece in enumerate(pieces):
        start = pl.multiple_of(partner(step, len(pieces)) * depth, depth)
        left_wide[pl.ds(start, depth), :] = piece[...].astype(F32)
    empty = jnp.zeros((left_rows, both_width // 2), BF16)
    for n in range(pairs):
        left = [left_wide[pl.ds(h, left_rows, stride=block), :] for h in (2 * n, 2 * n + 1)]
        left = [value.astype(BF16) for value in left]
        left_pairs[n, :left_rows, :] = jnp.concatenate([left[0], empty], axis=1)
        left_pairs[n, left_rows:, :] = jnp.concatenate([empty, left[1]], axis=1)


def left_of(left_pairs, h):
    _, both_rows, both_width = left_pairs.shape
    rows, width, side = both_rows // 2, both_width // 2, h % 2
    return left_pairs[
        h // 2, side * rows : (side + 1) * rows, side * width : (side + 1) * width
    ]


def tri_kernel(right_panel, left_pairs, after, products, right_all, left_wide, right_wide):
    del after
    block, left_rows = 2 * left_pairs.shape[0], left_pairs.shape[1] // 2
    right_rows = right_all.shape[1]
    for rank, place in wide_places(right_panel, products.shape[0], False):
        right_wide[place, :] = right_panel[rank].astype(F32)
    for h in range(block):
        right = right_wide[pl.ds(h, right_rows, stride=block), :].astype(BF16)
        right_all[h] = right
        left_wide[pl.ds(h, left_rows, stride=block), :] = dot(left_of(left_pairs, h), right, 1, 1)
    products[...] = left_wide[...].astype(BF16).reshape(products.shape)


def cell_row(ref, row, rows):
    count, depth, width = ref.shape
    block = depth // rows
    return ref[:, row * block : (row + 1) * block, :].astype(F32).reshape(count * block, width)


def middle_kernel(products, d_hat_centered, d_products):
    rows = d_hat_centered.shape[0]
    count, depth, width = products.shape
    block = depth // rows
    for row in range(rows):
        tri_hat, inv_std = norm_rows(cell_row(products, row, rows))
        d_hat = d_hat_centered[row]
        cross = jnp.mean(d_hat * tri_hat, axis=0, keepdims=True)
        d_tri = inv_std * (d_hat - tri_hat * cross)
        d_products[:, row * block : (row + 1) * block, :] = d_tri.reshape(
            count, block, width
        ).astype(BF16)


def d_right_kernel(d_products, left_pairs, d_right_panel, d_tri_all, left_wide, right_wide):
    block, left_rows, width = d_tri_all.shape
    right_rows = right_wide.shape[0] // block
    spread(d_products, left_wide)
    for n in range(block // 2):
        pair = (2 * n, 2 * n + 1)
        d_tri = [left_wide[pl.ds(h, left_rows, stride=block), :] for h in pair]
        d_tri = jnp.concatenate(d_tri, axis=0).astype(BF16)
        d_right = dot(d_tri, left_pairs[n], 0, 0)
        for side, h in enumerate(pair):
            d_tri_all[h] = d_tri[side * left_rows : (side + 1) * left_rows]
            right_wide[pl.ds(h, right_rows, stride=block), :] = d_right[
                :, side * width : (side + 1) * width
            ]
    for rank, place in wide_places(d_right_panel, d_products.shape[0], True):
        d_right_panel[rank] = right_wide[place, :].astype(BF16)


def d_left_kernel(d_tri_all, right_all, *refs):
    *pieces, left_wide = refs
    block, left_rows, _ = d_tri_all.shape
    for h in range(block):
        left_wide[pl.ds(h, left_rows, stride=block), :] = dot(d_tri_all[h], right_all[h], 1, 0)
    depth = pieces[0].shape[0]
    for step, piece in enumerate(pieces):
        start = pl.multiple_of(partner(step, len(pieces)) * depth, depth)
        piece[...] = left_wide[pl.ds(start, depth), :].astype(BF16)


def gate_back_kernel(products, gate_slope, out_gain, out_bias, w_out, d_gate_pre):
    rows = gate_slope.shape[0]
    out_flip = transposed(w_out[...])
    out_gain_col, out_bias_col = column(out_gain[...]), column(out_bias[...])
    for row in range(rows):
        tri_hat, _ = norm_rows(cell_row(products, row, rows))
        scaled = (tri_hat * out_gain_col + out_bias_col).astype(BF16)
        d_gate_pre[row] = (dot(out_flip, scaled, 1, 0) * gate_slope[row]).astype(BF16)


def slopes_kernel(
    pair, mask, gain, bias, w_proj, w_gate, after, slopes, normed_in, inv_in, in_gain, weights
):
    del after
    rows = pair.shape[0]
    hidden = w_proj.shape[1] // 4
    w_flip = transposed(w_proj[...])
    gain_col, bias_col = column(gain[...]), column(bias[...])
    in_gain[...] = gain_col
    weights[...] = jnp.concatenate([w_proj[...], w_gate[...]], axis=1)
    masks = cell_masks(mask, rows)
    for row in range(rows):
        normed, inv_std = norm_rows(jnp.transpose(pair[row].astype(F32)))
        normed_in[row] = normed.astype(normed_in.dtype)
        inv_in[row : row + 1] = inv_std
        zln = (normed * gain_col + bias_col).astype(BF16)
        proj = dot(w_flip, zln, 1, 0)
        for side in range(2):
            base = 2 * side * hidden
            sig = sigmoid(proj[base : base + hidden])
            masked = masks[row] * sig
            value = masked * (1.0 - sig) * proj[base + hidden : base + 2 * hidden]
            slopes[row, base : base + hidden, :] = value.astype(slopes.dtype)
            slopes[row, base + hidden : base + 2 * hidden, :] = masked.astype(slopes.dtype)


def sloped(d_value, slopes, row, side):
    hidden = d_value.shape[0]
    parts = []
    for base in (2 * side * hidden, (2 * side + 1) * hidden):
        slope = slopes[row, base : base + hidden, :].astype(F32)
        parts.append((d_value * slope).astype(BF16))
    return jnp.concatenate(parts, axis=0)


def finish_left_kernel(slopes, d_gate_pre, weights, *refs):
    *pieces, d_zln_left, panel = refs
    rows = d_zln_left.shape[0]
    for step, piece in enumerate(pieces):
        panel[partner(step, len(pieces))] = piece[...]
    half = slopes.shape[1] // 2
    own = jnp.concatenate([weights[:, :half], weights[:, 2 * half :]], axis=1)
    for row in range(rows):
        d_proj = sloped(cell_row(panel, row, rows), slopes, row, 0)
        d_zln_left[row] = dot(own, jnp.concatenate([d_proj, d_gate_pre[row]], axis=0), 1, 0)


def both_halves(blocks, count):
    order = wide_order(2 * count, count, True)
    return jnp.stack(
        [blocks[order.index(place)] + blocks[order.index(count + place)] for place in range(count)]
    )


def finish_kernel(
    d_right_panel, d_zln_left, slopes, normed_in, inv_in, gain_col, weights, grad
):
    rows = grad.shape[0]
    devices, depth, width = d_right_panel.shape
    half = slopes.shape[1] // 2
    for row in range(rows):
        d_right = cell_row(d_right_panel, row, rows)
        d_right = both_halves(d_right.reshape(devices, depth // rows, width), devices // 2)
        d_proj = sloped(d_right.reshape(half // 2, width), slopes, row, 1)
        d_zln = d_zln_left[row] + dot(weights[:, half : 2 * half], d_proj, 1, 0)
        d_in = d_zln * gain_col[...]
        normed = normed_in[row].astype(F32)
        mean_grad = jnp.mean(d_in, axis=0, keepdims=True)
        mean_cross = jnp.mean(d_in * normed, axis=0, keepdims=True)
        result = inv_in[row : row + 1] * (d_in - mean_grad - normed * mean_cross)
        grad[row] = jnp.transpose(result).astype(BF16)


def swap(values, count, back):
    groups = [wide_order(lax.axis_size("row"), count, back)]
    return lax.all_to_all(
        values, "row", split_axis=0, concat_axis=0, tiled=True, axis_index_groups=groups
    )


def swap_half(values, count):
    devices = range(lax.axis_size("row"))
    groups = [[d for d in devices if d // count == half] for half in range(len(devices) // count)]
    return lax.all_to_all(
        values, "row", split_axis=0, concat_axis=0, tiled=True, axis_index_groups=groups
    )


def swap_pieces(pieces):
    devices = range(lax.axis_size("row"))
    count = len(pieces)
    return [pieces[0]] + [
        lax.ppermute(pieces[step], "row", [(d, d ^ distance(step, count)) for d in devices])
        for step in range(1, count)
    ]


def kernel_shards(
    pair,
    cotangent,
    residue_mask,
    ln_in_gain,
    ln_in_bias,
    w_proj,
    w_gate,
    ln_out_gain,
    ln_out_bias,
    w_out,
):
    rows, width, channels = pair.shape
    hidden = w_out.shape[0]
    halves = 2
    devices = lax.axis_size("row")
    count = devices // halves
    block = hidden // count
    left_rows, right_rows = rows * count, rows * devices
    shape = jax.ShapeDtypeStruct
    panel = shape((count, rows * block, width), BF16)
    wide_panel = shape((devices, rows * block, width), BF16)
    mask = residue_mask.reshape(1, width)
    gain, bias = ln_in_gain.reshape(1, channels), ln_in_bias.reshape(1, channels)
    out_gain, out_bias = ln_out_gain.reshape(1, hidden), ln_out_bias.reshape(1, hidden)
    cells = rows * width
    piece = shape((rows * block, width), BF16)
    left_panel = pltpu.VMEM(panel.shape, BF16)
    left_wide = pltpu.VMEM((left_rows * block, width), F32)
    right_wide = pltpu.VMEM((right_rows * block, width), F32)
    (own_right,) = call(
        project_right_kernel,
        "project_right",
        [wide_panel],
        [pair, mask, gain, bias, w_proj],
        fetched=range(5),
        columns={4: pl.ds(2 * hidden, 2 * hidden)},
        flops=2 * cells * channels * 2 * hidden,
        limit=64 * 1024 * 1024 - 640 * 1024,
    )
    right_panel = swap(own_right, count, False)
    pieces = call(
        project_left_kernel,
        "project_left",
        [piece] * count,
        [pair, mask, gain, bias, w_proj, own_right],
        fetched=range(5),
        columns={4: pl.ds(0, 2 * hidden)},
        unread=(5,),
        scratch=[left_panel],
        flops=2 * cells * channels * 2 * hidden,
    )
    pieces = swap_pieces(pieces)
    (left_pairs,) = call(
        sort_left_kernel,
        "sort_left",
        [shape((block // 2, 2 * left_rows, 2 * width), BF16)],
        pieces,
        scratch=[left_wide],
    )
    d_hat_centered, gate_slope = call(
        prepare_kernel,
        "prepare",
        [shape((rows, hidden, width), F32), shape((rows, channels, width), F32)],
        [pair, cotangent, gain, bias, w_gate, out_gain, w_out],
        fetched=range(7),
        flops=2 * cells * channels * 2 * hidden,
    )
    products, right_all = call(
        tri_kernel,
        "tri",
        [panel, shape((block, right_rows, width), BF16)],
        [right_panel, left_pairs, d_hat_centered],
        unread=(2,),
        scratch=[left_wide, right_wide],
        flops=2 * block * left_rows * width * right_rows,
    )
    products = swap_half(products, count)
    (d_products,) = call(
        middle_kernel,
        "middle",
        [panel],
        [products, d_hat_centered],
        flops=20 * cells * hidden,
    )
    d_products = swap_half(d_products, count)
    d_right_panel, d_tri_all = call(
        d_right_kernel,
        "d_right",
        [wide_panel, shape((block, left_rows, width), BF16)],
        [d_products, left_pairs],
        scratch=[left_wide, right_wide],
        flops=2 * block * left_rows * width * right_rows,
    )
    d_right_panel = swap(d_right_panel, count, True)
    d_pieces = call(
        d_left_kernel,
        "d_left",
        [piece] * count,
        [d_tri_all, right_all],
        scratch=[left_wide],
        flops=2 * block * left_rows * width * right_rows,
    )
    d_pieces = swap_pieces(d_pieces)
    (d_gate_pre,) = call(
        gate_back_kernel,
        "gate_back",
        [shape((rows, channels, width), BF16)],
        [products, gate_slope, out_gain, out_bias, w_out],
        fetched=range(2, 5),
        flops=2 * cells * channels * hidden,
    )
    slopes, normed_in, inv_in, gain_col, weights = call(
        slopes_kernel,
        "slopes",
        [
            shape((rows, 4 * hidden, width), BF16),
            shape((rows, channels, width), BF16),
            shape((rows, width), F32),
            shape((channels, channels), F32),
            shape((channels, 4 * hidden + channels), BF16),
        ],
        [pair, mask, gain, bias, w_proj, w_gate, d_gate_pre],
        fetched=range(6),
        unread=(6,),
        flops=2 * cells * channels * 4 * hidden,
    )
    (d_zln_left,) = call(
        finish_left_kernel,
        "finish_left",
        [shape((rows, channels, width), F32)],
        [slopes, d_gate_pre, weights, *d_pieces],
        scratch=[left_panel],
        flops=2 * cells * channels * 3 * hidden,
    )
    (grad,) = call(
        finish_kernel,
        "finish",
        [shape(pair.shape, BF16)],
        [
            d_right_panel,
            d_zln_left,
            slopes,
            normed_in,
            inv_in,
            gain_col,
            weights,
        ],
        flops=2 * cells * channels * 4 * hidden,
    )
    return grad


def normalize(values, reduce_axis):
    mean_value = jnp.mean(values, axis=reduce_axis, keepdims=True)
    centered = values - mean_value
    variance = jnp.mean(centered * centered, axis=reduce_axis, keepdims=True)
    inv_std = lax.rsqrt(variance + 1e-05)
    return (centered * inv_std, inv_std)


def norm_backward(upstream, normed, inv_std, reduce_axis):
    mean_grad = jnp.mean(upstream, axis=reduce_axis, keepdims=True)
    mean_cross = jnp.mean(upstream * normed, axis=reduce_axis, keepdims=True)
    return inv_std * (upstream - mean_grad - normed * mean_cross)


def shards(
    pair,
    cotangent,
    residue_mask,
    ln_in_gain,
    ln_in_bias,
    w_proj,
    w_gate,
    ln_out_gain,
    ln_out_bias,
    w_out,
):
    local_rows = pair.shape[0]
    local_cols = pair.shape[1]
    hidden = w_out.shape[0]
    chan_index = lax.axis_index("chan")
    row_start = lax.axis_index("row") * local_rows
    col_start = chan_index * local_cols
    mask_float = residue_mask.astype(jnp.float32)
    row_mask = lax.dynamic_slice_in_dim(mask_float, row_start, local_rows)
    col_mask = lax.dynamic_slice_in_dim(mask_float, col_start, local_cols)
    cell_mask = (row_mask[:, None] * col_mask[None, :])[None]
    normed, inv_std = normalize(pair.astype(jnp.float32), -1)
    normed_pair = (normed * ln_in_gain + ln_in_bias).astype(jnp.bfloat16)
    projected = jnp.einsum("rmc,ch->hrm", normed_pair, w_proj, preferred_element_type=jnp.float32)
    left_panel = (
        cell_mask * jax.nn.sigmoid(projected[:hidden]) * projected[hidden : 2 * hidden]
    ).astype(jnp.bfloat16)
    right_panel = (
        cell_mask * jax.nn.sigmoid(projected[2 * hidden : 3 * hidden]) * projected[3 * hidden :]
    ).astype(jnp.bfloat16)
    panels = lax.all_to_all(
        jnp.stack([left_panel, right_panel]), "row", split_axis=1, concat_axis=2, tiled=True
    )
    left_all = panels[0]
    right_all = panels[1]
    right_rows = lax.all_to_all(right_all, "chan", split_axis=1, concat_axis=2, tiled=True)
    partner = right_rows
    tri_part = jnp.einsum(
        "gik,gjk->gij",
        lax.all_gather(left_all, "chan", axis=2, tiled=True),
        partner,
        preferred_element_type=jnp.float32,
    ).astype(jnp.bfloat16)
    tri_cells = lax.all_to_all(tri_part, "row", split_axis=1, concat_axis=0, tiled=True)
    tri_hat, inv_tri = normalize(tri_cells.astype(jnp.float32), 0)
    scaled = (tri_hat * ln_out_gain[:, None, None] + ln_out_bias[:, None, None]).astype(
        jnp.bfloat16
    )
    proj_out = jnp.einsum("hrm,hc->rmc", scaled, w_out, preferred_element_type=jnp.float32)
    gate_value = jax.nn.sigmoid(
        jnp.einsum("rmc,cd->rmd", normed_pair, w_gate, preferred_element_type=jnp.float32)
    )
    cot_float = cotangent.astype(jnp.float32)
    d_gate_pre = (cot_float * proj_out * gate_value * (1.0 - gate_value)).astype(jnp.bfloat16)
    d_scaled = (cot_float * gate_value).astype(jnp.bfloat16)
    d_hat = jnp.einsum("rmc,hc->hrm", d_scaled, w_out, preferred_element_type=jnp.float32)
    d_hat = d_hat * ln_out_gain[:, None, None]
    d_tri = norm_backward(d_hat, tri_hat, inv_tri, 0).astype(jnp.bfloat16)
    d_tri_all = lax.all_to_all(d_tri, "row", split_axis=0, concat_axis=1, tiled=True)
    panel_piece = lax.all_gather(d_tri_all, "chan", axis=2, tiled=True)
    partner = right_all
    d_left = jnp.einsum("gij,gjk->gik", panel_piece, partner, preferred_element_type=jnp.float32)
    contribution = jnp.einsum(
        "gij,gik->gjk", panel_piece, left_all, preferred_element_type=jnp.float32
    )
    d_right = contribution
    d_left, d_right = (d_left, d_right)
    d_stack = jnp.stack([d_left, d_right]).astype(jnp.bfloat16)
    d_panels = lax.all_to_all(d_stack, "row", split_axis=2, concat_axis=1, tiled=True)

    def gating(d_value, gate_proj, value_proj):
        sigmoid_val = jax.nn.sigmoid(gate_proj)
        masked_grad = d_value.astype(jnp.float32) * cell_mask
        return (
            masked_grad * value_proj * sigmoid_val * (1.0 - sigmoid_val),
            masked_grad * sigmoid_val,
        )

    gate_left, value_left = gating(d_panels[0], projected[:hidden], projected[hidden : 2 * hidden])
    gate_right, value_right = gating(
        d_panels[1], projected[2 * hidden : 3 * hidden], projected[3 * hidden :]
    )
    d_proj = jnp.concatenate([gate_left, value_left, gate_right, value_right], axis=0).astype(
        jnp.bfloat16
    )
    d_normed = jnp.einsum("hrm,ch->rmc", d_proj, w_proj, preferred_element_type=jnp.float32)
    d_normed = d_normed + jnp.einsum(
        "rmd,cd->rmc", d_gate_pre, w_gate, preferred_element_type=jnp.float32
    )
    d_input = d_normed * ln_in_gain
    return norm_backward(d_input, normed, inv_std, -1).astype(jnp.bfloat16)


def solution(mesh):
    fits = mesh.shape["chan"] == 1 and mesh.shape["row"] in (8, 16)
    return jax.shard_map(
        kernel_shards if fits else shards,
        mesh=mesh,
        in_specs=(
            P(("grp", "row"), "chan", None),
            P(("grp", "row"), "chan", None),
            P("grp"),
            P(),
            P(),
            P(),
            P(),
            P(),
            P(),
            P(),
        ),
        out_specs=P(("grp", "row"), "chan", None),
        check_vma=False,
    )
```
